32 devices in a mesh: rows: 8 (over z, y), heads: 4 (over x, core).
Axes of the slice: x: 2, y: 2, z: 4, core: 2. Of those that a mesh axis runs over, the one named last changes fastest.
Arguments:
- query_stream: bfloat16 [16384, 512], P('rows'), may hold values from -6 to 6
- content_stream: bfloat16 [16384, 512], P('rows'), may hold values from -6 to 6
- memory: bfloat16 [16384, 512], P('rows'), may hold values from -6 to 6
- segment_ids: int32 [16384], P('rows'), may hold values from 0 to 7, as said below
- source_segments: int32 [16384], P('rows'), may hold values from 0 to 7, as said below
- context_rank: int32 [16384], P('rows'), may hold values from 0 to 63
- context_limit: int32 [16384], P('rows'), may hold values from 1 to 64
- padding: int32 [16384], P('rows'), may hold values from 0 to 1, as said below
- ln_query_gain: float32 [512], replicated, may hold values from 0.25 to 1.75
- ln_query_bias: float32 [512], replicated, may hold values from -0.5 to 0.5
- ln_content_gain: float32 [512], replicated, may hold values from 0.25 to 1.75
- ln_content_bias: float32 [512], replicated, may hold values from -0.5 to 0.5
- self_query: bfloat16 [512, 512], P(None, 'heads'), may hold values from -0.25 to 0.25
- self_key: bfloat16 [512, 512], P(None, 'heads'), may hold values from -0.25 to 0.25
- self_value: bfloat16 [512, 512], P(None, 'heads'), may hold values from -0.25 to 0.25
- self_out: bfloat16 [512, 512], P('heads'), may hold values from -0.5 to 0.5
- ln_cross_gain: float32 [512], replicated, may hold values from 0.25 to 1.75
- ln_cross_bias: float32 [512], replicated, may hold values from -0.5 to 0.5
- cross_query: bfloat16 [512, 512], P(None, 'heads'), may hold values from -0.25 to 0.25
- cross_key: bfloat16 [512, 512], P(None, 'heads'), may hold values from -0.25 to 0.25
- cross_value: bfloat16 [512, 512], P(None, 'heads'), may hold values from -0.25 to 0.25
- cross_out: bfloat16 [512, 512], P('heads'), may hold values from -0.5 to 0.5
- ln_ffn_gain: float32 [512], replicated, may hold values from 0.25 to 1.75
- ln_ffn_bias: float32 [512], replicated, may hold values from -0.5 to 0.5
- ffn_in: bfloat16 [512, 2048], P(None, 'heads'), may hold values from -0.25 to 0.25
- ffn_out: bfloat16 [2048, 512], P('heads'), may hold values from -0.125 to 0.125
- cotangent: bfloat16 [16384, 512], P('rows'), may hold values from -6 to 6
Outputs:
- output: bfloat16 [16384, 512], P('rows')
- grad_query_stream: float32 [16384, 512], P('rows')
- grad_content_stream: float32 [16384, 512], P('rows')
- grad_memory: float32 [16384, 512], P('rows')
- grad_ln_query_gain: float32 [512], replicated
- grad_ln_query_bias: float32 [512], replicated
- grad_ln_content_gain: float32 [512], replicated
- grad_ln_content_bias: float32 [512], replicated
- grad_self_query: float32 [512, 512], P(None, 'heads')
- grad_self_key: float32 [512, 512], P(None, 'heads')
- grad_self_value: float32 [512, 512], P(None, 'heads')
- grad_self_out: float32 [512, 512], P('heads')
- grad_ln_cross_gain: float32 [512], replicated
- grad_ln_cross_bias: float32 [512], replicated
- grad_cross_query: float32 [512, 512], P(None, 'heads')
- grad_cross_key: float32 [512, 512], P(None, 'heads')
- grad_cross_value: float32 [512, 512], P(None, 'heads')
- grad_cross_out: float32 [512, 512], P('heads')
- grad_ln_ffn_gain: float32 [512], replicated
- grad_ln_ffn_bias: float32 [512], replicated
- grad_ffn_in: float32 [512, 2048], P(None, 'heads')
- grad_ffn_out: float32 [2048, 512], P('heads')
The draws below stay inside these ranges and needn't reach their ends.
Inputs may be any that keep to these rules, and one draw needn't show every extreme that they name: `segment_ids`: starts at 0 in each packed row of 1024 tokens and never falls along it; 8 documents a row, each of 64 tokens or more. `source_segments`: starts at 0 in each packed row of 1024 tokens and never falls along it; 8 documents a row, each of 64 tokens or more; source document k of a row belongs to target document k of the same row. `padding`: 1 on a tail of each packed row of 1 to 32 tokens, all inside the row's last document and after its first two tokens; 0 elsewhere.
All inputs are finite; a program needn't handle non-finite values.
Results may differ from the reference program's by a relative error of at most 0.04.
Values may be sent and summed in bfloat16 or wider, within the bound.
No kernel may reach another device: no remote copies, remote signals or barrier semaphores. Data moves between devices by JAX's collectives and lax.ppermute only.
A program may use at most 128 MiB of HBM per device.

```python
import jax
import jax.numpy as jnp
from jax import lax

D = 512
HEADS = 8
FF = 2048
HEAD_DIM = 64
SEQ = 1024
SRC = 1024
DOCS = 8
ROWS = 16
TOKENS = 16384
SOURCE = 16384
N_HEADS = 4


def document_numbers(key, length, doc_count, row_count):
    jitter_width = length // (4 * doc_count)
    centres = jnp.arange(1, doc_count, dtype=jnp.int32) * (length // doc_count)
    jitter = jax.random.randint(key, (row_count, doc_count - 1), -jitter_width, jitter_width + 1, dtype=jnp.int32)
    bounds = centres[None, :] + jitter
    places = jnp.arange(length, dtype=jnp.int32)
    numbers = jnp.sum((places[None, :, None] >= bounds[:, None, :]).astype(jnp.int32), axis=2)
    return numbers.reshape(row_count * length)


def draw_segment_ids(key, part):
    key = jax.random.fold_in(key, 31)
    return document_numbers(key, SEQ, DOCS, ROWS)


def draw_source_segments(key, part):
    key = jax.random.fold_in(key, 42)
    return document_numbers(key, SRC, DOCS, ROWS)


def draw_padding(key, part):
    key = jax.random.fold_in(key, 53)
    tail_lengths = jax.random.randint(key, (ROWS, 1), 1, SEQ // (4 * DOCS) + 1, dtype=jnp.int32)
    places = jnp.arange(SEQ, dtype=jnp.int32)
    return (places[None, :] >= SEQ - tail_lengths).astype(jnp.int32).reshape(ROWS * SEQ)


def touch_ends(values, stream_key, least, largest):
    shape = values.shape
    index_at = [jax.random.randint(jax.random.fold_in(stream_key, axis), (), 0, shape[axis]) for axis in range(len(shape))]
    values = values.at[tuple(index_at)].set(least)
    longest = shape.index(max(shape))
    index_at[longest] = (index_at[longest] + 1) % shape[longest]
    return values.at[tuple(index_at)].set(largest)


def block_scale(rng, extent, shards, smallest, top_value):
    def one(position, shards_of):
        draws = jax.random.uniform(jax.random.fold_in(jax.random.fold_in(rng, 6), position), (shards_of,), jnp.float32, smallest / len(shards), top_value / len(shards))
        return jnp.repeat(jnp.exp(draws), extent[position] // shards_of).reshape((-1,) + (1,) * (len(extent) - position - 1))

    factor_of = one(*shards[0])
    for cut in shards[1:]:
        factor_of = factor_of * one(*cut)
    return factor_of


def normal_values(rng, dims, deviation, limit, split=(), held_as=jnp.bfloat16):
    values = deviation * jax.random.normal(rng, dims, jnp.float32)
    if split:
        values = values * block_scale(rng, dims, split, -0.22, 0.18)
    return jnp.clip(values, -limit, limit).astype(held_as)


def setup_inputs(seed: int = 0) -> dict:
    keys = jax.random.split(jax.random.key(seed), 28)
    return {
        "query_stream": normal_values(keys[0], (TOKENS, D), 1.0, 6.0, ((0, 8),)),
        "content_stream": normal_values(keys[1], (TOKENS, D), 1.0, 6.0, ((0, 8),)),
        "memory": normal_values(keys[2], (SOURCE, D), 1.0, 6.0, ((0, 8),)),
        "segment_ids": draw_segment_ids(jax.random.fold_in(keys[27], 71), 0),
        "source_segments": draw_source_segments(jax.random.fold_in(keys[27], 71), 0),
        "context_rank": touch_ends(jax.random.randint(keys[5], (TOKENS,), 0, 64), jax.random.fold_in(keys[5], 1), 0, 63).astype(jnp.int32),
        "context_limit": touch_ends(jax.random.randint(keys[6], (TOKENS,), 1, 65), jax.random.fold_in(keys[6], 1), 1, 64).astype(jnp.int32),
        "padding": draw_padding(jax.random.fold_in(keys[27], 71), 0),
        "ln_query_gain": jnp.clip(1.0 + 0.15 * jax.random.normal(keys[8], (D,), jnp.float32), 0.25, 1.75),
        "ln_query_bias": jnp.clip(jax.random.uniform(keys[9], (D,), jnp.float32, -0.5, 0.5), -0.5, 0.5),
        "ln_content_gain": jnp.clip(1.0 + 0.15 * jax.random.normal(keys[10], (D,), jnp.float32), 0.25, 1.75),
        "ln_content_bias": jnp.clip(jax.random.uniform(keys[11], (D,), jnp.float32, -0.5, 0.5), -0.5, 0.5),
        "self_query": normal_values(keys[12], (D, D), D ** -0.5, 0.25, ((1, 4),)),
        "self_key": normal_values(keys[13], (D, D), D ** -0.5, 0.25, ((1, 4),)),
        "self_value": normal_values(keys[14], (D, D), D ** -0.5, 0.25, ((1, 4),)),
        "self_out": normal_values(keys[15], (D, D), (D // 4) ** -0.5, 0.5, ((0, 4),)),
        "ln_cross_gain": jnp.clip(1.0 + 0.15 * jax.random.normal(keys[16], (D,), jnp.float32), 0.25, 1.75),
        "ln_cross_bias": jnp.clip(jax.random.uniform(keys[17], (D,), jnp.float32, -0.5, 0.5), -0.5, 0.5),
        "cross_query": normal_values(keys[18], (D, D), D ** -0.5, 0.25, ((1, 4),)),
        "cross_key": normal_values(keys[19], (D, D), D ** -0.5, 0.25, ((1, 4),)),
        "cross_value": normal_values(keys[20], (D, D), D ** -0.5, 0.25, ((1, 4),)),
        "cross_out": normal_values(keys[21], (D, D), (D // 4) ** -0.5, 0.5, ((0, 4),)),
        "ln_ffn_gain": jnp.clip(1.0 + 0.15 * jax.random.normal(keys[22], (D,), jnp.float32), 0.25, 1.75),
        "ln_ffn_bias": jnp.clip(jax.random.uniform(keys[23], (D,), jnp.float32, -0.5, 0.5), -0.5, 0.5),
        "ffn_in": normal_values(keys[24], (D, FF), D ** -0.5, 0.25, ((1, 4),)),
        "ffn_out": normal_values(keys[25], (FF, D), FF ** -0.5, 0.125, ((0, 4),)),
        "cotangent": normal_values(keys[26], (TOKENS, D), 1.0, 6.0, ((0, 8),)),
    }


@jax.custom_vjp
def low(v):
    return lax.optimization_barrier(v.astype(jnp.bfloat16)).astype(jnp.float32)

@jax.custom_vjp
def low_back(v):
    return v

def low_keep(v):
    return (low(v), None)

def low_pass(kept, grad):
    return (grad,)

def back_keep(v):
    return (v, None)

def back_low(kept, grad):
    return (low(grad),)
low.defvjp(low_keep, low_pass)
low_back.defvjp(back_keep, back_low)
norm_eps = 1e-05
masked_score = -1e+30

def rounded_both(values):
    return low_back(low(values))

def matmul(left, right):
    return jnp.dot(left, right, precision=lax.Precision.HIGHEST)

def layer_norm(values, gain, shift):
    centre = values - lax.optimization_barrier(jnp.mean(values, axis=-1, keepdims=True))
    spread = lax.optimization_barrier(jnp.mean(centre * centre, axis=-1, keepdims=True))
    return centre * lax.rsqrt(spread + norm_eps) * gain + shift

def doc_start(segments):
    places = jnp.arange(segments.shape[0], dtype=jnp.int32)
    before_ids = jnp.concatenate([jnp.full((1,), -1, jnp.int32), segments[:-1].astype(jnp.int32)])
    return lax.cummax(jnp.where(segments != before_ids, places, 0).astype(jnp.int32), axis=0)

def self_mask(segments, ranks, limits, padding_row):
    places = jnp.arange(segments.shape[0], dtype=jnp.int32)
    starts = doc_start(segments)
    same_doc = segments[:, None] == segments[None, :]
    chosen = ranks[None, :] < limits[:, None]
    anchor = places[None, :] < starts[:, None] + 2
    others = places[:, None] != places[None, :]
    return same_doc & others & (padding_row[None, :] == 0) & (chosen | anchor)

def attention(queries, key_rows, value_rows, allowed):
    lead_rows = queries.shape[0]
    query_heads = queries.reshape(lead_rows, HEADS, HEAD_DIM)
    key_heads = key_rows.reshape(key_rows.shape[0], HEADS, HEAD_DIM)
    value_heads = value_rows.reshape(value_rows.shape[0], HEADS, HEAD_DIM)
    scores = jnp.einsum('qhd,khd->hqk', query_heads, key_heads, precision=lax.Precision.HIGHEST) * HEAD_DIM ** (-0.5)
    scores = low_back(jnp.where(allowed[None], scores, masked_score))
    row_top = lax.optimization_barrier(jnp.max(scores, axis=-1, keepdims=True))
    exponent = jnp.exp(scores - row_top)
    probabilities = exponent / lax.optimization_barrier(jnp.sum(exponent, axis=-1, keepdims=True))
    mixed_heads = jnp.einsum('hqk,khd->qhd', low(probabilities), value_heads, precision=lax.Precision.HIGHEST)
    return rounded_both(mixed_heads.reshape(lead_rows, HEADS * HEAD_DIM))

def grouped_projection(mixed_rows, weight):
    lead_rows = mixed_rows.shape[0]
    group_width = weight.shape[0] // N_HEADS
    pieces = jnp.einsum('lgc,gcd->gld', mixed_rows.reshape(lead_rows, N_HEADS, group_width), weight.reshape(N_HEADS, group_width, weight.shape[1]), precision=lax.Precision.HIGHEST)
    return low_back(lax.optimization_barrier(jnp.sum(low(pieces), axis=0)))

def layer_forward(stream, content, memory_rows, params, allowed):
    ln_query_gain, ln_query_bias, ln_content_gain, ln_content_bias, self_query, self_key, self_value, self_out, ln_cross_gain, ln_cross_bias, cross_query, cross_key, cross_value, cross_out, ln_ffn_gain, ln_ffn_bias, ffn_in, ffn_out = params
    self_allowed, cross_allowed = allowed
    normed_query = low(layer_norm(stream, ln_query_gain, ln_query_bias))
    normed_content = low(layer_norm(content, ln_content_gain, ln_content_bias))
    self_queries = rounded_both(matmul(normed_query, self_query))
    self_keys = rounded_both(matmul(normed_content, self_key))
    self_values = rounded_both(matmul(normed_content, self_value))
    self_mixed = attention(self_queries, self_keys, self_values, self_allowed)
    second = stream + grouped_projection(self_mixed, self_out)
    normed_cross = low(layer_norm(second, ln_cross_gain, ln_cross_bias))
    cross_queries = rounded_both(matmul(normed_cross, cross_query))
    cross_keys = rounded_both(matmul(memory_rows, cross_key))
    cross_values = rounded_both(matmul(memory_rows, cross_value))
    cross_mixed = attention(cross_queries, cross_keys, cross_values, cross_allowed)
    third = second + grouped_projection(cross_mixed, cross_out)
    normed_ffn = low(layer_norm(third, ln_ffn_gain, ln_ffn_bias))
    before = low_back(matmul(normed_ffn, ffn_in))
    hidden = low(jax.nn.gelu(before, approximate=True))
    return third + low_back(matmul(hidden, ffn_out))

def reference(query_stream, content_stream, memory, segment_ids, source_segments, context_rank, context_limit, padding, ln_query_gain, ln_query_bias, ln_content_gain, ln_content_bias, self_query, self_key, self_value, self_out, ln_cross_gain, ln_cross_bias, cross_query, cross_key, cross_value, cross_out, ln_ffn_gain, ln_ffn_bias, ffn_in, ffn_out, cotangent):
    weights = (ln_query_gain, ln_query_bias, ln_content_gain, ln_content_bias, self_query, self_key, self_value, self_out, ln_cross_gain, ln_cross_bias, cross_query, cross_key, cross_value, cross_out, ln_ffn_gain, ln_ffn_bias, ffn_in, ffn_out)
    params = tuple((item.astype(jnp.float32) for item in weights))
    row_count = query_stream.shape[0] // SEQ

    def per_row(array, length):
        return array.reshape((row_count, length) + array.shape[1:])
    row_inputs = (per_row(query_stream, SEQ), per_row(content_stream, SEQ), per_row(memory, SRC), per_row(segment_ids, SEQ), per_row(source_segments, SRC), per_row(context_rank, SEQ), per_row(context_limit, SEQ), per_row(padding, SEQ), per_row(cotangent, SEQ))

    def row_step(totals, row_data):
        stream, content, source_rows, segments, sources, ranks, limits, pads, upstream = row_data
        allowed = (self_mask(segments, ranks, limits, pads), segments[:, None] == sources[None, :])

        def forward(first_in, second_in, third_in, params_now):
            return layer_forward(first_in, second_in, third_in, params_now, allowed)
        result, pull_back = jax.vjp(forward, stream.astype(jnp.float32), content.astype(jnp.float32), source_rows.astype(jnp.float32), params)
        grads = pull_back(upstream.astype(jnp.float32))
        totals = tuple((total + grad_item for total, grad_item in zip(totals, grads[3])))
        return (totals, (result.astype(jnp.bfloat16), grads[0], grads[1], grads[2]))
    initial = tuple((jnp.zeros_like(item) for item in params))
    totals, row_outputs = lax.scan(row_step, initial, row_inputs)
    output = row_outputs[0].reshape(-1, D)
    grad_query_stream = row_outputs[1].reshape(-1, D)
    grad_content_stream = row_outputs[2].reshape(-1, D)
    grad_memory = row_outputs[3].reshape(-1, D)
    return (output, grad_query_stream, grad_content_stream, grad_memory, totals[0], totals[1], totals[2], totals[3], totals[4], totals[5], totals[6], totals[7], totals[8], totals[9], totals[10], totals[11], totals[12], totals[13], totals[14], totals[15], totals[16], totals[17])
```

```python
import functools

import jax
import jax.numpy as jnp
from jax import lax
from jax.experimental import pallas as pl
from jax.experimental.pallas import tpu as pltpu
from jax.sharding import PartitionSpec as P

HEAD_DIM = 64
SEQ = 1024
DOCS = 8
D = 512
TILE = 256
TILES = SEQ // TILE
FAST_Q = 208
FAST_K = 256
LONG_Q = 128
LONG_K = 640

norm_eps = 1e-05
masked_score = -1e30
hidden_rank = 1e6
gelu_root = 0.7978845608028654
gelu_cube = 0.044715

f32 = jnp.float32
bf16 = jnp.bfloat16


def dot(a, b):
    return lax.dot_general(a, b, (((1,), (0,)), ((), ())), preferred_element_type=f32)


def dot_nt(a, b):
    return lax.dot_general(a, b, (((1,), (1,)), ((), ())), preferred_element_type=f32)


def dot_tn(a, b):
    return lax.dot_general(a, b, (((0,), (0,)), ((), ())), preferred_element_type=f32)


def lanes(parts):
    return jnp.concatenate(parts, axis=1)


def layer_norm(values, gain, shift):
    centre = values - jnp.mean(values, axis=-1, keepdims=True)
    spread = jnp.mean(centre * centre, axis=-1, keepdims=True)
    return centre * lax.rsqrt(spread + norm_eps) * gain + shift


def norm_backward(values, gain, grad):
    centre = values - jnp.mean(values, axis=-1, keepdims=True)
    spread = jnp.mean(centre * centre, axis=-1, keepdims=True)
    scale = lax.rsqrt(spread + norm_eps)
    xhat = centre * scale
    eg = grad * gain
    mean_eg = jnp.mean(eg, axis=-1, keepdims=True)
    mean_egx = jnp.mean(eg * xhat, axis=-1, keepdims=True)
    grad_gain = jnp.sum(grad * xhat, axis=0, keepdims=True)
    grad_shift = jnp.sum(grad, axis=0, keepdims=True)
    return scale * (eg - mean_eg - xhat * mean_egx), grad_gain, grad_shift


def rows_of(i, size=TILE):
    return pl.ds(pl.multiple_of(i * size, size), size)


def w_query(ref):
    return ref[0:512, :]


def w_key(ref):
    return ref[512:1024, :]


def w_value(ref):
    return ref[1024:1536, :]


def w_out(ref):
    return lanes([ref[1536 + 128 * j : 1664 + 128 * j, :] for j in range(4)])


def half_masks():
    place = lax.broadcasted_iota(jnp.int32, (1, 128), 1)
    low = jnp.where(place < HEAD_DIM, 1.0, 0.0).astype(f32)
    return (low.astype(bf16), (1.0 - low).astype(bf16))


def doc_bounds(meta, d, source):
    base = 17 if source else 1
    return meta[base + d], meta[base + 8 + d]


def window_of(first, limit):
    return pl.multiple_of(jnp.minimum((first // 16) * 16, limit), 16)


def key_values(er_ref, ks, ke, k0, width):
    if er_ref is None:
        place = k0 + lax.broadcasted_iota(jnp.int32, (1, width), 1)
        return jnp.where((place >= ks) & (place < ke), 0.0, masked_score)
    ranks = jnp.broadcast_to(er_ref[...], (8, SEQ))
    ranks = pltpu.roll(ranks, lax.rem(SEQ - k0, SEQ), 1)[0:1, 0:width]
    place = k0 + lax.broadcasted_iota(jnp.int32, (1, width), 1)
    ranks = jnp.where((place < ks + 2) & (ranks < hidden_rank), -1.0, ranks)
    return jnp.where((place >= ks) & (place < ke), ranks, hidden_rank)


def make_bias(er_ref, lim_ref, ks, ke, q0, k0, span, width):
    keys = key_values(er_ref, ks, ke, k0, width)
    if er_ref is None:
        return keys
    limits = lim_ref[pl.ds(q0, span), :]
    limits = lanes([limits] * (width // 128))
    row = q0 + lax.broadcasted_iota(jnp.int32, (span, width), 0)
    column = k0 + lax.broadcasted_iota(jnp.int32, (span, width), 1)
    return jnp.where((keys < limits) & (row != column), 0.0, masked_score)


def raised(queries, keys, bias):
    scores = dot_nt(queries, keys) + bias
    return jnp.exp(scores - jnp.max(scores, axis=1, keepdims=True)).astype(bf16)


def for_doc(meta, d, cross, run):
    ts, te = doc_bounds(meta, d, False)
    ks, ke = doc_bounds(meta, d, cross)
    q0 = window_of(ts, SEQ - FAST_Q)
    k0 = window_of(ks, SEQ - FAST_K)
    fast = (te - q0 <= FAST_Q) & (ke - k0 <= FAST_K)

    @pl.when(fast)
    def _():
        run(q0, k0, FAST_Q, FAST_K, ts, te, ks, ke, True)

    @pl.when(jnp.logical_not(fast))
    def _():
        base = (ts // 16) * 16
        k_long = window_of(ks, SEQ - LONG_K)

        def chunk(i, carry):
            lower = base + i * LONG_Q
            q_long = pl.multiple_of(jnp.minimum(lower, SEQ - LONG_Q), 16)
            run(
                q_long,
                k_long,
                LONG_Q,
                LONG_K,
                jnp.maximum(ts, lower),
                jnp.minimum(te, lower + LONG_Q),
                ks,
                ke,
                False,
            )
            return carry

        lax.fori_loop(0, (te - base + LONG_Q - 1) // LONG_Q, chunk, 0)


def attend_doc(meta, d, cross, er_ref, lim_ref, q_ref, k_ref, v_ref, e_ref, mixed_ref, rt_ref):
    pairs = q_ref.shape[1] // 128
    masks = half_masks()

    def run(q0, k0, span, width, low, high, ks, ke, fast):
        bias = make_bias(er_ref, lim_ref, ks, ke, q0, k0, span, width)
        row = q0 + lax.broadcasted_iota(jnp.int32, (span, 128), 0)
        inside = (row >= low) & (row < high)
        ones = jnp.ones((width, 128), bf16)
        for p in range(pairs):
            cols = slice(128 * p, 128 * p + 128)
            queries = q_ref[pl.ds(q0, span), cols]
            keys = k_ref[pl.ds(k0, width), cols]
            values = v_ref[pl.ds(k0, width), cols]
            total = None
            for a in range(2):
                e = raised(queries, keys * masks[a], bias)
                if fast:
                    e_ref[0, 2 * p + a] = e
                part = dot(e, lanes([values * masks[a], ones * masks[a]]))
                total = part if total is None else total + part
            rt = 1.0 / total[:, 128:]
            mixed = total[:, :128] * rt
            old = mixed_ref[pl.ds(q0, span), cols].astype(f32)
            mixed_ref[pl.ds(q0, span), cols] = jnp.where(inside, mixed, old).astype(bf16)
            rt_ref[pl.ds(q0, span), cols] = jnp.where(inside, rt, rt_ref[pl.ds(q0, span), cols])

    for_doc(meta, d, cross, run)


def attend_doc_back(
    meta, d, cross, er_ref, lim_ref, q_ref, k_ref, v_ref, e_ref, mixed_ref, rt_ref, dm_ref,
    dq_ref, dk_ref, dv_ref,
):
    pairs = q_ref.shape[1] // 128
    masks = half_masks()

    def run(q0, k0, span, width, low, high, ks, ke, fast):
        row = q0 + lax.broadcasted_iota(jnp.int32, (span, 128), 0)
        inside = (row >= low) & (row < high)
        ones = jnp.ones((width, 128), bf16)
        if not fast:
            bias = make_bias(er_ref, lim_ref, ks, ke, q0, k0, span, width)
        for p in range(pairs):
            cols = slice(128 * p, 128 * p + 128)
            queries = q_ref[pl.ds(q0, span), cols]
            keys = k_ref[pl.ds(k0, width), cols]
            values = v_ref[pl.ds(k0, width), cols]
            mixed = mixed_ref[pl.ds(q0, span), cols].astype(f32)
            grad = dm_ref[pl.ds(q0, span), cols].astype(f32) * rt_ref[pl.ds(q0, span), cols]
            grad = jnp.where(inside, grad, 0.0)
            low_grad = grad.astype(bf16)
            left = lanes([low_grad, (-(grad * mixed)).astype(bf16)])
            dq = dk = dv = None
            for a in range(2):
                right = lanes([values * masks[a], ones * masks[a]])
                masked_keys = keys * masks[a]
                delta = dot_nt(left, right)
                e = e_ref[0, 2 * p + a] if fast else raised(queries, masked_keys, bias)
                ds = (e.astype(f32) * delta).astype(bf16)
                dq_a = dot(ds, masked_keys)
                dk_a = dot_tn(ds, queries * masks[a])
                dv_a = dot_tn(e, low_grad * masks[a])
                dq = dq_a if dq is None else dq + dq_a
                dk = dk_a if dk is None else dk + dk_a
                dv = dv_a if dv is None else dv + dv_a
            dq_ref[pl.ds(q0, span), cols] += dq * (HEAD_DIM**-0.5)
            dk_ref[pl.ds(k0, width), cols] += dk
            dv_ref[pl.ds(k0, width), cols] += dv

    for_doc(meta, d, cross, run)


def spread_limits(limit_ref, lim_ref):
    lim_ref[...] = jnp.transpose(jnp.broadcast_to(limit_ref[...], (128, SEQ)))


def self_first(
    meta, xq_ref, xc_ref, er_ref, limit_ref, norms_ref, w0_ref, w1_ref,
    nq_ref, nc_ref, q_ref, k_ref, v_ref, mixed_ref, rt_ref, e_ref, lim_ref,
):
    d = pl.program_id(0)

    @pl.when(d == 0)
    def _():
        spread_limits(limit_ref, lim_ref)
        wq = lanes([w_query(w0_ref), w_query(w1_ref)])
        wkv = lanes([w_key(w0_ref), w_key(w1_ref), w_value(w0_ref), w_value(w1_ref)])

        def tile(i, carry):
            rows = rows_of(i)
            nq = layer_norm(xq_ref[rows, :].astype(f32), norms_ref[0:1], norms_ref[1:2]).astype(bf16)
            nc = layer_norm(xc_ref[rows, :].astype(f32), norms_ref[2:3], norms_ref[3:4]).astype(bf16)
            nq_ref[rows, :] = nq
            nc_ref[rows, :] = nc
            q_ref[rows, :] = (dot(nq, wq) * (HEAD_DIM**-0.5)).astype(bf16)
            kv = dot(nc, wkv).astype(bf16)
            k_ref[rows, :] = kv[:, :256]
            v_ref[rows, :] = kv[:, 256:]
            return carry

        lax.fori_loop(0, TILES, tile, 0)

    attend_doc(meta, d, False, er_ref, lim_ref, q_ref, k_ref, v_ref, e_ref, mixed_ref, rt_ref)


def self_second(
    meta, xq_ref, nq_ref, nc_ref, er_ref, limit_ref, norms_ref, w0_ref, w1_ref, w2_ref, w3_ref,
    mixed_first_ref,
    q_ref, k_ref, v_ref, mixed_ref, rt_ref, e_ref, second_ref, ncross_ref, lim_ref,
):
    d = pl.program_id(0)

    @pl.when(d == 0)
    def _():
        spread_limits(limit_ref, lim_ref)
        wq = lanes([w_query(w2_ref), w_query(w3_ref)])
        wkv = lanes([w_key(w2_ref), w_key(w3_ref), w_value(w2_ref), w_value(w3_ref)])

        def tile(i, carry):
            rows = rows_of(i)
            q_ref[rows, :] = (dot(nq_ref[rows, :], wq) * (HEAD_DIM**-0.5)).astype(bf16)
            kv = dot(nc_ref[rows, :], wkv).astype(bf16)
            k_ref[rows, :] = kv[:, :256]
            v_ref[rows, :] = kv[:, 256:]
            return carry

        lax.fori_loop(0, TILES, tile, 0)

    attend_doc(meta, d, False, er_ref, lim_ref, q_ref, k_ref, v_ref, e_ref, mixed_ref, rt_ref)

    @pl.when(d == DOCS - 1)
    def _():
        out_first = jnp.concatenate([w_out(w0_ref), w_out(w1_ref)], axis=0)
        out_second = jnp.concatenate([w_out(w2_ref), w_out(w3_ref)], axis=0)

        def tile(i, carry):
            rows = rows_of(i)
            branch = dot(mixed_first_ref[rows, :], out_first) + dot(mixed_ref[rows, :], out_second)
            second = xq_ref[rows, :].astype(f32) + branch
            second_ref[rows, :] = second
            ncross_ref[rows, :] = layer_norm(second, norms_ref[4:5], norms_ref[5:6]).astype(bf16)
            return carry

        lax.fori_loop(0, TILES, tile, 0)


def cross_forward(
    meta, second_ref, ncross_ref, memory_ref, norms_ref, w0_ref, w1_ref, w2_ref, w3_ref,
    q_ref, k_ref, v_ref, mixed_ref, rt_ref, e_ref, third_ref, nffn_ref,
):
    d = pl.program_id(0)
    weights = (w0_ref, w1_ref, w2_ref, w3_ref)

    @pl.when(d == 0)
    def _():
        wq = lanes([w_query(w) for w in weights])
        wk = lanes([w_key(w) for w in weights])
        wv = lanes([w_value(w) for w in weights])

        def tile(i, carry):
            rows = rows_of(i)
            memory = memory_ref[rows, :]
            q_ref[rows, :] = (dot(ncross_ref[rows, :], wq) * (HEAD_DIM**-0.5)).astype(bf16)
            k_ref[rows, :] = dot(memory, wk).astype(bf16)
            v_ref[rows, :] = dot(memory, wv).astype(bf16)
            return carry

        lax.fori_loop(0, TILES, tile, 0)

    attend_doc(meta, d, True, None, None, q_ref, k_ref, v_ref, e_ref, mixed_ref, rt_ref)

    @pl.when(d == DOCS - 1)
    def _():
        out_first = jnp.concatenate([w_out(w0_ref), w_out(w1_ref)], axis=0)
        out_second = jnp.concatenate([w_out(w2_ref), w_out(w3_ref)], axis=0)

        def tile(i, carry):
            rows = rows_of(i)
            mixed = mixed_ref[rows, :]
            branch = dot(mixed[:, :256], out_first) + dot(mixed[:, 256:], out_second)
            third = second_ref[rows, :] + branch
            third_ref[rows, :] = third
            nffn_ref[rows, :] = layer_norm(third, norms_ref[6:7], norms_ref[7:8]).astype(bf16)
            return carry

        lax.fori_loop(0, TILES, tile, 0)


def ffn_both(
    meta, third_ref, nffn_ref, cot_ref, norms_ref, w0_ref, w1_ref, w2_ref, w3_ref,
    out_ref, g3_ref, gln_ref, own_ref, other_ref, hidden_ref, before_ref,
):
    i = pl.program_id(0)
    rows = rows_of(i)
    nffn = nffn_ref[rows, :]
    cot = cot_ref[rows, :]
    outs = []
    grads = []
    for g, w_ref in enumerate((w0_ref, w1_ref, w2_ref, w3_ref)):
        w_in = w_ref[0:512, :]
        w_out_rows = w_ref[512:1024, :]
        x = dot(nffn, w_in)
        square = x * x
        t = jnp.tanh(gelu_root * (x + gelu_cube * (square * x)))
        half = 0.5 + 0.5 * t
        hidden = (x * half).astype(bf16)
        slope = half + x * (0.5 - 0.5 * t * t) * (gelu_root + (3.0 * gelu_root * gelu_cube) * square)
        grad_before = (dot_nt(cot, w_out_rows) * slope).astype(bf16)
        outs.append(dot(hidden, w_out_rows))
        grads.append(dot_nt(grad_before, w_in))
        if g < 2:
            hidden_ref[rows, 512 * g : 512 * g + 512] = hidden
            before_ref[rows, 512 * g : 512 * g + 512] = grad_before
    third = third_ref[rows, :]
    out_ref[rows, :] = (third + ((outs[0] + outs[1]) + (outs[2] + outs[3]))).astype(bf16)
    grad_normed = (grads[0] + grads[1]) + (grads[2] + grads[3])
    grad_norm, grad_gain, grad_shift = norm_backward(third, norms_ref[6:7], grad_normed)
    g3_ref[rows, :] = cot.astype(f32) + grad_norm

    @pl.when(i == 0)
    def _():
        gln_ref[0:1, :] = grad_gain
        gln_ref[1:2, :] = grad_shift

    @pl.when(i > 0)
    def _():
        gln_ref[0:1, :] += grad_gain
        gln_ref[1:2, :] += grad_shift

    @pl.when(i == TILES - 1)
    def _():
        nffn_all = nffn_ref[...]
        cot_all = cot_ref[...]
        own_ref[0:512, :] = dot_tn(nffn_all, before_ref[:, 0:512])
        own_ref[512:1024, :] = dot_tn(hidden_ref[:, 0:512], cot_all)
        other_ref[0:512, :] = dot_tn(nffn_all, before_ref[:, 512:1024]).astype(bf16)
        other_ref[512:1024, :] = dot_tn(hidden_ref[:, 512:1024], cot_all).astype(bf16)


def back_start(g_ref, mixed_ref, w_refs, dm_ref, dq_ref, dk_ref, dv_ref):
    out_rows = jnp.concatenate([w_out(w) for w in w_refs], axis=0)

    def tile(i, carry):
        rows = rows_of(i)
        dm_ref[rows, :] = dot_nt(g_ref[rows, :].astype(bf16), out_rows).astype(bf16)
        zeros = jnp.zeros((TILE, 256), f32)
        dq_ref[rows, :] = zeros
        dk_ref[rows, :] = zeros
        dv_ref[rows, :] = zeros
        return carry

    lax.fori_loop(0, TILES, tile, 0)


def attention_back_first(
    cross, meta, g_ref, nq_ref, nkv_ref, er_ref, limit_ref, w0_ref, w1_ref,
    q_ref, k_ref, v_ref, mixed_ref, rt_ref, e_ref,
    dq_ref, dk_ref, dv_ref, own_ref, other_ref,
    lim_ref, dm_ref, dqs_ref, dks_ref, dvs_ref,
):
    d = pl.program_id(0)

    @pl.when(d == 0)
    def _():
        if not cross:
            spread_limits(limit_ref, lim_ref)
        back_start(g_ref, mixed_ref, (w0_ref, w1_ref), dm_ref, dqs_ref, dks_ref, dvs_ref)

    attend_doc_back(
        meta, d, cross, None if cross else er_ref, lim_ref, q_ref, k_ref, v_ref, e_ref, mixed_ref,
        rt_ref, dm_ref, dqs_ref, dks_ref, dvs_ref,
    )

    @pl.when(d == DOCS - 1)
    def _():
        dq_ref[...] = dqs_ref[...].astype(bf16)
        dk_ref[...] = dks_ref[...].astype(bf16)
        dv_ref[...] = dvs_ref[...].astype(bf16)
        nq = nq_ref[...]
        nkv = nkv_ref[...]
        for n, part in enumerate(
            (dot_tn(nq, dq_ref[...]), dot_tn(nkv, dk_ref[...]), dot_tn(nkv, dv_ref[...]))
        ):
            own_ref[512 * n : 512 * n + 512, :] = part[:, :128]
            other_ref[512 * n : 512 * n + 512, :] = part[:, 128:].astype(bf16)
        part = dot_tn(mixed_ref[...], g_ref[...].astype(bf16))
        for j in range(4):
            own_ref[1536 + 128 * j : 1664 + 128 * j, :] = part[:128, 128 * j : 128 * j + 128]
            other_ref[1536 + 128 * j : 1664 + 128 * j, :] = part[
                128:, 128 * j : 128 * j + 128
            ].astype(bf16)


def back_second_docs(
    cross, meta, g_ref, er_ref, limit_ref, w_refs, q_ref, k_ref, v_ref, mixed_ref, rt_ref, e_ref,
    lim_ref, dm_ref, dqs_ref, dks_ref, dvs_ref,
):
    d = pl.program_id(0)

    @pl.when(d == 0)
    def _():
        if not cross:
            spread_limits(limit_ref, lim_ref)
        back_start(g_ref, mixed_ref, w_refs, dm_ref, dqs_ref, dks_ref, dvs_ref)

    attend_doc_back(
        meta, d, cross, None if cross else er_ref, lim_ref, q_ref, k_ref, v_ref, e_ref, mixed_ref,
        rt_ref, dm_ref, dqs_ref, dks_ref, dvs_ref,
    )
    return d


def stream_grads(rows, first, second, firsts, seconds):
    dq, dk, dv = first
    dq2, dk2, dv2 = (ref[rows, :].astype(bf16) for ref in second)
    w0, w1 = firsts
    w2, w3 = seconds
    grad_q = dot_nt(dq[rows, :], lanes([w_query(w0), w_query(w1)])) + dot_nt(
        dq2, lanes([w_query(w2), w_query(w3)])
    )
    kv = lanes([dk[rows, :], dv[rows, :]])
    kv2 = lanes([dk2, dv2])
    grad_kv = dot_nt(kv, lanes([w_key(w0), w_key(w1), w_value(w0), w_value(w1)])) + dot_nt(
        kv2, lanes([w_key(w2), w_key(w3), w_value(w2), w_value(w3)])
    )
    return grad_q, grad_kv


def cross_back_second(
    meta, g_ref, second_ref, norms_ref, w0_ref, w1_ref, w2_ref, w3_ref,
    dq_ref, dk_ref, dv_ref, q_ref, k_ref, v_ref, mixed_ref, rt_ref, e_ref,
    g2_ref, gmem_ref, gln_ref,
    dm_ref, dqs_ref, dks_ref, dvs_ref,
):
    d = back_second_docs(
        True, meta, g_ref, None, None, (w2_ref, w3_ref), q_ref, k_ref, v_ref, mixed_ref, rt_ref,
        e_ref, None, dm_ref, dqs_ref, dks_ref, dvs_ref,
    )

    @pl.when(d == DOCS - 1)
    def _():
        gln_ref[...] = jnp.zeros_like(gln_ref)

        def tile(i, carry):
            rows = rows_of(i)
            grad_q, grad_kv = stream_grads(
                rows,
                (dq_ref, dk_ref, dv_ref),
                (dqs_ref, dks_ref, dvs_ref),
                (w0_ref, w1_ref),
                (w2_ref, w3_ref),
            )
            gmem_ref[rows, :] = grad_kv.astype(bf16)
            grad_norm, grad_gain, grad_shift = norm_backward(
                second_ref[rows, :], norms_ref[4:5], grad_q
            )
            g2_ref[rows, :] = g_ref[rows, :] + grad_norm
            gln_ref[0:1, :] += grad_gain
            gln_ref[1:2, :] += grad_shift
            return carry

        lax.fori_loop(0, TILES, tile, 0)


def self_back_second(
    meta, g_ref, xq_ref, xc_ref, er_ref, limit_ref, norms_ref, w0_ref, w1_ref, w2_ref, w3_ref,
    dq_ref, dk_ref, dv_ref, q_ref, k_ref, v_ref, mixed_ref, rt_ref, e_ref,
    gq_ref, gc_ref, gln_ref,
    lim_ref, dm_ref, dqs_ref, dks_ref, dvs_ref,
):
    d = back_second_docs(
        False, meta, g_ref, er_ref, limit_ref, (w2_ref, w3_ref), q_ref, k_ref, v_ref, mixed_ref,
        rt_ref, e_ref, lim_ref, dm_ref, dqs_ref, dks_ref, dvs_ref,
    )

    @pl.when(d == DOCS - 1)
    def _():
        gln_ref[...] = jnp.zeros_like(gln_ref)

        def tile(i, carry):
            rows = rows_of(i)
            grad_q, grad_kv = stream_grads(
                rows,
                (dq_ref, dk_ref, dv_ref),
                (dqs_ref, dks_ref, dvs_ref),
                (w0_ref, w1_ref),
                (w2_ref, w3_ref),
            )
            grad_norm, grad_gain, grad_shift = norm_backward(
                xq_ref[rows, :].astype(f32), norms_ref[0:1], grad_q
            )
            gq_ref[rows, :] = (g_ref[rows, :] + grad_norm).astype(bf16)
            gln_ref[0:1, :] += grad_gain
            gln_ref[1:2, :] += grad_shift
            grad_norm, grad_gain, grad_shift = norm_backward(
                xc_ref[rows, :].astype(f32), norms_ref[2:3], grad_kv
            )
            gc_ref[rows, :] = grad_norm.astype(bf16)
            gln_ref[2:3, :] += grad_gain
            gln_ref[3:4, :] += grad_shift
            return carry

        lax.fori_loop(0, TILES, tile, 0)


def place_rows(meta, *refs):
    count = len(refs) // 3
    mine = pl.program_id(0) == meta[0]
    for n in range(count):
        own, other, out = refs[n], refs[count + n], refs[2 * count + n]

        @pl.when(mine)
        def _():
            out[...] = own[...].astype(out.dtype)

        @pl.when(jnp.logical_not(mine))
        def _():
            out[...] = other[...].astype(out.dtype)


def whole(shape):
    zeros = (0,) * len(shape)
    return pl.BlockSpec(shape, lambda d, meta: zeros)


def own_row(width):
    return pl.BlockSpec((SEQ, width), lambda d, meta: (meta[0], 0))


def columns(width, n):
    return pl.BlockSpec((SEQ, width), lambda d, meta: (0, n))


def raised_spec(heads, n):
    return pl.BlockSpec((1, heads, FAST_Q, FAST_K), lambda d, meta: (d, n, 0, 0))


def call(kernel, name, grid, operands, outs, scratch, flops):
    moved = sum(x.size * x.dtype.itemsize for x, _ in operands[1:])
    return pl.pallas_call(
        kernel,
        name=name,
        grid_spec=pltpu.PrefetchScalarGridSpec(
            num_scalar_prefetch=1,
            grid=(grid,),
            in_specs=[spec for _, spec in operands[1:]],
            out_specs=[spec for _, _, spec in outs],
            scratch_shapes=scratch,
        ),
        out_shape=[jax.ShapeDtypeStruct(shape, dtype) for shape, dtype, _ in outs],
        compiler_params=pltpu.CompilerParams(
            dimension_semantics=("arbitrary",), vmem_limit_bytes=56 * 1024 * 1024
        ),
        cost_estimate=pl.CostEstimate(
            flops=int(flops), bytes_accessed=int(moved), transcendentals=0
        ),
    )(*[x for x, _ in operands])


def full(x):
    return (x, whole(x.shape))


def pack_attention(query, key, value, out):
    blocks = [out[:, 128 * j : 128 * j + 128] for j in range(4)]
    return jnp.concatenate([query, key, value] + blocks, axis=0)


def unpack_attention(packed):
    blocks = [packed[1536 + 128 * j : 1664 + 128 * j] for j in range(4)]
    return packed[0:512], packed[512:1024], packed[1024:1536], jnp.concatenate(blocks, axis=1)


def shards(
    query_stream,
    content_stream,
    memory,
    segment_ids,
    source_segments,
    context_rank,
    context_limit,
    padding,
    ln_query_gain,
    ln_query_bias,
    ln_content_gain,
    ln_content_bias,
    self_query,
    self_key,
    self_value,
    self_out,
    ln_cross_gain,
    ln_cross_bias,
    cross_query,
    cross_key,
    cross_value,
    cross_out,
    ln_ffn_gain,
    ln_ffn_bias,
    ffn_in,
    ffn_out,
    cotangent,
):
    core = lax.axis_index("heads") % 2

    def to_core(x):
        return lax.ppermute(x, "heads", [(h, h ^ 1) for h in range(4)])

    def to_chip(x):
        return lax.ppermute(x, "heads", [(h, h ^ 2) for h in range(4)])

    ws0 = pack_attention(self_query, self_key, self_value, self_out)
    wc0 = pack_attention(cross_query, cross_key, cross_value, cross_out)
    wf0 = jnp.concatenate([ffn_in, ffn_out], axis=0)
    ws1 = to_core(ws0)
    ws2 = to_chip(ws0)
    wc0, ws2 = lax.optimization_barrier((wc0, ws2))
    ws3 = to_core(ws2)
    wc1 = to_core(wc0)
    wc2 = to_chip(wc0)
    wf0, wc2 = lax.optimization_barrier((wf0, wc2))
    wc3 = to_core(wc2)
    wf1 = to_core(wf0)
    wf2 = to_chip(wf0)
    wf3 = to_core(wf2)

    seg = lax.dynamic_slice_in_dim(segment_ids, core * SEQ, SEQ)
    src = lax.dynamic_slice_in_dim(source_segments, core * SEQ, SEQ)
    docs = jnp.arange(1, DOCS, dtype=jnp.int32)
    cuts = jnp.sum(
        (jnp.stack([seg, src])[:, None, :] < docs[None, :, None]).astype(jnp.int32), axis=2
    )
    zero = jnp.zeros((1,), jnp.int32)
    last = jnp.full((1,), SEQ, jnp.int32)
    meta = jnp.concatenate(
        [core.astype(jnp.int32)[None], zero, cuts[0], cuts[0], last, zero, cuts[1], cuts[1], last]
    )
    rank = jnp.where(padding != 0, hidden_rank, context_rank.astype(f32))
    rank = lax.dynamic_slice_in_dim(rank, core * SEQ, SEQ).reshape(1, SEQ)
    limit = lax.dynamic_slice_in_dim(context_limit, core * SEQ, SEQ).astype(f32).reshape(1, SEQ)
    norms = jnp.stack(
        [
            ln_query_gain,
            ln_query_bias,
            ln_content_gain,
            ln_content_bias,
            ln_cross_gain,
            ln_cross_bias,
            ln_ffn_gain,
            ln_ffn_bias,
        ]
    )
    meta_in = (meta, None)
    xq = (query_stream, own_row(D))
    xc = (content_stream, own_row(D))
    mem = (memory, own_row(D))
    cot = (cotangent, own_row(D))

    def heads_out(width, heads):
        return [
            ((SEQ, width), bf16, whole((SEQ, width))),
            ((SEQ, width), bf16, whole((SEQ, width))),
            ((SEQ, width), bf16, whole((SEQ, width))),
            ((SEQ, width), bf16, whole((SEQ, width))),
            ((SEQ, width), f32, whole((SEQ, width))),
            ((DOCS, heads, FAST_Q, FAST_K), bf16, raised_spec(heads, 0)),
        ]

    def stream_out(dtype):
        return ((SEQ, D), dtype, whole((SEQ, D)))

    limits = pltpu.VMEM((SEQ, 128), f32)
    pair_flops = 2 * SEQ * D * 768 + 2 * 2 * 4 * DOCS * FAST_Q * FAST_K * 256

    nq, nc, *first = call(
        self_first,
        "self_first",
        DOCS,
        [meta_in, xq, xc, full(rank), full(limit), full(norms), full(ws0), full(ws1)],
        [stream_out(bf16), stream_out(bf16)] + heads_out(256, 4),
        [limits],
        pair_flops,
    )
    *second_heads, second, ncross = call(
        self_second,
        "self_second",
        DOCS,
        [meta_in, xq, full(nq), full(nc), full(rank), full(limit), full(norms)]
        + [full(w) for w in (ws0, ws1, ws2, ws3)]
        + [full(first[3])],
        heads_out(256, 4) + [stream_out(f32), stream_out(bf16)],
        [limits],
        pair_flops + 2 * SEQ * D * D,
    )
    *cross_heads, third, nffn = call(
        cross_forward,
        "cross_forward",
        DOCS,
        [meta_in, full(second), full(ncross), mem, full(norms)]
        + [full(w) for w in (wc0, wc1, wc2, wc3)],
        heads_out(512, 8) + [stream_out(f32), stream_out(bf16)],
        [],
        2 * pair_flops + 2 * SEQ * D * D,
    )
    grads_ln = ((8, D), f32, whole((8, D)))
    output, g3, gln_ffn, ffn_own, ffn_other = call(
        ffn_both,
        "ffn_both",
        TILES,
        [meta_in, full(third), full(nffn), cot, full(norms)]
        + [full(w) for w in (wf0, wf1, wf2, wf3)],
        [
            stream_out(bf16),
            stream_out(f32),
            grads_ln,
            ((1024, D), f32, whole((1024, D))),
            ((1024, D), bf16, whole((1024, D))),
        ],
        [pltpu.VMEM((SEQ, 1024), bf16), pltpu.VMEM((SEQ, 1024), bf16)],
        12 * SEQ * D * 2048,
    )

    def total_over_rows(own, other):
        both = (own + to_core(other).astype(f32)).astype(bf16)
        return lax.psum(both, "rows")

    grad_ffn = total_over_rows(ffn_own, ffn_other)

    back_scratch = [pltpu.VMEM((SEQ, 256), bf16)] + [pltpu.VMEM((SEQ, 256), f32)] * 3
    pair_out = ((SEQ, 256), bf16, whole((SEQ, 256)))
    packed_outs = [
        ((2048, 128), f32, whole((2048, 128))),
        ((2048, 128), bf16, whole((2048, 128))),
    ]
    back_flops = 2 * SEQ * D * 256 + 4 * 2 * 4 * DOCS * FAST_Q * FAST_K * 256

    def head_inputs(arrays, n):
        q, k, v, mixed, rt, e = arrays
        return [(x, columns(256, n)) for x in (q, k, v, mixed, rt)] + [(e, raised_spec(4, n))]

    *cross_grads, cross_own, cross_other = call(
        functools.partial(attention_back_first, True),
        "cross_back_first",
        DOCS,
        [meta_in, full(g3), full(ncross), mem, full(rank), full(limit), full(wc0), full(wc1)]
        + head_inputs(cross_heads, 0),
        [pair_out] * 3 + packed_outs,
        [limits] + back_scratch,
        back_flops + 2 * SEQ * D * 1024,
    )
    g2, grad_mem, gln_cross = call(
        cross_back_second,
        "cross_back_second",
        DOCS,
        [meta_in, full(g3), full(second), full(norms)]
        + [full(w) for w in (wc0, wc1, wc2, wc3)]
        + [full(x) for x in cross_grads]
        + head_inputs(cross_heads, 1),
        [stream_out(f32), stream_out(bf16), grads_ln],
        back_scratch,
        back_flops + 2 * SEQ * D * 1536,
    )
    cross_own, grad_ffn = lax.optimization_barrier((cross_own, grad_ffn))
    grad_cross = total_over_rows(cross_own, cross_other)

    *self_grads, self_own, self_other = call(
        functools.partial(attention_back_first, False),
        "self_back_first",
        DOCS,
        [meta_in, full(g2), full(nq), full(nc), full(rank), full(limit), full(ws0), full(ws1)]
        + head_inputs(first, 0),
        [pair_out] * 3 + packed_outs,
        [limits] + back_scratch,
        back_flops + 2 * SEQ * D * 1024,
    )
    self_own, grad_cross = lax.optimization_barrier((self_own, grad_cross))
    grad_self = total_over_rows(self_own, self_other)
    gq, gc, gln_self = call(
        self_back_second,
        "self_back_second",
        DOCS,
        [meta_in, full(g2), xq, xc, full(rank), full(limit), full(norms)]
        + [full(w) for w in (ws0, ws1, ws2, ws3)]
        + [full(x) for x in self_grads]
        + head_inputs(second_heads, 0),
        [stream_out(bf16), stream_out(bf16), grads_ln],
        [limits] + back_scratch,
        back_flops + 2 * SEQ * D * 1536,
    )

    gln = jnp.concatenate([gln_self[0:4], gln_cross[0:2], gln_ffn[0:2]], axis=0)
    gln = lax.psum(gln + to_core(gln), "rows")

    def both_rows(arrays, dtypes, name):
        count = len(arrays)
        others = [to_core(x) for x in arrays]
        one = pl.BlockSpec((TILE, D), lambda r, i, meta: (i, 0))
        placed = pl.BlockSpec((TILE, D), lambda r, i, meta: (r * TILES + i, 0))
        return pl.pallas_call(
            place_rows,
            name=name,
            grid_spec=pltpu.PrefetchScalarGridSpec(
                num_scalar_prefetch=1,
                grid=(2, TILES),
                in_specs=[one] * (2 * count),
                out_specs=[placed] * count,
            ),
            out_shape=[jax.ShapeDtypeStruct((2 * SEQ, D), t) for t in dtypes],
        )(meta, *arrays, *others)

    out_both, grad_mem_both = both_rows([output, grad_mem], [bf16, f32], "place_early")
    gq_both, gc_both = both_rows([gq, gc], [f32, f32], "place_late")

    grad_self_parts = unpack_attention(grad_self.astype(f32))
    grad_cross_parts = unpack_attention(grad_cross.astype(f32))
    grad_ffn = grad_ffn.astype(f32)
    return (
        out_both,
        gq_both,
        gc_both,
        grad_mem_both,
        gln[0],
        gln[1],
        gln[2],
        gln[3],
        *grad_self_parts,
        gln[4],
        gln[5],
        *grad_cross_parts,
        gln[6],
        gln[7],
        grad_ffn[0:512],
        grad_ffn[512:1024],
    )


def solution(mesh):
    assert mesh.shape["heads"] == 4
    row_spec = P("rows", None)
    flat = P("rows")
    by_column = P(None, "heads")
    by_row = P("heads", None)
    attention = (by_column, by_column, by_column, by_row)
    in_specs = (
        (row_spec,) * 3
        + (flat,) * 5
        + (P(),) * 4
        + attention
        + (P(),) * 2
        + attention
        + (P(),) * 2
        + (by_column, by_row, row_spec)
    )
    out_specs = (
        (row_spec,) * 4
        + (P(),) * 4
        + attention
        + (P(),) * 2
        + attention
        + (P(),) * 2
        + (by_column, by_row)
    )
    return jax.shard_map(shards, mesh=mesh, in_specs=in_specs, out_specs=out_specs, check_vma=False)
```

```python
import functools

import jax
import jax.numpy as jnp
from jax import lax
from jax.experimental import pallas as pl
from jax.experimental.pallas import tpu as pltpu
from jax.sharding import PartitionSpec as P

HEAD_DIM = 64
SEQ = 1024
DOCS = 8
D = 512
TILE = 256
TILES = SEQ // TILE
FAST_Q = 208
FAST_K = 256
LONG_Q = 128
LONG_K = 640

norm_eps = 1e-05
masked_score = -1e30
hidden_rank = 1e6
gelu_root = 0.7978845608028654
gelu_cube = 0.044715

f32 = jnp.float32
bf16 = jnp.bfloat16


def dot(a, b):
    return lax.dot_general(a, b, (((1,), (0,)), ((), ())), preferred_element_type=f32)


def dot_nt(a, b):
    return lax.dot_general(a, b, (((1,), (1,)), ((), ())), preferred_element_type=f32)


def dot_tn(a, b):
    return lax.dot_general(a, b, (((0,), (0,)), ((), ())), preferred_element_type=f32)


def lanes(parts):
    return jnp.concatenate(parts, axis=1)


def layer_norm(values, gain, shift):
    centre = values - jnp.mean(values, axis=-1, keepdims=True)
    spread = jnp.mean(centre * centre, axis=-1, keepdims=True)
    return centre * lax.rsqrt(spread + norm_eps) * gain + shift


def norm_backward(values, gain, grad):
    centre = values - jnp.mean(values, axis=-1, keepdims=True)
    spread = jnp.mean(centre * centre, axis=-1, keepdims=True)
    scale = lax.rsqrt(spread + norm_eps)
    xhat = centre * scale
    eg = grad * gain
    mean_eg = jnp.mean(eg, axis=-1, keepdims=True)
    mean_egx = jnp.mean(eg * xhat, axis=-1, keepdims=True)
    grad_gain = jnp.sum(grad * xhat, axis=0, keepdims=True)
    grad_shift = jnp.sum(grad, axis=0, keepdims=True)
    return scale * (eg - mean_eg - xhat * mean_egx), grad_gain, grad_shift


def rows_of(i, size=TILE):
    return pl.ds(pl.multiple_of(i * size, size), size)


def w_query(ref):
    return ref[0:512, :]


def w_key(ref):
    return ref[512:1024, :]


def w_value(ref):
    return ref[1024:1536, :]


def w_out(ref):
    return lanes([ref[1536 + 128 * j : 1664 + 128 * j, :] for j in range(4)])


def half_masks():
    place = lax.broadcasted_iota(jnp.int32, (1, 128), 1)
    low = jnp.where(place < HEAD_DIM, 1.0, 0.0).astype(f32)
    return (low.astype(bf16), (1.0 - low).astype(bf16))


def doc_bounds(meta, d, source):
    base = 17 if source else 1
    return meta[base + d], meta[base + 8 + d]


def window_of(first, limit):
    return pl.multiple_of(jnp.minimum((first // 16) * 16, limit), 16)


def key_values(er_ref, ks, ke, k0, width):
    if er_ref is None:
        place = k0 + lax.broadcasted_iota(jnp.int32, (1, width), 1)
        return jnp.where((place >= ks) & (place < ke), 0.0, masked_score)
    ranks = jnp.broadcast_to(er_ref[...], (8, SEQ))
    ranks = pltpu.roll(ranks, lax.rem(SEQ - k0, SEQ), 1)[0:1, 0:width]
    place = k0 + lax.broadcasted_iota(jnp.int32, (1, width), 1)
    ranks = jnp.where((place < ks + 2) & (ranks < hidden_rank), -1.0, ranks)
    return jnp.where((place >= ks) & (place < ke), ranks, hidden_rank)


def make_bias(er_ref, lim_ref, ks, ke, q0, k0, span, width):
    keys = key_values(er_ref, ks, ke, k0, width)
    if er_ref is None:
        return keys
    limits = lim_ref[pl.ds(q0, span), :]
    limits = lanes([limits] * (width // 128))
    row = q0 + lax.broadcasted_iota(jnp.int32, (span, width), 0)
    column = k0 + lax.broadcasted_iota(jnp.int32, (span, width), 1)
    return jnp.where((keys < limits) & (row != column), 0.0, masked_score)


def raised(queries, keys, bias):
    scores = dot_nt(queries, keys) + bias
    return jnp.exp(scores - jnp.max(scores, axis=1, keepdims=True)).astype(bf16)


def for_doc(meta, d, cross, run):
    ts, te = doc_bounds(meta, d, False)
    ks, ke = doc_bounds(meta, d, cross)
    q0 = window_of(ts, SEQ - FAST_Q)
    k0 = window_of(ks, SEQ - FAST_K)
    fast = (te - q0 <= FAST_Q) & (ke - k0 <= FAST_K)

    @pl.when(fast)
    def _():
        run(q0, k0, FAST_Q, FAST_K, ts, te, ks, ke, True)

    @pl.when(jnp.logical_not(fast))
    def _():
        base = (ts // 16) * 16
        k_long = window_of(ks, SEQ - LONG_K)

        def chunk(i, carry):
            lower = base + i * LONG_Q
            q_long = pl.multiple_of(jnp.minimum(lower, SEQ - LONG_Q), 16)
            run(
                q_long,
                k_long,
                LONG_Q,
                LONG_K,
                jnp.maximum(ts, lower),
                jnp.minimum(te, lower + LONG_Q),
                ks,
                ke,
                False,
            )
            return carry

        lax.fori_loop(0, (te - base + LONG_Q - 1) // LONG_Q, chunk, 0)


def attend_doc(meta, d, cross, er_ref, lim_ref, q_ref, k_ref, v_ref, e_ref, mixed_ref, rt_ref):
    pairs = q_ref.shape[1] // 128
    masks = half_masks()

    def run(q0, k0, span, width, low, high, ks, ke, fast):
        bias = make_bias(er_ref, lim_ref, ks, ke, q0, k0, span, width)
        row = q0 + lax.broadcasted_iota(jnp.int32, (span, 128), 0)
        inside = (row >= low) & (row < high)
        ones = jnp.ones((width, 128), bf16)
        for p in range(pairs):
            cols = slice(128 * p, 128 * p + 128)
            queries = q_ref[pl.ds(q0, span), cols]
            keys = k_ref[pl.ds(k0, width), cols]
            values = v_ref[pl.ds(k0, width), cols]
            total = None
            for a in range(2):
                e = raised(queries, keys * masks[a], bias)
                if fast:
                    e_ref[0, 2 * p + a] = e
                part = dot(e, lanes([values * masks[a], ones * masks[a]]))
                total = part if total is None else total + part
            rt = 1.0 / total[:, 128:]
            mixed = total[:, :128] * rt
            old = mixed_ref[pl.ds(q0, span), cols].astype(f32)
            mixed_ref[pl.ds(q0, span), cols] = jnp.where(inside, mixed, old).astype(bf16)
            rt_ref[pl.ds(q0, span), cols] = jnp.where(inside, rt, rt_ref[pl.ds(q0, span), cols])

    for_doc(meta, d, cross, run)


def attend_doc_back(
    meta, d, cross, er_ref, lim_ref, q_ref, k_ref, v_ref, e_ref, mixed_ref, rt_ref, dm_ref,
    dq_ref, dk_ref, dv_ref,
):
    pairs = q_ref.shape[1] // 128
    masks = half_masks()

    def run(q0, k0, span, width, low, high, ks, ke, fast):
        row = q0 + lax.broadcasted_iota(jnp.int32, (span, 128), 0)
        inside = (row >= low) & (row < high)
        ones = jnp.ones((width, 128), bf16)
        if not fast:
            bias = make_bias(er_ref, lim_ref, ks, ke, q0, k0, span, width)
        for p in range(pairs):
            cols = slice(128 * p, 128 * p + 128)
            queries = q_ref[pl.ds(q0, span), cols]
            keys = k_ref[pl.ds(k0, width), cols]
            values = v_ref[pl.ds(k0, width), cols]
            mixed = mixed_ref[pl.ds(q0, span), cols].astype(f32)
            grad = dm_ref[pl.ds(q0, span), cols].astype(f32) * rt_ref[pl.ds(q0, span), cols]
            grad = jnp.where(inside, grad, 0.0)
            low_grad = grad.astype(bf16)
            left = lanes([low_grad, (-(grad * mixed)).astype(bf16)])
            dq = dk = dv = None
            for a in range(2):
                right = lanes([values * masks[a], ones * masks[a]])
                masked_keys = keys * masks[a]
                delta = dot_nt(left, right)
                e = e_ref[0, 2 * p + a] if fast else raised(queries, masked_keys, bias)
                ds = (e.astype(f32) * delta).astype(bf16)
                dq_a = dot(ds, masked_keys)
                dk_a = dot_tn(ds, queries * masks[a])
                dv_a = dot_tn(e, low_grad * masks[a])
                dq = dq_a if dq is None else dq + dq_a
                dk = dk_a if dk is None else dk + dk_a
                dv = dv_a if dv is None else dv + dv_a
            dq_ref[pl.ds(q0, span), cols] += dq * (HEAD_DIM**-0.5)
            dk_ref[pl.ds(k0, width), cols] += dk
            dv_ref[pl.ds(k0, width), cols] += dv

    for_doc(meta, d, cross, run)


def spread_limits(limit_ref, lim_ref):
    lim_ref[...] = jnp.transpose(jnp.broadcast_to(limit_ref[...], (128, SEQ)))


def prepare(
    core, seg_ref, src_ref, rank_ref, limit_ref, pad_ref,
    n0, n1, n2, n3, n4, n5, n6, n7, sq, sk, sv, so, cq, ck, cv, co,
    meta_ref, ranks_ref, limits_ref, norms_ref, ws_ref, wc_ref,
):
    meta_ref[0] = core[0]
    for base, ref in ((1, seg_ref), (17, src_ref)):
        ids = ref[0]
        meta_ref[base] = 0
        meta_ref[base + 15] = SEQ
        for d in range(1, DOCS):
            cut = jnp.sum(jnp.where(ids < d, 1.0, 0.0)).astype(jnp.int32)
            meta_ref[base + d] = cut
            meta_ref[base + 7 + d] = cut
    ranks = jnp.where(pad_ref[0] != 0, hidden_rank, rank_ref[0].astype(f32))
    limits = limit_ref[0].astype(f32)
    for i in range(8):
        ranks_ref[0:1, 128 * i : 128 * i + 128] = ranks[i : i + 1]
        limits_ref[0:1, 128 * i : 128 * i + 128] = limits[i : i + 1]
    for i, ref in enumerate((n0, n1, n2, n3, n4, n5, n6, n7)):
        norms_ref[i : i + 1, :] = ref[...]
    for to, parts, out in ((ws_ref, (sq, sk, sv), so), (wc_ref, (cq, ck, cv), co)):
        for i, part in enumerate(parts):
            to[512 * i : 512 * i + 512, :] = part[...]
        for j in range(4):
            to[1536 + 128 * j : 1664 + 128 * j, :] = out[:, 128 * j : 128 * j + 128]


def self_first(
    meta, xq_ref, xc_ref, er_ref, limit_ref, norms_ref, w0_ref, w1_ref,
    nq_ref, nc_ref, q_ref, k_ref, v_ref, mixed_ref, rt_ref, e_ref, lim_ref,
):
    d = pl.program_id(0)

    @pl.when(d == 0)
    def _():
        spread_limits(limit_ref, lim_ref)
        wq = lanes([w_query(w0_ref), w_query(w1_ref)])
        wkv = lanes([w_key(w0_ref), w_key(w1_ref), w_value(w0_ref), w_value(w1_ref)])

        def tile(i, carry):
            rows = rows_of(i)
            nq = layer_norm(xq_ref[rows, :].astype(f32), norms_ref[0:1], norms_ref[1:2]).astype(bf16)
            nc = layer_norm(xc_ref[rows, :].astype(f32), norms_ref[2:3], norms_ref[3:4]).astype(bf16)
            nq_ref[rows, :] = nq
            nc_ref[rows, :] = nc
            q_ref[rows, :] = (dot(nq, wq) * (HEAD_DIM**-0.5)).astype(bf16)
            kv = dot(nc, wkv).astype(bf16)
            k_ref[rows, :] = kv[:, :256]
            v_ref[rows, :] = kv[:, 256:]
            return carry

        lax.fori_loop(0, TILES, tile, 0)

    attend_doc(meta, d, False, er_ref, lim_ref, q_ref, k_ref, v_ref, e_ref, mixed_ref, rt_ref)


def self_second(
    meta, xq_ref, nq_ref, nc_ref, er_ref, limit_ref, norms_ref, w0_ref, w1_ref, w2_ref, w3_ref,
    mixed_first_ref,
    q_ref, k_ref, v_ref, mixed_ref, rt_ref, e_ref, second_ref, ncross_ref, lim_ref,
):
    d = pl.program_id(0)

    @pl.when(d == 0)
    def _():
        spread_limits(limit_ref, lim_ref)
        wq = lanes([w_query(w2_ref), w_query(w3_ref)])
        wkv = lanes([w_key(w2_ref), w_key(w3_ref), w_value(w2_ref), w_value(w3_ref)])

        def tile(i, carry):
            rows = rows_of(i)
            q_ref[rows, :] = (dot(nq_ref[rows, :], wq) * (HEAD_DIM**-0.5)).astype(bf16)
            kv = dot(nc_ref[rows, :], wkv).astype(bf16)
            k_ref[rows, :] = kv[:, :256]
            v_ref[rows, :] = kv[:, 256:]
            return carry

        lax.fori_loop(0, TILES, tile, 0)

    attend_doc(meta, d, False, er_ref, lim_ref, q_ref, k_ref, v_ref, e_ref, mixed_ref, rt_ref)

    @pl.when(d == DOCS - 1)
    def _():
        out_first = jnp.concatenate([w_out(w0_ref), w_out(w1_ref)], axis=0)
        out_second = jnp.concatenate([w_out(w2_ref), w_out(w3_ref)], axis=0)

        def tile(i, carry):
            rows = rows_of(i)
            branch = dot(mixed_first_ref[rows, :], out_first) + dot(mixed_ref[rows, :], out_second)
            second = xq_ref[rows, :].astype(f32) + branch
            second_ref[rows, :] = second
            ncross_ref[rows, :] = layer_norm(second, norms_ref[4:5], norms_ref[5:6]).astype(bf16)
            return carry

        lax.fori_loop(0, TILES, tile, 0)


def cross_forward(
    meta, second_ref, ncross_ref, memory_ref, norms_ref, w0_ref, w1_ref, w2_ref, w3_ref,
    q_ref, k_ref, v_ref, mixed_ref, rt_ref, e_ref, third_ref, nffn_ref,
):
    d = pl.program_id(0)
    weights = (w0_ref, w1_ref, w2_ref, w3_ref)

    @pl.when(d == 0)
    def _():
        wq = lanes([w_query(w) for w in weights])
        wk = lanes([w_key(w) for w in weights])
        wv = lanes([w_value(w) for w in weights])

        def tile(i, carry):
            rows = rows_of(i)
            memory = memory_ref[rows, :]
            q_ref[rows, :] = (dot(ncross_ref[rows, :], wq) * (HEAD_DIM**-0.5)).astype(bf16)
            k_ref[rows, :] = dot(memory, wk).astype(bf16)
            v_ref[rows, :] = dot(memory, wv).astype(bf16)
            return carry

        lax.fori_loop(0, TILES, tile, 0)

    attend_doc(meta, d, True, None, None, q_ref, k_ref, v_ref, e_ref, mixed_ref, rt_ref)

    @pl.when(d == DOCS - 1)
    def _():
        out_first = jnp.concatenate([w_out(w0_ref), w_out(w1_ref)], axis=0)
        out_second = jnp.concatenate([w_out(w2_ref), w_out(w3_ref)], axis=0)

        def tile(i, carry):
            rows = rows_of(i)
            mixed = mixed_ref[rows, :]
            branch = dot(mixed[:, :256], out_first) + dot(mixed[:, 256:], out_second)
            third = second_ref[rows, :] + branch
            third_ref[rows, :] = third
            nffn_ref[rows, :] = layer_norm(third, norms_ref[6:7], norms_ref[7:8]).astype(bf16)
            return carry

        lax.fori_loop(0, TILES, tile, 0)


def ffn_both(
    meta, third_ref, nffn_ref, cot_ref, norms_ref, u0_ref, u1_ref, u2_ref, u3_ref,
    w0_ref, w1_ref, w2_ref, w3_ref,
    placed_ref, out_ref, g3_ref, gln_ref, own_ref, other_ref, hidden_ref, before_ref,
):
    i = pl.program_id(0)
    rows = rows_of(i)
    nffn = nffn_ref[rows, :]
    cot = cot_ref[rows, :]
    outs = []
    grads = []
    in_refs = (u0_ref, u1_ref, u2_ref, u3_ref)
    for g, w_ref in enumerate((w0_ref, w1_ref, w2_ref, w3_ref)):
        w_in = in_refs[g][...]
        w_out_rows = w_ref[...]
        x = dot(nffn, w_in)
        square = x * x
        t = jnp.tanh(gelu_root * (x + gelu_cube * (square * x)))
        half = 0.5 + 0.5 * t
        hidden = (x * half).astype(bf16)
        slope = half + x * (0.5 - 0.5 * t * t) * (gelu_root + (3.0 * gelu_root * gelu_cube) * square)
        grad_before = (dot_nt(cot, w_out_rows) * slope).astype(bf16)
        outs.append(dot(hidden, w_out_rows))
        grads.append(dot_nt(grad_before, w_in))
        if g < 2:
            hidden_ref[rows, 512 * g : 512 * g + 512] = hidden
            before_ref[rows, 512 * g : 512 * g + 512] = grad_before
    third = third_ref[rows, :]
    out = (third + ((outs[0] + outs[1]) + (outs[2] + outs[3]))).astype(bf16)
    out_ref[rows, :] = out
    placed_ref[rows, :] = out
    grad_normed = (grads[0] + grads[1]) + (grads[2] + grads[3])
    grad_norm, grad_gain, grad_shift = norm_backward(third, norms_ref[6:7], grad_normed)
    g3_ref[rows, :] = cot.astype(f32) + grad_norm

    @pl.when(i == 0)
    def _():
        gln_ref[0:1, :] = grad_gain
        gln_ref[1:2, :] = grad_shift

    @pl.when(i > 0)
    def _():
        gln_ref[0:1, :] += grad_gain
        gln_ref[1:2, :] += grad_shift

    @pl.when(i == TILES - 1)
    def _():
        nffn_all = nffn_ref[...]
        cot_all = cot_ref[...]
        own_ref[0:512, :] = dot_tn(nffn_all, before_ref[:, 0:512])
        own_ref[512:1024, :] = dot_tn(hidden_ref[:, 0:512], cot_all)
        other_ref[0:512, :] = dot_tn(nffn_all, before_ref[:, 512:1024]).astype(bf16)
        other_ref[512:1024, :] = dot_tn(hidden_ref[:, 512:1024], cot_all).astype(bf16)


def back_start(g_ref, mixed_ref, w_refs, dm_ref, dq_ref, dk_ref, dv_ref):
    out_rows = jnp.concatenate([w_out(w) for w in w_refs], axis=0)

    def tile(i, carry):
        rows = rows_of(i)
        dm_ref[rows, :] = dot_nt(g_ref[rows, :].astype(bf16), out_rows).astype(bf16)
        zeros = jnp.zeros((TILE, 256), f32)
        dq_ref[rows, :] = zeros
        dk_ref[rows, :] = zeros
        dv_ref[rows, :] = zeros
        return carry

    lax.fori_loop(0, TILES, tile, 0)


def attention_back_first(
    cross, meta, g_ref, nq_ref, nkv_ref, er_ref, limit_ref, w0_ref, w1_ref,
    q_ref, k_ref, v_ref, mixed_ref, rt_ref, e_ref,
    dq_ref, dk_ref, dv_ref, own_ref, other_ref,
    lim_ref, dm_ref, dqs_ref, dks_ref, dvs_ref,
):
    d = pl.program_id(0)

    @pl.when(d == 0)
    def _():
        if not cross:
            spread_limits(limit_ref, lim_ref)
        back_start(g_ref, mixed_ref, (w0_ref, w1_ref), dm_ref, dqs_ref, dks_ref, dvs_ref)

    attend_doc_back(
        meta, d, cross, None if cross else er_ref, lim_ref, q_ref, k_ref, v_ref, e_ref, mixed_ref,
        rt_ref, dm_ref, dqs_ref, dks_ref, dvs_ref,
    )

    @pl.when(d == DOCS - 1)
    def _():
        dq_ref[...] = dqs_ref[...].astype(bf16)
        dk_ref[...] = dks_ref[...].astype(bf16)
        dv_ref[...] = dvs_ref[...].astype(bf16)
        nq = nq_ref[...]
        nkv = nkv_ref[...]
        for n, part in enumerate(
            (dot_tn(nq, dq_ref[...]), dot_tn(nkv, dk_ref[...]), dot_tn(nkv, dv_ref[...]))
        ):
            own_ref[512 * n : 512 * n + 512, :] = part[:, :128]
            other_ref[512 * n : 512 * n + 512, :] = part[:, 128:].astype(bf16)
        part = dot_tn(mixed_ref[...], g_ref[...].astype(bf16))
        for j in range(4):
            own_ref[1536 + 128 * j : 1664 + 128 * j, :] = part[:128, 128 * j : 128 * j + 128]
            other_ref[1536 + 128 * j : 1664 + 128 * j, :] = part[
                128:, 128 * j : 128 * j + 128
            ].astype(bf16)


def back_second_docs(
    cross, meta, g_ref, er_ref, limit_ref, w_refs, q_ref, k_ref, v_ref, mixed_ref, rt_ref, e_ref,
    lim_ref, dm_ref, dqs_ref, dks_ref, dvs_ref,
):
    d = pl.program_id(0)

    @pl.when(d == 0)
    def _():
        if not cross:
            spread_limits(limit_ref, lim_ref)
        back_start(g_ref, mixed_ref, w_refs, dm_ref, dqs_ref, dks_ref, dvs_ref)

    attend_doc_back(
        meta, d, cross, None if cross else er_ref, lim_ref, q_ref, k_ref, v_ref, e_ref, mixed_ref,
        rt_ref, dm_ref, dqs_ref, dks_ref, dvs_ref,
    )
    return d


def stream_grads(rows, first, second, firsts, seconds):
    dq, dk, dv = first
    dq2, dk2, dv2 = (ref[rows, :].astype(bf16) for ref in second)
    w0, w1 = firsts
    w2, w3 = seconds
    grad_q = dot_nt(dq[rows, :], lanes([w_query(w0), w_query(w1)])) + dot_nt(
        dq2, lanes([w_query(w2), w_query(w3)])
    )
    kv = lanes([dk[rows, :], dv[rows, :]])
    kv2 = lanes([dk2, dv2])
    grad_kv = dot_nt(kv, lanes([w_key(w0), w_key(w1), w_value(w0), w_value(w1)])) + dot_nt(
        kv2, lanes([w_key(w2), w_key(w3), w_value(w2), w_value(w3)])
    )
    return grad_q, grad_kv


def cross_back_second(
    meta, g_ref, second_ref, norms_ref, w0_ref, w1_ref, w2_ref, w3_ref,
    dq_ref, dk_ref, dv_ref, q_ref, k_ref, v_ref, mixed_ref, rt_ref, e_ref,
    g2_ref, placed_ref, gmem_ref, gln_ref,
    dm_ref, dqs_ref, dks_ref, dvs_ref,
):
    d = back_second_docs(
        True, meta, g_ref, None, None, (w2_ref, w3_ref), q_ref, k_ref, v_ref, mixed_ref, rt_ref,
        e_ref, None, dm_ref, dqs_ref, dks_ref, dvs_ref,
    )

    @pl.when(d == DOCS - 1)
    def _():
        gln_ref[...] = jnp.zeros_like(gln_ref)

        def tile(i, carry):
            rows = rows_of(i)
            grad_q, grad_kv = stream_grads(
                rows,
                (dq_ref, dk_ref, dv_ref),
                (dqs_ref, dks_ref, dvs_ref),
                (w0_ref, w1_ref),
                (w2_ref, w3_ref),
            )
            low_kv = grad_kv.astype(bf16)
            gmem_ref[rows, :] = low_kv
            placed_ref[rows, :] = low_kv.astype(f32)
            grad_norm, grad_gain, grad_shift = norm_backward(
                second_ref[rows, :], norms_ref[4:5], grad_q
            )
            g2_ref[rows, :] = g_ref[rows, :] + grad_norm
            gln_ref[0:1, :] += grad_gain
            gln_ref[1:2, :] += grad_shift
            return carry

        lax.fori_loop(0, TILES, tile, 0)


def self_back_second(
    meta, g_ref, xq_ref, xc_ref, er_ref, limit_ref, norms_ref, w0_ref, w1_ref, w2_ref, w3_ref,
    dq_ref, dk_ref, dv_ref, q_ref, k_ref, v_ref, mixed_ref, rt_ref, e_ref,
    placed_q_ref, placed_c_ref, gq_ref, gc_ref, gln_ref,
    lim_ref, dm_ref, dqs_ref, dks_ref, dvs_ref,
):
    d = back_second_docs(
        False, meta, g_ref, er_ref, limit_ref, (w2_ref, w3_ref), q_ref, k_ref, v_ref, mixed_ref,
        rt_ref, e_ref, lim_ref, dm_ref, dqs_ref, dks_ref, dvs_ref,
    )

    @pl.when(d == DOCS - 1)
    def _():
        gln_ref[...] = jnp.zeros_like(gln_ref)

        def tile(i, carry):
            rows = rows_of(i)
            grad_q, grad_kv = stream_grads(
                rows,
                (dq_ref, dk_ref, dv_ref),
                (dqs_ref, dks_ref, dvs_ref),
                (w0_ref, w1_ref),
                (w2_ref, w3_ref),
            )
            grad_norm, grad_gain, grad_shift = norm_backward(
                xq_ref[rows, :].astype(f32), norms_ref[0:1], grad_q
            )
            low_q = (g_ref[rows, :] + grad_norm).astype(bf16)
            gq_ref[rows, :] = low_q
            placed_q_ref[rows, :] = low_q.astype(f32)
            gln_ref[0:1, :] += grad_gain
            gln_ref[1:2, :] += grad_shift
            grad_norm, grad_gain, grad_shift = norm_backward(
                xc_ref[rows, :].astype(f32), norms_ref[2:3], grad_kv
            )
            low_c = grad_norm.astype(bf16)
            gc_ref[rows, :] = low_c
            placed_c_ref[rows, :] = low_c.astype(f32)
            gln_ref[2:3, :] += grad_gain
            gln_ref[3:4, :] += grad_shift
            return carry

        lax.fori_loop(0, TILES, tile, 0)


def place_rows(meta, *refs):
    count = len(refs) // 3
    for n in range(count):
        refs[2 * count + n][...] = refs[n][...].astype(refs[2 * count + n].dtype)


def join_cores(own_ref, other_ref, both_ref):
    both_ref[...] = (own_ref[...] + other_ref[...].astype(f32)).astype(bf16)


def join_rows(parts_ref, total_ref):
    count = parts_ref.shape[0]
    total = parts_ref[0].astype(f32)
    for r in range(1, count):
        total = total + parts_ref[r].astype(f32)
    total = total.astype(bf16)
    for r in range(count):
        total_ref[r] = total


def unpack_grads(*refs):
    count = len(refs) // 5
    for n in range(count):
        packed = refs[n]
        outs = refs[count + 4 * n : count + 4 * n + 4]
        for i in range(3):
            outs[i][...] = packed[512 * i : 512 * i + 512, :].astype(f32)
        for j in range(4):
            outs[3][:, 128 * j : 128 * j + 128] = packed[
                1536 + 128 * j : 1664 + 128 * j, :
            ].astype(f32)


def whole(shape):
    zeros = (0,) * len(shape)
    return pl.BlockSpec(shape, lambda d, meta: zeros)


def own_row(width):
    return pl.BlockSpec((SEQ, width), lambda d, meta: (meta[0], 0))


def columns(width, n):
    return pl.BlockSpec((SEQ, width), lambda d, meta: (0, n))


def raised_spec(heads, n):
    return pl.BlockSpec((1, heads, FAST_Q, FAST_K), lambda d, meta: (d, n, 0, 0))


def call(kernel, name, grid, operands, outs, scratch, flops):
    moved = sum(x.size * x.dtype.itemsize for x, _ in operands[1:])
    return pl.pallas_call(
        kernel,
        name=name,
        grid_spec=pltpu.PrefetchScalarGridSpec(
            num_scalar_prefetch=1,
            grid=(grid,),
            in_specs=[spec for _, spec in operands[1:]],
            out_specs=[spec for _, _, spec in outs],
            scratch_shapes=scratch,
        ),
        out_shape=[jax.ShapeDtypeStruct(shape, dtype) for shape, dtype, _ in outs],
        compiler_params=pltpu.CompilerParams(
            dimension_semantics=("arbitrary",), vmem_limit_bytes=56 * 1024 * 1024
        ),
        cost_estimate=pl.CostEstimate(
            flops=int(flops), bytes_accessed=int(moved), transcendentals=0
        ),
    )(*[x for x, _ in operands])


def simple(kernel, name, operands, outs):
    return pl.pallas_call(
        kernel,
        name=name,
        out_shape=[jax.ShapeDtypeStruct(shape, dtype) for shape, dtype in outs],
        compiler_params=pltpu.CompilerParams(vmem_limit_bytes=32 * 1024 * 1024),
    )(*operands)


def full(x):
    return (x, whole(x.shape))


def shards(
    query_stream,
    content_stream,
    memory,
    segment_ids,
    source_segments,
    context_rank,
    context_limit,
    padding,
    ln_query_gain,
    ln_query_bias,
    ln_content_gain,
    ln_content_bias,
    self_query,
    self_key,
    self_value,
    self_out,
    ln_cross_gain,
    ln_cross_bias,
    cross_query,
    cross_key,
    cross_value,
    cross_out,
    ln_ffn_gain,
    ln_ffn_bias,
    ffn_in,
    ffn_out,
    cotangent,
):
    core = lax.axis_index("heads") % 2

    def to_core(x):
        return lax.ppermute(x, "heads", [(h, h ^ 1) for h in range(4)])

    hold = lambda *xs: lax.optimization_barrier(xs)

    def to_chip(x):
        return lax.ppermute(x, "heads", [(h, h ^ 2) for h in range(4)])

    row = pl.BlockSpec((1, 8, 128), lambda d, core: (core[0], 0, 0))

    def token_row(x):
        return (x.reshape(2, 8, 128), row)

    def fixed(x):
        zeros = (0,) * x.ndim
        return (x, pl.BlockSpec(x.shape, lambda d, core: zeros))

    prepared = [
        ((33,), jnp.int32, pl.BlockSpec(memory_space=pltpu.SMEM)),
        ((1, SEQ), f32, whole((1, SEQ))),
        ((1, SEQ), f32, whole((1, SEQ))),
        ((8, D), f32, whole((8, D))),
        ((2048, 128), bf16, whole((2048, 128))),
        ((2048, 128), bf16, whole((2048, 128))),
    ]
    gains = (
        ln_query_gain,
        ln_query_bias,
        ln_content_gain,
        ln_content_bias,
        ln_cross_gain,
        ln_cross_bias,
        ln_ffn_gain,
        ln_ffn_bias,
    )
    weights = (self_query, self_key, self_value, self_out)
    weights += (cross_query, cross_key, cross_value, cross_out)
    tokens = (segment_ids, source_segments, context_rank, context_limit, padding)
    meta, rank, limit, norms, ws0, wc0 = call(
        prepare,
        "prepare",
        1,
        [(core.astype(jnp.int32)[None], None)]
        + [token_row(x) for x in tokens]
        + [fixed(x.reshape(1, D)) for x in gains]
        + [fixed(x) for x in weights],
        prepared,
        [],
        0,
    )

    ws1 = to_core(ws0)
    ws2 = to_chip(ws0)
    wc2 = to_chip(wc0)
    u0, u2 = ffn_in, to_chip(ffn_in)
    wf0, wf2 = ffn_out, to_chip(ffn_out)
    meta_in = (meta, None)
    xq = (query_stream, own_row(D))
    xc = (content_stream, own_row(D))
    mem = (memory, own_row(D))
    cot = (cotangent, own_row(D))

    def heads_out(width, heads):
        return [
            ((SEQ, width), bf16, whole((SEQ, width))),
            ((SEQ, width), bf16, whole((SEQ, width))),
            ((SEQ, width), bf16, whole((SEQ, width))),
            ((SEQ, width), bf16, whole((SEQ, width))),
            ((SEQ, width), f32, whole((SEQ, width))),
            ((DOCS, heads, FAST_Q, FAST_K), bf16, raised_spec(heads, 0)),
        ]

    def stream_out(dtype):
        return ((SEQ, D), dtype, whole((SEQ, D)))

    def placed(dtype):
        return ((2 * SEQ, D), dtype, own_row(D))

    limits = pltpu.VMEM((SEQ, 128), f32)
    pair_flops = 2 * SEQ * D * 768 + 2 * 2 * 4 * DOCS * FAST_Q * FAST_K * 256

    nq, nc, *first = call(
        self_first,
        "self_first",
        DOCS,
        [meta_in, xq, xc, full(rank), full(limit), full(norms), full(ws0), full(ws1)],
        [stream_out(bf16), stream_out(bf16)] + heads_out(256, 4),
        [limits],
        pair_flops,
    )
    ws2, wc0, nq = hold(ws2, wc0, nq)
    ws3 = to_core(ws2)
    wc1 = to_core(wc0)
    *second_heads, second, ncross = call(
        self_second,
        "self_second",
        DOCS,
        [meta_in, xq, full(nq), full(nc), full(rank), full(limit), full(norms)]
        + [full(w) for w in (ws0, ws1, ws2, ws3)]
        + [full(first[3])],
        heads_out(256, 4) + [stream_out(f32), stream_out(bf16)],
        [limits],
        pair_flops + 2 * SEQ * D * D,
    )
    wc2, u0, wf0, second = hold(wc2, u0, wf0, second)
    wc3 = to_core(wc2)
    u1 = to_core(u0)
    wf1 = to_core(wf0)
    *cross_heads, third, nffn = call(
        cross_forward,
        "cross_forward",
        DOCS,
        [meta_in, full(second), full(ncross), mem, full(norms)]
        + [full(w) for w in (wc0, wc1, wc2, wc3)],
        heads_out(512, 8) + [stream_out(f32), stream_out(bf16)],
        [],
        2 * pair_flops + 2 * SEQ * D * D,
    )
    u2, wf2, third = hold(u2, wf2, third)
    u3 = to_core(u2)
    wf3 = to_core(wf2)
    grads_ln = ((8, D), f32, whole((8, D)))
    placed_output, output, g3, gln_ffn, ffn_own, ffn_other = call(
        ffn_both,
        "ffn_both",
        TILES,
        [meta_in, full(third), full(nffn), cot, full(norms)]
        + [full(w) for w in (u0, u1, u2, u3, wf0, wf1, wf2, wf3)],
        [
            placed(bf16),
            stream_out(bf16),
            stream_out(f32),
            grads_ln,
            ((1024, D), f32, whole((1024, D))),
            ((1024, D), bf16, whole((1024, D))),
        ],
        [pltpu.VMEM((SEQ, 1024), bf16), pltpu.VMEM((SEQ, 1024), bf16)],
        12 * SEQ * D * 2048,
    )

    row_count = lax.axis_size("rows")

    def over_cores(own, other):
        shape = own.shape
        both = simple(join_cores, "join_cores", [own, to_core(other)], [(shape, bf16)])[0]
        return both.reshape(row_count, shape[0] // row_count, shape[1])

    def exchange(x):
        return lax.all_to_all(x, "rows", 0, 0)

    def over_rows(parts):
        return simple(join_rows, "join_rows", [parts], [(parts.shape, bf16)])[0]

    back_scratch = [pltpu.VMEM((SEQ, 256), bf16)] + [pltpu.VMEM((SEQ, 256), f32)] * 3
    pair_out = ((SEQ, 256), bf16, whole((SEQ, 256)))
    packed_outs = [
        ((2048, 128), f32, whole((2048, 128))),
        ((2048, 128), bf16, whole((2048, 128))),
    ]
    back_flops = 2 * SEQ * D * 256 + 4 * 2 * 4 * DOCS * FAST_Q * FAST_K * 256

    def head_inputs(arrays, n):
        q, k, v, mixed, rt, e = arrays
        return [(x, columns(256, n)) for x in (q, k, v, mixed, rt)] + [(e, raised_spec(4, n))]

    *cross_grads, cross_own, cross_other = call(
        functools.partial(attention_back_first, True),
        "cross_back_first",
        DOCS,
        [meta_in, full(g3), full(ncross), mem, full(rank), full(limit), full(wc0), full(wc1)]
        + head_inputs(cross_heads, 0),
        [pair_out] * 3 + packed_outs,
        [limits] + back_scratch,
        back_flops + 2 * SEQ * D * 1024,
    )
    ffn_joined = over_cores(ffn_own, ffn_other)
    ffn_joined, g3_now = hold(ffn_joined, g3)
    grad_ffn = lax.psum(ffn_joined.reshape(1024, D), "rows")
    g2, placed_mem, grad_mem, gln_cross = call(
        cross_back_second,
        "cross_back_second",
        DOCS,
        [meta_in, full(g3_now), full(second), full(norms)]
        + [full(w) for w in (wc0, wc1, wc2, wc3)]
        + [full(x) for x in cross_grads]
        + head_inputs(cross_heads, 1),
        [stream_out(f32), placed(f32), stream_out(bf16), grads_ln],
        back_scratch,
        back_flops + 2 * SEQ * D * 1536,
    )
    cross_joined = over_cores(cross_own, cross_other)
    cross_joined, g2 = hold(cross_joined, g2)
    cross_parts = exchange(cross_joined)

    *self_grads, self_own, self_other = call(
        functools.partial(attention_back_first, False),
        "self_back_first",
        DOCS,
        [meta_in, full(g2), full(nq), full(nc), full(rank), full(limit), full(ws0), full(ws1)]
        + head_inputs(first, 0),
        [pair_out] * 3 + packed_outs,
        [limits] + back_scratch,
        back_flops + 2 * SEQ * D * 1024,
    )
    self_joined = over_cores(self_own, self_other)
    cross_total = over_rows(cross_parts)
    self_joined, cross_total, g2 = hold(self_joined, cross_total, g2)
    self_parts = exchange(self_joined)
    grad_cross = exchange(cross_total).reshape(2048, 128)
    placed_q, placed_c, gq, gc, gln_self = call(
        self_back_second,
        "self_back_second",
        DOCS,
        [meta_in, full(g2), xq, xc, full(rank), full(limit), full(norms)]
        + [full(w) for w in (ws0, ws1, ws2, ws3)]
        + [full(x) for x in self_grads]
        + head_inputs(second_heads, 0),
        [placed(f32), placed(f32), stream_out(bf16), stream_out(bf16), grads_ln],
        [limits] + back_scratch,
        back_flops + 2 * SEQ * D * 1536,
    )

    gln = jnp.concatenate([gln_self[0:4], gln_cross[0:2], gln_ffn[0:2]], axis=0)
    gln = jnp.broadcast_to(gln + to_core(gln), (lax.axis_size("rows"), 8, D))
    gln = jnp.sum(lax.all_to_all(gln, "rows", 0, 0), axis=0)

    def both_rows(placed_own, arrays, name):
        count = len(arrays)
        size = SEQ // 2
        one = pl.BlockSpec((size, D), lambda i, meta: (i, 0))
        block = pl.BlockSpec((size, D), lambda i, meta: (2 * (1 - meta[0]) + i, 0))
        return pl.pallas_call(
            place_rows,
            name=name,
            grid_spec=pltpu.PrefetchScalarGridSpec(
                num_scalar_prefetch=1,
                grid=(2,),
                in_specs=[one] * count + [pl.BlockSpec(memory_space=pl.ANY)] * count,
                out_specs=[block] * count,
            ),
            out_shape=[jax.ShapeDtypeStruct(x.shape, x.dtype) for x in placed_own],
            input_output_aliases={1 + count + n: n for n in range(count)},
        )(meta, *[to_core(x) for x in arrays], *placed_own)

    out_both, grad_mem_both = both_rows([placed_output, placed_mem], [output, grad_mem], "place_early")
    gq_both, gc_both = both_rows([placed_q, placed_c], [gq, gc], "place_late")

    grad_self = exchange(over_rows(self_parts)).reshape(2048, 128)
    parts = [((512, 128), f32)] * 3 + [((128, 512), f32)]
    parts = simple(unpack_grads, "unpack_grads", [grad_self, grad_cross], parts * 2)
    grad_self_parts, grad_cross_parts = parts[:4], parts[4:]
    grad_ffn = grad_ffn.astype(f32)
    return (
        out_both,
        gq_both,
        gc_both,
        grad_mem_both,
        gln[0],
        gln[1],
        gln[2],
        gln[3],
        *grad_self_parts,
        gln[4],
        gln[5],
        *grad_cross_parts,
        gln[6],
        gln[7],
        grad_ffn[0:512],
        grad_ffn[512:1024],
    )


def solution(mesh):
    assert mesh.shape["heads"] == 4
    row_spec = P("rows", None)
    flat = P("rows")
    by_column = P(None, "heads")
    by_row = P("heads", None)
    attention = (by_column, by_column, by_column, by_row)
    in_specs = (
        (row_spec,) * 3
        + (flat,) * 5
        + (P(),) * 4
        + attention
        + (P(),) * 2
        + attention
        + (P(),) * 2
        + (by_column, by_row, row_spec)
    )
    out_specs = (
        (row_spec,) * 4
        + (P(),) * 4
        + attention
        + (P(),) * 2
        + attention
        + (P(),) * 2
        + (by_column, by_row)
    )
    return jax.shard_map(shards, mesh=mesh, in_specs=in_specs, out_specs=out_specs, check_vma=False)
```

```python
import functools

import jax
import jax.numpy as jnp
from jax import lax
from jax.experimental import pallas as pl
from jax.experimental.pallas import tpu as pltpu
from jax.sharding import PartitionSpec as P

HEAD_DIM = 64
SEQ = 1024
DOCS = 8
D = 512
TILE = 256
TILES = SEQ // TILE
FAST_Q = 208
FAST_K = 256
LONG_Q = 128
LONG_K = 640

norm_eps = 1e-05
masked_score = -1e30
hidden_rank = 1e6
gelu_root = 0.7978845608028654
gelu_cube = 0.044715

f32 = jnp.float32
bf16 = jnp.bfloat16


def dot(a, b):
    return lax.dot_general(a, b, (((1,), (0,)), ((), ())), preferred_element_type=f32)


def dot_nt(a, b):
    return lax.dot_general(a, b, (((1,), (1,)), ((), ())), preferred_element_type=f32)


def dot_tn(a, b):
    return lax.dot_general(a, b, (((0,), (0,)), ((), ())), preferred_element_type=f32)


def lanes(parts):
    return jnp.concatenate(parts, axis=1)


def layer_norm(values, gain, shift):
    centre = values - jnp.mean(values, axis=-1, keepdims=True)
    spread = jnp.mean(centre * centre, axis=-1, keepdims=True)
    return centre * lax.rsqrt(spread + norm_eps) * gain + shift


def norm_backward(values, gain, grad):
    centre = values - jnp.mean(values, axis=-1, keepdims=True)
    spread = jnp.mean(centre * centre, axis=-1, keepdims=True)
    scale = lax.rsqrt(spread + norm_eps)
    xhat = centre * scale
    eg = grad * gain
    mean_eg = jnp.mean(eg, axis=-1, keepdims=True)
    mean_egx = jnp.mean(eg * xhat, axis=-1, keepdims=True)
    grad_gain = jnp.sum(grad * xhat, axis=0, keepdims=True)
    grad_shift = jnp.sum(grad, axis=0, keepdims=True)
    return scale * (eg - mean_eg - xhat * mean_egx), grad_gain, grad_shift


def rows_of(i, size=TILE):
    return pl.ds(pl.multiple_of(i * size, size), size)


def w_query(ref):
    return ref[0:512, :]


def w_key(ref):
    return ref[512:1024, :]


def w_value(ref):
    return ref[1024:1536, :]


def w_out(ref):
    return lanes([ref[1536 + 128 * j : 1664 + 128 * j, :] for j in range(4)])


def half_masks():
    place = lax.broadcasted_iota(jnp.int32, (1, 128), 1)
    low = jnp.where(place < HEAD_DIM, 1.0, 0.0).astype(f32)
    return (low.astype(bf16), (1.0 - low).astype(bf16))


def doc_bounds(meta, d, source):
    base = 17 if source else 1
    return meta[base + d], meta[base + 8 + d]


def window_of(first, limit):
    return pl.multiple_of(jnp.minimum((first // 16) * 16, limit), 16)


def key_values(er_ref, ks, ke, k0, width):
    if er_ref is None:
        place = k0 + lax.broadcasted_iota(jnp.int32, (1, width), 1)
        return jnp.where((place >= ks) & (place < ke), 0.0, masked_score)
    ranks = jnp.broadcast_to(er_ref[...], (8, SEQ))
    ranks = pltpu.roll(ranks, lax.rem(SEQ - k0, SEQ), 1)[0:1, 0:width]
    place = k0 + lax.broadcasted_iota(jnp.int32, (1, width), 1)
    ranks = jnp.where((place < ks + 2) & (ranks < hidden_rank), -1.0, ranks)
    return jnp.where((place >= ks) & (place < ke), ranks, hidden_rank)


def make_bias(er_ref, lim_ref, ks, ke, q0, k0, span, width):
    keys = key_values(er_ref, ks, ke, k0, width)
    if er_ref is None:
        return keys
    limits = lim_ref[pl.ds(q0, span), :]
    limits = lanes([limits] * (width // 128))
    row = q0 + lax.broadcasted_iota(jnp.int32, (span, width), 0)
    column = k0 + lax.broadcasted_iota(jnp.int32, (span, width), 1)
    return jnp.where((keys < limits) & (row != column), 0.0, masked_score)


def raised(queries, keys, bias):
    scores = dot_nt(queries, keys) + bias
    return jnp.exp(scores - jnp.max(scores, axis=1, keepdims=True)).astype(bf16)


def for_doc(meta, d, cross, run):
    ts, te = doc_bounds(meta, d, False)
    ks, ke = doc_bounds(meta, d, cross)
    q0 = window_of(ts, SEQ - FAST_Q)
    k0 = window_of(ks, SEQ - FAST_K)
    fast = (te - q0 <= FAST_Q) & (ke - k0 <= FAST_K)

    @pl.when(fast)
    def _():
        run(q0, k0, FAST_Q, FAST_K, ts, te, ks, ke, True)

    @pl.when(jnp.logical_not(fast))
    def _():
        base = (ts // 16) * 16
        k_long = window_of(ks, SEQ - LONG_K)

        def chunk(i, carry):
            lower = base + i * LONG_Q
            q_long = pl.multiple_of(jnp.minimum(lower, SEQ - LONG_Q), 16)
            run(
                q_long,
                k_long,
                LONG_Q,
                LONG_K,
                jnp.maximum(ts, lower),
                jnp.minimum(te, lower + LONG_Q),
                ks,
                ke,
                False,
            )
            return carry

        lax.fori_loop(0, (te - base + LONG_Q - 1) // LONG_Q, chunk, 0)


def attend_doc(meta, d, cross, er_ref, lim_ref, q_ref, k_ref, v_ref, e_ref, mixed_ref, rt_ref):
    pairs = q_ref.shape[1] // 128
    masks = half_masks()

    def run(q0, k0, span, width, low, high, ks, ke, fast):
        bias = make_bias(er_ref, lim_ref, ks, ke, q0, k0, span, width)
        row = q0 + lax.broadcasted_iota(jnp.int32, (span, 128), 0)
        inside = (row >= low) & (row < high)
        ones = jnp.ones((width, 128), bf16)
        for p in range(pairs):
            cols = slice(128 * p, 128 * p + 128)
            queries = q_ref[pl.ds(q0, span), cols]
            keys = k_ref[pl.ds(k0, width), cols]
            values = v_ref[pl.ds(k0, width), cols]
            total = None
            for a in range(2):
                e = raised(queries, keys * masks[a], bias)
                if fast:
                    e_ref[0, 2 * p + a] = e
                part = dot(e, lanes([values * masks[a], ones * masks[a]]))
                total = part if total is None else total + part
            rt = 1.0 / total[:, 128:]
            mixed = total[:, :128] * rt
            old = mixed_ref[pl.ds(q0, span), cols].astype(f32)
            mixed_ref[pl.ds(q0, span), cols] = jnp.where(inside, mixed, old).astype(bf16)
            rt_ref[pl.ds(q0, span), cols] = jnp.where(inside, rt, rt_ref[pl.ds(q0, span), cols])

    for_doc(meta, d, cross, run)


def attend_doc_back(
    meta, d, cross, er_ref, lim_ref, q_ref, k_ref, v_ref, e_ref, mixed_ref, rt_ref, dm_ref,
    dq_ref, dk_ref, dv_ref,
):
    pairs = q_ref.shape[1] // 128
    masks = half_masks()

    def run(q0, k0, span, width, low, high, ks, ke, fast):
        row = q0 + lax.broadcasted_iota(jnp.int32, (span, 128), 0)
        inside = (row >= low) & (row < high)
        ones = jnp.ones((width, 128), bf16)
        if not fast:
            bias = make_bias(er_ref, lim_ref, ks, ke, q0, k0, span, width)
        for p in range(pairs):
            cols = slice(128 * p, 128 * p + 128)
            queries = q_ref[pl.ds(q0, span), cols]
            keys = k_ref[pl.ds(k0, width), cols]
            values = v_ref[pl.ds(k0, width), cols]
            mixed = mixed_ref[pl.ds(q0, span), cols].astype(f32)
            grad = dm_ref[pl.ds(q0, span), cols].astype(f32) * rt_ref[pl.ds(q0, span), cols]
            grad = jnp.where(inside, grad, 0.0)
            low_grad = grad.astype(bf16)
            left = lanes([low_grad, (-(grad * mixed)).astype(bf16)])
            dq = dk = dv = None
            for a in range(2):
                right = lanes([values * masks[a], ones * masks[a]])
                masked_keys = keys * masks[a]
                delta = dot_nt(left, right)
                e = e_ref[0, 2 * p + a] if fast else raised(queries, masked_keys, bias)
                ds = (e.astype(f32) * delta).astype(bf16)
                dq_a = dot(ds, masked_keys)
                dk_a = dot_tn(ds, queries * masks[a])
                dv_a = dot_tn(e, low_grad * masks[a])
                dq = dq_a if dq is None else dq + dq_a
                dk = dk_a if dk is None else dk + dk_a
                dv = dv_a if dv is None else dv + dv_a
            dq_ref[pl.ds(q0, span), cols] += dq * (HEAD_DIM**-0.5)
            dk_ref[pl.ds(k0, width), cols] += dk
            dv_ref[pl.ds(k0, width), cols] += dv

    for_doc(meta, d, cross, run)


def spread_limits(limit_ref, lim_ref):
    lim_ref[...] = jnp.transpose(jnp.broadcast_to(limit_ref[...], (128, SEQ)))


def prepare(
    core, seg_ref, src_ref, rank_ref, limit_ref, pad_ref,
    n0, n1, n2, n3, n4, n5, n6, n7, sq, sk, sv, so, cq, ck, cv, co,
    meta_ref, ranks_ref, limits_ref, norms_ref, ws_ref, wc_ref,
):
    meta_ref[0] = core[0]
    for base, ref in ((1, seg_ref), (17, src_ref)):
        ids = ref[0]
        meta_ref[base] = 0
        meta_ref[base + 15] = SEQ
        for d in range(1, DOCS):
            cut = jnp.sum(jnp.where(ids < d, 1.0, 0.0)).astype(jnp.int32)
            meta_ref[base + d] = cut
            meta_ref[base + 7 + d] = cut
    ranks = jnp.where(pad_ref[0] != 0, hidden_rank, rank_ref[0].astype(f32))
    limits = limit_ref[0].astype(f32)
    for i in range(8):
        ranks_ref[0:1, 128 * i : 128 * i + 128] = ranks[i : i + 1]
        limits_ref[0:1, 128 * i : 128 * i + 128] = limits[i : i + 1]
    for i, ref in enumerate((n0, n1, n2, n3, n4, n5, n6, n7)):
        norms_ref[i : i + 1, :] = ref[...]
    for to, parts, out in ((ws_ref, (sq, sk, sv), so), (wc_ref, (cq, ck, cv), co)):
        for i, part in enumerate(parts):
            to[512 * i : 512 * i + 512, :] = part[...]
        for j in range(4):
            to[1536 + 128 * j : 1664 + 128 * j, :] = out[:, 128 * j : 128 * j + 128]


def self_first(
    meta, xq_ref, xc_ref, er_ref, limit_ref, norms_ref, w0_ref, w1_ref,
    nq_ref, nc_ref, q_ref, k_ref, v_ref, mixed_ref, rt_ref, e_ref, lim_ref,
):
    d = pl.program_id(0)

    @pl.when(d == 0)
    def _():
        spread_limits(limit_ref, lim_ref)
        wq = lanes([w_query(w0_ref), w_query(w1_ref)])
        wkv = lanes([w_key(w0_ref), w_key(w1_ref), w_value(w0_ref), w_value(w1_ref)])

        def tile(i, carry):
            rows = rows_of(i)
            nq = layer_norm(xq_ref[rows, :].astype(f32), norms_ref[0:1], norms_ref[1:2]).astype(bf16)
            nc = layer_norm(xc_ref[rows, :].astype(f32), norms_ref[2:3], norms_ref[3:4]).astype(bf16)
            nq_ref[rows, :] = nq
            nc_ref[rows, :] = nc
            q_ref[rows, :] = (dot(nq, wq) * (HEAD_DIM**-0.5)).astype(bf16)
            kv = dot(nc, wkv).astype(bf16)
            k_ref[rows, :] = kv[:, :256]
            v_ref[rows, :] = kv[:, 256:]
            return carry

        lax.fori_loop(0, TILES, tile, 0)

    attend_doc(meta, d, False, er_ref, lim_ref, q_ref, k_ref, v_ref, e_ref, mixed_ref, rt_ref)


def self_second(
    meta, xq_ref, nq_ref, nc_ref, er_ref, limit_ref, norms_ref, w0_ref, w1_ref, w2_ref, w3_ref,
    mixed_first_ref,
    q_ref, k_ref, v_ref, mixed_ref, rt_ref, e_ref, second_ref, ncross_ref, lim_ref,
):
    d = pl.program_id(0)

    @pl.when(d == 0)
    def _():
        spread_limits(limit_ref, lim_ref)
        wq = lanes([w_query(w2_ref), w_query(w3_ref)])
        wkv = lanes([w_key(w2_ref), w_key(w3_ref), w_value(w2_ref), w_value(w3_ref)])

        def tile(i, carry):
            rows = rows_of(i)
            q_ref[rows, :] = (dot(nq_ref[rows, :], wq) * (HEAD_DIM**-0.5)).astype(bf16)
            kv = dot(nc_ref[rows, :], wkv).astype(bf16)
            k_ref[rows, :] = kv[:, :256]
            v_ref[rows, :] = kv[:, 256:]
            return carry

        lax.fori_loop(0, TILES, tile, 0)

    attend_doc(meta, d, False, er_ref, lim_ref, q_ref, k_ref, v_ref, e_ref, mixed_ref, rt_ref)

    @pl.when(d == DOCS - 1)
    def _():
        out_first = jnp.concatenate([w_out(w0_ref), w_out(w1_ref)], axis=0)
        out_second = jnp.concatenate([w_out(w2_ref), w_out(w3_ref)], axis=0)

        def tile(i, carry):
            rows = rows_of(i)
            branch = dot(mixed_first_ref[rows, :], out_first) + dot(mixed_ref[rows, :], out_second)
            second = xq_ref[rows, :].astype(f32) + branch
            second_ref[rows, :] = second
            ncross_ref[rows, :] = layer_norm(second, norms_ref[4:5], norms_ref[5:6]).astype(bf16)
            return carry

        lax.fori_loop(0, TILES, tile, 0)


def cross_forward(
    meta, second_ref, ncross_ref, memory_ref, norms_ref, w0_ref, w1_ref, w2_ref, w3_ref,
    q_ref, k_ref, v_ref, mixed_ref, rt_ref, e_ref, third_ref, nffn_ref,
):
    d = pl.program_id(0)
    weights = (w0_ref, w1_ref, w2_ref, w3_ref)

    @pl.when(d == 0)
    def _():
        wq = lanes([w_query(w) for w in weights])
        wk = lanes([w_key(w) for w in weights])
        wv = lanes([w_value(w) for w in weights])

        def tile(i, carry):
            rows = rows_of(i)
            memory = memory_ref[rows, :]
            q_ref[rows, :] = (dot(ncross_ref[rows, :], wq) * (HEAD_DIM**-0.5)).astype(bf16)
            k_ref[rows, :] = dot(memory, wk).astype(bf16)
            v_ref[rows, :] = dot(memory, wv).astype(bf16)
            return carry

        lax.fori_loop(0, TILES, tile, 0)

    attend_doc(meta, d, True, None, None, q_ref, k_ref, v_ref, e_ref, mixed_ref, rt_ref)

    @pl.when(d == DOCS - 1)
    def _():
        out_first = jnp.concatenate([w_out(w0_ref), w_out(w1_ref)], axis=0)
        out_second = jnp.concatenate([w_out(w2_ref), w_out(w3_ref)], axis=0)

        def tile(i, carry):
            rows = rows_of(i)
            mixed = mixed_ref[rows, :]
            branch = dot(mixed[:, :256], out_first) + dot(mixed[:, 256:], out_second)
            third = second_ref[rows, :] + branch
            third_ref[rows, :] = third
            nffn_ref[rows, :] = layer_norm(third, norms_ref[6:7], norms_ref[7:8]).astype(bf16)
            return carry

        lax.fori_loop(0, TILES, tile, 0)


def ffn_both(
    meta, third_ref, nffn_ref, cot_ref, norms_ref, u0_ref, u1_ref, u2_ref, u3_ref,
    w0_ref, w1_ref, w2_ref, w3_ref,
    placed_ref, out_ref, g3_ref, gln_ref, own_ref, other_ref, hidden_ref, before_ref,
):
    i = pl.program_id(0)
    rows = rows_of(i)
    nffn = nffn_ref[rows, :]
    cot = cot_ref[rows, :]
    outs = []
    grads = []
    in_refs = (u0_ref, u1_ref, u2_ref, u3_ref)
    for g, w_ref in enumerate((w0_ref, w1_ref, w2_ref, w3_ref)):
        w_in = in_refs[g][...]
        w_out_rows = w_ref[...]
        x = dot(nffn, w_in)
        square = x * x
        t = jnp.tanh(gelu_root * (x + gelu_cube * (square * x)))
        half = 0.5 + 0.5 * t
        hidden = (x * half).astype(bf16)
        slope = half + x * (0.5 - 0.5 * t * t) * (gelu_root + (3.0 * gelu_root * gelu_cube) * square)
        grad_before = (dot_nt(cot, w_out_rows) * slope).astype(bf16)
        outs.append(dot(hidden, w_out_rows))
        grads.append(dot_nt(grad_before, w_in))
        if g < 2:
            hidden_ref[rows, 512 * g : 512 * g + 512] = hidden
            before_ref[rows, 512 * g : 512 * g + 512] = grad_before
    third = third_ref[rows, :]
    out = (third + ((outs[0] + outs[1]) + (outs[2] + outs[3]))).astype(bf16)
    out_ref[rows, :] = out
    placed_ref[rows, :] = out
    grad_normed = (grads[0] + grads[1]) + (grads[2] + grads[3])
    grad_norm, grad_gain, grad_shift = norm_backward(third, norms_ref[6:7], grad_normed)
    g3_ref[rows, :] = cot.astype(f32) + grad_norm

    @pl.when(i == 0)
    def _():
        gln_ref[0:1, :] = grad_gain
        gln_ref[1:2, :] = grad_shift

    @pl.when(i > 0)
    def _():
        gln_ref[0:1, :] += grad_gain
        gln_ref[1:2, :] += grad_shift

    @pl.when(i == TILES - 1)
    def _():
        nffn_all = nffn_ref[...]
        cot_all = cot_ref[...]
        own_ref[0:512, :] = dot_tn(nffn_all, before_ref[:, 0:512])
        own_ref[512:1024, :] = dot_tn(hidden_ref[:, 0:512], cot_all)
        other_ref[0:512, :] = dot_tn(nffn_all, before_ref[:, 512:1024]).astype(bf16)
        other_ref[512:1024, :] = dot_tn(hidden_ref[:, 512:1024], cot_all).astype(bf16)


def back_start(g_ref, mixed_ref, w_refs, dm_ref, dq_ref, dk_ref, dv_ref):
    out_rows = jnp.concatenate([w_out(w) for w in w_refs], axis=0)

    def tile(i, carry):
        rows = rows_of(i)
        dm_ref[rows, :] = dot_nt(g_ref[rows, :].astype(bf16), out_rows).astype(bf16)
        zeros = jnp.zeros((TILE, 256), f32)
        dq_ref[rows, :] = zeros
        dk_ref[rows, :] = zeros
        dv_ref[rows, :] = zeros
        return carry

    lax.fori_loop(0, TILES, tile, 0)


def attention_back_first(
    cross, meta, g_ref, nq_ref, nkv_ref, er_ref, limit_ref, w0_ref, w1_ref,
    q_ref, k_ref, v_ref, mixed_ref, rt_ref, e_ref,
    dq_ref, dk_ref, dv_ref, own_ref, other_ref,
    lim_ref, dm_ref, dqs_ref, dks_ref, dvs_ref,
):
    d = pl.program_id(0)

    @pl.when(d == 0)
    def _():
        if not cross:
            spread_limits(limit_ref, lim_ref)
        back_start(g_ref, mixed_ref, (w0_ref, w1_ref), dm_ref, dqs_ref, dks_ref, dvs_ref)

    attend_doc_back(
        meta, d, cross, None if cross else er_ref, lim_ref, q_ref, k_ref, v_ref, e_ref, mixed_ref,
        rt_ref, dm_ref, dqs_ref, dks_ref, dvs_ref,
    )

    @pl.when(d == DOCS - 1)
    def _():
        dq_ref[...] = dqs_ref[...].astype(bf16)
        dk_ref[...] = dks_ref[...].astype(bf16)
        dv_ref[...] = dvs_ref[...].astype(bf16)
        nq = nq_ref[...]
        nkv = nkv_ref[...]
        for n, part in enumerate(
            (dot_tn(nq, dq_ref[...]), dot_tn(nkv, dk_ref[...]), dot_tn(nkv, dv_ref[...]))
        ):
            own_ref[:, 128 * n : 128 * n + 128] = part[:, :128]
            other_ref[:, 128 * n : 128 * n + 128] = part[:, 128:].astype(bf16)
        part = dot_tn(mixed_ref[...], g_ref[...].astype(bf16))
        for j in range(4):
            rows = slice(128 * j, 128 * j + 128)
            own_ref[rows, 384:512] = part[:128, rows]
            other_ref[rows, 384:512] = part[128:, rows].astype(bf16)


def back_second_docs(
    cross, meta, g_ref, er_ref, limit_ref, w_refs, q_ref, k_ref, v_ref, mixed_ref, rt_ref, e_ref,
    lim_ref, dm_ref, dqs_ref, dks_ref, dvs_ref,
):
    d = pl.program_id(0)

    @pl.when(d == 0)
    def _():
        if not cross:
            spread_limits(limit_ref, lim_ref)
        back_start(g_ref, mixed_ref, w_refs, dm_ref, dqs_ref, dks_ref, dvs_ref)

    attend_doc_back(
        meta, d, cross, None if cross else er_ref, lim_ref, q_ref, k_ref, v_ref, e_ref, mixed_ref,
        rt_ref, dm_ref, dqs_ref, dks_ref, dvs_ref,
    )
    return d


def stream_grads(rows, first, second, firsts, seconds):
    dq, dk, dv = first
    dq2, dk2, dv2 = (ref[rows, :].astype(bf16) for ref in second)
    w0, w1 = firsts
    w2, w3 = seconds
    grad_q = dot_nt(dq[rows, :], lanes([w_query(w0), w_query(w1)])) + dot_nt(
        dq2, lanes([w_query(w2), w_query(w3)])
    )
    kv = lanes([dk[rows, :], dv[rows, :]])
    kv2 = lanes([dk2, dv2])
    grad_kv = dot_nt(kv, lanes([w_key(w0), w_key(w1), w_value(w0), w_value(w1)])) + dot_nt(
        kv2, lanes([w_key(w2), w_key(w3), w_value(w2), w_value(w3)])
    )
    return grad_q, grad_kv


def cross_back_second(
    meta, g_ref, second_ref, norms_ref, w0_ref, w1_ref, w2_ref, w3_ref,
    dq_ref, dk_ref, dv_ref, q_ref, k_ref, v_ref, mixed_ref, rt_ref, e_ref,
    g2_ref, placed_ref, gmem_ref, gln_ref,
    dm_ref, dqs_ref, dks_ref, dvs_ref,
):
    d = back_second_docs(
        True, meta, g_ref, None, None, (w2_ref, w3_ref), q_ref, k_ref, v_ref, mixed_ref, rt_ref,
        e_ref, None, dm_ref, dqs_ref, dks_ref, dvs_ref,
    )

    @pl.when(d == DOCS - 1)
    def _():
        gln_ref[...] = jnp.zeros_like(gln_ref)

        def tile(i, carry):
            rows = rows_of(i)
            grad_q, grad_kv = stream_grads(
                rows,
                (dq_ref, dk_ref, dv_ref),
                (dqs_ref, dks_ref, dvs_ref),
                (w0_ref, w1_ref),
                (w2_ref, w3_ref),
            )
            low_kv = grad_kv.astype(bf16)
            gmem_ref[rows, :] = low_kv
            placed_ref[rows, :] = low_kv.astype(f32)
            grad_norm, grad_gain, grad_shift = norm_backward(
                second_ref[rows, :], norms_ref[4:5], grad_q
            )
            g2_ref[rows, :] = g_ref[rows, :] + grad_norm
            gln_ref[0:1, :] += grad_gain
            gln_ref[1:2, :] += grad_shift
            return carry

        lax.fori_loop(0, TILES, tile, 0)


def self_back_second(
    meta, g_ref, xq_ref, xc_ref, er_ref, limit_ref, norms_ref, w0_ref, w1_ref, w2_ref, w3_ref,
    dq_ref, dk_ref, dv_ref, q_ref, k_ref, v_ref, mixed_ref, rt_ref, e_ref,
    placed_q_ref, placed_c_ref, gq_ref, gc_ref, gln_ref,
    lim_ref, dm_ref, dqs_ref, dks_ref, dvs_ref,
):
    d = back_second_docs(
        False, meta, g_ref, er_ref, limit_ref, (w2_ref, w3_ref), q_ref, k_ref, v_ref, mixed_ref,
        rt_ref, e_ref, lim_ref, dm_ref, dqs_ref, dks_ref, dvs_ref,
    )

    @pl.when(d == DOCS - 1)
    def _():
        gln_ref[...] = jnp.zeros_like(gln_ref)

        def tile(i, carry):
            rows = rows_of(i)
            grad_q, grad_kv = stream_grads(
                rows,
                (dq_ref, dk_ref, dv_ref),
                (dqs_ref, dks_ref, dvs_ref),
                (w0_ref, w1_ref),
                (w2_ref, w3_ref),
            )
            grad_norm, grad_gain, grad_shift = norm_backward(
                xq_ref[rows, :].astype(f32), norms_ref[0:1], grad_q
            )
            low_q = (g_ref[rows, :] + grad_norm).astype(bf16)
            gq_ref[rows, :] = low_q
            placed_q_ref[rows, :] = low_q.astype(f32)
            gln_ref[0:1, :] += grad_gain
            gln_ref[1:2, :] += grad_shift
            grad_norm, grad_gain, grad_shift = norm_backward(
                xc_ref[rows, :].astype(f32), norms_ref[2:3], grad_kv
            )
            low_c = grad_norm.astype(bf16)
            gc_ref[rows, :] = low_c
            placed_c_ref[rows, :] = low_c.astype(f32)
            gln_ref[2:3, :] += grad_gain
            gln_ref[3:4, :] += grad_shift
            return carry

        lax.fori_loop(0, TILES, tile, 0)


def place_rows(meta, *refs):
    count = len(refs) // 3
    for n in range(count):
        refs[2 * count + n][...] = refs[n][...].astype(refs[2 * count + n].dtype)


def join_cores(own, other, send):
    joined = own[...] + other[...].astype(f32)
    send[...] = joined.astype(bf16).reshape(send.shape)


def summed(parts, size, first):
    total = parts[0, first : first + size, :].astype(f32)
    for r in range(1, parts.shape[0]):
        total = total + parts[r, first : first + size, :].astype(f32)
    return total.astype(bf16)


def sum_rows(parts, send):
    count, size, _ = parts.shape
    total = summed(parts, size, 0)
    for r in range(count):
        send[r] = total


def sum_rows_join(parts, own, other, send):
    count, done, _ = parts.shape
    size = own.shape[0] // count
    total = summed(parts, done, 0)
    for r in range(count):
        rows = slice(size * r, size * r + size)
        send[r, 0:done, :] = total
        send[r, done : done + size, :] = (own[rows, :] + other[rows, :].astype(f32)).astype(bf16)


def sum_last(done, parts, gln_own, gln_other, send):
    count = parts.shape[0]
    size = parts.shape[1] - done
    total = summed(parts, size, done)
    gln = gln_own[...] + gln_other[...]
    gln = jnp.concatenate([gln, jnp.zeros((8, D), f32)], axis=0).astype(bf16)
    for r in range(count):
        send[r, 0:size, :] = total
        send[r, size : size + 16, :] = gln


def unpack_attention(parts, outs):
    count = parts.shape[0]
    size = D // count
    for r in range(count):
        rows = slice(size * r, size * r + size)
        for i in range(3):
            outs[i][rows, :] = parts[r, 0:size, 128 * i : 128 * i + 128].astype(f32)
        j, first = divmod(size * r, 128)
        outs[3][first : first + size, 128 * j : 128 * j + 128] = parts[r, 0:size, 384:512].astype(f32)


def unpack_early(ffn, cross, *outs):
    count, size, _ = ffn.shape
    for r in range(count):
        out = outs[2 * r // count]
        first = (size * r) % D
        out[first : first + size, :] = ffn[r].astype(f32)
    unpack_attention(cross, outs[2:])


def unpack_late(parts, *outs):
    unpack_attention(parts, outs[:4])
    size = parts.shape[1] - 16
    total = parts[0, size : size + 16, :].astype(f32)
    for r in range(1, parts.shape[0]):
        total = total + parts[r, size : size + 16, :].astype(f32)
    outs[4][...] = total[0:8]


def whole(shape):
    zeros = (0,) * len(shape)
    return pl.BlockSpec(shape, lambda d, meta: zeros)


def own_row(width):
    return pl.BlockSpec((SEQ, width), lambda d, meta: (meta[0], 0))


def columns(width, n):
    return pl.BlockSpec((SEQ, width), lambda d, meta: (0, n))


def raised_spec(heads, n):
    return pl.BlockSpec((1, heads, FAST_Q, FAST_K), lambda d, meta: (d, n, 0, 0))


def call(kernel, name, grid, operands, outs, scratch, flops):
    moved = sum(x.size * x.dtype.itemsize for x, _ in operands[1:])
    return pl.pallas_call(
        kernel,
        name=name,
        grid_spec=pltpu.PrefetchScalarGridSpec(
            num_scalar_prefetch=1,
            grid=(grid,),
            in_specs=[spec for _, spec in operands[1:]],
            out_specs=[spec for _, _, spec in outs],
            scratch_shapes=scratch,
        ),
        out_shape=[jax.ShapeDtypeStruct(shape, dtype) for shape, dtype, _ in outs],
        compiler_params=pltpu.CompilerParams(
            dimension_semantics=("arbitrary",), vmem_limit_bytes=56 * 1024 * 1024
        ),
        cost_estimate=pl.CostEstimate(
            flops=int(flops), bytes_accessed=int(moved), transcendentals=0
        ),
    )(*[x for x, _ in operands])


def simple(kernel, name, operands, outs):
    return pl.pallas_call(
        kernel,
        name=name,
        out_shape=[jax.ShapeDtypeStruct(shape, dtype) for shape, dtype in outs],
        compiler_params=pltpu.CompilerParams(vmem_limit_bytes=32 * 1024 * 1024),
    )(*operands)


def full(x):
    return (x, whole(x.shape))


def shards(
    query_stream,
    content_stream,
    memory,
    segment_ids,
    source_segments,
    context_rank,
    context_limit,
    padding,
    ln_query_gain,
    ln_query_bias,
    ln_content_gain,
    ln_content_bias,
    self_query,
    self_key,
    self_value,
    self_out,
    ln_cross_gain,
    ln_cross_bias,
    cross_query,
    cross_key,
    cross_value,
    cross_out,
    ln_ffn_gain,
    ln_ffn_bias,
    ffn_in,
    ffn_out,
    cotangent,
):
    core = lax.axis_index("heads") % 2

    def to_core(x):
        return lax.ppermute(x, "heads", [(h, h ^ 1) for h in range(4)])

    hold = lambda *xs: lax.optimization_barrier(xs)

    def to_chip(x):
        return lax.ppermute(x, "heads", [(h, h ^ 2) for h in range(4)])

    row = pl.BlockSpec((1, 8, 128), lambda d, core: (core[0], 0, 0))

    def token_row(x):
        return (x.reshape(2, 8, 128), row)

    def fixed(x):
        zeros = (0,) * x.ndim
        return (x, pl.BlockSpec(x.shape, lambda d, core: zeros))

    prepared = [
        ((33,), jnp.int32, pl.BlockSpec(memory_space=pltpu.SMEM)),
        ((1, SEQ), f32, whole((1, SEQ))),
        ((1, SEQ), f32, whole((1, SEQ))),
        ((8, D), f32, whole((8, D))),
        ((2048, 128), bf16, whole((2048, 128))),
        ((2048, 128), bf16, whole((2048, 128))),
    ]
    gains = (
        ln_query_gain,
        ln_query_bias,
        ln_content_gain,
        ln_content_bias,
        ln_cross_gain,
        ln_cross_bias,
        ln_ffn_gain,
        ln_ffn_bias,
    )
    weights = (self_query, self_key, self_value, self_out)
    weights += (cross_query, cross_key, cross_value, cross_out)
    tokens = (segment_ids, source_segments, context_rank, context_limit, padding)
    meta, rank, limit, norms, ws0, wc0 = call(
        prepare,
        "prepare",
        1,
        [(core.astype(jnp.int32)[None], None)]
        + [token_row(x) for x in tokens]
        + [fixed(x.reshape(1, D)) for x in gains]
        + [fixed(x) for x in weights],
        prepared,
        [],
        0,
    )

    ws1 = to_core(ws0)
    ws2 = to_chip(ws0)
    wc2 = to_chip(wc0)
    u0, u2 = ffn_in, to_chip(ffn_in)
    wf0, wf2 = ffn_out, to_chip(ffn_out)
    meta_in = (meta, None)
    xq = (query_stream, own_row(D))
    xc = (content_stream, own_row(D))
    mem = (memory, own_row(D))
    cot = (cotangent, own_row(D))

    def heads_out(width, heads):
        return [
            ((SEQ, width), bf16, whole((SEQ, width))),
            ((SEQ, width), bf16, whole((SEQ, width))),
            ((SEQ, width), bf16, whole((SEQ, width))),
            ((SEQ, width), bf16, whole((SEQ, width))),
            ((SEQ, width), f32, whole((SEQ, width))),
            ((DOCS, heads, FAST_Q, FAST_K), bf16, raised_spec(heads, 0)),
        ]

    def stream_out(dtype):
        return ((SEQ, D), dtype, whole((SEQ, D)))

    def placed(dtype):
        return ((2 * SEQ, D), dtype, own_row(D))

    limits = pltpu.VMEM((SEQ, 128), f32)
    pair_flops = 2 * SEQ * D * 768 + 2 * 2 * 4 * DOCS * FAST_Q * FAST_K * 256

    nq, nc, *first = call(
        self_first,
        "self_first",
        DOCS,
        [meta_in, xq, xc, full(rank), full(limit), full(norms), full(ws0), full(ws1)],
        [stream_out(bf16), stream_out(bf16)] + heads_out(256, 4),
        [limits],
        pair_flops,
    )
    ws2, wc0, nq = hold(ws2, wc0, nq)
    ws3 = to_core(ws2)
    wc1 = to_core(wc0)
    *second_heads, second, ncross = call(
        self_second,
        "self_second",
        DOCS,
        [meta_in, xq, full(nq), full(nc), full(rank), full(limit), full(norms)]
        + [full(w) for w in (ws0, ws1, ws2, ws3)]
        + [full(first[3])],
        heads_out(256, 4) + [stream_out(f32), stream_out(bf16)],
        [limits],
        pair_flops + 2 * SEQ * D * D,
    )
    wc2, u0, wf0, second = hold(wc2, u0, wf0, second)
    wc3 = to_core(wc2)
    u1 = to_core(u0)
    wf1 = to_core(wf0)
    *cross_heads, third, nffn = call(
        cross_forward,
        "cross_forward",
        DOCS,
        [meta_in, full(second), full(ncross), mem, full(norms)]
        + [full(w) for w in (wc0, wc1, wc2, wc3)],
        heads_out(512, 8) + [stream_out(f32), stream_out(bf16)],
        [],
        2 * pair_flops + 2 * SEQ * D * D,
    )
    u2, wf2, third = hold(u2, wf2, third)
    u3 = to_core(u2)
    wf3 = to_core(wf2)
    grads_ln = ((8, D), f32, whole((8, D)))
    placed_output, output, g3, gln_ffn, ffn_own, ffn_other = call(
        ffn_both,
        "ffn_both",
        TILES,
        [meta_in, full(third), full(nffn), cot, full(norms)]
        + [full(w) for w in (u0, u1, u2, u3, wf0, wf1, wf2, wf3)],
        [
            placed(bf16),
            stream_out(bf16),
            stream_out(f32),
            grads_ln,
            ((1024, D), f32, whole((1024, D))),
            ((1024, D), bf16, whole((1024, D))),
        ],
        [pltpu.VMEM((SEQ, 1024), bf16), pltpu.VMEM((SEQ, 1024), bf16)],
        12 * SEQ * D * 2048,
    )

    row_count = lax.axis_size("rows")

    def exchange(x):
        return lax.all_to_all(x, "rows", 0, 0)

    def chunks(n):
        return [((row_count, n, D), bf16)]

    size = 1024 // row_count
    half = size // 2
    (ffn_send,) = simple(join_cores, "join_ffn", [ffn_own, to_core(ffn_other)], chunks(size))
    g3, ffn_send = hold(g3, ffn_send)
    ffn_parts = exchange(ffn_send)

    back_scratch = [pltpu.VMEM((SEQ, 256), bf16)] + [pltpu.VMEM((SEQ, 256), f32)] * 3
    pair_out = ((SEQ, 256), bf16, whole((SEQ, 256)))
    packed_outs = [
        ((D, D), f32, whole((D, D))),
        ((D, D), bf16, whole((D, D))),
    ]
    back_flops = 2 * SEQ * D * 256 + 4 * 2 * 4 * DOCS * FAST_Q * FAST_K * 256

    def head_inputs(arrays, n):
        q, k, v, mixed, rt, e = arrays
        return [(x, columns(256, n)) for x in (q, k, v, mixed, rt)] + [(e, raised_spec(4, n))]

    *cross_grads, cross_own, cross_other = call(
        functools.partial(attention_back_first, True),
        "cross_back_first",
        DOCS,
        [meta_in, full(g3), full(ncross), mem, full(rank), full(limit), full(wc0), full(wc1)]
        + head_inputs(cross_heads, 0),
        [pair_out] * 3 + packed_outs,
        [limits] + back_scratch,
        back_flops + 2 * SEQ * D * 1024,
    )
    ffn_parts, cross_own = hold(ffn_parts, cross_own)
    (ffn_total,) = simple(sum_rows, "sum_ffn", [ffn_parts], chunks(size))
    ffn_total, cross_grads[0] = hold(ffn_total, cross_grads[0])
    ffn_sums = exchange(ffn_total)
    cross_other = to_core(cross_other)
    g2, placed_mem, grad_mem, gln_cross = call(
        cross_back_second,
        "cross_back_second",
        DOCS,
        [meta_in, full(g3), full(second), full(norms)]
        + [full(w) for w in (wc0, wc1, wc2, wc3)]
        + [full(x) for x in cross_grads]
        + head_inputs(cross_heads, 1),
        [stream_out(f32), placed(f32), stream_out(bf16), grads_ln],
        back_scratch,
        back_flops + 2 * SEQ * D * 1536,
    )
    ffn_sums, cross_other, g2 = hold(ffn_sums, cross_other, g2)
    (cross_send,) = simple(join_cores, "join_cross", [cross_own, cross_other], chunks(half))
    cross_send, g2 = hold(cross_send, g2)
    cross_parts = exchange(cross_send)

    *self_grads, self_own, self_other = call(
        functools.partial(attention_back_first, False),
        "self_back_first",
        DOCS,
        [meta_in, full(g2), full(nq), full(nc), full(rank), full(limit), full(ws0), full(ws1)]
        + head_inputs(first, 0),
        [pair_out] * 3 + packed_outs,
        [limits] + back_scratch,
        back_flops + 2 * SEQ * D * 1024,
    )
    self_other = to_core(self_other)
    cross_parts, self_own = hold(cross_parts, self_own)
    (both_send,) = simple(
        sum_rows_join, "sum_cross", [cross_parts, self_own, self_other], chunks(2 * half)
    )
    both_send, g2 = hold(both_send, g2)
    both_parts = exchange(both_send)
    placed_q, placed_c, gq, gc, gln_self = call(
        self_back_second,
        "self_back_second",
        DOCS,
        [meta_in, full(g2), xq, xc, full(rank), full(limit), full(norms)]
        + [full(w) for w in (ws0, ws1, ws2, ws3)]
        + [full(x) for x in self_grads]
        + head_inputs(second_heads, 0),
        [placed(f32), placed(f32), stream_out(bf16), stream_out(bf16), grads_ln],
        [limits] + back_scratch,
        back_flops + 2 * SEQ * D * 1536,
    )

    gln = jnp.concatenate([gln_self[0:4], gln_cross[0:2], gln_ffn[0:2]], axis=0)
    both_parts, gln = hold(both_parts, gln)
    (last_send,) = simple(
        functools.partial(sum_last, half), "sum_self", [both_parts, gln, to_core(gln)], chunks(half + 16)
    )
    last_parts = exchange(last_send)

    def both_rows(placed_own, arrays, name):
        count = len(arrays)
        size = SEQ // 2
        one = pl.BlockSpec((size, D), lambda i, meta: (i, 0))
        block = pl.BlockSpec((size, D), lambda i, meta: (2 * (1 - meta[0]) + i, 0))
        return pl.pallas_call(
            place_rows,
            name=name,
            grid_spec=pltpu.PrefetchScalarGridSpec(
                num_scalar_prefetch=1,
                grid=(2,),
                in_specs=[one] * count + [pl.BlockSpec(memory_space=pl.ANY)] * count,
                out_specs=[block] * count,
            ),
            out_shape=[jax.ShapeDtypeStruct(x.shape, x.dtype) for x in placed_own],
            input_output_aliases={1 + count + n: n for n in range(count)},
        )(meta, *[to_core(x) for x in arrays], *placed_own)

    out_both, grad_mem_both = both_rows([placed_output, placed_mem], [output, grad_mem], "place_early")
    gq_both, gc_both = both_rows([placed_q, placed_c], [gq, gc], "place_late")

    attention_outs = [((512, 128), f32)] * 3 + [((128, 512), f32)]
    grad_ffn_in, grad_ffn_out, *grad_cross_parts = simple(
        unpack_early, "unpack_early", [ffn_sums, both_parts], [((D, D), f32)] * 2 + attention_outs
    )
    *grad_self_parts, gln = simple(
        unpack_late, "unpack_late", [last_parts], attention_outs + [((8, D), f32)]
    )
    return (
        out_both,
        gq_both,
        gc_both,
        grad_mem_both,
        gln[0],
        gln[1],
        gln[2],
        gln[3],
        *grad_self_parts,
        gln[4],
        gln[5],
        *grad_cross_parts,
        gln[6],
        gln[7],
        grad_ffn_in,
        grad_ffn_out,
    )


def solution(mesh):
    assert mesh.shape["heads"] == 4
    row_spec = P("rows", None)
    flat = P("rows")
    by_column = P(None, "heads")
    by_row = P("heads", None)
    attention = (by_column, by_column, by_column, by_row)
    in_specs = (
        (row_spec,) * 3
        + (flat,) * 5
        + (P(),) * 4
        + attention
        + (P(),) * 2
        + attention
        + (P(),) * 2
        + (by_column, by_row, row_spec)
    )
    out_specs = (
        (row_spec,) * 4
        + (P(),) * 4
        + attention
        + (P(),) * 2
        + attention
        + (P(),) * 2
        + (by_column, by_row)
    )
    return jax.shard_map(shards, mesh=mesh, in_specs=in_specs, out_specs=out_specs, check_vma=False)
```

```python
import functools

import jax
import jax.numpy as jnp
from jax import lax
from jax.experimental import pallas as pl
from jax.experimental.pallas import tpu as pltpu
from jax.sharding import PartitionSpec as P

HEAD_DIM = 64
SEQ = 1024
DOCS = 8
D = 512
TILE = 256
TILES = SEQ // TILE
FAST_Q = 256
FAST_K = 208
LONG_Q = 128
LONG_K = 640

norm_eps = 1e-05
masked_score = -1e30
hidden_rank = 1e6
gelu_root = 0.7978845608028654
gelu_cube = 0.044715

f32 = jnp.float32
bf16 = jnp.bfloat16


def dot(a, b):
    return lax.dot_general(a, b, (((1,), (0,)), ((), ())), preferred_element_type=f32)


def dot_nt(a, b):
    return lax.dot_general(a, b, (((1,), (1,)), ((), ())), preferred_element_type=f32)


def dot_tn(a, b):
    return lax.dot_general(a, b, (((0,), (0,)), ((), ())), preferred_element_type=f32)


def lanes(parts):
    return jnp.concatenate(parts, axis=1)


def layer_norm(values, gain, shift):
    centre = values - jnp.mean(values, axis=-1, keepdims=True)
    spread = jnp.mean(centre * centre, axis=-1, keepdims=True)
    return centre * lax.rsqrt(spread + norm_eps) * gain + shift


def norm_backward(values, gain, grad):
    centre = values - jnp.mean(values, axis=-1, keepdims=True)
    spread = jnp.mean(centre * centre, axis=-1, keepdims=True)
    scale = lax.rsqrt(spread + norm_eps)
    xhat = centre * scale
    eg = grad * gain
    mean_eg = jnp.mean(eg, axis=-1, keepdims=True)
    mean_egx = jnp.mean(eg * xhat, axis=-1, keepdims=True)
    grad_gain = jnp.sum(grad * xhat, axis=0, keepdims=True)
    grad_shift = jnp.sum(grad, axis=0, keepdims=True)
    return scale * (eg - mean_eg - xhat * mean_egx), grad_gain, grad_shift


def rows_of(i, size=TILE):
    return pl.ds(pl.multiple_of(i * size, size), size)


def w_query(ref):
    return ref[0:512, :]


def w_key(ref):
    return ref[512:1024, :]


def w_value(ref):
    return ref[1024:1536, :]


def w_out(ref):
    return lanes([ref[1536 + 128 * j : 1664 + 128 * j, :] for j in range(4)])


def half_masks():
    place = lax.broadcasted_iota(jnp.int32, (1, 128), 1)
    low = jnp.where(place < HEAD_DIM, 1.0, 0.0).astype(f32)
    return (low.astype(bf16), (1.0 - low).astype(bf16))


def doc_bounds(meta, d, source):
    base = 17 if source else 1
    return meta[base + d], meta[base + 8 + d]


def window_of(first, limit):
    return pl.multiple_of(jnp.minimum((first // 16) * 16, limit), 16)


def key_bias(ks, ke, k0, width):
    place = k0 + lax.broadcasted_iota(jnp.int32, (width, 128), 0)
    return jnp.where((place >= ks) & (place < ke), 0.0, masked_score)


def make_bias(rank_ref, limit_ref, ks, ke, q0, k0, span, width):
    if rank_ref is None:
        return lanes([key_bias(ks, ke, k0, width)] * (span // 128))
    place = k0 + lax.broadcasted_iota(jnp.int32, (width, 128), 0)
    ranks = rank_ref[pl.ds(k0, width), :]
    ranks = jnp.where((place < ks + 2) & (ranks < hidden_rank), -1.0, ranks)
    ranks = jnp.where((place >= ks) & (place < ke), ranks, hidden_rank)
    limits = jnp.broadcast_to(limit_ref[...], (8, SEQ))
    limits = pltpu.roll(limits, lax.rem(SEQ - q0, SEQ), 1)[0:1, 0:span]
    row = k0 + lax.broadcasted_iota(jnp.int32, (width, span), 0)
    column = q0 + lax.broadcasted_iota(jnp.int32, (width, span), 1)
    seen = (lanes([ranks] * (span // 128)) < limits) & (row != column)
    return jnp.where(seen, 0.0, masked_score)


def both_heads(x, masks):
    return jnp.concatenate([x * masks[0], x * masks[1]], axis=0)


def pair_probabilities(queries, keys, masks, bias):
    width = keys.shape[0]
    scores = dot_nt(both_heads(keys, masks), queries)
    result = []
    for a in range(2):
        part = scores[width * a : width * a + width] + bias
        part = jnp.exp(part - jnp.max(part, axis=0, keepdims=True))
        part = part * (1.0 / jnp.sum(part, axis=0, keepdims=True))
        result.append(part.astype(bf16))
    return result


def pair_product(rows, parts):
    across = jnp.transpose(rows)
    halves = [dot(across[64 * a : 64 * a + 64], part) for a, part in enumerate(parts)]
    return jnp.transpose(jnp.concatenate(halves, axis=0))


def for_docs(meta, cross, run):
    fast = meta[34 if cross else 33] == 1

    @pl.when(fast)
    def _():
        def doc(d, carry):
            ts, te = doc_bounds(meta, d, False)
            ks, ke = doc_bounds(meta, d, cross)
            q0 = window_of(ts, SEQ - FAST_Q)
            k0 = window_of(ks, SEQ - FAST_K)
            run(d, q0, k0, FAST_Q, FAST_K, ts, te, ks, ke, True)
            return carry

        lax.fori_loop(0, DOCS, doc, 0, unroll=2)

    @pl.when(jnp.logical_not(fast))
    def _():
        def doc(d, carry):
            ts, te = doc_bounds(meta, d, False)
            ks, ke = doc_bounds(meta, d, cross)
            base = (ts // 16) * 16
            k0 = window_of(ks, SEQ - LONG_K)

            def chunk(i, carry):
                lower = base + i * LONG_Q
                q0 = pl.multiple_of(jnp.minimum(lower, SEQ - LONG_Q), 16)
                low = jnp.maximum(ts, lower)
                high = jnp.minimum(te, lower + LONG_Q)
                run(d, q0, k0, LONG_Q, LONG_K, low, high, ks, ke, False)
                return carry

            return lax.fori_loop(0, (te - base + LONG_Q - 1) // LONG_Q, chunk, carry)

        lax.fori_loop(0, DOCS, doc, 0)


def attend_docs(meta, cross, rank_ref, limit_ref, q_ref, k_ref, v_ref, p_ref, mixed_ref):
    pairs = q_ref.shape[1] // 128
    masks = half_masks()

    def run(d, q0, k0, span, width, low, high, ks, ke, fast):
        bias = make_bias(rank_ref, limit_ref, ks, ke, q0, k0, span, width)
        row = q0 + lax.broadcasted_iota(jnp.int32, (span, 128), 0)
        inside = (row >= low) & (row < high)
        for n in range(pairs):
            cols = slice(128 * n, 128 * n + 128)
            queries = q_ref[pl.ds(q0, span), cols]
            keys = k_ref[pl.ds(k0, width), cols]
            values = v_ref[pl.ds(k0, width), cols]
            parts = pair_probabilities(queries, keys, masks, bias)
            if fast:
                for a in range(2):
                    p_ref[d, 2 * n + a] = parts[a]
            mixed = pair_product(values, parts)
            old = mixed_ref[pl.ds(q0, span), cols].astype(f32)
            mixed_ref[pl.ds(q0, span), cols] = jnp.where(inside, mixed, old).astype(bf16)

    for_docs(meta, cross, run)


def attend_docs_back(
    meta, cross, rank_ref, limit_ref, q_ref, k_ref, v_ref, p_ref, mixed_ref, dm_ref,
    dq_ref, dk_ref, dv_ref,
):
    pairs = q_ref.shape[1] // 128
    masks = half_masks()

    def run(d, q0, k0, span, width, low, high, ks, ke, fast):
        row = q0 + lax.broadcasted_iota(jnp.int32, (span, 128), 0)
        inside = (row >= low) & (row < high)
        ones = jnp.ones((width, 128), bf16)
        if not fast:
            bias = make_bias(rank_ref, limit_ref, ks, ke, q0, k0, span, width)
        for n in range(pairs):
            cols = slice(128 * n, 128 * n + 128)
            queries = q_ref[pl.ds(q0, span), cols]
            keys = k_ref[pl.ds(k0, width), cols]
            values = v_ref[pl.ds(k0, width), cols]
            mixed = mixed_ref[pl.ds(q0, span), cols].astype(f32)
            grad = jnp.where(inside, dm_ref[pl.ds(q0, span), cols].astype(f32), 0.0)
            low_grad = grad.astype(bf16)
            left = lanes([low_grad, (-(grad * mixed)).astype(bf16)])
            delta = dot_nt(both_heads(lanes([values, ones]), [lanes([m, m]) for m in masks]), left)
            if fast:
                parts = [p_ref[d, 2 * n + a] for a in range(2)]
            else:
                parts = pair_probabilities(queries, keys, masks, bias)
            slopes = []
            dk = dv = None
            for a in range(2):
                slope = parts[a].astype(f32) * delta[width * a : width * a + width]
                slopes.append(slope.astype(bf16))
                dk_a = dot(slopes[a], queries * masks[a])
                dv_a = dot(parts[a], low_grad * masks[a])
                dk = dk_a if dk is None else dk + dk_a
                dv = dv_a if dv is None else dv + dv_a
            dq = pair_product(keys, slopes)
            dq_ref[pl.ds(q0, span), cols] += dq * (HEAD_DIM**-0.5)
            dk_ref[pl.ds(k0, width), cols] += dk
            dv_ref[pl.ds(k0, width), cols] += dv

    for_docs(meta, cross, run)


def spread_ranks(rank_row_ref, rank_ref):
    rank_ref[...] = jnp.transpose(jnp.broadcast_to(rank_row_ref[...], (128, SEQ)))


def prepare(
    core, seg_ref, src_ref, rank_ref, limit_ref, pad_ref,
    n0, n1, n2, n3, n4, n5, n6, n7, sq, sk, sv, so, cq, ck, cv, co,
    meta_ref, ranks_ref, limits_ref, norms_ref, ws_ref, wc_ref,
):
    meta_ref[0] = core[0]
    for base, ref in ((1, seg_ref), (17, src_ref)):
        ids = ref[0]
        meta_ref[base] = 0
        meta_ref[base + 15] = SEQ
        for d in range(1, DOCS):
            cut = jnp.sum(jnp.where(ids < d, 1.0, 0.0)).astype(jnp.int32)
            meta_ref[base + d] = cut
            meta_ref[base + 7 + d] = cut
    for place, base in ((33, 1), (34, 17)):
        fast = jnp.int32(1)
        for d in range(DOCS):
            q0 = window_of(meta_ref[1 + d], SEQ - FAST_Q)
            k0 = window_of(meta_ref[base + d], SEQ - FAST_K)
            fits = (meta_ref[9 + d] - q0 <= FAST_Q) & (meta_ref[base + 8 + d] - k0 <= FAST_K)
            fast = fast & fits.astype(jnp.int32)
        meta_ref[place] = fast
    ranks = jnp.where(pad_ref[0] != 0, hidden_rank, rank_ref[0].astype(f32))
    limits = limit_ref[0].astype(f32)
    for i in range(8):
        ranks_ref[0:1, 128 * i : 128 * i + 128] = ranks[i : i + 1]
        limits_ref[0:1, 128 * i : 128 * i + 128] = limits[i : i + 1]
    for i, ref in enumerate((n0, n1, n2, n3, n4, n5, n6, n7)):
        norms_ref[i : i + 1, :] = ref[...]
    for to, parts, out in ((ws_ref, (sq, sk, sv), so), (wc_ref, (cq, ck, cv), co)):
        for i, part in enumerate(parts):
            to[512 * i : 512 * i + 512, :] = part[...]
        for j in range(4):
            to[1536 + 128 * j : 1664 + 128 * j, :] = out[:, 128 * j : 128 * j + 128]


def self_first(
    meta, xq_ref, xc_ref, rank_row_ref, limit_ref, norms_ref, w0_ref, w1_ref,
    nq_ref, nc_ref, q_ref, k_ref, v_ref, mixed_ref, p_ref, rank_ref,
):

    spread_ranks(rank_row_ref, rank_ref)
    wq = lanes([w_query(w0_ref), w_query(w1_ref)])
    wkv = lanes([w_key(w0_ref), w_key(w1_ref), w_value(w0_ref), w_value(w1_ref)])

    def tile(i, carry):
        rows = rows_of(i)
        nq = layer_norm(xq_ref[rows, :].astype(f32), norms_ref[0:1], norms_ref[1:2]).astype(bf16)
        nc = layer_norm(xc_ref[rows, :].astype(f32), norms_ref[2:3], norms_ref[3:4]).astype(bf16)
        nq_ref[rows, :] = nq
        nc_ref[rows, :] = nc
        q_ref[rows, :] = (dot(nq, wq) * (HEAD_DIM**-0.5)).astype(bf16)
        kv = dot(nc, wkv).astype(bf16)
        k_ref[rows, :] = kv[:, :256]
        v_ref[rows, :] = kv[:, 256:]
        return carry

    lax.fori_loop(0, TILES, tile, 0)

    attend_docs(meta, False, rank_ref, limit_ref, q_ref, k_ref, v_ref, p_ref, mixed_ref)


def self_second(
    meta, xq_ref, nq_ref, nc_ref, rank_row_ref, limit_ref, norms_ref, w0_ref, w1_ref, w2_ref, w3_ref,
    mixed_first_ref,
    q_ref, k_ref, v_ref, mixed_ref, p_ref, second_ref, ncross_ref, rank_ref,
):

    spread_ranks(rank_row_ref, rank_ref)
    wq = lanes([w_query(w2_ref), w_query(w3_ref)])
    wkv = lanes([w_key(w2_ref), w_key(w3_ref), w_value(w2_ref), w_value(w3_ref)])

    def tile(i, carry):
        rows = rows_of(i)
        q_ref[rows, :] = (dot(nq_ref[rows, :], wq) * (HEAD_DIM**-0.5)).astype(bf16)
        kv = dot(nc_ref[rows, :], wkv).astype(bf16)
        k_ref[rows, :] = kv[:, :256]
        v_ref[rows, :] = kv[:, 256:]
        return carry

    lax.fori_loop(0, TILES, tile, 0)

    attend_docs(meta, False, rank_ref, limit_ref, q_ref, k_ref, v_ref, p_ref, mixed_ref)

    out_first = jnp.concatenate([w_out(w0_ref), w_out(w1_ref)], axis=0)
    out_second = jnp.concatenate([w_out(w2_ref), w_out(w3_ref)], axis=0)

    def tile(i, carry):
        rows = rows_of(i)
        branch = dot(mixed_first_ref[rows, :], out_first) + dot(mixed_ref[rows, :], out_second)
        second = xq_ref[rows, :].astype(f32) + branch
        second_ref[rows, :] = second
        ncross_ref[rows, :] = layer_norm(second, norms_ref[4:5], norms_ref[5:6]).astype(bf16)
        return carry

    lax.fori_loop(0, TILES, tile, 0)


def cross_forward(
    meta, second_ref, ncross_ref, memory_ref, norms_ref, w0_ref, w1_ref, w2_ref, w3_ref,
    q_ref, k_ref, v_ref, mixed_ref, p_ref, third_ref, nffn_ref,
):
    weights = (w0_ref, w1_ref, w2_ref, w3_ref)

    wq = lanes([w_query(w) for w in weights])
    wk = lanes([w_key(w) for w in weights])
    wv = lanes([w_value(w) for w in weights])

    def tile(i, carry):
        rows = rows_of(i)
        memory = memory_ref[rows, :]
        q_ref[rows, :] = (dot(ncross_ref[rows, :], wq) * (HEAD_DIM**-0.5)).astype(bf16)
        k_ref[rows, :] = dot(memory, wk).astype(bf16)
        v_ref[rows, :] = dot(memory, wv).astype(bf16)
        return carry

    lax.fori_loop(0, TILES, tile, 0)

    attend_docs(meta, True, None, None, q_ref, k_ref, v_ref, p_ref, mixed_ref)

    out_first = jnp.concatenate([w_out(w0_ref), w_out(w1_ref)], axis=0)
    out_second = jnp.concatenate([w_out(w2_ref), w_out(w3_ref)], axis=0)

    def tile(i, carry):
        rows = rows_of(i)
        mixed = mixed_ref[rows, :]
        branch = dot(mixed[:, :256], out_first) + dot(mixed[:, 256:], out_second)
        third = second_ref[rows, :] + branch
        third_ref[rows, :] = third
        nffn_ref[rows, :] = layer_norm(third, norms_ref[6:7], norms_ref[7:8]).astype(bf16)
        return carry

    lax.fori_loop(0, TILES, tile, 0)


def ffn_both(
    meta, third_ref, nffn_ref, cot_ref, norms_ref, u0_ref, u1_ref, u2_ref, u3_ref,
    w0_ref, w1_ref, w2_ref, w3_ref,
    placed_ref, out_ref, g3_ref, gln_ref, own_ref, other_ref, hidden_ref, before_ref,
):
    i = pl.program_id(0)
    rows = rows_of(i)
    nffn = nffn_ref[rows, :]
    cot = cot_ref[rows, :]
    outs = []
    grads = []
    in_refs = (u0_ref, u1_ref, u2_ref, u3_ref)
    for g, w_ref in enumerate((w0_ref, w1_ref, w2_ref, w3_ref)):
        w_in = in_refs[g][...]
        w_out_rows = w_ref[...]
        x = dot(nffn, w_in)
        square = x * x
        half = 0.5 + 0.5 * jnp.tanh(x * (gelu_root + (gelu_root * gelu_cube) * square))
        value = x * half
        hidden = value.astype(bf16)
        rise = 2.0 * gelu_root + (6.0 * gelu_root * gelu_cube) * square
        slope = half + value * (1.0 - half) * rise
        grad_before = (dot_nt(cot, w_out_rows) * slope).astype(bf16)
        outs.append(dot(hidden, w_out_rows))
        grads.append(dot_nt(grad_before, w_in))
        if g < 2:
            hidden_ref[rows, 512 * g : 512 * g + 512] = hidden
            before_ref[rows, 512 * g : 512 * g + 512] = grad_before
    third = third_ref[rows, :]
    out = (third + ((outs[0] + outs[1]) + (outs[2] + outs[3]))).astype(bf16)
    out_ref[rows, :] = out
    placed_ref[rows, :] = out
    grad_normed = (grads[0] + grads[1]) + (grads[2] + grads[3])
    grad_norm, grad_gain, grad_shift = norm_backward(third, norms_ref[6:7], grad_normed)
    g3_ref[rows, :] = cot.astype(f32) + grad_norm

    @pl.when(i == 0)
    def _():
        gln_ref[0:1, :] = grad_gain
        gln_ref[1:2, :] = grad_shift

    @pl.when(i > 0)
    def _():
        gln_ref[0:1, :] += grad_gain
        gln_ref[1:2, :] += grad_shift

    @pl.when(i == TILES - 1)
    def _():
        nffn_all = nffn_ref[...]
        cot_all = cot_ref[...]
        part = dot_tn(nffn_all, before_ref[...])
        own_ref[0:512, :] = part[:, 0:512]
        other_ref[0:512, :] = part[:, 512:1024].astype(bf16)
        part = dot_tn(hidden_ref[...], cot_all)
        own_ref[512:1024, :] = part[0:512]
        other_ref[512:1024, :] = part[512:1024].astype(bf16)


def back_start(g_ref, mixed_ref, w_refs, dm_ref, dq_ref, dk_ref, dv_ref):
    out_rows = jnp.concatenate([w_out(w) for w in w_refs], axis=0)

    def tile(i, carry):
        rows = rows_of(i)
        dm_ref[rows, :] = dot_nt(g_ref[rows, :].astype(bf16), out_rows).astype(bf16)
        zeros = jnp.zeros((TILE, 256), f32)
        dq_ref[rows, :] = zeros
        dk_ref[rows, :] = zeros
        dv_ref[rows, :] = zeros
        return carry

    lax.fori_loop(0, TILES, tile, 0)


def attention_back_first(
    cross, meta, g_ref, nq_ref, nkv_ref, rank_row_ref, limit_ref, w0_ref, w1_ref,
    q_ref, k_ref, v_ref, mixed_ref, p_ref,
    dq_ref, dk_ref, dv_ref, own_ref, other_ref,
    rank_ref, dm_ref, dqs_ref, dks_ref, dvs_ref,
):

    if not cross:
        spread_ranks(rank_row_ref, rank_ref)
    back_start(g_ref, mixed_ref, (w0_ref, w1_ref), dm_ref, dqs_ref, dks_ref, dvs_ref)

    attend_docs_back(
        meta, cross, None if cross else rank_ref, limit_ref, q_ref, k_ref, v_ref, p_ref, mixed_ref,
        dm_ref, dqs_ref, dks_ref, dvs_ref,
    )

    dq_ref[...] = dqs_ref[...].astype(bf16)
    dk_ref[...] = dks_ref[...].astype(bf16)
    dv_ref[...] = dvs_ref[...].astype(bf16)
    nq = nq_ref[...]
    nkv = nkv_ref[...]
    for n, part in enumerate(
        (dot_tn(nq, dq_ref[...]), dot_tn(nkv, dk_ref[...]), dot_tn(nkv, dv_ref[...]))
    ):
        own_ref[:, 128 * n : 128 * n + 128] = part[:, :128]
        other_ref[:, 128 * n : 128 * n + 128] = part[:, 128:].astype(bf16)
    part = dot_tn(mixed_ref[...], g_ref[...].astype(bf16))
    for j in range(4):
        rows = slice(128 * j, 128 * j + 128)
        own_ref[rows, 384:512] = part[:128, rows]
        other_ref[rows, 384:512] = part[128:, rows].astype(bf16)


def back_second_docs(
    cross, meta, g_ref, rank_row_ref, limit_ref, w_refs, q_ref, k_ref, v_ref, mixed_ref, p_ref,
    rank_ref, dm_ref, dqs_ref, dks_ref, dvs_ref,
):

    if not cross:
        spread_ranks(rank_row_ref, rank_ref)
    back_start(g_ref, mixed_ref, w_refs, dm_ref, dqs_ref, dks_ref, dvs_ref)

    attend_docs_back(
        meta, cross, None if cross else rank_ref, limit_ref, q_ref, k_ref, v_ref, p_ref, mixed_ref,
        dm_ref, dqs_ref, dks_ref, dvs_ref,
    )


def stream_grads(rows, first, second, firsts, seconds):
    dq, dk, dv = first
    dq2, dk2, dv2 = (ref[rows, :].astype(bf16) for ref in second)
    w0, w1 = firsts
    w2, w3 = seconds
    grad_q = dot_nt(dq[rows, :], lanes([w_query(w0), w_query(w1)])) + dot_nt(
        dq2, lanes([w_query(w2), w_query(w3)])
    )
    kv = lanes([dk[rows, :], dv[rows, :]])
    kv2 = lanes([dk2, dv2])
    grad_kv = dot_nt(kv, lanes([w_key(w0), w_key(w1), w_value(w0), w_value(w1)])) + dot_nt(
        kv2, lanes([w_key(w2), w_key(w3), w_value(w2), w_value(w3)])
    )
    return grad_q, grad_kv


def cross_back_second(
    meta, g_ref, second_ref, norms_ref, w0_ref, w1_ref, w2_ref, w3_ref,
    dq_ref, dk_ref, dv_ref, q_ref, k_ref, v_ref, mixed_ref, p_ref,
    g2_ref, placed_ref, gmem_ref, gln_ref,
    dm_ref, dqs_ref, dks_ref, dvs_ref,
):
    back_second_docs(
        True, meta, g_ref, None, None, (w2_ref, w3_ref), q_ref, k_ref, v_ref, mixed_ref, p_ref,
        None, dm_ref, dqs_ref, dks_ref, dvs_ref,
    )

    gln_ref[...] = jnp.zeros_like(gln_ref)

    def tile(i, carry):
        rows = rows_of(i)
        grad_q, grad_kv = stream_grads(
            rows,
            (dq_ref, dk_ref, dv_ref),
            (dqs_ref, dks_ref, dvs_ref),
            (w0_ref, w1_ref),
            (w2_ref, w3_ref),
        )
        low_kv = grad_kv.astype(bf16)
        gmem_ref[rows, :] = low_kv
        placed_ref[rows, :] = low_kv.astype(f32)
        grad_norm, grad_gain, grad_shift = norm_backward(
            second_ref[rows, :], norms_ref[4:5], grad_q
        )
        g2_ref[rows, :] = g_ref[rows, :] + grad_norm
        gln_ref[0:1, :] += grad_gain
        gln_ref[1:2, :] += grad_shift
        return carry

    lax.fori_loop(0, TILES, tile, 0)


def self_back_second(
    meta, g_ref, xq_ref, xc_ref, rank_row_ref, limit_ref, norms_ref, w0_ref, w1_ref, w2_ref, w3_ref,
    dq_ref, dk_ref, dv_ref, q_ref, k_ref, v_ref, mixed_ref, p_ref,
    placed_q_ref, placed_c_ref, gq_ref, gc_ref, gln_ref,
    rank_ref, dm_ref, dqs_ref, dks_ref, dvs_ref,
):
    back_second_docs(
        False, meta, g_ref, rank_row_ref, limit_ref, (w2_ref, w3_ref), q_ref, k_ref, v_ref, mixed_ref,
        p_ref, rank_ref, dm_ref, dqs_ref, dks_ref, dvs_ref,
    )

    gln_ref[...] = jnp.zeros_like(gln_ref)

    def tile(i, carry):
        rows = rows_of(i)
        grad_q, grad_kv = stream_grads(
            rows,
            (dq_ref, dk_ref, dv_ref),
            (dqs_ref, dks_ref, dvs_ref),
            (w0_ref, w1_ref),
            (w2_ref, w3_ref),
        )
        grad_norm, grad_gain, grad_shift = norm_backward(
            xq_ref[rows, :].astype(f32), norms_ref[0:1], grad_q
        )
        low_q = (g_ref[rows, :] + grad_norm).astype(bf16)
        gq_ref[rows, :] = low_q
        placed_q_ref[rows, :] = low_q.astype(f32)
        gln_ref[0:1, :] += grad_gain
        gln_ref[1:2, :] += grad_shift
        grad_norm, grad_gain, grad_shift = norm_backward(
            xc_ref[rows, :].astype(f32), norms_ref[2:3], grad_kv
        )
        low_c = grad_norm.astype(bf16)
        gc_ref[rows, :] = low_c
        placed_c_ref[rows, :] = low_c.astype(f32)
        gln_ref[2:3, :] += grad_gain
        gln_ref[3:4, :] += grad_shift
        return carry

    lax.fori_loop(0, TILES, tile, 0)


def place_rows(meta, *refs):
    count = len(refs) // 3
    for n in range(count):
        refs[2 * count + n][...] = refs[n][...].astype(refs[2 * count + n].dtype)


def join_cores(own, other, send):
    joined = own[...] + other[...].astype(f32)
    send[...] = joined.astype(bf16).reshape(send.shape)


def summed(parts, size, first):
    total = parts[0, first : first + size, :].astype(f32)
    for r in range(1, parts.shape[0]):
        total = total + parts[r, first : first + size, :].astype(f32)
    return total.astype(bf16)


def sum_rows(parts, send):
    count, size, _ = parts.shape
    total = summed(parts, size, 0)
    for r in range(count):
        send[r] = total


def sum_rows_join(parts, own, other, send):
    count, done, _ = parts.shape
    size = own.shape[0] // count
    total = summed(parts, done, 0)
    for r in range(count):
        rows = slice(size * r, size * r + size)
        send[r, 0:done, :] = total
        send[r, done : done + size, :] = (own[rows, :] + other[rows, :].astype(f32)).astype(bf16)


def sum_last(done, parts, gln_own, gln_other, send):
    count = parts.shape[0]
    size = parts.shape[1] - done
    total = summed(parts, size, done)
    gln = gln_own[...] + gln_other[...]
    gln = jnp.concatenate([gln, jnp.zeros((8, D), f32)], axis=0).astype(bf16)
    for r in range(count):
        send[r, 0:size, :] = total
        send[r, size : size + 16, :] = gln


def unpack_attention(parts, outs):
    count = parts.shape[0]
    size = D // count
    for r in range(count):
        rows = slice(size * r, size * r + size)
        for i in range(3):
            outs[i][rows, :] = parts[r, 0:size, 128 * i : 128 * i + 128].astype(f32)
        j, first = divmod(size * r, 128)
        outs[3][first : first + size, 128 * j : 128 * j + 128] = parts[r, 0:size, 384:512].astype(f32)


def unpack_early(ffn, cross, *outs):
    count, size, _ = ffn.shape
    for r in range(count):
        out = outs[2 * r // count]
        first = (size * r) % D
        out[first : first + size, :] = ffn[r].astype(f32)
    unpack_attention(cross, outs[2:])


def unpack_late(parts, *outs):
    unpack_attention(parts, outs[:4])
    size = parts.shape[1] - 16
    total = parts[0, size : size + 16, :].astype(f32)
    for r in range(1, parts.shape[0]):
        total = total + parts[r, size : size + 16, :].astype(f32)
    outs[4][...] = total[0:8]


def whole(shape):
    zeros = (0,) * len(shape)
    return pl.BlockSpec(shape, lambda d, meta: zeros)


def own_row(width):
    return pl.BlockSpec((SEQ, width), lambda d, meta: (meta[0], 0))


def columns(width, n):
    return pl.BlockSpec((SEQ, width), lambda d, meta: (0, n))


def probability_spec(heads, n):
    return pl.BlockSpec((DOCS, heads, FAST_K, FAST_Q), lambda d, meta: (0, n, 0, 0))


def call(kernel, name, grid, operands, outs, scratch, flops):
    moved = sum(x.size * x.dtype.itemsize for x, _ in operands[1:])
    return pl.pallas_call(
        kernel,
        name=name,
        grid_spec=pltpu.PrefetchScalarGridSpec(
            num_scalar_prefetch=1,
            grid=(grid,),
            in_specs=[spec for _, spec in operands[1:]],
            out_specs=[spec for _, _, spec in outs],
            scratch_shapes=scratch,
        ),
        out_shape=[jax.ShapeDtypeStruct(shape, dtype) for shape, dtype, _ in outs],
        compiler_params=pltpu.CompilerParams(
            dimension_semantics=("arbitrary",), vmem_limit_bytes=56 * 1024 * 1024
        ),
        cost_estimate=pl.CostEstimate(
            flops=int(flops), bytes_accessed=int(moved), transcendentals=0
        ),
    )(*[x for x, _ in operands])


def simple(kernel, name, operands, outs):
    return pl.pallas_call(
        kernel,
        name=name,
        out_shape=[jax.ShapeDtypeStruct(shape, dtype) for shape, dtype in outs],
        compiler_params=pltpu.CompilerParams(vmem_limit_bytes=32 * 1024 * 1024),
    )(*operands)


def full(x):
    return (x, whole(x.shape))


def shards(
    query_stream,
    content_stream,
    memory,
    segment_ids,
    source_segments,
    context_rank,
    context_limit,
    padding,
    ln_query_gain,
    ln_query_bias,
    ln_content_gain,
    ln_content_bias,
    self_query,
    self_key,
    self_value,
    self_out,
    ln_cross_gain,
    ln_cross_bias,
    cross_query,
    cross_key,
    cross_value,
    cross_out,
    ln_ffn_gain,
    ln_ffn_bias,
    ffn_in,
    ffn_out,
    cotangent,
):
    core = lax.axis_index("heads") % 2

    def to_core(x):
        return lax.ppermute(x, "heads", [(h, h ^ 1) for h in range(4)])

    hold = lambda *xs: lax.optimization_barrier(xs)

    def to_chip(x):
        return lax.ppermute(x, "heads", [(h, h ^ 2) for h in range(4)])

    row = pl.BlockSpec((1, 8, 128), lambda d, core: (core[0], 0, 0))

    def token_row(x):
        return (x.reshape(2, 8, 128), row)

    def fixed(x):
        zeros = (0,) * x.ndim
        return (x, pl.BlockSpec(x.shape, lambda d, core: zeros))

    prepared = [
        ((35,), jnp.int32, pl.BlockSpec(memory_space=pltpu.SMEM)),
        ((1, SEQ), f32, whole((1, SEQ))),
        ((1, SEQ), f32, whole((1, SEQ))),
        ((8, D), f32, whole((8, D))),
        ((2048, 128), bf16, whole((2048, 128))),
        ((2048, 128), bf16, whole((2048, 128))),
    ]
    gains = (
        ln_query_gain,
        ln_query_bias,
        ln_content_gain,
        ln_content_bias,
        ln_cross_gain,
        ln_cross_bias,
        ln_ffn_gain,
        ln_ffn_bias,
    )
    weights = (self_query, self_key, self_value, self_out)
    weights += (cross_query, cross_key, cross_value, cross_out)
    tokens = (segment_ids, source_segments, context_rank, context_limit, padding)
    meta, rank, limit, norms, ws0, wc0 = call(
        prepare,
        "prepare",
        1,
        [(core.astype(jnp.int32)[None], None)]
        + [token_row(x) for x in tokens]
        + [fixed(x.reshape(1, D)) for x in gains]
        + [fixed(x) for x in weights],
        prepared,
        [],
        0,
    )

    ws1 = to_core(ws0)
    ws2 = to_chip(ws0)
    wc2 = to_chip(wc0)
    u0, u2 = ffn_in, to_chip(ffn_in)
    wf0, wf2 = ffn_out, to_chip(ffn_out)
    meta_in = (meta, None)
    xq = (query_stream, own_row(D))
    xc = (content_stream, own_row(D))
    mem = (memory, own_row(D))
    cot = (cotangent, own_row(D))

    def heads_out(width, heads):
        return [
            ((SEQ, width), bf16, whole((SEQ, width))),
            ((SEQ, width), bf16, whole((SEQ, width))),
            ((SEQ, width), bf16, whole((SEQ, width))),
            ((SEQ, width), bf16, whole((SEQ, width))),
            ((DOCS, heads, FAST_K, FAST_Q), bf16, probability_spec(heads, 0)),
        ]

    def stream_out(dtype):
        return ((SEQ, D), dtype, whole((SEQ, D)))

    def placed(dtype):
        return ((2 * SEQ, D), dtype, own_row(D))

    limits = pltpu.VMEM((SEQ, 128), f32)
    pair_flops = 2 * SEQ * D * 768 + 2 * 2 * 4 * DOCS * FAST_Q * FAST_K * 256

    nq, nc, *first = call(
        self_first,
        "self_first",
        1,
        [meta_in, xq, xc, full(rank), full(limit), full(norms), full(ws0), full(ws1)],
        [stream_out(bf16), stream_out(bf16)] + heads_out(256, 4),
        [limits],
        pair_flops,
    )
    ws2, wc0, nq = hold(ws2, wc0, nq)
    ws3 = to_core(ws2)
    wc1 = to_core(wc0)
    *second_heads, second, ncross = call(
        self_second,
        "self_second",
        1,
        [meta_in, xq, full(nq), full(nc), full(rank), full(limit), full(norms)]
        + [full(w) for w in (ws0, ws1, ws2, ws3)]
        + [full(first[3])],
        heads_out(256, 4) + [stream_out(f32), stream_out(bf16)],
        [limits],
        pair_flops + 2 * SEQ * D * D,
    )
    wc2, u0, wf0, second = hold(wc2, u0, wf0, second)
    wc3 = to_core(wc2)
    u1 = to_core(u0)
    wf1 = to_core(wf0)
    *cross_heads, third, nffn = call(
        cross_forward,
        "cross_forward",
        1,
        [meta_in, full(second), full(ncross), mem, full(norms)]
        + [full(w) for w in (wc0, wc1, wc2, wc3)],
        heads_out(512, 8) + [stream_out(f32), stream_out(bf16)],
        [],
        2 * pair_flops + 2 * SEQ * D * D,
    )
    u2, wf2, third = hold(u2, wf2, third)
    u3 = to_core(u2)
    wf3 = to_core(wf2)
    grads_ln = ((8, D), f32, whole((8, D)))
    placed_output, output, g3, gln_ffn, ffn_own, ffn_other = call(
        ffn_both,
        "ffn_both",
        TILES,
        [meta_in, full(third), full(nffn), cot, full(norms)]
        + [full(w) for w in (u0, u1, u2, u3, wf0, wf1, wf2, wf3)],
        [
            placed(bf16),
            stream_out(bf16),
            stream_out(f32),
            grads_ln,
            ((1024, D), f32, whole((1024, D))),
            ((1024, D), bf16, whole((1024, D))),
        ],
        [pltpu.VMEM((SEQ, 1024), bf16), pltpu.VMEM((SEQ, 1024), bf16)],
        12 * SEQ * D * 2048,
    )

    row_count = lax.axis_size("rows")

    def exchange(x):
        return lax.all_to_all(x, "rows", 0, 0)

    def chunks(n):
        return [((row_count, n, D), bf16)]

    size = 1024 // row_count
    half = size // 2
    (ffn_send,) = simple(join_cores, "join_ffn", [ffn_own, to_core(ffn_other)], chunks(size))
    g3, ffn_send = hold(g3, ffn_send)
    ffn_parts = exchange(ffn_send)

    back_scratch = [pltpu.VMEM((SEQ, 256), bf16)] + [pltpu.VMEM((SEQ, 256), f32)] * 3
    pair_out = ((SEQ, 256), bf16, whole((SEQ, 256)))
    packed_outs = [
        ((D, D), f32, whole((D, D))),
        ((D, D), bf16, whole((D, D))),
    ]
    back_flops = 2 * SEQ * D * 256 + 4 * 2 * 4 * DOCS * FAST_Q * FAST_K * 256

    def head_inputs(arrays, n):
        *natural, p = arrays
        return [(x, columns(256, n)) for x in natural] + [(p, probability_spec(4, n))]

    *cross_grads, cross_own, cross_other = call(
        functools.partial(attention_back_first, True),
        "cross_back_first",
        1,
        [meta_in, full(g3), full(ncross), mem, full(rank), full(limit), full(wc0), full(wc1)]
        + head_inputs(cross_heads, 0),
        [pair_out] * 3 + packed_outs,
        [limits] + back_scratch,
        back_flops + 2 * SEQ * D * 1024,
    )
    ffn_parts, cross_own = hold(ffn_parts, cross_own)
    (ffn_total,) = simple(sum_rows, "sum_ffn", [ffn_parts], chunks(size))
    ffn_total, cross_grads[0] = hold(ffn_total, cross_grads[0])
    ffn_sums = exchange(ffn_total)
    cross_other = to_core(cross_other)
    g2, placed_mem, grad_mem, gln_cross = call(
        cross_back_second,
        "cross_back_second",
        1,
        [meta_in, full(g3), full(second), full(norms)]
        + [full(w) for w in (wc0, wc1, wc2, wc3)]
        + [full(x) for x in cross_grads]
        + head_inputs(cross_heads, 1),
        [stream_out(f32), placed(f32), stream_out(bf16), grads_ln],
        back_scratch,
        back_flops + 2 * SEQ * D * 1536,
    )
    ffn_sums, cross_other, g2 = hold(ffn_sums, cross_other, g2)
    (cross_send,) = simple(join_cores, "join_cross", [cross_own, cross_other], chunks(half))
    cross_send, g2 = hold(cross_send, g2)
    cross_parts = exchange(cross_send)

    *self_grads, self_own, self_other = call(
        functools.partial(attention_back_first, False),
        "self_back_first",
        1,
        [meta_in, full(g2), full(nq), full(nc), full(rank), full(limit), full(ws0), full(ws1)]
        + head_inputs(first, 0),
        [pair_out] * 3 + packed_outs,
        [limits] + back_scratch,
        back_flops + 2 * SEQ * D * 1024,
    )
    self_other = to_core(self_other)
    cross_parts, self_own = hold(cross_parts, self_own)
    (both_send,) = simple(
        sum_rows_join, "sum_cross", [cross_parts, self_own, self_other], chunks(2 * half)
    )
    both_send, g2 = hold(both_send, g2)
    both_parts = exchange(both_send)
    placed_q, placed_c, gq, gc, gln_self = call(
        self_back_second,
        "self_back_second",
        1,
        [meta_in, full(g2), xq, xc, full(rank), full(limit), full(norms)]
        + [full(w) for w in (ws0, ws1, ws2, ws3)]
        + [full(x) for x in self_grads]
        + head_inputs(second_heads, 0),
        [placed(f32), placed(f32), stream_out(bf16), stream_out(bf16), grads_ln],
        [limits] + back_scratch,
        back_flops + 2 * SEQ * D * 1536,
    )

    gln = jnp.concatenate([gln_self[0:4], gln_cross[0:2], gln_ffn[0:2]], axis=0)
    both_parts, gln = hold(both_parts, gln)
    (last_send,) = simple(
        functools.partial(sum_last, half), "sum_self", [both_parts, gln, to_core(gln)], chunks(half + 16)
    )
    last_parts = exchange(last_send)

    def both_rows(placed_own, arrays, name):
        count = len(arrays)
        size = SEQ // 2
        one = pl.BlockSpec((size, D), lambda i, meta: (i, 0))
        block = pl.BlockSpec((size, D), lambda i, meta: (2 * (1 - meta[0]) + i, 0))
        return pl.pallas_call(
            place_rows,
            name=name,
            grid_spec=pltpu.PrefetchScalarGridSpec(
                num_scalar_prefetch=1,
                grid=(2,),
                in_specs=[one] * count + [pl.BlockSpec(memory_space=pl.ANY)] * count,
                out_specs=[block] * count,
            ),
            out_shape=[jax.ShapeDtypeStruct(x.shape, x.dtype) for x in placed_own],
            input_output_aliases={1 + count + n: n for n in range(count)},
        )(meta, *[to_core(x) for x in arrays], *placed_own)

    out_both, grad_mem_both = both_rows([placed_output, placed_mem], [output, grad_mem], "place_early")
    gq_both, gc_both = both_rows([placed_q, placed_c], [gq, gc], "place_late")

    attention_outs = [((512, 128), f32)] * 3 + [((128, 512), f32)]
    grad_ffn_in, grad_ffn_out, *grad_cross_parts = simple(
        unpack_early, "unpack_early", [ffn_sums, both_parts], [((D, D), f32)] * 2 + attention_outs
    )
    *grad_self_parts, gln = simple(
        unpack_late, "unpack_late", [last_parts], attention_outs + [((8, D), f32)]
    )
    return (
        out_both,
        gq_both,
        gc_both,
        grad_mem_both,
        gln[0],
        gln[1],
        gln[2],
        gln[3],
        *grad_self_parts,
        gln[4],
        gln[5],
        *grad_cross_parts,
        gln[6],
        gln[7],
        grad_ffn_in,
        grad_ffn_out,
    )


def solution(mesh):
    assert mesh.shape["heads"] == 4
    row_spec = P("rows", None)
    flat = P("rows")
    by_column = P(None, "heads")
    by_row = P("heads", None)
    attention = (by_column, by_column, by_column, by_row)
    in_specs = (
        (row_spec,) * 3
        + (flat,) * 5
        + (P(),) * 4
        + attention
        + (P(),) * 2
        + attention
        + (P(),) * 2
        + (by_column, by_row, row_spec)
    )
    out_specs = (
        (row_spec,) * 4
        + (P(),) * 4
        + attention
        + (P(),) * 2
        + attention
        + (P(),) * 2
        + (by_column, by_row)
    )
    return jax.shard_map(shards, mesh=mesh, in_specs=in_specs, out_specs=out_specs, check_vma=False)
```

```python
import functools

import jax
import jax.numpy as jnp
from jax import lax
from jax.experimental import pallas as pl
from jax.experimental.pallas import tpu as pltpu
from jax.sharding import PartitionSpec as P

HEAD_DIM = 64
SEQ = 1024
DOCS = 8
D = 512
TILE = 256
TILES = SEQ // TILE
FAST_Q = 256
FAST_K = 208
LONG_Q = 128
LONG_K = 640

norm_eps = 1e-05
masked_score = -1e30
hidden_rank = 1e6
gelu_root = 0.7978845608028654
gelu_cube = 0.044715

f32 = jnp.float32
bf16 = jnp.bfloat16


def dot(a, b):
    return lax.dot_general(a, b, (((1,), (0,)), ((), ())), preferred_element_type=f32)


def dot_nt(a, b):
    return lax.dot_general(a, b, (((1,), (1,)), ((), ())), preferred_element_type=f32)


def dot_tn(a, b):
    return lax.dot_general(a, b, (((0,), (0,)), ((), ())), preferred_element_type=f32)


def lanes(parts):
    return jnp.concatenate(parts, axis=1)


def layer_norm(values, gain, shift):
    centre = values - jnp.mean(values, axis=-1, keepdims=True)
    spread = jnp.mean(centre * centre, axis=-1, keepdims=True)
    return centre * lax.rsqrt(spread + norm_eps) * gain + shift


def norm_backward(values, gain, grad):
    centre = values - jnp.mean(values, axis=-1, keepdims=True)
    spread = jnp.mean(centre * centre, axis=-1, keepdims=True)
    scale = lax.rsqrt(spread + norm_eps)
    xhat = centre * scale
    eg = grad * gain
    mean_eg = jnp.mean(eg, axis=-1, keepdims=True)
    mean_egx = jnp.mean(eg * xhat, axis=-1, keepdims=True)
    grad_gain = jnp.sum(grad * xhat, axis=0, keepdims=True)
    grad_shift = jnp.sum(grad, axis=0, keepdims=True)
    return scale * (eg - mean_eg - xhat * mean_egx), grad_gain, grad_shift


def rows_of(i, size=TILE):
    return pl.ds(pl.multiple_of(i * size, size), size)


def w_query(ref):
    return ref[0:512, :]


def w_key(ref):
    return ref[512:1024, :]


def w_value(ref):
    return ref[1024:1536, :]


def w_out(ref):
    return lanes([ref[1536 + 128 * j : 1664 + 128 * j, :] for j in range(4)])


def half_masks():
    place = lax.broadcasted_iota(jnp.int32, (1, 128), 1)
    low = jnp.where(place < HEAD_DIM, 1.0, 0.0).astype(f32)
    return (low.astype(bf16), (1.0 - low).astype(bf16))


def doc_bounds(meta, d, source):
    base = 17 if source else 1
    return meta[base + d], meta[base + 8 + d]


def window_of(first, limit):
    return pl.multiple_of(jnp.minimum((first // 16) * 16, limit), 16)


def key_bias(ks, ke, k0, width):
    place = k0 + lax.broadcasted_iota(jnp.int32, (width, 128), 0)
    return jnp.where((place >= ks) & (place < ke), 0.0, masked_score)


def make_bias(rank_ref, limit_ref, ks, ke, q0, k0, span, width):
    if rank_ref is None:
        return lanes([key_bias(ks, ke, k0, width)] * (span // 128))
    place = k0 + lax.broadcasted_iota(jnp.int32, (width, 128), 0)
    ranks = rank_ref[pl.ds(k0, width), :]
    ranks = jnp.where((place < ks + 2) & (ranks < hidden_rank), -1.0, ranks)
    ranks = jnp.where((place >= ks) & (place < ke), ranks, hidden_rank)
    limits = jnp.broadcast_to(limit_ref[...], (8, SEQ))
    limits = pltpu.roll(limits, lax.rem(SEQ - q0, SEQ), 1)[0:1, 0:span]
    row = k0 + lax.broadcasted_iota(jnp.int32, (width, span), 0)
    column = q0 + lax.broadcasted_iota(jnp.int32, (width, span), 1)
    seen = (lanes([ranks] * (span // 128)) < limits) & (row != column)
    return jnp.where(seen, 0.0, masked_score)


def both_heads(x, masks):
    return jnp.concatenate([x * masks[0], x * masks[1]], axis=0)


def pair_probabilities(queries, keys, masks, bias):
    width = keys.shape[0]
    scores = dot_nt(both_heads(keys, masks), queries)
    result = []
    for a in range(2):
        part = scores[width * a : width * a + width] + bias
        part = jnp.exp(part - jnp.max(part, axis=0, keepdims=True))
        part = part * (1.0 / jnp.sum(part, axis=0, keepdims=True))
        result.append(part.astype(bf16))
    return result


def pair_product(rows, parts):
    across = jnp.transpose(rows)
    halves = [dot(across[64 * a : 64 * a + 64], part) for a, part in enumerate(parts)]
    return jnp.transpose(jnp.concatenate(halves, axis=0))


def for_docs(meta, cross, run):
    fast = meta[34 if cross else 33] == 1

    @pl.when(fast)
    def _():
        def doc(d, carry):
            ts, te = doc_bounds(meta, d, False)
            ks, ke = doc_bounds(meta, d, cross)
            q0 = window_of(ts, SEQ - FAST_Q)
            k0 = window_of(ks, SEQ - FAST_K)
            run(d, q0, k0, FAST_Q, FAST_K, ts, te, ks, ke, True)
            return carry

        lax.fori_loop(0, DOCS, doc, 0, unroll=2)

    @pl.when(jnp.logical_not(fast))
    def _():
        def doc(d, carry):
            ts, te = doc_bounds(meta, d, False)
            ks, ke = doc_bounds(meta, d, cross)
            base = (ts // 16) * 16
            k0 = window_of(ks, SEQ - LONG_K)

            def chunk(i, carry):
                lower = base + i * LONG_Q
                q0 = pl.multiple_of(jnp.minimum(lower, SEQ - LONG_Q), 16)
                low = jnp.maximum(ts, lower)
                high = jnp.minimum(te, lower + LONG_Q)
                run(d, q0, k0, LONG_Q, LONG_K, low, high, ks, ke, False)
                return carry

            return lax.fori_loop(0, (te - base + LONG_Q - 1) // LONG_Q, chunk, carry)

        lax.fori_loop(0, DOCS, doc, 0)


def attend_docs(meta, cross, rank_ref, limit_ref, q_ref, k_ref, v_ref, p_ref, mixed_ref):
    pairs = q_ref.shape[1] // 128
    masks = half_masks()

    def run(d, q0, k0, span, width, low, high, ks, ke, fast):
        bias = make_bias(rank_ref, limit_ref, ks, ke, q0, k0, span, width)
        row = q0 + lax.broadcasted_iota(jnp.int32, (span, 128), 0)
        inside = (row >= low) & (row < high)
        for n in range(pairs):
            cols = slice(128 * n, 128 * n + 128)
            queries = q_ref[pl.ds(q0, span), cols]
            keys = k_ref[pl.ds(k0, width), cols]
            values = v_ref[pl.ds(k0, width), cols]
            parts = pair_probabilities(queries, keys, masks, bias)
            if fast:
                for a in range(2):
                    p_ref[d, 2 * n + a] = parts[a]
            mixed = pair_product(values, parts)
            old = mixed_ref[pl.ds(q0, span), cols].astype(f32)
            mixed_ref[pl.ds(q0, span), cols] = jnp.where(inside, mixed, old).astype(bf16)

    for_docs(meta, cross, run)


def attend_docs_back(
    meta, cross, rank_ref, limit_ref, q_ref, k_ref, v_ref, p_ref, mixed_ref, dm_ref,
    dq_ref, dk_ref, dv_ref,
):
    pairs = q_ref.shape[1] // 128
    masks = half_masks()

    def run(d, q0, k0, span, width, low, high, ks, ke, fast):
        row = q0 + lax.broadcasted_iota(jnp.int32, (span, 128), 0)
        inside = (row >= low) & (row < high)
        ones = jnp.ones((width, 128), bf16)
        if not fast:
            bias = make_bias(rank_ref, limit_ref, ks, ke, q0, k0, span, width)
        for n in range(pairs):
            cols = slice(128 * n, 128 * n + 128)
            queries = q_ref[pl.ds(q0, span), cols]
            keys = k_ref[pl.ds(k0, width), cols]
            values = v_ref[pl.ds(k0, width), cols]
            mixed = mixed_ref[pl.ds(q0, span), cols].astype(f32)
            grad = jnp.where(inside, dm_ref[pl.ds(q0, span), cols].astype(f32), 0.0)
            low_grad = grad.astype(bf16)
            left = lanes([low_grad, (-(grad * mixed)).astype(bf16)])
            delta = dot_nt(both_heads(lanes([values, ones]), [lanes([m, m]) for m in masks]), left)
            if fast:
                parts = [p_ref[d, 2 * n + a] for a in range(2)]
            else:
                parts = pair_probabilities(queries, keys, masks, bias)
            slopes = []
            dk = dv = None
            for a in range(2):
                slope = parts[a].astype(f32) * delta[width * a : width * a + width]
                slopes.append(slope.astype(bf16))
                dk_a = dot(slopes[a], queries * masks[a])
                dv_a = dot(parts[a], low_grad * masks[a])
                dk = dk_a if dk is None else dk + dk_a
                dv = dv_a if dv is None else dv + dv_a
            dq = pair_product(keys, slopes)
            dq_ref[pl.ds(q0, span), cols] += dq * (HEAD_DIM**-0.5)
            dk_ref[pl.ds(k0, width), cols] += dk
            dv_ref[pl.ds(k0, width), cols] += dv

    for_docs(meta, cross, run)


def spread_ranks(rank_row_ref, rank_ref):
    rank_ref[...] = jnp.transpose(jnp.broadcast_to(rank_row_ref[...], (128, SEQ)))


def prepare(
    core, seg_ref, src_ref, rank_ref, limit_ref, pad_ref,
    n0, n1, n2, n3, n4, n5, n6, n7, sq, sk, sv, so, cq, ck, cv, co,
    meta_ref, ranks_ref, limits_ref, norms_ref, ws_ref, wc_ref,
):
    meta_ref[0] = core[0]
    for base, ref in ((1, seg_ref), (17, src_ref)):
        ids = ref[0]
        meta_ref[base] = 0
        meta_ref[base + 15] = SEQ
        for d in range(1, DOCS):
            cut = jnp.sum(jnp.where(ids < d, 1.0, 0.0)).astype(jnp.int32)
            meta_ref[base + d] = cut
            meta_ref[base + 7 + d] = cut
    for place, base in ((33, 1), (34, 17)):
        fast = jnp.int32(1)
        for d in range(DOCS):
            q0 = window_of(meta_ref[1 + d], SEQ - FAST_Q)
            k0 = window_of(meta_ref[base + d], SEQ - FAST_K)
            fits = (meta_ref[9 + d] - q0 <= FAST_Q) & (meta_ref[base + 8 + d] - k0 <= FAST_K)
            fast = fast & fits.astype(jnp.int32)
        meta_ref[place] = fast
    ranks = jnp.where(pad_ref[0] != 0, hidden_rank, rank_ref[0].astype(f32))
    limits = limit_ref[0].astype(f32)
    for i in range(8):
        ranks_ref[0:1, 128 * i : 128 * i + 128] = ranks[i : i + 1]
        limits_ref[0:1, 128 * i : 128 * i + 128] = limits[i : i + 1]
    for i, ref in enumerate((n0, n1, n2, n3, n4, n5, n6, n7)):
        norms_ref[i : i + 1, :] = ref[...]
    for to, parts, out in ((ws_ref, (sq, sk, sv), so), (wc_ref, (cq, ck, cv), co)):
        for i, part in enumerate(parts):
            to[512 * i : 512 * i + 512, :] = part[...]
        for j in range(4):
            to[1536 + 128 * j : 1664 + 128 * j, :] = out[:, 128 * j : 128 * j + 128]


def self_first(
    meta, xq_ref, xc_ref, rank_row_ref, limit_ref, norms_ref, w0_ref, w1_ref,
    nq_ref, nc_ref, q_ref, k_ref, v_ref, mixed_ref, p_ref, rank_ref,
):

    spread_ranks(rank_row_ref, rank_ref)
    wq = lanes([w_query(w0_ref), w_query(w1_ref)])
    wkv = lanes([w_key(w0_ref), w_key(w1_ref), w_value(w0_ref), w_value(w1_ref)])

    def tile(i, carry):
        rows = rows_of(i)
        nq = layer_norm(xq_ref[rows, :].astype(f32), norms_ref[0:1], norms_ref[1:2]).astype(bf16)
        nc = layer_norm(xc_ref[rows, :].astype(f32), norms_ref[2:3], norms_ref[3:4]).astype(bf16)
        nq_ref[rows, :] = nq
        nc_ref[rows, :] = nc
        q_ref[rows, :] = (dot(nq, wq) * (HEAD_DIM**-0.5)).astype(bf16)
        kv = dot(nc, wkv).astype(bf16)
        k_ref[rows, :] = kv[:, :256]
        v_ref[rows, :] = kv[:, 256:]
        return carry

    lax.fori_loop(0, TILES, tile, 0)

    attend_docs(meta, False, rank_ref, limit_ref, q_ref, k_ref, v_ref, p_ref, mixed_ref)


def self_second(
    meta, xq_ref, nq_ref, nc_ref, rank_row_ref, limit_ref, norms_ref, w0_ref, w1_ref, w2_ref, w3_ref,
    mixed_first_ref,
    q_ref, k_ref, v_ref, mixed_ref, p_ref, second_ref, ncross_ref, rank_ref,
):

    spread_ranks(rank_row_ref, rank_ref)
    wq = lanes([w_query(w2_ref), w_query(w3_ref)])
    wkv = lanes([w_key(w2_ref), w_key(w3_ref), w_value(w2_ref), w_value(w3_ref)])

    def tile(i, carry):
        rows = rows_of(i)
        q_ref[rows, :] = (dot(nq_ref[rows, :], wq) * (HEAD_DIM**-0.5)).astype(bf16)
        kv = dot(nc_ref[rows, :], wkv).astype(bf16)
        k_ref[rows, :] = kv[:, :256]
        v_ref[rows, :] = kv[:, 256:]
        return carry

    lax.fori_loop(0, TILES, tile, 0)

    attend_docs(meta, False, rank_ref, limit_ref, q_ref, k_ref, v_ref, p_ref, mixed_ref)

    out_first = jnp.concatenate([w_out(w0_ref), w_out(w1_ref)], axis=0)
    out_second = jnp.concatenate([w_out(w2_ref), w_out(w3_ref)], axis=0)

    def tile(i, carry):
        rows = rows_of(i)
        branch = dot(mixed_first_ref[rows, :], out_first) + dot(mixed_ref[rows, :], out_second)
        second = xq_ref[rows, :].astype(f32) + branch
        second_ref[rows, :] = second
        ncross_ref[rows, :] = layer_norm(second, norms_ref[4:5], norms_ref[5:6]).astype(bf16)
        return carry

    lax.fori_loop(0, TILES, tile, 0)


def cross_forward(
    meta, second_ref, ncross_ref, memory_ref, norms_ref, w0_ref, w1_ref, w2_ref, w3_ref,
    q_ref, k_ref, v_ref, mixed_ref, p_ref, third_ref, nffn_ref,
):
    weights = (w0_ref, w1_ref, w2_ref, w3_ref)

    wq = lanes([w_query(w) for w in weights])
    wk = lanes([w_key(w) for w in weights])
    wv = lanes([w_value(w) for w in weights])

    def tile(i, carry):
        rows = rows_of(i)
        memory = memory_ref[rows, :]
        q_ref[rows, :] = (dot(ncross_ref[rows, :], wq) * (HEAD_DIM**-0.5)).astype(bf16)
        k_ref[rows, :] = dot(memory, wk).astype(bf16)
        v_ref[rows, :] = dot(memory, wv).astype(bf16)
        return carry

    lax.fori_loop(0, TILES, tile, 0)

    attend_docs(meta, True, None, None, q_ref, k_ref, v_ref, p_ref, mixed_ref)

    out_first = jnp.concatenate([w_out(w0_ref), w_out(w1_ref)], axis=0)
    out_second = jnp.concatenate([w_out(w2_ref), w_out(w3_ref)], axis=0)

    def tile(i, carry):
        rows = rows_of(i)
        mixed = mixed_ref[rows, :]
        branch = dot(mixed[:, :256], out_first) + dot(mixed[:, 256:], out_second)
        third = second_ref[rows, :] + branch
        third_ref[rows, :] = third
        nffn_ref[rows, :] = layer_norm(third, norms_ref[6:7], norms_ref[7:8]).astype(bf16)
        return carry

    lax.fori_loop(0, TILES, tile, 0)


def ffn_both(
    meta, third_ref, nffn_ref, cot_ref, norms_ref, u0_ref, u1_ref, u2_ref, u3_ref,
    w0_ref, w1_ref, w2_ref, w3_ref,
    placed_ref, out_ref, g3_ref, gln_ref, own_ref, other_ref, hidden_ref, before_ref,
):
    i = pl.program_id(0)
    rows = rows_of(i)
    nffn = nffn_ref[rows, :]
    cot = cot_ref[rows, :]
    outs = []
    grads = []
    in_refs = (u0_ref, u1_ref, u2_ref, u3_ref)
    for g, w_ref in enumerate((w0_ref, w1_ref, w2_ref, w3_ref)):
        w_in = in_refs[g][...]
        w_out_rows = w_ref[...]
        x = dot(nffn, w_in)
        square = x * x
        half = 0.5 + 0.5 * jnp.tanh(x * (gelu_root + (gelu_root * gelu_cube) * square))
        value = x * half
        hidden = value.astype(bf16)
        rise = 2.0 * gelu_root + (6.0 * gelu_root * gelu_cube) * square
        slope = half + value * (1.0 - half) * rise
        grad_before = (dot_nt(cot, w_out_rows) * slope).astype(bf16)
        outs.append(dot(hidden, w_out_rows))
        grads.append(dot_nt(grad_before, w_in))
        if g < 2:
            hidden_ref[rows, 512 * g : 512 * g + 512] = hidden
            before_ref[rows, 512 * g : 512 * g + 512] = grad_before
    third = third_ref[rows, :]
    out = (third + ((outs[0] + outs[1]) + (outs[2] + outs[3]))).astype(bf16)
    out_ref[rows, :] = out
    placed_ref[rows, :] = out
    grad_normed = (grads[0] + grads[1]) + (grads[2] + grads[3])
    grad_norm, grad_gain, grad_shift = norm_backward(third, norms_ref[6:7], grad_normed)
    g3_ref[rows, :] = cot.astype(f32) + grad_norm

    @pl.when(i == 0)
    def _():
        gln_ref[0:1, :] = grad_gain
        gln_ref[1:2, :] = grad_shift

    @pl.when(i > 0)
    def _():
        gln_ref[0:1, :] += grad_gain
        gln_ref[1:2, :] += grad_shift

    @pl.when(i == TILES - 1)
    def _():
        nffn_all = nffn_ref[...]
        cot_all = cot_ref[...]
        part = dot_tn(nffn_all, before_ref[...])
        own_ref[0:512, :] = part[:, 0:512]
        other_ref[0:512, :] = part[:, 512:1024].astype(bf16)
        part = dot_tn(hidden_ref[...], cot_all)
        own_ref[512:1024, :] = part[0:512]
        other_ref[512:1024, :] = part[512:1024].astype(bf16)


def back_start(g_ref, mixed_ref, w_refs, dm_ref, dq_ref, dk_ref, dv_ref):
    out_rows = jnp.concatenate([w_out(w) for w in w_refs], axis=0)

    def tile(i, carry):
        rows = rows_of(i)
        dm_ref[rows, :] = dot_nt(g_ref[rows, :].astype(bf16), out_rows).astype(bf16)
        zeros = jnp.zeros((TILE, 256), f32)
        dq_ref[rows, :] = zeros
        dk_ref[rows, :] = zeros
        dv_ref[rows, :] = zeros
        return carry

    lax.fori_loop(0, TILES, tile, 0)


def attention_back_first(
    cross, meta, g_ref, nq_ref, nkv_ref, rank_row_ref, limit_ref, w0_ref, w1_ref,
    q_ref, k_ref, v_ref, mixed_ref, p_ref,
    dq_ref, dk_ref, dv_ref, own_ref, other_ref,
    rank_ref, dm_ref, dqs_ref, dks_ref, dvs_ref,
):

    if not cross:
        spread_ranks(rank_row_ref, rank_ref)
    back_start(g_ref, mixed_ref, (w0_ref, w1_ref), dm_ref, dqs_ref, dks_ref, dvs_ref)

    attend_docs_back(
        meta, cross, None if cross else rank_ref, limit_ref, q_ref, k_ref, v_ref, p_ref, mixed_ref,
        dm_ref, dqs_ref, dks_ref, dvs_ref,
    )

    dq_ref[...] = dqs_ref[...].astype(bf16)
    dk_ref[...] = dks_ref[...].astype(bf16)
    dv_ref[...] = dvs_ref[...].astype(bf16)
    nq = nq_ref[...]
    nkv = nkv_ref[...]
    for n, part in enumerate(
        (dot_tn(nq, dq_ref[...]), dot_tn(nkv, dk_ref[...]), dot_tn(nkv, dv_ref[...]))
    ):
        own_ref[:, 128 * n : 128 * n + 128] = part[:, :128]
        other_ref[:, 128 * n : 128 * n + 128] = part[:, 128:].astype(bf16)
    part = dot_tn(mixed_ref[...], g_ref[...].astype(bf16))
    for j in range(4):
        rows = slice(128 * j, 128 * j + 128)
        own_ref[rows, 384:512] = part[:128, rows]
        other_ref[rows, 384:512] = part[128:, rows].astype(bf16)


def back_second_docs(
    cross, meta, g_ref, rank_row_ref, limit_ref, w_refs, q_ref, k_ref, v_ref, mixed_ref, p_ref,
    rank_ref, dm_ref, dqs_ref, dks_ref, dvs_ref,
):

    if not cross:
        spread_ranks(rank_row_ref, rank_ref)
    back_start(g_ref, mixed_ref, w_refs, dm_ref, dqs_ref, dks_ref, dvs_ref)

    attend_docs_back(
        meta, cross, None if cross else rank_ref, limit_ref, q_ref, k_ref, v_ref, p_ref, mixed_ref,
        dm_ref, dqs_ref, dks_ref, dvs_ref,
    )


def stream_grads(rows, first, second, firsts, seconds):
    dq, dk, dv = first
    dq2, dk2, dv2 = (ref[rows, :].astype(bf16) for ref in second)
    w0, w1 = firsts
    w2, w3 = seconds
    grad_q = dot_nt(dq[rows, :], lanes([w_query(w0), w_query(w1)])) + dot_nt(
        dq2, lanes([w_query(w2), w_query(w3)])
    )
    kv = lanes([dk[rows, :], dv[rows, :]])
    kv2 = lanes([dk2, dv2])
    grad_kv = dot_nt(kv, lanes([w_key(w0), w_key(w1), w_value(w0), w_value(w1)])) + dot_nt(
        kv2, lanes([w_key(w2), w_key(w3), w_value(w2), w_value(w3)])
    )
    return grad_q, grad_kv


def cross_back_second(
    meta, g_ref, second_ref, norms_ref, w0_ref, w1_ref, w2_ref, w3_ref,
    dq_ref, dk_ref, dv_ref, q_ref, k_ref, v_ref, mixed_ref, p_ref,
    g2_ref, placed_ref, gmem_ref, gln_ref,
    dm_ref, dqs_ref, dks_ref, dvs_ref,
):
    back_second_docs(
        True, meta, g_ref, None, None, (w2_ref, w3_ref), q_ref, k_ref, v_ref, mixed_ref, p_ref,
        None, dm_ref, dqs_ref, dks_ref, dvs_ref,
    )

    gln_ref[...] = jnp.zeros_like(gln_ref)

    def tile(i, carry):
        rows = rows_of(i)
        grad_q, grad_kv = stream_grads(
            rows,
            (dq_ref, dk_ref, dv_ref),
            (dqs_ref, dks_ref, dvs_ref),
            (w0_ref, w1_ref),
            (w2_ref, w3_ref),
        )
        low_kv = grad_kv.astype(bf16)
        gmem_ref[rows, :] = low_kv
        placed_ref[rows, :] = low_kv.astype(f32)
        grad_norm, grad_gain, grad_shift = norm_backward(
            second_ref[rows, :], norms_ref[4:5], grad_q
        )
        g2_ref[rows, :] = g_ref[rows, :] + grad_norm
        gln_ref[0:1, :] += grad_gain
        gln_ref[1:2, :] += grad_shift
        return carry

    lax.fori_loop(0, TILES, tile, 0)


def self_back_second(
    meta, g_ref, xq_ref, xc_ref, rank_row_ref, limit_ref, norms_ref, w0_ref, w1_ref, w2_ref, w3_ref,
    dq_ref, dk_ref, dv_ref, q_ref, k_ref, v_ref, mixed_ref, p_ref,
    placed_q_ref, placed_c_ref, gq_ref, gc_ref, gln_ref,
    rank_ref, dm_ref, dqs_ref, dks_ref, dvs_ref,
):
    back_second_docs(
        False, meta, g_ref, rank_row_ref, limit_ref, (w2_ref, w3_ref), q_ref, k_ref, v_ref, mixed_ref,
        p_ref, rank_ref, dm_ref, dqs_ref, dks_ref, dvs_ref,
    )

    gln_ref[...] = jnp.zeros_like(gln_ref)

    def tile(i, carry):
        rows = rows_of(i)
        grad_q, grad_kv = stream_grads(
            rows,
            (dq_ref, dk_ref, dv_ref),
            (dqs_ref, dks_ref, dvs_ref),
            (w0_ref, w1_ref),
            (w2_ref, w3_ref),
        )
        grad_norm, grad_gain, grad_shift = norm_backward(
            xq_ref[rows, :].astype(f32), norms_ref[0:1], grad_q
        )
        low_q = (g_ref[rows, :] + grad_norm).astype(bf16)
        gq_ref[rows, :] = low_q
        placed_q_ref[rows, :] = low_q.astype(f32)
        gln_ref[0:1, :] += grad_gain
        gln_ref[1:2, :] += grad_shift
        grad_norm, grad_gain, grad_shift = norm_backward(
            xc_ref[rows, :].astype(f32), norms_ref[2:3], grad_kv
        )
        low_c = grad_norm.astype(bf16)
        gc_ref[rows, :] = low_c
        placed_c_ref[rows, :] = low_c.astype(f32)
        gln_ref[2:3, :] += grad_gain
        gln_ref[3:4, :] += grad_shift
        return carry

    lax.fori_loop(0, TILES, tile, 0)


def place_rows(meta, *refs):
    count = len(refs) // 3
    for n in range(count):
        refs[2 * count + n][...] = refs[n][...].astype(refs[2 * count + n].dtype)


def join_cores(own, other, send):
    joined = own[...] + other[...].astype(f32)
    send[...] = joined.astype(bf16).reshape(send.shape)


def summed(parts, size, first):
    total = parts[0, first : first + size, :].astype(f32)
    for r in range(1, parts.shape[0]):
        total = total + parts[r, first : first + size, :].astype(f32)
    return total.astype(bf16)


def sum_rows(parts, send):
    count, size, _ = parts.shape
    total = summed(parts, size, 0)
    for r in range(count):
        send[r] = total


def sum_rows_join(parts, own, other, send):
    count, done, _ = parts.shape
    size = own.shape[0] // count
    total = summed(parts, done, 0)
    for r in range(count):
        rows = slice(size * r, size * r + size)
        send[r, 0:done, :] = total
        send[r, done : done + size, :] = (own[rows, :] + other[rows, :].astype(f32)).astype(bf16)


def sum_last(done, parts, gln_own, gln_other, send):
    count = parts.shape[0]
    size = parts.shape[1] - done
    total = summed(parts, size, done)
    gln = gln_own[...] + gln_other[...]
    gln = jnp.concatenate([gln, jnp.zeros((8, D), f32)], axis=0).astype(bf16)
    for r in range(count):
        send[r, 0:size, :] = total
        send[r, size : size + 16, :] = gln


def unpack_attention(parts, outs):
    count = parts.shape[0]
    size = D // count
    for r in range(count):
        rows = slice(size * r, size * r + size)
        for i in range(3):
            outs[i][rows, :] = parts[r, 0:size, 128 * i : 128 * i + 128].astype(f32)
        j, first = divmod(size * r, 128)
        outs[3][first : first + size, 128 * j : 128 * j + 128] = parts[r, 0:size, 384:512].astype(f32)


def unpack_early(ffn, cross, *outs):
    count, size, _ = ffn.shape
    for r in range(count):
        out = outs[2 * r // count]
        first = (size * r) % D
        out[first : first + size, :] = ffn[r].astype(f32)
    unpack_attention(cross, outs[2:])


def unpack_late(parts, *outs):
    unpack_attention(parts, outs[:4])
    size = parts.shape[1] - 16
    total = parts[0, size : size + 16, :].astype(f32)
    for r in range(1, parts.shape[0]):
        total = total + parts[r, size : size + 16, :].astype(f32)
    outs[4][...] = total[0:8]


def whole(shape):
    zeros = (0,) * len(shape)
    return pl.BlockSpec(shape, lambda d, meta: zeros)


def own_row(width):
    return pl.BlockSpec((SEQ, width), lambda d, meta: (meta[0], 0))


def columns(width, n):
    return pl.BlockSpec((SEQ, width), lambda d, meta: (0, n))


def probability_spec(heads, n):
    return pl.BlockSpec((DOCS, heads, FAST_K, FAST_Q), lambda d, meta: (0, n, 0, 0))


def call(kernel, name, grid, operands, outs, scratch, flops):
    moved = sum(x.size * x.dtype.itemsize for x, _ in operands[1:])
    return pl.pallas_call(
        kernel,
        name=name,
        grid_spec=pltpu.PrefetchScalarGridSpec(
            num_scalar_prefetch=1,
            grid=(grid,),
            in_specs=[spec for _, spec in operands[1:]],
            out_specs=[spec for _, _, spec in outs],
            scratch_shapes=scratch,
        ),
        out_shape=[jax.ShapeDtypeStruct(shape, dtype) for shape, dtype, _ in outs],
        compiler_params=pltpu.CompilerParams(
            dimension_semantics=("arbitrary",), vmem_limit_bytes=24 * 1024 * 1024
        ),
        cost_estimate=pl.CostEstimate(
            flops=int(flops), bytes_accessed=int(moved), transcendentals=0
        ),
    )(*[x for x, _ in operands])


def simple(kernel, name, operands, outs):
    return pl.pallas_call(
        kernel,
        name=name,
        out_shape=[jax.ShapeDtypeStruct(shape, dtype) for shape, dtype in outs],
        compiler_params=pltpu.CompilerParams(vmem_limit_bytes=8 * 1024 * 1024),
    )(*operands)


def full(x):
    return (x, whole(x.shape))


def shards(
    query_stream,
    content_stream,
    memory,
    segment_ids,
    source_segments,
    context_rank,
    context_limit,
    padding,
    ln_query_gain,
    ln_query_bias,
    ln_content_gain,
    ln_content_bias,
    self_query,
    self_key,
    self_value,
    self_out,
    ln_cross_gain,
    ln_cross_bias,
    cross_query,
    cross_key,
    cross_value,
    cross_out,
    ln_ffn_gain,
    ln_ffn_bias,
    ffn_in,
    ffn_out,
    cotangent,
):
    core = lax.axis_index("heads") % 2

    def to_core(x):
        return lax.ppermute(x, "heads", [(h, h ^ 1) for h in range(4)])

    hold = lambda *xs: lax.optimization_barrier(xs)

    def to_chip(x):
        return lax.ppermute(x, "heads", [(h, h ^ 2) for h in range(4)])

    row = pl.BlockSpec((1, 8, 128), lambda d, core: (core[0], 0, 0))

    def token_row(x):
        return (x.reshape(2, 8, 128), row)

    def fixed(x):
        zeros = (0,) * x.ndim
        return (x, pl.BlockSpec(x.shape, lambda d, core: zeros))

    prepared = [
        ((35,), jnp.int32, pl.BlockSpec(memory_space=pltpu.SMEM)),
        ((1, SEQ), f32, whole((1, SEQ))),
        ((1, SEQ), f32, whole((1, SEQ))),
        ((8, D), f32, whole((8, D))),
        ((2048, 128), bf16, whole((2048, 128))),
        ((2048, 128), bf16, whole((2048, 128))),
    ]
    gains = (
        ln_query_gain,
        ln_query_bias,
        ln_content_gain,
        ln_content_bias,
        ln_cross_gain,
        ln_cross_bias,
        ln_ffn_gain,
        ln_ffn_bias,
    )
    weights = (self_query, self_key, self_value, self_out)
    weights += (cross_query, cross_key, cross_value, cross_out)
    tokens = (segment_ids, source_segments, context_rank, context_limit, padding)
    meta, rank, limit, norms, ws0, wc0 = call(
        prepare,
        "prepare",
        1,
        [(core.astype(jnp.int32)[None], None)]
        + [token_row(x) for x in tokens]
        + [fixed(x.reshape(1, D)) for x in gains]
        + [fixed(x) for x in weights],
        prepared,
        [],
        0,
    )

    ws1 = to_core(ws0)
    ws2 = to_chip(ws0)
    wc2 = to_chip(wc0)
    u0, u2 = ffn_in, to_chip(ffn_in)
    wf0, wf2 = ffn_out, to_chip(ffn_out)
    meta_in = (meta, None)
    xq = (query_stream, own_row(D))
    xc = (content_stream, own_row(D))
    mem = (memory, own_row(D))
    cot = (cotangent, own_row(D))

    def heads_out(width, heads):
        return [
            ((SEQ, width), bf16, whole((SEQ, width))),
            ((SEQ, width), bf16, whole((SEQ, width))),
            ((SEQ, width), bf16, whole((SEQ, width))),
            ((SEQ, width), bf16, whole((SEQ, width))),
            ((DOCS, heads, FAST_K, FAST_Q), bf16, probability_spec(heads, 0)),
        ]

    def stream_out(dtype):
        return ((SEQ, D), dtype, whole((SEQ, D)))

    def placed(dtype):
        return ((2 * SEQ, D), dtype, own_row(D))

    limits = pltpu.VMEM((SEQ, 128), f32)
    pair_flops = 2 * SEQ * D * 768 + 2 * 2 * 4 * DOCS * FAST_Q * FAST_K * 256

    nq, nc, *first = call(
        self_first,
        "self_first",
        1,
        [meta_in, xq, xc, full(rank), full(limit), full(norms), full(ws0), full(ws1)],
        [stream_out(bf16), stream_out(bf16)] + heads_out(256, 4),
        [limits],
        pair_flops,
    )
    ws2, wc0, nq = hold(ws2, wc0, nq)
    ws3 = to_core(ws2)
    wc1 = to_core(wc0)
    *second_heads, second, ncross = call(
        self_second,
        "self_second",
        1,
        [meta_in, xq, full(nq), full(nc), full(rank), full(limit), full(norms)]
        + [full(w) for w in (ws0, ws1, ws2, ws3)]
        + [full(first[3])],
        heads_out(256, 4) + [stream_out(f32), stream_out(bf16)],
        [limits],
        pair_flops + 2 * SEQ * D * D,
    )
    wc2, u0, wf0, second = hold(wc2, u0, wf0, second)
    wc3 = to_core(wc2)
    u1 = to_core(u0)
    wf1 = to_core(wf0)
    *cross_heads, third, nffn = call(
        cross_forward,
        "cross_forward",
        1,
        [meta_in, full(second), full(ncross), mem, full(norms)]
        + [full(w) for w in (wc0, wc1, wc2, wc3)],
        heads_out(512, 8) + [stream_out(f32), stream_out(bf16)],
        [],
        2 * pair_flops + 2 * SEQ * D * D,
    )
    u2, wf2, third = hold(u2, wf2, third)
    u3 = to_core(u2)
    wf3 = to_core(wf2)
    grads_ln = ((8, D), f32, whole((8, D)))
    placed_output, output, g3, gln_ffn, ffn_own, ffn_other = call(
        ffn_both,
        "ffn_both",
        TILES,
        [meta_in, full(third), full(nffn), cot, full(norms)]
        + [full(w) for w in (u0, u1, u2, u3, wf0, wf1, wf2, wf3)],
        [
            placed(bf16),
            stream_out(bf16),
            stream_out(f32),
            grads_ln,
            ((1024, D), f32, whole((1024, D))),
            ((1024, D), bf16, whole((1024, D))),
        ],
        [pltpu.VMEM((SEQ, 1024), bf16), pltpu.VMEM((SEQ, 1024), bf16)],
        12 * SEQ * D * 2048,
    )

    row_count = lax.axis_size("rows")

    def exchange(x):
        return lax.all_to_all(x, "rows", 0, 0)

    def chunks(n):
        return [((row_count, n, D), bf16)]

    size = 1024 // row_count
    half = size // 2
    (ffn_send,) = simple(join_cores, "join_ffn", [ffn_own, to_core(ffn_other)], chunks(size))
    g3, ffn_send = hold(g3, ffn_send)
    ffn_parts = exchange(ffn_send)

    back_scratch = [pltpu.VMEM((SEQ, 256), bf16)] + [pltpu.VMEM((SEQ, 256), f32)] * 3
    pair_out = ((SEQ, 256), bf16, whole((SEQ, 256)))
    packed_outs = [
        ((D, D), f32, whole((D, D))),
        ((D, D), bf16, whole((D, D))),
    ]
    back_flops = 2 * SEQ * D * 256 + 4 * 2 * 4 * DOCS * FAST_Q * FAST_K * 256

    def head_inputs(arrays, n):
        *natural, p = arrays
        return [(x, columns(256, n)) for x in natural] + [(p, probability_spec(4, n))]

    *cross_grads, cross_own, cross_other = call(
        functools.partial(attention_back_first, True),
        "cross_back_first",
        1,
        [meta_in, full(g3), full(ncross), mem, full(rank), full(limit), full(wc0), full(wc1)]
        + head_inputs(cross_heads, 0),
        [pair_out] * 3 + packed_outs,
        [limits] + back_scratch,
        back_flops + 2 * SEQ * D * 1024,
    )
    ffn_parts, cross_own = hold(ffn_parts, cross_own)
    (ffn_total,) = simple(sum_rows, "sum_ffn", [ffn_parts], chunks(size))
    ffn_total, cross_grads[0] = hold(ffn_total, cross_grads[0])
    ffn_sums = exchange(ffn_total)
    cross_other = to_core(cross_other)
    g2, placed_mem, grad_mem, gln_cross = call(
        cross_back_second,
        "cross_back_second",
        1,
        [meta_in, full(g3), full(second), full(norms)]
        + [full(w) for w in (wc0, wc1, wc2, wc3)]
        + [full(x) for x in cross_grads]
        + head_inputs(cross_heads, 1),
        [stream_out(f32), placed(f32), stream_out(bf16), grads_ln],
        back_scratch,
        back_flops + 2 * SEQ * D * 1536,
    )
    ffn_sums, cross_other, g2 = hold(ffn_sums, cross_other, g2)
    (cross_send,) = simple(join_cores, "join_cross", [cross_own, cross_other], chunks(half))
    cross_send, g2 = hold(cross_send, g2)
    cross_parts = exchange(cross_send)

    *self_grads, self_own, self_other = call(
        functools.partial(attention_back_first, False),
        "self_back_first",
        1,
        [meta_in, full(g2), full(nq), full(nc), full(rank), full(limit), full(ws0), full(ws1)]
        + head_inputs(first, 0),
        [pair_out] * 3 + packed_outs,
        [limits] + back_scratch,
        back_flops + 2 * SEQ * D * 1024,
    )
    self_other = to_core(self_other)
    cross_parts, self_own = hold(cross_parts, self_own)
    (both_send,) = simple(
        sum_rows_join, "sum_cross", [cross_parts, self_own, self_other], chunks(2 * half)
    )
    both_send, g2 = hold(both_send, g2)
    both_parts = exchange(both_send)
    placed_q, placed_c, gq, gc, gln_self = call(
        self_back_second,
        "self_back_second",
        1,
        [meta_in, full(g2), xq, xc, full(rank), full(limit), full(norms)]
        + [full(w) for w in (ws0, ws1, ws2, ws3)]
        + [full(x) for x in self_grads]
        + head_inputs(second_heads, 0),
        [placed(f32), placed(f32), stream_out(bf16), stream_out(bf16), grads_ln],
        [limits] + back_scratch,
        back_flops + 2 * SEQ * D * 1536,
    )

    gln = jnp.concatenate([gln_self[0:4], gln_cross[0:2], gln_ffn[0:2]], axis=0)
    both_parts, gln = hold(both_parts, gln)
    (last_send,) = simple(
        functools.partial(sum_last, half), "sum_self", [both_parts, gln, to_core(gln)], chunks(half + 16)
    )
    last_parts = exchange(last_send)

    def both_rows(placed_own, arrays, name):
        count = len(arrays)
        size = SEQ // 2
        one = pl.BlockSpec((size, D), lambda i, meta: (i, 0))
        block = pl.BlockSpec((size, D), lambda i, meta: (2 * (1 - meta[0]) + i, 0))
        return pl.pallas_call(
            place_rows,
            name=name,
            grid_spec=pltpu.PrefetchScalarGridSpec(
                num_scalar_prefetch=1,
                grid=(2,),
                in_specs=[one] * count + [pl.BlockSpec(memory_space=pl.ANY)] * count,
                out_specs=[block] * count,
            ),
            out_shape=[jax.ShapeDtypeStruct(x.shape, x.dtype) for x in placed_own],
            input_output_aliases={1 + count + n: n for n in range(count)},
        )(meta, *[to_core(x) for x in arrays], *placed_own)

    out_both, grad_mem_both = both_rows([placed_output, placed_mem], [output, grad_mem], "place_early")
    gq_both, gc_both = both_rows([placed_q, placed_c], [gq, gc], "place_late")

    attention_outs = [((512, 128), f32)] * 3 + [((128, 512), f32)]
    grad_ffn_in, grad_ffn_out, *grad_cross_parts = simple(
        unpack_early, "unpack_early", [ffn_sums, both_parts], [((D, D), f32)] * 2 + attention_outs
    )
    *grad_self_parts, gln = simple(
        unpack_late, "unpack_late", [last_parts], attention_outs + [((8, D), f32)]
    )
    return (
        out_both,
        gq_both,
        gc_both,
        grad_mem_both,
        gln[0],
        gln[1],
        gln[2],
        gln[3],
        *grad_self_parts,
        gln[4],
        gln[5],
        *grad_cross_parts,
        gln[6],
        gln[7],
        grad_ffn_in,
        grad_ffn_out,
    )


def solution(mesh):
    assert mesh.shape["heads"] == 4
    row_spec = P("rows", None)
    flat = P("rows")
    by_column = P(None, "heads")
    by_row = P("heads", None)
    attention = (by_column, by_column, by_column, by_row)
    in_specs = (
        (row_spec,) * 3
        + (flat,) * 5
        + (P(),) * 4
        + attention
        + (P(),) * 2
        + attention
        + (P(),) * 2
        + (by_column, by_row, row_spec)
    )
    out_specs = (
        (row_spec,) * 4
        + (P(),) * 4
        + attention
        + (P(),) * 2
        + attention
        + (P(),) * 2
        + (by_column, by_row)
    )
    return jax.shard_map(shards, mesh=mesh, in_specs=in_specs, out_specs=out_specs, check_vma=False)
```

```python
import functools

import jax
import jax.numpy as jnp
from jax import lax
from jax.experimental import pallas as pl
from jax.experimental.pallas import tpu as pltpu
from jax.sharding import PartitionSpec as P

HEAD_DIM = 64
SEQ = 1024
DOCS = 8
D = 512
TILE = 256
TILES = SEQ // TILE
FAST_Q = 256
FAST_K = 208
LONG_Q = 128
LONG_K = 640

norm_eps = 1e-05
masked_score = -1e30
hidden_rank = 1e6
gelu_root = 0.7978845608028654
gelu_cube = 0.044715

f32 = jnp.float32
bf16 = jnp.bfloat16


def dot(a, b):
    return lax.dot_general(a, b, (((1,), (0,)), ((), ())), preferred_element_type=f32)


def dot_nt(a, b):
    return lax.dot_general(a, b, (((1,), (1,)), ((), ())), preferred_element_type=f32)


def dot_tn(a, b):
    return lax.dot_general(a, b, (((0,), (0,)), ((), ())), preferred_element_type=f32)


def lanes(parts):
    return jnp.concatenate(parts, axis=1)


def layer_norm(values, gain, shift):
    centre = values - jnp.mean(values, axis=-1, keepdims=True)
    spread = jnp.mean(centre * centre, axis=-1, keepdims=True)
    return centre * lax.rsqrt(spread + norm_eps) * gain + shift


def norm_backward(values, gain, grad):
    centre = values - jnp.mean(values, axis=-1, keepdims=True)
    spread = jnp.mean(centre * centre, axis=-1, keepdims=True)
    scale = lax.rsqrt(spread + norm_eps)
    xhat = centre * scale
    eg = grad * gain
    mean_eg = jnp.mean(eg, axis=-1, keepdims=True)
    mean_egx = jnp.mean(eg * xhat, axis=-1, keepdims=True)
    grad_gain = jnp.sum(grad * xhat, axis=0, keepdims=True)
    grad_shift = jnp.sum(grad, axis=0, keepdims=True)
    return scale * (eg - mean_eg - xhat * mean_egx), grad_gain, grad_shift


def rows_of(i, size=TILE):
    return pl.ds(pl.multiple_of(i * size, size), size)


def w_query(ref):
    return ref[0:512, :]


def w_key(ref):
    return ref[512:1024, :]


def w_value(ref):
    return ref[1024:1536, :]


def w_out(ref):
    return lanes([ref[1536 + 128 * j : 1664 + 128 * j, :] for j in range(4)])


def half_masks():
    place = lax.broadcasted_iota(jnp.int32, (1, 128), 1)
    low = jnp.where(place < HEAD_DIM, 1.0, 0.0).astype(f32)
    return (low.astype(bf16), (1.0 - low).astype(bf16))


def doc_bounds(meta, d, source):
    base = 17 if source else 1
    return meta[base + d], meta[base + 8 + d]


def window_of(first, limit):
    return pl.multiple_of(jnp.minimum((first // 16) * 16, limit), 16)


def key_bias(ks, ke, k0, width):
    place = k0 + lax.broadcasted_iota(jnp.int32, (width, 128), 0)
    return jnp.where((place >= ks) & (place < ke), 0.0, masked_score)


def make_bias(rank_ref, limit_ref, ks, ke, q0, k0, span, width):
    if rank_ref is None:
        return lanes([key_bias(ks, ke, k0, width)] * (span // 128))
    place = k0 + lax.broadcasted_iota(jnp.int32, (width, 128), 0)
    ranks = rank_ref[pl.ds(k0, width), :]
    ranks = jnp.where((place < ks + 2) & (ranks < hidden_rank), -1.0, ranks)
    ranks = jnp.where((place >= ks) & (place < ke), ranks, hidden_rank)
    limits = jnp.broadcast_to(limit_ref[...], (8, SEQ))
    limits = pltpu.roll(limits, lax.rem(SEQ - q0, SEQ), 1)[0:1, 0:span]
    row = k0 + lax.broadcasted_iota(jnp.int32, (width, span), 0)
    column = q0 + lax.broadcasted_iota(jnp.int32, (width, span), 1)
    seen = (lanes([ranks] * (span // 128)) < limits) & (row != column)
    return jnp.where(seen, 0.0, masked_score)


STEPS = DOCS // 2


def is_fast(meta, cross):
    return meta[34 if cross else 33] == 1


def both_heads(x, masks):
    return jnp.concatenate([x * masks[0], x * masks[1]], axis=0)


def pair_probabilities(queries, keys, masks, bias):
    width = keys.shape[0]
    scores = dot_nt(both_heads(keys, masks), queries)
    result = []
    for a in range(2):
        part = scores[width * a : width * a + width] + bias
        part = jnp.exp(part - jnp.max(part, axis=0, keepdims=True))
        part = part * (1.0 / jnp.sum(part, axis=0, keepdims=True))
        result.append(part.astype(bf16))
    return result


def pair_product(rows, parts):
    across = jnp.transpose(rows)
    halves = [dot(across[64 * a : 64 * a + 64], part) for a, part in enumerate(parts)]
    return jnp.transpose(jnp.concatenate(halves, axis=0))


def for_docs(meta, cross, run, before, after):
    @pl.when(is_fast(meta, cross))
    def _():
        def step(i, carry):
            slot = lax.rem(i, 2)
            before(i, slot)
            for place in range(2):
                d = 2 * i + place
                ts, te = doc_bounds(meta, d, False)
                ks, ke = doc_bounds(meta, d, cross)
                q0 = window_of(ts, SEQ - FAST_Q)
                k0 = window_of(ks, SEQ - FAST_K)
                run(d, slot, place, q0, k0, FAST_Q, FAST_K, ts, te, ks, ke, True)
            after(i, slot)
            return carry

        lax.fori_loop(0, STEPS, step, 0)

    @pl.when(jnp.logical_not(is_fast(meta, cross)))
    def _():
        def doc(d, carry):
            ts, te = doc_bounds(meta, d, False)
            ks, ke = doc_bounds(meta, d, cross)
            base = (ts // 16) * 16
            k0 = window_of(ks, SEQ - LONG_K)

            def chunk(i, carry):
                lower = base + i * LONG_Q
                q0 = pl.multiple_of(jnp.minimum(lower, SEQ - LONG_Q), 16)
                low = jnp.maximum(ts, lower)
                high = jnp.minimum(te, lower + LONG_Q)
                run(d, None, None, q0, k0, LONG_Q, LONG_K, low, high, ks, ke, False)
                return carry

            return lax.fori_loop(0, (te - base + LONG_Q - 1) // LONG_Q, chunk, carry)

        lax.fori_loop(0, DOCS, doc, 0)


def attend_docs(meta, cross, rank_ref, limit_ref, halves, p_ref, p_buf, p_sem):
    pairs = 2 * len(halves)
    masks = half_masks()

    def save(i, slot):
        return pltpu.make_async_copy(p_buf.at[slot], p_ref.at[pl.ds(2 * i, 2)], p_sem.at[slot])

    def before(i, slot):
        @pl.when(i >= 2)
        def _():
            save(i - 2, slot).wait()

    def after(i, slot):
        save(i, slot).start()

    def run(d, slot, place, q0, k0, span, width, low, high, ks, ke, fast):
        bias = make_bias(rank_ref, limit_ref, ks, ke, q0, k0, span, width)
        row = q0 + lax.broadcasted_iota(jnp.int32, (span, 128), 0)
        inside = (row >= low) & (row < high)
        for n in range(pairs):
            q_ref, k_ref, v_ref, mixed_ref = halves[n // 2]
            cols = slice(128 * (n % 2), 128 * (n % 2) + 128)
            queries = q_ref[pl.ds(q0, span), cols]
            keys = k_ref[pl.ds(k0, width), cols]
            values = v_ref[pl.ds(k0, width), cols]
            parts = pair_probabilities(queries, keys, masks, bias)
            if fast:
                for a in range(2):
                    p_buf[slot, place, 2 * n + a] = parts[a]
            mixed = pair_product(values, parts)
            old = mixed_ref[pl.ds(q0, span), cols].astype(f32)
            mixed_ref[pl.ds(q0, span), cols] = jnp.where(inside, mixed, old).astype(bf16)

    for_docs(meta, cross, run, before, after)

    @pl.when(is_fast(meta, cross))
    def _():
        for i in range(STEPS - 2, STEPS):
            save(i, i % 2).wait()


def load_step(load, i, slot):
    p_ref, p_buf, p_sem, first = load
    part = p_ref.at[pl.ds(2 * i, 2), pl.ds(first, 4)]
    return pltpu.make_async_copy(part, p_buf.at[slot], p_sem.at[slot])


def start_load(meta, cross, load):
    @pl.when(is_fast(meta, cross))
    def _():
        load_step(load, 0, 0).start()


def attend_docs_back(
    meta, cross, rank_ref, limit_ref, q_ref, k_ref, v_ref, mixed_ref, dm_ref,
    dq_ref, dk_ref, dv_ref, load,
):
    pairs = q_ref.shape[1] // 128
    masks = half_masks()
    p_buf = load[1]

    def before(i, slot):
        @pl.when(i + 1 < STEPS)
        def _():
            load_step(load, i + 1, 1 - slot).start()

        load_step(load, i, slot).wait()

    def after(i, slot):
        pass

    def run(d, slot, place, q0, k0, span, width, low, high, ks, ke, fast):
        row = q0 + lax.broadcasted_iota(jnp.int32, (span, 128), 0)
        inside = (row >= low) & (row < high)
        ones = jnp.ones((width, 128), bf16)
        if not fast:
            bias = make_bias(rank_ref, limit_ref, ks, ke, q0, k0, span, width)
        for n in range(pairs):
            cols = slice(128 * n, 128 * n + 128)
            queries = q_ref[pl.ds(q0, span), cols]
            keys = k_ref[pl.ds(k0, width), cols]
            values = v_ref[pl.ds(k0, width), cols]
            mixed = mixed_ref[pl.ds(q0, span), cols].astype(f32)
            grad = jnp.where(inside, dm_ref[pl.ds(q0, span), cols].astype(f32), 0.0)
            low_grad = grad.astype(bf16)
            left = lanes([low_grad, (-(grad * mixed)).astype(bf16)])
            delta = dot_nt(both_heads(lanes([values, ones]), [lanes([m, m]) for m in masks]), left)
            if fast:
                parts = [p_buf[slot, place, 2 * n + a] for a in range(2)]
            else:
                parts = pair_probabilities(queries, keys, masks, bias)
            slopes = []
            dk = dv = None
            for a in range(2):
                slope = parts[a].astype(f32) * delta[width * a : width * a + width]
                slopes.append(slope.astype(bf16))
                dk_a = dot(slopes[a], queries * masks[a])
                dv_a = dot(parts[a], low_grad * masks[a])
                dk = dk_a if dk is None else dk + dk_a
                dv = dv_a if dv is None else dv + dv_a
            dq = pair_product(keys, slopes)
            dq_ref[pl.ds(q0, span), cols] += dq * (HEAD_DIM**-0.5)
            dk_ref[pl.ds(k0, width), cols] += dk
            dv_ref[pl.ds(k0, width), cols] += dv

    for_docs(meta, cross, run, before, after)


def spread_ranks(rank_row_ref, rank_ref):
    rank_ref[...] = jnp.transpose(jnp.broadcast_to(rank_row_ref[...], (128, SEQ)))


def prepare(
    core, seg_ref, src_ref, rank_ref, limit_ref, pad_ref,
    n0, n1, n2, n3, n4, n5, n6, n7, sq, sk, sv, so, cq, ck, cv, co,
    meta_ref, ranks_ref, limits_ref, norms_ref, ws_ref, wc_ref,
):
    meta_ref[0] = core[0]
    for base, ref in ((1, seg_ref), (17, src_ref)):
        ids = ref[0]
        meta_ref[base] = 0
        meta_ref[base + 15] = SEQ
        for d in range(1, DOCS):
            cut = jnp.sum(jnp.where(ids < d, 1.0, 0.0)).astype(jnp.int32)
            meta_ref[base + d] = cut
            meta_ref[base + 7 + d] = cut
    for place, base in ((33, 1), (34, 17)):
        fast = jnp.int32(1)
        for d in range(DOCS):
            q0 = window_of(meta_ref[1 + d], SEQ - FAST_Q)
            k0 = window_of(meta_ref[base + d], SEQ - FAST_K)
            fits = (meta_ref[9 + d] - q0 <= FAST_Q) & (meta_ref[base + 8 + d] - k0 <= FAST_K)
            fast = fast & fits.astype(jnp.int32)
        meta_ref[place] = fast
    ranks = jnp.where(pad_ref[0] != 0, hidden_rank, rank_ref[0].astype(f32))
    limits = limit_ref[0].astype(f32)
    for i in range(8):
        ranks_ref[0:1, 128 * i : 128 * i + 128] = ranks[i : i + 1]
        limits_ref[0:1, 128 * i : 128 * i + 128] = limits[i : i + 1]
    for i, ref in enumerate((n0, n1, n2, n3, n4, n5, n6, n7)):
        norms_ref[i : i + 1, :] = ref[...]
    for to, parts, out in ((ws_ref, (sq, sk, sv), so), (wc_ref, (cq, ck, cv), co)):
        for i, part in enumerate(parts):
            to[512 * i : 512 * i + 512, :] = part[...]
        for j in range(4):
            to[1536 + 128 * j : 1664 + 128 * j, :] = out[:, 128 * j : 128 * j + 128]


def self_first(
    meta, xq_ref, xc_ref, rank_row_ref, limit_ref, norms_ref, w0_ref, w1_ref,
    nq_ref, nc_ref, q_ref, k_ref, v_ref, mixed_ref, p_ref, rank_ref, p_buf, p_sem,
):

    spread_ranks(rank_row_ref, rank_ref)
    wq = lanes([w_query(w0_ref), w_query(w1_ref)])
    wkv = lanes([w_key(w0_ref), w_key(w1_ref), w_value(w0_ref), w_value(w1_ref)])

    def tile(i, carry):
        rows = rows_of(i)
        nq = layer_norm(xq_ref[rows, :].astype(f32), norms_ref[0:1], norms_ref[1:2]).astype(bf16)
        nc = layer_norm(xc_ref[rows, :].astype(f32), norms_ref[2:3], norms_ref[3:4]).astype(bf16)
        nq_ref[rows, :] = nq
        nc_ref[rows, :] = nc
        q_ref[rows, :] = (dot(nq, wq) * (HEAD_DIM**-0.5)).astype(bf16)
        kv = dot(nc, wkv).astype(bf16)
        k_ref[rows, :] = kv[:, :256]
        v_ref[rows, :] = kv[:, 256:]
        return carry

    lax.fori_loop(0, TILES, tile, 0)

    attend_docs(meta, False, rank_ref, limit_ref, [(q_ref, k_ref, v_ref, mixed_ref)], p_ref, p_buf, p_sem)


def self_second(
    meta, xq_ref, nq_ref, nc_ref, rank_row_ref, limit_ref, norms_ref, w0_ref, w1_ref, w2_ref, w3_ref,
    mixed_first_ref,
    q_ref, k_ref, v_ref, mixed_ref, p_ref, second_ref, ncross_ref, rank_ref, p_buf, p_sem,
):

    spread_ranks(rank_row_ref, rank_ref)
    wq = lanes([w_query(w2_ref), w_query(w3_ref)])
    wkv = lanes([w_key(w2_ref), w_key(w3_ref), w_value(w2_ref), w_value(w3_ref)])

    def tile(i, carry):
        rows = rows_of(i)
        q_ref[rows, :] = (dot(nq_ref[rows, :], wq) * (HEAD_DIM**-0.5)).astype(bf16)
        kv = dot(nc_ref[rows, :], wkv).astype(bf16)
        k_ref[rows, :] = kv[:, :256]
        v_ref[rows, :] = kv[:, 256:]
        return carry

    lax.fori_loop(0, TILES, tile, 0)

    attend_docs(meta, False, rank_ref, limit_ref, [(q_ref, k_ref, v_ref, mixed_ref)], p_ref, p_buf, p_sem)

    out_first = jnp.concatenate([w_out(w0_ref), w_out(w1_ref)], axis=0)
    out_second = jnp.concatenate([w_out(w2_ref), w_out(w3_ref)], axis=0)

    def tile(i, carry):
        rows = rows_of(i)
        branch = dot(mixed_first_ref[rows, :], out_first) + dot(mixed_ref[rows, :], out_second)
        second = xq_ref[rows, :].astype(f32) + branch
        second_ref[rows, :] = second
        ncross_ref[rows, :] = layer_norm(second, norms_ref[4:5], norms_ref[5:6]).astype(bf16)
        return carry

    lax.fori_loop(0, TILES, tile, 0)


def cross_forward(
    meta, second_ref, ncross_ref, memory_ref, norms_ref, w0_ref, w1_ref, w2_ref, w3_ref,
    qa_ref, ka_ref, va_ref, ma_ref, qb_ref, kb_ref, vb_ref, mb_ref, p_ref, third_ref, nffn_ref, p_buf, p_sem,
):
    halves = ((qa_ref, ka_ref, va_ref, ma_ref), (qb_ref, kb_ref, vb_ref, mb_ref))
    weights = (w0_ref, w1_ref, w2_ref, w3_ref)

    wq = lanes([w_query(w) for w in weights])
    wk = lanes([w_key(w) for w in weights])
    wv = lanes([w_value(w) for w in weights])

    def tile(i, carry):
        rows = rows_of(i)
        memory = memory_ref[rows, :]
        q = (dot(ncross_ref[rows, :], wq) * (HEAD_DIM**-0.5)).astype(bf16)
        k = dot(memory, wk).astype(bf16)
        v = dot(memory, wv).astype(bf16)
        for n, (q_ref, k_ref, v_ref, _) in enumerate(halves):
            cols = slice(256 * n, 256 * n + 256)
            q_ref[rows, :] = q[:, cols]
            k_ref[rows, :] = k[:, cols]
            v_ref[rows, :] = v[:, cols]
        return carry

    lax.fori_loop(0, TILES, tile, 0)

    attend_docs(meta, True, None, None, halves, p_ref, p_buf, p_sem)

    out_first = jnp.concatenate([w_out(w0_ref), w_out(w1_ref)], axis=0)
    out_second = jnp.concatenate([w_out(w2_ref), w_out(w3_ref)], axis=0)

    def tile(i, carry):
        rows = rows_of(i)
        branch = dot(ma_ref[rows, :], out_first) + dot(mb_ref[rows, :], out_second)
        third = second_ref[rows, :] + branch
        third_ref[rows, :] = third
        nffn_ref[rows, :] = layer_norm(third, norms_ref[6:7], norms_ref[7:8]).astype(bf16)
        return carry

    lax.fori_loop(0, TILES, tile, 0)


def ffn_both(
    meta, third_ref, nffn_ref, cot_ref, norms_ref, u0_ref, u1_ref, u2_ref, u3_ref,
    w0_ref, w1_ref, w2_ref, w3_ref,
    placed_ref, out_ref, g3_ref, gln_ref, own_ref, other_ref, hidden_ref, before_ref,
):
    i = pl.program_id(0)
    rows = rows_of(i)
    nffn = nffn_ref[rows, :]
    cot = cot_ref[rows, :]
    outs = []
    grads = []
    in_refs = (u0_ref, u1_ref, u2_ref, u3_ref)
    for g, w_ref in enumerate((w0_ref, w1_ref, w2_ref, w3_ref)):
        w_in = in_refs[g][...]
        w_out_rows = w_ref[...]
        x = dot(nffn, w_in)
        square = x * x
        half = 0.5 + 0.5 * jnp.tanh(x * (gelu_root + (gelu_root * gelu_cube) * square))
        value = x * half
        hidden = value.astype(bf16)
        rise = 2.0 * gelu_root + (6.0 * gelu_root * gelu_cube) * square
        slope = half + value * (1.0 - half) * rise
        grad_before = (dot_nt(cot, w_out_rows) * slope).astype(bf16)
        outs.append(dot(hidden, w_out_rows))
        grads.append(dot_nt(grad_before, w_in))
        if g < 2:
            hidden_ref[rows, 512 * g : 512 * g + 512] = hidden
            before_ref[rows, 512 * g : 512 * g + 512] = grad_before
    third = third_ref[rows, :]
    out = (third + ((outs[0] + outs[1]) + (outs[2] + outs[3]))).astype(bf16)
    out_ref[rows, :] = out
    placed_ref[rows, :] = out
    grad_normed = (grads[0] + grads[1]) + (grads[2] + grads[3])
    grad_norm, grad_gain, grad_shift = norm_backward(third, norms_ref[6:7], grad_normed)
    g3_ref[rows, :] = cot.astype(f32) + grad_norm

    @pl.when(i == 0)
    def _():
        gln_ref[0:1, :] = grad_gain
        gln_ref[1:2, :] = grad_shift

    @pl.when(i > 0)
    def _():
        gln_ref[0:1, :] += grad_gain
        gln_ref[1:2, :] += grad_shift

    @pl.when(i == TILES - 1)
    def _():
        nffn_all = nffn_ref[...]
        cot_all = cot_ref[...]
        part = dot_tn(nffn_all, before_ref[...])
        own_ref[0:512, :] = part[:, 0:512]
        other_ref[0:512, :] = part[:, 512:1024].astype(bf16)
        part = dot_tn(hidden_ref[...], cot_all)
        own_ref[512:1024, :] = part[0:512]
        other_ref[512:1024, :] = part[512:1024].astype(bf16)


def back_start(g_ref, mixed_ref, w_refs, dm_ref, dq_ref, dk_ref, dv_ref):
    out_rows = jnp.concatenate([w_out(w) for w in w_refs], axis=0)

    def tile(i, carry):
        rows = rows_of(i)
        dm_ref[rows, :] = dot_nt(g_ref[rows, :].astype(bf16), out_rows).astype(bf16)
        zeros = jnp.zeros((TILE, 256), f32)
        dq_ref[rows, :] = zeros
        dk_ref[rows, :] = zeros
        dv_ref[rows, :] = zeros
        return carry

    lax.fori_loop(0, TILES, tile, 0)


def attention_back_first(
    cross, meta, g_ref, nq_ref, nkv_ref, rank_row_ref, limit_ref, w0_ref, w1_ref,
    q_ref, k_ref, v_ref, mixed_ref, p_ref,
    dq_ref, dk_ref, dv_ref, own_ref, other_ref,
    rank_ref, dm_ref, dqs_ref, dks_ref, dvs_ref, p_buf, p_sem,
):
    load = (p_ref, p_buf, p_sem, 0)
    start_load(meta, cross, load)
    if not cross:
        spread_ranks(rank_row_ref, rank_ref)
    back_start(g_ref, mixed_ref, (w0_ref, w1_ref), dm_ref, dqs_ref, dks_ref, dvs_ref)

    attend_docs_back(
        meta, cross, None if cross else rank_ref, limit_ref, q_ref, k_ref, v_ref, mixed_ref,
        dm_ref, dqs_ref, dks_ref, dvs_ref, load,
    )

    dq_ref[...] = dqs_ref[...].astype(bf16)
    dk_ref[...] = dks_ref[...].astype(bf16)
    dv_ref[...] = dvs_ref[...].astype(bf16)
    nq = nq_ref[...]
    nkv = nkv_ref[...]
    for n, part in enumerate(
        (dot_tn(nq, dq_ref[...]), dot_tn(nkv, dk_ref[...]), dot_tn(nkv, dv_ref[...]))
    ):
        own_ref[:, 128 * n : 128 * n + 128] = part[:, :128]
        other_ref[:, 128 * n : 128 * n + 128] = part[:, 128:].astype(bf16)
    part = dot_tn(mixed_ref[...], g_ref[...].astype(bf16))
    for j in range(4):
        rows = slice(128 * j, 128 * j + 128)
        own_ref[rows, 384:512] = part[:128, rows]
        other_ref[rows, 384:512] = part[128:, rows].astype(bf16)


def back_second_docs(
    cross, meta, g_ref, rank_row_ref, limit_ref, w_refs, q_ref, k_ref, v_ref, mixed_ref, p_ref,
    rank_ref, dm_ref, dqs_ref, dks_ref, dvs_ref, p_buf, p_sem,
):
    load = (p_ref, p_buf, p_sem, 4 if cross else 0)
    start_load(meta, cross, load)
    if not cross:
        spread_ranks(rank_row_ref, rank_ref)
    back_start(g_ref, mixed_ref, w_refs, dm_ref, dqs_ref, dks_ref, dvs_ref)

    attend_docs_back(
        meta, cross, None if cross else rank_ref, limit_ref, q_ref, k_ref, v_ref, mixed_ref,
        dm_ref, dqs_ref, dks_ref, dvs_ref, load,
    )


def stream_grads(rows, first, second, firsts, seconds):
    dq, dk, dv = first
    dq2, dk2, dv2 = (ref[rows, :].astype(bf16) for ref in second)
    w0, w1 = firsts
    w2, w3 = seconds
    grad_q = dot_nt(dq[rows, :], lanes([w_query(w0), w_query(w1)])) + dot_nt(
        dq2, lanes([w_query(w2), w_query(w3)])
    )
    kv = lanes([dk[rows, :], dv[rows, :]])
    kv2 = lanes([dk2, dv2])
    grad_kv = dot_nt(kv, lanes([w_key(w0), w_key(w1), w_value(w0), w_value(w1)])) + dot_nt(
        kv2, lanes([w_key(w2), w_key(w3), w_value(w2), w_value(w3)])
    )
    return grad_q, grad_kv


def cross_back_second(
    meta, g_ref, second_ref, norms_ref, w0_ref, w1_ref, w2_ref, w3_ref,
    dq_ref, dk_ref, dv_ref, q_ref, k_ref, v_ref, mixed_ref, p_ref,
    g2_ref, placed_ref, gmem_ref, gln_ref,
    dm_ref, dqs_ref, dks_ref, dvs_ref, p_buf, p_sem,
):
    back_second_docs(
        True, meta, g_ref, None, None, (w2_ref, w3_ref), q_ref, k_ref, v_ref, mixed_ref, p_ref,
        None, dm_ref, dqs_ref, dks_ref, dvs_ref, p_buf, p_sem,
    )

    gln_ref[...] = jnp.zeros_like(gln_ref)

    def tile(i, carry):
        rows = rows_of(i)
        grad_q, grad_kv = stream_grads(
            rows,
            (dq_ref, dk_ref, dv_ref),
            (dqs_ref, dks_ref, dvs_ref),
            (w0_ref, w1_ref),
            (w2_ref, w3_ref),
        )
        low_kv = grad_kv.astype(bf16)
        gmem_ref[rows, :] = low_kv
        placed_ref[rows, :] = low_kv.astype(f32)
        grad_norm, grad_gain, grad_shift = norm_backward(
            second_ref[rows, :], norms_ref[4:5], grad_q
        )
        g2_ref[rows, :] = g_ref[rows, :] + grad_norm
        gln_ref[0:1, :] += grad_gain
        gln_ref[1:2, :] += grad_shift
        return carry

    lax.fori_loop(0, TILES, tile, 0)


def self_back_second(
    meta, g_ref, xq_ref, xc_ref, rank_row_ref, limit_ref, norms_ref, w0_ref, w1_ref, w2_ref, w3_ref,
    dq_ref, dk_ref, dv_ref, q_ref, k_ref, v_ref, mixed_ref, p_ref,
    placed_q_ref, placed_c_ref, gq_ref, gc_ref, gln_ref,
    rank_ref, dm_ref, dqs_ref, dks_ref, dvs_ref, p_buf, p_sem,
):
    back_second_docs(
        False, meta, g_ref, rank_row_ref, limit_ref, (w2_ref, w3_ref), q_ref, k_ref, v_ref, mixed_ref,
        p_ref, rank_ref, dm_ref, dqs_ref, dks_ref, dvs_ref, p_buf, p_sem,
    )

    gln_ref[...] = jnp.zeros_like(gln_ref)

    def tile(i, carry):
        rows = rows_of(i)
        grad_q, grad_kv = stream_grads(
            rows,
            (dq_ref, dk_ref, dv_ref),
            (dqs_ref, dks_ref, dvs_ref),
            (w0_ref, w1_ref),
            (w2_ref, w3_ref),
        )
        grad_norm, grad_gain, grad_shift = norm_backward(
            xq_ref[rows, :].astype(f32), norms_ref[0:1], grad_q
        )
        low_q = (g_ref[rows, :] + grad_norm).astype(bf16)
        gq_ref[rows, :] = low_q
        placed_q_ref[rows, :] = low_q.astype(f32)
        gln_ref[0:1, :] += grad_gain
        gln_ref[1:2, :] += grad_shift
        grad_norm, grad_gain, grad_shift = norm_backward(
            xc_ref[rows, :].astype(f32), norms_ref[2:3], grad_kv
        )
        low_c = grad_norm.astype(bf16)
        gc_ref[rows, :] = low_c
        placed_c_ref[rows, :] = low_c.astype(f32)
        gln_ref[2:3, :] += grad_gain
        gln_ref[3:4, :] += grad_shift
        return carry

    lax.fori_loop(0, TILES, tile, 0)


def place_rows(meta, *refs):
    count = len(refs) // 3
    for n in range(count):
        refs[2 * count + n][...] = refs[n][...].astype(refs[2 * count + n].dtype)


def join_cores(own, other, send):
    joined = own[...] + other[...].astype(f32)
    send[...] = joined.astype(bf16).reshape(send.shape)


def summed(parts, size, first):
    total = parts[0, first : first + size, :].astype(f32)
    for r in range(1, parts.shape[0]):
        total = total + parts[r, first : first + size, :].astype(f32)
    return total.astype(bf16)


def sum_rows(parts, send):
    count, size, _ = parts.shape
    total = summed(parts, size, 0)
    for r in range(count):
        send[r] = total


def sum_rows_join(parts, own, other, send):
    count, done, _ = parts.shape
    size = own.shape[0] // count
    total = summed(parts, done, 0)
    for r in range(count):
        rows = slice(size * r, size * r + size)
        send[r, 0:done, :] = total
        send[r, done : done + size, :] = (own[rows, :] + other[rows, :].astype(f32)).astype(bf16)


def sum_last(done, parts, gln_own, gln_other, send):
    count = parts.shape[0]
    size = parts.shape[1] - done
    total = summed(parts, size, done)
    gln = gln_own[...] + gln_other[...]
    gln = jnp.concatenate([gln, jnp.zeros((8, D), f32)], axis=0).astype(bf16)
    for r in range(count):
        send[r, 0:size, :] = total
        send[r, size : size + 16, :] = gln


def unpack_attention(parts, outs):
    count = parts.shape[0]
    size = D // count
    for r in range(count):
        rows = slice(size * r, size * r + size)
        for i in range(3):
            outs[i][rows, :] = parts[r, 0:size, 128 * i : 128 * i + 128].astype(f32)
        j, first = divmod(size * r, 128)
        outs[3][first : first + size, 128 * j : 128 * j + 128] = parts[r, 0:size, 384:512].astype(f32)


def unpack_early(ffn, cross, *outs):
    count, size, _ = ffn.shape
    for r in range(count):
        out = outs[2 * r // count]
        first = (size * r) % D
        out[first : first + size, :] = ffn[r].astype(f32)
    unpack_attention(cross, outs[2:])


def unpack_late(parts, *outs):
    unpack_attention(parts, outs[:4])
    size = parts.shape[1] - 16
    total = parts[0, size : size + 16, :].astype(f32)
    for r in range(1, parts.shape[0]):
        total = total + parts[r, size : size + 16, :].astype(f32)
    outs[4][...] = total[0:8]


def whole(shape):
    zeros = (0,) * len(shape)
    return pl.BlockSpec(shape, lambda d, meta: zeros)


def own_row(width):
    return pl.BlockSpec((SEQ, width), lambda d, meta: (meta[0], 0))


def in_hbm(x):
    return pltpu.with_memory_space_constraint(x, pltpu.HBM)


def probability_out(heads):
    return (pltpu.HBM((DOCS, heads, FAST_K, FAST_Q), bf16), None, pl.BlockSpec(memory_space=pl.ANY))


def probability_scratch(heads):
    return [pltpu.VMEM((2, 2, heads, FAST_K, FAST_Q), bf16), pltpu.SemaphoreType.DMA((2,))]


def call(kernel, name, grid, operands, outs, scratch, flops):
    moved = sum(x.size * x.dtype.itemsize for x, _ in operands[1:])
    return pl.pallas_call(
        kernel,
        name=name,
        grid_spec=pltpu.PrefetchScalarGridSpec(
            num_scalar_prefetch=1,
            grid=(grid,),
            in_specs=[spec for _, spec in operands[1:]],
            out_specs=[spec for _, _, spec in outs],
            scratch_shapes=scratch,
        ),
        out_shape=[
            jax.ShapeDtypeStruct(shape, dtype) if dtype else shape for shape, dtype, _ in outs
        ],
        compiler_params=pltpu.CompilerParams(
            dimension_semantics=("arbitrary",), vmem_limit_bytes=16 * 1024 * 1024
        ),
        cost_estimate=pl.CostEstimate(
            flops=int(flops), bytes_accessed=int(moved), transcendentals=0
        ),
    )(*[x for x, _ in operands])


def simple(kernel, name, operands, outs):
    return pl.pallas_call(
        kernel,
        name=name,
        out_shape=[jax.ShapeDtypeStruct(shape, dtype) for shape, dtype in outs],
        compiler_params=pltpu.CompilerParams(vmem_limit_bytes=8 * 1024 * 1024),
    )(*operands)


def full(x):
    return (x, whole(x.shape))


def shards(
    query_stream,
    content_stream,
    memory,
    segment_ids,
    source_segments,
    context_rank,
    context_limit,
    padding,
    ln_query_gain,
    ln_query_bias,
    ln_content_gain,
    ln_content_bias,
    self_query,
    self_key,
    self_value,
    self_out,
    ln_cross_gain,
    ln_cross_bias,
    cross_query,
    cross_key,
    cross_value,
    cross_out,
    ln_ffn_gain,
    ln_ffn_bias,
    ffn_in,
    ffn_out,
    cotangent,
):
    core = lax.axis_index("heads") % 2

    def to_core(x):
        return lax.ppermute(x, "heads", [(h, h ^ 1) for h in range(4)])

    hold = lambda *xs: lax.optimization_barrier(xs)

    def to_chip(x):
        return lax.ppermute(x, "heads", [(h, h ^ 2) for h in range(4)])

    row = pl.BlockSpec((1, 8, 128), lambda d, core: (core[0], 0, 0))

    def token_row(x):
        return (in_hbm(x.reshape(2, 8, 128)), row)

    def fixed(x):
        zeros = (0,) * x.ndim
        return (in_hbm(x), pl.BlockSpec(x.shape, lambda d, core: zeros))

    prepared = [
        ((35,), jnp.int32, pl.BlockSpec(memory_space=pltpu.SMEM)),
        ((1, SEQ), f32, whole((1, SEQ))),
        ((1, SEQ), f32, whole((1, SEQ))),
        ((8, D), f32, whole((8, D))),
        ((2048, 128), bf16, whole((2048, 128))),
        ((2048, 128), bf16, whole((2048, 128))),
    ]
    gains = (
        ln_query_gain,
        ln_query_bias,
        ln_content_gain,
        ln_content_bias,
        ln_cross_gain,
        ln_cross_bias,
        ln_ffn_gain,
        ln_ffn_bias,
    )
    weights = (self_query, self_key, self_value, self_out)
    weights += (cross_query, cross_key, cross_value, cross_out)
    tokens = (segment_ids, source_segments, context_rank, context_limit, padding)
    meta, rank, limit, norms, ws0, wc0 = call(
        prepare,
        "prepare",
        1,
        [(core.astype(jnp.int32)[None], None)]
        + [token_row(x) for x in tokens]
        + [fixed(x.reshape(1, D)) for x in gains]
        + [fixed(x) for x in weights],
        prepared,
        [],
        0,
    )

    ws1 = to_core(ws0)
    ws2 = to_chip(ws0)
    wc2 = to_chip(wc0)
    u0, u2 = ffn_in, to_chip(ffn_in)
    wf0, wf2 = ffn_out, to_chip(ffn_out)
    meta_in = (meta, None)
    xq = (in_hbm(query_stream), own_row(D))
    xc = (in_hbm(content_stream), own_row(D))
    mem = (in_hbm(memory), own_row(D))
    cot = (in_hbm(cotangent), own_row(D))

    def heads_out(width=256):
        return [
            ((SEQ, width), bf16, whole((SEQ, width))),
            ((SEQ, width), bf16, whole((SEQ, width))),
            ((SEQ, width), bf16, whole((SEQ, width))),
            ((SEQ, width), bf16, whole((SEQ, width))),
        ]

    def stream_out(dtype):
        return ((SEQ, D), dtype, whole((SEQ, D)))

    def placed(dtype):
        return ((2 * SEQ, D), dtype, own_row(D))

    limits = pltpu.VMEM((SEQ, 128), f32)
    pair_flops = 2 * SEQ * D * 768 + 2 * 2 * 4 * DOCS * FAST_Q * FAST_K * 256

    nq, nc, *first = call(
        self_first,
        "self_first",
        1,
        [meta_in, xq, xc, full(rank), full(limit), full(norms), full(ws0), full(ws1)],
        [stream_out(bf16), stream_out(bf16)] + heads_out() + [probability_out(4)],
        [limits] + probability_scratch(4),
        pair_flops,
    )
    ws2, wc0, nq = hold(ws2, wc0, nq)
    ws3 = to_core(ws2)
    wc1 = to_core(wc0)
    *second_heads, second, ncross = call(
        self_second,
        "self_second",
        1,
        [meta_in, xq, full(nq), full(nc), full(rank), full(limit), full(norms)]
        + [full(w) for w in (ws0, ws1, ws2, ws3)]
        + [full(first[3])],
        heads_out() + [probability_out(4), stream_out(f32), stream_out(bf16)],
        [limits] + probability_scratch(4),
        pair_flops + 2 * SEQ * D * D,
    )
    wc2, u0, wf0, second = hold(wc2, u0, wf0, second)
    wc3 = to_core(wc2)
    u1 = to_core(u0)
    wf1 = to_core(wf0)
    *cross_heads, third, nffn = call(
        cross_forward,
        "cross_forward",
        1,
        [meta_in, full(second), full(ncross), mem, full(norms)]
        + [full(w) for w in (wc0, wc1, wc2, wc3)],
        heads_out() + heads_out() + [probability_out(8), stream_out(f32), stream_out(bf16)],
        probability_scratch(8),
        2 * pair_flops + 2 * SEQ * D * D,
    )
    u2, wf2, third = hold(u2, wf2, third)
    u3 = to_core(u2)
    wf3 = to_core(wf2)
    grads_ln = ((8, D), f32, whole((8, D)))
    placed_output, output, g3, gln_ffn, ffn_own, ffn_other = call(
        ffn_both,
        "ffn_both",
        TILES,
        [meta_in, full(third), full(nffn), cot, full(norms)]
        + [full(w) for w in (u0, u1, u2, u3, wf0, wf1, wf2, wf3)],
        [
            placed(bf16),
            stream_out(bf16),
            stream_out(f32),
            grads_ln,
            ((1024, D), f32, whole((1024, D))),
            ((1024, D), bf16, whole((1024, D))),
        ],
        [pltpu.VMEM((SEQ, 1024), bf16), pltpu.VMEM((SEQ, 1024), bf16)],
        12 * SEQ * D * 2048,
    )

    row_count = lax.axis_size("rows")

    def exchange(x):
        return lax.all_to_all(x, "rows", 0, 0)

    def chunks(n):
        return [((row_count, n, D), bf16)]

    size = 1024 // row_count
    half = size // 2
    (ffn_send,) = simple(join_cores, "join_ffn", [ffn_own, to_core(ffn_other)], chunks(size))
    g3, ffn_send = hold(g3, ffn_send)
    ffn_parts = exchange(ffn_send)

    back_scratch = [pltpu.VMEM((SEQ, 256), bf16)] + [pltpu.VMEM((SEQ, 256), f32)] * 3
    back_scratch += probability_scratch(4)
    pair_out = ((SEQ, 256), bf16, whole((SEQ, 256)))
    packed_outs = [
        ((D, D), f32, whole((D, D))),
        ((D, D), bf16, whole((D, D))),
    ]
    back_flops = 2 * SEQ * D * 256 + 4 * 2 * 4 * DOCS * FAST_Q * FAST_K * 256

    def head_inputs(natural, p):
        return [full(x) for x in natural] + [(in_hbm(p), pl.BlockSpec(memory_space=pl.ANY))]

    *cross_grads, cross_own, cross_other = call(
        functools.partial(attention_back_first, True),
        "cross_back_first",
        1,
        [meta_in, full(g3), full(ncross), mem, full(rank), full(limit), full(wc0), full(wc1)]
        + head_inputs(cross_heads[0:4], cross_heads[8]),
        [pair_out] * 3 + packed_outs,
        [limits] + back_scratch,
        back_flops + 2 * SEQ * D * 1024,
    )
    ffn_parts, cross_own = hold(ffn_parts, cross_own)
    (ffn_total,) = simple(sum_rows, "sum_ffn", [ffn_parts], chunks(size))
    ffn_total, cross_grads[0] = hold(ffn_total, cross_grads[0])
    ffn_sums = exchange(ffn_total)
    cross_other = to_core(cross_other)
    g2, placed_mem, grad_mem, gln_cross = call(
        cross_back_second,
        "cross_back_second",
        1,
        [meta_in, full(g3), full(second), full(norms)]
        + [full(w) for w in (wc0, wc1, wc2, wc3)]
        + [full(x) for x in cross_grads]
        + head_inputs(cross_heads[4:8], cross_heads[8]),
        [stream_out(f32), placed(f32), stream_out(bf16), grads_ln],
        back_scratch,
        back_flops + 2 * SEQ * D * 1536,
    )
    ffn_sums, cross_other, g2 = hold(ffn_sums, cross_other, g2)
    (cross_send,) = simple(join_cores, "join_cross", [cross_own, cross_other], chunks(half))
    cross_send, g2 = hold(cross_send, g2)
    cross_parts = exchange(cross_send)

    *self_grads, self_own, self_other = call(
        functools.partial(attention_back_first, False),
        "self_back_first",
        1,
        [meta_in, full(g2), full(nq), full(nc), full(rank), full(limit), full(ws0), full(ws1)]
        + head_inputs(first[0:4], first[4]),
        [pair_out] * 3 + packed_outs,
        [limits] + back_scratch,
        back_flops + 2 * SEQ * D * 1024,
    )
    self_other = to_core(self_other)
    cross_parts, self_own = hold(cross_parts, self_own)
    (both_send,) = simple(
        sum_rows_join, "sum_cross", [cross_parts, self_own, self_other], chunks(2 * half)
    )
    both_send, g2 = hold(both_send, g2)
    both_parts = exchange(both_send)
    placed_q, placed_c, gq, gc, gln_self = call(
        self_back_second,
        "self_back_second",
        1,
        [meta_in, full(g2), xq, xc, full(rank), full(limit), full(norms)]
        + [full(w) for w in (ws0, ws1, ws2, ws3)]
        + [full(x) for x in self_grads]
        + head_inputs(second_heads[0:4], second_heads[4]),
        [placed(f32), placed(f32), stream_out(bf16), stream_out(bf16), grads_ln],
        [limits] + back_scratch,
        back_flops + 2 * SEQ * D * 1536,
    )

    gln = jnp.concatenate([gln_self[0:4], gln_cross[0:2], gln_ffn[0:2]], axis=0)
    both_parts, gln = hold(both_parts, gln)
    (last_send,) = simple(
        functools.partial(sum_last, half), "sum_self", [both_parts, gln, to_core(gln)], chunks(half + 16)
    )
    last_parts = exchange(last_send)

    def both_rows(placed_own, arrays, name):
        count = len(arrays)
        size = SEQ // 2
        one = pl.BlockSpec((size, D), lambda i, meta: (i, 0))
        block = pl.BlockSpec((size, D), lambda i, meta: (2 * (1 - meta[0]) + i, 0))
        return pl.pallas_call(
            place_rows,
            name=name,
            grid_spec=pltpu.PrefetchScalarGridSpec(
                num_scalar_prefetch=1,
                grid=(2,),
                in_specs=[one] * count + [pl.BlockSpec(memory_space=pl.ANY)] * count,
                out_specs=[block] * count,
            ),
            out_shape=[jax.ShapeDtypeStruct(x.shape, x.dtype) for x in placed_own],
            input_output_aliases={1 + count + n: n for n in range(count)},
        )(meta, *[to_core(x) for x in arrays], *placed_own)

    out_both, grad_mem_both = both_rows([placed_output, placed_mem], [output, grad_mem], "place_early")
    gq_both, gc_both = both_rows([placed_q, placed_c], [gq, gc], "place_late")

    attention_outs = [((512, 128), f32)] * 3 + [((128, 512), f32)]
    grad_ffn_in, grad_ffn_out, *grad_cross_parts = simple(
        unpack_early, "unpack_early", [ffn_sums, both_parts], [((D, D), f32)] * 2 + attention_outs
    )
    *grad_self_parts, gln = simple(
        unpack_late, "unpack_late", [last_parts], attention_outs + [((8, D), f32)]
    )
    return (
        out_both,
        gq_both,
        gc_both,
        grad_mem_both,
        gln[0],
        gln[1],
        gln[2],
        gln[3],
        *grad_self_parts,
        gln[4],
        gln[5],
        *grad_cross_parts,
        gln[6],
        gln[7],
        grad_ffn_in,
        grad_ffn_out,
    )


def solution(mesh):
    assert mesh.shape["heads"] == 4
    row_spec = P("rows", None)
    flat = P("rows")
    by_column = P(None, "heads")
    by_row = P("heads", None)
    attention = (by_column, by_column, by_column, by_row)
    in_specs = (
        (row_spec,) * 3
        + (flat,) * 5
        + (P(),) * 4
        + attention
        + (P(),) * 2
        + attention
        + (P(),) * 2
        + (by_column, by_row, row_spec)
    )
    out_specs = (
        (row_spec,) * 4
        + (P(),) * 4
        + attention
        + (P(),) * 2
        + attention
        + (P(),) * 2
        + (by_column, by_row)
    )
    return jax.shard_map(shards, mesh=mesh, in_specs=in_specs, out_specs=out_specs, check_vma=False)
```

```python
import functools

import jax
import jax.numpy as jnp
from jax import lax
from jax.experimental import pallas as pl
from jax.experimental.pallas import tpu as pltpu
from jax.sharding import PartitionSpec as P

HEAD_DIM = 64
SEQ = 1024
DOCS = 8
D = 512
TILE = 256
TILES = SEQ // TILE
FAST_Q = 256
FAST_K = 208
LONG_Q = 128
LONG_K = 640

norm_eps = 1e-05
masked_score = -1e30
hidden_rank = 1e6
gelu_root = 0.7978845608028654
gelu_cube = 0.044715

f32 = jnp.float32
bf16 = jnp.bfloat16


def dot(a, b):
    return lax.dot_general(a, b, (((1,), (0,)), ((), ())), preferred_element_type=f32)


def dot_nt(a, b):
    return lax.dot_general(a, b, (((1,), (1,)), ((), ())), preferred_element_type=f32)


def dot_tn(a, b):
    return lax.dot_general(a, b, (((0,), (0,)), ((), ())), preferred_element_type=f32)


def lanes(parts):
    return jnp.concatenate(parts, axis=1)


def layer_norm(values, gain, shift):
    centre = values - jnp.mean(values, axis=-1, keepdims=True)
    spread = jnp.mean(centre * centre, axis=-1, keepdims=True)
    return centre * lax.rsqrt(spread + norm_eps) * gain + shift


def norm_backward(values, gain, grad):
    centre = values - jnp.mean(values, axis=-1, keepdims=True)
    spread = jnp.mean(centre * centre, axis=-1, keepdims=True)
    scale = lax.rsqrt(spread + norm_eps)
    xhat = centre * scale
    eg = grad * gain
    mean_eg = jnp.mean(eg, axis=-1, keepdims=True)
    mean_egx = jnp.mean(eg * xhat, axis=-1, keepdims=True)
    grad_gain = jnp.sum(grad * xhat, axis=0, keepdims=True)
    grad_shift = jnp.sum(grad, axis=0, keepdims=True)
    return scale * (eg - mean_eg - xhat * mean_egx), grad_gain, grad_shift


def rows_of(i, size=TILE):
    return pl.ds(pl.multiple_of(i * size, size), size)


def w_query(ref):
    return ref[0:512, :]


def w_key(ref):
    return ref[512:1024, :]


def w_value(ref):
    return ref[1024:1536, :]


def w_out(ref):
    return lanes([ref[1536 + 128 * j : 1664 + 128 * j, :] for j in range(4)])


def half_masks():
    place = lax.broadcasted_iota(jnp.int32, (1, 128), 1)
    low = jnp.where(place < HEAD_DIM, 1.0, 0.0).astype(f32)
    return (low.astype(bf16), (1.0 - low).astype(bf16))


def doc_bounds(meta, d, source):
    base = 17 if source else 1
    return meta[base + d], meta[base + 8 + d]


def window_of(first, limit):
    return pl.multiple_of(jnp.minimum((first // 16) * 16, limit), 16)


def key_bias(ks, ke, k0, width):
    place = k0 + lax.broadcasted_iota(jnp.int32, (width, 128), 0)
    return jnp.where((place >= ks) & (place < ke), 0.0, masked_score)


def make_bias(rank_ref, limit_ref, ks, ke, q0, k0, span, width):
    if rank_ref is None:
        return lanes([key_bias(ks, ke, k0, width)] * (span // 128))
    place = k0 + lax.broadcasted_iota(jnp.int32, (width, 128), 0)
    ranks = rank_ref[pl.ds(k0, width), :]
    ranks = jnp.where((place < ks + 2) & (ranks < hidden_rank), -1.0, ranks)
    ranks = jnp.where((place >= ks) & (place < ke), ranks, hidden_rank)
    limits = jnp.broadcast_to(limit_ref[...], (8, SEQ))
    limits = pltpu.roll(limits, lax.rem(SEQ - q0, SEQ), 1)[0:1, 0:span]
    row = k0 + lax.broadcasted_iota(jnp.int32, (width, span), 0)
    column = q0 + lax.broadcasted_iota(jnp.int32, (width, span), 1)
    seen = (lanes([ranks] * (span // 128)) < limits) & (row != column)
    return jnp.where(seen, 0.0, masked_score)


STEPS = DOCS // 2


def is_fast(meta, cross):
    return meta[34 if cross else 33] == 1


def both_heads(x, masks):
    return jnp.concatenate([x * masks[0], x * masks[1]], axis=0)


def pair_probabilities(queries, keys, masks, bias):
    width = keys.shape[0]
    scores = dot_nt(both_heads(keys, masks), queries)
    result = []
    for a in range(2):
        part = scores[width * a : width * a + width] + bias
        part = jnp.exp(part - jnp.max(part, axis=0, keepdims=True))
        part = part * (1.0 / jnp.sum(part, axis=0, keepdims=True))
        result.append(part.astype(bf16))
    return result


def pair_product(rows, parts):
    across = jnp.transpose(rows)
    halves = [dot(across[64 * a : 64 * a + 64], part) for a, part in enumerate(parts)]
    return jnp.transpose(jnp.concatenate(halves, axis=0))


def for_docs(meta, cross, run, before, after):
    @pl.when(is_fast(meta, cross))
    def _():
        def step(i, carry):
            slot = lax.rem(i, 2)
            before(i, slot)
            for place in range(2):
                d = 2 * i + place
                ts, te = doc_bounds(meta, d, False)
                ks, ke = doc_bounds(meta, d, cross)
                q0 = window_of(ts, SEQ - FAST_Q)
                k0 = window_of(ks, SEQ - FAST_K)
                run(d, slot, place, q0, k0, FAST_Q, FAST_K, ts, te, ks, ke, True)
            after(i, slot)
            return carry

        lax.fori_loop(0, STEPS, step, 0)

    @pl.when(jnp.logical_not(is_fast(meta, cross)))
    def _():
        def doc(d, carry):
            ts, te = doc_bounds(meta, d, False)
            ks, ke = doc_bounds(meta, d, cross)
            base = (ts // 16) * 16
            k0 = window_of(ks, SEQ - LONG_K)

            def chunk(i, carry):
                lower = base + i * LONG_Q
                q0 = pl.multiple_of(jnp.minimum(lower, SEQ - LONG_Q), 16)
                low = jnp.maximum(ts, lower)
                high = jnp.minimum(te, lower + LONG_Q)
                run(d, None, None, q0, k0, LONG_Q, LONG_K, low, high, ks, ke, False)
                return carry

            return lax.fori_loop(0, (te - base + LONG_Q - 1) // LONG_Q, chunk, carry)

        lax.fori_loop(0, DOCS, doc, 0)


def attend_docs(meta, cross, rank_ref, limit_ref, halves, p_ref, p_buf, p_sem):
    pairs = 2 * len(halves)
    masks = half_masks()

    def save(i, slot):
        return pltpu.make_async_copy(p_buf.at[slot], p_ref.at[pl.ds(2 * i, 2)], p_sem.at[slot])

    def before(i, slot):
        @pl.when(i >= 2)
        def _():
            save(i - 2, slot).wait()

    def after(i, slot):
        save(i, slot).start()

    def run(d, slot, place, q0, k0, span, width, low, high, ks, ke, fast):
        bias = make_bias(rank_ref, limit_ref, ks, ke, q0, k0, span, width)
        row = q0 + lax.broadcasted_iota(jnp.int32, (span, 128), 0)
        inside = (row >= low) & (row < high)
        for n in range(pairs):
            q_ref, k_ref, v_ref, mixed_ref = halves[n // 2]
            cols = slice(128 * (n % 2), 128 * (n % 2) + 128)
            queries = q_ref[pl.ds(q0, span), cols]
            keys = k_ref[pl.ds(k0, width), cols]
            values = v_ref[pl.ds(k0, width), cols]
            parts = pair_probabilities(queries, keys, masks, bias)
            if fast:
                for a in range(2):
                    p_buf[slot, place, 2 * n + a] = parts[a]
            mixed = pair_product(values, parts)
            old = mixed_ref[pl.ds(q0, span), cols].astype(f32)
            mixed_ref[pl.ds(q0, span), cols] = jnp.where(inside, mixed, old).astype(bf16)

    for_docs(meta, cross, run, before, after)

    @pl.when(is_fast(meta, cross))
    def _():
        for i in range(STEPS - 2, STEPS):
            save(i, i % 2).wait()


def load_step(load, i, slot):
    p_ref, p_buf, p_sem, first = load
    part = p_ref.at[pl.ds(2 * i, 2), pl.ds(first, 4)]
    return pltpu.make_async_copy(part, p_buf.at[slot], p_sem.at[slot])


def start_load(meta, cross, load):
    @pl.when(is_fast(meta, cross))
    def _():
        load_step(load, 0, 0).start()


def attend_docs_back(
    meta, cross, rank_ref, limit_ref, q_ref, k_ref, v_ref, mixed_ref, dm_ref,
    dq_ref, dk_ref, dv_ref, load,
):
    pairs = q_ref.shape[1] // 128
    masks = half_masks()
    p_buf = load[1]

    def before(i, slot):
        @pl.when(i + 1 < STEPS)
        def _():
            load_step(load, i + 1, 1 - slot).start()

        load_step(load, i, slot).wait()

    def after(i, slot):
        pass

    def run(d, slot, place, q0, k0, span, width, low, high, ks, ke, fast):
        row = q0 + lax.broadcasted_iota(jnp.int32, (span, 128), 0)
        inside = (row >= low) & (row < high)
        ones = jnp.ones((width, 128), bf16)
        if not fast:
            bias = make_bias(rank_ref, limit_ref, ks, ke, q0, k0, span, width)
        for n in range(pairs):
            cols = slice(128 * n, 128 * n + 128)
            queries = q_ref[pl.ds(q0, span), cols]
            keys = k_ref[pl.ds(k0, width), cols]
            values = v_ref[pl.ds(k0, width), cols]
            mixed = mixed_ref[pl.ds(q0, span), cols].astype(f32)
            grad = jnp.where(inside, dm_ref[pl.ds(q0, span), cols].astype(f32), 0.0)
            low_grad = grad.astype(bf16)
            left = lanes([low_grad, (-(grad * mixed)).astype(bf16)])
            delta = dot_nt(both_heads(lanes([values, ones]), [lanes([m, m]) for m in masks]), left)
            if fast:
                parts = [p_buf[slot, place, 2 * n + a] for a in range(2)]
            else:
                parts = pair_probabilities(queries, keys, masks, bias)
            slopes = []
            dk = dv = None
            for a in range(2):
                slope = parts[a].astype(f32) * delta[width * a : width * a + width]
                slopes.append(slope.astype(bf16))
                dk_a = dot(slopes[a], queries * masks[a])
                dv_a = dot(parts[a], low_grad * masks[a])
                dk = dk_a if dk is None else dk + dk_a
                dv = dv_a if dv is None else dv + dv_a
            dq = pair_product(keys, slopes)
            dq_ref[pl.ds(q0, span), cols] += dq * (HEAD_DIM**-0.5)
            dk_ref[pl.ds(k0, width), cols] += dk
            dv_ref[pl.ds(k0, width), cols] += dv

    for_docs(meta, cross, run, before, after)


def spread_ranks(rank_row_ref, rank_ref):
    rank_ref[...] = jnp.transpose(jnp.broadcast_to(rank_row_ref[...], (128, SEQ)))


def prepare(
    core, seg_ref, src_ref, rank_ref, limit_ref, pad_ref,
    n0, n1, n2, n3, n4, n5, n6, n7, sq, sk, sv, so, cq, ck, cv, co,
    meta_ref, ranks_ref, limits_ref, norms_ref, ws_ref, wc_ref,
):
    meta_ref[0] = core[0]
    for base, ref in ((1, seg_ref), (17, src_ref)):
        ids = ref[0]
        meta_ref[base] = 0
        meta_ref[base + 15] = SEQ
        for d in range(1, DOCS):
            cut = jnp.sum(jnp.where(ids < d, 1.0, 0.0)).astype(jnp.int32)
            meta_ref[base + d] = cut
            meta_ref[base + 7 + d] = cut
    for place, base in ((33, 1), (34, 17)):
        fast = jnp.int32(1)
        for d in range(DOCS):
            q0 = window_of(meta_ref[1 + d], SEQ - FAST_Q)
            k0 = window_of(meta_ref[base + d], SEQ - FAST_K)
            fits = (meta_ref[9 + d] - q0 <= FAST_Q) & (meta_ref[base + 8 + d] - k0 <= FAST_K)
            fast = fast & fits.astype(jnp.int32)
        meta_ref[place] = fast
    ranks = jnp.where(pad_ref[0] != 0, hidden_rank, rank_ref[0].astype(f32))
    limits = limit_ref[0].astype(f32)
    for i in range(8):
        ranks_ref[0:1, 128 * i : 128 * i + 128] = ranks[i : i + 1]
        limits_ref[0:1, 128 * i : 128 * i + 128] = limits[i : i + 1]
    for i, ref in enumerate((n0, n1, n2, n3, n4, n5, n6, n7)):
        norms_ref[i : i + 1, :] = ref[...]
    for to, parts, out in ((ws_ref, (sq, sk, sv), so), (wc_ref, (cq, ck, cv), co)):
        for i, part in enumerate(parts):
            to[512 * i : 512 * i + 512, :] = part[...]
        for j in range(4):
            to[1536 + 128 * j : 1664 + 128 * j, :] = out[:, 128 * j : 128 * j + 128]


def self_first(
    meta, xq_ref, xc_ref, rank_row_ref, limit_ref, norms_ref, w0_ref, w1_ref,
    nq_ref, nc_ref, q_ref, k_ref, v_ref, mixed_ref, p_ref, rank_ref, p_buf, p_sem,
):

    spread_ranks(rank_row_ref, rank_ref)
    wq = lanes([w_query(w0_ref), w_query(w1_ref)])
    wkv = lanes([w_key(w0_ref), w_key(w1_ref), w_value(w0_ref), w_value(w1_ref)])

    def tile(i, carry):
        rows = rows_of(i)
        nq = layer_norm(xq_ref[rows, :].astype(f32), norms_ref[0:1], norms_ref[1:2]).astype(bf16)
        nc = layer_norm(xc_ref[rows, :].astype(f32), norms_ref[2:3], norms_ref[3:4]).astype(bf16)
        nq_ref[rows, :] = nq
        nc_ref[rows, :] = nc
        q_ref[rows, :] = (dot(nq, wq) * (HEAD_DIM**-0.5)).astype(bf16)
        kv = dot(nc, wkv).astype(bf16)
        k_ref[rows, :] = kv[:, :256]
        v_ref[rows, :] = kv[:, 256:]
        return carry

    lax.fori_loop(0, TILES, tile, 0)

    attend_docs(meta, False, rank_ref, limit_ref, [(q_ref, k_ref, v_ref, mixed_ref)], p_ref, p_buf, p_sem)


def self_second(
    meta, xq_ref, nq_ref, nc_ref, rank_row_ref, limit_ref, norms_ref, w0_ref, w1_ref, w2_ref, w3_ref,
    mixed_first_ref,
    q_ref, k_ref, v_ref, mixed_ref, p_ref, second_ref, ncross_ref, rank_ref, p_buf, p_sem,
):

    spread_ranks(rank_row_ref, rank_ref)
    wq = lanes([w_query(w2_ref), w_query(w3_ref)])
    wkv = lanes([w_key(w2_ref), w_key(w3_ref), w_value(w2_ref), w_value(w3_ref)])

    def tile(i, carry):
        rows = rows_of(i)
        q_ref[rows, :] = (dot(nq_ref[rows, :], wq) * (HEAD_DIM**-0.5)).astype(bf16)
        kv = dot(nc_ref[rows, :], wkv).astype(bf16)
        k_ref[rows, :] = kv[:, :256]
        v_ref[rows, :] = kv[:, 256:]
        return carry

    lax.fori_loop(0, TILES, tile, 0)

    attend_docs(meta, False, rank_ref, limit_ref, [(q_ref, k_ref, v_ref, mixed_ref)], p_ref, p_buf, p_sem)

    out_first = jnp.concatenate([w_out(w0_ref), w_out(w1_ref)], axis=0)
    out_second = jnp.concatenate([w_out(w2_ref), w_out(w3_ref)], axis=0)

    def tile(i, carry):
        rows = rows_of(i)
        branch = dot(mixed_first_ref[rows, :], out_first) + dot(mixed_ref[rows, :], out_second)
        second = xq_ref[rows, :].astype(f32) + branch
        second_ref[rows, :] = second
        ncross_ref[rows, :] = layer_norm(second, norms_ref[4:5], norms_ref[5:6]).astype(bf16)
        return carry

    lax.fori_loop(0, TILES, tile, 0)


def cross_forward(
    meta, second_ref, ncross_ref, memory_ref, norms_ref, w0_ref, w1_ref, w2_ref, w3_ref,
    qa_ref, ka_ref, va_ref, ma_ref, qb_ref, kb_ref, vb_ref, mb_ref, p_ref, third_ref, nffn_ref, p_buf, p_sem,
):
    halves = ((qa_ref, ka_ref, va_ref, ma_ref), (qb_ref, kb_ref, vb_ref, mb_ref))
    weights = (w0_ref, w1_ref, w2_ref, w3_ref)

    wq = lanes([w_query(w) for w in weights])
    wk = lanes([w_key(w) for w in weights])
    wv = lanes([w_value(w) for w in weights])

    def tile(i, carry):
        rows = rows_of(i)
        memory = memory_ref[rows, :]
        q = (dot(ncross_ref[rows, :], wq) * (HEAD_DIM**-0.5)).astype(bf16)
        k = dot(memory, wk).astype(bf16)
        v = dot(memory, wv).astype(bf16)
        for n, (q_ref, k_ref, v_ref, _) in enumerate(halves):
            cols = slice(256 * n, 256 * n + 256)
            q_ref[rows, :] = q[:, cols]
            k_ref[rows, :] = k[:, cols]
            v_ref[rows, :] = v[:, cols]
        return carry

    lax.fori_loop(0, TILES, tile, 0)

    attend_docs(meta, True, None, None, halves, p_ref, p_buf, p_sem)

    out_first = jnp.concatenate([w_out(w0_ref), w_out(w1_ref)], axis=0)
    out_second = jnp.concatenate([w_out(w2_ref), w_out(w3_ref)], axis=0)

    def tile(i, carry):
        rows = rows_of(i)
        branch = dot(ma_ref[rows, :], out_first) + dot(mb_ref[rows, :], out_second)
        third = second_ref[rows, :] + branch
        third_ref[rows, :] = third
        nffn_ref[rows, :] = layer_norm(third, norms_ref[6:7], norms_ref[7:8]).astype(bf16)
        return carry

    lax.fori_loop(0, TILES, tile, 0)


def ffn_both(
    meta, third_ref, nffn_ref, cot_ref, norms_ref, u0_ref, u1_ref, u2_ref, u3_ref,
    w0_ref, w1_ref, w2_ref, w3_ref,
    placed_ref, out_ref, g3_ref, gln_ref, own_ref, other_ref, hidden_ref, before_ref,
):
    i = pl.program_id(0)
    rows = rows_of(i)
    nffn = nffn_ref[rows, :]
    cot = cot_ref[rows, :]
    outs = []
    grads = []
    in_refs = (u0_ref, u1_ref, u2_ref, u3_ref)
    for g, w_ref in enumerate((w0_ref, w1_ref, w2_ref, w3_ref)):
        w_in = in_refs[g][...]
        w_out_rows = w_ref[...]
        x = dot(nffn, w_in)
        square = x * x
        half = 0.5 + 0.5 * jnp.tanh(x * (gelu_root + (gelu_root * gelu_cube) * square))
        value = x * half
        hidden = value.astype(bf16)
        rise = 2.0 * gelu_root + (6.0 * gelu_root * gelu_cube) * square
        slope = half + value * (1.0 - half) * rise
        grad_before = (dot_nt(cot, w_out_rows) * slope).astype(bf16)
        outs.append(dot(hidden, w_out_rows))
        grads.append(dot_nt(grad_before, w_in))
        if g < 2:
            hidden_ref[rows, 512 * g : 512 * g + 512] = hidden
            before_ref[rows, 512 * g : 512 * g + 512] = grad_before
    third = third_ref[rows, :]
    out = (third + ((outs[0] + outs[1]) + (outs[2] + outs[3]))).astype(bf16)
    out_ref[rows, :] = out
    placed_ref[rows, :] = out
    grad_normed = (grads[0] + grads[1]) + (grads[2] + grads[3])
    grad_norm, grad_gain, grad_shift = norm_backward(third, norms_ref[6:7], grad_normed)
    g3_ref[rows, :] = cot.astype(f32) + grad_norm

    @pl.when(i == 0)
    def _():
        gln_ref[0:1, :] = grad_gain
        gln_ref[1:2, :] = grad_shift

    @pl.when(i > 0)
    def _():
        gln_ref[0:1, :] += grad_gain
        gln_ref[1:2, :] += grad_shift

    @pl.when(i == TILES - 1)
    def _():
        nffn_all = nffn_ref[...]
        cot_all = cot_ref[...]
        part = dot_tn(nffn_all, before_ref[...])
        own_ref[0:512, :] = part[:, 0:512]
        other_ref[0:512, :] = part[:, 512:1024].astype(bf16)
        part = dot_tn(hidden_ref[...], cot_all)
        own_ref[512:1024, :] = part[0:512]
        other_ref[512:1024, :] = part[512:1024].astype(bf16)


def back_start(g_ref, mixed_ref, w_refs, dm_ref, dq_ref, dk_ref, dv_ref):
    out_rows = jnp.concatenate([w_out(w) for w in w_refs], axis=0)

    def tile(i, carry):
        rows = rows_of(i)
        dm_ref[rows, :] = dot_nt(g_ref[rows, :].astype(bf16), out_rows).astype(bf16)
        zeros = jnp.zeros((TILE, 256), f32)
        dq_ref[rows, :] = zeros
        dk_ref[rows, :] = zeros
        dv_ref[rows, :] = zeros
        return carry

    lax.fori_loop(0, TILES, tile, 0)


def attention_back_first(
    cross, meta, g_ref, nq_ref, nkv_ref, rank_row_ref, limit_ref, w0_ref, w1_ref,
    q_ref, k_ref, v_ref, mixed_ref, p_ref,
    dq_ref, dk_ref, dv_ref, own_ref, other_ref,
    rank_ref, dm_ref, dqs_ref, dks_ref, dvs_ref, p_buf, p_sem,
):
    load = (p_ref, p_buf, p_sem, 0)
    start_load(meta, cross, load)
    if not cross:
        spread_ranks(rank_row_ref, rank_ref)
    back_start(g_ref, mixed_ref, (w0_ref, w1_ref), dm_ref, dqs_ref, dks_ref, dvs_ref)

    attend_docs_back(
        meta, cross, None if cross else rank_ref, limit_ref, q_ref, k_ref, v_ref, mixed_ref,
        dm_ref, dqs_ref, dks_ref, dvs_ref, load,
    )

    dq_ref[...] = dqs_ref[...].astype(bf16)
    dk_ref[...] = dks_ref[...].astype(bf16)
    dv_ref[...] = dvs_ref[...].astype(bf16)
    nq = nq_ref[...]
    nkv = nkv_ref[...]
    for n, part in enumerate(
        (dot_tn(nq, dq_ref[...]), dot_tn(nkv, dk_ref[...]), dot_tn(nkv, dv_ref[...]))
    ):
        own_ref[:, 128 * n : 128 * n + 128] = part[:, :128]
        other_ref[:, 128 * n : 128 * n + 128] = part[:, 128:].astype(bf16)
    part = dot_tn(mixed_ref[...], g_ref[...].astype(bf16))
    for j in range(4):
        rows = slice(128 * j, 128 * j + 128)
        own_ref[rows, 384:512] = part[:128, rows]
        other_ref[rows, 384:512] = part[128:, rows].astype(bf16)


def back_second_docs(
    cross, meta, g_ref, rank_row_ref, limit_ref, w_refs, q_ref, k_ref, v_ref, mixed_ref, p_ref,
    rank_ref, dm_ref, dqs_ref, dks_ref, dvs_ref, p_buf, p_sem,
):
    load = (p_ref, p_buf, p_sem, 4 if cross else 0)
    start_load(meta, cross, load)
    if not cross:
        spread_ranks(rank_row_ref, rank_ref)
    back_start(g_ref, mixed_ref, w_refs, dm_ref, dqs_ref, dks_ref, dvs_ref)

    attend_docs_back(
        meta, cross, None if cross else rank_ref, limit_ref, q_ref, k_ref, v_ref, mixed_ref,
        dm_ref, dqs_ref, dks_ref, dvs_ref, load,
    )


def stream_grads(rows, first, second, firsts, seconds):
    dq, dk, dv = first
    dq2, dk2, dv2 = (ref[rows, :].astype(bf16) for ref in second)
    w0, w1 = firsts
    w2, w3 = seconds
    grad_q = dot_nt(dq[rows, :], lanes([w_query(w0), w_query(w1)])) + dot_nt(
        dq2, lanes([w_query(w2), w_query(w3)])
    )
    kv = lanes([dk[rows, :], dv[rows, :]])
    kv2 = lanes([dk2, dv2])
    grad_kv = dot_nt(kv, lanes([w_key(w0), w_key(w1), w_value(w0), w_value(w1)])) + dot_nt(
        kv2, lanes([w_key(w2), w_key(w3), w_value(w2), w_value(w3)])
    )
    return grad_q, grad_kv


def cross_back_second(
    meta, g_ref, second_ref, norms_ref, w0_ref, w1_ref, w2_ref, w3_ref,
    dq_ref, dk_ref, dv_ref, q_ref, k_ref, v_ref, mixed_ref, p_ref,
    g2_ref, placed_ref, gmem_ref, gln_ref,
    dm_ref, dqs_ref, dks_ref, dvs_ref, p_buf, p_sem,
):
    back_second_docs(
        True, meta, g_ref, None, None, (w2_ref, w3_ref), q_ref, k_ref, v_ref, mixed_ref, p_ref,
        None, dm_ref, dqs_ref, dks_ref, dvs_ref, p_buf, p_sem,
    )

    gln_ref[...] = jnp.zeros_like(gln_ref)

    def tile(i, carry):
        rows = rows_of(i)
        grad_q, grad_kv = stream_grads(
            rows,
            (dq_ref, dk_ref, dv_ref),
            (dqs_ref, dks_ref, dvs_ref),
            (w0_ref, w1_ref),
            (w2_ref, w3_ref),
        )
        low_kv = grad_kv.astype(bf16)
        gmem_ref[rows, :] = low_kv
        placed_ref[rows, :] = low_kv.astype(f32)
        grad_norm, grad_gain, grad_shift = norm_backward(
            second_ref[rows, :], norms_ref[4:5], grad_q
        )
        g2_ref[rows, :] = g_ref[rows, :] + grad_norm
        gln_ref[0:1, :] += grad_gain
        gln_ref[1:2, :] += grad_shift
        return carry

    lax.fori_loop(0, TILES, tile, 0)


def self_back_second(
    meta, g_ref, xq_ref, xc_ref, rank_row_ref, limit_ref, norms_ref, w0_ref, w1_ref, w2_ref, w3_ref,
    dq_ref, dk_ref, dv_ref, q_ref, k_ref, v_ref, mixed_ref, p_ref,
    placed_q_ref, placed_c_ref, gq_ref, gc_ref, gln_ref,
    rank_ref, dm_ref, dqs_ref, dks_ref, dvs_ref, p_buf, p_sem,
):
    back_second_docs(
        False, meta, g_ref, rank_row_ref, limit_ref, (w2_ref, w3_ref), q_ref, k_ref, v_ref, mixed_ref,
        p_ref, rank_ref, dm_ref, dqs_ref, dks_ref, dvs_ref, p_buf, p_sem,
    )

    gln_ref[...] = jnp.zeros_like(gln_ref)

    def tile(i, carry):
        rows = rows_of(i)
        grad_q, grad_kv = stream_grads(
            rows,
            (dq_ref, dk_ref, dv_ref),
            (dqs_ref, dks_ref, dvs_ref),
            (w0_ref, w1_ref),
            (w2_ref, w3_ref),
        )
        grad_norm, grad_gain, grad_shift = norm_backward(
            xq_ref[rows, :].astype(f32), norms_ref[0:1], grad_q
        )
        low_q = (g_ref[rows, :] + grad_norm).astype(bf16)
        gq_ref[rows, :] = low_q
        placed_q_ref[rows, :] = low_q.astype(f32)
        gln_ref[0:1, :] += grad_gain
        gln_ref[1:2, :] += grad_shift
        grad_norm, grad_gain, grad_shift = norm_backward(
            xc_ref[rows, :].astype(f32), norms_ref[2:3], grad_kv
        )
        low_c = grad_norm.astype(bf16)
        gc_ref[rows, :] = low_c
        placed_c_ref[rows, :] = low_c.astype(f32)
        gln_ref[2:3, :] += grad_gain
        gln_ref[3:4, :] += grad_shift
        return carry

    lax.fori_loop(0, TILES, tile, 0)


def place_rows(meta, *refs):
    count = len(refs) // 3
    for n in range(count):
        refs[2 * count + n][...] = refs[n][...].astype(refs[2 * count + n].dtype)


def join_cores(own, other, send):
    joined = own[...] + other[...].astype(f32)
    send[...] = joined.astype(bf16).reshape(send.shape)


def summed(parts, size, first):
    total = parts[0, first : first + size, :].astype(f32)
    for r in range(1, parts.shape[0]):
        total = total + parts[r, first : first + size, :].astype(f32)
    return total.astype(bf16)


def sum_rows(parts, send):
    count, size, _ = parts.shape
    total = summed(parts, size, 0)
    for r in range(count):
        send[r] = total


def sum_rows_join(parts, own, other, send):
    count, done, _ = parts.shape
    size = own.shape[0] // count
    total = summed(parts, done, 0)
    for r in range(count):
        rows = slice(size * r, size * r + size)
        send[r, 0:done, :] = total
        send[r, done : done + size, :] = (own[rows, :] + other[rows, :].astype(f32)).astype(bf16)


def sum_last(done, parts, gln_own, gln_other, send):
    count = parts.shape[0]
    size = parts.shape[1] - done
    total = summed(parts, size, done)
    gln = gln_own[...] + gln_other[...]
    gln = jnp.concatenate([gln, jnp.zeros((8, D), f32)], axis=0).astype(bf16)
    for r in range(count):
        send[r, 0:size, :] = total
        send[r, size : size + 16, :] = gln


def unpack_attention(parts, outs):
    count = parts.shape[0]
    size = D // count
    for r in range(count):
        rows = slice(size * r, size * r + size)
        for i in range(3):
            outs[i][rows, :] = parts[r, 0:size, 128 * i : 128 * i + 128].astype(f32)
        j, first = divmod(size * r, 128)
        outs[3][first : first + size, 128 * j : 128 * j + 128] = parts[r, 0:size, 384:512].astype(f32)


def unpack_early(ffn, cross, *outs):
    count, size, _ = ffn.shape
    for r in range(count):
        out = outs[2 * r // count]
        first = (size * r) % D
        out[first : first + size, :] = ffn[r].astype(f32)
    unpack_attention(cross, outs[2:])


def unpack_late(parts, *outs):
    unpack_attention(parts, outs[:4])
    size = parts.shape[1] - 16
    total = parts[0, size : size + 16, :].astype(f32)
    for r in range(1, parts.shape[0]):
        total = total + parts[r, size : size + 16, :].astype(f32)
    outs[4][...] = total[0:8]


def whole(shape):
    zeros = (0,) * len(shape)
    return pl.BlockSpec(shape, lambda d, meta: zeros)


def own_row(width):
    return pl.BlockSpec((SEQ, width), lambda d, meta: (meta[0], 0))


def in_hbm(x):
    return pltpu.with_memory_space_constraint(x, pltpu.HBM)


def probability_out(heads):
    return (pltpu.HBM((DOCS, heads, FAST_K, FAST_Q), bf16), None, pl.BlockSpec(memory_space=pl.ANY))


def probability_scratch(heads):
    return [pltpu.VMEM((2, 2, heads, FAST_K, FAST_Q), bf16), pltpu.SemaphoreType.DMA((2,))]


def kept(shape, dtype):
    return (pltpu.VMEM(shape, dtype), None, whole(shape))


def keep(x):
    return (pltpu.with_memory_space_constraint(x, pltpu.VMEM), whole(x.shape))


def call(kernel, name, grid, operands, outs, scratch, flops, token=None):
    moved = sum(x.size * x.dtype.itemsize for x, _ in operands[1:])
    count = len(operands) - 1
    body = kernel
    if token is not None:
        operands = operands + [(token, whole((8, 128)))]
        outs = outs + [((8, 128), f32, whole((8, 128)))]

        def body(meta, *refs):
            token_in, token_out = refs[count], refs[count + len(outs)]
            kernel(meta, *refs[:count], *refs[count + 1 : count + len(outs)], *refs[count + len(outs) + 1 :])
            token_out[...] = token_in[...]

    return pl.pallas_call(
        body,
        name=name,
        grid_spec=pltpu.PrefetchScalarGridSpec(
            num_scalar_prefetch=1,
            grid=(grid,),
            in_specs=[spec for _, spec in operands[1:]],
            out_specs=[spec for _, _, spec in outs],
            scratch_shapes=scratch,
        ),
        out_shape=[
            jax.ShapeDtypeStruct(shape, dtype) if dtype else shape for shape, dtype, _ in outs
        ],
        compiler_params=pltpu.CompilerParams(
            dimension_semantics=("arbitrary",), vmem_limit_bytes=16 * 1024 * 1024
        ),
        cost_estimate=pl.CostEstimate(
            flops=int(flops), bytes_accessed=int(moved), transcendentals=0
        ),
    )(*[x for x, _ in operands])


def simple(kernel, name, operands, outs, own=None):
    if own is not None:
        operands = list(operands)
        operands[own] = pltpu.with_memory_space_constraint(operands[own], pltpu.VMEM)
    return pl.pallas_call(
        kernel,
        name=name,
        out_shape=[jax.ShapeDtypeStruct(shape, dtype) for shape, dtype in outs],
        compiler_params=pltpu.CompilerParams(vmem_limit_bytes=8 * 1024 * 1024),
    )(*operands)


def full(x):
    return (x, whole(x.shape))


def shards(
    query_stream,
    content_stream,
    memory,
    segment_ids,
    source_segments,
    context_rank,
    context_limit,
    padding,
    ln_query_gain,
    ln_query_bias,
    ln_content_gain,
    ln_content_bias,
    self_query,
    self_key,
    self_value,
    self_out,
    ln_cross_gain,
    ln_cross_bias,
    cross_query,
    cross_key,
    cross_value,
    cross_out,
    ln_ffn_gain,
    ln_ffn_bias,
    ffn_in,
    ffn_out,
    cotangent,
):
    core = lax.axis_index("heads") % 2

    def to_core(x):
        return lax.ppermute(x, "heads", [(h, h ^ 1) for h in range(4)])

    hold = lambda *xs: lax.optimization_barrier(xs)

    def to_chip(x):
        return lax.ppermute(x, "heads", [(h, h ^ 2) for h in range(4)])

    row = pl.BlockSpec((1, 8, 128), lambda d, core: (core[0], 0, 0))

    def token_row(x):
        return (in_hbm(x.reshape(2, 8, 128)), row)

    def fixed(x):
        zeros = (0,) * x.ndim
        return (in_hbm(x), pl.BlockSpec(x.shape, lambda d, core: zeros))

    prepared = [
        ((35,), jnp.int32, pl.BlockSpec(memory_space=pltpu.SMEM)),
        ((1, SEQ), f32, whole((1, SEQ))),
        ((1, SEQ), f32, whole((1, SEQ))),
        ((8, D), f32, whole((8, D))),
        ((2048, 128), bf16, whole((2048, 128))),
        ((2048, 128), bf16, whole((2048, 128))),
    ]
    gains = (
        ln_query_gain,
        ln_query_bias,
        ln_content_gain,
        ln_content_bias,
        ln_cross_gain,
        ln_cross_bias,
        ln_ffn_gain,
        ln_ffn_bias,
    )
    weights = (self_query, self_key, self_value, self_out)
    weights += (cross_query, cross_key, cross_value, cross_out)
    tokens = (segment_ids, source_segments, context_rank, context_limit, padding)
    meta, rank, limit, norms, ws0, wc0 = call(
        prepare,
        "prepare",
        1,
        [(core.astype(jnp.int32)[None], None)]
        + [token_row(x) for x in tokens]
        + [fixed(x.reshape(1, D)) for x in gains]
        + [fixed(x) for x in weights],
        prepared,
        [],
        0,
    )

    ws1 = to_core(ws0)
    ws2 = to_chip(ws0)
    wc2 = to_chip(wc0)
    u0, u2 = ffn_in, to_chip(ffn_in)
    wf0, wf2 = ffn_out, to_chip(ffn_out)
    meta_in = (meta, None)
    xq = (in_hbm(query_stream), own_row(D))
    xc = (in_hbm(content_stream), own_row(D))
    mem = (in_hbm(memory), own_row(D))
    cot = (in_hbm(cotangent), own_row(D))

    heads_out = [kept((SEQ, 256), bf16)] * 4

    def stream_out(dtype):
        return ((SEQ, D), dtype, whole((SEQ, D)))

    def stream_kept(dtype):
        return kept((SEQ, D), dtype)

    def placed(dtype):
        return ((2 * SEQ, D), dtype, own_row(D))

    limits = pltpu.VMEM((SEQ, 128), f32)
    pair_flops = 2 * SEQ * D * 768 + 2 * 2 * 4 * DOCS * FAST_Q * FAST_K * 256

    nq, nc, *first, token = call(
        self_first,
        "self_first",
        1,
        [meta_in, xq, xc, full(rank), full(limit), full(norms), full(ws0), full(ws1)],
        [stream_kept(bf16), stream_kept(bf16)] + heads_out + [probability_out(4)],
        [limits] + probability_scratch(4),
        pair_flops,
        jnp.zeros((8, 128), f32),
    )
    ws2, wc0, token = hold(ws2, wc0, token)
    ws3 = to_core(ws2)
    wc1 = to_core(wc0)
    *second_heads, second, ncross, token = call(
        self_second,
        "self_second",
        1,
        [meta_in, xq, keep(nq), keep(nc), full(rank), full(limit), full(norms)]
        + [full(w) for w in (ws0, ws1, ws2, ws3)]
        + [keep(first[3])],
        heads_out + [probability_out(4), stream_kept(f32), stream_kept(bf16)],
        [limits] + probability_scratch(4),
        pair_flops + 2 * SEQ * D * D,
        token,
    )
    wc2, u0, wf0, token = hold(wc2, u0, wf0, token)
    wc3 = to_core(wc2)
    u1 = to_core(u0)
    wf1 = to_core(wf0)
    *cross_heads, third, nffn, token = call(
        cross_forward,
        "cross_forward",
        1,
        [meta_in, keep(second), keep(ncross), mem, full(norms)]
        + [full(w) for w in (wc0, wc1, wc2, wc3)],
        heads_out + heads_out + [probability_out(8), stream_kept(f32), stream_kept(bf16)],
        probability_scratch(8),
        2 * pair_flops + 2 * SEQ * D * D,
        token,
    )
    u2, wf2, token = hold(u2, wf2, token)
    u3 = to_core(u2)
    wf3 = to_core(wf2)
    grads_ln = ((8, D), f32, whole((8, D)))
    placed_output, output, g3, gln_ffn, ffn_own, ffn_other, token = call(
        ffn_both,
        "ffn_both",
        TILES,
        [meta_in, keep(third), keep(nffn), cot, full(norms)]
        + [full(w) for w in (u0, u1, u2, u3, wf0, wf1, wf2, wf3)],
        [
            placed(bf16),
            stream_out(bf16),
            stream_kept(f32),
            grads_ln,
            kept((1024, D), f32),
            ((1024, D), bf16, whole((1024, D))),
        ],
        [pltpu.VMEM((SEQ, 1024), bf16), pltpu.VMEM((SEQ, 1024), bf16)],
        12 * SEQ * D * 2048,
        token,
    )

    row_count = lax.axis_size("rows")

    def exchange(x):
        return lax.all_to_all(x, "rows", 0, 0)

    def chunks(n):
        return [((row_count, n, D), bf16)]

    size = 1024 // row_count
    half = size // 2
    (ffn_send,) = simple(join_cores, "join_ffn", [ffn_own, to_core(ffn_other)], chunks(size), 0)
    token, ffn_send = hold(token, ffn_send)
    ffn_parts = exchange(ffn_send)

    back_scratch = [pltpu.VMEM((SEQ, 256), bf16)] + [pltpu.VMEM((SEQ, 256), f32)] * 3
    back_scratch += probability_scratch(4)
    pair_out = kept((SEQ, 256), bf16)
    packed_outs = [
        kept((D, D), f32),
        ((D, D), bf16, whole((D, D))),
    ]
    back_flops = 2 * SEQ * D * 256 + 4 * 2 * 4 * DOCS * FAST_Q * FAST_K * 256

    def head_inputs(natural, p):
        return [keep(x) for x in natural] + [(in_hbm(p), pl.BlockSpec(memory_space=pl.ANY))]

    *cross_grads, cross_own, cross_other, token = call(
        functools.partial(attention_back_first, True),
        "cross_back_first",
        1,
        [meta_in, keep(g3), keep(ncross), mem, full(rank), full(limit), full(wc0), full(wc1)]
        + head_inputs(cross_heads[0:4], cross_heads[8]),
        [pair_out] * 3 + packed_outs,
        [limits] + back_scratch,
        back_flops + 2 * SEQ * D * 1024,
        token,
    )
    ffn_parts, token = hold(ffn_parts, token)
    (ffn_total,) = simple(sum_rows, "sum_ffn", [ffn_parts], chunks(size))
    ffn_total, token = hold(ffn_total, token)
    ffn_sums = exchange(ffn_total)
    cross_other = to_core(cross_other)
    g2, placed_mem, grad_mem, gln_cross, token = call(
        cross_back_second,
        "cross_back_second",
        1,
        [meta_in, keep(g3), keep(second), full(norms)]
        + [full(w) for w in (wc0, wc1, wc2, wc3)]
        + [keep(x) for x in cross_grads]
        + head_inputs(cross_heads[4:8], cross_heads[8]),
        [stream_kept(f32), placed(f32), stream_out(bf16), grads_ln],
        back_scratch,
        back_flops + 2 * SEQ * D * 1536,
        token,
    )
    ffn_sums, cross_other, token = hold(ffn_sums, cross_other, token)
    (cross_send,) = simple(join_cores, "join_cross", [cross_own, cross_other], chunks(half), 0)
    cross_send, token = hold(cross_send, token)
    cross_parts = exchange(cross_send)

    *self_grads, self_own, self_other, token = call(
        functools.partial(attention_back_first, False),
        "self_back_first",
        1,
        [meta_in, keep(g2), keep(nq), keep(nc), full(rank), full(limit), full(ws0), full(ws1)]
        + head_inputs(first[0:4], first[4]),
        [pair_out] * 3 + packed_outs,
        [limits] + back_scratch,
        back_flops + 2 * SEQ * D * 1024,
        token,
    )
    self_other = to_core(self_other)
    cross_parts, token = hold(cross_parts, token)
    (both_send,) = simple(
        sum_rows_join, "sum_cross", [cross_parts, self_own, self_other], chunks(2 * half), 1
    )
    both_send, token = hold(both_send, token)
    both_parts = exchange(both_send)
    placed_q, placed_c, gq, gc, gln_self, token = call(
        self_back_second,
        "self_back_second",
        1,
        [meta_in, keep(g2), xq, xc, full(rank), full(limit), full(norms)]
        + [full(w) for w in (ws0, ws1, ws2, ws3)]
        + [keep(x) for x in self_grads]
        + head_inputs(second_heads[0:4], second_heads[4]),
        [placed(f32), placed(f32), stream_out(bf16), stream_out(bf16), grads_ln],
        [limits] + back_scratch,
        back_flops + 2 * SEQ * D * 1536,
        token,
    )

    gln = jnp.concatenate([gln_self[0:4], gln_cross[0:2], gln_ffn[0:2]], axis=0)
    both_parts, gln = hold(both_parts, gln)
    (last_send,) = simple(
        functools.partial(sum_last, half), "sum_self", [both_parts, gln, to_core(gln)], chunks(half + 16)
    )
    last_parts = exchange(last_send)

    def both_rows(placed_own, arrays, name):
        count = len(arrays)
        size = SEQ // 2
        one = pl.BlockSpec((size, D), lambda i, meta: (i, 0))
        block = pl.BlockSpec((size, D), lambda i, meta: (2 * (1 - meta[0]) + i, 0))
        return pl.pallas_call(
            place_rows,
            name=name,
            grid_spec=pltpu.PrefetchScalarGridSpec(
                num_scalar_prefetch=1,
                grid=(2,),
                in_specs=[one] * count + [pl.BlockSpec(memory_space=pl.ANY)] * count,
                out_specs=[block] * count,
            ),
            out_shape=[jax.ShapeDtypeStruct(x.shape, x.dtype) for x in placed_own],
            input_output_aliases={1 + count + n: n for n in range(count)},
        )(meta, *[to_core(x) for x in arrays], *placed_own)

    out_both, grad_mem_both = both_rows([placed_output, placed_mem], [output, grad_mem], "place_early")
    gq_both, gc_both = both_rows([placed_q, placed_c], [gq, gc], "place_late")

    attention_outs = [((512, 128), f32)] * 3 + [((128, 512), f32)]
    grad_ffn_in, grad_ffn_out, *grad_cross_parts = simple(
        unpack_early, "unpack_early", [ffn_sums, both_parts], [((D, D), f32)] * 2 + attention_outs
    )
    *grad_self_parts, gln = simple(
        unpack_late, "unpack_late", [last_parts], attention_outs + [((8, D), f32)]
    )
    return (
        out_both,
        gq_both,
        gc_both,
        grad_mem_both,
        gln[0],
        gln[1],
        gln[2],
        gln[3],
        *grad_self_parts,
        gln[4],
        gln[5],
        *grad_cross_parts,
        gln[6],
        gln[7],
        grad_ffn_in,
        grad_ffn_out,
    )


def solution(mesh):
    assert mesh.shape["heads"] == 4
    row_spec = P("rows", None)
    flat = P("rows")
    by_column = P(None, "heads")
    by_row = P("heads", None)
    attention = (by_column, by_column, by_column, by_row)
    in_specs = (
        (row_spec,) * 3
        + (flat,) * 5
        + (P(),) * 4
        + attention
        + (P(),) * 2
        + attention
        + (P(),) * 2
        + (by_column, by_row, row_spec)
    )
    out_specs = (
        (row_spec,) * 4
        + (P(),) * 4
        + attention
        + (P(),) * 2
        + attention
        + (P(),) * 2
        + (by_column, by_row)
    )
    return jax.shard_map(shards, mesh=mesh, in_specs=in_specs, out_specs=out_specs, check_vma=False)
```

```python
import functools

import jax
import jax.numpy as jnp
from jax import lax
from jax.experimental import pallas as pl
from jax.experimental.pallas import tpu as pltpu
from jax.sharding import PartitionSpec as P

HEAD_DIM = 64
SEQ = 1024
DOCS = 8
D = 512
TILE = 256
TILES = SEQ // TILE
FAST_Q = 256
FAST_K = 208
LONG_Q = 128
LONG_K = 640

norm_eps = 1e-05
masked_score = -1e30
hidden_rank = 1e6
gelu_root = 0.7978845608028654
gelu_cube = 0.044715

f32 = jnp.float32
bf16 = jnp.bfloat16


def dot(a, b):
    return lax.dot_general(a, b, (((1,), (0,)), ((), ())), preferred_element_type=f32)


def dot_nt(a, b):
    return lax.dot_general(a, b, (((1,), (1,)), ((), ())), preferred_element_type=f32)


def dot_tn(a, b):
    return lax.dot_general(a, b, (((0,), (0,)), ((), ())), preferred_element_type=f32)


def lanes(parts):
    return jnp.concatenate(parts, axis=1)


def layer_norm(values, gain, shift):
    centre = values - jnp.mean(values, axis=-1, keepdims=True)
    spread = jnp.mean(centre * centre, axis=-1, keepdims=True)
    return centre * lax.rsqrt(spread + norm_eps) * gain + shift


def norm_backward(values, gain, grad):
    centre = values - jnp.mean(values, axis=-1, keepdims=True)
    spread = jnp.mean(centre * centre, axis=-1, keepdims=True)
    scale = lax.rsqrt(spread + norm_eps)
    xhat = centre * scale
    eg = grad * gain
    mean_eg = jnp.mean(eg, axis=-1, keepdims=True)
    mean_egx = jnp.mean(eg * xhat, axis=-1, keepdims=True)
    grad_gain = jnp.sum(grad * xhat, axis=0, keepdims=True)
    grad_shift = jnp.sum(grad, axis=0, keepdims=True)
    return scale * (eg - mean_eg - xhat * mean_egx), grad_gain, grad_shift


def rows_of(i, size=TILE):
    return pl.ds(pl.multiple_of(i * size, size), size)


def w_query(ref):
    return ref[0:512, :]


def w_key(ref):
    return ref[512:1024, :]


def w_value(ref):
    return ref[1024:1536, :]


def w_out(ref):
    return lanes([ref[1536 + 128 * j : 1664 + 128 * j, :] for j in range(4)])


def half_masks():
    place = lax.broadcasted_iota(jnp.int32, (1, 128), 1)
    low = jnp.where(place < HEAD_DIM, 1.0, 0.0).astype(f32)
    return (low.astype(bf16), (1.0 - low).astype(bf16))


def doc_bounds(meta, d, source):
    base = 17 if source else 1
    return meta[base + d], meta[base + 8 + d]


def window_of(first, limit):
    return pl.multiple_of(jnp.minimum((first // 16) * 16, limit), 16)


def key_bias(ks, ke, k0, width):
    place = k0 + lax.broadcasted_iota(jnp.int32, (width, 128), 0)
    return jnp.where((place >= ks) & (place < ke), 0.0, masked_score)


def make_bias(rank_ref, limit_ref, ks, ke, q0, k0, span, width):
    if rank_ref is None:
        return lanes([key_bias(ks, ke, k0, width)] * (span // 128))
    place = k0 + lax.broadcasted_iota(jnp.int32, (width, 128), 0)
    ranks = rank_ref[pl.ds(k0, width), :]
    ranks = jnp.where((place < ks + 2) & (ranks < hidden_rank), -1.0, ranks)
    ranks = jnp.where((place >= ks) & (place < ke), ranks, hidden_rank)
    limits = jnp.broadcast_to(limit_ref[...], (8, SEQ))
    limits = pltpu.roll(limits, lax.rem(SEQ - q0, SEQ), 1)[0:1, 0:span]
    row = k0 + lax.broadcasted_iota(jnp.int32, (width, span), 0)
    column = q0 + lax.broadcasted_iota(jnp.int32, (width, span), 1)
    seen = (lanes([ranks] * (span // 128)) < limits) & (row != column)
    return jnp.where(seen, 0.0, masked_score)


STEPS = DOCS // 2


def is_fast(meta, cross):
    return meta[34 if cross else 33] == 1


def both_heads(x, masks):
    return jnp.concatenate([x * masks[0], x * masks[1]], axis=0)


def pair_probabilities(queries, keys, masks, bias):
    width = keys.shape[0]
    scores = dot_nt(both_heads(keys, masks), queries)
    result = []
    for a in range(2):
        part = scores[width * a : width * a + width] + bias
        part = jnp.exp(part - jnp.max(part, axis=0, keepdims=True))
        part = part * (1.0 / jnp.sum(part, axis=0, keepdims=True))
        result.append(part.astype(bf16))
    return result


def pair_product(rows, parts):
    across = jnp.transpose(rows)
    halves = [dot(across[64 * a : 64 * a + 64], part) for a, part in enumerate(parts)]
    return jnp.transpose(jnp.concatenate(halves, axis=0))


def for_docs(meta, cross, run, before, after):
    @pl.when(is_fast(meta, cross))
    def _():
        def step(i, carry):
            slot = lax.rem(i, 2)
            before(i, slot)
            for place in range(2):
                d = 2 * i + place
                ts, te = doc_bounds(meta, d, False)
                ks, ke = doc_bounds(meta, d, cross)
                q0 = window_of(ts, SEQ - FAST_Q)
                k0 = window_of(ks, SEQ - FAST_K)
                run(d, slot, place, q0, k0, FAST_Q, FAST_K, ts, te, ks, ke, True)
            after(i, slot)
            return carry

        lax.fori_loop(0, STEPS, step, 0)

    @pl.when(jnp.logical_not(is_fast(meta, cross)))
    def _():
        def doc(d, carry):
            ts, te = doc_bounds(meta, d, False)
            ks, ke = doc_bounds(meta, d, cross)
            base = (ts // 16) * 16
            k0 = window_of(ks, SEQ - LONG_K)

            def chunk(i, carry):
                lower = base + i * LONG_Q
                q0 = pl.multiple_of(jnp.minimum(lower, SEQ - LONG_Q), 16)
                low = jnp.maximum(ts, lower)
                high = jnp.minimum(te, lower + LONG_Q)
                run(d, None, None, q0, k0, LONG_Q, LONG_K, low, high, ks, ke, False)
                return carry

            return lax.fori_loop(0, (te - base + LONG_Q - 1) // LONG_Q, chunk, carry)

        lax.fori_loop(0, DOCS, doc, 0)


def attend_docs(meta, cross, rank_ref, limit_ref, halves, p_ref, p_buf, p_sem):
    pairs = 2 * len(halves)
    masks = half_masks()

    def save(i, slot):
        return pltpu.make_async_copy(p_buf.at[slot], p_ref.at[pl.ds(2 * i, 2)], p_sem.at[slot])

    def before(i, slot):
        @pl.when(i >= 2)
        def _():
            save(i - 2, slot).wait()

    def after(i, slot):
        save(i, slot).start()

    def run(d, slot, place, q0, k0, span, width, low, high, ks, ke, fast):
        bias = make_bias(rank_ref, limit_ref, ks, ke, q0, k0, span, width)
        row = q0 + lax.broadcasted_iota(jnp.int32, (span, 128), 0)
        inside = (row >= low) & (row < high)
        for n in range(pairs):
            q_ref, k_ref, v_ref, mixed_ref = halves[n // 2]
            cols = slice(128 * (n % 2), 128 * (n % 2) + 128)
            queries = q_ref[pl.ds(q0, span), cols]
            keys = k_ref[pl.ds(k0, width), cols]
            values = v_ref[pl.ds(k0, width), cols]
            parts = pair_probabilities(queries, keys, masks, bias)
            if fast:
                for a in range(2):
                    p_buf[slot, place, 2 * n + a] = parts[a]
            mixed = pair_product(values, parts)
            old = mixed_ref[pl.ds(q0, span), cols].astype(f32)
            mixed_ref[pl.ds(q0, span), cols] = jnp.where(inside, mixed, old).astype(bf16)

    for_docs(meta, cross, run, before, after)

    @pl.when(is_fast(meta, cross))
    def _():
        for i in range(STEPS - 2, STEPS):
            save(i, i % 2).wait()


def load_step(load, i, slot):
    p_ref, p_buf, p_sem, first = load
    part = p_ref.at[pl.ds(2 * i, 2), pl.ds(first, 4)]
    return pltpu.make_async_copy(part, p_buf.at[slot], p_sem.at[slot])


def start_load(meta, cross, load):
    @pl.when(is_fast(meta, cross))
    def _():
        load_step(load, 0, 0).start()


def attend_docs_back(
    meta, cross, rank_ref, limit_ref, q_ref, k_ref, v_ref, mixed_ref, dm_ref,
    dq_ref, dk_ref, dv_ref, load,
):
    pairs = q_ref.shape[1] // 128
    masks = half_masks()
    p_buf = load[1]

    def before(i, slot):
        @pl.when(i + 1 < STEPS)
        def _():
            load_step(load, i + 1, 1 - slot).start()

        load_step(load, i, slot).wait()

    def after(i, slot):
        pass

    def run(d, slot, place, q0, k0, span, width, low, high, ks, ke, fast):
        row = q0 + lax.broadcasted_iota(jnp.int32, (span, 128), 0)
        inside = (row >= low) & (row < high)
        ones = jnp.ones((width, 128), bf16)
        if not fast:
            bias = make_bias(rank_ref, limit_ref, ks, ke, q0, k0, span, width)
        for n in range(pairs):
            cols = slice(128 * n, 128 * n + 128)
            queries = q_ref[pl.ds(q0, span), cols]
            keys = k_ref[pl.ds(k0, width), cols]
            values = v_ref[pl.ds(k0, width), cols]
            mixed = mixed_ref[pl.ds(q0, span), cols].astype(f32)
            grad = jnp.where(inside, dm_ref[pl.ds(q0, span), cols].astype(f32), 0.0)
            low_grad = grad.astype(bf16)
            left = lanes([low_grad, (-(grad * mixed)).astype(bf16)])
            delta = dot_nt(both_heads(lanes([values, ones]), [lanes([m, m]) for m in masks]), left)
            if fast:
                parts = [p_buf[slot, place, 2 * n + a] for a in range(2)]
            else:
                parts = pair_probabilities(queries, keys, masks, bias)
            slopes = []
            dk = dv = None
            for a in range(2):
                slope = parts[a].astype(f32) * delta[width * a : width * a + width]
                slopes.append(slope.astype(bf16))
                dk_a = dot(slopes[a], queries * masks[a])
                dv_a = dot(parts[a], low_grad * masks[a])
                dk = dk_a if dk is None else dk + dk_a
                dv = dv_a if dv is None else dv + dv_a
            dq = pair_product(keys, slopes)
            dq_ref[pl.ds(q0, span), cols] += dq * (HEAD_DIM**-0.5)
            dk_ref[pl.ds(k0, width), cols] += dk
            dv_ref[pl.ds(k0, width), cols] += dv

    for_docs(meta, cross, run, before, after)


def spread_ranks(rank_row_ref, rank_ref):
    rank_ref[...] = jnp.transpose(jnp.broadcast_to(rank_row_ref[...], (128, SEQ)))


def prepare(
    core, seg_ref, src_ref, rank_ref, limit_ref, pad_ref,
    n0, n1, n2, n3, n4, n5, n6, n7, sq, sk, sv, so, cq, ck, cv, co,
    meta_ref, ranks_ref, limits_ref, norms_ref, ws_ref, wc_ref,
):
    meta_ref[0] = core[0]
    for base, ref in ((1, seg_ref), (17, src_ref)):
        ids = ref[0]
        meta_ref[base] = 0
        meta_ref[base + 15] = SEQ
        for d in range(1, DOCS):
            cut = jnp.sum(jnp.where(ids < d, 1.0, 0.0)).astype(jnp.int32)
            meta_ref[base + d] = cut
            meta_ref[base + 7 + d] = cut
    for place, base in ((33, 1), (34, 17)):
        fast = jnp.int32(1)
        for d in range(DOCS):
            q0 = window_of(meta_ref[1 + d], SEQ - FAST_Q)
            k0 = window_of(meta_ref[base + d], SEQ - FAST_K)
            fits = (meta_ref[9 + d] - q0 <= FAST_Q) & (meta_ref[base + 8 + d] - k0 <= FAST_K)
            fast = fast & fits.astype(jnp.int32)
        meta_ref[place] = fast
    ranks = jnp.where(pad_ref[0] != 0, hidden_rank, rank_ref[0].astype(f32))
    limits = limit_ref[0].astype(f32)
    for i in range(8):
        ranks_ref[0:1, 128 * i : 128 * i + 128] = ranks[i : i + 1]
        limits_ref[0:1, 128 * i : 128 * i + 128] = limits[i : i + 1]
    for i, ref in enumerate((n0, n1, n2, n3, n4, n5, n6, n7)):
        norms_ref[i : i + 1, :] = ref[...]
    for to, parts, out in ((ws_ref, (sq, sk, sv), so), (wc_ref, (cq, ck, cv), co)):
        for i, part in enumerate(parts):
            to[512 * i : 512 * i + 512, :] = part[...]
        for j in range(4):
            to[1536 + 128 * j : 1664 + 128 * j, :] = out[:, 128 * j : 128 * j + 128]


def self_first(
    meta, io, xq_ref, xc_ref, rank_row_ref, limit_ref, norms_ref, w0_ref, w1_ref,
    nq_ref, nc_ref, q_ref, k_ref, v_ref, mixed_ref, p_ref, rank_ref, p_buf, p_sem,
):

    spread_ranks(rank_row_ref, rank_ref)
    wq = lanes([w_query(w0_ref), w_query(w1_ref)])
    wkv = lanes([w_key(w0_ref), w_key(w1_ref), w_value(w0_ref), w_value(w1_ref)])

    def tile(i, carry):
        rows = rows_of(i)
        nq = layer_norm(xq_ref[rows, :].astype(f32), norms_ref[0:1], norms_ref[1:2]).astype(bf16)
        nc = layer_norm(xc_ref[rows, :].astype(f32), norms_ref[2:3], norms_ref[3:4]).astype(bf16)
        nq_ref[rows, :] = nq
        nc_ref[rows, :] = nc
        q_ref[rows, :] = (dot(nq, wq) * (HEAD_DIM**-0.5)).astype(bf16)
        kv = dot(nc, wkv).astype(bf16)
        k_ref[rows, :] = kv[:, :256]
        v_ref[rows, :] = kv[:, 256:]
        return carry

    lax.fori_loop(0, TILES, tile, 0)

    for ref in (nq_ref, nc_ref, q_ref, k_ref, v_ref):
        io.send(ref)
    attend_docs(meta, False, rank_ref, limit_ref, [(q_ref, k_ref, v_ref, mixed_ref)], p_ref, p_buf, p_sem)


def self_second(
    meta, io, xq_ref, nq_ref, nc_ref, rank_row_ref, limit_ref, norms_ref, w0_ref, w1_ref, w2_ref, w3_ref,
    mixed_first_ref,
    q_ref, k_ref, v_ref, mixed_ref, p_ref, second_ref, ncross_ref, rank_ref, p_buf, p_sem,
):

    spread_ranks(rank_row_ref, rank_ref)
    wq = lanes([w_query(w2_ref), w_query(w3_ref)])
    wkv = lanes([w_key(w2_ref), w_key(w3_ref), w_value(w2_ref), w_value(w3_ref)])

    def tile(i, carry):
        rows = rows_of(i)
        q_ref[rows, :] = (dot(nq_ref[rows, :], wq) * (HEAD_DIM**-0.5)).astype(bf16)
        kv = dot(nc_ref[rows, :], wkv).astype(bf16)
        k_ref[rows, :] = kv[:, :256]
        v_ref[rows, :] = kv[:, 256:]
        return carry

    lax.fori_loop(0, TILES, tile, 0)

    for ref in (q_ref, k_ref, v_ref):
        io.send(ref)
    attend_docs(meta, False, rank_ref, limit_ref, [(q_ref, k_ref, v_ref, mixed_ref)], p_ref, p_buf, p_sem)

    io.send(mixed_ref)
    io.wait("late")
    out_first = jnp.concatenate([w_out(w0_ref), w_out(w1_ref)], axis=0)
    out_second = jnp.concatenate([w_out(w2_ref), w_out(w3_ref)], axis=0)

    def tile(i, carry):
        rows = rows_of(i)
        branch = dot(mixed_first_ref[rows, :], out_first) + dot(mixed_ref[rows, :], out_second)
        second = xq_ref[rows, :].astype(f32) + branch
        second_ref[rows, :] = second
        io.send(second_ref, rows)
        ncross_ref[rows, :] = layer_norm(second, norms_ref[4:5], norms_ref[5:6]).astype(bf16)
        io.send(ncross_ref, rows)
        return carry

    lax.fori_loop(0, TILES, tile, 0)


def cross_forward(
    meta, io, second_ref, ncross_ref, memory_ref, norms_ref, w0_ref, w1_ref, w2_ref, w3_ref,
    qa_ref, ka_ref, va_ref, ma_ref, qb_ref, kb_ref, vb_ref, mb_ref, p_ref, third_ref, nffn_ref, p_buf, p_sem,
):
    halves = ((qa_ref, ka_ref, va_ref, ma_ref), (qb_ref, kb_ref, vb_ref, mb_ref))
    weights = (w0_ref, w1_ref, w2_ref, w3_ref)

    wq = lanes([w_query(w) for w in weights])
    wk = lanes([w_key(w) for w in weights])
    wv = lanes([w_value(w) for w in weights])

    def tile(i, carry):
        rows = rows_of(i)
        memory = memory_ref[rows, :]
        q = (dot(ncross_ref[rows, :], wq) * (HEAD_DIM**-0.5)).astype(bf16)
        k = dot(memory, wk).astype(bf16)
        v = dot(memory, wv).astype(bf16)
        for n, (q_ref, k_ref, v_ref, _) in enumerate(halves):
            cols = slice(256 * n, 256 * n + 256)
            q_ref[rows, :] = q[:, cols]
            k_ref[rows, :] = k[:, cols]
            v_ref[rows, :] = v[:, cols]
        return carry

    lax.fori_loop(0, TILES, tile, 0)

    for half in halves:
        for ref in half[0:3]:
            io.send(ref)
    attend_docs(meta, True, None, None, halves, p_ref, p_buf, p_sem)

    io.send(ma_ref)
    io.send(mb_ref)
    io.wait("late")
    out_first = jnp.concatenate([w_out(w0_ref), w_out(w1_ref)], axis=0)
    out_second = jnp.concatenate([w_out(w2_ref), w_out(w3_ref)], axis=0)

    def tile(i, carry):
        rows = rows_of(i)
        branch = dot(ma_ref[rows, :], out_first) + dot(mb_ref[rows, :], out_second)
        third = second_ref[rows, :] + branch
        third_ref[rows, :] = third
        io.send(third_ref, rows)
        nffn_ref[rows, :] = layer_norm(third, norms_ref[6:7], norms_ref[7:8]).astype(bf16)
        io.send(nffn_ref, rows)
        return carry

    lax.fori_loop(0, TILES, tile, 0)


def ffn_both(
    meta, io, third_ref, nffn_ref, cot_ref, norms_ref, u0_ref, u1_ref, u2_ref, u3_ref,
    w0_ref, w1_ref, w2_ref, w3_ref,
    placed_ref, out_ref, g3_ref, g3_low_ref, gln_ref, own_ref, other_ref, hidden_ref, before_ref,
):
    gln_ref[...] = jnp.zeros_like(gln_ref)
    in_refs = (u0_ref, u1_ref, u2_ref, u3_ref)

    def tile(i, carry):
        rows = rows_of(i)
        nffn = nffn_ref[rows, :]
        cot = cot_ref[rows, :]
        outs = []
        grads = []
        for g, w_ref in enumerate((w0_ref, w1_ref, w2_ref, w3_ref)):
            w_in = in_refs[g][...]
            w_out_rows = w_ref[...]
            x = dot(nffn, w_in)
            square = x * x
            half = 0.5 + 0.5 * jnp.tanh(x * (gelu_root + (gelu_root * gelu_cube) * square))
            value = x * half
            hidden = value.astype(bf16)
            rise = 2.0 * gelu_root + (6.0 * gelu_root * gelu_cube) * square
            slope = half + value * (1.0 - half) * rise
            grad_before = (dot_nt(cot, w_out_rows) * slope).astype(bf16)
            outs.append(dot(hidden, w_out_rows))
            grads.append(dot_nt(grad_before, w_in))
            if g < 2:
                hidden_ref[rows, 512 * g : 512 * g + 512] = hidden
                before_ref[rows, 512 * g : 512 * g + 512] = grad_before
        third = third_ref[rows, :]
        result = (third + ((outs[0] + outs[1]) + (outs[2] + outs[3]))).astype(bf16)
        out_ref[rows, :] = result
        placed_ref[rows, :] = result
        grad_normed = (grads[0] + grads[1]) + (grads[2] + grads[3])
        grad_norm, grad_gain, grad_shift = norm_backward(third, norms_ref[6:7], grad_normed)
        g3 = cot.astype(f32) + grad_norm
        g3_ref[rows, :] = g3
        g3_low_ref[rows, :] = g3.astype(bf16)
        gln_ref[0:1, :] += grad_gain
        gln_ref[1:2, :] += grad_shift
        for ref in (out_ref, placed_ref, g3_ref, g3_low_ref):
            io.send(ref, rows)
        return carry

    lax.fori_loop(0, TILES, tile, 0)
    part = dot_tn(nffn_ref[...], before_ref[...])
    own_ref[0:512, :] = part[:, 0:512]
    other_ref[0:512, :] = part[:, 512:1024].astype(bf16)
    io.send(own_ref, pl.ds(0, 512))
    io.send(other_ref, pl.ds(0, 512))
    part = dot_tn(hidden_ref[...], cot_ref[...])
    own_ref[512:1024, :] = part[0:512]
    other_ref[512:1024, :] = part[512:1024].astype(bf16)
    io.send(own_ref, pl.ds(512, 512))
    io.send(other_ref, pl.ds(512, 512))


def back_start(g_ref, mixed_ref, w_refs, dm_ref, dq_ref, dk_ref, dv_ref):
    out_rows = jnp.concatenate([w_out(w) for w in w_refs], axis=0)

    def tile(i, carry):
        rows = rows_of(i)
        dm_ref[rows, :] = dot_nt(g_ref[rows, :], out_rows).astype(bf16)
        zeros = jnp.zeros((TILE, 256), f32)
        dq_ref[rows, :] = zeros
        dk_ref[rows, :] = zeros
        dv_ref[rows, :] = zeros
        return carry

    lax.fori_loop(0, TILES, tile, 0)


def attention_back_first(
    cross, meta, io, g_ref, nq_ref, nkv_ref, rank_row_ref, limit_ref, w0_ref, w1_ref,
    q_ref, k_ref, v_ref, mixed_ref, p_ref,
    dq_ref, dk_ref, dv_ref, own_ref, other_ref,
    rank_ref, dm_ref, dqs_ref, dks_ref, dvs_ref, p_buf, p_sem,
):
    load = (p_ref, p_buf, p_sem, 0)
    start_load(meta, cross, load)
    if not cross:
        spread_ranks(rank_row_ref, rank_ref)
    io.wait("soon")
    back_start(g_ref, mixed_ref, (w0_ref, w1_ref), dm_ref, dqs_ref, dks_ref, dvs_ref)

    attend_docs_back(
        meta, cross, None if cross else rank_ref, limit_ref, q_ref, k_ref, v_ref, mixed_ref,
        dm_ref, dqs_ref, dks_ref, dvs_ref, load,
    )

    dq_ref[...] = dqs_ref[...].astype(bf16)
    dk_ref[...] = dks_ref[...].astype(bf16)
    dv_ref[...] = dvs_ref[...].astype(bf16)
    for ref in (dq_ref, dk_ref, dv_ref):
        io.send(ref)
    io.wait("late")
    nq = nq_ref[...]
    nkv = nkv_ref[...]
    for n, part in enumerate(
        (dot_tn(nq, dq_ref[...]), dot_tn(nkv, dk_ref[...]), dot_tn(nkv, dv_ref[...]))
    ):
        own_ref[:, 128 * n : 128 * n + 128] = part[:, :128]
        other_ref[:, 128 * n : 128 * n + 128] = part[:, 128:].astype(bf16)
    part = dot_tn(mixed_ref[...], g_ref[...])
    for j in range(4):
        rows = slice(128 * j, 128 * j + 128)
        own_ref[rows, 384:512] = part[:128, rows]
        other_ref[rows, 384:512] = part[128:, rows].astype(bf16)


def back_second_docs(
    cross, meta, io, g_ref, rank_row_ref, limit_ref, w_refs, q_ref, k_ref, v_ref, mixed_ref, p_ref,
    rank_ref, dm_ref, dqs_ref, dks_ref, dvs_ref, p_buf, p_sem,
):
    load = (p_ref, p_buf, p_sem, 4 if cross else 0)
    start_load(meta, cross, load)
    if not cross:
        spread_ranks(rank_row_ref, rank_ref)
    io.wait("soon")
    back_start(g_ref, mixed_ref, w_refs, dm_ref, dqs_ref, dks_ref, dvs_ref)

    attend_docs_back(
        meta, cross, None if cross else rank_ref, limit_ref, q_ref, k_ref, v_ref, mixed_ref,
        dm_ref, dqs_ref, dks_ref, dvs_ref, load,
    )


def stream_grads(rows, first, second, firsts, seconds):
    dq, dk, dv = first
    dq2, dk2, dv2 = (ref[rows, :].astype(bf16) for ref in second)
    w0, w1 = firsts
    w2, w3 = seconds
    grad_q = dot_nt(dq[rows, :], lanes([w_query(w0), w_query(w1)])) + dot_nt(
        dq2, lanes([w_query(w2), w_query(w3)])
    )
    kv = lanes([dk[rows, :], dv[rows, :]])
    kv2 = lanes([dk2, dv2])
    grad_kv = dot_nt(kv, lanes([w_key(w0), w_key(w1), w_value(w0), w_value(w1)])) + dot_nt(
        kv2, lanes([w_key(w2), w_key(w3), w_value(w2), w_value(w3)])
    )
    return grad_q, grad_kv


def cross_back_second(
    meta, io, g_low_ref, g_ref, second_ref, norms_ref, w0_ref, w1_ref, w2_ref, w3_ref,
    dq_ref, dk_ref, dv_ref, q_ref, k_ref, v_ref, mixed_ref, p_ref,
    g2_ref, g2_low_ref, placed_ref, gmem_ref, gln_ref,
    dm_ref, dqs_ref, dks_ref, dvs_ref, p_buf, p_sem,
):
    back_second_docs(
        True, meta, io, g_low_ref, None, None, (w2_ref, w3_ref), q_ref, k_ref, v_ref, mixed_ref, p_ref,
        None, dm_ref, dqs_ref, dks_ref, dvs_ref, p_buf, p_sem,
    )

    io.wait("late")
    gln_ref[...] = jnp.zeros_like(gln_ref)

    def tile(i, carry):
        rows = rows_of(i)
        grad_q, grad_kv = stream_grads(
            rows,
            (dq_ref, dk_ref, dv_ref),
            (dqs_ref, dks_ref, dvs_ref),
            (w0_ref, w1_ref),
            (w2_ref, w3_ref),
        )
        low_kv = grad_kv.astype(bf16)
        gmem_ref[rows, :] = low_kv
        placed_ref[rows, :] = low_kv.astype(f32)
        io.send(gmem_ref, rows)
        io.send(placed_ref, rows)
        grad_norm, grad_gain, grad_shift = norm_backward(
            second_ref[rows, :], norms_ref[4:5], grad_q
        )
        g2 = g_ref[rows, :] + grad_norm
        g2_ref[rows, :] = g2
        g2_low_ref[rows, :] = g2.astype(bf16)
        io.send(g2_ref, rows)
        io.send(g2_low_ref, rows)
        gln_ref[0:1, :] += grad_gain
        gln_ref[1:2, :] += grad_shift
        return carry

    lax.fori_loop(0, TILES, tile, 0)


def self_back_second(
    meta, io, g_low_ref, g_ref, xq_ref, xc_ref, rank_row_ref, limit_ref, norms_ref, w0_ref, w1_ref, w2_ref, w3_ref,
    dq_ref, dk_ref, dv_ref, q_ref, k_ref, v_ref, mixed_ref, p_ref,
    placed_q_ref, placed_c_ref, gq_ref, gc_ref, gln_ref,
    rank_ref, dm_ref, dqs_ref, dks_ref, dvs_ref, p_buf, p_sem,
):
    back_second_docs(
        False, meta, io, g_low_ref, rank_row_ref, limit_ref, (w2_ref, w3_ref), q_ref, k_ref, v_ref, mixed_ref,
        p_ref, rank_ref, dm_ref, dqs_ref, dks_ref, dvs_ref, p_buf, p_sem,
    )

    io.wait("late")
    gln_ref[...] = jnp.zeros_like(gln_ref)

    def tile(i, carry):
        rows = rows_of(i)
        grad_q, grad_kv = stream_grads(
            rows,
            (dq_ref, dk_ref, dv_ref),
            (dqs_ref, dks_ref, dvs_ref),
            (w0_ref, w1_ref),
            (w2_ref, w3_ref),
        )
        grad_norm, grad_gain, grad_shift = norm_backward(
            xq_ref[rows, :].astype(f32), norms_ref[0:1], grad_q
        )
        low_q = (g_ref[rows, :] + grad_norm).astype(bf16)
        gq_ref[rows, :] = low_q
        placed_q_ref[rows, :] = low_q.astype(f32)
        io.send(gq_ref, rows)
        io.send(placed_q_ref, rows)
        gln_ref[0:1, :] += grad_gain
        gln_ref[1:2, :] += grad_shift
        grad_norm, grad_gain, grad_shift = norm_backward(
            xc_ref[rows, :].astype(f32), norms_ref[2:3], grad_kv
        )
        low_c = grad_norm.astype(bf16)
        gc_ref[rows, :] = low_c
        placed_c_ref[rows, :] = low_c.astype(f32)
        io.send(gc_ref, rows)
        io.send(placed_c_ref, rows)
        gln_ref[2:3, :] += grad_gain
        gln_ref[3:4, :] += grad_shift
        return carry

    lax.fori_loop(0, TILES, tile, 0)


def place_rows(meta, *refs):
    count = len(refs) // 3
    for n in range(count):
        refs[2 * count + n][...] = refs[n][...].astype(refs[2 * count + n].dtype)


def join_cores(own, other, send):
    joined = own[...] + other[...].astype(f32)
    send[...] = joined.astype(bf16).reshape(send.shape)


def summed(parts, size, first):
    total = parts[0, first : first + size, :].astype(f32)
    for r in range(1, parts.shape[0]):
        total = total + parts[r, first : first + size, :].astype(f32)
    return total.astype(bf16)


def sum_rows(parts, send):
    count, size, _ = parts.shape
    total = summed(parts, size, 0)
    for r in range(count):
        send[r] = total


def sum_rows_join(parts, own, other, send):
    count, done, _ = parts.shape
    size = own.shape[0] // count
    total = summed(parts, done, 0)
    for r in range(count):
        rows = slice(size * r, size * r + size)
        send[r, 0:done, :] = total
        send[r, done : done + size, :] = (own[rows, :] + other[rows, :].astype(f32)).astype(bf16)


def sum_last(done, parts, gln_own, gln_other, send):
    count = parts.shape[0]
    size = parts.shape[1] - done
    total = summed(parts, size, done)
    gln = gln_own[...] + gln_other[...]
    gln = jnp.concatenate([gln, jnp.zeros((8, D), f32)], axis=0).astype(bf16)
    for r in range(count):
        send[r, 0:size, :] = total
        send[r, size : size + 16, :] = gln


def unpack_attention(parts, outs):
    count = parts.shape[0]
    size = D // count
    for r in range(count):
        rows = slice(size * r, size * r + size)
        for i in range(3):
            outs[i][rows, :] = parts[r, 0:size, 128 * i : 128 * i + 128].astype(f32)
        j, first = divmod(size * r, 128)
        outs[3][first : first + size, 128 * j : 128 * j + 128] = parts[r, 0:size, 384:512].astype(f32)


def unpack_early(ffn, cross, *outs):
    count, size, _ = ffn.shape
    for r in range(count):
        out = outs[2 * r // count]
        first = (size * r) % D
        out[first : first + size, :] = ffn[r].astype(f32)
    unpack_attention(cross, outs[2:])


def unpack_late(parts, *outs):
    unpack_attention(parts, outs[:4])
    size = parts.shape[1] - 16
    total = parts[0, size : size + 16, :].astype(f32)
    for r in range(1, parts.shape[0]):
        total = total + parts[r, size : size + 16, :].astype(f32)
    outs[4][...] = total[0:8]


def whole(shape):
    zeros = (0,) * len(shape)
    return pl.BlockSpec(shape, lambda d, meta: zeros)


def own_row(width):
    return pl.BlockSpec((SEQ, width), lambda d, meta: (meta[0], 0))


ANY = pl.BlockSpec(memory_space=pl.ANY)


def in_hbm(x):
    return pltpu.with_memory_space_constraint(x, pltpu.HBM)


def probability_out(heads):
    return (pltpu.HBM((DOCS, heads, FAST_K, FAST_Q), bf16), None, ANY)


def probability_scratch(heads):
    return [pltpu.VMEM((2, 2, heads, FAST_K, FAST_Q), bf16), pltpu.SemaphoreType.DMA((2,))]


class Copies:
    def __init__(self, meta):
        self.first = meta[0] * SEQ
        self.loads = {}
        self.sends = []

    def load(self, stage, source, target, sem, own_row):
        if own_row:
            source = source.at[pl.ds(pl.multiple_of(self.first, SEQ), SEQ)]
        copy = pltpu.make_async_copy(source, target, sem)
        self.loads.setdefault(stage, []).append(copy)

    def start(self):
        for stage in ("now", "soon", "late"):
            for copy in self.loads.get(stage, []):
                copy.start()

    def wait(self, stage):
        for copy in self.loads.pop(stage, []):
            copy.wait()

    def result(self, source, target, sem, own_row):
        self.sends.append([source, target, sem, own_row, False])

    def send(self, ref, rows=None):
        for entry in self.sends:
            source, target, sem, own_row, _ = entry
            if source is ref:
                entry[4] = True
                first = self.first if own_row else 0
                if rows is None:
                    size = source.shape[0]
                else:
                    source = source.at[rows]
                    first, size = first + rows.start, rows.size
                if rows is not None or own_row:
                    target = target.at[pl.ds(pl.multiple_of(first, size), size)]
                pltpu.make_async_copy(source, target, sem).start()

    def finish(self):
        for stage in list(self.loads):
            self.wait(stage)
        for source, _, _, _, started in self.sends:
            if not started:
                self.send(source)
        for source, target, sem, own_row, _ in self.sends:
            if own_row:
                target = target.at[pl.ds(pl.multiple_of(self.first, SEQ), SEQ)]
            pltpu.make_async_copy(source, target, sem).wait()


def out(shape, dtype, own_row=False):
    return (shape, dtype, own_row)


def call(kernel, name, operands, outs, scratch, flops, token=None):
    arrays = [operands[0][0]]
    in_specs, out_specs, out_shapes = [], [], []
    buffers = []
    loads = []
    for n, (x, how) in enumerate(operands[1:]):
        if isinstance(how, str):
            stage, _, row = how.partition("_")
            shape = ((SEQ,) + x.shape[1:]) if row else x.shape
            loads.append((n, stage, len(buffers), bool(row)))
            buffers.append(pltpu.VMEM(shape, x.dtype))
            arrays.append(in_hbm(x))
            in_specs.append(ANY)
        else:
            arrays.append(x)
            in_specs.append(how)
    results = []
    for n, (shape, dtype, how) in enumerate(outs):
        if isinstance(how, bool):
            results.append((n, len(buffers), how))
            buffers.append(pltpu.VMEM(shape, dtype))
            shape = ((2 * SEQ,) + shape[1:]) if how else shape
            out_shapes.append(pltpu.HBM(shape, dtype))
            out_specs.append(ANY)
        else:
            out_shapes.append(jax.ShapeDtypeStruct(shape, dtype) if dtype else shape)
            out_specs.append(how)
    n_in, n_out = len(in_specs), len(out_specs)
    if token is not None:
        arrays.append(token)
        in_specs.append(whole((8, 128)))
        out_specs.append(whole((8, 128)))
        out_shapes.append(jax.ShapeDtypeStruct((8, 128), f32))

    def body(meta, *refs):
        ins, refs = list(refs[:n_in]), refs[len(in_specs) - n_in + n_in :]
        results_out, refs = list(refs[:n_out]), refs[n_out:]
        if token is not None:
            token_out, refs = refs[0], refs[1:]
            token_out[...] = jnp.zeros_like(token_out)
        bufs, refs = refs[: len(buffers)], refs[len(buffers) :]
        rest = refs[: len(scratch)]
        copies = Copies(meta)
        if buffers:
            sems = refs[len(scratch)]
        for n, stage, b, row in loads:
            copies.load(stage, ins[n], bufs[b], sems.at[b], row)
            ins[n] = bufs[b]
        for n, b, row in results:
            copies.result(bufs[b], results_out[n], sems.at[b], row)
            results_out[n] = bufs[b]
        copies.start()
        copies.wait("now")
        if buffers:
            kernel(meta, copies, *ins, *results_out, *rest)
        else:
            kernel(meta, *ins, *results_out, *rest)
        copies.finish()

    moved = sum(x.size * x.dtype.itemsize for x in arrays[1:])
    sems = [pltpu.SemaphoreType.DMA((len(buffers),))] if buffers else []
    return pl.pallas_call(
        body,
        name=name,
        grid_spec=pltpu.PrefetchScalarGridSpec(
            num_scalar_prefetch=1,
            grid=(1,),
            in_specs=in_specs,
            out_specs=out_specs,
            scratch_shapes=buffers + scratch + sems,
        ),
        out_shape=out_shapes,
        compiler_params=pltpu.CompilerParams(
            dimension_semantics=("arbitrary",), vmem_limit_bytes=50 * 1024 * 1024
        ),
        cost_estimate=pl.CostEstimate(
            flops=int(flops), bytes_accessed=int(moved), transcendentals=0
        ),
    )(*arrays)


def simple(kernel, name, operands, outs):
    return pl.pallas_call(
        kernel,
        name=name,
        out_shape=[jax.ShapeDtypeStruct(shape, dtype) for shape, dtype in outs],
        compiler_params=pltpu.CompilerParams(vmem_limit_bytes=8 * 1024 * 1024),
    )(*operands)


def full(x):
    return (x, whole(x.shape))


def shards(
    query_stream,
    content_stream,
    memory,
    segment_ids,
    source_segments,
    context_rank,
    context_limit,
    padding,
    ln_query_gain,
    ln_query_bias,
    ln_content_gain,
    ln_content_bias,
    self_query,
    self_key,
    self_value,
    self_out,
    ln_cross_gain,
    ln_cross_bias,
    cross_query,
    cross_key,
    cross_value,
    cross_out,
    ln_ffn_gain,
    ln_ffn_bias,
    ffn_in,
    ffn_out,
    cotangent,
):
    core = lax.axis_index("heads") % 2

    def to_core(x):
        return lax.ppermute(x, "heads", [(h, h ^ 1) for h in range(4)])

    hold = lambda *xs: lax.optimization_barrier(xs)

    def to_chip(x):
        return lax.ppermute(x, "heads", [(h, h ^ 2) for h in range(4)])

    row = pl.BlockSpec((1, 8, 128), lambda d, core: (core[0], 0, 0))

    def token_row(x):
        return (in_hbm(x.reshape(2, 8, 128)), row)

    def fixed(x):
        zeros = (0,) * x.ndim
        return (in_hbm(x), pl.BlockSpec(x.shape, lambda d, core: zeros))

    prepared = [
        ((35,), jnp.int32, pl.BlockSpec(memory_space=pltpu.SMEM)),
        ((1, SEQ), f32, whole((1, SEQ))),
        ((1, SEQ), f32, whole((1, SEQ))),
        ((8, D), f32, whole((8, D))),
        ((2048, 128), bf16, whole((2048, 128))),
        ((2048, 128), bf16, whole((2048, 128))),
    ]
    gains = (
        ln_query_gain,
        ln_query_bias,
        ln_content_gain,
        ln_content_bias,
        ln_cross_gain,
        ln_cross_bias,
        ln_ffn_gain,
        ln_ffn_bias,
    )
    weights = (self_query, self_key, self_value, self_out)
    weights += (cross_query, cross_key, cross_value, cross_out)
    tokens = (segment_ids, source_segments, context_rank, context_limit, padding)
    meta, rank, limit, norms, ws0, wc0 = call(
        prepare,
        "prepare",
        [(core.astype(jnp.int32)[None], None)]
        + [token_row(x) for x in tokens]
        + [fixed(x.reshape(1, D)) for x in gains]
        + [fixed(x) for x in weights],
        prepared,
        [],
        0,
    )

    ws1 = to_core(ws0)
    ws2 = to_chip(ws0)
    wc2 = to_chip(wc0)
    u0, u2 = ffn_in, to_chip(ffn_in)
    wf0, wf2 = ffn_out, to_chip(ffn_out)
    meta_in = (meta, None)

    heads_out = [out((SEQ, 256), bf16)] * 4

    def stream_out(dtype, own_row=False):
        return out((SEQ, D), dtype, own_row)

    def now(*xs):
        return [(x, "now") for x in xs]

    def soon(*xs):
        return [(x, "soon") for x in xs]

    def late(*xs):
        return [(x, "late") for x in xs]

    def small(*xs):
        return [(x, whole(x.shape)) for x in xs]

    limits = pltpu.VMEM((SEQ, 128), f32)
    pair_flops = 2 * SEQ * D * 768 + 2 * 2 * 4 * DOCS * FAST_Q * FAST_K * 256

    nq, nc, *first, token = call(
        self_first,
        "self_first",
        [meta_in, (query_stream, "now_row"), (content_stream, "now_row")]
        + small(rank, limit, norms)
        + now(ws0, ws1),
        [stream_out(bf16), stream_out(bf16)] + heads_out + [probability_out(4)],
        [limits] + probability_scratch(4),
        pair_flops,
        jnp.zeros((8, 128), f32),
    )
    ws2, wc0, token = hold(ws2, wc0, token)
    ws3 = to_core(ws2)
    wc1 = to_core(wc0)
    *second_heads, second, ncross, token = call(
        self_second,
        "self_second",
        [meta_in, (query_stream, "late_row")]
        + now(nq, nc)
        + small(rank, limit, norms)
        + late(ws0, ws1)
        + now(ws2, ws3)
        + late(first[3]),
        heads_out + [probability_out(4), stream_out(f32), stream_out(bf16)],
        [limits] + probability_scratch(4),
        pair_flops + 2 * SEQ * D * D,
        token,
    )
    wc2, u0, wf0, token = hold(wc2, u0, wf0, token)
    wc3 = to_core(wc2)
    u1 = to_core(u0)
    wf1 = to_core(wf0)
    *cross_heads, third, nffn, token = call(
        cross_forward,
        "cross_forward",
        [meta_in]
        + late(second)
        + now(ncross)
        + [(memory, "now_row")]
        + small(norms)
        + now(wc0, wc1, wc2, wc3),
        heads_out + heads_out + [probability_out(8), stream_out(f32), stream_out(bf16)],
        probability_scratch(8),
        2 * pair_flops + 2 * SEQ * D * D,
        token,
    )
    u2, wf2, token = hold(u2, wf2, token)
    u3 = to_core(u2)
    wf3 = to_core(wf2)
    grads_ln = ((8, D), f32, whole((8, D)))
    placed_output, output, g3, g3_low, gln_ffn, ffn_own, ffn_other, token = call(
        ffn_both,
        "ffn_both",
        [meta_in]
        + now(third, nffn)
        + [(cotangent, "now_row")]
        + small(norms)
        + now(u0, u1, u2, u3, wf0, wf1, wf2, wf3),
        [
            stream_out(bf16, True),
            stream_out(bf16),
            stream_out(f32),
            stream_out(bf16),
            grads_ln,
            out((1024, D), f32),
            out((1024, D), bf16),
        ],
        [pltpu.VMEM((SEQ, 1024), bf16), pltpu.VMEM((SEQ, 1024), bf16)],
        12 * SEQ * D * 2048,
        token,
    )

    row_count = lax.axis_size("rows")

    def exchange(x):
        return lax.all_to_all(x, "rows", 0, 0)

    def chunks(n):
        return [((row_count, n, D), bf16)]

    size = 1024 // row_count
    half = size // 2
    (ffn_send,) = simple(join_cores, "join_ffn", [ffn_own, to_core(ffn_other)], chunks(size))
    token, ffn_send = hold(token, ffn_send)
    ffn_parts = exchange(ffn_send)

    back_scratch = [pltpu.VMEM((SEQ, 256), bf16)] + [pltpu.VMEM((SEQ, 256), f32)] * 3
    back_scratch += probability_scratch(4)
    pair_out = out((SEQ, 256), bf16)
    packed_outs = [out((D, D), f32), out((D, D), bf16)]
    back_flops = 2 * SEQ * D * 256 + 4 * 2 * 4 * DOCS * FAST_Q * FAST_K * 256

    def head_inputs(natural, p):
        return soon(*natural) + [(in_hbm(p), ANY)]

    *cross_grads, cross_own, cross_other, token = call(
        functools.partial(attention_back_first, True),
        "cross_back_first",
        [meta_in]
        + now(g3_low)
        + late(ncross)
        + [(memory, "late_row")]
        + small(rank, limit)
        + now(wc0, wc1)
        + head_inputs(cross_heads[0:4], cross_heads[8]),
        [pair_out] * 3 + packed_outs,
        [limits] + back_scratch,
        back_flops + 2 * SEQ * D * 1024,
        token,
    )
    ffn_parts, token = hold(ffn_parts, token)
    (ffn_total,) = simple(sum_rows, "sum_ffn", [ffn_parts], chunks(size))
    ffn_total, token = hold(ffn_total, token)
    ffn_sums = exchange(ffn_total)
    cross_other = to_core(cross_other)
    g2, g2_low, placed_mem, grad_mem, gln_cross, token = call(
        cross_back_second,
        "cross_back_second",
        [meta_in]
        + now(g3_low)
        + late(g3, second)
        + small(norms)
        + late(wc0, wc1)
        + now(wc2, wc3)
        + late(*cross_grads)
        + head_inputs(cross_heads[4:8], cross_heads[8]),
        [stream_out(f32), stream_out(bf16), stream_out(f32, True), stream_out(bf16), grads_ln],
        back_scratch,
        back_flops + 2 * SEQ * D * 1536,
        token,
    )
    ffn_sums, cross_other, token = hold(ffn_sums, cross_other, token)
    (cross_send,) = simple(join_cores, "join_cross", [cross_own, cross_other], chunks(half))
    cross_send, token = hold(cross_send, token)
    cross_parts = exchange(cross_send)

    *self_grads, self_own, self_other, token = call(
        functools.partial(attention_back_first, False),
        "self_back_first",
        [meta_in]
        + now(g2_low)
        + late(nq, nc)
        + small(rank, limit)
        + now(ws0, ws1)
        + head_inputs(first[0:4], first[4]),
        [pair_out] * 3 + packed_outs,
        [limits] + back_scratch,
        back_flops + 2 * SEQ * D * 1024,
        token,
    )
    self_other = to_core(self_other)
    cross_parts, token = hold(cross_parts, token)
    (both_send,) = simple(
        sum_rows_join, "sum_cross", [cross_parts, self_own, self_other], chunks(2 * half)
    )
    both_send, token = hold(both_send, token)
    both_parts = exchange(both_send)
    placed_q, placed_c, gq, gc, gln_self, token = call(
        self_back_second,
        "self_back_second",
        [meta_in]
        + now(g2_low)
        + late(g2)
        + [(query_stream, "late_row"), (content_stream, "late_row")]
        + small(rank, limit, norms)
        + late(ws0, ws1)
        + now(ws2, ws3)
        + late(*self_grads)
        + head_inputs(second_heads[0:4], second_heads[4]),
        [stream_out(f32, True), stream_out(f32, True), stream_out(bf16), stream_out(bf16), grads_ln],
        [limits] + back_scratch,
        back_flops + 2 * SEQ * D * 1536,
        token,
    )

    gln = jnp.concatenate([gln_self[0:4], gln_cross[0:2], gln_ffn[0:2]], axis=0)
    both_parts, gln = hold(both_parts, gln)
    (last_send,) = simple(
        functools.partial(sum_last, half), "sum_self", [both_parts, gln, to_core(gln)], chunks(half + 16)
    )
    last_parts = exchange(last_send)

    def both_rows(placed_own, arrays, name):
        count = len(arrays)
        size = SEQ // 2
        one = pl.BlockSpec((size, D), lambda i, meta: (i, 0))
        block = pl.BlockSpec((size, D), lambda i, meta: (2 * (1 - meta[0]) + i, 0))
        return pl.pallas_call(
            place_rows,
            name=name,
            grid_spec=pltpu.PrefetchScalarGridSpec(
                num_scalar_prefetch=1,
                grid=(2,),
                in_specs=[one] * count + [pl.BlockSpec(memory_space=pl.ANY)] * count,
                out_specs=[block] * count,
            ),
            out_shape=[jax.ShapeDtypeStruct(x.shape, x.dtype) for x in placed_own],
            input_output_aliases={1 + count + n: n for n in range(count)},
        )(meta, *[to_core(x) for x in arrays], *placed_own)

    out_both, grad_mem_both = both_rows([placed_output, placed_mem], [output, grad_mem], "place_early")
    gq_both, gc_both = both_rows([placed_q, placed_c], [gq, gc], "place_late")

    attention_outs = [((512, 128), f32)] * 3 + [((128, 512), f32)]
    grad_ffn_in, grad_ffn_out, *grad_cross_parts = simple(
        unpack_early, "unpack_early", [ffn_sums, both_parts], [((D, D), f32)] * 2 + attention_outs
    )
    *grad_self_parts, gln = simple(
        unpack_late, "unpack_late", [last_parts], attention_outs + [((8, D), f32)]
    )
    return (
        out_both,
        gq_both,
        gc_both,
        grad_mem_both,
        gln[0],
        gln[1],
        gln[2],
        gln[3],
        *grad_self_parts,
        gln[4],
        gln[5],
        *grad_cross_parts,
        gln[6],
        gln[7],
        grad_ffn_in,
        grad_ffn_out,
    )


def solution(mesh):
    assert mesh.shape["heads"] == 4
    row_spec = P("rows", None)
    flat = P("rows")
    by_column = P(None, "heads")
    by_row = P("heads", None)
    attention = (by_column, by_column, by_column, by_row)
    in_specs = (
        (row_spec,) * 3
        + (flat,) * 5
        + (P(),) * 4
        + attention
        + (P(),) * 2
        + attention
        + (P(),) * 2
        + (by_column, by_row, row_spec)
    )
    out_specs = (
        (row_spec,) * 4
        + (P(),) * 4
        + attention
        + (P(),) * 2
        + attention
        + (P(),) * 2
        + (by_column, by_row)
    )
    return jax.shard_map(shards, mesh=mesh, in_specs=in_specs, out_specs=out_specs, check_vma=False)
```

```python
import functools

import jax
import jax.numpy as jnp
from jax import lax
from jax.experimental import pallas as pl
from jax.experimental.pallas import tpu as pltpu
from jax.sharding import PartitionSpec as P

HEAD_DIM = 64
SEQ = 1024
DOCS = 8
D = 512
TILE = 256
TILES = SEQ // TILE
FAST_Q = 256
FAST_K = 208
LONG_Q = 128
LONG_K = 640

norm_eps = 1e-05
masked_score = -1e30
hidden_rank = 1e6
gelu_root = 0.7978845608028654
gelu_cube = 0.044715

f32 = jnp.float32
bf16 = jnp.bfloat16


def dot(a, b):
    return lax.dot_general(a, b, (((1,), (0,)), ((), ())), preferred_element_type=f32)


def dot_nt(a, b):
    return lax.dot_general(a, b, (((1,), (1,)), ((), ())), preferred_element_type=f32)


def dot_tn(a, b):
    return lax.dot_general(a, b, (((0,), (0,)), ((), ())), preferred_element_type=f32)


def lanes(parts):
    return jnp.concatenate(parts, axis=1)


def layer_norm(values, gain, shift):
    centre = values - jnp.mean(values, axis=-1, keepdims=True)
    spread = jnp.mean(centre * centre, axis=-1, keepdims=True)
    return centre * lax.rsqrt(spread + norm_eps) * gain + shift


def norm_backward(values, gain, grad):
    centre = values - jnp.mean(values, axis=-1, keepdims=True)
    spread = jnp.mean(centre * centre, axis=-1, keepdims=True)
    scale = lax.rsqrt(spread + norm_eps)
    xhat = centre * scale
    eg = grad * gain
    mean_eg = jnp.mean(eg, axis=-1, keepdims=True)
    mean_egx = jnp.mean(eg * xhat, axis=-1, keepdims=True)
    grad_gain = jnp.sum(grad * xhat, axis=0, keepdims=True)
    grad_shift = jnp.sum(grad, axis=0, keepdims=True)
    return scale * (eg - mean_eg - xhat * mean_egx), grad_gain, grad_shift


def rows_of(i, size=TILE):
    return pl.ds(pl.multiple_of(i * size, size), size)


def w_query(ref):
    return ref[0:512, :]


def w_key(ref):
    return ref[512:1024, :]


def w_value(ref):
    return ref[1024:1536, :]


def w_out(ref):
    return lanes([ref[1536 + 128 * j : 1664 + 128 * j, :] for j in range(4)])


def half_masks():
    place = lax.broadcasted_iota(jnp.int32, (1, 128), 1)
    low = jnp.where(place < HEAD_DIM, 1.0, 0.0).astype(f32)
    return (low.astype(bf16), (1.0 - low).astype(bf16))


def doc_bounds(meta, d, source):
    base = 17 if source else 1
    return meta[base + d], meta[base + 8 + d]


def window_of(first, limit):
    return pl.multiple_of(jnp.minimum((first // 16) * 16, limit), 16)


def key_bias(ks, ke, k0, width):
    place = k0 + lax.broadcasted_iota(jnp.int32, (width, 128), 0)
    return jnp.where((place >= ks) & (place < ke), 0.0, masked_score)


def make_bias(rank_ref, limit_ref, ks, ke, q0, k0, span, width):
    if rank_ref is None:
        return lanes([key_bias(ks, ke, k0, width)] * (span // 128))
    place = k0 + lax.broadcasted_iota(jnp.int32, (width, 128), 0)
    ranks = rank_ref[pl.ds(k0, width), :]
    ranks = jnp.where((place < ks + 2) & (ranks < hidden_rank), -1.0, ranks)
    ranks = jnp.where((place >= ks) & (place < ke), ranks, hidden_rank)
    limits = jnp.broadcast_to(limit_ref[...], (8, SEQ))
    limits = pltpu.roll(limits, lax.rem(SEQ - q0, SEQ), 1)[0:1, 0:span]
    row = k0 + lax.broadcasted_iota(jnp.int32, (width, span), 0)
    column = q0 + lax.broadcasted_iota(jnp.int32, (width, span), 1)
    seen = (lanes([ranks] * (span // 128)) < limits) & (row != column)
    return jnp.where(seen, 0.0, masked_score)


STEPS = DOCS // 2


def is_fast(meta, cross):
    return meta[34 if cross else 33] == 1


def both_heads(x, masks):
    return jnp.concatenate([x * masks[0], x * masks[1]], axis=0)


def pair_probabilities(queries, keys, masks, bias):
    width = keys.shape[0]
    scores = dot_nt(both_heads(keys, masks), queries)
    result = []
    for a in range(2):
        part = scores[width * a : width * a + width] + bias
        part = jnp.exp(part - jnp.max(part, axis=0, keepdims=True))
        part = part * (1.0 / jnp.sum(part, axis=0, keepdims=True))
        result.append(part.astype(bf16))
    return result


def pair_product(rows, parts):
    across = jnp.transpose(rows)
    halves = [dot(across[64 * a : 64 * a + 64], part) for a, part in enumerate(parts)]
    return jnp.transpose(jnp.concatenate(halves, axis=0))


def for_docs(meta, cross, run, before, after):
    @pl.when(is_fast(meta, cross))
    def _():
        def step(i, carry):
            slot = lax.rem(i, 2)
            before(i, slot)
            for place in range(2):
                d = 2 * i + place
                ts, te = doc_bounds(meta, d, False)
                ks, ke = doc_bounds(meta, d, cross)
                q0 = window_of(ts, SEQ - FAST_Q)
                k0 = window_of(ks, SEQ - FAST_K)
                run(d, slot, place, q0, k0, FAST_Q, FAST_K, ts, te, ks, ke, True)
            after(i, slot)
            return carry

        lax.fori_loop(0, STEPS, step, 0)

    @pl.when(jnp.logical_not(is_fast(meta, cross)))
    def _():
        def doc(d, carry):
            ts, te = doc_bounds(meta, d, False)
            ks, ke = doc_bounds(meta, d, cross)
            base = (ts // 16) * 16
            k0 = window_of(ks, SEQ - LONG_K)

            def chunk(i, carry):
                lower = base + i * LONG_Q
                q0 = pl.multiple_of(jnp.minimum(lower, SEQ - LONG_Q), 16)
                low = jnp.maximum(ts, lower)
                high = jnp.minimum(te, lower + LONG_Q)
                run(d, None, None, q0, k0, LONG_Q, LONG_K, low, high, ks, ke, False)
                return carry

            return lax.fori_loop(0, (te - base + LONG_Q - 1) // LONG_Q, chunk, carry)

        lax.fori_loop(0, DOCS, doc, 0)


def attend_docs(meta, cross, rank_ref, limit_ref, halves, p_ref, p_buf, p_sem):
    pairs = 2 * len(halves)
    masks = half_masks()

    def save(i, slot):
        return pltpu.make_async_copy(p_buf.at[slot], p_ref.at[pl.ds(2 * i, 2)], p_sem.at[slot])

    def before(i, slot):
        @pl.when(i >= 2)
        def _():
            save(i - 2, slot).wait()

    def after(i, slot):
        save(i, slot).start()

    def run(d, slot, place, q0, k0, span, width, low, high, ks, ke, fast):
        bias = make_bias(rank_ref, limit_ref, ks, ke, q0, k0, span, width)
        row = q0 + lax.broadcasted_iota(jnp.int32, (span, 128), 0)
        inside = (row >= low) & (row < high)
        for n in range(pairs):
            q_ref, k_ref, v_ref, mixed_ref = halves[n // 2]
            cols = slice(128 * (n % 2), 128 * (n % 2) + 128)
            queries = q_ref[pl.ds(q0, span), cols]
            keys = k_ref[pl.ds(k0, width), cols]
            values = v_ref[pl.ds(k0, width), cols]
            parts = pair_probabilities(queries, keys, masks, bias)
            if fast:
                for a in range(2):
                    p_buf[slot, place, 2 * n + a] = parts[a]
            mixed = pair_product(values, parts)
            old = mixed_ref[pl.ds(q0, span), cols].astype(f32)
            mixed_ref[pl.ds(q0, span), cols] = jnp.where(inside, mixed, old).astype(bf16)

    for_docs(meta, cross, run, before, after)

    @pl.when(is_fast(meta, cross))
    def _():
        for i in range(STEPS - 2, STEPS):
            save(i, i % 2).wait()


def load_step(load, i, slot):
    p_ref, p_buf, p_sem, first = load
    part = p_ref.at[pl.ds(2 * i, 2), pl.ds(first, 4)]
    return pltpu.make_async_copy(part, p_buf.at[slot], p_sem.at[slot])


def start_load(meta, cross, load):
    @pl.when(is_fast(meta, cross))
    def _():
        load_step(load, 0, 0).start()


def attend_docs_back(
    meta, cross, rank_ref, limit_ref, q_ref, k_ref, v_ref, mixed_ref, dm_ref,
    dq_ref, dk_ref, dv_ref, load,
):
    pairs = q_ref.shape[1] // 128
    masks = half_masks()
    p_buf = load[1]

    def before(i, slot):
        @pl.when(i + 1 < STEPS)
        def _():
            load_step(load, i + 1, 1 - slot).start()

        load_step(load, i, slot).wait()

    def after(i, slot):
        pass

    def run(d, slot, place, q0, k0, span, width, low, high, ks, ke, fast):
        row = q0 + lax.broadcasted_iota(jnp.int32, (span, 128), 0)
        inside = (row >= low) & (row < high)
        ones = jnp.ones((width, 128), bf16)
        if not fast:
            bias = make_bias(rank_ref, limit_ref, ks, ke, q0, k0, span, width)
        for n in range(pairs):
            cols = slice(128 * n, 128 * n + 128)
            queries = q_ref[pl.ds(q0, span), cols]
            keys = k_ref[pl.ds(k0, width), cols]
            values = v_ref[pl.ds(k0, width), cols]
            mixed = mixed_ref[pl.ds(q0, span), cols].astype(f32)
            grad = jnp.where(inside, dm_ref[pl.ds(q0, span), cols].astype(f32), 0.0)
            low_grad = grad.astype(bf16)
            left = lanes([low_grad, (-(grad * mixed)).astype(bf16)])
            delta = dot_nt(both_heads(lanes([values, ones]), [lanes([m, m]) for m in masks]), left)
            if fast:
                parts = [p_buf[slot, place, 2 * n + a] for a in range(2)]
            else:
                parts = pair_probabilities(queries, keys, masks, bias)
            slopes = []
            dk = dv = None
            for a in range(2):
                slope = parts[a].astype(f32) * delta[width * a : width * a + width]
                slopes.append(slope.astype(bf16))
                dk_a = dot(slopes[a], queries * masks[a])
                dv_a = dot(parts[a], low_grad * masks[a])
                dk = dk_a if dk is None else dk + dk_a
                dv = dv_a if dv is None else dv + dv_a
            dq = pair_product(keys, slopes)
            dq_ref[pl.ds(q0, span), cols] += dq * (HEAD_DIM**-0.5)
            dk_ref[pl.ds(k0, width), cols] += dk
            dv_ref[pl.ds(k0, width), cols] += dv

    for_docs(meta, cross, run, before, after)


def spread_ranks(rank_row_ref, rank_ref):
    rank_ref[...] = jnp.transpose(jnp.broadcast_to(rank_row_ref[...], (128, SEQ)))


def prepare(
    core, seg_ref, src_ref, rank_ref, limit_ref, pad_ref,
    n0, n1, n2, n3, n4, n5, n6, n7, sq, sk, sv, so, cq, ck, cv, co,
    meta_ref, ranks_ref, limits_ref, norms_ref, ws_ref, wc_ref,
):
    meta_ref[0] = core[0]
    meta_ref[35] = core[1]
    for base, ref in ((1, seg_ref), (17, src_ref)):
        ids = ref[0]
        meta_ref[base] = 0
        meta_ref[base + 15] = SEQ
        for d in range(1, DOCS):
            cut = jnp.sum(jnp.where(ids < d, 1.0, 0.0)).astype(jnp.int32)
            meta_ref[base + d] = cut
            meta_ref[base + 7 + d] = cut
    for place, base in ((33, 1), (34, 17)):
        fast = jnp.int32(1)
        for d in range(DOCS):
            q0 = window_of(meta_ref[1 + d], SEQ - FAST_Q)
            k0 = window_of(meta_ref[base + d], SEQ - FAST_K)
            fits = (meta_ref[9 + d] - q0 <= FAST_Q) & (meta_ref[base + 8 + d] - k0 <= FAST_K)
            fast = fast & fits.astype(jnp.int32)
        meta_ref[place] = fast
    ranks = jnp.where(pad_ref[0] != 0, hidden_rank, rank_ref[0].astype(f32))
    limits = limit_ref[0].astype(f32)
    for i in range(8):
        ranks_ref[0:1, 128 * i : 128 * i + 128] = ranks[i : i + 1]
        limits_ref[0:1, 128 * i : 128 * i + 128] = limits[i : i + 1]
    for i, ref in enumerate((n0, n1, n2, n3, n4, n5, n6, n7)):
        norms_ref[i : i + 1, :] = ref[...]
    for to, parts, out in ((ws_ref, (sq, sk, sv), so), (wc_ref, (cq, ck, cv), co)):
        for i, part in enumerate(parts):
            to[512 * i : 512 * i + 512, :] = part[...]
        for j in range(4):
            to[1536 + 128 * j : 1664 + 128 * j, :] = out[:, 128 * j : 128 * j + 128]


def self_first(
    meta, io, xq_ref, xc_ref, rank_row_ref, limit_ref, norms_ref, w0_ref, w1_ref,
    nq_ref, nc_ref, q_ref, k_ref, v_ref, mixed_ref, p_ref, rank_ref, p_buf, p_sem,
):

    spread_ranks(rank_row_ref, rank_ref)
    wq = lanes([w_query(w0_ref), w_query(w1_ref)])
    wkv = lanes([w_key(w0_ref), w_key(w1_ref), w_value(w0_ref), w_value(w1_ref)])

    def tile(i, carry):
        rows = rows_of(i)
        io.wait_rows(i)
        nq = layer_norm(xq_ref[rows, :].astype(f32), norms_ref[0:1], norms_ref[1:2]).astype(bf16)
        nc = layer_norm(xc_ref[rows, :].astype(f32), norms_ref[2:3], norms_ref[3:4]).astype(bf16)
        nq_ref[rows, :] = nq
        nc_ref[rows, :] = nc
        q_ref[rows, :] = (dot(nq, wq) * (HEAD_DIM**-0.5)).astype(bf16)
        kv = dot(nc, wkv).astype(bf16)
        k_ref[rows, :] = kv[:, :256]
        v_ref[rows, :] = kv[:, 256:]
        return carry

    lax.fori_loop(0, TILES, tile, 0)

    for ref in (nq_ref, nc_ref, q_ref, k_ref, v_ref):
        io.send(ref)
    attend_docs(meta, False, rank_ref, limit_ref, [(q_ref, k_ref, v_ref, mixed_ref)], p_ref, p_buf, p_sem)


def self_second(
    meta, io, xq_ref, nq_ref, nc_ref, rank_row_ref, limit_ref, norms_ref, w0_ref, w1_ref, w2_ref, w3_ref,
    mixed_first_ref,
    q_ref, k_ref, v_ref, mixed_ref, p_ref, second_ref, ncross_ref, rank_ref, p_buf, p_sem,
):

    spread_ranks(rank_row_ref, rank_ref)
    wq = lanes([w_query(w2_ref), w_query(w3_ref)])
    wkv = lanes([w_key(w2_ref), w_key(w3_ref), w_value(w2_ref), w_value(w3_ref)])

    def tile(i, carry):
        rows = rows_of(i)
        io.wait_rows(i)
        q_ref[rows, :] = (dot(nq_ref[rows, :], wq) * (HEAD_DIM**-0.5)).astype(bf16)
        kv = dot(nc_ref[rows, :], wkv).astype(bf16)
        k_ref[rows, :] = kv[:, :256]
        v_ref[rows, :] = kv[:, 256:]
        return carry

    lax.fori_loop(0, TILES, tile, 0)

    for ref in (q_ref, k_ref, v_ref):
        io.send(ref)
    attend_docs(meta, False, rank_ref, limit_ref, [(q_ref, k_ref, v_ref, mixed_ref)], p_ref, p_buf, p_sem)

    io.send(mixed_ref)
    io.wait("late")
    out_first = jnp.concatenate([w_out(w0_ref), w_out(w1_ref)], axis=0)
    out_second = jnp.concatenate([w_out(w2_ref), w_out(w3_ref)], axis=0)

    def tile(i, carry):
        rows = rows_of(i)
        branch = dot(mixed_first_ref[rows, :], out_first) + dot(mixed_ref[rows, :], out_second)
        second = xq_ref[rows, :].astype(f32) + branch
        second_ref[rows, :] = second
        io.send(second_ref, rows)
        ncross_ref[rows, :] = layer_norm(second, norms_ref[4:5], norms_ref[5:6]).astype(bf16)
        io.send(ncross_ref, rows)
        return carry

    lax.fori_loop(0, TILES, tile, 0)


def cross_forward(
    meta, io, second_ref, ncross_ref, memory_ref, norms_ref, w0_ref, w1_ref, w2_ref, w3_ref,
    qa_ref, ka_ref, va_ref, ma_ref, qb_ref, kb_ref, vb_ref, mb_ref, p_ref, third_ref, nffn_ref, p_buf, p_sem,
):
    halves = ((qa_ref, ka_ref, va_ref, ma_ref), (qb_ref, kb_ref, vb_ref, mb_ref))
    weights = (w0_ref, w1_ref, w2_ref, w3_ref)

    wq = lanes([w_query(w) for w in weights])
    wk = lanes([w_key(w) for w in weights])
    wv = lanes([w_value(w) for w in weights])

    def tile(i, carry):
        rows = rows_of(i)
        io.wait_rows(i)
        memory = memory_ref[rows, :]
        q = (dot(ncross_ref[rows, :], wq) * (HEAD_DIM**-0.5)).astype(bf16)
        k = dot(memory, wk).astype(bf16)
        v = dot(memory, wv).astype(bf16)
        for n, (q_ref, k_ref, v_ref, _) in enumerate(halves):
            cols = slice(256 * n, 256 * n + 256)
            q_ref[rows, :] = q[:, cols]
            k_ref[rows, :] = k[:, cols]
            v_ref[rows, :] = v[:, cols]
        return carry

    lax.fori_loop(0, TILES, tile, 0)

    for half in halves:
        for ref in half[0:3]:
            io.send(ref)
    attend_docs(meta, True, None, None, halves, p_ref, p_buf, p_sem)

    io.send(ma_ref)
    io.send(mb_ref)
    io.wait("late")
    out_first = jnp.concatenate([w_out(w0_ref), w_out(w1_ref)], axis=0)
    out_second = jnp.concatenate([w_out(w2_ref), w_out(w3_ref)], axis=0)

    def tile(i, carry):
        rows = rows_of(i)
        branch = dot(ma_ref[rows, :], out_first) + dot(mb_ref[rows, :], out_second)
        third = second_ref[rows, :] + branch
        third_ref[rows, :] = third
        io.send(third_ref, rows)
        nffn_ref[rows, :] = layer_norm(third, norms_ref[6:7], norms_ref[7:8]).astype(bf16)
        io.send(nffn_ref, rows)
        return carry

    lax.fori_loop(0, TILES, tile, 0)


def ffn_both(
    meta, io, third_ref, nffn_ref, cot_ref, norms_ref, u0_ref, u1_ref, u2_ref, u3_ref,
    w0_ref, w1_ref, w2_ref, w3_ref,
    placed_ref, out_ref, g3_ref, g3_low_ref, gln_ref, own_ref, other_ref, hidden_ref, before_ref,
):
    gln_ref[...] = jnp.zeros_like(gln_ref)
    in_refs = (u0_ref, u1_ref, u2_ref, u3_ref)

    def tile(i, carry):
        rows = rows_of(i)
        io.wait_rows(i)
        nffn = nffn_ref[rows, :]
        cot = cot_ref[rows, :]
        outs = []
        grads = []
        for g, w_ref in enumerate((w0_ref, w1_ref, w2_ref, w3_ref)):
            w_in = in_refs[g][...]
            w_out_rows = w_ref[...]
            x = dot(nffn, w_in)
            square = x * x
            half = 0.5 + 0.5 * jnp.tanh(x * (gelu_root + (gelu_root * gelu_cube) * square))
            value = x * half
            hidden = value.astype(bf16)
            rise = 2.0 * gelu_root + (6.0 * gelu_root * gelu_cube) * square
            slope = half + value * (1.0 - half) * rise
            grad_before = (dot_nt(cot, w_out_rows) * slope).astype(bf16)
            outs.append(dot(hidden, w_out_rows))
            grads.append(dot_nt(grad_before, w_in))
            if g < 2:
                hidden_ref[rows, 512 * g : 512 * g + 512] = hidden
                before_ref[rows, 512 * g : 512 * g + 512] = grad_before
        third = third_ref[rows, :]
        result = (third + ((outs[0] + outs[1]) + (outs[2] + outs[3]))).astype(bf16)
        out_ref[rows, :] = result
        placed_ref[rows, :] = result
        grad_normed = (grads[0] + grads[1]) + (grads[2] + grads[3])
        grad_norm, grad_gain, grad_shift = norm_backward(third, norms_ref[6:7], grad_normed)
        g3 = cot.astype(f32) + grad_norm
        g3_ref[rows, :] = g3
        g3_low_ref[rows, :] = g3.astype(bf16)
        gln_ref[0:1, :] += grad_gain
        gln_ref[1:2, :] += grad_shift
        for ref in (out_ref, placed_ref, g3_ref, g3_low_ref):
            io.send(ref, rows)
        return carry

    lax.fori_loop(0, TILES, tile, 0)
    part = dot_tn(nffn_ref[...], before_ref[...])
    own_ref[0:512, :] = part[:, 0:512]
    other_ref[0:512, :] = part[:, 512:1024].astype(bf16)
    io.send(own_ref, pl.ds(0, 512))
    io.send(other_ref, pl.ds(0, 512))
    part = dot_tn(hidden_ref[...], cot_ref[...])
    own_ref[512:1024, :] = part[0:512]
    other_ref[512:1024, :] = part[512:1024].astype(bf16)
    io.send(own_ref, pl.ds(512, 512))
    io.send(other_ref, pl.ds(512, 512))


def back_start(io, g_ref, mixed_ref, w_refs, dm_ref, dq_ref, dk_ref, dv_ref):
    out_rows = jnp.concatenate([w_out(w) for w in w_refs], axis=0)

    def tile(i, carry):
        rows = rows_of(i)
        io.wait_rows(i)
        dm_ref[rows, :] = dot_nt(g_ref[rows, :], out_rows).astype(bf16)
        zeros = jnp.zeros((TILE, 256), f32)
        dq_ref[rows, :] = zeros
        dk_ref[rows, :] = zeros
        dv_ref[rows, :] = zeros
        return carry

    lax.fori_loop(0, TILES, tile, 0)


def attention_back_first(
    cross, meta, io, g_ref, nq_ref, nkv_ref, rank_row_ref, limit_ref, w0_ref, w1_ref,
    q_ref, k_ref, v_ref, mixed_ref, p_ref,
    dq_ref, dk_ref, dv_ref, own_ref, other_ref,
    rank_ref, dm_ref, dqs_ref, dks_ref, dvs_ref, p_buf, p_sem,
):
    load = (p_ref, p_buf, p_sem, 0)
    start_load(meta, cross, load)
    if not cross:
        spread_ranks(rank_row_ref, rank_ref)
    back_start(io, g_ref, mixed_ref, (w0_ref, w1_ref), dm_ref, dqs_ref, dks_ref, dvs_ref)

    io.wait("soon")
    attend_docs_back(
        meta, cross, None if cross else rank_ref, limit_ref, q_ref, k_ref, v_ref, mixed_ref,
        dm_ref, dqs_ref, dks_ref, dvs_ref, load,
    )

    dq_ref[...] = dqs_ref[...].astype(bf16)
    dk_ref[...] = dks_ref[...].astype(bf16)
    dv_ref[...] = dvs_ref[...].astype(bf16)
    for ref in (dq_ref, dk_ref, dv_ref):
        io.send(ref)
    io.wait("late")
    nq = nq_ref[...]
    nkv = nkv_ref[...]
    for n, part in enumerate(
        (dot_tn(nq, dq_ref[...]), dot_tn(nkv, dk_ref[...]), dot_tn(nkv, dv_ref[...]))
    ):
        own_ref[:, 128 * n : 128 * n + 128] = part[:, :128]
        other_ref[:, 128 * n : 128 * n + 128] = part[:, 128:].astype(bf16)
    part = dot_tn(mixed_ref[...], g_ref[...])
    for j in range(4):
        rows = slice(128 * j, 128 * j + 128)
        own_ref[rows, 384:512] = part[:128, rows]
        other_ref[rows, 384:512] = part[128:, rows].astype(bf16)


def back_second_docs(
    cross, meta, io, g_ref, rank_row_ref, limit_ref, w_refs, q_ref, k_ref, v_ref, mixed_ref, p_ref,
    rank_ref, dm_ref, dqs_ref, dks_ref, dvs_ref, p_buf, p_sem,
):
    load = (p_ref, p_buf, p_sem, 4 if cross else 0)
    start_load(meta, cross, load)
    if not cross:
        spread_ranks(rank_row_ref, rank_ref)
    back_start(io, g_ref, mixed_ref, w_refs, dm_ref, dqs_ref, dks_ref, dvs_ref)

    io.wait("soon")
    attend_docs_back(
        meta, cross, None if cross else rank_ref, limit_ref, q_ref, k_ref, v_ref, mixed_ref,
        dm_ref, dqs_ref, dks_ref, dvs_ref, load,
    )


def stream_grads(rows, first, second, firsts, seconds):
    dq, dk, dv = first
    dq2, dk2, dv2 = (ref[rows, :].astype(bf16) for ref in second)
    w0, w1 = firsts
    w2, w3 = seconds
    grad_q = dot_nt(dq[rows, :], lanes([w_query(w0), w_query(w1)])) + dot_nt(
        dq2, lanes([w_query(w2), w_query(w3)])
    )
    kv = lanes([dk[rows, :], dv[rows, :]])
    kv2 = lanes([dk2, dv2])
    grad_kv = dot_nt(kv, lanes([w_key(w0), w_key(w1), w_value(w0), w_value(w1)])) + dot_nt(
        kv2, lanes([w_key(w2), w_key(w3), w_value(w2), w_value(w3)])
    )
    return grad_q, grad_kv


def cross_back_second(
    meta, io, g_low_ref, g_ref, second_ref, norms_ref, w0_ref, w1_ref, w2_ref, w3_ref,
    dq_ref, dk_ref, dv_ref, q_ref, k_ref, v_ref, mixed_ref, p_ref,
    g2_ref, g2_low_ref, placed_ref, gmem_ref, gln_ref,
    dm_ref, dqs_ref, dks_ref, dvs_ref, p_buf, p_sem,
):
    back_second_docs(
        True, meta, io, g_low_ref, None, None, (w2_ref, w3_ref), q_ref, k_ref, v_ref, mixed_ref, p_ref,
        None, dm_ref, dqs_ref, dks_ref, dvs_ref, p_buf, p_sem,
    )

    io.wait("late")
    gln_ref[...] = jnp.zeros_like(gln_ref)

    def tile(i, carry):
        rows = rows_of(i)
        grad_q, grad_kv = stream_grads(
            rows,
            (dq_ref, dk_ref, dv_ref),
            (dqs_ref, dks_ref, dvs_ref),
            (w0_ref, w1_ref),
            (w2_ref, w3_ref),
        )
        low_kv = grad_kv.astype(bf16)
        gmem_ref[rows, :] = low_kv
        placed_ref[rows, :] = low_kv.astype(f32)
        io.send(gmem_ref, rows)
        io.send(placed_ref, rows)
        grad_norm, grad_gain, grad_shift = norm_backward(
            second_ref[rows, :], norms_ref[4:5], grad_q
        )
        g2 = g_ref[rows, :] + grad_norm
        g2_ref[rows, :] = g2
        g2_low_ref[rows, :] = g2.astype(bf16)
        io.send(g2_ref, rows)
        io.send(g2_low_ref, rows)
        gln_ref[0:1, :] += grad_gain
        gln_ref[1:2, :] += grad_shift
        return carry

    lax.fori_loop(0, TILES, tile, 0)


def self_back_second(
    meta, io, g_low_ref, rank_row_ref, limit_ref, w2_ref, w3_ref,
    q_ref, k_ref, v_ref, mixed_ref, p_ref,
    dq_ref, dk_ref, dv_ref,
    rank_ref, dm_ref, dqs_ref, dks_ref, dvs_ref, p_buf, p_sem,
):
    back_second_docs(
        False, meta, io, g_low_ref, rank_row_ref, limit_ref, (w2_ref, w3_ref), q_ref, k_ref, v_ref,
        mixed_ref, p_ref, rank_ref, dm_ref, dqs_ref, dks_ref, dvs_ref, p_buf, p_sem,
    )
    dq_ref[...] = dqs_ref[...].astype(bf16)
    dk_ref[...] = dks_ref[...].astype(bf16)
    dv_ref[...] = dvs_ref[...].astype(bf16)


def self_back_finish(
    meta, io, g_ref, xq_ref, xc_ref, norms_ref, w0_ref, w1_ref, w2_ref, w3_ref,
    dq_ref, dk_ref, dv_ref, dq2_ref, dk2_ref, dv2_ref,
    placed_q_ref, placed_c_ref, gq_ref, gc_ref, gln_ref,
):
    gln_ref[...] = jnp.zeros_like(gln_ref)

    def tile(i, carry):
        rows = rows_of(i)
        io.wait_rows(i)
        grad_q, grad_kv = stream_grads(
            rows,
            (dq_ref, dk_ref, dv_ref),
            (dq2_ref, dk2_ref, dv2_ref),
            (w0_ref, w1_ref),
            (w2_ref, w3_ref),
        )
        grad_norm, grad_gain, grad_shift = norm_backward(
            xq_ref[rows, :].astype(f32), norms_ref[0:1], grad_q
        )
        low_q = (g_ref[rows, :] + grad_norm).astype(bf16)
        gq_ref[rows, :] = low_q
        placed_q_ref[rows, :] = low_q.astype(f32)
        io.send(gq_ref, rows)
        io.send(placed_q_ref, rows)
        gln_ref[0:1, :] += grad_gain
        gln_ref[1:2, :] += grad_shift
        grad_norm, grad_gain, grad_shift = norm_backward(
            xc_ref[rows, :].astype(f32), norms_ref[2:3], grad_kv
        )
        low_c = grad_norm.astype(bf16)
        gc_ref[rows, :] = low_c
        placed_c_ref[rows, :] = low_c.astype(f32)
        io.send(gc_ref, rows)
        io.send(placed_c_ref, rows)
        gln_ref[2:3, :] += grad_gain
        gln_ref[3:4, :] += grad_shift
        return carry

    lax.fori_loop(0, TILES, tile, 0)


def place_rows(meta, *refs):
    count = len(refs) // 3
    for n in range(count):
        refs[2 * count + n][...] = refs[n][...].astype(refs[2 * count + n].dtype)


GROUP = 8


def position(meta):
    r = meta[35]
    return lax.rem(r, 2), r // 2


def join(own, other, rows):
    return (own[rows, :] + other[rows, :].astype(f32)).astype(bf16)


def join_halves(meta, own, other, keep, send):
    y, _ = position(meta)
    size = keep.shape[0]
    keep[...] = join(own, other, rows_of(y, size))
    send[...] = join(own, other, rows_of(1 - y, size))


def join_chunks(meta, kept, arrived, keep, sends):
    _, z = position(meta)
    size = keep.shape[0]
    keep[...] = join(kept, arrived, rows_of(z, size))
    for s, (send, first) in enumerate(sends, 1):
        send[first : first + size, :] = join(kept, arrived, rows_of(z ^ s, size))


def add_up(kept, parts, first):
    size = kept.shape[0]
    total = kept[...].astype(f32)
    for part in parts:
        total = total + part[first : first + size, :].astype(f32)
    return total.astype(bf16)


def half_of(meta, total, parts, first, half):
    _, z = position(meta)
    size = total.shape[0]
    half[rows_of(z, size), :] = total[...]
    for s, part in enumerate(parts, 1):
        half[rows_of(z ^ s, size), :] = part[first : first + size, :]


def slot_0(meta, ffn_own, ffn_other, keep, send):
    join_halves(meta, ffn_own, ffn_other, keep, send)


def slot_1(meta, ffn_kept, ffn_arrived, keep, *sends):
    join_chunks(meta, ffn_kept, ffn_arrived, keep, [(send, 0) for send in sends])


def slot_2(meta, ffn_kept, f1, f2, f3, cross_own, cross_other, ffn_total, keep, send):
    ffn_total[...] = add_up(ffn_kept, (f1, f2, f3), 0)
    join_halves(meta, cross_own, cross_other, keep, send)


def slot_3(
    meta, ffn_total, f1, f2, f3, cross_kept, cross_arrived, self_own, self_other,
    ffn_half, cross_keep, c1, c2, c3, self_keep, self_send,
):
    join_halves(meta, self_own, self_other, self_keep, self_send)
    join_chunks(meta, cross_kept, cross_arrived, cross_keep, [(c1, 0), (c2, 0), (c3, 0)])
    half_of(meta, ffn_total, (f1, f2, f3), 0, ffn_half)


def slot_4(meta, cross_kept, c1, c2, c3, self_kept, self_arrived, cross_total, self_keep, *sends):
    join_chunks(meta, self_kept, self_arrived, self_keep, [(send, 0) for send in sends])
    total = add_up(cross_kept, (c1, c2, c3), 0)
    cross_total[...] = total
    size = total.shape[0]
    for send in sends:
        send[size:, :] = total


def slot_5(meta, self_kept, cross_total, m1, m2, m3, gln_own, gln_other, send, cross_half):
    size = self_kept.shape[0]
    total = add_up(self_kept, (m1, m2, m3), 0)
    gln = gln_own[...] + gln_other[...]
    gln = jnp.concatenate([gln, jnp.zeros((8, D), f32)], axis=0).astype(bf16)
    for r in range(GROUP):
        send[r, 0:size, :] = total
        send[r, size : size + 16, :] = gln
    half_of(meta, cross_total, (m1, m2, m3), size, cross_half)


def unpack_attention(whole_ref, outs):
    for i in range(3):
        outs[i][...] = whole_ref[:, 128 * i : 128 * i + 128].astype(f32)
    for j in range(4):
        rows = slice(128 * j, 128 * j + 128)
        outs[3][:, rows] = whole_ref[rows, 384:512].astype(f32)


def unpack_early(meta, ffn_half, ffn_arrived, cross_half, cross_arrived, *refs):
    *outs, cross_whole, ffn_whole = refs
    y, _ = position(meta)
    cross_whole[rows_of(y, 256), :] = cross_half[...]
    cross_whole[rows_of(1 - y, 256), :] = cross_arrived[...]
    unpack_attention(cross_whole, outs[2:])
    ffn_whole[rows_of(y, 512), :] = ffn_half[...]
    ffn_whole[rows_of(1 - y, 512), :] = ffn_arrived[...]
    outs[0][...] = ffn_whole[0:512, :].astype(f32)
    outs[1][...] = ffn_whole[512:1024, :].astype(f32)


def unpack_late(meta, parts, *refs):
    *outs, gln, whole_ref = refs
    size = parts.shape[1] - 16
    total = parts[0, size : size + 16, :].astype(f32)
    for r in range(1, GROUP):
        total = total + parts[r, size : size + 16, :].astype(f32)
    gln[...] = total[0:8]
    for r in range(GROUP):
        first = size * (4 * (r % 2) + r // 2)
        whole_ref[first : first + size, :] = parts[r, 0:size, :]
    unpack_attention(whole_ref, outs)


def whole(shape):
    zeros = (0,) * len(shape)
    return pl.BlockSpec(shape, lambda d, meta: zeros)


def own_row(width):
    return pl.BlockSpec((SEQ, width), lambda d, meta: (meta[0], 0))


ANY = pl.BlockSpec(memory_space=pl.ANY)


def in_hbm(x):
    return pltpu.with_memory_space_constraint(x, pltpu.HBM)


def probability_out(heads):
    return (pltpu.HBM((DOCS, heads, FAST_K, FAST_Q), bf16), None, ANY)


def probability_scratch(heads):
    return [pltpu.VMEM((2, 2, heads, FAST_K, FAST_Q), bf16), pltpu.SemaphoreType.DMA((2,))]


class Copies:
    def __init__(self, meta):
        self.first = meta[0] * SEQ
        self.loads = {}
        self.tiles = []
        self.sends = []

    def load(self, stage, source, target, sems, own_row):
        if stage == "tiles":
            first = self.first if own_row else 0
            self.tiles.append((source, target, sems, first))
            return
        if own_row:
            source = source.at[pl.ds(pl.multiple_of(self.first, SEQ), SEQ)]
        copy = pltpu.make_async_copy(source, target, sems[0].at[sems[1], 0])
        self.loads.setdefault(stage, []).append(copy)

    def tile(self, entry, i):
        source, target, (sems, b), first = entry
        rows = pl.ds(pl.multiple_of(first + i * TILE, TILE), TILE)
        return pltpu.make_async_copy(source.at[rows], target.at[rows_of(i)], sems.at[b, i])

    def start(self):
        for copy in self.loads.get("now", []):
            copy.start()
        for i in range(TILES):
            for entry in self.tiles:
                self.tile(entry, i).start()
        for stage in ("soon", "late"):
            for copy in self.loads.get(stage, []):
                copy.start()

    def wait(self, stage):
        for copy in self.loads.pop(stage, []):
            copy.wait()

    def wait_rows(self, i):
        for entry in self.tiles:
            self.tile(entry, i).wait()

    def result(self, source, target, sem, own_row):
        self.sends.append([source, target, sem, own_row, False])

    def send(self, ref, rows=None):
        for entry in self.sends:
            source, target, sem, own_row, _ = entry
            if source is ref:
                entry[4] = True
                first = self.first if own_row else 0
                if rows is None:
                    size = source.shape[0]
                else:
                    source = source.at[rows]
                    first, size = first + rows.start, rows.size
                if rows is not None or own_row:
                    target = target.at[pl.ds(pl.multiple_of(first, size), size)]
                pltpu.make_async_copy(source, target, sem).start()

    def finish(self):
        for stage in list(self.loads):
            self.wait(stage)
        for source, _, _, _, started in self.sends:
            if not started:
                self.send(source)
        for source, target, sem, own_row, _ in self.sends:
            if own_row:
                target = target.at[pl.ds(pl.multiple_of(self.first, SEQ), SEQ)]
            pltpu.make_async_copy(source, target, sem).wait()


def out(shape, dtype, own_row=False):
    return (shape, dtype, own_row)


def call(kernel, name, operands, outs, scratch, flops, token=None):
    arrays = [operands[0][0]]
    in_specs, out_specs, out_shapes = [], [], []
    buffers = []
    loads = []
    for n, (x, how) in enumerate(operands[1:]):
        if isinstance(how, str):
            stage, _, row = how.partition("_")
            shape = ((SEQ,) + x.shape[1:]) if row else x.shape
            loads.append((n, stage, len(buffers), bool(row)))
            buffers.append(pltpu.VMEM(shape, x.dtype))
            arrays.append(in_hbm(x))
            in_specs.append(ANY)
        else:
            arrays.append(x)
            in_specs.append(how)
    results = []
    for n, (shape, dtype, how) in enumerate(outs):
        if isinstance(how, bool):
            results.append((n, len(buffers), how))
            buffers.append(pltpu.VMEM(shape, dtype))
            shape = ((2 * SEQ,) + shape[1:]) if how else shape
            out_shapes.append(pltpu.HBM(shape, dtype))
            out_specs.append(ANY)
        else:
            out_shapes.append(jax.ShapeDtypeStruct(shape, dtype) if dtype else shape)
            out_specs.append(how)
    n_in, n_out = len(in_specs), len(out_specs)
    if token is not None:
        arrays.append(token)
        in_specs.append(whole((8, 128)))
        out_specs.append(whole((8, 128)))
        out_shapes.append(jax.ShapeDtypeStruct((8, 128), f32))

    def body(meta, *refs):
        ins, refs = list(refs[:n_in]), refs[len(in_specs) - n_in + n_in :]
        results_out, refs = list(refs[:n_out]), refs[n_out:]
        if token is not None:
            token_out, refs = refs[0], refs[1:]
            token_out[...] = jnp.zeros_like(token_out)
        bufs, refs = refs[: len(buffers)], refs[len(buffers) :]
        rest = refs[: len(scratch)]
        copies = Copies(meta)
        if buffers:
            sems = refs[len(scratch)]
        for n, stage, b, row in loads:
            copies.load(stage, ins[n], bufs[b], (sems, b), row)
            ins[n] = bufs[b]
        for n, b, row in results:
            copies.result(bufs[b], results_out[n], sems.at[b, 0], row)
            results_out[n] = bufs[b]
        copies.start()
        copies.wait("now")
        if buffers:
            kernel(meta, copies, *ins, *results_out, *rest)
        else:
            kernel(meta, *ins, *results_out, *rest)
        copies.finish()

    moved = sum(x.size * x.dtype.itemsize for x in arrays[1:])
    sems = [pltpu.SemaphoreType.DMA((len(buffers), TILES))] if buffers else []
    return pl.pallas_call(
        body,
        name=name,
        grid_spec=pltpu.PrefetchScalarGridSpec(
            num_scalar_prefetch=1,
            grid=(1,),
            in_specs=in_specs,
            out_specs=out_specs,
            scratch_shapes=buffers + scratch + sems,
        ),
        out_shape=out_shapes,
        compiler_params=pltpu.CompilerParams(
            dimension_semantics=("arbitrary",), vmem_limit_bytes=50 * 1024 * 1024
        ),
        cost_estimate=pl.CostEstimate(
            flops=int(flops), bytes_accessed=int(moved), transcendentals=0
        ),
    )(*arrays)


def simple(kernel, name, meta, operands, outs, scratch=()):
    return pl.pallas_call(
        kernel,
        name=name,
        grid_spec=pltpu.PrefetchScalarGridSpec(
            num_scalar_prefetch=1,
            grid=(1,),
            in_specs=[whole(x.shape) for x in operands],
            out_specs=[whole(shape) for shape, _ in outs],
            scratch_shapes=scratch,
        ),
        out_shape=[jax.ShapeDtypeStruct(shape, dtype) for shape, dtype in outs],
        compiler_params=pltpu.CompilerParams(vmem_limit_bytes=16 * 1024 * 1024),
    )(meta, *operands)


def full(x):
    return (x, whole(x.shape))


def shards(
    query_stream,
    content_stream,
    memory,
    segment_ids,
    source_segments,
    context_rank,
    context_limit,
    padding,
    ln_query_gain,
    ln_query_bias,
    ln_content_gain,
    ln_content_bias,
    self_query,
    self_key,
    self_value,
    self_out,
    ln_cross_gain,
    ln_cross_bias,
    cross_query,
    cross_key,
    cross_value,
    cross_out,
    ln_ffn_gain,
    ln_ffn_bias,
    ffn_in,
    ffn_out,
    cotangent,
):
    core = lax.axis_index("heads") % 2

    def to_core(x):
        return lax.ppermute(x, "heads", [(h, h ^ 1) for h in range(4)])

    hold = lambda *xs: lax.optimization_barrier(xs)

    def to_chip(x):
        return lax.ppermute(x, "heads", [(h, h ^ 2) for h in range(4)])

    row = pl.BlockSpec((1, 8, 128), lambda d, core: (core[0], 0, 0))

    def token_row(x):
        return (in_hbm(x.reshape(2, 8, 128)), row)

    def fixed(x):
        zeros = (0,) * x.ndim
        return (in_hbm(x), pl.BlockSpec(x.shape, lambda d, core: zeros))

    prepared = [
        ((36,), jnp.int32, pl.BlockSpec(memory_space=pltpu.SMEM)),
        ((1, SEQ), f32, whole((1, SEQ))),
        ((1, SEQ), f32, whole((1, SEQ))),
        ((8, D), f32, whole((8, D))),
        ((2048, 128), bf16, whole((2048, 128))),
        ((2048, 128), bf16, whole((2048, 128))),
    ]
    gains = (
        ln_query_gain,
        ln_query_bias,
        ln_content_gain,
        ln_content_bias,
        ln_cross_gain,
        ln_cross_bias,
        ln_ffn_gain,
        ln_ffn_bias,
    )
    weights = (self_query, self_key, self_value, self_out)
    weights += (cross_query, cross_key, cross_value, cross_out)
    tokens = (segment_ids, source_segments, context_rank, context_limit, padding)
    meta, rank, limit, norms, ws0, wc0 = call(
        prepare,
        "prepare",
        [(jnp.stack([core, lax.axis_index("rows") % GROUP]).astype(jnp.int32), None)]
        + [token_row(x) for x in tokens]
        + [fixed(x.reshape(1, D)) for x in gains]
        + [fixed(x) for x in weights],
        prepared,
        [],
        0,
    )

    ws1 = to_core(ws0)
    ws2 = to_chip(ws0)
    wc2 = to_chip(wc0)
    u0, u2 = ffn_in, to_chip(ffn_in)
    wf0, wf2 = ffn_out, to_chip(ffn_out)
    meta_in = (meta, None)

    heads_out = [out((SEQ, 256), bf16)] * 4

    def stream_out(dtype, own_row=False):
        return out((SEQ, D), dtype, own_row)

    def now(*xs):
        return [(x, "now") for x in xs]

    def soon(*xs):
        return [(x, "soon") for x in xs]

    def late(*xs):
        return [(x, "late") for x in xs]

    def small(*xs):
        return [(x, whole(x.shape)) for x in xs]

    limits = pltpu.VMEM((SEQ, 128), f32)
    pair_flops = 2 * SEQ * D * 768 + 2 * 2 * 4 * DOCS * FAST_Q * FAST_K * 256

    nq, nc, *first, token = call(
        self_first,
        "self_first",
        [meta_in, (query_stream, "tiles_row"), (content_stream, "tiles_row")]
        + small(rank, limit, norms)
        + now(ws0, ws1),
        [stream_out(bf16), stream_out(bf16)] + heads_out + [probability_out(4)],
        [limits] + probability_scratch(4),
        pair_flops,
        jnp.zeros((8, 128), f32),
    )
    ws2, wc0, token = hold(ws2, wc0, token)
    ws3 = to_core(ws2)
    wc1 = to_core(wc0)
    *second_heads, second, ncross, token = call(
        self_second,
        "self_second",
        [meta_in, (query_stream, "late_row")]
        + [(nq, "tiles"), (nc, "tiles")]
        + small(rank, limit, norms)
        + late(ws0, ws1)
        + now(ws2, ws3)
        + late(first[3]),
        heads_out + [probability_out(4), stream_out(f32), stream_out(bf16)],
        [limits] + probability_scratch(4),
        pair_flops + 2 * SEQ * D * D,
        token,
    )
    wc2, u0, wf0, token = hold(wc2, u0, wf0, token)
    wc3 = to_core(wc2)
    u1 = to_core(u0)
    wf1 = to_core(wf0)
    *cross_heads, third, nffn, token = call(
        cross_forward,
        "cross_forward",
        [meta_in]
        + late(second)
        + [(ncross, "tiles"), (memory, "tiles_row")]
        + small(norms)
        + now(wc0, wc1, wc2, wc3),
        heads_out + heads_out + [probability_out(8), stream_out(f32), stream_out(bf16)],
        probability_scratch(8),
        2 * pair_flops + 2 * SEQ * D * D,
        token,
    )
    u2, wf2, token = hold(u2, wf2, token)
    u3 = to_core(u2)
    wf3 = to_core(wf2)
    grads_ln = ((8, D), f32, whole((8, D)))
    placed_output, output, g3, g3_low, gln_ffn, ffn_own, ffn_other, token = call(
        ffn_both,
        "ffn_both",
        [meta_in]
        + [(third, "tiles"), (nffn, "tiles"), (cotangent, "tiles_row")]
        + small(norms)
        + now(u0, u1, u2, u3, wf0, wf1, wf2, wf3),
        [
            stream_out(bf16, True),
            stream_out(bf16),
            stream_out(f32),
            stream_out(bf16),
            grads_ln,
            out((1024, D), f32),
            out((1024, D), bf16),
        ],
        [pltpu.VMEM((SEQ, 1024), bf16), pltpu.VMEM((SEQ, 1024), bf16)],
        12 * SEQ * D * 2048,
        token,
    )

    row_count = lax.axis_size("rows")
    assert row_count % GROUP == 0

    def along_rows(x, s):
        return lax.ppermute(x, "rows", [(r, r ^ s) for r in range(row_count)])

    def to_y(x):
        return along_rows(x, 1)

    def to_z(sends):
        return [along_rows(x, 2 * s) for s, x in enumerate(sends, 1)]

    def rows_out(*sizes):
        return [((n, D), bf16) for n in sizes]

    ffn_keep, ffn_send = simple(
        slot_0, "slot_0", meta, [ffn_own, to_core(ffn_other)], rows_out(512, 512)
    )
    token, ffn_send = hold(token, ffn_send)
    ffn_arrived = to_y(ffn_send)

    back_scratch = [pltpu.VMEM((SEQ, 256), bf16)] + [pltpu.VMEM((SEQ, 256), f32)] * 3
    back_scratch += probability_scratch(4)
    pair_out = out((SEQ, 256), bf16)
    packed_outs = [out((D, D), f32), out((D, D), bf16)]
    back_flops = 2 * SEQ * D * 256 + 4 * 2 * 4 * DOCS * FAST_Q * FAST_K * 256

    def head_inputs(natural, p):
        return soon(*natural) + [(in_hbm(p), ANY)]

    *cross_grads, cross_own, cross_other, token = call(
        functools.partial(attention_back_first, True),
        "cross_back_first",
        [meta_in]
        + [(g3_low, "tiles")]
        + late(ncross)
        + [(memory, "late_row")]
        + small(rank, limit)
        + now(wc0, wc1)
        + head_inputs(cross_heads[0:4], cross_heads[8]),
        [pair_out] * 3 + packed_outs,
        [limits] + back_scratch,
        back_flops + 2 * SEQ * D * 1024,
        token,
    )
    ffn_arrived, token = hold(ffn_arrived, token)
    ffn_keep, *sends = simple(
        slot_1, "slot_1", meta, [ffn_keep, ffn_arrived], rows_out(128, 128, 128, 128)
    )
    ffn_keep, token = hold(ffn_keep, token)
    ffn_parts = to_z(sends)
    cross_other = to_core(cross_other)
    g2, g2_low, placed_mem, grad_mem, gln_cross, token = call(
        cross_back_second,
        "cross_back_second",
        [meta_in]
        + [(g3_low, "tiles")]
        + late(g3, second)
        + small(norms)
        + late(wc0, wc1)
        + now(wc2, wc3)
        + late(*cross_grads)
        + head_inputs(cross_heads[4:8], cross_heads[8]),
        [stream_out(f32), stream_out(bf16), stream_out(f32, True), stream_out(bf16), grads_ln],
        back_scratch,
        back_flops + 2 * SEQ * D * 1536,
        token,
    )
    *ffn_parts, cross_other, token = hold(*ffn_parts, cross_other, token)
    ffn_total, cross_keep, cross_send = simple(
        slot_2,
        "slot_2",
        meta,
        [ffn_keep, *ffn_parts, cross_own, cross_other],
        rows_out(128, 256, 256),
    )
    ffn_total, cross_send, token = hold(ffn_total, cross_send, token)
    ffn_parts = to_z([ffn_total] * 3)
    cross_arrived = to_y(cross_send)

    *self_grads, self_own, self_other, token = call(
        functools.partial(attention_back_first, False),
        "self_back_first",
        [meta_in]
        + [(g2_low, "tiles")]
        + late(nq, nc)
        + small(rank, limit)
        + now(ws0, ws1)
        + head_inputs(first[0:4], first[4]),
        [pair_out] * 3 + packed_outs,
        [limits] + back_scratch,
        back_flops + 2 * SEQ * D * 1024,
        token,
    )
    *ffn_parts, cross_arrived, self_other, token = hold(
        *ffn_parts, cross_arrived, self_other, token
    )
    self_other = to_core(self_other)
    ffn_half, cross_keep, *sends, self_keep, self_send = simple(
        slot_3,
        "slot_3",
        meta,
        [ffn_total, *ffn_parts, cross_keep, cross_arrived, self_own, self_other],
        rows_out(512, 64, 64, 64, 64, 256, 256),
    )
    ffn_half, self_send, token = hold(ffn_half, self_send, token)
    self_arrived = to_y(self_send)
    cross_parts = to_z(sends)
    ffn_arrived = to_y(ffn_half)
    *self_grads_second, token = call(
        self_back_second,
        "self_back_second",
        [meta_in, (g2_low, "tiles")]
        + small(rank, limit)
        + now(ws2, ws3)
        + head_inputs(second_heads[0:4], second_heads[4]),
        [pair_out] * 3,
        [limits] + back_scratch,
        back_flops,
        token,
    )
    *cross_parts, self_arrived, token = hold(*cross_parts, self_arrived, token)
    cross_total, self_keep, *sends = simple(
        slot_4,
        "slot_4",
        meta,
        [cross_keep, *cross_parts, self_keep, self_arrived],
        rows_out(64, 64, 128, 128, 128),
    )
    cross_total, token = hold(cross_total, token)
    messages = to_z(sends)
    placed_q, placed_c, gq, gc, gln_self, token = call(
        self_back_finish,
        "self_back_finish",
        [meta_in, (g2, "tiles"), (query_stream, "tiles_row"), (content_stream, "tiles_row")]
        + small(norms)
        + now(ws0, ws1, ws2, ws3)
        + [(x, "tiles") for x in self_grads + self_grads_second],
        [stream_out(f32, True), stream_out(f32, True), stream_out(bf16), stream_out(bf16), grads_ln],
        [],
        2 * SEQ * D * 1536,
        token,
    )
    gln = jnp.concatenate([gln_self[0:4], gln_cross[0:2], gln_ffn[0:2]], axis=0)
    *messages, gln = hold(*messages, gln)
    last_send, cross_half = simple(
        slot_5,
        "slot_5",
        meta,
        [self_keep, cross_total, *messages, gln, to_core(gln)],
        [((GROUP, 80, D), bf16), ((256, D), bf16)],
    )
    output, grad_mem, last_send = hold(output, grad_mem, last_send)
    groups = None
    if row_count > GROUP:
        groups = [list(range(r, r + GROUP)) for r in range(0, row_count, GROUP)]
    last_parts = lax.all_to_all(last_send, "rows", 0, 0, axis_index_groups=groups)
    cross_arrived = to_y(cross_half)

    def over_groups(totals):
        if row_count == GROUP:
            return totals
        groups = [list(range(r, row_count, GROUP)) for r in range(GROUP)]
        return lax.psum(totals, "rows", axis_index_groups=groups)

    def both_rows(placed_own, arrays, name):
        count = len(arrays)
        size = SEQ // 2
        one = pl.BlockSpec((size, D), lambda i, meta: (i, 0))
        block = pl.BlockSpec((size, D), lambda i, meta: (2 * (1 - meta[0]) + i, 0))
        return pl.pallas_call(
            place_rows,
            name=name,
            grid_spec=pltpu.PrefetchScalarGridSpec(
                num_scalar_prefetch=1,
                grid=(2,),
                in_specs=[one] * count + [pl.BlockSpec(memory_space=pl.ANY)] * count,
                out_specs=[block] * count,
            ),
            out_shape=[jax.ShapeDtypeStruct(x.shape, x.dtype) for x in placed_own],
            input_output_aliases={1 + count + n: n for n in range(count)},
        )(meta, *[to_core(x) for x in arrays], *placed_own)

    out_both, grad_mem_both = both_rows([placed_output, placed_mem], [output, grad_mem], "place_early")
    gq_both, gc_both = both_rows([placed_q, placed_c], [gq, gc], "place_late")

    attention_outs = [((512, 128), f32)] * 3 + [((128, 512), f32)]
    grad_ffn_in, grad_ffn_out, *grad_cross_parts = simple(
        unpack_early,
        "unpack_early",
        meta,
        [ffn_half, ffn_arrived, cross_half, cross_arrived],
        [((D, D), f32)] * 2 + attention_outs,
        [pltpu.VMEM((D, D), bf16), pltpu.VMEM((2 * D, D), bf16)],
    )
    *grad_self_parts, gln = simple(
        unpack_late,
        "unpack_late",
        meta,
        [last_parts],
        attention_outs + [((8, D), f32)],
        [pltpu.VMEM((D, D), bf16)],
    )
    grad_ffn_in, grad_ffn_out, grad_cross_parts, grad_self_parts, gln = over_groups(
        (grad_ffn_in, grad_ffn_out, grad_cross_parts, grad_self_parts, gln)
    )
    return (
        out_both,
        gq_both,
        gc_both,
        grad_mem_both,
        gln[0],
        gln[1],
        gln[2],
        gln[3],
        *grad_self_parts,
        gln[4],
        gln[5],
        *grad_cross_parts,
        gln[6],
        gln[7],
        grad_ffn_in,
        grad_ffn_out,
    )


def solution(mesh):
    assert mesh.shape["heads"] == 4
    row_spec = P("rows", None)
    flat = P("rows")
    by_column = P(None, "heads")
    by_row = P("heads", None)
    attention = (by_column, by_column, by_column, by_row)
    in_specs = (
        (row_spec,) * 3
        + (flat,) * 5
        + (P(),) * 4
        + attention
        + (P(),) * 2
        + attention
        + (P(),) * 2
        + (by_column, by_row, row_spec)
    )
    out_specs = (
        (row_spec,) * 4
        + (P(),) * 4
        + attention
        + (P(),) * 2
        + attention
        + (P(),) * 2
        + (by_column, by_row)
    )
    return jax.shard_map(shards, mesh=mesh, in_specs=in_specs, out_specs=out_specs, check_vma=False)
```

```python
import functools

import jax
import jax.numpy as jnp
from jax import lax
from jax.experimental import pallas as pl
from jax.experimental.pallas import tpu as pltpu
from jax.sharding import PartitionSpec as P

HEAD_DIM = 64
SEQ = 1024
DOCS = 8
D = 512
TILE = 256
TILES = SEQ // TILE
FAST_Q = 256
FAST_K = 208
LONG_Q = 128
LONG_K = 640

norm_eps = 1e-05
masked_score = -1e30
hidden_rank = 1e6
gelu_root = 0.7978845608028654
gelu_cube = 0.044715

f32 = jnp.float32
bf16 = jnp.bfloat16


def dot(a, b):
    return lax.dot_general(a, b, (((1,), (0,)), ((), ())), preferred_element_type=f32)


def dot_nt(a, b):
    return lax.dot_general(a, b, (((1,), (1,)), ((), ())), preferred_element_type=f32)


def dot_tn(a, b):
    return lax.dot_general(a, b, (((0,), (0,)), ((), ())), preferred_element_type=f32)


def lanes(parts):
    return jnp.concatenate(parts, axis=1)


def layer_norm(values, gain, shift):
    centre = values - jnp.mean(values, axis=-1, keepdims=True)
    spread = jnp.mean(centre * centre, axis=-1, keepdims=True)
    return centre * lax.rsqrt(spread + norm_eps) * gain + shift


def norm_backward(values, gain, grad):
    centre = values - jnp.mean(values, axis=-1, keepdims=True)
    spread = jnp.mean(centre * centre, axis=-1, keepdims=True)
    scale = lax.rsqrt(spread + norm_eps)
    xhat = centre * scale
    eg = grad * gain
    mean_eg = jnp.mean(eg, axis=-1, keepdims=True)
    mean_egx = jnp.mean(eg * xhat, axis=-1, keepdims=True)
    grad_gain = jnp.sum(grad * xhat, axis=0, keepdims=True)
    grad_shift = jnp.sum(grad, axis=0, keepdims=True)
    return scale * (eg - mean_eg - xhat * mean_egx), grad_gain, grad_shift


def rows_of(i, size=TILE):
    return pl.ds(pl.multiple_of(i * size, size), size)


def w_query(ref):
    return ref[:, 0:128]


def w_key(ref):
    return ref[:, 128:256]


def w_value(ref):
    return ref[:, 256:384]


def w_out(ref):
    return lanes([ref[128 * j : 128 * j + 128, 384:512] for j in range(4)])


def half_masks():
    place = lax.broadcasted_iota(jnp.int32, (1, 128), 1)
    low = jnp.where(place < HEAD_DIM, 1.0, 0.0).astype(f32)
    return (low.astype(bf16), (1.0 - low).astype(bf16))


def doc_bounds(meta, d, source):
    base = 17 if source else 1
    return meta[base + d], meta[base + 8 + d]


def window_of(first, limit):
    return pl.multiple_of(jnp.minimum((first // 16) * 16, limit), 16)


def key_bias(ks, ke, k0, width):
    place = k0 + lax.broadcasted_iota(jnp.int32, (width, 128), 0)
    return jnp.where((place >= ks) & (place < ke), 0.0, masked_score)


def make_bias(rank_ref, limit_ref, ks, ke, q0, k0, span, width):
    if rank_ref is None:
        return lanes([key_bias(ks, ke, k0, width)] * (span // 128))
    place = k0 + lax.broadcasted_iota(jnp.int32, (width, 128), 0)
    ranks = rank_ref[pl.ds(k0, width), :]
    ranks = jnp.where((place < ks + 2) & (ranks < hidden_rank), -1.0, ranks)
    ranks = jnp.where((place >= ks) & (place < ke), ranks, hidden_rank)
    limits = jnp.broadcast_to(limit_ref[...], (8, SEQ))
    limits = pltpu.roll(limits, lax.rem(SEQ - q0, SEQ), 1)[0:1, 0:span]
    row = k0 + lax.broadcasted_iota(jnp.int32, (width, span), 0)
    column = q0 + lax.broadcasted_iota(jnp.int32, (width, span), 1)
    seen = (lanes([ranks] * (span // 128)) < limits) & (row != column)
    return jnp.where(seen, 0.0, masked_score)


STEPS = DOCS // 2


def is_fast(meta, cross):
    return meta[34 if cross else 33] == 1


def both_heads(x, masks):
    return jnp.concatenate([x * masks[0], x * masks[1]], axis=0)


def pair_probabilities(queries, keys, masks, bias):
    width = keys.shape[0]
    scores = dot_nt(both_heads(keys, masks), queries)
    result = []
    for a in range(2):
        part = scores[width * a : width * a + width] + bias
        part = jnp.exp(part - jnp.max(part, axis=0, keepdims=True))
        part = part * (1.0 / jnp.sum(part, axis=0, keepdims=True))
        result.append(part.astype(bf16))
    return result


def pair_product(rows, parts):
    across = jnp.transpose(rows)
    halves = [dot(across[64 * a : 64 * a + 64], part) for a, part in enumerate(parts)]
    return jnp.transpose(jnp.concatenate(halves, axis=0))


def for_docs(meta, cross, run, before, after):
    @pl.when(is_fast(meta, cross))
    def _():
        def step(i, carry):
            slot = lax.rem(i, 2)
            before(i, slot)
            for place in range(2):
                d = 2 * i + place
                ts, te = doc_bounds(meta, d, False)
                ks, ke = doc_bounds(meta, d, cross)
                q0 = window_of(ts, SEQ - FAST_Q)
                k0 = window_of(ks, SEQ - FAST_K)
                run(d, slot, place, q0, k0, FAST_Q, FAST_K, ts, te, ks, ke, True)
            after(i, slot)
            return carry

        lax.fori_loop(0, STEPS, step, 0)

    @pl.when(jnp.logical_not(is_fast(meta, cross)))
    def _():
        def doc(d, carry):
            ts, te = doc_bounds(meta, d, False)
            ks, ke = doc_bounds(meta, d, cross)
            base = (ts // 16) * 16
            k0 = window_of(ks, SEQ - LONG_K)

            def chunk(i, carry):
                lower = base + i * LONG_Q
                q0 = pl.multiple_of(jnp.minimum(lower, SEQ - LONG_Q), 16)
                low = jnp.maximum(ts, lower)
                high = jnp.minimum(te, lower + LONG_Q)
                run(d, None, None, q0, k0, LONG_Q, LONG_K, low, high, ks, ke, False)
                return carry

            return lax.fori_loop(0, (te - base + LONG_Q - 1) // LONG_Q, chunk, carry)

        lax.fori_loop(0, DOCS, doc, 0)


def attend_docs(meta, cross, rank_ref, limit_ref, halves, p_ref, p_buf, p_sem):
    pairs = 2 * len(halves)
    masks = half_masks()

    def save(i, slot):
        return pltpu.make_async_copy(p_buf.at[slot], p_ref.at[pl.ds(2 * i, 2)], p_sem.at[slot])

    def before(i, slot):
        @pl.when(i >= 2)
        def _():
            save(i - 2, slot).wait()

    def after(i, slot):
        save(i, slot).start()

    def run(d, slot, place, q0, k0, span, width, low, high, ks, ke, fast):
        bias = make_bias(rank_ref, limit_ref, ks, ke, q0, k0, span, width)
        row = q0 + lax.broadcasted_iota(jnp.int32, (span, 128), 0)
        inside = (row >= low) & (row < high)
        for n in range(pairs):
            q_ref, k_ref, v_ref, mixed_ref = halves[n // 2]
            cols = slice(128 * (n % 2), 128 * (n % 2) + 128)
            queries = q_ref[pl.ds(q0, span), cols]
            keys = k_ref[pl.ds(k0, width), cols]
            values = v_ref[pl.ds(k0, width), cols]
            parts = pair_probabilities(queries, keys, masks, bias)
            if fast:
                for a in range(2):
                    p_buf[slot, place, 2 * n + a] = parts[a]
            mixed = pair_product(values, parts)
            old = mixed_ref[pl.ds(q0, span), cols].astype(f32)
            mixed_ref[pl.ds(q0, span), cols] = jnp.where(inside, mixed, old).astype(bf16)

    for_docs(meta, cross, run, before, after)

    @pl.when(is_fast(meta, cross))
    def _():
        for i in range(STEPS - 2, STEPS):
            save(i, i % 2).wait()


def load_step(load, i, slot):
    p_ref, p_buf, p_sem = load
    return pltpu.make_async_copy(p_ref.at[pl.ds(2 * i, 2)], p_buf.at[slot], p_sem.at[slot])


def start_load(meta, cross, load):
    @pl.when(is_fast(meta, cross))
    def _():
        load_step(load, 0, 0).start()


def attend_docs_back(
    meta, cross, rank_ref, limit_ref, q_ref, k_ref, v_ref, mixed_ref, dm_ref,
    dq_ref, dk_ref, dv_ref, load,
):
    pairs = q_ref.shape[1] // 128
    masks = half_masks()
    p_buf = load[1]

    def before(i, slot):
        @pl.when(i + 1 < STEPS)
        def _():
            load_step(load, i + 1, 1 - slot).start()

        load_step(load, i, slot).wait()

    def after(i, slot):
        pass

    def run(d, slot, place, q0, k0, span, width, low, high, ks, ke, fast):
        row = q0 + lax.broadcasted_iota(jnp.int32, (span, 128), 0)
        inside = (row >= low) & (row < high)
        ones = jnp.ones((width, 128), bf16)
        if not fast:
            bias = make_bias(rank_ref, limit_ref, ks, ke, q0, k0, span, width)
        for n in range(pairs):
            cols = slice(128 * n, 128 * n + 128)
            queries = q_ref[pl.ds(q0, span), cols]
            keys = k_ref[pl.ds(k0, width), cols]
            values = v_ref[pl.ds(k0, width), cols]
            mixed = mixed_ref[pl.ds(q0, span), cols].astype(f32)
            grad = jnp.where(inside, dm_ref[pl.ds(q0, span), cols].astype(f32), 0.0)
            low_grad = grad.astype(bf16)
            left = lanes([low_grad, (-(grad * mixed)).astype(bf16)])
            delta = dot_nt(both_heads(lanes([values, ones]), [lanes([m, m]) for m in masks]), left)
            if fast:
                parts = [p_buf[slot, place, 2 * n + a] for a in range(2)]
            else:
                parts = pair_probabilities(queries, keys, masks, bias)
            slopes = []
            dk = dv = None
            for a in range(2):
                slope = parts[a].astype(f32) * delta[width * a : width * a + width]
                slopes.append(slope.astype(bf16))
                dk_a = dot(slopes[a], queries * masks[a])
                dv_a = dot(parts[a], low_grad * masks[a])
                dk = dk_a if dk is None else dk + dk_a
                dv = dv_a if dv is None else dv + dv_a
            dq = pair_product(keys, slopes)
            dq_ref[pl.ds(q0, span), cols] += dq * (HEAD_DIM**-0.5)
            dk_ref[pl.ds(k0, width), cols] += dk
            dv_ref[pl.ds(k0, width), cols] += dv

    for_docs(meta, cross, run, before, after)


def spread_ranks(rank_row_ref, rank_ref):
    rank_ref[...] = jnp.transpose(jnp.broadcast_to(rank_row_ref[...], (128, SEQ)))


def prepare(
    core, seg_ref, src_ref, rank_ref, limit_ref, pad_ref,
    n0, n1, n2, n3, n4, n5, n6, n7, sq, sk, sv, so, cq, ck, cv, co,
    meta_ref, ranks_ref, limits_ref, norms_ref, ws_ref, wc_ref,
):
    meta_ref[0] = core[0]
    meta_ref[35] = core[1]
    for base, ref in ((1, seg_ref), (17, src_ref)):
        ids = ref[0]
        meta_ref[base] = 0
        meta_ref[base + 15] = SEQ
        for d in range(1, DOCS):
            cut = jnp.sum(jnp.where(ids < d, 1.0, 0.0)).astype(jnp.int32)
            meta_ref[base + d] = cut
            meta_ref[base + 7 + d] = cut
    for place, base in ((33, 1), (34, 17)):
        fast = jnp.int32(1)
        for d in range(DOCS):
            q0 = window_of(meta_ref[1 + d], SEQ - FAST_Q)
            k0 = window_of(meta_ref[base + d], SEQ - FAST_K)
            fits = (meta_ref[9 + d] - q0 <= FAST_Q) & (meta_ref[base + 8 + d] - k0 <= FAST_K)
            fast = fast & fits.astype(jnp.int32)
        meta_ref[place] = fast
    ranks = jnp.where(pad_ref[0] != 0, hidden_rank, rank_ref[0].astype(f32))
    limits = limit_ref[0].astype(f32)
    for i in range(8):
        ranks_ref[0:1, 128 * i : 128 * i + 128] = ranks[i : i + 1]
        limits_ref[0:1, 128 * i : 128 * i + 128] = limits[i : i + 1]
    for i, ref in enumerate((n0, n1, n2, n3, n4, n5, n6, n7)):
        norms_ref[i : i + 1, :] = ref[...]
    for to, parts, out in ((ws_ref, (sq, sk, sv), so), (wc_ref, (cq, ck, cv), co)):
        for i, part in enumerate(parts):
            to[:, 128 * i : 128 * i + 128] = part[...]
        for j in range(4):
            to[128 * j : 128 * j + 128, 384:512] = out[:, 128 * j : 128 * j + 128]


def self_first(
    meta, io, xq_ref, xc_ref, rank_row_ref, limit_ref, norms_ref, w0_ref, w1_ref,
    nq_ref, nc_ref, q_ref, k_ref, v_ref, mixed_ref, p_ref, rank_ref, p_buf, p_sem,
):

    spread_ranks(rank_row_ref, rank_ref)
    wq = lanes([w_query(w0_ref), w_query(w1_ref)])
    wkv = lanes([w_key(w0_ref), w_key(w1_ref), w_value(w0_ref), w_value(w1_ref)])

    def tile(i, carry):
        rows = rows_of(i)
        io.wait_rows(i)
        nq = layer_norm(xq_ref[rows, :].astype(f32), norms_ref[0:1], norms_ref[1:2]).astype(bf16)
        nc = layer_norm(xc_ref[rows, :].astype(f32), norms_ref[2:3], norms_ref[3:4]).astype(bf16)
        nq_ref[rows, :] = nq
        nc_ref[rows, :] = nc
        q_ref[rows, :] = (dot(nq, wq) * (HEAD_DIM**-0.5)).astype(bf16)
        kv = dot(nc, wkv).astype(bf16)
        k_ref[rows, :] = kv[:, :256]
        v_ref[rows, :] = kv[:, 256:]
        return carry

    lax.fori_loop(0, TILES, tile, 0)

    for ref in (nq_ref, nc_ref, q_ref, k_ref, v_ref):
        io.send(ref)
    attend_docs(meta, False, rank_ref, limit_ref, [(q_ref, k_ref, v_ref, mixed_ref)], p_ref, p_buf, p_sem)


def self_second(
    meta, io, xq_ref, nq_ref, nc_ref, rank_row_ref, limit_ref, norms_ref, w0_ref, w1_ref, w2_ref, w3_ref,
    mixed_first_ref,
    q_ref, k_ref, v_ref, mixed_ref, p_ref, second_ref, ncross_ref, rank_ref, p_buf, p_sem,
):

    spread_ranks(rank_row_ref, rank_ref)
    wq = lanes([w_query(w2_ref), w_query(w3_ref)])
    wkv = lanes([w_key(w2_ref), w_key(w3_ref), w_value(w2_ref), w_value(w3_ref)])

    def tile(i, carry):
        rows = rows_of(i)
        io.wait_rows(i)
        q_ref[rows, :] = (dot(nq_ref[rows, :], wq) * (HEAD_DIM**-0.5)).astype(bf16)
        kv = dot(nc_ref[rows, :], wkv).astype(bf16)
        k_ref[rows, :] = kv[:, :256]
        v_ref[rows, :] = kv[:, 256:]
        return carry

    lax.fori_loop(0, TILES, tile, 0)

    for ref in (q_ref, k_ref, v_ref):
        io.send(ref)
    attend_docs(meta, False, rank_ref, limit_ref, [(q_ref, k_ref, v_ref, mixed_ref)], p_ref, p_buf, p_sem)

    io.send(mixed_ref)
    io.wait("late")
    out_first = jnp.concatenate([w_out(w0_ref), w_out(w1_ref)], axis=0)
    out_second = jnp.concatenate([w_out(w2_ref), w_out(w3_ref)], axis=0)

    def tile(i, carry):
        rows = rows_of(i)
        branch = dot(mixed_first_ref[rows, :], out_first) + dot(mixed_ref[rows, :], out_second)
        second = xq_ref[rows, :].astype(f32) + branch
        second_ref[rows, :] = second
        io.send(second_ref, rows)
        ncross_ref[rows, :] = layer_norm(second, norms_ref[4:5], norms_ref[5:6]).astype(bf16)
        io.send(ncross_ref, rows)
        return carry

    lax.fori_loop(0, TILES, tile, 0)


def project_cross(io, ncross_ref, memory_ref, weights, q_ref, k_ref, v_ref):
    wq = lanes([w_query(w) for w in weights])
    wkv = lanes([w_key(w) for w in weights] + [w_value(w) for w in weights])

    def tile(i, carry):
        rows = rows_of(i)
        io.wait_rows(i)
        q_ref[rows, :] = (dot(ncross_ref[rows, :], wq) * (HEAD_DIM**-0.5)).astype(bf16)
        kv = dot(memory_ref[rows, :], wkv).astype(bf16)
        k_ref[rows, :] = kv[:, :256]
        v_ref[rows, :] = kv[:, 256:]
        return carry

    lax.fori_loop(0, TILES, tile, 0)
    for ref in (q_ref, k_ref, v_ref):
        io.send(ref)


def cross_first(
    meta, io, ncross_ref, memory_ref, w0_ref, w1_ref,
    q_ref, k_ref, v_ref, mixed_ref, p_ref, p_buf, p_sem,
):
    project_cross(io, ncross_ref, memory_ref, (w0_ref, w1_ref), q_ref, k_ref, v_ref)
    attend_docs(meta, True, None, None, [(q_ref, k_ref, v_ref, mixed_ref)], p_ref, p_buf, p_sem)


def cross_second(
    meta, io, second_ref, ncross_ref, memory_ref, norms_ref, w0_ref, w1_ref, w2_ref, w3_ref,
    mixed_first_ref,
    q_ref, k_ref, v_ref, mixed_ref, p_ref, third_ref, nffn_ref, p_buf, p_sem,
):
    project_cross(io, ncross_ref, memory_ref, (w2_ref, w3_ref), q_ref, k_ref, v_ref)
    attend_docs(meta, True, None, None, [(q_ref, k_ref, v_ref, mixed_ref)], p_ref, p_buf, p_sem)
    io.send(mixed_ref)
    io.wait("late")
    out_first = jnp.concatenate([w_out(w0_ref), w_out(w1_ref)], axis=0)
    out_second = jnp.concatenate([w_out(w2_ref), w_out(w3_ref)], axis=0)

    def tile(i, carry):
        rows = rows_of(i)
        branch = dot(mixed_first_ref[rows, :], out_first) + dot(mixed_ref[rows, :], out_second)
        third = second_ref[rows, :] + branch
        third_ref[rows, :] = third
        io.send(third_ref, rows)
        nffn_ref[rows, :] = layer_norm(third, norms_ref[6:7], norms_ref[7:8]).astype(bf16)
        io.send(nffn_ref, rows)
        return carry

    lax.fori_loop(0, TILES, tile, 0)


def ffn_both(
    meta, io, third_ref, nffn_ref, cot_ref, norms_ref, u0_ref, u1_ref, u2_ref, u3_ref,
    w0_ref, w1_ref, w2_ref, w3_ref,
    placed_ref, out_ref, g3_ref, g3_low_ref, gln_ref, own_ref, other_ref, hidden_ref, before_ref,
):
    gln_ref[...] = jnp.zeros_like(gln_ref)
    in_refs = (u0_ref, u1_ref, u2_ref, u3_ref)

    def tile(i, carry):
        rows = rows_of(i)
        io.wait_rows(i)
        nffn = nffn_ref[rows, :]
        cot = cot_ref[rows, :]
        outs = []
        grads = []
        for g, w_ref in enumerate((w0_ref, w1_ref, w2_ref, w3_ref)):
            w_in = in_refs[g][...]
            w_out_rows = w_ref[...]
            x = dot(nffn, w_in)
            square = x * x
            half = 0.5 + 0.5 * jnp.tanh(x * (gelu_root + (gelu_root * gelu_cube) * square))
            value = x * half
            hidden = value.astype(bf16)
            rise = 2.0 * gelu_root + (6.0 * gelu_root * gelu_cube) * square
            slope = half + value * (1.0 - half) * rise
            grad_before = (dot_nt(cot, w_out_rows) * slope).astype(bf16)
            outs.append(dot(hidden, w_out_rows))
            grads.append(dot_nt(grad_before, w_in))
            if g < 2:
                hidden_ref[rows, 512 * g : 512 * g + 512] = hidden
                before_ref[rows, 512 * g : 512 * g + 512] = grad_before
        third = third_ref[rows, :]
        result = (third + ((outs[0] + outs[1]) + (outs[2] + outs[3]))).astype(bf16)
        out_ref[rows, :] = result
        placed_ref[rows, :] = result
        grad_normed = (grads[0] + grads[1]) + (grads[2] + grads[3])
        grad_norm, grad_gain, grad_shift = norm_backward(third, norms_ref[6:7], grad_normed)
        g3 = cot.astype(f32) + grad_norm
        g3_ref[rows, :] = g3
        g3_low_ref[rows, :] = g3.astype(bf16)
        gln_ref[0:1, :] += grad_gain
        gln_ref[1:2, :] += grad_shift
        for ref in (out_ref, placed_ref, g3_ref, g3_low_ref):
            io.send(ref, rows)
        return carry

    lax.fori_loop(0, TILES, tile, 0)
    part = dot_tn(nffn_ref[...], before_ref[...])
    own_ref[0:512, :] = part[:, 0:512].astype(bf16)
    other_ref[0:512, :] = part[:, 512:1024].astype(bf16)
    io.send(own_ref, pl.ds(0, 512))
    io.send(other_ref, pl.ds(0, 512))
    part = dot_tn(hidden_ref[...], cot_ref[...])
    own_ref[512:1024, :] = part[0:512].astype(bf16)
    other_ref[512:1024, :] = part[512:1024].astype(bf16)
    io.send(own_ref, pl.ds(512, 512))
    io.send(other_ref, pl.ds(512, 512))


def back_start(io, g_ref, mixed_ref, w_refs, dm_ref, dq_ref, dk_ref, dv_ref):
    out_rows = jnp.concatenate([w_out(w) for w in w_refs], axis=0)

    def tile(i, carry):
        rows = rows_of(i)
        io.wait_rows(i)
        dm_ref[rows, :] = dot_nt(g_ref[rows, :], out_rows).astype(bf16)
        zeros = jnp.zeros((TILE, 256), f32)
        dq_ref[rows, :] = zeros
        dk_ref[rows, :] = zeros
        dv_ref[rows, :] = zeros
        return carry

    lax.fori_loop(0, TILES, tile, 0)


def attention_back_first(
    cross, meta, io, g_ref, nq_ref, nkv_ref, rank_row_ref, limit_ref, w0_ref, w1_ref,
    q_ref, k_ref, v_ref, mixed_ref, p_ref,
    dq_ref, dk_ref, dv_ref, own_ref, other_ref,
    rank_ref, dm_ref, dqs_ref, dks_ref, dvs_ref, p_buf, p_sem,
):
    load = (p_ref, p_buf, p_sem)
    start_load(meta, cross, load)
    if not cross:
        spread_ranks(rank_row_ref, rank_ref)
    back_start(io, g_ref, mixed_ref, (w0_ref, w1_ref), dm_ref, dqs_ref, dks_ref, dvs_ref)

    io.wait("soon")
    attend_docs_back(
        meta, cross, None if cross else rank_ref, limit_ref, q_ref, k_ref, v_ref, mixed_ref,
        dm_ref, dqs_ref, dks_ref, dvs_ref, load,
    )

    dq_ref[...] = dqs_ref[...].astype(bf16)
    dk_ref[...] = dks_ref[...].astype(bf16)
    dv_ref[...] = dvs_ref[...].astype(bf16)
    for ref in (dq_ref, dk_ref, dv_ref):
        io.send(ref)
    io.wait("late")
    nq = nq_ref[...]
    nkv = nkv_ref[...]
    for n, part in enumerate(
        (dot_tn(nq, dq_ref[...]), dot_tn(nkv, dk_ref[...]), dot_tn(nkv, dv_ref[...]))
    ):
        own_ref[:, 128 * n : 128 * n + 128] = part[:, :128].astype(bf16)
        other_ref[:, 128 * n : 128 * n + 128] = part[:, 128:].astype(bf16)
    part = dot_tn(mixed_ref[...], g_ref[...])
    for j in range(4):
        rows = slice(128 * j, 128 * j + 128)
        own_ref[rows, 384:512] = part[:128, rows].astype(bf16)
        other_ref[rows, 384:512] = part[128:, rows].astype(bf16)


def back_second_docs(
    cross, meta, io, g_ref, rank_row_ref, limit_ref, w_refs, q_ref, k_ref, v_ref, mixed_ref, p_ref,
    rank_ref, dm_ref, dqs_ref, dks_ref, dvs_ref, p_buf, p_sem,
):
    load = (p_ref, p_buf, p_sem)
    start_load(meta, cross, load)
    if not cross:
        spread_ranks(rank_row_ref, rank_ref)
    back_start(io, g_ref, mixed_ref, w_refs, dm_ref, dqs_ref, dks_ref, dvs_ref)

    io.wait("soon")
    attend_docs_back(
        meta, cross, None if cross else rank_ref, limit_ref, q_ref, k_ref, v_ref, mixed_ref,
        dm_ref, dqs_ref, dks_ref, dvs_ref, load,
    )


def stream_grads(rows, first, second, firsts, seconds):
    dq, dk, dv = first
    dq2, dk2, dv2 = (ref[rows, :].astype(bf16) for ref in second)
    w0, w1 = firsts
    w2, w3 = seconds
    grad_q = dot_nt(dq[rows, :], lanes([w_query(w0), w_query(w1)])) + dot_nt(
        dq2, lanes([w_query(w2), w_query(w3)])
    )
    kv = lanes([dk[rows, :], dv[rows, :]])
    kv2 = lanes([dk2, dv2])
    grad_kv = dot_nt(kv, lanes([w_key(w0), w_key(w1), w_value(w0), w_value(w1)])) + dot_nt(
        kv2, lanes([w_key(w2), w_key(w3), w_value(w2), w_value(w3)])
    )
    return grad_q, grad_kv


def cross_back_second(
    meta, io, g_low_ref, g_ref, second_ref, norms_ref, w0_ref, w1_ref, w2_ref, w3_ref,
    dq_ref, dk_ref, dv_ref, q_ref, k_ref, v_ref, mixed_ref, p_ref,
    g2_ref, g2_low_ref, placed_ref, gmem_ref, gln_ref,
    dm_ref, dqs_ref, dks_ref, dvs_ref, p_buf, p_sem,
):
    back_second_docs(
        True, meta, io, g_low_ref, None, None, (w2_ref, w3_ref), q_ref, k_ref, v_ref, mixed_ref, p_ref,
        None, dm_ref, dqs_ref, dks_ref, dvs_ref, p_buf, p_sem,
    )

    io.wait("late")
    gln_ref[...] = jnp.zeros_like(gln_ref)

    def tile(i, carry):
        rows = rows_of(i)
        grad_q, grad_kv = stream_grads(
            rows,
            (dq_ref, dk_ref, dv_ref),
            (dqs_ref, dks_ref, dvs_ref),
            (w0_ref, w1_ref),
            (w2_ref, w3_ref),
        )
        low_kv = grad_kv.astype(bf16)
        gmem_ref[rows, :] = low_kv
        placed_ref[rows, :] = low_kv.astype(f32)
        io.send(gmem_ref, rows)
        io.send(placed_ref, rows)
        grad_norm, grad_gain, grad_shift = norm_backward(
            second_ref[rows, :], norms_ref[4:5], grad_q
        )
        g2 = g_ref[rows, :] + grad_norm
        g2_ref[rows, :] = g2
        g2_low_ref[rows, :] = g2.astype(bf16)
        io.send(g2_ref, rows)
        io.send(g2_low_ref, rows)
        gln_ref[0:1, :] += grad_gain
        gln_ref[1:2, :] += grad_shift
        return carry

    lax.fori_loop(0, TILES, tile, 0)


def self_back_second(
    meta, io, g_low_ref, rank_row_ref, limit_ref, w2_ref, w3_ref,
    q_ref, k_ref, v_ref, mixed_ref, p_ref,
    dq_ref, dk_ref, dv_ref,
    rank_ref, dm_ref, dqs_ref, dks_ref, dvs_ref, p_buf, p_sem,
):
    back_second_docs(
        False, meta, io, g_low_ref, rank_row_ref, limit_ref, (w2_ref, w3_ref), q_ref, k_ref, v_ref,
        mixed_ref, p_ref, rank_ref, dm_ref, dqs_ref, dks_ref, dvs_ref, p_buf, p_sem,
    )
    dq_ref[...] = dqs_ref[...].astype(bf16)
    dk_ref[...] = dks_ref[...].astype(bf16)
    dv_ref[...] = dvs_ref[...].astype(bf16)


def self_back_finish(
    meta, io, g_ref, xq_ref, xc_ref, norms_ref, w0_ref, w1_ref, w2_ref, w3_ref,
    dq_ref, dk_ref, dv_ref, dq2_ref, dk2_ref, dv2_ref,
    placed_q_ref, placed_c_ref, gq_ref, gc_ref, gln_ref,
):
    gln_ref[...] = jnp.zeros_like(gln_ref)

    def tile(i, carry):
        rows = rows_of(i)
        io.wait_rows(i)
        grad_q, grad_kv = stream_grads(
            rows,
            (dq_ref, dk_ref, dv_ref),
            (dq2_ref, dk2_ref, dv2_ref),
            (w0_ref, w1_ref),
            (w2_ref, w3_ref),
        )
        grad_norm, grad_gain, grad_shift = norm_backward(
            xq_ref[rows, :].astype(f32), norms_ref[0:1], grad_q
        )
        low_q = (g_ref[rows, :] + grad_norm).astype(bf16)
        gq_ref[rows, :] = low_q
        placed_q_ref[rows, :] = low_q.astype(f32)
        io.send(gq_ref, rows)
        io.send(placed_q_ref, rows)
        gln_ref[0:1, :] += grad_gain
        gln_ref[1:2, :] += grad_shift
        grad_norm, grad_gain, grad_shift = norm_backward(
            xc_ref[rows, :].astype(f32), norms_ref[2:3], grad_kv
        )
        low_c = grad_norm.astype(bf16)
        gc_ref[rows, :] = low_c
        placed_c_ref[rows, :] = low_c.astype(f32)
        io.send(gc_ref, rows)
        io.send(placed_c_ref, rows)
        gln_ref[2:3, :] += grad_gain
        gln_ref[3:4, :] += grad_shift
        return carry

    lax.fori_loop(0, TILES, tile, 0)


def place_rows(meta, *refs):
    count = len(refs) // 3
    for n in range(count):
        refs[2 * count + n][...] = refs[n][...].astype(refs[2 * count + n].dtype)


GROUP = 8


def position(meta):
    r = meta[35]
    return lax.rem(r, 2), r // 2


def join(own, other, rows):
    return (own[rows, :].astype(f32) + other[rows, :].astype(f32)).astype(bf16)


def join_halves(meta, own, other, keep, send):
    y, _ = position(meta)
    size = keep.shape[0]
    keep[...] = join(own, other, rows_of(y, size))
    send[...] = join(own, other, rows_of(1 - y, size))


def join_chunks(meta, kept, arrived, keep, sends):
    _, z = position(meta)
    size = keep.shape[0]
    keep[...] = join(kept, arrived, rows_of(z, size))
    for s, (send, first) in enumerate(sends, 1):
        send[first : first + size, :] = join(kept, arrived, rows_of(z ^ s, size))


def add_up(kept, parts, first):
    size = kept.shape[0]
    total = kept[...].astype(f32)
    for part in parts:
        total = total + part[first : first + size, :].astype(f32)
    return total.astype(bf16)


def half_of(meta, total, parts, first, half):
    _, z = position(meta)
    size = total.shape[0]
    half[rows_of(z, size), :] = total[...]
    for s, part in enumerate(parts, 1):
        half[rows_of(z ^ s, size), :] = part[first : first + size, :]


def slot_1(meta, ffn_own, ffn_other, keep, send):
    join_halves(meta, ffn_own, ffn_other, keep, send)


def slot_2(
    meta, ffn_kept, ffn_arrived, cross_own, cross_other, ffn_keep, f1, f2, f3, keep, send
):
    join_chunks(meta, ffn_kept, ffn_arrived, ffn_keep, [(f1, 0), (f2, 0), (f3, 0)])
    join_halves(meta, cross_own, cross_other, keep, send)


def slot_3(
    meta, ffn_kept, f1, f2, f3, cross_kept, cross_arrived, self_own, self_other,
    ffn_total, cross_keep, m1, m2, m3, self_keep, self_send,
):
    join_halves(meta, self_own, self_other, self_keep, self_send)
    total = add_up(ffn_kept, (f1, f2, f3), 0)
    ffn_total[...] = total
    size = total.shape[0]
    join_chunks(meta, cross_kept, cross_arrived, cross_keep, [(m, size) for m in (m1, m2, m3)])
    for m in (m1, m2, m3):
        m[0:size, :] = total


def slot_4(
    meta, ffn_total, m1, m2, m3, cross_kept, self_kept, self_arrived,
    ffn_half, cross_total, self_keep, *sends,
):
    join_chunks(meta, self_kept, self_arrived, self_keep, [(send, 0) for send in sends])
    total = add_up(cross_kept, (m1, m2, m3), ffn_total.shape[0])
    cross_total[...] = total
    size = total.shape[0]
    for send in sends:
        send[size:, :] = total
    half_of(meta, ffn_total, (m1, m2, m3), 0, ffn_half)


def slot_5(meta, self_kept, cross_total, m1, m2, m3, gln_own, gln_other, send, cross_half):
    size = self_kept.shape[0]
    total = add_up(self_kept, (m1, m2, m3), 0)
    gln = gln_own[...] + gln_other[...]
    gln = jnp.concatenate([gln, jnp.zeros((8, D), f32)], axis=0).astype(bf16)
    for r in range(GROUP):
        send[r, 0:size, :] = total
        send[r, size : size + 16, :] = gln
    half_of(meta, cross_total, (m1, m2, m3), size, cross_half)


def unpack_attention(whole_ref, outs):
    for i in range(3):
        outs[i][...] = whole_ref[:, 128 * i : 128 * i + 128].astype(f32)
    for j in range(4):
        rows = slice(128 * j, 128 * j + 128)
        outs[3][:, rows] = whole_ref[rows, 384:512].astype(f32)


def unpack_early(meta, ffn_half, ffn_arrived, cross_half, cross_arrived, *refs):
    *outs, cross_whole, ffn_whole = refs
    y, _ = position(meta)
    cross_whole[rows_of(y, 256), :] = cross_half[...]
    cross_whole[rows_of(1 - y, 256), :] = cross_arrived[...]
    unpack_attention(cross_whole, outs[2:])
    ffn_whole[rows_of(y, 512), :] = ffn_half[...]
    ffn_whole[rows_of(1 - y, 512), :] = ffn_arrived[...]
    outs[0][...] = ffn_whole[0:512, :].astype(f32)
    outs[1][...] = ffn_whole[512:1024, :].astype(f32)


def unpack_late(meta, parts, *refs):
    *outs, gln, whole_ref = refs
    size = parts.shape[1] - 16
    total = parts[0, size : size + 16, :].astype(f32)
    for r in range(1, GROUP):
        total = total + parts[r, size : size + 16, :].astype(f32)
    gln[...] = total[0:8]
    for r in range(GROUP):
        first = size * (4 * (r % 2) + r // 2)
        whole_ref[first : first + size, :] = parts[r, 0:size, :]
    unpack_attention(whole_ref, outs)


def whole(shape):
    zeros = (0,) * len(shape)
    return pl.BlockSpec(shape, lambda d, meta: zeros)


def own_row(width):
    return pl.BlockSpec((SEQ, width), lambda d, meta: (meta[0], 0))


ANY = pl.BlockSpec(memory_space=pl.ANY)


def in_hbm(x):
    return pltpu.with_memory_space_constraint(x, pltpu.HBM)


probability_out = (pltpu.HBM((DOCS, 4, FAST_K, FAST_Q), bf16), None, ANY)
probability_scratch = [
    pltpu.VMEM((2, 2, 4, FAST_K, FAST_Q), bf16),
    pltpu.SemaphoreType.DMA((2,)),
]


class Copies:
    def __init__(self, meta):
        self.first = meta[0] * SEQ
        self.loads = {}
        self.tiles = []
        self.sends = []

    def load(self, stage, source, target, sems, own_row):
        if stage == "tiles":
            first = self.first if own_row else 0
            self.tiles.append((source, target, sems, first))
            return
        if own_row:
            source = source.at[pl.ds(pl.multiple_of(self.first, SEQ), SEQ)]
        copy = pltpu.make_async_copy(source, target, sems[0].at[sems[1], 0])
        self.loads.setdefault(stage, []).append(copy)

    def tile(self, entry, i):
        source, target, (sems, b), first = entry
        rows = pl.ds(pl.multiple_of(first + i * TILE, TILE), TILE)
        return pltpu.make_async_copy(source.at[rows], target.at[rows_of(i)], sems.at[b, i])

    def start(self):
        for copy in self.loads.get("now", []):
            copy.start()
        for i in range(TILES):
            for entry in self.tiles:
                self.tile(entry, i).start()
        for stage in ("soon", "late"):
            for copy in self.loads.get(stage, []):
                copy.start()

    def wait(self, stage):
        for copy in self.loads.pop(stage, []):
            copy.wait()

    def wait_rows(self, i):
        for entry in self.tiles:
            self.tile(entry, i).wait()

    def result(self, source, target, sem, own_row):
        self.sends.append([source, target, sem, own_row, False])

    def send(self, ref, rows=None):
        for entry in self.sends:
            source, target, sem, own_row, _ = entry
            if source is ref:
                entry[4] = True
                first = self.first if own_row else 0
                if rows is None:
                    size = source.shape[0]
                else:
                    source = source.at[rows]
                    first, size = first + rows.start, rows.size
                if rows is not None or own_row:
                    target = target.at[pl.ds(pl.multiple_of(first, size), size)]
                pltpu.make_async_copy(source, target, sem).start()

    def finish(self):
        for stage in list(self.loads):
            self.wait(stage)
        for source, _, _, _, started in self.sends:
            if not started:
                self.send(source)
        for source, target, sem, own_row, _ in self.sends:
            if own_row:
                target = target.at[pl.ds(pl.multiple_of(self.first, SEQ), SEQ)]
            pltpu.make_async_copy(source, target, sem).wait()


def out(shape, dtype, own_row=False):
    return (shape, dtype, own_row)


def call(kernel, name, operands, outs, scratch, flops, token=None):
    arrays = [operands[0][0]]
    in_specs, out_specs, out_shapes = [], [], []
    buffers = []
    loads = []
    for n, (x, how) in enumerate(operands[1:]):
        if isinstance(how, str):
            stage, _, row = how.partition("_")
            shape = ((SEQ,) + x.shape[1:]) if row else x.shape
            loads.append((n, stage, len(buffers), bool(row)))
            buffers.append(pltpu.VMEM(shape, x.dtype))
            arrays.append(in_hbm(x))
            in_specs.append(ANY)
        else:
            arrays.append(x)
            in_specs.append(how)
    results = []
    for n, (shape, dtype, how) in enumerate(outs):
        if isinstance(how, bool):
            results.append((n, len(buffers), how))
            buffers.append(pltpu.VMEM(shape, dtype))
            shape = ((2 * SEQ,) + shape[1:]) if how else shape
            out_shapes.append(pltpu.HBM(shape, dtype))
            out_specs.append(ANY)
        else:
            out_shapes.append(jax.ShapeDtypeStruct(shape, dtype) if dtype else shape)
            out_specs.append(how)
    n_in, n_out = len(in_specs), len(out_specs)
    if token is not None:
        arrays.append(token)
        in_specs.append(whole((8, 128)))
        out_specs.append(whole((8, 128)))
        out_shapes.append(jax.ShapeDtypeStruct((8, 128), f32))

    def body(meta, *refs):
        ins, refs = list(refs[:n_in]), refs[len(in_specs) - n_in + n_in :]
        results_out, refs = list(refs[:n_out]), refs[n_out:]
        if token is not None:
            token_out, refs = refs[0], refs[1:]
            token_out[...] = jnp.zeros_like(token_out)
        bufs, refs = refs[: len(buffers)], refs[len(buffers) :]
        rest = refs[: len(scratch)]
        copies = Copies(meta)
        if buffers:
            sems = refs[len(scratch)]
        for n, stage, b, row in loads:
            copies.load(stage, ins[n], bufs[b], (sems, b), row)
            ins[n] = bufs[b]
        for n, b, row in results:
            copies.result(bufs[b], results_out[n], sems.at[b, 0], row)
            results_out[n] = bufs[b]
        copies.start()
        copies.wait("now")
        if buffers:
            kernel(meta, copies, *ins, *results_out, *rest)
        else:
            kernel(meta, *ins, *results_out, *rest)
        copies.finish()

    moved = sum(x.size * x.dtype.itemsize for x in arrays[1:])
    sems = [pltpu.SemaphoreType.DMA((len(buffers), TILES))] if buffers else []
    return pl.pallas_call(
        body,
        name=name,
        grid_spec=pltpu.PrefetchScalarGridSpec(
            num_scalar_prefetch=1,
            grid=(1,),
            in_specs=in_specs,
            out_specs=out_specs,
            scratch_shapes=buffers + scratch + sems,
        ),
        out_shape=out_shapes,
        compiler_params=pltpu.CompilerParams(
            dimension_semantics=("arbitrary",), vmem_limit_bytes=50 * 1024 * 1024
        ),
        cost_estimate=pl.CostEstimate(
            flops=int(flops), bytes_accessed=int(moved), transcendentals=0
        ),
    )(*arrays)


def simple(kernel, name, meta, operands, outs, scratch=()):
    return pl.pallas_call(
        kernel,
        name=name,
        grid_spec=pltpu.PrefetchScalarGridSpec(
            num_scalar_prefetch=1,
            grid=(1,),
            in_specs=[whole(x.shape) for x in operands],
            out_specs=[whole(shape) for shape, _ in outs],
            scratch_shapes=scratch,
        ),
        out_shape=[jax.ShapeDtypeStruct(shape, dtype) for shape, dtype in outs],
        compiler_params=pltpu.CompilerParams(vmem_limit_bytes=16 * 1024 * 1024),
    )(meta, *operands)


def full(x):
    return (x, whole(x.shape))


def shards(
    query_stream,
    content_stream,
    memory,
    segment_ids,
    source_segments,
    context_rank,
    context_limit,
    padding,
    ln_query_gain,
    ln_query_bias,
    ln_content_gain,
    ln_content_bias,
    self_query,
    self_key,
    self_value,
    self_out,
    ln_cross_gain,
    ln_cross_bias,
    cross_query,
    cross_key,
    cross_value,
    cross_out,
    ln_ffn_gain,
    ln_ffn_bias,
    ffn_in,
    ffn_out,
    cotangent,
):
    core = lax.axis_index("heads") % 2

    def to_core(x):
        return lax.ppermute(x, "heads", [(h, h ^ 1) for h in range(4)])

    hold = lambda *xs: lax.optimization_barrier(xs)

    def to_chip(x):
        return lax.ppermute(x, "heads", [(h, h ^ 2) for h in range(4)])

    row = pl.BlockSpec((1, 8, 128), lambda d, core: (core[0], 0, 0))

    def token_row(x):
        return (in_hbm(x.reshape(2, 8, 128)), row)

    def fixed(x):
        zeros = (0,) * x.ndim
        return (in_hbm(x), pl.BlockSpec(x.shape, lambda d, core: zeros))

    prepared = [
        ((36,), jnp.int32, pl.BlockSpec(memory_space=pltpu.SMEM)),
        ((1, SEQ), f32, whole((1, SEQ))),
        ((1, SEQ), f32, whole((1, SEQ))),
        ((8, D), f32, whole((8, D))),
        ((D, D), bf16, whole((D, D))),
        ((D, D), bf16, whole((D, D))),
    ]
    gains = (
        ln_query_gain,
        ln_query_bias,
        ln_content_gain,
        ln_content_bias,
        ln_cross_gain,
        ln_cross_bias,
        ln_ffn_gain,
        ln_ffn_bias,
    )
    weights = (self_query, self_key, self_value, self_out)
    weights += (cross_query, cross_key, cross_value, cross_out)
    tokens = (segment_ids, source_segments, context_rank, context_limit, padding)
    meta, rank, limit, norms, ws0, wc0 = call(
        prepare,
        "prepare",
        [(jnp.stack([core, lax.axis_index("rows") % GROUP]).astype(jnp.int32), None)]
        + [token_row(x) for x in tokens]
        + [fixed(x.reshape(1, D)) for x in gains]
        + [fixed(x) for x in weights],
        prepared,
        [],
        0,
    )

    ws1 = to_core(ws0)
    ws2 = to_chip(ws0)
    wc1 = to_core(wc0)
    u0, v0 = ffn_in, ffn_out
    meta_in = (meta, None)

    heads_out = [out((SEQ, 256), bf16)] * 4

    def stream_out(dtype, own_row=False):
        return out((SEQ, D), dtype, own_row)

    def now(*xs):
        return [(x, "now") for x in xs]

    def soon(*xs):
        return [(x, "soon") for x in xs]

    def late(*xs):
        return [(x, "late") for x in xs]

    def small(*xs):
        return [(x, whole(x.shape)) for x in xs]

    limits = pltpu.VMEM((SEQ, 128), f32)
    pair_flops = 2 * SEQ * D * 768 + 2 * 2 * 4 * DOCS * FAST_Q * FAST_K * 256

    nq, nc, *first, token = call(
        self_first,
        "self_first",
        [meta_in, (query_stream, "tiles_row"), (content_stream, "tiles_row")]
        + small(rank, limit, norms)
        + now(ws0, ws1),
        [stream_out(bf16), stream_out(bf16)] + heads_out + [probability_out],
        [limits] + probability_scratch,
        pair_flops,
        jnp.zeros((8, 128), f32),
    )
    ws2, wc0, token = hold(ws2, wc0, token)
    ws3 = to_core(ws2)
    wc2 = to_chip(wc0)
    *second_heads, second, ncross, token = call(
        self_second,
        "self_second",
        [meta_in, (query_stream, "late_row")]
        + [(nq, "tiles"), (nc, "tiles")]
        + small(rank, limit, norms)
        + late(ws0, ws1)
        + now(ws2, ws3)
        + late(first[3]),
        heads_out + [probability_out, stream_out(f32), stream_out(bf16)],
        [limits] + probability_scratch,
        pair_flops + 2 * SEQ * D * D,
        token,
    )
    wc2, u0, v0, token = hold(wc2, u0, v0, token)
    wc3 = to_core(wc2)
    u2 = to_chip(u0)
    u1 = to_core(u0)
    *cross_heads, token = call(
        cross_first,
        "cross_first",
        [meta_in, (ncross, "tiles"), (memory, "tiles_row")] + now(wc0, wc1),
        heads_out + [probability_out],
        probability_scratch,
        pair_flops,
        token,
    )
    wc3, u2, v0, token = hold(wc3, u2, v0, token)
    u3 = to_core(u2)
    v2 = to_chip(v0)
    v1 = to_core(v0)
    *cross_heads_second, third, nffn, token = call(
        cross_second,
        "cross_second",
        [meta_in]
        + late(second)
        + [(ncross, "tiles"), (memory, "tiles_row")]
        + small(norms)
        + late(wc0, wc1)
        + now(wc2, wc3)
        + late(cross_heads[3]),
        heads_out + [probability_out, stream_out(f32), stream_out(bf16)],
        probability_scratch,
        pair_flops + 2 * SEQ * D * D,
        token,
    )
    u3, v2, token = hold(u3, v2, token)
    v3 = to_core(v2)
    grads_ln = ((8, D), f32, whole((8, D)))
    placed_output, output, g3, g3_low, gln_ffn, ffn_own, ffn_other, token = call(
        ffn_both,
        "ffn_both",
        [meta_in]
        + [(third, "tiles"), (nffn, "tiles"), (cotangent, "tiles_row")]
        + small(norms)
        + now(u0, u1, u2, u3, v0, v1, v2, v3),
        [
            stream_out(bf16, True),
            stream_out(bf16),
            stream_out(f32),
            stream_out(bf16),
            grads_ln,
            out((1024, D), bf16),
            out((1024, D), bf16),
        ],
        [pltpu.VMEM((SEQ, 1024), bf16), pltpu.VMEM((SEQ, 1024), bf16)],
        12 * SEQ * D * 2048,
        token,
    )

    row_count = lax.axis_size("rows")
    assert row_count % GROUP == 0

    def along_rows(x, s):
        return lax.ppermute(x, "rows", [(r, r ^ s) for r in range(row_count)])

    def to_y(x):
        return along_rows(x, 1)

    def to_z(sends):
        return [along_rows(x, 2 * s) for s, x in enumerate(sends, 1)]

    def rows_out(*sizes):
        return [((n, D), bf16) for n in sizes]

    ffn_other = to_core(ffn_other)

    back_scratch = [pltpu.VMEM((SEQ, 256), bf16)] + [pltpu.VMEM((SEQ, 256), f32)] * 3
    back_scratch += probability_scratch
    pair_out = out((SEQ, 256), bf16)
    packed_outs = [out((D, D), bf16), out((D, D), bf16)]
    back_flops = 2 * SEQ * D * 256 + 4 * 2 * 4 * DOCS * FAST_Q * FAST_K * 256

    def head_inputs(natural, p):
        return soon(*natural) + [(in_hbm(p), ANY)]

    *cross_grads, cross_own, cross_other, token = call(
        functools.partial(attention_back_first, True),
        "cross_back_first",
        [meta_in]
        + [(g3_low, "tiles")]
        + late(ncross)
        + [(memory, "late_row")]
        + small(rank, limit)
        + now(wc0, wc1)
        + head_inputs(cross_heads[0:4], cross_heads[4]),
        [pair_out] * 3 + packed_outs,
        [limits] + back_scratch,
        back_flops + 2 * SEQ * D * 1024,
        token,
    )
    ffn_other, token = hold(ffn_other, token)
    ffn_keep, ffn_send = simple(slot_1, "slot_1", meta, [ffn_own, ffn_other], rows_out(512, 512))
    ffn_send, token = hold(ffn_send, token)
    ffn_arrived = to_y(ffn_send)
    cross_other = to_core(cross_other)
    g2, g2_low, placed_mem, grad_mem, gln_cross, token = call(
        cross_back_second,
        "cross_back_second",
        [meta_in]
        + [(g3_low, "tiles")]
        + late(g3, second)
        + small(norms)
        + late(wc0, wc1)
        + now(wc2, wc3)
        + late(*cross_grads)
        + head_inputs(cross_heads_second[0:4], cross_heads_second[4]),
        [stream_out(f32), stream_out(bf16), stream_out(f32, True), stream_out(bf16), grads_ln],
        back_scratch,
        back_flops + 2 * SEQ * D * 1536,
        token,
    )
    ffn_arrived, cross_other, token = hold(ffn_arrived, cross_other, token)
    ffn_keep, *sends, cross_keep, cross_send = simple(
        slot_2,
        "slot_2",
        meta,
        [ffn_keep, ffn_arrived, cross_own, cross_other],
        rows_out(128, 128, 128, 128, 256, 256),
    )
    ffn_keep, cross_send, token = hold(ffn_keep, cross_send, token)
    ffn_parts = to_z(sends)
    cross_arrived = to_y(cross_send)

    *self_grads, self_own, self_other, token = call(
        functools.partial(attention_back_first, False),
        "self_back_first",
        [meta_in]
        + [(g2_low, "tiles")]
        + late(nq, nc)
        + small(rank, limit)
        + now(ws0, ws1)
        + head_inputs(first[0:4], first[4]),
        [pair_out] * 3 + packed_outs,
        [limits] + back_scratch,
        back_flops + 2 * SEQ * D * 1024,
        token,
    )
    *ffn_parts, cross_arrived, self_other, token = hold(
        *ffn_parts, cross_arrived, self_other, token
    )
    self_other = to_core(self_other)
    ffn_total, cross_keep, *sends, self_keep, self_send = simple(
        slot_3,
        "slot_3",
        meta,
        [ffn_keep, *ffn_parts, cross_keep, cross_arrived, self_own, self_other],
        rows_out(128, 64, 192, 192, 192, 256, 256),
    )
    ffn_total, self_send, token = hold(ffn_total, self_send, token)
    self_arrived = to_y(self_send)
    messages = to_z(sends)
    *self_grads_second, token = call(
        self_back_second,
        "self_back_second",
        [meta_in, (g2_low, "tiles")]
        + small(rank, limit)
        + now(ws2, ws3)
        + head_inputs(second_heads[0:4], second_heads[4]),
        [pair_out] * 3,
        [limits] + back_scratch,
        back_flops,
        token,
    )
    *messages, self_arrived, token = hold(*messages, self_arrived, token)
    ffn_half, cross_total, self_keep, *sends = simple(
        slot_4,
        "slot_4",
        meta,
        [ffn_total, *messages, cross_keep, self_keep, self_arrived],
        rows_out(512, 64, 64, 128, 128, 128),
    )
    cross_total, ffn_half, token = hold(cross_total, ffn_half, token)
    messages = to_z(sends)
    ffn_arrived = to_y(ffn_half)
    placed_q, placed_c, gq, gc, gln_self, token = call(
        self_back_finish,
        "self_back_finish",
        [meta_in, (g2, "tiles"), (query_stream, "tiles_row"), (content_stream, "tiles_row")]
        + small(norms)
        + now(ws0, ws1, ws2, ws3)
        + [(x, "tiles") for x in self_grads + self_grads_second],
        [stream_out(f32, True), stream_out(f32, True), stream_out(bf16), stream_out(bf16), grads_ln],
        [],
        2 * SEQ * D * 1536,
        token,
    )
    gln = jnp.concatenate([gln_self[0:4], gln_cross[0:2], gln_ffn[0:2]], axis=0)
    *messages, ffn_arrived, gln = hold(*messages, ffn_arrived, gln)
    last_send, cross_half = simple(
        slot_5,
        "slot_5",
        meta,
        [self_keep, cross_total, *messages, gln, to_core(gln)],
        [((GROUP, 80, D), bf16), ((256, D), bf16)],
    )
    output, grad_mem, last_send = hold(output, grad_mem, last_send)
    groups = None
    if row_count > GROUP:
        groups = [list(range(r, r + GROUP)) for r in range(0, row_count, GROUP)]
    last_parts = lax.all_to_all(last_send, "rows", 0, 0, axis_index_groups=groups)
    cross_arrived = to_y(cross_half)

    def over_groups(totals):
        if row_count == GROUP:
            return totals
        groups = [list(range(r, row_count, GROUP)) for r in range(GROUP)]
        return lax.psum(totals, "rows", axis_index_groups=groups)

    def both_rows(placed_own, arrays, name):
        count = len(arrays)
        size = SEQ // 2
        one = pl.BlockSpec((size, D), lambda i, meta: (i, 0))
        block = pl.BlockSpec((size, D), lambda i, meta: (2 * (1 - meta[0]) + i, 0))
        return pl.pallas_call(
            place_rows,
            name=name,
            grid_spec=pltpu.PrefetchScalarGridSpec(
                num_scalar_prefetch=1,
                grid=(2,),
                in_specs=[one] * count + [pl.BlockSpec(memory_space=pl.ANY)] * count,
                out_specs=[block] * count,
            ),
            out_shape=[jax.ShapeDtypeStruct(x.shape, x.dtype) for x in placed_own],
            input_output_aliases={1 + count + n: n for n in range(count)},
        )(meta, *[to_core(x) for x in arrays], *placed_own)

    out_both, grad_mem_both = both_rows([placed_output, placed_mem], [output, grad_mem], "place_early")
    gq_both, gc_both = both_rows([placed_q, placed_c], [gq, gc], "place_late")

    attention_outs = [((512, 128), f32)] * 3 + [((128, 512), f32)]
    grad_ffn_in, grad_ffn_out, *grad_cross_parts = simple(
        unpack_early,
        "unpack_early",
        meta,
        [ffn_half, ffn_arrived, cross_half, cross_arrived],
        [((D, D), f32)] * 2 + attention_outs,
        [pltpu.VMEM((D, D), bf16), pltpu.VMEM((2 * D, D), bf16)],
    )
    *grad_self_parts, gln = simple(
        unpack_late,
        "unpack_late",
        meta,
        [last_parts],
        attention_outs + [((8, D), f32)],
        [pltpu.VMEM((D, D), bf16)],
    )
    grad_ffn_in, grad_ffn_out, grad_cross_parts, grad_self_parts, gln = over_groups(
        (grad_ffn_in, grad_ffn_out, grad_cross_parts, grad_self_parts, gln)
    )
    return (
        out_both,
        gq_both,
        gc_both,
        grad_mem_both,
        gln[0],
        gln[1],
        gln[2],
        gln[3],
        *grad_self_parts,
        gln[4],
        gln[5],
        *grad_cross_parts,
        gln[6],
        gln[7],
        grad_ffn_in,
        grad_ffn_out,
    )


def solution(mesh):
    assert mesh.shape["heads"] == 4
    row_spec = P("rows", None)
    flat = P("rows")
    by_column = P(None, "heads")
    by_row = P("heads", None)
    attention = (by_column, by_column, by_column, by_row)
    in_specs = (
        (row_spec,) * 3
        + (flat,) * 5
        + (P(),) * 4
        + attention
        + (P(),) * 2
        + attention
        + (P(),) * 2
        + (by_column, by_row, row_spec)
    )
    out_specs = (
        (row_spec,) * 4
        + (P(),) * 4
        + attention
        + (P(),) * 2
        + attention
        + (P(),) * 2
        + (by_column, by_row)
    )
    return jax.shard_map(shards, mesh=mesh, in_specs=in_specs, out_specs=out_specs, check_vma=False)
```

```python
import functools

import jax
import jax.numpy as jnp
from jax import lax
from jax.experimental import pallas as pl
from jax.experimental.pallas import tpu as pltpu
from jax.sharding import PartitionSpec as P

HEAD_DIM = 64
SEQ = 1024
DOCS = 8
D = 512
TILE = 256
TILES = SEQ // TILE
FAST_Q = 256
FAST_K = 208
LONG_Q = 128
LONG_K = 640

norm_eps = 1e-05
masked_score = -1e30
hidden_rank = 1e6
gelu_root = 0.7978845608028654
gelu_cube = 0.044715

f32 = jnp.float32
bf16 = jnp.bfloat16


def dot(a, b):
    return lax.dot_general(a, b, (((1,), (0,)), ((), ())), preferred_element_type=f32)


def dot_nt(a, b):
    return lax.dot_general(a, b, (((1,), (1,)), ((), ())), preferred_element_type=f32)


def dot_tn(a, b):
    return lax.dot_general(a, b, (((0,), (0,)), ((), ())), preferred_element_type=f32)


def lanes(parts):
    return jnp.concatenate(parts, axis=1)


def layer_norm(values, gain, shift):
    centre = values - jnp.mean(values, axis=-1, keepdims=True)
    spread = jnp.mean(centre * centre, axis=-1, keepdims=True)
    return centre * lax.rsqrt(spread + norm_eps) * gain + shift


def norm_backward(values, gain, grad):
    centre = values - jnp.mean(values, axis=-1, keepdims=True)
    spread = jnp.mean(centre * centre, axis=-1, keepdims=True)
    scale = lax.rsqrt(spread + norm_eps)
    xhat = centre * scale
    eg = grad * gain
    mean_eg = jnp.mean(eg, axis=-1, keepdims=True)
    mean_egx = jnp.mean(eg * xhat, axis=-1, keepdims=True)
    grad_gain = jnp.sum(grad * xhat, axis=0, keepdims=True)
    grad_shift = jnp.sum(grad, axis=0, keepdims=True)
    return scale * (eg - mean_eg - xhat * mean_egx), grad_gain, grad_shift


def rows_of(i, size=TILE):
    return pl.ds(pl.multiple_of(i * size, size), size)


def w_query(ref):
    return ref[:, 0:128]


def w_key(ref):
    return ref[:, 128:256]


def w_value(ref):
    return ref[:, 256:384]


def w_out(ref):
    return lanes([ref[128 * j : 128 * j + 128, 384:512] for j in range(4)])


def half_masks():
    place = lax.broadcasted_iota(jnp.int32, (1, 128), 1)
    low = jnp.where(place < HEAD_DIM, 1.0, 0.0).astype(f32)
    return (low.astype(bf16), (1.0 - low).astype(bf16))


def doc_bounds(meta, d, source):
    base = 17 if source else 1
    return meta[base + d], meta[base + 8 + d]


def window_of(first, limit):
    return pl.multiple_of(jnp.minimum((first // 16) * 16, limit), 16)


def key_bias(ks, ke, k0, width):
    place = k0 + lax.broadcasted_iota(jnp.int32, (width, 128), 0)
    return jnp.where((place >= ks) & (place < ke), 0.0, masked_score)


def make_bias(rank_ref, limit_ref, ks, ke, q0, k0, span, width):
    if rank_ref is None:
        return lanes([key_bias(ks, ke, k0, width)] * (span // 128))
    place = k0 + lax.broadcasted_iota(jnp.int32, (width, 128), 0)
    ranks = rank_ref[pl.ds(k0, width), :]
    ranks = jnp.where((place < ks + 2) & (ranks < hidden_rank), -1.0, ranks)
    ranks = jnp.where((place >= ks) & (place < ke), ranks, hidden_rank)
    limits = jnp.broadcast_to(limit_ref[...], (8, SEQ))
    limits = pltpu.roll(limits, lax.rem(SEQ - q0, SEQ), 1)[0:1, 0:span]
    row = k0 + lax.broadcasted_iota(jnp.int32, (width, span), 0)
    column = q0 + lax.broadcasted_iota(jnp.int32, (width, span), 1)
    seen = (lanes([ranks] * (span // 128)) < limits) & (row != column)
    return jnp.where(seen, 0.0, masked_score)


STEPS = DOCS // 2


def is_fast(meta, cross):
    return meta[34 if cross else 33] == 1


def both_heads(x, masks):
    return jnp.concatenate([x * masks[0], x * masks[1]], axis=0)


def pair_probabilities(queries, keys, masks, bias):
    width = keys.shape[0]
    scores = dot_nt(both_heads(keys, masks), queries)
    result = []
    for a in range(2):
        part = scores[width * a : width * a + width] + bias
        part = jnp.exp(part - jnp.max(part, axis=0, keepdims=True))
        part = part * (1.0 / jnp.sum(part, axis=0, keepdims=True))
        result.append(part.astype(bf16))
    return result


def pair_product(rows, parts):
    across = jnp.transpose(rows)
    halves = [dot(across[64 * a : 64 * a + 64], part) for a, part in enumerate(parts)]
    return jnp.transpose(jnp.concatenate(halves, axis=0))


def pick_heads(both):
    width = both.shape[0] // 2
    first = lax.broadcasted_iota(jnp.int32, (width, 128), 1) < HEAD_DIM
    return jnp.where(first, both[:width], both[width:])


def for_docs(meta, cross, run, before, after):
    @pl.when(is_fast(meta, cross))
    def _():
        def step(i, carry):
            slot = lax.rem(i, 2)
            before(i, slot)
            for place in range(2):
                d = 2 * i + place
                ts, te = doc_bounds(meta, d, False)
                ks, ke = doc_bounds(meta, d, cross)
                q0 = window_of(ts, SEQ - FAST_Q)
                k0 = window_of(ks, SEQ - FAST_K)
                run(d, slot, place, q0, k0, FAST_Q, FAST_K, ts, te, ks, ke, True)
            after(i, slot)
            return carry

        lax.fori_loop(0, STEPS, step, 0)

    @pl.when(jnp.logical_not(is_fast(meta, cross)))
    def _():
        def doc(d, carry):
            ts, te = doc_bounds(meta, d, False)
            ks, ke = doc_bounds(meta, d, cross)
            base = (ts // 16) * 16
            k0 = window_of(ks, SEQ - LONG_K)

            def chunk(i, carry):
                lower = base + i * LONG_Q
                q0 = pl.multiple_of(jnp.minimum(lower, SEQ - LONG_Q), 16)
                low = jnp.maximum(ts, lower)
                high = jnp.minimum(te, lower + LONG_Q)
                run(d, None, None, q0, k0, LONG_Q, LONG_K, low, high, ks, ke, False)
                return carry

            return lax.fori_loop(0, (te - base + LONG_Q - 1) // LONG_Q, chunk, carry)

        lax.fori_loop(0, DOCS, doc, 0)


def attend_docs(meta, cross, rank_ref, limit_ref, halves, p_ref, p_buf, p_sem):
    pairs = 2 * len(halves)
    masks = half_masks()

    def save(i, slot):
        return pltpu.make_async_copy(p_buf.at[slot], p_ref.at[pl.ds(2 * i, 2)], p_sem.at[slot])

    def before(i, slot):
        @pl.when(i >= 2)
        def _():
            save(i - 2, slot).wait()

    def after(i, slot):
        save(i, slot).start()

    def run(d, slot, place, q0, k0, span, width, low, high, ks, ke, fast):
        bias = make_bias(rank_ref, limit_ref, ks, ke, q0, k0, span, width)
        row = q0 + lax.broadcasted_iota(jnp.int32, (span, 128), 0)
        inside = (row >= low) & (row < high)
        for n in range(pairs):
            q_ref, k_ref, v_ref, mixed_ref = halves[n // 2]
            cols = slice(128 * (n % 2), 128 * (n % 2) + 128)
            queries = q_ref[pl.ds(q0, span), cols]
            keys = k_ref[pl.ds(k0, width), cols]
            values = v_ref[pl.ds(k0, width), cols]
            parts = pair_probabilities(queries, keys, masks, bias)
            if fast:
                for a in range(2):
                    p_buf[slot, place, 2 * n + a] = parts[a]
            mixed = pair_product(values, parts)
            old = mixed_ref[pl.ds(q0, span), cols].astype(f32)
            mixed_ref[pl.ds(q0, span), cols] = jnp.where(inside, mixed, old).astype(bf16)

    for_docs(meta, cross, run, before, after)

    @pl.when(is_fast(meta, cross))
    def _():
        for i in range(STEPS - 2, STEPS):
            save(i, i % 2).wait()


def load_step(load, i, slot):
    p_ref, p_buf, p_sem = load
    return pltpu.make_async_copy(p_ref.at[pl.ds(2 * i, 2)], p_buf.at[slot], p_sem.at[slot])


def start_load(meta, cross, load):
    @pl.when(is_fast(meta, cross))
    def _():
        load_step(load, 0, 0).start()


def attend_docs_back(
    meta, cross, rank_ref, limit_ref, q_ref, k_ref, v_ref, mixed_ref, dm_ref,
    dq_ref, dk_ref, dv_ref, load,
):
    pairs = q_ref.shape[1] // 128
    masks = half_masks()
    p_buf = load[1]

    def before(i, slot):
        @pl.when(i + 1 < STEPS)
        def _():
            load_step(load, i + 1, 1 - slot).start()

        load_step(load, i, slot).wait()

    def after(i, slot):
        pass

    def run(d, slot, place, q0, k0, span, width, low, high, ks, ke, fast):
        row = q0 + lax.broadcasted_iota(jnp.int32, (span, 128), 0)
        inside = (row >= low) & (row < high)
        ones = jnp.ones((width, 128), bf16)
        if not fast:
            bias = make_bias(rank_ref, limit_ref, ks, ke, q0, k0, span, width)
        for n in range(pairs):
            cols = slice(128 * n, 128 * n + 128)
            queries = q_ref[pl.ds(q0, span), cols]
            keys = k_ref[pl.ds(k0, width), cols]
            values = v_ref[pl.ds(k0, width), cols]
            mixed = mixed_ref[pl.ds(q0, span), cols].astype(f32)
            grad = jnp.where(inside, dm_ref[pl.ds(q0, span), cols].astype(f32), 0.0)
            low_grad = grad.astype(bf16)
            left = lanes([low_grad, (-(grad * mixed)).astype(bf16)])
            delta = dot_nt(both_heads(lanes([values, ones]), [lanes([m, m]) for m in masks]), left)
            if fast:
                parts = [p_buf[slot, place, 2 * n + a] for a in range(2)]
            else:
                parts = pair_probabilities(queries, keys, masks, bias)
            slopes = [
                (parts[a].astype(f32) * delta[width * a : width * a + width]).astype(bf16)
                for a in range(2)
            ]
            dk = pick_heads(dot(jnp.concatenate(slopes, axis=0), queries))
            dv = pick_heads(dot(jnp.concatenate(parts, axis=0), low_grad))
            dq = pair_product(keys, slopes)
            dq_ref[pl.ds(q0, span), cols] += dq * (HEAD_DIM**-0.5)
            dk_ref[pl.ds(k0, width), cols] += dk
            dv_ref[pl.ds(k0, width), cols] += dv

    for_docs(meta, cross, run, before, after)


def spread_ranks(rank_row_ref, rank_ref):
    rank_ref[...] = jnp.transpose(jnp.broadcast_to(rank_row_ref[...], (128, SEQ)))


def prepare(
    core, seg_ref, src_ref, rank_ref, limit_ref, pad_ref,
    n0, n1, n2, n3, n4, n5, n6, n7, sq, sk, sv, so, cq, ck, cv, co,
    meta_ref, ranks_ref, limits_ref, norms_ref, ws_ref, wc_ref,
):
    meta_ref[0] = core[0]
    meta_ref[35] = core[1]
    for base, ref in ((1, seg_ref), (17, src_ref)):
        ids = ref[0]
        meta_ref[base] = 0
        meta_ref[base + 15] = SEQ
        for d in range(1, DOCS):
            cut = jnp.sum(jnp.where(ids < d, 1.0, 0.0)).astype(jnp.int32)
            meta_ref[base + d] = cut
            meta_ref[base + 7 + d] = cut
    for place, base in ((33, 1), (34, 17)):
        fast = jnp.int32(1)
        for d in range(DOCS):
            q0 = window_of(meta_ref[1 + d], SEQ - FAST_Q)
            k0 = window_of(meta_ref[base + d], SEQ - FAST_K)
            fits = (meta_ref[9 + d] - q0 <= FAST_Q) & (meta_ref[base + 8 + d] - k0 <= FAST_K)
            fast = fast & fits.astype(jnp.int32)
        meta_ref[place] = fast
    ranks = jnp.where(pad_ref[0] != 0, hidden_rank, rank_ref[0].astype(f32))
    limits = limit_ref[0].astype(f32)
    for i in range(8):
        ranks_ref[0:1, 128 * i : 128 * i + 128] = ranks[i : i + 1]
        limits_ref[0:1, 128 * i : 128 * i + 128] = limits[i : i + 1]
    for i, ref in enumerate((n0, n1, n2, n3, n4, n5, n6, n7)):
        norms_ref[i : i + 1, :] = ref[...]
    for to, parts, out in ((ws_ref, (sq, sk, sv), so), (wc_ref, (cq, ck, cv), co)):
        for i, part in enumerate(parts):
            to[:, 128 * i : 128 * i + 128] = part[...]
        for j in range(4):
            to[128 * j : 128 * j + 128, 384:512] = out[:, 128 * j : 128 * j + 128]


def self_first(
    meta, io, xq_ref, xc_ref, rank_row_ref, limit_ref, norms_ref, w0_ref, w1_ref,
    nq_ref, nc_ref, q_ref, k_ref, v_ref, mixed_ref, p_ref, rank_ref, p_buf, p_sem,
):

    spread_ranks(rank_row_ref, rank_ref)
    wq = lanes([w_query(w0_ref), w_query(w1_ref)])
    wkv = lanes([w_key(w0_ref), w_key(w1_ref), w_value(w0_ref), w_value(w1_ref)])

    def tile(i, carry):
        rows = rows_of(i)
        io.wait_rows(i)
        nq = layer_norm(xq_ref[rows, :].astype(f32), norms_ref[0:1], norms_ref[1:2]).astype(bf16)
        nc = layer_norm(xc_ref[rows, :].astype(f32), norms_ref[2:3], norms_ref[3:4]).astype(bf16)
        nq_ref[rows, :] = nq
        nc_ref[rows, :] = nc
        q_ref[rows, :] = (dot(nq, wq) * (HEAD_DIM**-0.5)).astype(bf16)
        kv = dot(nc, wkv).astype(bf16)
        k_ref[rows, :] = kv[:, :256]
        v_ref[rows, :] = kv[:, 256:]
        return carry

    lax.fori_loop(0, TILES, tile, 0)

    for ref in (nq_ref, nc_ref, q_ref, k_ref, v_ref):
        io.send(ref)
    attend_docs(meta, False, rank_ref, limit_ref, [(q_ref, k_ref, v_ref, mixed_ref)], p_ref, p_buf, p_sem)


def self_second(
    meta, io, xq_ref, nq_ref, nc_ref, rank_row_ref, limit_ref, norms_ref, w0_ref, w1_ref, w2_ref, w3_ref,
    mixed_first_ref,
    q_ref, k_ref, v_ref, mixed_ref, p_ref, second_ref, ncross_ref, rank_ref, p_buf, p_sem,
):

    spread_ranks(rank_row_ref, rank_ref)
    wq = lanes([w_query(w2_ref), w_query(w3_ref)])
    wkv = lanes([w_key(w2_ref), w_key(w3_ref), w_value(w2_ref), w_value(w3_ref)])

    def tile(i, carry):
        rows = rows_of(i)
        io.wait_rows(i)
        q_ref[rows, :] = (dot(nq_ref[rows, :], wq) * (HEAD_DIM**-0.5)).astype(bf16)
        kv = dot(nc_ref[rows, :], wkv).astype(bf16)
        k_ref[rows, :] = kv[:, :256]
        v_ref[rows, :] = kv[:, 256:]
        return carry

    lax.fori_loop(0, TILES, tile, 0)

    for ref in (q_ref, k_ref, v_ref):
        io.send(ref)
    attend_docs(meta, False, rank_ref, limit_ref, [(q_ref, k_ref, v_ref, mixed_ref)], p_ref, p_buf, p_sem)

    io.send(mixed_ref)
    io.wait("late")
    out_first = jnp.concatenate([w_out(w0_ref), w_out(w1_ref)], axis=0)
    out_second = jnp.concatenate([w_out(w2_ref), w_out(w3_ref)], axis=0)

    def tile(i, carry):
        rows = rows_of(i)
        branch = dot(mixed_first_ref[rows, :], out_first) + dot(mixed_ref[rows, :], out_second)
        second = xq_ref[rows, :].astype(f32) + branch
        second_ref[rows, :] = second
        io.send(second_ref, rows)
        ncross_ref[rows, :] = layer_norm(second, norms_ref[4:5], norms_ref[5:6]).astype(bf16)
        io.send(ncross_ref, rows)
        return carry

    lax.fori_loop(0, TILES, tile, 0)


def project_cross(io, ncross_ref, memory_ref, weights, q_ref, k_ref, v_ref):
    wq = lanes([w_query(w) for w in weights])
    wkv = lanes([w_key(w) for w in weights] + [w_value(w) for w in weights])

    def tile(i, carry):
        rows = rows_of(i)
        io.wait_rows(i)
        q_ref[rows, :] = (dot(ncross_ref[rows, :], wq) * (HEAD_DIM**-0.5)).astype(bf16)
        kv = dot(memory_ref[rows, :], wkv).astype(bf16)
        k_ref[rows, :] = kv[:, :256]
        v_ref[rows, :] = kv[:, 256:]
        return carry

    lax.fori_loop(0, TILES, tile, 0)
    for ref in (q_ref, k_ref, v_ref):
        io.send(ref)


def cross_first(
    meta, io, ncross_ref, memory_ref, w0_ref, w1_ref,
    q_ref, k_ref, v_ref, mixed_ref, p_ref, p_buf, p_sem,
):
    project_cross(io, ncross_ref, memory_ref, (w0_ref, w1_ref), q_ref, k_ref, v_ref)
    attend_docs(meta, True, None, None, [(q_ref, k_ref, v_ref, mixed_ref)], p_ref, p_buf, p_sem)


def cross_second(
    meta, io, second_ref, ncross_ref, memory_ref, norms_ref, w0_ref, w1_ref, w2_ref, w3_ref,
    mixed_first_ref,
    q_ref, k_ref, v_ref, mixed_ref, p_ref, third_ref, nffn_ref, p_buf, p_sem,
):
    project_cross(io, ncross_ref, memory_ref, (w2_ref, w3_ref), q_ref, k_ref, v_ref)
    attend_docs(meta, True, None, None, [(q_ref, k_ref, v_ref, mixed_ref)], p_ref, p_buf, p_sem)
    io.send(mixed_ref)
    io.wait("late")
    out_first = jnp.concatenate([w_out(w0_ref), w_out(w1_ref)], axis=0)
    out_second = jnp.concatenate([w_out(w2_ref), w_out(w3_ref)], axis=0)

    def tile(i, carry):
        rows = rows_of(i)
        branch = dot(mixed_first_ref[rows, :], out_first) + dot(mixed_ref[rows, :], out_second)
        third = second_ref[rows, :] + branch
        third_ref[rows, :] = third
        io.send(third_ref, rows)
        nffn_ref[rows, :] = layer_norm(third, norms_ref[6:7], norms_ref[7:8]).astype(bf16)
        io.send(nffn_ref, rows)
        return carry

    lax.fori_loop(0, TILES, tile, 0)


def ffn_both(
    meta, io, third_ref, nffn_ref, cot_ref, norms_ref, u0_ref, u1_ref, u2_ref, u3_ref,
    w0_ref, w1_ref, w2_ref, w3_ref,
    placed_ref, out_ref, g3_ref, g3_low_ref, gln_ref, own_ref, other_ref, hidden_ref, before_ref,
):
    gln_ref[...] = jnp.zeros_like(gln_ref)
    in_refs = (u0_ref, u1_ref, u2_ref, u3_ref)

    def tile(i, carry):
        rows = rows_of(i, 2 * TILE)
        io.wait_rows(2 * i)
        io.wait_rows(2 * i + 1)
        nffn = nffn_ref[rows, :]
        cot = cot_ref[rows, :]
        outs = []
        grads = []
        for g, w_ref in enumerate((w0_ref, w1_ref, w2_ref, w3_ref)):
            w_in = in_refs[g][...]
            w_out_rows = w_ref[...]
            x = dot(nffn, w_in)
            square = x * x
            half = 0.5 + 0.5 * jnp.tanh(x * (gelu_root + (gelu_root * gelu_cube) * square))
            value = x * half
            hidden = value.astype(bf16)
            rise = 2.0 * gelu_root + (6.0 * gelu_root * gelu_cube) * square
            slope = half + value * (1.0 - half) * rise
            grad_before = (dot_nt(cot, w_out_rows) * slope).astype(bf16)
            outs.append(dot(hidden, w_out_rows))
            grads.append(dot_nt(grad_before, w_in))
            if g < 2:
                hidden_ref[rows, 512 * g : 512 * g + 512] = hidden
                before_ref[rows, 512 * g : 512 * g + 512] = grad_before
        third = third_ref[rows, :]
        result = (third + ((outs[0] + outs[1]) + (outs[2] + outs[3]))).astype(bf16)
        out_ref[rows, :] = result
        placed_ref[rows, :] = result
        grad_normed = (grads[0] + grads[1]) + (grads[2] + grads[3])
        grad_norm, grad_gain, grad_shift = norm_backward(third, norms_ref[6:7], grad_normed)
        g3 = cot.astype(f32) + grad_norm
        g3_ref[rows, :] = g3
        g3_low_ref[rows, :] = g3.astype(bf16)
        gln_ref[0:1, :] += grad_gain
        gln_ref[1:2, :] += grad_shift
        for ref in (out_ref, placed_ref, g3_ref, g3_low_ref):
            io.send(ref, rows)
        return carry

    lax.fori_loop(0, TILES // 2, tile, 0)
    part = dot_tn(nffn_ref[...], before_ref[...])
    own_ref[0:512, :] = part[:, 0:512].astype(bf16)
    other_ref[0:512, :] = part[:, 512:1024].astype(bf16)
    io.send(own_ref, pl.ds(0, 512))
    io.send(other_ref, pl.ds(0, 512))
    part = dot_tn(hidden_ref[...], cot_ref[...])
    own_ref[512:1024, :] = part[0:512].astype(bf16)
    other_ref[512:1024, :] = part[512:1024].astype(bf16)
    io.send(own_ref, pl.ds(512, 512))
    io.send(other_ref, pl.ds(512, 512))


def back_start(io, g_ref, mixed_ref, w_refs, dm_ref, dq_ref, dk_ref, dv_ref):
    out_rows = jnp.concatenate([w_out(w) for w in w_refs], axis=0)

    def tile(i, carry):
        rows = rows_of(i)
        io.wait_rows(i)
        dm_ref[rows, :] = dot_nt(g_ref[rows, :], out_rows).astype(bf16)
        zeros = jnp.zeros((TILE, 256), f32)
        dq_ref[rows, :] = zeros
        dk_ref[rows, :] = zeros
        dv_ref[rows, :] = zeros
        return carry

    lax.fori_loop(0, TILES, tile, 0)


def attention_back_first(
    cross, meta, io, g_ref, nq_ref, nkv_ref, rank_row_ref, limit_ref, w0_ref, w1_ref,
    q_ref, k_ref, v_ref, mixed_ref, p_ref,
    dq_ref, dk_ref, dv_ref, own_ref, other_ref,
    rank_ref, dm_ref, dqs_ref, dks_ref, dvs_ref, p_buf, p_sem,
):
    load = (p_ref, p_buf, p_sem)
    start_load(meta, cross, load)
    if not cross:
        spread_ranks(rank_row_ref, rank_ref)
    back_start(io, g_ref, mixed_ref, (w0_ref, w1_ref), dm_ref, dqs_ref, dks_ref, dvs_ref)

    io.wait("soon")
    attend_docs_back(
        meta, cross, None if cross else rank_ref, limit_ref, q_ref, k_ref, v_ref, mixed_ref,
        dm_ref, dqs_ref, dks_ref, dvs_ref, load,
    )

    dq_ref[...] = dqs_ref[...].astype(bf16)
    dk_ref[...] = dks_ref[...].astype(bf16)
    dv_ref[...] = dvs_ref[...].astype(bf16)
    for ref in (dq_ref, dk_ref, dv_ref):
        io.send(ref)
    io.wait("late")
    nq = nq_ref[...]
    nkv = nkv_ref[...]
    for n, part in enumerate(
        (dot_tn(nq, dq_ref[...]), dot_tn(nkv, dk_ref[...]), dot_tn(nkv, dv_ref[...]))
    ):
        own_ref[:, 128 * n : 128 * n + 128] = part[:, :128].astype(bf16)
        other_ref[:, 128 * n : 128 * n + 128] = part[:, 128:].astype(bf16)
    part = dot_tn(mixed_ref[...], g_ref[...])
    for j in range(4):
        rows = slice(128 * j, 128 * j + 128)
        own_ref[rows, 384:512] = part[:128, rows].astype(bf16)
        other_ref[rows, 384:512] = part[128:, rows].astype(bf16)


def back_second_docs(
    cross, meta, io, g_ref, rank_row_ref, limit_ref, w_refs, q_ref, k_ref, v_ref, mixed_ref, p_ref,
    rank_ref, dm_ref, dqs_ref, dks_ref, dvs_ref, p_buf, p_sem,
):
    load = (p_ref, p_buf, p_sem)
    start_load(meta, cross, load)
    if not cross:
        spread_ranks(rank_row_ref, rank_ref)
    back_start(io, g_ref, mixed_ref, w_refs, dm_ref, dqs_ref, dks_ref, dvs_ref)

    io.wait("soon")
    attend_docs_back(
        meta, cross, None if cross else rank_ref, limit_ref, q_ref, k_ref, v_ref, mixed_ref,
        dm_ref, dqs_ref, dks_ref, dvs_ref, load,
    )


def stream_grads(rows, first, second, firsts, seconds):
    dq, dk, dv = first
    dq2, dk2, dv2 = (ref[rows, :].astype(bf16) for ref in second)
    w0, w1 = firsts
    w2, w3 = seconds
    grad_q = dot_nt(dq[rows, :], lanes([w_query(w0), w_query(w1)])) + dot_nt(
        dq2, lanes([w_query(w2), w_query(w3)])
    )
    kv = lanes([dk[rows, :], dv[rows, :]])
    kv2 = lanes([dk2, dv2])
    grad_kv = dot_nt(kv, lanes([w_key(w0), w_key(w1), w_value(w0), w_value(w1)])) + dot_nt(
        kv2, lanes([w_key(w2), w_key(w3), w_value(w2), w_value(w3)])
    )
    return grad_q, grad_kv


def cross_back_second(
    meta, io, g_low_ref, g_ref, second_ref, norms_ref, w0_ref, w1_ref, w2_ref, w3_ref,
    dq_ref, dk_ref, dv_ref, q_ref, k_ref, v_ref, mixed_ref, p_ref,
    g2_ref, g2_low_ref, placed_ref, gmem_ref, gln_ref,
    dm_ref, dqs_ref, dks_ref, dvs_ref, p_buf, p_sem,
):
    back_second_docs(
        True, meta, io, g_low_ref, None, None, (w2_ref, w3_ref), q_ref, k_ref, v_ref, mixed_ref, p_ref,
        None, dm_ref, dqs_ref, dks_ref, dvs_ref, p_buf, p_sem,
    )

    io.wait("late")
    gln_ref[...] = jnp.zeros_like(gln_ref)

    def tile(i, carry):
        rows = rows_of(i)
        grad_q, grad_kv = stream_grads(
            rows,
            (dq_ref, dk_ref, dv_ref),
            (dqs_ref, dks_ref, dvs_ref),
            (w0_ref, w1_ref),
            (w2_ref, w3_ref),
        )
        low_kv = grad_kv.astype(bf16)
        gmem_ref[rows, :] = low_kv
        placed_ref[rows, :] = low_kv.astype(f32)
        io.send(gmem_ref, rows)
        io.send(placed_ref, rows)
        grad_norm, grad_gain, grad_shift = norm_backward(
            second_ref[rows, :], norms_ref[4:5], grad_q
        )
        g2 = g_ref[rows, :] + grad_norm
        g2_ref[rows, :] = g2
        g2_low_ref[rows, :] = g2.astype(bf16)
        io.send(g2_ref, rows)
        io.send(g2_low_ref, rows)
        gln_ref[0:1, :] += grad_gain
        gln_ref[1:2, :] += grad_shift
        return carry

    lax.fori_loop(0, TILES, tile, 0)


def self_back_second(
    meta, io, g_low_ref, rank_row_ref, limit_ref, w2_ref, w3_ref,
    q_ref, k_ref, v_ref, mixed_ref, p_ref,
    dq_ref, dk_ref, dv_ref,
    rank_ref, dm_ref, dqs_ref, dks_ref, dvs_ref, p_buf, p_sem,
):
    back_second_docs(
        False, meta, io, g_low_ref, rank_row_ref, limit_ref, (w2_ref, w3_ref), q_ref, k_ref, v_ref,
        mixed_ref, p_ref, rank_ref, dm_ref, dqs_ref, dks_ref, dvs_ref, p_buf, p_sem,
    )
    dq_ref[...] = dqs_ref[...].astype(bf16)
    dk_ref[...] = dks_ref[...].astype(bf16)
    dv_ref[...] = dvs_ref[...].astype(bf16)


def self_back_finish(
    meta, io, g_ref, xq_ref, xc_ref, norms_ref, w0_ref, w1_ref, w2_ref, w3_ref,
    dq_ref, dk_ref, dv_ref, dq2_ref, dk2_ref, dv2_ref,
    placed_q_ref, placed_c_ref, gq_ref, gc_ref, gln_ref,
):
    gln_ref[...] = jnp.zeros_like(gln_ref)

    def tile(i, carry):
        rows = rows_of(i)
        io.wait_rows(i)
        grad_q, grad_kv = stream_grads(
            rows,
            (dq_ref, dk_ref, dv_ref),
            (dq2_ref, dk2_ref, dv2_ref),
            (w0_ref, w1_ref),
            (w2_ref, w3_ref),
        )
        grad_norm, grad_gain, grad_shift = norm_backward(
            xq_ref[rows, :].astype(f32), norms_ref[0:1], grad_q
        )
        low_q = (g_ref[rows, :] + grad_norm).astype(bf16)
        gq_ref[rows, :] = low_q
        placed_q_ref[rows, :] = low_q.astype(f32)
        io.send(gq_ref, rows)
        io.send(placed_q_ref, rows)
        gln_ref[0:1, :] += grad_gain
        gln_ref[1:2, :] += grad_shift
        grad_norm, grad_gain, grad_shift = norm_backward(
            xc_ref[rows, :].astype(f32), norms_ref[2:3], grad_kv
        )
        low_c = grad_norm.astype(bf16)
        gc_ref[rows, :] = low_c
        placed_c_ref[rows, :] = low_c.astype(f32)
        io.send(gc_ref, rows)
        io.send(placed_c_ref, rows)
        gln_ref[2:3, :] += grad_gain
        gln_ref[3:4, :] += grad_shift
        return carry

    lax.fori_loop(0, TILES, tile, 0)


def place_rows(meta, *refs):
    count = len(refs) // 3
    for n in range(count):
        refs[2 * count + n][...] = refs[n][...].astype(refs[2 * count + n].dtype)


GROUP = 8


def join(own, other, rows):
    return (own[rows, :].astype(f32) + other[rows, :].astype(f32)).astype(bf16)


def join_halves(meta, own, other, keep, send):
    y = lax.rem(meta[35], 2)
    size = keep.shape[0]
    keep[...] = join(own, other, rows_of(y, size))
    send[...] = join(own, other, rows_of(1 - y, size))


def join_chunks(kept, arrived, send, first):
    size = kept.shape[0] // 4
    for z in range(4):
        rows = slice(size * z, size * z + size)
        send[z, first : first + size, :] = join(kept, arrived, rows)


def add_up(parts, first, size):
    total = parts[0, first : first + size, :].astype(f32)
    for z in range(1, 4):
        total = total + parts[z, first : first + size, :].astype(f32)
    return total.astype(bf16)


def half_of(parts, first, half):
    size = half.shape[0] // 4
    for z in range(4):
        half[size * z : size * z + size, :] = parts[z, first : first + size, :]


def slot_1(meta, ffn_own, ffn_other, keep, send):
    join_halves(meta, ffn_own, ffn_other, keep, send)


def slot_2(meta, ffn_kept, ffn_arrived, cross_own, cross_other, ffn_send, keep, send):
    join_chunks(ffn_kept, ffn_arrived, ffn_send, 0)
    join_halves(meta, cross_own, cross_other, keep, send)


def slot_3(
    meta, ffn_parts, cross_kept, cross_arrived, self_own, self_other,
    message, self_keep, self_send,
):
    join_halves(meta, self_own, self_other, self_keep, self_send)
    size = ffn_parts.shape[1]
    total = add_up(ffn_parts, 0, size)
    for z in range(4):
        message[z, 0:size, :] = total
    join_chunks(cross_kept, cross_arrived, message, size)


def slot_4(meta, parts, self_kept, self_arrived, ffn_half, message):
    size = ffn_half.shape[0] // 4
    half_of(parts, 0, ffn_half)
    total = add_up(parts, size, parts.shape[1] - size)
    join_chunks(self_kept, self_arrived, message, 0)
    for z in range(4):
        message[z, self_kept.shape[0] // 4 :, :] = total


def slot_5(meta, parts, gln_own, gln_other, send, cross_half):
    size = cross_half.shape[0] // 4
    half_of(parts, parts.shape[1] - size, cross_half)
    size = parts.shape[1] - size
    total = add_up(parts, 0, size)
    gln = gln_own[...] + gln_other[...]
    gln = jnp.concatenate([gln, jnp.zeros((8, D), f32)], axis=0).astype(bf16)
    for r in range(GROUP):
        send[r, 0:size, :] = total
        send[r, size : size + 16, :] = gln


def unpack_attention(whole_ref, outs):
    for i in range(3):
        outs[i][...] = whole_ref[:, 128 * i : 128 * i + 128].astype(f32)
    for j in range(4):
        rows = slice(128 * j, 128 * j + 128)
        outs[3][:, rows] = whole_ref[rows, 384:512].astype(f32)


def unpack_early(meta, ffn_half, ffn_arrived, cross_half, cross_arrived, *refs):
    *outs, cross_whole, ffn_whole = refs
    y = lax.rem(meta[35], 2)
    cross_whole[rows_of(y, 256), :] = cross_half[...]
    cross_whole[rows_of(1 - y, 256), :] = cross_arrived[...]
    unpack_attention(cross_whole, outs[2:])
    ffn_whole[rows_of(y, 512), :] = ffn_half[...]
    ffn_whole[rows_of(1 - y, 512), :] = ffn_arrived[...]
    outs[0][...] = ffn_whole[0:512, :].astype(f32)
    outs[1][...] = ffn_whole[512:1024, :].astype(f32)


def unpack_late(meta, parts, *refs):
    *outs, gln, whole_ref = refs
    size = parts.shape[1] - 16
    total = parts[0, size : size + 16, :].astype(f32)
    for r in range(1, GROUP):
        total = total + parts[r, size : size + 16, :].astype(f32)
    gln[...] = total[0:8]
    for r in range(GROUP):
        first = size * (4 * (r % 2) + r // 2)
        whole_ref[first : first + size, :] = parts[r, 0:size, :]
    unpack_attention(whole_ref, outs)


def whole(shape):
    zeros = (0,) * len(shape)
    return pl.BlockSpec(shape, lambda d, meta: zeros)


def own_row(width):
    return pl.BlockSpec((SEQ, width), lambda d, meta: (meta[0], 0))


ANY = pl.BlockSpec(memory_space=pl.ANY)


def in_hbm(x):
    return pltpu.with_memory_space_constraint(x, pltpu.HBM)


probability_out = (pltpu.HBM((DOCS, 4, FAST_K, FAST_Q), bf16), None, ANY)
probability_scratch = [
    pltpu.VMEM((2, 2, 4, FAST_K, FAST_Q), bf16),
    pltpu.SemaphoreType.DMA((2,)),
]


class Copies:
    def __init__(self, meta):
        self.first = meta[0] * SEQ
        self.loads = {}
        self.tiles = []
        self.sends = []

    def load(self, stage, source, target, sems, own_row):
        if stage == "tiles":
            first = self.first if own_row else 0
            self.tiles.append((source, target, sems, first))
            return
        if own_row:
            source = source.at[pl.ds(pl.multiple_of(self.first, SEQ), SEQ)]
        copy = pltpu.make_async_copy(source, target, sems[0].at[sems[1], 0])
        self.loads.setdefault(stage, []).append(copy)

    def tile(self, entry, i):
        source, target, (sems, b), first = entry
        rows = pl.ds(pl.multiple_of(first + i * TILE, TILE), TILE)
        return pltpu.make_async_copy(source.at[rows], target.at[rows_of(i)], sems.at[b, i])

    def start(self):
        for copy in self.loads.get("now", []):
            copy.start()
        for i in range(TILES):
            for entry in self.tiles:
                self.tile(entry, i).start()
        for stage in ("soon", "late"):
            for copy in self.loads.get(stage, []):
                copy.start()

    def wait(self, stage):
        for copy in self.loads.pop(stage, []):
            copy.wait()

    def wait_rows(self, i):
        for entry in self.tiles:
            self.tile(entry, i).wait()

    def result(self, source, target, sem, own_row):
        self.sends.append([source, target, sem, own_row, False])

    def send(self, ref, rows=None):
        for entry in self.sends:
            source, target, sem, own_row, _ = entry
            if source is ref:
                entry[4] = True
                first = self.first if own_row else 0
                if rows is None:
                    size = source.shape[0]
                else:
                    source = source.at[rows]
                    first, size = first + rows.start, rows.size
                if rows is not None or own_row:
                    target = target.at[pl.ds(pl.multiple_of(first, size), size)]
                pltpu.make_async_copy(source, target, sem).start()

    def finish(self):
        for stage in list(self.loads):
            self.wait(stage)
        for source, _, _, _, started in self.sends:
            if not started:
                self.send(source)
        for source, target, sem, own_row, _ in self.sends:
            if own_row:
                target = target.at[pl.ds(pl.multiple_of(self.first, SEQ), SEQ)]
            pltpu.make_async_copy(source, target, sem).wait()


def out(shape, dtype, own_row=False):
    return (shape, dtype, own_row)


def call(kernel, name, operands, outs, scratch, flops, token=None):
    arrays = [operands[0][0]]
    in_specs, out_specs, out_shapes = [], [], []
    buffers = []
    loads = []
    for n, (x, how) in enumerate(operands[1:]):
        if isinstance(how, str):
            stage, _, row = how.partition("_")
            shape = ((SEQ,) + x.shape[1:]) if row else x.shape
            loads.append((n, stage, len(buffers), bool(row)))
            buffers.append(pltpu.VMEM(shape, x.dtype))
            arrays.append(in_hbm(x))
            in_specs.append(ANY)
        else:
            arrays.append(x)
            in_specs.append(how)
    results = []
    for n, (shape, dtype, how) in enumerate(outs):
        if isinstance(how, bool):
            results.append((n, len(buffers), how))
            buffers.append(pltpu.VMEM(shape, dtype))
            shape = ((2 * SEQ,) + shape[1:]) if how else shape
            out_shapes.append(pltpu.HBM(shape, dtype))
            out_specs.append(ANY)
        else:
            out_shapes.append(jax.ShapeDtypeStruct(shape, dtype) if dtype else shape)
            out_specs.append(how)
    n_in, n_out = len(in_specs), len(out_specs)
    if token is not None:
        arrays.append(token)
        in_specs.append(whole((8, 128)))
        out_specs.append(whole((8, 128)))
        out_shapes.append(jax.ShapeDtypeStruct((8, 128), f32))

    def body(meta, *refs):
        ins, refs = list(refs[:n_in]), refs[len(in_specs) - n_in + n_in :]
        results_out, refs = list(refs[:n_out]), refs[n_out:]
        if token is not None:
            token_out, refs = refs[0], refs[1:]
            token_out[...] = jnp.zeros_like(token_out)
        bufs, refs = refs[: len(buffers)], refs[len(buffers) :]
        rest = refs[: len(scratch)]
        copies = Copies(meta)
        if buffers:
            sems = refs[len(scratch)]
        for n, stage, b, row in loads:
            copies.load(stage, ins[n], bufs[b], (sems, b), row)
            ins[n] = bufs[b]
        for n, b, row in results:
            copies.result(bufs[b], results_out[n], sems.at[b, 0], row)
            results_out[n] = bufs[b]
        copies.start()
        copies.wait("now")
        if buffers:
            kernel(meta, copies, *ins, *results_out, *rest)
        else:
            kernel(meta, *ins, *results_out, *rest)
        copies.finish()

    moved = sum(x.size * x.dtype.itemsize for x in arrays[1:])
    sems = [pltpu.SemaphoreType.DMA((len(buffers), TILES))] if buffers else []
    return pl.pallas_call(
        body,
        name=name,
        grid_spec=pltpu.PrefetchScalarGridSpec(
            num_scalar_prefetch=1,
            grid=(1,),
            in_specs=in_specs,
            out_specs=out_specs,
            scratch_shapes=buffers + scratch + sems,
        ),
        out_shape=out_shapes,
        compiler_params=pltpu.CompilerParams(
            dimension_semantics=("arbitrary",), vmem_limit_bytes=50 * 1024 * 1024
        ),
        cost_estimate=pl.CostEstimate(
            flops=int(flops), bytes_accessed=int(moved), transcendentals=0
        ),
    )(*arrays)


def simple(kernel, name, meta, operands, outs, scratch=()):
    return pl.pallas_call(
        kernel,
        name=name,
        grid_spec=pltpu.PrefetchScalarGridSpec(
            num_scalar_prefetch=1,
            grid=(1,),
            in_specs=[whole(x.shape) for x in operands],
            out_specs=[whole(shape) for shape, _ in outs],
            scratch_shapes=scratch,
        ),
        out_shape=[jax.ShapeDtypeStruct(shape, dtype) for shape, dtype in outs],
        compiler_params=pltpu.CompilerParams(vmem_limit_bytes=16 * 1024 * 1024),
    )(meta, *operands)


def full(x):
    return (x, whole(x.shape))


def shards(
    query_stream,
    content_stream,
    memory,
    segment_ids,
    source_segments,
    context_rank,
    context_limit,
    padding,
    ln_query_gain,
    ln_query_bias,
    ln_content_gain,
    ln_content_bias,
    self_query,
    self_key,
    self_value,
    self_out,
    ln_cross_gain,
    ln_cross_bias,
    cross_query,
    cross_key,
    cross_value,
    cross_out,
    ln_ffn_gain,
    ln_ffn_bias,
    ffn_in,
    ffn_out,
    cotangent,
):
    core = lax.axis_index("heads") % 2

    def to_core(x):
        return lax.ppermute(x, "heads", [(h, h ^ 1) for h in range(4)])

    hold = lambda *xs: lax.optimization_barrier(xs)

    def to_chip(x):
        return lax.ppermute(x, "heads", [(h, h ^ 2) for h in range(4)])

    row = pl.BlockSpec((1, 8, 128), lambda d, core: (core[0], 0, 0))

    def token_row(x):
        return (in_hbm(x.reshape(2, 8, 128)), row)

    def fixed(x):
        zeros = (0,) * x.ndim
        return (in_hbm(x), pl.BlockSpec(x.shape, lambda d, core: zeros))

    prepared = [
        ((36,), jnp.int32, pl.BlockSpec(memory_space=pltpu.SMEM)),
        ((1, SEQ), f32, whole((1, SEQ))),
        ((1, SEQ), f32, whole((1, SEQ))),
        ((8, D), f32, whole((8, D))),
        ((D, D), bf16, whole((D, D))),
        ((D, D), bf16, whole((D, D))),
    ]
    gains = (
        ln_query_gain,
        ln_query_bias,
        ln_content_gain,
        ln_content_bias,
        ln_cross_gain,
        ln_cross_bias,
        ln_ffn_gain,
        ln_ffn_bias,
    )
    weights = (self_query, self_key, self_value, self_out)
    weights += (cross_query, cross_key, cross_value, cross_out)
    tokens = (segment_ids, source_segments, context_rank, context_limit, padding)
    meta, rank, limit, norms, ws0, wc0 = call(
        prepare,
        "prepare",
        [(jnp.stack([core, lax.axis_index("rows") % GROUP]).astype(jnp.int32), None)]
        + [token_row(x) for x in tokens]
        + [fixed(x.reshape(1, D)) for x in gains]
        + [fixed(x) for x in weights],
        prepared,
        [],
        0,
    )

    ws1 = to_core(ws0)
    ws2 = to_chip(ws0)
    wc1 = to_core(wc0)
    u0, v0 = ffn_in, ffn_out
    meta_in = (meta, None)

    heads_out = [out((SEQ, 256), bf16)] * 4

    def stream_out(dtype, own_row=False):
        return out((SEQ, D), dtype, own_row)

    def now(*xs):
        return [(x, "now") for x in xs]

    def soon(*xs):
        return [(x, "soon") for x in xs]

    def late(*xs):
        return [(x, "late") for x in xs]

    def small(*xs):
        return [(x, whole(x.shape)) for x in xs]

    limits = pltpu.VMEM((SEQ, 128), f32)
    pair_flops = 2 * SEQ * D * 768 + 2 * 2 * 4 * DOCS * FAST_Q * FAST_K * 256

    nq, nc, *first, token = call(
        self_first,
        "self_first",
        [meta_in, (query_stream, "tiles_row"), (content_stream, "tiles_row")]
        + small(rank, limit, norms)
        + now(ws0, ws1),
        [stream_out(bf16), stream_out(bf16)] + heads_out + [probability_out],
        [limits] + probability_scratch,
        pair_flops,
        jnp.zeros((8, 128), f32),
    )
    ws2, wc0, token = hold(ws2, wc0, token)
    ws3 = to_core(ws2)
    wc2 = to_chip(wc0)
    *second_heads, second, ncross, token = call(
        self_second,
        "self_second",
        [meta_in, (query_stream, "late_row")]
        + [(nq, "tiles"), (nc, "tiles")]
        + small(rank, limit, norms)
        + late(ws0, ws1)
        + now(ws2, ws3)
        + late(first[3]),
        heads_out + [probability_out, stream_out(f32), stream_out(bf16)],
        [limits] + probability_scratch,
        pair_flops + 2 * SEQ * D * D,
        token,
    )
    wc2, u0, v0, token = hold(wc2, u0, v0, token)
    wc3 = to_core(wc2)
    u2 = to_chip(u0)
    u1 = to_core(u0)
    *cross_heads, token = call(
        cross_first,
        "cross_first",
        [meta_in, (ncross, "tiles"), (memory, "tiles_row")] + now(wc0, wc1),
        heads_out + [probability_out],
        probability_scratch,
        pair_flops,
        token,
    )
    wc3, u2, v0, token = hold(wc3, u2, v0, token)
    u3 = to_core(u2)
    v2 = to_chip(v0)
    v1 = to_core(v0)
    *cross_heads_second, third, nffn, token = call(
        cross_second,
        "cross_second",
        [meta_in]
        + late(second)
        + [(ncross, "tiles"), (memory, "tiles_row")]
        + small(norms)
        + late(wc0, wc1)
        + now(wc2, wc3)
        + late(cross_heads[3]),
        heads_out + [probability_out, stream_out(f32), stream_out(bf16)],
        probability_scratch,
        pair_flops + 2 * SEQ * D * D,
        token,
    )
    u3, v2, token = hold(u3, v2, token)
    v3 = to_core(v2)
    grads_ln = ((8, D), f32, whole((8, D)))
    placed_output, output, g3, g3_low, gln_ffn, ffn_own, ffn_other, token = call(
        ffn_both,
        "ffn_both",
        [meta_in]
        + [(third, "tiles"), (nffn, "tiles"), (cotangent, "tiles_row")]
        + small(norms)
        + now(u0, u1, u2, u3, v0, v1, v2, v3),
        [
            stream_out(bf16, True),
            stream_out(bf16),
            stream_out(f32),
            stream_out(bf16),
            grads_ln,
            out((1024, D), bf16),
            out((1024, D), bf16),
        ],
        [pltpu.VMEM((SEQ, 1024), bf16), pltpu.VMEM((SEQ, 1024), bf16)],
        12 * SEQ * D * 2048,
        token,
    )

    row_count = lax.axis_size("rows")
    assert row_count % GROUP == 0

    def to_y(x):
        return lax.ppermute(x, "rows", [(r, r ^ 1) for r in range(row_count)])

    columns = [
        [first + 2 * z + y for z in range(4)]
        for first in range(0, row_count, GROUP)
        for y in range(2)
    ]

    def along_z(x):
        return lax.all_to_all(x, "rows", 0, 0, axis_index_groups=columns)

    def rows_out(*sizes):
        return [((n, D), bf16) for n in sizes]

    ffn_other = to_core(ffn_other)

    back_scratch = [pltpu.VMEM((SEQ, 256), bf16)] + [pltpu.VMEM((SEQ, 256), f32)] * 3
    back_scratch += probability_scratch
    pair_out = out((SEQ, 256), bf16)
    packed_outs = [out((D, D), bf16), out((D, D), bf16)]
    back_flops = 2 * SEQ * D * 256 + 4 * 2 * 4 * DOCS * FAST_Q * FAST_K * 256

    def head_inputs(natural, p):
        return soon(*natural) + [(in_hbm(p), ANY)]

    *cross_grads, cross_own, cross_other, token = call(
        functools.partial(attention_back_first, True),
        "cross_back_first",
        [meta_in]
        + [(g3_low, "tiles")]
        + late(ncross)
        + [(memory, "late_row")]
        + small(rank, limit)
        + now(wc0, wc1)
        + head_inputs(cross_heads[0:4], cross_heads[4]),
        [pair_out] * 3 + packed_outs,
        [limits] + back_scratch,
        back_flops + 2 * SEQ * D * 1024,
        token,
    )
    ffn_other, token = hold(ffn_other, token)
    ffn_keep, ffn_send = simple(slot_1, "slot_1", meta, [ffn_own, ffn_other], rows_out(512, 512))
    ffn_send, token = hold(ffn_send, token)
    ffn_arrived = to_y(ffn_send)
    cross_other = to_core(cross_other)
    g2, g2_low, placed_mem, grad_mem, gln_cross, token = call(
        cross_back_second,
        "cross_back_second",
        [meta_in]
        + [(g3_low, "tiles")]
        + late(g3, second)
        + small(norms)
        + late(wc0, wc1)
        + now(wc2, wc3)
        + late(*cross_grads)
        + head_inputs(cross_heads_second[0:4], cross_heads_second[4]),
        [stream_out(f32), stream_out(bf16), stream_out(f32, True), stream_out(bf16), grads_ln],
        back_scratch,
        back_flops + 2 * SEQ * D * 1536,
        token,
    )
    ffn_arrived, cross_other, token = hold(ffn_arrived, cross_other, token)
    ffn_send, cross_keep, cross_send = simple(
        slot_2,
        "slot_2",
        meta,
        [ffn_keep, ffn_arrived, cross_own, cross_other],
        [((4, 128, D), bf16)] + rows_out(256, 256),
    )
    ffn_send, cross_send, token = hold(ffn_send, cross_send, token)
    ffn_parts = along_z(ffn_send)
    cross_arrived = to_y(cross_send)

    *self_grads, self_own, self_other, token = call(
        functools.partial(attention_back_first, False),
        "self_back_first",
        [meta_in]
        + [(g2_low, "tiles")]
        + late(nq, nc)
        + small(rank, limit)
        + now(ws0, ws1)
        + head_inputs(first[0:4], first[4]),
        [pair_out] * 3 + packed_outs,
        [limits] + back_scratch,
        back_flops + 2 * SEQ * D * 1024,
        token,
    )
    ffn_parts, cross_arrived, self_other, token = hold(
        ffn_parts, cross_arrived, self_other, token
    )
    self_other = to_core(self_other)
    message, self_keep, self_send = simple(
        slot_3,
        "slot_3",
        meta,
        [ffn_parts, cross_keep, cross_arrived, self_own, self_other],
        [((4, 192, D), bf16)] + rows_out(256, 256),
    )
    message, self_send, token = hold(message, self_send, token)
    self_arrived = to_y(self_send)
    parts = along_z(message)
    *self_grads_second, token = call(
        self_back_second,
        "self_back_second",
        [meta_in, (g2_low, "tiles")]
        + small(rank, limit)
        + now(ws2, ws3)
        + head_inputs(second_heads[0:4], second_heads[4]),
        [pair_out] * 3,
        [limits] + back_scratch,
        back_flops,
        token,
    )
    parts, self_arrived, token = hold(parts, self_arrived, token)
    ffn_half, message = simple(
        slot_4,
        "slot_4",
        meta,
        [parts, self_keep, self_arrived],
        rows_out(512) + [((4, 128, D), bf16)],
    )
    message, ffn_half, token = hold(message, ffn_half, token)
    parts = along_z(message)
    ffn_arrived = to_y(ffn_half)
    placed_q, placed_c, gq, gc, gln_self, token = call(
        self_back_finish,
        "self_back_finish",
        [meta_in, (g2, "tiles"), (query_stream, "tiles_row"), (content_stream, "tiles_row")]
        + small(norms)
        + now(ws0, ws1, ws2, ws3)
        + [(x, "tiles") for x in self_grads + self_grads_second],
        [stream_out(f32, True), stream_out(f32, True), stream_out(bf16), stream_out(bf16), grads_ln],
        [],
        2 * SEQ * D * 1536,
        token,
    )
    gln = jnp.concatenate([gln_self[0:4], gln_cross[0:2], gln_ffn[0:2]], axis=0)
    parts, ffn_arrived, gln = hold(parts, ffn_arrived, gln)
    last_send, cross_half = simple(
        slot_5,
        "slot_5",
        meta,
        [parts, gln, to_core(gln)],
        [((GROUP, 80, D), bf16), ((256, D), bf16)],
    )
    output, grad_mem, last_send = hold(output, grad_mem, last_send)
    groups = None
    if row_count > GROUP:
        groups = [list(range(r, r + GROUP)) for r in range(0, row_count, GROUP)]
    last_parts = lax.all_to_all(last_send, "rows", 0, 0, axis_index_groups=groups)
    cross_arrived = to_y(cross_half)

    def over_groups(totals):
        if row_count == GROUP:
            return totals
        groups = [list(range(r, row_count, GROUP)) for r in range(GROUP)]
        return lax.psum(totals, "rows", axis_index_groups=groups)

    def both_rows(placed_own, arrays, name):
        count = len(arrays)
        size = SEQ // 2
        one = pl.BlockSpec((size, D), lambda i, meta: (i, 0))
        block = pl.BlockSpec((size, D), lambda i, meta: (2 * (1 - meta[0]) + i, 0))
        return pl.pallas_call(
            place_rows,
            name=name,
            grid_spec=pltpu.PrefetchScalarGridSpec(
                num_scalar_prefetch=1,
                grid=(2,),
                in_specs=[one] * count + [pl.BlockSpec(memory_space=pl.ANY)] * count,
                out_specs=[block] * count,
            ),
            out_shape=[jax.ShapeDtypeStruct(x.shape, x.dtype) for x in placed_own],
            input_output_aliases={1 + count + n: n for n in range(count)},
        )(meta, *[to_core(x) for x in arrays], *placed_own)

    out_both, grad_mem_both = both_rows([placed_output, placed_mem], [output, grad_mem], "place_early")
    gq_both, gc_both = both_rows([placed_q, placed_c], [gq, gc], "place_late")

    cross_arrived, out_both, gq_both = hold(cross_arrived, out_both, gq_both)
    attention_outs = [((512, 128), f32)] * 3 + [((128, 512), f32)]
    grad_ffn_in, grad_ffn_out, *grad_cross_parts = simple(
        unpack_early,
        "unpack_early",
        meta,
        [ffn_half, ffn_arrived, cross_half, cross_arrived],
        [((D, D), f32)] * 2 + attention_outs,
        [pltpu.VMEM((D, D), bf16), pltpu.VMEM((2 * D, D), bf16)],
    )
    *grad_self_parts, gln = simple(
        unpack_late,
        "unpack_late",
        meta,
        [last_parts],
        attention_outs + [((8, D), f32)],
        [pltpu.VMEM((D, D), bf16)],
    )
    grad_ffn_in, grad_ffn_out, grad_cross_parts, grad_self_parts, gln = over_groups(
        (grad_ffn_in, grad_ffn_out, grad_cross_parts, grad_self_parts, gln)
    )
    return (
        out_both,
        gq_both,
        gc_both,
        grad_mem_both,
        gln[0],
        gln[1],
        gln[2],
        gln[3],
        *grad_self_parts,
        gln[4],
        gln[5],
        *grad_cross_parts,
        gln[6],
        gln[7],
        grad_ffn_in,
        grad_ffn_out,
    )


def solution(mesh):
    assert mesh.shape["heads"] == 4
    row_spec = P("rows", None)
    flat = P("rows")
    by_column = P(None, "heads")
    by_row = P("heads", None)
    attention = (by_column, by_column, by_column, by_row)
    in_specs = (
        (row_spec,) * 3
        + (flat,) * 5
        + (P(),) * 4
        + attention
        + (P(),) * 2
        + attention
        + (P(),) * 2
        + (by_column, by_row, row_spec)
    )
    out_specs = (
        (row_spec,) * 4
        + (P(),) * 4
        + attention
        + (P(),) * 2
        + attention
        + (P(),) * 2
        + (by_column, by_row)
    )
    return jax.shard_map(shards, mesh=mesh, in_specs=in_specs, out_specs=out_specs, check_vma=False)
```

```python
import functools

import jax
import jax.numpy as jnp
from jax import lax
from jax.experimental import pallas as pl
from jax.experimental.pallas import tpu as pltpu
from jax.sharding import PartitionSpec as P

HEAD_DIM = 64
SEQ = 1024
DOCS = 8
D = 512
TILE = 256
TILES = SEQ // TILE
FAST_Q = 256
FAST_K = 208
LONG_Q = 128
LONG_K = 640

norm_eps = 1e-05
masked_score = -1e30
hidden_rank = 1e6
gelu_root = 0.7978845608028654
gelu_cube = 0.044715

f32 = jnp.float32
bf16 = jnp.bfloat16


def dot(a, b):
    return lax.dot_general(a, b, (((1,), (0,)), ((), ())), preferred_element_type=f32)


def dot_nt(a, b):
    return lax.dot_general(a, b, (((1,), (1,)), ((), ())), preferred_element_type=f32)


def dot_tn(a, b):
    return lax.dot_general(a, b, (((0,), (0,)), ((), ())), preferred_element_type=f32)


def lanes(parts):
    return jnp.concatenate(parts, axis=1)


def layer_norm(values, gain, shift):
    centre = values - jnp.mean(values, axis=-1, keepdims=True)
    spread = jnp.mean(centre * centre, axis=-1, keepdims=True)
    return centre * lax.rsqrt(spread + norm_eps) * gain + shift


def norm_backward(values, gain, grad):
    centre = values - jnp.mean(values, axis=-1, keepdims=True)
    spread = jnp.mean(centre * centre, axis=-1, keepdims=True)
    scale = lax.rsqrt(spread + norm_eps)
    xhat = centre * scale
    eg = grad * gain
    mean_eg = jnp.mean(eg, axis=-1, keepdims=True)
    mean_egx = jnp.mean(eg * xhat, axis=-1, keepdims=True)
    grad_gain = jnp.sum(grad * xhat, axis=0, keepdims=True)
    grad_shift = jnp.sum(grad, axis=0, keepdims=True)
    return scale * (eg - mean_eg - xhat * mean_egx), grad_gain, grad_shift


def rows_of(i, size=TILE):
    return pl.ds(pl.multiple_of(i * size, size), size)


def w_query(ref):
    return ref[:, 0:128]


def w_key(ref):
    return ref[:, 128:256]


def w_value(ref):
    return ref[:, 256:384]


def w_out(ref):
    return lanes([ref[128 * j : 128 * j + 128, 384:512] for j in range(4)])


def half_masks():
    place = lax.broadcasted_iota(jnp.int32, (1, 128), 1)
    low = jnp.where(place < HEAD_DIM, 1.0, 0.0).astype(f32)
    return (low.astype(bf16), (1.0 - low).astype(bf16))


def doc_bounds(meta, d, source):
    base = 17 if source else 1
    return meta[base + d], meta[base + 8 + d]


def window_of(first, limit):
    return pl.multiple_of(jnp.minimum((first // 16) * 16, limit), 16)


def key_bias(ks, ke, k0, width):
    place = k0 + lax.broadcasted_iota(jnp.int32, (width, 128), 0)
    return jnp.where((place >= ks) & (place < ke), 0.0, masked_score)


def make_bias(rank_ref, limit_ref, ks, ke, q0, k0, span, width):
    if rank_ref is None:
        return lanes([key_bias(ks, ke, k0, width)] * (span // 128))
    place = k0 + lax.broadcasted_iota(jnp.int32, (width, 128), 0)
    ranks = rank_ref[pl.ds(k0, width), :]
    ranks = jnp.where((place < ks + 2) & (ranks < hidden_rank), -1.0, ranks)
    ranks = jnp.where((place >= ks) & (place < ke), ranks, hidden_rank)
    limits = jnp.broadcast_to(limit_ref[...], (8, SEQ))
    limits = pltpu.roll(limits, lax.rem(SEQ - q0, SEQ), 1)[0:1, 0:span]
    row = k0 + lax.broadcasted_iota(jnp.int32, (width, span), 0)
    column = q0 + lax.broadcasted_iota(jnp.int32, (width, span), 1)
    seen = (lanes([ranks] * (span // 128)) < limits) & (row != column)
    return jnp.where(seen, 0.0, masked_score)


TOGETHER = 4
STEPS = DOCS // TOGETHER


def is_fast(meta, cross):
    return meta[34 if cross else 33] == 1


def both_heads(x, masks):
    return jnp.concatenate([x * masks[0], x * masks[1]], axis=0)


def pair_probabilities(queries, keys, masks, bias):
    width = keys.shape[0]
    scores = dot_nt(both_heads(keys, masks), queries)
    result = []
    for a in range(2):
        part = scores[width * a : width * a + width] + bias
        part = jnp.exp(part - jnp.max(part, axis=0, keepdims=True))
        part = part * (1.0 / jnp.sum(part, axis=0, keepdims=True))
        result.append(part.astype(bf16))
    return result


def pair_product(rows, parts):
    across = jnp.transpose(rows)
    halves = [dot(across[64 * a : 64 * a + 64], part) for a, part in enumerate(parts)]
    return jnp.transpose(jnp.concatenate(halves, axis=0))


def for_docs(meta, cross, run, before, after):
    @pl.when(is_fast(meta, cross))
    def _():
        def step(i, carry):
            slot = lax.rem(i, 2)
            before(i, slot)
            for place in range(TOGETHER):
                d = TOGETHER * i + place
                ts, te = doc_bounds(meta, d, False)
                ks, ke = doc_bounds(meta, d, cross)
                q0 = window_of(ts, SEQ - FAST_Q)
                k0 = window_of(ks, SEQ - FAST_K)
                run(d, slot, place, q0, k0, FAST_Q, FAST_K, ts, te, ks, ke, True)
            after(i, slot)
            return carry

        lax.fori_loop(0, STEPS, step, 0)

    @pl.when(jnp.logical_not(is_fast(meta, cross)))
    def _():
        def doc(d, carry):
            ts, te = doc_bounds(meta, d, False)
            ks, ke = doc_bounds(meta, d, cross)
            base = (ts // 16) * 16
            k0 = window_of(ks, SEQ - LONG_K)

            def chunk(i, carry):
                lower = base + i * LONG_Q
                q0 = pl.multiple_of(jnp.minimum(lower, SEQ - LONG_Q), 16)
                low = jnp.maximum(ts, lower)
                high = jnp.minimum(te, lower + LONG_Q)
                run(d, None, None, q0, k0, LONG_Q, LONG_K, low, high, ks, ke, False)
                return carry

            return lax.fori_loop(0, (te - base + LONG_Q - 1) // LONG_Q, chunk, carry)

        lax.fori_loop(0, DOCS, doc, 0)


def attend_docs(meta, cross, rank_ref, limit_ref, halves, p_ref, p_buf, p_sem):
    pairs = 2 * len(halves)
    masks = half_masks()

    def save(i, slot):
        return pltpu.make_async_copy(p_buf.at[slot], p_ref.at[pl.ds(TOGETHER * i, TOGETHER)], p_sem.at[slot])

    def before(i, slot):
        @pl.when(i >= 2)
        def _():
            save(i - 2, slot).wait()

    def after(i, slot):
        save(i, slot).start()

    def run(d, slot, place, q0, k0, span, width, low, high, ks, ke, fast):
        bias = make_bias(rank_ref, limit_ref, ks, ke, q0, k0, span, width)
        row = q0 + lax.broadcasted_iota(jnp.int32, (span, 128), 0)
        inside = (row >= low) & (row < high)
        for n in range(pairs):
            q_ref, k_ref, v_ref, mixed_ref = halves[n // 2]
            cols = slice(128 * (n % 2), 128 * (n % 2) + 128)
            queries = q_ref[pl.ds(q0, span), cols]
            keys = k_ref[pl.ds(k0, width), cols]
            values = v_ref[pl.ds(k0, width), cols]
            parts = pair_probabilities(queries, keys, masks, bias)
            if fast:
                for a in range(2):
                    p_buf[slot, place, 2 * n + a] = parts[a]
            mixed = pair_product(values, parts)
            old = mixed_ref[pl.ds(q0, span), cols].astype(f32)
            mixed_ref[pl.ds(q0, span), cols] = jnp.where(inside, mixed, old).astype(bf16)

    for_docs(meta, cross, run, before, after)

    @pl.when(is_fast(meta, cross))
    def _():
        for i in range(STEPS - 2, STEPS):
            save(i, i % 2).wait()


def load_step(load, i, slot):
    p_ref, p_buf, p_sem = load
    return pltpu.make_async_copy(p_ref.at[pl.ds(TOGETHER * i, TOGETHER)], p_buf.at[slot], p_sem.at[slot])


def start_load(meta, cross, load):
    @pl.when(is_fast(meta, cross))
    def _():
        load_step(load, 0, 0).start()


def attend_docs_back(
    meta, cross, rank_ref, limit_ref, q_ref, k_ref, v_ref, mixed_ref, dm_ref,
    dq_ref, dk_ref, dv_ref, load,
):
    pairs = q_ref.shape[1] // 128
    masks = half_masks()
    p_buf = load[1]

    def before(i, slot):
        @pl.when(i + 1 < STEPS)
        def _():
            load_step(load, i + 1, 1 - slot).start()

        load_step(load, i, slot).wait()

    def after(i, slot):
        pass

    def run(d, slot, place, q0, k0, span, width, low, high, ks, ke, fast):
        row = q0 + lax.broadcasted_iota(jnp.int32, (span, 128), 0)
        inside = (row >= low) & (row < high)
        ones = jnp.ones((width, 128), bf16)
        if not fast:
            bias = make_bias(rank_ref, limit_ref, ks, ke, q0, k0, span, width)
        for n in range(pairs):
            cols = slice(128 * n, 128 * n + 128)
            queries = q_ref[pl.ds(q0, span), cols]
            keys = k_ref[pl.ds(k0, width), cols]
            values = v_ref[pl.ds(k0, width), cols]
            mixed = mixed_ref[pl.ds(q0, span), cols].astype(f32)
            grad = jnp.where(inside, dm_ref[pl.ds(q0, span), cols].astype(f32), 0.0)
            low_grad = grad.astype(bf16)
            left = lanes([low_grad, (-(grad * mixed)).astype(bf16)])
            delta = dot_nt(both_heads(lanes([values, ones]), [lanes([m, m]) for m in masks]), left)
            if fast:
                parts = [p_buf[slot, place, 2 * n + a] for a in range(2)]
            else:
                parts = pair_probabilities(queries, keys, masks, bias)
            slopes = []
            dk = dv = None
            for a in range(2):
                slope = parts[a].astype(f32) * delta[width * a : width * a + width]
                slopes.append(slope.astype(bf16))
                dk_a = dot(slopes[a], queries * masks[a])
                dv_a = dot(parts[a], low_grad * masks[a])
                dk = dk_a if dk is None else dk + dk_a
                dv = dv_a if dv is None else dv + dv_a
            dq = pair_product(keys, slopes)
            dq_ref[pl.ds(q0, span), cols] += dq * (HEAD_DIM**-0.5)
            dk_ref[pl.ds(k0, width), cols] += dk
            dv_ref[pl.ds(k0, width), cols] += dv

    for_docs(meta, cross, run, before, after)


def spread_ranks(rank_row_ref, rank_ref):
    rank_ref[...] = jnp.transpose(jnp.broadcast_to(rank_row_ref[...], (128, SEQ)))


def prepare(
    core, seg_ref, src_ref, rank_ref, limit_ref, pad_ref,
    n0, n1, n2, n3, n4, n5, n6, n7, sq, sk, sv, so, cq, ck, cv, co,
    meta_ref, ranks_ref, limits_ref, norms_ref, ws_ref, wc_ref,
):
    meta_ref[0] = core[0]
    meta_ref[35] = core[1]
    for base, ref in ((1, seg_ref), (17, src_ref)):
        ids = ref[0]
        meta_ref[base] = 0
        meta_ref[base + 15] = SEQ
        for d in range(1, DOCS):
            cut = jnp.sum(jnp.where(ids < d, 1.0, 0.0)).astype(jnp.int32)
            meta_ref[base + d] = cut
            meta_ref[base + 7 + d] = cut
    for place, base in ((33, 1), (34, 17)):
        fast = jnp.int32(1)
        for d in range(DOCS):
            q0 = window_of(meta_ref[1 + d], SEQ - FAST_Q)
            k0 = window_of(meta_ref[base + d], SEQ - FAST_K)
            fits = (meta_ref[9 + d] - q0 <= FAST_Q) & (meta_ref[base + 8 + d] - k0 <= FAST_K)
            fast = fast & fits.astype(jnp.int32)
        meta_ref[place] = fast
    ranks = jnp.where(pad_ref[0] != 0, hidden_rank, rank_ref[0].astype(f32))
    limits = limit_ref[0].astype(f32)
    for i in range(8):
        ranks_ref[0:1, 128 * i : 128 * i + 128] = ranks[i : i + 1]
        limits_ref[0:1, 128 * i : 128 * i + 128] = limits[i : i + 1]
    for i, ref in enumerate((n0, n1, n2, n3, n4, n5, n6, n7)):
        norms_ref[i : i + 1, :] = ref[...]
    for to, parts, out in ((ws_ref, (sq, sk, sv), so), (wc_ref, (cq, ck, cv), co)):
        for i, part in enumerate(parts):
            to[:, 128 * i : 128 * i + 128] = part[...]
        for j in range(4):
            to[128 * j : 128 * j + 128, 384:512] = out[:, 128 * j : 128 * j + 128]


def self_first(
    meta, io, xq_ref, xc_ref, rank_row_ref, limit_ref, norms_ref, w0_ref, w1_ref,
    nq_ref, nc_ref, q_ref, k_ref, v_ref, mixed_ref, p_ref, rank_ref, p_buf, p_sem,
):

    spread_ranks(rank_row_ref, rank_ref)
    wq = lanes([w_query(w0_ref), w_query(w1_ref)])
    wkv = lanes([w_key(w0_ref), w_key(w1_ref), w_value(w0_ref), w_value(w1_ref)])

    def tile(i, carry):
        rows = rows_of(i)
        io.wait_rows(i)
        nq = layer_norm(xq_ref[rows, :].astype(f32), norms_ref[0:1], norms_ref[1:2]).astype(bf16)
        nc = layer_norm(xc_ref[rows, :].astype(f32), norms_ref[2:3], norms_ref[3:4]).astype(bf16)
        nq_ref[rows, :] = nq
        nc_ref[rows, :] = nc
        q_ref[rows, :] = (dot(nq, wq) * (HEAD_DIM**-0.5)).astype(bf16)
        kv = dot(nc, wkv).astype(bf16)
        k_ref[rows, :] = kv[:, :256]
        v_ref[rows, :] = kv[:, 256:]
        return carry

    lax.fori_loop(0, TILES, tile, 0)

    for ref in (nq_ref, nc_ref, q_ref, k_ref, v_ref):
        io.send(ref)
    attend_docs(meta, False, rank_ref, limit_ref, [(q_ref, k_ref, v_ref, mixed_ref)], p_ref, p_buf, p_sem)


def self_second(
    meta, io, xq_ref, nq_ref, nc_ref, rank_row_ref, limit_ref, norms_ref, w0_ref, w1_ref, w2_ref, w3_ref,
    mixed_first_ref,
    q_ref, k_ref, v_ref, mixed_ref, p_ref, second_ref, ncross_ref, rank_ref, p_buf, p_sem,
):

    spread_ranks(rank_row_ref, rank_ref)
    wq = lanes([w_query(w2_ref), w_query(w3_ref)])
    wkv = lanes([w_key(w2_ref), w_key(w3_ref), w_value(w2_ref), w_value(w3_ref)])

    def tile(i, carry):
        rows = rows_of(i)
        io.wait_rows(i)
        q_ref[rows, :] = (dot(nq_ref[rows, :], wq) * (HEAD_DIM**-0.5)).astype(bf16)
        kv = dot(nc_ref[rows, :], wkv).astype(bf16)
        k_ref[rows, :] = kv[:, :256]
        v_ref[rows, :] = kv[:, 256:]
        return carry

    lax.fori_loop(0, TILES, tile, 0)

    for ref in (q_ref, k_ref, v_ref):
        io.send(ref)
    attend_docs(meta, False, rank_ref, limit_ref, [(q_ref, k_ref, v_ref, mixed_ref)], p_ref, p_buf, p_sem)

    io.send(mixed_ref)
    io.wait("late")
    out_first = jnp.concatenate([w_out(w0_ref), w_out(w1_ref)], axis=0)
    out_second = jnp.concatenate([w_out(w2_ref), w_out(w3_ref)], axis=0)

    def tile(i, carry):
        rows = rows_of(i)
        branch = dot(mixed_first_ref[rows, :], out_first) + dot(mixed_ref[rows, :], out_second)
        second = xq_ref[rows, :].astype(f32) + branch
        second_ref[rows, :] = second
        io.send(second_ref, rows)
        ncross_ref[rows, :] = layer_norm(second, norms_ref[4:5], norms_ref[5:6]).astype(bf16)
        io.send(ncross_ref, rows)
        return carry

    lax.fori_loop(0, TILES, tile, 0)


def project_cross(io, ncross_ref, memory_ref, weights, q_ref, k_ref, v_ref):
    wq = lanes([w_query(w) for w in weights])
    wkv = lanes([w_key(w) for w in weights] + [w_value(w) for w in weights])

    def tile(i, carry):
        rows = rows_of(i)
        io.wait_rows(i)
        q_ref[rows, :] = (dot(ncross_ref[rows, :], wq) * (HEAD_DIM**-0.5)).astype(bf16)
        kv = dot(memory_ref[rows, :], wkv).astype(bf16)
        k_ref[rows, :] = kv[:, :256]
        v_ref[rows, :] = kv[:, 256:]
        return carry

    lax.fori_loop(0, TILES, tile, 0)
    for ref in (q_ref, k_ref, v_ref):
        io.send(ref)


def cross_first(
    meta, io, ncross_ref, memory_ref, w0_ref, w1_ref,
    q_ref, k_ref, v_ref, mixed_ref, p_ref, p_buf, p_sem,
):
    project_cross(io, ncross_ref, memory_ref, (w0_ref, w1_ref), q_ref, k_ref, v_ref)
    attend_docs(meta, True, None, None, [(q_ref, k_ref, v_ref, mixed_ref)], p_ref, p_buf, p_sem)


def cross_second(
    meta, io, second_ref, ncross_ref, memory_ref, norms_ref, w0_ref, w1_ref, w2_ref, w3_ref,
    mixed_first_ref,
    q_ref, k_ref, v_ref, mixed_ref, p_ref, third_ref, nffn_ref, p_buf, p_sem,
):
    project_cross(io, ncross_ref, memory_ref, (w2_ref, w3_ref), q_ref, k_ref, v_ref)
    attend_docs(meta, True, None, None, [(q_ref, k_ref, v_ref, mixed_ref)], p_ref, p_buf, p_sem)
    io.send(mixed_ref)
    io.wait("late")
    out_first = jnp.concatenate([w_out(w0_ref), w_out(w1_ref)], axis=0)
    out_second = jnp.concatenate([w_out(w2_ref), w_out(w3_ref)], axis=0)

    def tile(i, carry):
        rows = rows_of(i)
        branch = dot(mixed_first_ref[rows, :], out_first) + dot(mixed_ref[rows, :], out_second)
        third = second_ref[rows, :] + branch
        third_ref[rows, :] = third
        io.send(third_ref, rows)
        nffn_ref[rows, :] = layer_norm(third, norms_ref[6:7], norms_ref[7:8]).astype(bf16)
        io.send(nffn_ref, rows)
        return carry

    lax.fori_loop(0, TILES, tile, 0)


def ffn_both(
    meta, io, third_ref, nffn_ref, cot_ref, norms_ref, u0_ref, u1_ref, u2_ref, u3_ref,
    w0_ref, w1_ref, w2_ref, w3_ref,
    placed_ref, out_ref, g3_ref, g3_low_ref, gln_ref, own_ref, other_ref, hidden_ref, before_ref,
):
    gln_ref[...] = jnp.zeros_like(gln_ref)
    in_refs = (u0_ref, u1_ref, u2_ref, u3_ref)

    def tile(i, carry):
        rows = rows_of(i)
        io.wait_rows(i)
        nffn = nffn_ref[rows, :]
        cot = cot_ref[rows, :]
        outs = []
        grads = []
        for g, w_ref in enumerate((w0_ref, w1_ref, w2_ref, w3_ref)):
            w_in = in_refs[g][...]
            w_out_rows = w_ref[...]
            x = dot(nffn, w_in)
            square = x * x
            half = 0.5 + 0.5 * jnp.tanh(x * (gelu_root + (gelu_root * gelu_cube) * square))
            value = x * half
            hidden = value.astype(bf16)
            rise = 2.0 * gelu_root + (6.0 * gelu_root * gelu_cube) * square
            slope = half + value * (1.0 - half) * rise
            grad_before = (dot_nt(cot, w_out_rows) * slope).astype(bf16)
            outs.append(dot(hidden, w_out_rows))
            grads.append(dot_nt(grad_before, w_in))
            if g < 2:
                hidden_ref[rows, 512 * g : 512 * g + 512] = hidden
                before_ref[rows, 512 * g : 512 * g + 512] = grad_before
        third = third_ref[rows, :]
        result = (third + ((outs[0] + outs[1]) + (outs[2] + outs[3]))).astype(bf16)
        out_ref[rows, :] = result
        placed_ref[rows, :] = result
        grad_normed = (grads[0] + grads[1]) + (grads[2] + grads[3])
        grad_norm, grad_gain, grad_shift = norm_backward(third, norms_ref[6:7], grad_normed)
        g3 = cot.astype(f32) + grad_norm
        g3_ref[rows, :] = g3
        g3_low_ref[rows, :] = g3.astype(bf16)
        gln_ref[0:1, :] += grad_gain
        gln_ref[1:2, :] += grad_shift
        for ref in (out_ref, placed_ref, g3_ref, g3_low_ref):
            io.send(ref, rows)
        return carry

    lax.fori_loop(0, TILES, tile, 0)
    part = dot_tn(nffn_ref[...], before_ref[...])
    own_ref[0:512, :] = part[:, 0:512].astype(bf16)
    other_ref[0:512, :] = part[:, 512:1024].astype(bf16)
    io.send(own_ref, pl.ds(0, 512))
    io.send(other_ref, pl.ds(0, 512))
    part = dot_tn(hidden_ref[...], cot_ref[...])
    own_ref[512:1024, :] = part[0:512].astype(bf16)
    other_ref[512:1024, :] = part[512:1024].astype(bf16)
    io.send(own_ref, pl.ds(512, 512))
    io.send(other_ref, pl.ds(512, 512))


def back_start(io, g_ref, mixed_ref, w_refs, dm_ref, dq_ref, dk_ref, dv_ref):
    out_rows = jnp.concatenate([w_out(w) for w in w_refs], axis=0)

    def tile(i, carry):
        rows = rows_of(i)
        io.wait_rows(i)
        dm_ref[rows, :] = dot_nt(g_ref[rows, :], out_rows).astype(bf16)
        zeros = jnp.zeros((TILE, 256), f32)
        dq_ref[rows, :] = zeros
        dk_ref[rows, :] = zeros
        dv_ref[rows, :] = zeros
        return carry

    lax.fori_loop(0, TILES, tile, 0)


def attention_back_first(
    cross, meta, io, g_ref, nq_ref, nkv_ref, rank_row_ref, limit_ref, w0_ref, w1_ref,
    q_ref, k_ref, v_ref, mixed_ref, p_ref,
    dq_ref, dk_ref, dv_ref, own_ref, other_ref,
    rank_ref, dm_ref, dqs_ref, dks_ref, dvs_ref, p_buf, p_sem,
):
    load = (p_ref, p_buf, p_sem)
    start_load(meta, cross, load)
    if not cross:
        spread_ranks(rank_row_ref, rank_ref)
    back_start(io, g_ref, mixed_ref, (w0_ref, w1_ref), dm_ref, dqs_ref, dks_ref, dvs_ref)

    io.wait("soon")
    attend_docs_back(
        meta, cross, None if cross else rank_ref, limit_ref, q_ref, k_ref, v_ref, mixed_ref,
        dm_ref, dqs_ref, dks_ref, dvs_ref, load,
    )

    dq_ref[...] = dqs_ref[...].astype(bf16)
    dk_ref[...] = dks_ref[...].astype(bf16)
    dv_ref[...] = dvs_ref[...].astype(bf16)
    for ref in (dq_ref, dk_ref, dv_ref):
        io.send(ref)
    io.wait("late")
    nq = nq_ref[...]
    nkv = nkv_ref[...]
    for n, part in enumerate(
        (dot_tn(nq, dq_ref[...]), dot_tn(nkv, dk_ref[...]), dot_tn(nkv, dv_ref[...]))
    ):
        own_ref[:, 128 * n : 128 * n + 128] = part[:, :128].astype(bf16)
        other_ref[:, 128 * n : 128 * n + 128] = part[:, 128:].astype(bf16)
    part = dot_tn(mixed_ref[...], g_ref[...])
    for j in range(4):
        rows = slice(128 * j, 128 * j + 128)
        own_ref[rows, 384:512] = part[:128, rows].astype(bf16)
        other_ref[rows, 384:512] = part[128:, rows].astype(bf16)


def back_second_docs(
    cross, meta, io, g_ref, rank_row_ref, limit_ref, w_refs, q_ref, k_ref, v_ref, mixed_ref, p_ref,
    rank_ref, dm_ref, dqs_ref, dks_ref, dvs_ref, p_buf, p_sem,
):
    load = (p_ref, p_buf, p_sem)
    start_load(meta, cross, load)
    if not cross:
        spread_ranks(rank_row_ref, rank_ref)
    back_start(io, g_ref, mixed_ref, w_refs, dm_ref, dqs_ref, dks_ref, dvs_ref)

    io.wait("soon")
    attend_docs_back(
        meta, cross, None if cross else rank_ref, limit_ref, q_ref, k_ref, v_ref, mixed_ref,
        dm_ref, dqs_ref, dks_ref, dvs_ref, load,
    )


def stream_grads(rows, first, second, firsts, seconds):
    dq, dk, dv = first
    dq2, dk2, dv2 = (ref[rows, :].astype(bf16) for ref in second)
    w0, w1 = firsts
    w2, w3 = seconds
    grad_q = dot_nt(dq[rows, :], lanes([w_query(w0), w_query(w1)])) + dot_nt(
        dq2, lanes([w_query(w2), w_query(w3)])
    )
    kv = lanes([dk[rows, :], dv[rows, :]])
    kv2 = lanes([dk2, dv2])
    grad_kv = dot_nt(kv, lanes([w_key(w0), w_key(w1), w_value(w0), w_value(w1)])) + dot_nt(
        kv2, lanes([w_key(w2), w_key(w3), w_value(w2), w_value(w3)])
    )
    return grad_q, grad_kv


def cross_back_second(
    meta, io, g_low_ref, g_ref, second_ref, norms_ref, w0_ref, w1_ref, w2_ref, w3_ref,
    dq_ref, dk_ref, dv_ref, q_ref, k_ref, v_ref, mixed_ref, p_ref,
    g2_ref, g2_low_ref, placed_ref, gmem_ref, gln_ref,
    dm_ref, dqs_ref, dks_ref, dvs_ref, p_buf, p_sem,
):
    back_second_docs(
        True, meta, io, g_low_ref, None, None, (w2_ref, w3_ref), q_ref, k_ref, v_ref, mixed_ref, p_ref,
        None, dm_ref, dqs_ref, dks_ref, dvs_ref, p_buf, p_sem,
    )

    io.wait("late")
    gln_ref[...] = jnp.zeros_like(gln_ref)

    def tile(i, carry):
        rows = rows_of(i)
        grad_q, grad_kv = stream_grads(
            rows,
            (dq_ref, dk_ref, dv_ref),
            (dqs_ref, dks_ref, dvs_ref),
            (w0_ref, w1_ref),
            (w2_ref, w3_ref),
        )
        low_kv = grad_kv.astype(bf16)
        gmem_ref[rows, :] = low_kv
        placed_ref[rows, :] = low_kv.astype(f32)
        io.send(gmem_ref, rows)
        io.send(placed_ref, rows)
        grad_norm, grad_gain, grad_shift = norm_backward(
            second_ref[rows, :], norms_ref[4:5], grad_q
        )
        g2 = g_ref[rows, :] + grad_norm
        g2_ref[rows, :] = g2
        g2_low_ref[rows, :] = g2.astype(bf16)
        io.send(g2_ref, rows)
        io.send(g2_low_ref, rows)
        gln_ref[0:1, :] += grad_gain
        gln_ref[1:2, :] += grad_shift
        return carry

    lax.fori_loop(0, TILES, tile, 0)


def self_back_second(
    meta, io, g_low_ref, rank_row_ref, limit_ref, w2_ref, w3_ref,
    q_ref, k_ref, v_ref, mixed_ref, p_ref,
    dq_ref, dk_ref, dv_ref,
    rank_ref, dm_ref, dqs_ref, dks_ref, dvs_ref, p_buf, p_sem,
):
    back_second_docs(
        False, meta, io, g_low_ref, rank_row_ref, limit_ref, (w2_ref, w3_ref), q_ref, k_ref, v_ref,
        mixed_ref, p_ref, rank_ref, dm_ref, dqs_ref, dks_ref, dvs_ref, p_buf, p_sem,
    )
    dq_ref[...] = dqs_ref[...].astype(bf16)
    dk_ref[...] = dks_ref[...].astype(bf16)
    dv_ref[...] = dvs_ref[...].astype(bf16)


def self_back_finish(
    meta, io, g_ref, xq_ref, xc_ref, norms_ref, w0_ref, w1_ref, w2_ref, w3_ref,
    dq_ref, dk_ref, dv_ref, dq2_ref, dk2_ref, dv2_ref,
    placed_q_ref, placed_c_ref, gq_ref, gc_ref, gln_ref,
):
    gln_ref[...] = jnp.zeros_like(gln_ref)

    def tile(i, carry):
        rows = rows_of(i)
        io.wait_rows(i)
        grad_q, grad_kv = stream_grads(
            rows,
            (dq_ref, dk_ref, dv_ref),
            (dq2_ref, dk2_ref, dv2_ref),
            (w0_ref, w1_ref),
            (w2_ref, w3_ref),
        )
        grad_norm, grad_gain, grad_shift = norm_backward(
            xq_ref[rows, :].astype(f32), norms_ref[0:1], grad_q
        )
        low_q = (g_ref[rows, :] + grad_norm).astype(bf16)
        gq_ref[rows, :] = low_q
        placed_q_ref[rows, :] = low_q.astype(f32)
        io.send(gq_ref, rows)
        io.send(placed_q_ref, rows)
        gln_ref[0:1, :] += grad_gain
        gln_ref[1:2, :] += grad_shift
        grad_norm, grad_gain, grad_shift = norm_backward(
            xc_ref[rows, :].astype(f32), norms_ref[2:3], grad_kv
        )
        low_c = grad_norm.astype(bf16)
        gc_ref[rows, :] = low_c
        placed_c_ref[rows, :] = low_c.astype(f32)
        io.send(gc_ref, rows)
        io.send(placed_c_ref, rows)
        gln_ref[2:3, :] += grad_gain
        gln_ref[3:4, :] += grad_shift
        return carry

    lax.fori_loop(0, TILES, tile, 0)


def place_rows(meta, *refs):
    count = len(refs) // 3
    for n in range(count):
        refs[2 * count + n][...] = refs[n][...].astype(refs[2 * count + n].dtype)


GROUP = 8


def position(meta):
    r = meta[35]
    return lax.rem(r, 2), r // 2


def join(own, other, rows):
    return (own[rows, :].astype(f32) + other[rows, :].astype(f32)).astype(bf16)


def join_halves(meta, own, other, keep, send):
    y, _ = position(meta)
    size = keep.shape[0]
    keep[...] = join(own, other, rows_of(y, size))
    send[...] = join(own, other, rows_of(1 - y, size))


def join_chunks(meta, kept, arrived, keep, sends):
    _, z = position(meta)
    size = keep.shape[0]
    keep[...] = join(kept, arrived, rows_of(z, size))
    for s, (send, first) in enumerate(sends, 1):
        send[first : first + size, :] = join(kept, arrived, rows_of(z ^ s, size))


def add_up(kept, parts, first):
    size = kept.shape[0]
    total = kept[...].astype(f32)
    for part in parts:
        total = total + part[first : first + size, :].astype(f32)
    return total.astype(bf16)


def half_of(meta, total, parts, first, half):
    _, z = position(meta)
    size = total.shape[0]
    half[rows_of(z, size), :] = total[...]
    for s, part in enumerate(parts, 1):
        half[rows_of(z ^ s, size), :] = part[first : first + size, :]


def slot_1(meta, ffn_own, ffn_other, keep, send):
    join_halves(meta, ffn_own, ffn_other, keep, send)


def slot_2(
    meta, ffn_kept, ffn_arrived, cross_own, cross_other, ffn_keep, f1, f2, f3, keep, send
):
    join_chunks(meta, ffn_kept, ffn_arrived, ffn_keep, [(f1, 0), (f2, 0), (f3, 0)])
    join_halves(meta, cross_own, cross_other, keep, send)


def slot_3(
    meta, ffn_kept, f1, f2, f3, cross_kept, cross_arrived, self_own, self_other,
    ffn_total, cross_keep, m1, m2, m3, self_keep, self_send,
):
    join_halves(meta, self_own, self_other, self_keep, self_send)
    total = add_up(ffn_kept, (f1, f2, f3), 0)
    ffn_total[...] = total
    size = total.shape[0]
    join_chunks(meta, cross_kept, cross_arrived, cross_keep, [(m, size) for m in (m1, m2, m3)])
    for m in (m1, m2, m3):
        m[0:size, :] = total


def slot_4(
    meta, ffn_total, m1, m2, m3, cross_kept, self_kept, self_arrived,
    ffn_half, cross_total, self_keep, *sends,
):
    join_chunks(meta, self_kept, self_arrived, self_keep, [(send, 0) for send in sends])
    total = add_up(cross_kept, (m1, m2, m3), ffn_total.shape[0])
    cross_total[...] = total
    size = total.shape[0]
    for send in sends:
        send[size:, :] = total
    half_of(meta, ffn_total, (m1, m2, m3), 0, ffn_half)


def slot_5(meta, self_kept, cross_total, m1, m2, m3, gln_own, gln_other, send, cross_half):
    size = self_kept.shape[0]
    total = add_up(self_kept, (m1, m2, m3), 0)
    gln = gln_own[...] + gln_other[...]
    gln = jnp.concatenate([gln, jnp.zeros((8, D), f32)], axis=0).astype(bf16)
    for r in range(GROUP):
        send[r, 0:size, :] = total
        send[r, size : size + 16, :] = gln
    half_of(meta, cross_total, (m1, m2, m3), size, cross_half)


def unpack_attention(whole_ref, outs):
    for i in range(3):
        outs[i][...] = whole_ref[:, 128 * i : 128 * i + 128].astype(f32)
    for j in range(4):
        rows = slice(128 * j, 128 * j + 128)
        outs[3][:, rows] = whole_ref[rows, 384:512].astype(f32)


def unpack_early(meta, ffn_half, ffn_arrived, cross_half, cross_arrived, *refs):
    *outs, cross_whole, ffn_whole = refs
    y, _ = position(meta)
    cross_whole[rows_of(y, 256), :] = cross_half[...]
    cross_whole[rows_of(1 - y, 256), :] = cross_arrived[...]
    unpack_attention(cross_whole, outs[2:])
    ffn_whole[rows_of(y, 512), :] = ffn_half[...]
    ffn_whole[rows_of(1 - y, 512), :] = ffn_arrived[...]
    outs[0][...] = ffn_whole[0:512, :].astype(f32)
    outs[1][...] = ffn_whole[512:1024, :].astype(f32)


def unpack_late(meta, parts, *refs):
    *outs, gln, whole_ref = refs
    size = parts.shape[1] - 16
    total = parts[0, size : size + 16, :].astype(f32)
    for r in range(1, GROUP):
        total = total + parts[r, size : size + 16, :].astype(f32)
    gln[...] = total[0:8]
    for r in range(GROUP):
        first = size * (4 * (r % 2) + r // 2)
        whole_ref[first : first + size, :] = parts[r, 0:size, :]
    unpack_attention(whole_ref, outs)


def whole(shape):
    zeros = (0,) * len(shape)
    return pl.BlockSpec(shape, lambda d, meta: zeros)


def own_row(width):
    return pl.BlockSpec((SEQ, width), lambda d, meta: (meta[0], 0))


ANY = pl.BlockSpec(memory_space=pl.ANY)


def in_hbm(x):
    return pltpu.with_memory_space_constraint(x, pltpu.HBM)


probability_out = (pltpu.HBM((DOCS, 4, FAST_K, FAST_Q), bf16), None, ANY)
probability_scratch = [
    pltpu.VMEM((2, TOGETHER, 4, FAST_K, FAST_Q), bf16),
    pltpu.SemaphoreType.DMA((2,)),
]


class Copies:
    def __init__(self, meta):
        self.first = meta[0] * SEQ
        self.loads = {}
        self.tiles = []
        self.sends = []

    def load(self, stage, source, target, sems, own_row):
        if stage == "tiles":
            first = self.first if own_row else 0
            self.tiles.append((source, target, sems, first))
            return
        if own_row:
            source = source.at[pl.ds(pl.multiple_of(self.first, SEQ), SEQ)]
        copy = pltpu.make_async_copy(source, target, sems[0].at[sems[1], 0])
        self.loads.setdefault(stage, []).append(copy)

    def tile(self, entry, i):
        source, target, (sems, b), first = entry
        rows = pl.ds(pl.multiple_of(first + i * TILE, TILE), TILE)
        return pltpu.make_async_copy(source.at[rows], target.at[rows_of(i)], sems.at[b, i])

    def start(self):
        for copy in self.loads.get("now", []):
            copy.start()
        for i in range(TILES):
            for entry in self.tiles:
                self.tile(entry, i).start()
        for stage in ("soon", "late"):
            for copy in self.loads.get(stage, []):
                copy.start()

    def wait(self, stage):
        for copy in self.loads.pop(stage, []):
            copy.wait()

    def wait_rows(self, i):
        for entry in self.tiles:
            self.tile(entry, i).wait()

    def result(self, source, target, sem, own_row):
        self.sends.append([source, target, sem, own_row, False])

    def send(self, ref, rows=None):
        for entry in self.sends:
            source, target, sem, own_row, _ = entry
            if source is ref:
                entry[4] = True
                first = self.first if own_row else 0
                if rows is None:
                    size = source.shape[0]
                else:
                    source = source.at[rows]
                    first, size = first + rows.start, rows.size
                if rows is not None or own_row:
                    target = target.at[pl.ds(pl.multiple_of(first, size), size)]
                pltpu.make_async_copy(source, target, sem).start()

    def finish(self):
        for stage in list(self.loads):
            self.wait(stage)
        for source, _, _, _, started in self.sends:
            if not started:
                self.send(source)
        for source, target, sem, own_row, _ in self.sends:
            if own_row:
                target = target.at[pl.ds(pl.multiple_of(self.first, SEQ), SEQ)]
            pltpu.make_async_copy(source, target, sem).wait()


def out(shape, dtype, own_row=False):
    return (shape, dtype, own_row)


def call(kernel, name, operands, outs, scratch, flops, token=None):
    arrays = [operands[0][0]]
    in_specs, out_specs, out_shapes = [], [], []
    buffers = []
    loads = []
    for n, (x, how) in enumerate(operands[1:]):
        if isinstance(how, str):
            stage, _, row = how.partition("_")
            shape = ((SEQ,) + x.shape[1:]) if row else x.shape
            loads.append((n, stage, len(buffers), bool(row)))
            buffers.append(pltpu.VMEM(shape, x.dtype))
            arrays.append(in_hbm(x))
            in_specs.append(ANY)
        else:
            arrays.append(x)
            in_specs.append(how)
    results = []
    for n, (shape, dtype, how) in enumerate(outs):
        if isinstance(how, bool):
            results.append((n, len(buffers), how))
            buffers.append(pltpu.VMEM(shape, dtype))
            shape = ((2 * SEQ,) + shape[1:]) if how else shape
            out_shapes.append(pltpu.HBM(shape, dtype))
            out_specs.append(ANY)
        else:
            out_shapes.append(jax.ShapeDtypeStruct(shape, dtype) if dtype else shape)
            out_specs.append(how)
    n_in, n_out = len(in_specs), len(out_specs)
    if token is not None:
        arrays.append(token)
        in_specs.append(whole((8, 128)))
        out_specs.append(whole((8, 128)))
        out_shapes.append(jax.ShapeDtypeStruct((8, 128), f32))

    def body(meta, *refs):
        ins, refs = list(refs[:n_in]), refs[len(in_specs) - n_in + n_in :]
        results_out, refs = list(refs[:n_out]), refs[n_out:]
        if token is not None:
            token_out, refs = refs[0], refs[1:]
            token_out[...] = jnp.zeros_like(token_out)
        bufs, refs = refs[: len(buffers)], refs[len(buffers) :]
        rest = refs[: len(scratch)]
        copies = Copies(meta)
        if buffers:
            sems = refs[len(scratch)]
        for n, stage, b, row in loads:
            copies.load(stage, ins[n], bufs[b], (sems, b), row)
            ins[n] = bufs[b]
        for n, b, row in results:
            copies.result(bufs[b], results_out[n], sems.at[b, 0], row)
            results_out[n] = bufs[b]
        copies.start()
        copies.wait("now")
        if buffers:
            kernel(meta, copies, *ins, *results_out, *rest)
        else:
            kernel(meta, *ins, *results_out, *rest)
        copies.finish()

    moved = sum(x.size * x.dtype.itemsize for x in arrays[1:])
    sems = [pltpu.SemaphoreType.DMA((len(buffers), TILES))] if buffers else []
    return pl.pallas_call(
        body,
        name=name,
        grid_spec=pltpu.PrefetchScalarGridSpec(
            num_scalar_prefetch=1,
            grid=(1,),
            in_specs=in_specs,
            out_specs=out_specs,
            scratch_shapes=buffers + scratch + sems,
        ),
        out_shape=out_shapes,
        compiler_params=pltpu.CompilerParams(
            dimension_semantics=("arbitrary",), vmem_limit_bytes=50 * 1024 * 1024
        ),
        cost_estimate=pl.CostEstimate(
            flops=int(flops), bytes_accessed=int(moved), transcendentals=0
        ),
    )(*arrays)


def simple(kernel, name, meta, operands, outs, scratch=()):
    return pl.pallas_call(
        kernel,
        name=name,
        grid_spec=pltpu.PrefetchScalarGridSpec(
            num_scalar_prefetch=1,
            grid=(1,),
            in_specs=[whole(x.shape) for x in operands],
            out_specs=[whole(shape) for shape, _ in outs],
            scratch_shapes=scratch,
        ),
        out_shape=[jax.ShapeDtypeStruct(shape, dtype) for shape, dtype in outs],
        compiler_params=pltpu.CompilerParams(vmem_limit_bytes=16 * 1024 * 1024),
    )(meta, *operands)


def full(x):
    return (x, whole(x.shape))


def shards(
    query_stream,
    content_stream,
    memory,
    segment_ids,
    source_segments,
    context_rank,
    context_limit,
    padding,
    ln_query_gain,
    ln_query_bias,
    ln_content_gain,
    ln_content_bias,
    self_query,
    self_key,
    self_value,
    self_out,
    ln_cross_gain,
    ln_cross_bias,
    cross_query,
    cross_key,
    cross_value,
    cross_out,
    ln_ffn_gain,
    ln_ffn_bias,
    ffn_in,
    ffn_out,
    cotangent,
):
    core = lax.axis_index("heads") % 2

    def to_core(x):
        return lax.ppermute(x, "heads", [(h, h ^ 1) for h in range(4)])

    hold = lambda *xs: lax.optimization_barrier(xs)

    def to_chip(x):
        return lax.ppermute(x, "heads", [(h, h ^ 2) for h in range(4)])

    row = pl.BlockSpec((1, 8, 128), lambda d, core: (core[0], 0, 0))

    def token_row(x):
        return (in_hbm(x.reshape(2, 8, 128)), row)

    def fixed(x):
        zeros = (0,) * x.ndim
        return (in_hbm(x), pl.BlockSpec(x.shape, lambda d, core: zeros))

    prepared = [
        ((36,), jnp.int32, pl.BlockSpec(memory_space=pltpu.SMEM)),
        ((1, SEQ), f32, whole((1, SEQ))),
        ((1, SEQ), f32, whole((1, SEQ))),
        ((8, D), f32, whole((8, D))),
        ((D, D), bf16, whole((D, D))),
        ((D, D), bf16, whole((D, D))),
    ]
    gains = (
        ln_query_gain,
        ln_query_bias,
        ln_content_gain,
        ln_content_bias,
        ln_cross_gain,
        ln_cross_bias,
        ln_ffn_gain,
        ln_ffn_bias,
    )
    weights = (self_query, self_key, self_value, self_out)
    weights += (cross_query, cross_key, cross_value, cross_out)
    tokens = (segment_ids, source_segments, context_rank, context_limit, padding)
    meta, rank, limit, norms, ws0, wc0 = call(
        prepare,
        "prepare",
        [(jnp.stack([core, lax.axis_index("rows") % GROUP]).astype(jnp.int32), None)]
        + [token_row(x) for x in tokens]
        + [fixed(x.reshape(1, D)) for x in gains]
        + [fixed(x) for x in weights],
        prepared,
        [],
        0,
    )

    ws1 = to_core(ws0)
    ws2 = to_chip(ws0)
    wc1 = to_core(wc0)
    u0, v0 = ffn_in, ffn_out
    meta_in = (meta, None)

    heads_out = [out((SEQ, 256), bf16)] * 4

    def stream_out(dtype, own_row=False):
        return out((SEQ, D), dtype, own_row)

    def now(*xs):
        return [(x, "now") for x in xs]

    def soon(*xs):
        return [(x, "soon") for x in xs]

    def late(*xs):
        return [(x, "late") for x in xs]

    def small(*xs):
        return [(x, whole(x.shape)) for x in xs]

    limits = pltpu.VMEM((SEQ, 128), f32)
    pair_flops = 2 * SEQ * D * 768 + 2 * 2 * 4 * DOCS * FAST_Q * FAST_K * 256

    nq, nc, *first, token = call(
        self_first,
        "self_first",
        [meta_in, (query_stream, "tiles_row"), (content_stream, "tiles_row")]
        + small(rank, limit, norms)
        + now(ws0, ws1),
        [stream_out(bf16), stream_out(bf16)] + heads_out + [probability_out],
        [limits] + probability_scratch,
        pair_flops,
        jnp.zeros((8, 128), f32),
    )
    ws2, wc0, token = hold(ws2, wc0, token)
    ws3 = to_core(ws2)
    wc2 = to_chip(wc0)
    *second_heads, second, ncross, token = call(
        self_second,
        "self_second",
        [meta_in, (query_stream, "late_row")]
        + [(nq, "tiles"), (nc, "tiles")]
        + small(rank, limit, norms)
        + late(ws0, ws1)
        + now(ws2, ws3)
        + late(first[3]),
        heads_out + [probability_out, stream_out(f32), stream_out(bf16)],
        [limits] + probability_scratch,
        pair_flops + 2 * SEQ * D * D,
        token,
    )
    wc2, u0, v0, token = hold(wc2, u0, v0, token)
    wc3 = to_core(wc2)
    u2 = to_chip(u0)
    u1 = to_core(u0)
    *cross_heads, token = call(
        cross_first,
        "cross_first",
        [meta_in, (ncross, "tiles"), (memory, "tiles_row")] + now(wc0, wc1),
        heads_out + [probability_out],
        probability_scratch,
        pair_flops,
        token,
    )
    wc3, u2, v0, token = hold(wc3, u2, v0, token)
    u3 = to_core(u2)
    v2 = to_chip(v0)
    v1 = to_core(v0)
    *cross_heads_second, third, nffn, token = call(
        cross_second,
        "cross_second",
        [meta_in]
        + late(second)
        + [(ncross, "tiles"), (memory, "tiles_row")]
        + small(norms)
        + late(wc0, wc1)
        + now(wc2, wc3)
        + late(cross_heads[3]),
        heads_out + [probability_out, stream_out(f32), stream_out(bf16)],
        probability_scratch,
        pair_flops + 2 * SEQ * D * D,
        token,
    )
    u3, v2, token = hold(u3, v2, token)
    v3 = to_core(v2)
    grads_ln = ((8, D), f32, whole((8, D)))
    placed_output, output, g3, g3_low, gln_ffn, ffn_own, ffn_other, token = call(
        ffn_both,
        "ffn_both",
        [meta_in]
        + [(third, "tiles"), (nffn, "tiles"), (cotangent, "tiles_row")]
        + small(norms)
        + now(u0, u1, u2, u3, v0, v1, v2, v3),
        [
            stream_out(bf16, True),
            stream_out(bf16),
            stream_out(f32),
            stream_out(bf16),
            grads_ln,
            out((1024, D), bf16),
            out((1024, D), bf16),
        ],
        [pltpu.VMEM((SEQ, 1024), bf16), pltpu.VMEM((SEQ, 1024), bf16)],
        12 * SEQ * D * 2048,
        token,
    )

    row_count = lax.axis_size("rows")
    assert row_count % GROUP == 0

    def along_rows(x, s):
        return lax.ppermute(x, "rows", [(r, r ^ s) for r in range(row_count)])

    def to_y(x):
        return along_rows(x, 1)

    def to_z(sends):
        return [along_rows(x, 2 * s) for s, x in enumerate(sends, 1)]

    def rows_out(*sizes):
        return [((n, D), bf16) for n in sizes]

    ffn_other = to_core(ffn_other)

    back_scratch = [pltpu.VMEM((SEQ, 256), bf16)] + [pltpu.VMEM((SEQ, 256), f32)] * 3
    back_scratch += probability_scratch
    pair_out = out((SEQ, 256), bf16)
    packed_outs = [out((D, D), bf16), out((D, D), bf16)]
    back_flops = 2 * SEQ * D * 256 + 4 * 2 * 4 * DOCS * FAST_Q * FAST_K * 256

    def head_inputs(natural, p):
        return soon(*natural) + [(in_hbm(p), ANY)]

    *cross_grads, cross_own, cross_other, token = call(
        functools.partial(attention_back_first, True),
        "cross_back_first",
        [meta_in]
        + [(g3_low, "tiles")]
        + late(ncross)
        + [(memory, "late_row")]
        + small(rank, limit)
        + now(wc0, wc1)
        + head_inputs(cross_heads[0:4], cross_heads[4]),
        [pair_out] * 3 + packed_outs,
        [limits] + back_scratch,
        back_flops + 2 * SEQ * D * 1024,
        token,
    )
    ffn_other, token = hold(ffn_other, token)
    ffn_keep, ffn_send = simple(slot_1, "slot_1", meta, [ffn_own, ffn_other], rows_out(512, 512))
    ffn_send, token = hold(ffn_send, token)
    ffn_arrived = to_y(ffn_send)
    cross_other = to_core(cross_other)
    g2, g2_low, placed_mem, grad_mem, gln_cross, token = call(
        cross_back_second,
        "cross_back_second",
        [meta_in]
        + [(g3_low, "tiles")]
        + late(g3, second)
        + small(norms)
        + late(wc0, wc1)
        + now(wc2, wc3)
        + late(*cross_grads)
        + head_inputs(cross_heads_second[0:4], cross_heads_second[4]),
        [stream_out(f32), stream_out(bf16), stream_out(f32, True), stream_out(bf16), grads_ln],
        back_scratch,
        back_flops + 2 * SEQ * D * 1536,
        token,
    )
    ffn_arrived, cross_other, token = hold(ffn_arrived, cross_other, token)
    ffn_keep, *sends, cross_keep, cross_send = simple(
        slot_2,
        "slot_2",
        meta,
        [ffn_keep, ffn_arrived, cross_own, cross_other],
        rows_out(128, 128, 128, 128, 256, 256),
    )
    ffn_keep, cross_send, token = hold(ffn_keep, cross_send, token)
    ffn_parts = to_z(sends)
    cross_arrived = to_y(cross_send)

    *self_grads, self_own, self_other, token = call(
        functools.partial(attention_back_first, False),
        "self_back_first",
        [meta_in]
        + [(g2_low, "tiles")]
        + late(nq, nc)
        + small(rank, limit)
        + now(ws0, ws1)
        + head_inputs(first[0:4], first[4]),
        [pair_out] * 3 + packed_outs,
        [limits] + back_scratch,
        back_flops + 2 * SEQ * D * 1024,
        token,
    )
    *ffn_parts, cross_arrived, self_other, token = hold(
        *ffn_parts, cross_arrived, self_other, token
    )
    self_other = to_core(self_other)
    ffn_total, cross_keep, *sends, self_keep, self_send = simple(
        slot_3,
        "slot_3",
        meta,
        [ffn_keep, *ffn_parts, cross_keep, cross_arrived, self_own, self_other],
        rows_out(128, 64, 192, 192, 192, 256, 256),
    )
    ffn_total, self_send, token = hold(ffn_total, self_send, token)
    self_arrived = to_y(self_send)
    messages = to_z(sends)
    *self_grads_second, token = call(
        self_back_second,
        "self_back_second",
        [meta_in, (g2_low, "tiles")]
        + small(rank, limit)
        + now(ws2, ws3)
        + head_inputs(second_heads[0:4], second_heads[4]),
        [pair_out] * 3,
        [limits] + back_scratch,
        back_flops,
        token,
    )
    *messages, self_arrived, token = hold(*messages, self_arrived, token)
    ffn_half, cross_total, self_keep, *sends = simple(
        slot_4,
        "slot_4",
        meta,
        [ffn_total, *messages, cross_keep, self_keep, self_arrived],
        rows_out(512, 64, 64, 128, 128, 128),
    )
    cross_total, ffn_half, token = hold(cross_total, ffn_half, token)
    messages = to_z(sends)
    ffn_arrived = to_y(ffn_half)
    placed_q, placed_c, gq, gc, gln_self, token = call(
        self_back_finish,
        "self_back_finish",
        [meta_in, (g2, "tiles"), (query_stream, "tiles_row"), (content_stream, "tiles_row")]
        + small(norms)
        + now(ws0, ws1, ws2, ws3)
        + [(x, "tiles") for x in self_grads + self_grads_second],
        [stream_out(f32, True), stream_out(f32, True), stream_out(bf16), stream_out(bf16), grads_ln],
        [],
        2 * SEQ * D * 1536,
        token,
    )
    gln = jnp.concatenate([gln_self[0:4], gln_cross[0:2], gln_ffn[0:2]], axis=0)
    *messages, ffn_arrived, gln = hold(*messages, ffn_arrived, gln)
    last_send, cross_half = simple(
        slot_5,
        "slot_5",
        meta,
        [self_keep, cross_total, *messages, gln, to_core(gln)],
        [((GROUP, 80, D), bf16), ((256, D), bf16)],
    )
    output, grad_mem, last_send = hold(output, grad_mem, last_send)
    groups = None
    if row_count > GROUP:
        groups = [list(range(r, r + GROUP)) for r in range(0, row_count, GROUP)]
    last_parts = lax.all_to_all(last_send, "rows", 0, 0, axis_index_groups=groups)
    cross_arrived = to_y(cross_half)

    def over_groups(totals):
        if row_count == GROUP:
            return totals
        groups = [list(range(r, row_count, GROUP)) for r in range(GROUP)]
        return lax.psum(totals, "rows", axis_index_groups=groups)

    def both_rows(placed_own, arrays, name):
        count = len(arrays)
        size = SEQ // 2
        one = pl.BlockSpec((size, D), lambda i, meta: (i, 0))
        block = pl.BlockSpec((size, D), lambda i, meta: (2 * (1 - meta[0]) + i, 0))
        return pl.pallas_call(
            place_rows,
            name=name,
            grid_spec=pltpu.PrefetchScalarGridSpec(
                num_scalar_prefetch=1,
                grid=(2,),
                in_specs=[one] * count + [pl.BlockSpec(memory_space=pl.ANY)] * count,
                out_specs=[block] * count,
            ),
            out_shape=[jax.ShapeDtypeStruct(x.shape, x.dtype) for x in placed_own],
            input_output_aliases={1 + count + n: n for n in range(count)},
        )(meta, *[to_core(x) for x in arrays], *placed_own)

    out_both, grad_mem_both = both_rows([placed_output, placed_mem], [output, grad_mem], "place_early")
    gq_both, gc_both = both_rows([placed_q, placed_c], [gq, gc], "place_late")

    cross_arrived, out_both, gq_both = hold(cross_arrived, out_both, gq_both)
    attention_outs = [((512, 128), f32)] * 3 + [((128, 512), f32)]
    grad_ffn_in, grad_ffn_out, *grad_cross_parts = simple(
        unpack_early,
        "unpack_early",
        meta,
        [ffn_half, ffn_arrived, cross_half, cross_arrived],
        [((D, D), f32)] * 2 + attention_outs,
        [pltpu.VMEM((D, D), bf16), pltpu.VMEM((2 * D, D), bf16)],
    )
    *grad_self_parts, gln = simple(
        unpack_late,
        "unpack_late",
        meta,
        [last_parts],
        attention_outs + [((8, D), f32)],
        [pltpu.VMEM((D, D), bf16)],
    )
    grad_ffn_in, grad_ffn_out, grad_cross_parts, grad_self_parts, gln = over_groups(
        (grad_ffn_in, grad_ffn_out, grad_cross_parts, grad_self_parts, gln)
    )
    return (
        out_both,
        gq_both,
        gc_both,
        grad_mem_both,
        gln[0],
        gln[1],
        gln[2],
        gln[3],
        *grad_self_parts,
        gln[4],
        gln[5],
        *grad_cross_parts,
        gln[6],
        gln[7],
        grad_ffn_in,
        grad_ffn_out,
    )


def solution(mesh):
    assert mesh.shape["heads"] == 4
    row_spec = P("rows", None)
    flat = P("rows")
    by_column = P(None, "heads")
    by_row = P("heads", None)
    attention = (by_column, by_column, by_column, by_row)
    in_specs = (
        (row_spec,) * 3
        + (flat,) * 5
        + (P(),) * 4
        + attention
        + (P(),) * 2
        + attention
        + (P(),) * 2
        + (by_column, by_row, row_spec)
    )
    out_specs = (
        (row_spec,) * 4
        + (P(),) * 4
        + attention
        + (P(),) * 2
        + attention
        + (P(),) * 2
        + (by_column, by_row)
    )
    return jax.shard_map(shards, mesh=mesh, in_specs=in_specs, out_specs=out_specs, check_vma=False)
```

```python
import functools

import jax
import jax.numpy as jnp
from jax import lax
from jax.experimental import pallas as pl
from jax.experimental.pallas import tpu as pltpu
from jax.sharding import PartitionSpec as P

HEAD_DIM = 64
SEQ = 1024
DOCS = 8
D = 512
TILE = 256
TILES = SEQ // TILE
FAST_Q = 256
FAST_K = 208
LONG_Q = 128
LONG_K = 640

norm_eps = 1e-05
masked_score = -1e30
hidden_rank = 1e6
gelu_root = 0.7978845608028654
gelu_cube = 0.044715

f32 = jnp.float32
bf16 = jnp.bfloat16


def dot(a, b):
    return lax.dot_general(a, b, (((1,), (0,)), ((), ())), preferred_element_type=f32)


def dot_nt(a, b):
    return lax.dot_general(a, b, (((1,), (1,)), ((), ())), preferred_element_type=f32)


def dot_tn(a, b):
    return lax.dot_general(a, b, (((0,), (0,)), ((), ())), preferred_element_type=f32)


def lanes(parts):
    return jnp.concatenate(parts, axis=1)


def layer_norm(values, gain, shift):
    centre = values - jnp.mean(values, axis=-1, keepdims=True)
    spread = jnp.mean(centre * centre, axis=-1, keepdims=True)
    return centre * lax.rsqrt(spread + norm_eps) * gain + shift


def norm_backward(values, gain, grad):
    centre = values - jnp.mean(values, axis=-1, keepdims=True)
    spread = jnp.mean(centre * centre, axis=-1, keepdims=True)
    scale = lax.rsqrt(spread + norm_eps)
    xhat = centre * scale
    eg = grad * gain
    mean_eg = jnp.mean(eg, axis=-1, keepdims=True)
    mean_egx = jnp.mean(eg * xhat, axis=-1, keepdims=True)
    grad_gain = jnp.sum(grad * xhat, axis=0, keepdims=True)
    grad_shift = jnp.sum(grad, axis=0, keepdims=True)
    return scale * (eg - mean_eg - xhat * mean_egx), grad_gain, grad_shift


def rows_of(i, size=TILE):
    return pl.ds(pl.multiple_of(i * size, size), size)


def w_query(ref):
    return ref[:, 0:128]


def w_key(ref):
    return ref[:, 128:256]


def w_value(ref):
    return ref[:, 256:384]


def w_out(ref):
    return lanes([ref[128 * j : 128 * j + 128, 384:512] for j in range(4)])


def half_masks():
    place = lax.broadcasted_iota(jnp.int32, (1, 128), 1)
    low = jnp.where(place < HEAD_DIM, 1.0, 0.0).astype(f32)
    return (low.astype(bf16), (1.0 - low).astype(bf16))


def doc_bounds(meta, d, source):
    base = 17 if source else 1
    return meta[base + d], meta[base + 8 + d]


def window_of(first, limit):
    return pl.multiple_of(jnp.minimum((first // 16) * 16, limit), 16)


def key_bias(ks, ke, k0, width):
    place = k0 + lax.broadcasted_iota(jnp.int32, (width, 128), 0)
    return jnp.where((place >= ks) & (place < ke), 0.0, masked_score)


def make_bias(rank_ref, limit_ref, ks, ke, q0, k0, span, width):
    if rank_ref is None:
        return lanes([key_bias(ks, ke, k0, width)] * (span // 128))
    place = k0 + lax.broadcasted_iota(jnp.int32, (width, 128), 0)
    ranks = rank_ref[pl.ds(k0, width), :]
    ranks = jnp.where((place < ks + 2) & (ranks < hidden_rank), -1.0, ranks)
    ranks = jnp.where((place >= ks) & (place < ke), ranks, hidden_rank)
    limits = jnp.broadcast_to(limit_ref[...], (8, SEQ))
    limits = pltpu.roll(limits, lax.rem(SEQ - q0, SEQ), 1)[0:1, 0:span]
    row = k0 + lax.broadcasted_iota(jnp.int32, (width, span), 0)
    column = q0 + lax.broadcasted_iota(jnp.int32, (width, span), 1)
    seen = (lanes([ranks] * (span // 128)) < limits) & (row != column)
    return jnp.where(seen, 0.0, masked_score)


TOGETHER = 4
STEPS = DOCS // TOGETHER


def interleave(items):
    items = [list(phases) for phases in items]
    depth = max(len(phases) for phases in items)
    results = [None] * len(items)
    for tick in range(len(items) + depth - 1):
        for phase in range(depth):
            n = tick - phase
            if 0 <= n < len(items) and phase < len(items[n]):
                run = items[n][phase]
                results[n] = run() if phase == 0 else run(results[n])
    return results


def is_fast(meta, cross):
    return meta[34 if cross else 33] == 1


def both_heads(x, masks):
    return jnp.concatenate([x * masks[0], x * masks[1]], axis=0)


def pair_scores(queries, keys, masks):
    return dot_nt(both_heads(keys, masks), queries)


def pair_probabilities(scores, bias):
    width = bias.shape[0]
    result = []
    for a in range(2):
        part = scores[width * a : width * a + width] + bias
        part = jnp.exp(part - jnp.max(part, axis=0, keepdims=True))
        part = part * (1.0 / jnp.sum(part, axis=0, keepdims=True))
        result.append(part.astype(bf16))
    return result


def pair_product(rows, parts):
    across = jnp.transpose(rows)
    halves = [dot(across[64 * a : 64 * a + 64], part) for a, part in enumerate(parts)]
    return jnp.transpose(jnp.concatenate(halves, axis=0))


def for_docs(meta, cross, run, before, after):
    @pl.when(is_fast(meta, cross))
    def _():
        def step(i, carry):
            slot = lax.rem(i, 2)
            before(i, slot)
            items = []
            for place in range(TOGETHER):
                d = TOGETHER * i + place
                ts, te = doc_bounds(meta, d, False)
                ks, ke = doc_bounds(meta, d, cross)
                q0 = window_of(ts, SEQ - FAST_Q)
                k0 = window_of(ks, SEQ - FAST_K)
                items += run(d, slot, place, q0, k0, FAST_Q, FAST_K, ts, te, ks, ke, True)
            interleave(items)
            after(i, slot)
            return carry

        lax.fori_loop(0, STEPS, step, 0)

    @pl.when(jnp.logical_not(is_fast(meta, cross)))
    def _():
        def doc(d, carry):
            ts, te = doc_bounds(meta, d, False)
            ks, ke = doc_bounds(meta, d, cross)
            base = (ts // 16) * 16
            k0 = window_of(ks, SEQ - LONG_K)

            def chunk(i, carry):
                lower = base + i * LONG_Q
                q0 = pl.multiple_of(jnp.minimum(lower, SEQ - LONG_Q), 16)
                low = jnp.maximum(ts, lower)
                high = jnp.minimum(te, lower + LONG_Q)
                interleave(run(d, None, None, q0, k0, LONG_Q, LONG_K, low, high, ks, ke, False))
                return carry

            return lax.fori_loop(0, (te - base + LONG_Q - 1) // LONG_Q, chunk, carry)

        lax.fori_loop(0, DOCS, doc, 0)


def attend_docs(meta, cross, rank_ref, limit_ref, halves, p_ref, p_buf, p_sem):
    pairs = 2 * len(halves)
    masks = half_masks()

    def save(i, slot):
        return pltpu.make_async_copy(p_buf.at[slot], p_ref.at[pl.ds(TOGETHER * i, TOGETHER)], p_sem.at[slot])

    def before(i, slot):
        @pl.when(i >= 2)
        def _():
            save(i - 2, slot).wait()

    def after(i, slot):
        save(i, slot).start()

    def run(d, slot, place, q0, k0, span, width, low, high, ks, ke, fast):
        bias = make_bias(rank_ref, limit_ref, ks, ke, q0, k0, span, width)
        row = q0 + lax.broadcasted_iota(jnp.int32, (span, 128), 0)
        inside = (row >= low) & (row < high)

        def phases(n):
            q_ref, k_ref, v_ref, mixed_ref = halves[n // 2]
            cols = slice(128 * (n % 2), 128 * (n % 2) + 128)

            def score():
                return pair_scores(q_ref[pl.ds(q0, span), cols], k_ref[pl.ds(k0, width), cols], masks)

            def weigh(scores):
                parts = pair_probabilities(scores, bias)
                if fast:
                    for a in range(2):
                        p_buf[slot, place, 2 * n + a] = parts[a]
                return parts

            def mix(parts):
                mixed = pair_product(v_ref[pl.ds(k0, width), cols], parts)
                old = mixed_ref[pl.ds(q0, span), cols].astype(f32)
                mixed_ref[pl.ds(q0, span), cols] = jnp.where(inside, mixed, old).astype(bf16)

            return score, weigh, mix

        return [phases(n) for n in range(pairs)]

    for_docs(meta, cross, run, before, after)

    @pl.when(is_fast(meta, cross))
    def _():
        for i in range(STEPS - 2, STEPS):
            save(i, i % 2).wait()


def load_step(load, i, slot):
    p_ref, p_buf, p_sem = load
    return pltpu.make_async_copy(p_ref.at[pl.ds(TOGETHER * i, TOGETHER)], p_buf.at[slot], p_sem.at[slot])


def start_load(meta, cross, load):
    @pl.when(is_fast(meta, cross))
    def _():
        load_step(load, 0, 0).start()


def attend_docs_back(
    meta, cross, rank_ref, limit_ref, q_ref, k_ref, v_ref, mixed_ref, dm_ref,
    dq_ref, dk_ref, dv_ref, load,
):
    pairs = q_ref.shape[1] // 128
    masks = half_masks()
    p_buf = load[1]

    def before(i, slot):
        @pl.when(i + 1 < STEPS)
        def _():
            load_step(load, i + 1, 1 - slot).start()

        load_step(load, i, slot).wait()

    def after(i, slot):
        pass

    def run(d, slot, place, q0, k0, span, width, low, high, ks, ke, fast):
        row = q0 + lax.broadcasted_iota(jnp.int32, (span, 128), 0)
        inside = jnp.where((row >= low) & (row < high), 1.0, 0.0).astype(bf16)
        ones = jnp.ones((width, 128), bf16)
        if not fast:
            bias = make_bias(rank_ref, limit_ref, ks, ke, q0, k0, span, width)

        def phases(n):
            cols = slice(128 * n, 128 * n + 128)

            def differ():
                values = v_ref[pl.ds(k0, width), cols]
                mixed = mixed_ref[pl.ds(q0, span), cols]
                grad = dm_ref[pl.ds(q0, span), cols] * inside
                left = lanes([grad, -(grad * mixed)])
                right = both_heads(lanes([values, ones]), [lanes([m, m]) for m in masks])
                return grad, dot_nt(right, left)

            def slope(state):
                grad, delta = state
                if fast:
                    parts = [p_buf[slot, place, 2 * n + a] for a in range(2)]
                else:
                    queries = q_ref[pl.ds(q0, span), cols]
                    keys = k_ref[pl.ds(k0, width), cols]
                    parts = pair_probabilities(pair_scores(queries, keys, masks), bias)
                slopes = [
                    parts[a] * delta[width * a : width * a + width].astype(bf16) for a in range(2)
                ]
                return grad, parts, slopes

            def spread(state):
                grad, parts, slopes = state
                queries = q_ref[pl.ds(q0, span), cols]
                dk = dv = None
                for a in range(2):
                    dk_a = dot(slopes[a], queries * masks[a])
                    dv_a = dot(parts[a], grad * masks[a])
                    dk = dk_a if dk is None else dk + dk_a
                    dv = dv_a if dv is None else dv + dv_a
                dq = pair_product(k_ref[pl.ds(k0, width), cols], slopes)
                dq_ref[pl.ds(q0, span), cols] += dq * (HEAD_DIM**-0.5)
                dk_ref[pl.ds(k0, width), cols] += dk
                dv_ref[pl.ds(k0, width), cols] += dv

            return differ, slope, spread

        return [phases(n) for n in range(pairs)]

    for_docs(meta, cross, run, before, after)


def spread_ranks(rank_row_ref, rank_ref):
    rank_ref[...] = jnp.transpose(jnp.broadcast_to(rank_row_ref[...], (128, SEQ)))


def prepare(
    core, seg_ref, src_ref, rank_ref, limit_ref, pad_ref,
    n0, n1, n2, n3, n4, n5, n6, n7, sq, sk, sv, so, cq, ck, cv, co,
    meta_ref, ranks_ref, limits_ref, norms_ref, ws_ref, wc_ref,
):
    meta_ref[0] = core[0]
    meta_ref[35] = core[1]
    for base, ref in ((1, seg_ref), (17, src_ref)):
        ids = ref[0]
        meta_ref[base] = 0
        meta_ref[base + 15] = SEQ
        for d in range(1, DOCS):
            cut = jnp.sum(jnp.where(ids < d, 1.0, 0.0)).astype(jnp.int32)
            meta_ref[base + d] = cut
            meta_ref[base + 7 + d] = cut
    for place, base in ((33, 1), (34, 17)):
        fast = jnp.int32(1)
        for d in range(DOCS):
            q0 = window_of(meta_ref[1 + d], SEQ - FAST_Q)
            k0 = window_of(meta_ref[base + d], SEQ - FAST_K)
            fits = (meta_ref[9 + d] - q0 <= FAST_Q) & (meta_ref[base + 8 + d] - k0 <= FAST_K)
            fast = fast & fits.astype(jnp.int32)
        meta_ref[place] = fast
    ranks = jnp.where(pad_ref[0] != 0, hidden_rank, rank_ref[0].astype(f32))
    limits = limit_ref[0].astype(f32)
    for i in range(8):
        ranks_ref[0:1, 128 * i : 128 * i + 128] = ranks[i : i + 1]
        limits_ref[0:1, 128 * i : 128 * i + 128] = limits[i : i + 1]
    for i, ref in enumerate((n0, n1, n2, n3, n4, n5, n6, n7)):
        norms_ref[i : i + 1, :] = ref[...]
    for to, parts, out in ((ws_ref, (sq, sk, sv), so), (wc_ref, (cq, ck, cv), co)):
        for i, part in enumerate(parts):
            to[:, 128 * i : 128 * i + 128] = part[...]
        for j in range(4):
            to[128 * j : 128 * j + 128, 384:512] = out[:, 128 * j : 128 * j + 128]


def self_first(
    meta, io, xq_ref, xc_ref, rank_row_ref, limit_ref, norms_ref, w0_ref, w1_ref,
    nq_ref, nc_ref, q_ref, k_ref, v_ref, mixed_ref, p_ref, rank_ref, p_buf, p_sem,
):

    spread_ranks(rank_row_ref, rank_ref)
    wq = lanes([w_query(w0_ref), w_query(w1_ref)])
    wkv = lanes([w_key(w0_ref), w_key(w1_ref), w_value(w0_ref), w_value(w1_ref)])

    def tile(i, carry):
        rows = rows_of(i)
        io.wait_rows(i)
        nq = layer_norm(xq_ref[rows, :].astype(f32), norms_ref[0:1], norms_ref[1:2]).astype(bf16)
        nc = layer_norm(xc_ref[rows, :].astype(f32), norms_ref[2:3], norms_ref[3:4]).astype(bf16)
        nq_ref[rows, :] = nq
        nc_ref[rows, :] = nc
        q_ref[rows, :] = (dot(nq, wq) * (HEAD_DIM**-0.5)).astype(bf16)
        kv = dot(nc, wkv).astype(bf16)
        k_ref[rows, :] = kv[:, :256]
        v_ref[rows, :] = kv[:, 256:]
        return carry

    lax.fori_loop(0, TILES, tile, 0)

    for ref in (nq_ref, nc_ref, q_ref, k_ref, v_ref):
        io.send(ref)
    attend_docs(meta, False, rank_ref, limit_ref, [(q_ref, k_ref, v_ref, mixed_ref)], p_ref, p_buf, p_sem)


def self_second(
    meta, io, xq_ref, nq_ref, nc_ref, rank_row_ref, limit_ref, norms_ref, w0_ref, w1_ref, w2_ref, w3_ref,
    mixed_first_ref,
    q_ref, k_ref, v_ref, mixed_ref, p_ref, second_ref, ncross_ref, rank_ref, p_buf, p_sem,
):

    spread_ranks(rank_row_ref, rank_ref)
    wq = lanes([w_query(w2_ref), w_query(w3_ref)])
    wkv = lanes([w_key(w2_ref), w_key(w3_ref), w_value(w2_ref), w_value(w3_ref)])

    def tile(i, carry):
        rows = rows_of(i)
        io.wait_rows(i)
        q_ref[rows, :] = (dot(nq_ref[rows, :], wq) * (HEAD_DIM**-0.5)).astype(bf16)
        kv = dot(nc_ref[rows, :], wkv).astype(bf16)
        k_ref[rows, :] = kv[:, :256]
        v_ref[rows, :] = kv[:, 256:]
        return carry

    lax.fori_loop(0, TILES, tile, 0)

    for ref in (q_ref, k_ref, v_ref):
        io.send(ref)
    attend_docs(meta, False, rank_ref, limit_ref, [(q_ref, k_ref, v_ref, mixed_ref)], p_ref, p_buf, p_sem)

    io.send(mixed_ref)
    io.wait("late")
    out_first = jnp.concatenate([w_out(w0_ref), w_out(w1_ref)], axis=0)
    out_second = jnp.concatenate([w_out(w2_ref), w_out(w3_ref)], axis=0)

    def tile(i, carry):
        rows = rows_of(i)
        branch = dot(mixed_first_ref[rows, :], out_first) + dot(mixed_ref[rows, :], out_second)
        second = xq_ref[rows, :].astype(f32) + branch
        second_ref[rows, :] = second
        io.send(second_ref, rows)
        ncross_ref[rows, :] = layer_norm(second, norms_ref[4:5], norms_ref[5:6]).astype(bf16)
        io.send(ncross_ref, rows)
        return carry

    lax.fori_loop(0, TILES, tile, 0)


def project_cross(io, ncross_ref, memory_ref, weights, q_ref, k_ref, v_ref):
    wq = lanes([w_query(w) for w in weights])
    wkv = lanes([w_key(w) for w in weights] + [w_value(w) for w in weights])

    def tile(i, carry):
        rows = rows_of(i)
        io.wait_rows(i)
        q_ref[rows, :] = (dot(ncross_ref[rows, :], wq) * (HEAD_DIM**-0.5)).astype(bf16)
        kv = dot(memory_ref[rows, :], wkv).astype(bf16)
        k_ref[rows, :] = kv[:, :256]
        v_ref[rows, :] = kv[:, 256:]
        return carry

    lax.fori_loop(0, TILES, tile, 0)
    for ref in (q_ref, k_ref, v_ref):
        io.send(ref)


def cross_first(
    meta, io, ncross_ref, memory_ref, w0_ref, w1_ref,
    q_ref, k_ref, v_ref, mixed_ref, p_ref, p_buf, p_sem,
):
    project_cross(io, ncross_ref, memory_ref, (w0_ref, w1_ref), q_ref, k_ref, v_ref)
    attend_docs(meta, True, None, None, [(q_ref, k_ref, v_ref, mixed_ref)], p_ref, p_buf, p_sem)


def cross_second(
    meta, io, second_ref, ncross_ref, memory_ref, norms_ref, w0_ref, w1_ref, w2_ref, w3_ref,
    mixed_first_ref,
    q_ref, k_ref, v_ref, mixed_ref, p_ref, third_ref, nffn_ref, p_buf, p_sem,
):
    project_cross(io, ncross_ref, memory_ref, (w2_ref, w3_ref), q_ref, k_ref, v_ref)
    attend_docs(meta, True, None, None, [(q_ref, k_ref, v_ref, mixed_ref)], p_ref, p_buf, p_sem)
    io.send(mixed_ref)
    io.wait("late")
    out_first = jnp.concatenate([w_out(w0_ref), w_out(w1_ref)], axis=0)
    out_second = jnp.concatenate([w_out(w2_ref), w_out(w3_ref)], axis=0)

    def tile(i, carry):
        rows = rows_of(i)
        branch = dot(mixed_first_ref[rows, :], out_first) + dot(mixed_ref[rows, :], out_second)
        third = second_ref[rows, :] + branch
        third_ref[rows, :] = third
        io.send(third_ref, rows)
        nffn_ref[rows, :] = layer_norm(third, norms_ref[6:7], norms_ref[7:8]).astype(bf16)
        io.send(nffn_ref, rows)
        return carry

    lax.fori_loop(0, TILES, tile, 0)


def ffn_both(
    meta, io, third_ref, nffn_ref, cot_ref, norms_ref, u0_ref, u1_ref, u2_ref, u3_ref,
    w0_ref, w1_ref, w2_ref, w3_ref,
    placed_ref, out_ref, g3_ref, g3_low_ref, gln_ref, own_ref, other_ref, hidden_ref, before_ref,
):
    gln_ref[...] = jnp.zeros_like(gln_ref)
    in_refs = (u0_ref, u1_ref, u2_ref, u3_ref)

    def tile(i, carry):
        rows = rows_of(i)
        io.wait_rows(i)
        nffn = nffn_ref[rows, :]
        cot = cot_ref[rows, :]
        outs = []
        grads = []

        def phases(g, w_ref):
            def enter():
                return dot(nffn, in_refs[g][...]), dot_nt(cot, w_ref[...])

            def bend(state):
                x, grad_hidden = state
                square = x * x
                half = 0.5 + 0.5 * jnp.tanh(x * (gelu_root + (gelu_root * gelu_cube) * square))
                value = x * half
                rise = 2.0 * gelu_root + (6.0 * gelu_root * gelu_cube) * square
                slope = half + value * (1.0 - half) * rise
                return value.astype(bf16), (grad_hidden * slope).astype(bf16)

            def leave(state):
                hidden, grad_before = state
                outs.append(dot(hidden, w_ref[...]))
                grads.append(dot_nt(grad_before, in_refs[g][...]))
                if g < 2:
                    hidden_ref[rows, 512 * g : 512 * g + 512] = hidden
                    before_ref[rows, 512 * g : 512 * g + 512] = grad_before

            return enter, bend, leave

        interleave([phases(g, w) for g, w in enumerate((w0_ref, w1_ref, w2_ref, w3_ref))])
        third = third_ref[rows, :]
        result = (third + ((outs[0] + outs[1]) + (outs[2] + outs[3]))).astype(bf16)
        out_ref[rows, :] = result
        placed_ref[rows, :] = result
        grad_normed = (grads[0] + grads[1]) + (grads[2] + grads[3])
        grad_norm, grad_gain, grad_shift = norm_backward(third, norms_ref[6:7], grad_normed)
        g3 = cot.astype(f32) + grad_norm
        g3_ref[rows, :] = g3
        g3_low_ref[rows, :] = g3.astype(bf16)
        gln_ref[0:1, :] += grad_gain
        gln_ref[1:2, :] += grad_shift
        for ref in (out_ref, placed_ref, g3_ref, g3_low_ref):
            io.send(ref, rows)
        return carry

    lax.fori_loop(0, TILES, tile, 0)
    part = dot_tn(nffn_ref[...], before_ref[...])
    own_ref[0:512, :] = part[:, 0:512].astype(bf16)
    other_ref[0:512, :] = part[:, 512:1024].astype(bf16)
    io.send(own_ref, pl.ds(0, 512))
    io.send(other_ref, pl.ds(0, 512))
    part = dot_tn(hidden_ref[...], cot_ref[...])
    own_ref[512:1024, :] = part[0:512].astype(bf16)
    other_ref[512:1024, :] = part[512:1024].astype(bf16)
    io.send(own_ref, pl.ds(512, 512))
    io.send(other_ref, pl.ds(512, 512))


def back_start(io, g_ref, mixed_ref, w_refs, dm_ref, dq_ref, dk_ref, dv_ref):
    out_rows = jnp.concatenate([w_out(w) for w in w_refs], axis=0)

    def tile(i, carry):
        rows = rows_of(i)
        io.wait_rows(i)
        dm_ref[rows, :] = dot_nt(g_ref[rows, :], out_rows).astype(bf16)
        zeros = jnp.zeros((TILE, 256), f32)
        dq_ref[rows, :] = zeros
        dk_ref[rows, :] = zeros
        dv_ref[rows, :] = zeros
        return carry

    lax.fori_loop(0, TILES, tile, 0)


def attention_back_first(
    cross, meta, io, g_ref, nq_ref, nkv_ref, rank_row_ref, limit_ref, w0_ref, w1_ref,
    q_ref, k_ref, v_ref, mixed_ref, p_ref,
    dq_ref, dk_ref, dv_ref, own_ref, other_ref,
    rank_ref, dm_ref, dqs_ref, dks_ref, dvs_ref, p_buf, p_sem,
):
    load = (p_ref, p_buf, p_sem)
    start_load(meta, cross, load)
    if not cross:
        spread_ranks(rank_row_ref, rank_ref)
    back_start(io, g_ref, mixed_ref, (w0_ref, w1_ref), dm_ref, dqs_ref, dks_ref, dvs_ref)

    io.wait("soon")
    attend_docs_back(
        meta, cross, None if cross else rank_ref, limit_ref, q_ref, k_ref, v_ref, mixed_ref,
        dm_ref, dqs_ref, dks_ref, dvs_ref, load,
    )

    dq_ref[...] = dqs_ref[...].astype(bf16)
    dk_ref[...] = dks_ref[...].astype(bf16)
    dv_ref[...] = dvs_ref[...].astype(bf16)
    for ref in (dq_ref, dk_ref, dv_ref):
        io.send(ref)
    io.wait("late")
    nq = nq_ref[...]
    nkv = nkv_ref[...]
    for n, part in enumerate(
        (dot_tn(nq, dq_ref[...]), dot_tn(nkv, dk_ref[...]), dot_tn(nkv, dv_ref[...]))
    ):
        own_ref[:, 128 * n : 128 * n + 128] = part[:, :128].astype(bf16)
        other_ref[:, 128 * n : 128 * n + 128] = part[:, 128:].astype(bf16)
    part = dot_tn(mixed_ref[...], g_ref[...])
    for j in range(4):
        rows = slice(128 * j, 128 * j + 128)
        own_ref[rows, 384:512] = part[:128, rows].astype(bf16)
        other_ref[rows, 384:512] = part[128:, rows].astype(bf16)


def back_second_docs(
    cross, meta, io, g_ref, rank_row_ref, limit_ref, w_refs, q_ref, k_ref, v_ref, mixed_ref, p_ref,
    rank_ref, dm_ref, dqs_ref, dks_ref, dvs_ref, p_buf, p_sem,
):
    load = (p_ref, p_buf, p_sem)
    start_load(meta, cross, load)
    if not cross:
        spread_ranks(rank_row_ref, rank_ref)
    back_start(io, g_ref, mixed_ref, w_refs, dm_ref, dqs_ref, dks_ref, dvs_ref)

    io.wait("soon")
    attend_docs_back(
        meta, cross, None if cross else rank_ref, limit_ref, q_ref, k_ref, v_ref, mixed_ref,
        dm_ref, dqs_ref, dks_ref, dvs_ref, load,
    )


def stream_grads(rows, first, second, firsts, seconds):
    dq, dk, dv = first
    dq2, dk2, dv2 = (ref[rows, :].astype(bf16) for ref in second)
    w0, w1 = firsts
    w2, w3 = seconds
    grad_q = dot_nt(dq[rows, :], lanes([w_query(w0), w_query(w1)])) + dot_nt(
        dq2, lanes([w_query(w2), w_query(w3)])
    )
    kv = lanes([dk[rows, :], dv[rows, :]])
    kv2 = lanes([dk2, dv2])
    grad_kv = dot_nt(kv, lanes([w_key(w0), w_key(w1), w_value(w0), w_value(w1)])) + dot_nt(
        kv2, lanes([w_key(w2), w_key(w3), w_value(w2), w_value(w3)])
    )
    return grad_q, grad_kv


def cross_back_second(
    meta, io, g_low_ref, g_ref, second_ref, norms_ref, w0_ref, w1_ref, w2_ref, w3_ref,
    dq_ref, dk_ref, dv_ref, q_ref, k_ref, v_ref, mixed_ref, p_ref,
    g2_ref, g2_low_ref, placed_ref, gmem_ref, gln_ref,
    dm_ref, dqs_ref, dks_ref, dvs_ref, p_buf, p_sem,
):
    back_second_docs(
        True, meta, io, g_low_ref, None, None, (w2_ref, w3_ref), q_ref, k_ref, v_ref, mixed_ref, p_ref,
        None, dm_ref, dqs_ref, dks_ref, dvs_ref, p_buf, p_sem,
    )

    io.wait("late")
    gln_ref[...] = jnp.zeros_like(gln_ref)

    def tile(i, carry):
        rows = rows_of(i)
        grad_q, grad_kv = stream_grads(
            rows,
            (dq_ref, dk_ref, dv_ref),
            (dqs_ref, dks_ref, dvs_ref),
            (w0_ref, w1_ref),
            (w2_ref, w3_ref),
        )
        low_kv = grad_kv.astype(bf16)
        gmem_ref[rows, :] = low_kv
        placed_ref[rows, :] = low_kv.astype(f32)
        io.send(gmem_ref, rows)
        io.send(placed_ref, rows)
        grad_norm, grad_gain, grad_shift = norm_backward(
            second_ref[rows, :], norms_ref[4:5], grad_q
        )
        g2 = g_ref[rows, :] + grad_norm
        g2_ref[rows, :] = g2
        g2_low_ref[rows, :] = g2.astype(bf16)
        io.send(g2_ref, rows)
        io.send(g2_low_ref, rows)
        gln_ref[0:1, :] += grad_gain
        gln_ref[1:2, :] += grad_shift
        return carry

    lax.fori_loop(0, TILES, tile, 0)


def self_back_second(
    meta, io, g_low_ref, rank_row_ref, limit_ref, w2_ref, w3_ref,
    q_ref, k_ref, v_ref, mixed_ref, p_ref,
    dq_ref, dk_ref, dv_ref,
    rank_ref, dm_ref, dqs_ref, dks_ref, dvs_ref, p_buf, p_sem,
):
    back_second_docs(
        False, meta, io, g_low_ref, rank_row_ref, limit_ref, (w2_ref, w3_ref), q_ref, k_ref, v_ref,
        mixed_ref, p_ref, rank_ref, dm_ref, dqs_ref, dks_ref, dvs_ref, p_buf, p_sem,
    )
    dq_ref[...] = dqs_ref[...].astype(bf16)
    dk_ref[...] = dks_ref[...].astype(bf16)
    dv_ref[...] = dvs_ref[...].astype(bf16)


def self_back_finish(
    meta, io, g_ref, xq_ref, xc_ref, norms_ref, w0_ref, w1_ref, w2_ref, w3_ref,
    dq_ref, dk_ref, dv_ref, dq2_ref, dk2_ref, dv2_ref,
    placed_q_ref, placed_c_ref, gq_ref, gc_ref, gln_ref,
):
    gln_ref[...] = jnp.zeros_like(gln_ref)

    def tile(i, carry):
        rows = rows_of(i)
        io.wait_rows(i)
        grad_q, grad_kv = stream_grads(
            rows,
            (dq_ref, dk_ref, dv_ref),
            (dq2_ref, dk2_ref, dv2_ref),
            (w0_ref, w1_ref),
            (w2_ref, w3_ref),
        )
        grad_norm, grad_gain, grad_shift = norm_backward(
            xq_ref[rows, :].astype(f32), norms_ref[0:1], grad_q
        )
        low_q = (g_ref[rows, :] + grad_norm).astype(bf16)
        gq_ref[rows, :] = low_q
        placed_q_ref[rows, :] = low_q.astype(f32)
        io.send(gq_ref, rows)
        io.send(placed_q_ref, rows)
        gln_ref[0:1, :] += grad_gain
        gln_ref[1:2, :] += grad_shift
        grad_norm, grad_gain, grad_shift = norm_backward(
            xc_ref[rows, :].astype(f32), norms_ref[2:3], grad_kv
        )
        low_c = grad_norm.astype(bf16)
        gc_ref[rows, :] = low_c
        placed_c_ref[rows, :] = low_c.astype(f32)
        io.send(gc_ref, rows)
        io.send(placed_c_ref, rows)
        gln_ref[2:3, :] += grad_gain
        gln_ref[3:4, :] += grad_shift
        return carry

    lax.fori_loop(0, TILES, tile, 0)


def place_rows(meta, *refs):
    count = len(refs) // 3
    for n in range(count):
        refs[2 * count + n][...] = refs[n][...].astype(refs[2 * count + n].dtype)


GROUP = 8


def position(meta):
    r = meta[35]
    return lax.rem(r, 2), r // 2


def join(own, other, rows):
    return (own[rows, :].astype(f32) + other[rows, :].astype(f32)).astype(bf16)


def join_halves(meta, own, other, keep, send):
    y, _ = position(meta)
    size = keep.shape[0]
    keep[...] = join(own, other, rows_of(y, size))
    send[...] = join(own, other, rows_of(1 - y, size))


def join_chunks(meta, kept, arrived, keep, sends):
    _, z = position(meta)
    size = keep.shape[0]
    keep[...] = join(kept, arrived, rows_of(z, size))
    for s, (send, first) in enumerate(sends, 1):
        send[first : first + size, :] = join(kept, arrived, rows_of(z ^ s, size))


def add_up(kept, parts, first):
    size = kept.shape[0]
    total = kept[...].astype(f32)
    for part in parts:
        total = total + part[first : first + size, :].astype(f32)
    return total.astype(bf16)


def half_of(meta, total, parts, first, half):
    _, z = position(meta)
    size = total.shape[0]
    half[rows_of(z, size), :] = total[...]
    for s, part in enumerate(parts, 1):
        half[rows_of(z ^ s, size), :] = part[first : first + size, :]


def slot_1(meta, ffn_own, ffn_other, keep, send):
    join_halves(meta, ffn_own, ffn_other, keep, send)


def slot_2(
    meta, ffn_kept, ffn_arrived, cross_own, cross_other, ffn_keep, f1, f2, f3, keep, send
):
    join_chunks(meta, ffn_kept, ffn_arrived, ffn_keep, [(f1, 0), (f2, 0), (f3, 0)])
    join_halves(meta, cross_own, cross_other, keep, send)


def slot_3(
    meta, ffn_kept, f1, f2, f3, cross_kept, cross_arrived, self_own, self_other,
    ffn_total, cross_keep, m1, m2, m3, self_keep, self_send,
):
    join_halves(meta, self_own, self_other, self_keep, self_send)
    total = add_up(ffn_kept, (f1, f2, f3), 0)
    ffn_total[...] = total
    size = total.shape[0]
    join_chunks(meta, cross_kept, cross_arrived, cross_keep, [(m, size) for m in (m1, m2, m3)])
    for m in (m1, m2, m3):
        m[0:size, :] = total


def slot_4(
    meta, ffn_total, m1, m2, m3, cross_kept, self_kept, self_arrived,
    ffn_half, cross_total, self_keep, *sends,
):
    join_chunks(meta, self_kept, self_arrived, self_keep, [(send, 0) for send in sends])
    total = add_up(cross_kept, (m1, m2, m3), ffn_total.shape[0])
    cross_total[...] = total
    size = total.shape[0]
    for send in sends:
        send[size:, :] = total
    half_of(meta, ffn_total, (m1, m2, m3), 0, ffn_half)


def slot_5(meta, self_kept, cross_total, m1, m2, m3, gln_own, gln_other, send, cross_half):
    size = self_kept.shape[0]
    total = add_up(self_kept, (m1, m2, m3), 0)
    gln = gln_own[...] + gln_other[...]
    gln = jnp.concatenate([gln, jnp.zeros((8, D), f32)], axis=0).astype(bf16)
    for r in range(GROUP):
        send[r, 0:size, :] = total
        send[r, size : size + 16, :] = gln
    half_of(meta, cross_total, (m1, m2, m3), size, cross_half)


def unpack_attention(whole_ref, outs):
    for i in range(3):
        outs[i][...] = whole_ref[:, 128 * i : 128 * i + 128].astype(f32)
    for j in range(4):
        rows = slice(128 * j, 128 * j + 128)
        outs[3][:, rows] = whole_ref[rows, 384:512].astype(f32)


def unpack_early(meta, ffn_half, ffn_arrived, cross_half, cross_arrived, *refs):
    *outs, cross_whole, ffn_whole = refs
    y, _ = position(meta)
    cross_whole[rows_of(y, 256), :] = cross_half[...]
    cross_whole[rows_of(1 - y, 256), :] = cross_arrived[...]
    unpack_attention(cross_whole, outs[2:])
    ffn_whole[rows_of(y, 512), :] = ffn_half[...]
    ffn_whole[rows_of(1 - y, 512), :] = ffn_arrived[...]
    outs[0][...] = ffn_whole[0:512, :].astype(f32)
    outs[1][...] = ffn_whole[512:1024, :].astype(f32)


def unpack_late(meta, parts, *refs):
    *outs, gln, whole_ref = refs
    size = parts.shape[1] - 16
    total = parts[0, size : size + 16, :].astype(f32)
    for r in range(1, GROUP):
        total = total + parts[r, size : size + 16, :].astype(f32)
    gln[...] = total[0:8]
    for r in range(GROUP):
        first = size * (4 * (r % 2) + r // 2)
        whole_ref[first : first + size, :] = parts[r, 0:size, :]
    unpack_attention(whole_ref, outs)


def whole(shape):
    zeros = (0,) * len(shape)
    return pl.BlockSpec(shape, lambda d, meta: zeros)


def own_row(width):
    return pl.BlockSpec((SEQ, width), lambda d, meta: (meta[0], 0))


ANY = pl.BlockSpec(memory_space=pl.ANY)


def in_hbm(x):
    return pltpu.with_memory_space_constraint(x, pltpu.HBM)


probability_out = (pltpu.HBM((DOCS, 4, FAST_K, FAST_Q), bf16), None, ANY)
probability_scratch = [
    pltpu.VMEM((2, TOGETHER, 4, FAST_K, FAST_Q), bf16),
    pltpu.SemaphoreType.DMA((2,)),
]


class Copies:
    def __init__(self, meta):
        self.first = meta[0] * SEQ
        self.loads = {}
        self.tiles = []
        self.sends = []

    def load(self, stage, source, target, sems, own_row):
        if stage == "tiles":
            first = self.first if own_row else 0
            self.tiles.append((source, target, sems, first))
            return
        if own_row:
            source = source.at[pl.ds(pl.multiple_of(self.first, SEQ), SEQ)]
        copy = pltpu.make_async_copy(source, target, sems[0].at[sems[1], 0])
        self.loads.setdefault(stage, []).append(copy)

    def tile(self, entry, i):
        source, target, (sems, b), first = entry
        rows = pl.ds(pl.multiple_of(first + i * TILE, TILE), TILE)
        return pltpu.make_async_copy(source.at[rows], target.at[rows_of(i)], sems.at[b, i])

    def start(self):
        for copy in self.loads.get("now", []):
            copy.start()
        for i in range(TILES):
            for entry in self.tiles:
                self.tile(entry, i).start()
        for stage in ("soon", "late"):
            for copy in self.loads.get(stage, []):
                copy.start()

    def wait(self, stage):
        for copy in self.loads.pop(stage, []):
            copy.wait()

    def wait_rows(self, i):
        for entry in self.tiles:
            self.tile(entry, i).wait()

    def result(self, source, target, sem, own_row):
        self.sends.append([source, target, sem, own_row, False])

    def send(self, ref, rows=None):
        for entry in self.sends:
            source, target, sem, own_row, _ = entry
            if source is ref:
                entry[4] = True
                first = self.first if own_row else 0
                if rows is None:
                    size = source.shape[0]
                else:
                    source = source.at[rows]
                    first, size = first + rows.start, rows.size
                if rows is not None or own_row:
                    target = target.at[pl.ds(pl.multiple_of(first, size), size)]
                pltpu.make_async_copy(source, target, sem).start()

    def finish(self):
        for stage in list(self.loads):
            self.wait(stage)
        for source, _, _, _, started in self.sends:
            if not started:
                self.send(source)
        for source, target, sem, own_row, _ in self.sends:
            if own_row:
                target = target.at[pl.ds(pl.multiple_of(self.first, SEQ), SEQ)]
            pltpu.make_async_copy(source, target, sem).wait()


def out(shape, dtype, own_row=False):
    return (shape, dtype, own_row)


def call(kernel, name, operands, outs, scratch, flops, token=None):
    arrays = [operands[0][0]]
    in_specs, out_specs, out_shapes = [], [], []
    buffers = []
    loads = []
    for n, (x, how) in enumerate(operands[1:]):
        if isinstance(how, str):
            stage, _, row = how.partition("_")
            shape = ((SEQ,) + x.shape[1:]) if row else x.shape
            loads.append((n, stage, len(buffers), bool(row)))
            buffers.append(pltpu.VMEM(shape, x.dtype))
            arrays.append(in_hbm(x))
            in_specs.append(ANY)
        else:
            arrays.append(x)
            in_specs.append(how)
    results = []
    for n, (shape, dtype, how) in enumerate(outs):
        if isinstance(how, bool):
            results.append((n, len(buffers), how))
            buffers.append(pltpu.VMEM(shape, dtype))
            shape = ((2 * SEQ,) + shape[1:]) if how else shape
            out_shapes.append(pltpu.HBM(shape, dtype))
            out_specs.append(ANY)
        else:
            out_shapes.append(jax.ShapeDtypeStruct(shape, dtype) if dtype else shape)
            out_specs.append(how)
    n_in, n_out = len(in_specs), len(out_specs)
    if token is not None:
        arrays.append(token)
        in_specs.append(whole((8, 128)))
        out_specs.append(whole((8, 128)))
        out_shapes.append(jax.ShapeDtypeStruct((8, 128), f32))

    def body(meta, *refs):
        ins, refs = list(refs[:n_in]), refs[len(in_specs) - n_in + n_in :]
        results_out, refs = list(refs[:n_out]), refs[n_out:]
        if token is not None:
            token_out, refs = refs[0], refs[1:]
            token_out[...] = jnp.zeros_like(token_out)
        bufs, refs = refs[: len(buffers)], refs[len(buffers) :]
        rest = refs[: len(scratch)]
        copies = Copies(meta)
        if buffers:
            sems = refs[len(scratch)]
        for n, stage, b, row in loads:
            copies.load(stage, ins[n], bufs[b], (sems, b), row)
            ins[n] = bufs[b]
        for n, b, row in results:
            copies.result(bufs[b], results_out[n], sems.at[b, 0], row)
            results_out[n] = bufs[b]
        copies.start()
        copies.wait("now")
        if buffers:
            kernel(meta, copies, *ins, *results_out, *rest)
        else:
            kernel(meta, *ins, *results_out, *rest)
        copies.finish()

    moved = sum(x.size * x.dtype.itemsize for x in arrays[1:])
    sems = [pltpu.SemaphoreType.DMA((len(buffers), TILES))] if buffers else []
    return pl.pallas_call(
        body,
        name=name,
        grid_spec=pltpu.PrefetchScalarGridSpec(
            num_scalar_prefetch=1,
            grid=(1,),
            in_specs=in_specs,
            out_specs=out_specs,
            scratch_shapes=buffers + scratch + sems,
        ),
        out_shape=out_shapes,
        compiler_params=pltpu.CompilerParams(
            dimension_semantics=("arbitrary",), vmem_limit_bytes=50 * 1024 * 1024
        ),
        cost_estimate=pl.CostEstimate(
            flops=int(flops), bytes_accessed=int(moved), transcendentals=0
        ),
    )(*arrays)


def simple(kernel, name, meta, operands, outs, scratch=()):
    return pl.pallas_call(
        kernel,
        name=name,
        grid_spec=pltpu.PrefetchScalarGridSpec(
            num_scalar_prefetch=1,
            grid=(1,),
            in_specs=[whole(x.shape) for x in operands],
            out_specs=[whole(shape) for shape, _ in outs],
            scratch_shapes=scratch,
        ),
        out_shape=[jax.ShapeDtypeStruct(shape, dtype) for shape, dtype in outs],
        compiler_params=pltpu.CompilerParams(vmem_limit_bytes=16 * 1024 * 1024),
    )(meta, *operands)


def full(x):
    return (x, whole(x.shape))


def shards(
    query_stream,
    content_stream,
    memory,
    segment_ids,
    source_segments,
    context_rank,
    context_limit,
    padding,
    ln_query_gain,
    ln_query_bias,
    ln_content_gain,
    ln_content_bias,
    self_query,
    self_key,
    self_value,
    self_out,
    ln_cross_gain,
    ln_cross_bias,
    cross_query,
    cross_key,
    cross_value,
    cross_out,
    ln_ffn_gain,
    ln_ffn_bias,
    ffn_in,
    ffn_out,
    cotangent,
):
    core = lax.axis_index("heads") % 2

    def to_core(x):
        return lax.ppermute(x, "heads", [(h, h ^ 1) for h in range(4)])

    hold = lambda *xs: lax.optimization_barrier(xs)

    def to_chip(x):
        return lax.ppermute(x, "heads", [(h, h ^ 2) for h in range(4)])

    row = pl.BlockSpec((1, 8, 128), lambda d, core: (core[0], 0, 0))

    def token_row(x):
        return (in_hbm(x.reshape(2, 8, 128)), row)

    def fixed(x):
        zeros = (0,) * x.ndim
        return (in_hbm(x), pl.BlockSpec(x.shape, lambda d, core: zeros))

    prepared = [
        ((36,), jnp.int32, pl.BlockSpec(memory_space=pltpu.SMEM)),
        ((1, SEQ), f32, whole((1, SEQ))),
        ((1, SEQ), f32, whole((1, SEQ))),
        ((8, D), f32, whole((8, D))),
        ((D, D), bf16, whole((D, D))),
        ((D, D), bf16, whole((D, D))),
    ]
    gains = (
        ln_query_gain,
        ln_query_bias,
        ln_content_gain,
        ln_content_bias,
        ln_cross_gain,
        ln_cross_bias,
        ln_ffn_gain,
        ln_ffn_bias,
    )
    weights = (self_query, self_key, self_value, self_out)
    weights += (cross_query, cross_key, cross_value, cross_out)
    tokens = (segment_ids, source_segments, context_rank, context_limit, padding)
    meta, rank, limit, norms, ws0, wc0 = call(
        prepare,
        "prepare",
        [(jnp.stack([core, lax.axis_index("rows") % GROUP]).astype(jnp.int32), None)]
        + [token_row(x) for x in tokens]
        + [fixed(x.reshape(1, D)) for x in gains]
        + [fixed(x) for x in weights],
        prepared,
        [],
        0,
    )

    ws1 = to_core(ws0)
    ws2 = to_chip(ws0)
    wc1 = to_core(wc0)
    u0, v0 = ffn_in, ffn_out
    meta_in = (meta, None)

    heads_out = [out((SEQ, 256), bf16)] * 4

    def stream_out(dtype, own_row=False):
        return out((SEQ, D), dtype, own_row)

    def now(*xs):
        return [(x, "now") for x in xs]

    def soon(*xs):
        return [(x, "soon") for x in xs]

    def late(*xs):
        return [(x, "late") for x in xs]

    def small(*xs):
        return [(x, whole(x.shape)) for x in xs]

    limits = pltpu.VMEM((SEQ, 128), f32)
    pair_flops = 2 * SEQ * D * 768 + 2 * 2 * 4 * DOCS * FAST_Q * FAST_K * 256

    nq, nc, *first, token = call(
        self_first,
        "self_first",
        [meta_in, (query_stream, "tiles_row"), (content_stream, "tiles_row")]
        + small(rank, limit, norms)
        + now(ws0, ws1),
        [stream_out(bf16), stream_out(bf16)] + heads_out + [probability_out],
        [limits] + probability_scratch,
        pair_flops,
        jnp.zeros((8, 128), f32),
    )
    ws2, wc0, token = hold(ws2, wc0, token)
    ws3 = to_core(ws2)
    wc2 = to_chip(wc0)
    *second_heads, second, ncross, token = call(
        self_second,
        "self_second",
        [meta_in, (query_stream, "late_row")]
        + [(nq, "tiles"), (nc, "tiles")]
        + small(rank, limit, norms)
        + late(ws0, ws1)
        + now(ws2, ws3)
        + late(first[3]),
        heads_out + [probability_out, stream_out(f32), stream_out(bf16)],
        [limits] + probability_scratch,
        pair_flops + 2 * SEQ * D * D,
        token,
    )
    wc2, u0, v0, token = hold(wc2, u0, v0, token)
    wc3 = to_core(wc2)
    u2 = to_chip(u0)
    u1 = to_core(u0)
    *cross_heads, token = call(
        cross_first,
        "cross_first",
        [meta_in, (ncross, "tiles"), (memory, "tiles_row")] + now(wc0, wc1),
        heads_out + [probability_out],
        probability_scratch,
        pair_flops,
        token,
    )
    wc3, u2, v0, token = hold(wc3, u2, v0, token)
    u3 = to_core(u2)
    v2 = to_chip(v0)
    v1 = to_core(v0)
    *cross_heads_second, third, nffn, token = call(
        cross_second,
        "cross_second",
        [meta_in]
        + late(second)
        + [(ncross, "tiles"), (memory, "tiles_row")]
        + small(norms)
        + late(wc0, wc1)
        + now(wc2, wc3)
        + late(cross_heads[3]),
        heads_out + [probability_out, stream_out(f32), stream_out(bf16)],
        probability_scratch,
        pair_flops + 2 * SEQ * D * D,
        token,
    )
    u3, v2, token = hold(u3, v2, token)
    v3 = to_core(v2)
    grads_ln = ((8, D), f32, whole((8, D)))
    placed_output, output, g3, g3_low, gln_ffn, ffn_own, ffn_other, token = call(
        ffn_both,
        "ffn_both",
        [meta_in]
        + [(third, "tiles"), (nffn, "tiles"), (cotangent, "tiles_row")]
        + small(norms)
        + now(u0, u1, u2, u3, v0, v1, v2, v3),
        [
            stream_out(bf16, True),
            stream_out(bf16),
            stream_out(f32),
            stream_out(bf16),
            grads_ln,
            out((1024, D), bf16),
            out((1024, D), bf16),
        ],
        [pltpu.VMEM((SEQ, 1024), bf16), pltpu.VMEM((SEQ, 1024), bf16)],
        12 * SEQ * D * 2048,
        token,
    )

    row_count = lax.axis_size("rows")
    assert row_count % GROUP == 0

    def along_rows(x, s):
        return lax.ppermute(x, "rows", [(r, r ^ s) for r in range(row_count)])

    def to_y(x):
        return along_rows(x, 1)

    def to_z(sends):
        return [along_rows(x, 2 * s) for s, x in enumerate(sends, 1)]

    def rows_out(*sizes):
        return [((n, D), bf16) for n in sizes]

    ffn_other = to_core(ffn_other)

    back_scratch = [pltpu.VMEM((SEQ, 256), bf16)] + [pltpu.VMEM((SEQ, 256), f32)] * 3
    back_scratch += probability_scratch
    pair_out = out((SEQ, 256), bf16)
    packed_outs = [out((D, D), bf16), out((D, D), bf16)]
    back_flops = 2 * SEQ * D * 256 + 4 * 2 * 4 * DOCS * FAST_Q * FAST_K * 256

    def head_inputs(natural, p):
        return soon(*natural) + [(in_hbm(p), ANY)]

    *cross_grads, cross_own, cross_other, token = call(
        functools.partial(attention_back_first, True),
        "cross_back_first",
        [meta_in]
        + [(g3_low, "tiles")]
        + late(ncross)
        + [(memory, "late_row")]
        + small(rank, limit)
        + now(wc0, wc1)
        + head_inputs(cross_heads[0:4], cross_heads[4]),
        [pair_out] * 3 + packed_outs,
        [limits] + back_scratch,
        back_flops + 2 * SEQ * D * 1024,
        token,
    )
    ffn_other, token = hold(ffn_other, token)
    ffn_keep, ffn_send = simple(slot_1, "slot_1", meta, [ffn_own, ffn_other], rows_out(512, 512))
    ffn_send, token = hold(ffn_send, token)
    ffn_arrived = to_y(ffn_send)
    cross_other = to_core(cross_other)
    g2, g2_low, placed_mem, grad_mem, gln_cross, token = call(
        cross_back_second,
        "cross_back_second",
        [meta_in]
        + [(g3_low, "tiles")]
        + late(g3, second)
        + small(norms)
        + late(wc0, wc1)
        + now(wc2, wc3)
        + late(*cross_grads)
        + head_inputs(cross_heads_second[0:4], cross_heads_second[4]),
        [stream_out(f32), stream_out(bf16), stream_out(f32, True), stream_out(bf16), grads_ln],
        back_scratch,
        back_flops + 2 * SEQ * D * 1536,
        token,
    )
    ffn_arrived, cross_other, token = hold(ffn_arrived, cross_other, token)
    ffn_keep, *sends, cross_keep, cross_send = simple(
        slot_2,
        "slot_2",
        meta,
        [ffn_keep, ffn_arrived, cross_own, cross_other],
        rows_out(128, 128, 128, 128, 256, 256),
    )
    ffn_keep, cross_send, token = hold(ffn_keep, cross_send, token)
    ffn_parts = to_z(sends)
    cross_arrived = to_y(cross_send)

    *self_grads, self_own, self_other, token = call(
        functools.partial(attention_back_first, False),
        "self_back_first",
        [meta_in]
        + [(g2_low, "tiles")]
        + late(nq, nc)
        + small(rank, limit)
        + now(ws0, ws1)
        + head_inputs(first[0:4], first[4]),
        [pair_out] * 3 + packed_outs,
        [limits] + back_scratch,
        back_flops + 2 * SEQ * D * 1024,
        token,
    )
    *ffn_parts, cross_arrived, self_other, token = hold(
        *ffn_parts, cross_arrived, self_other, token
    )
    self_other = to_core(self_other)
    ffn_total, cross_keep, *sends, self_keep, self_send = simple(
        slot_3,
        "slot_3",
        meta,
        [ffn_keep, *ffn_parts, cross_keep, cross_arrived, self_own, self_other],
        rows_out(128, 64, 192, 192, 192, 256, 256),
    )
    ffn_total, self_send, token = hold(ffn_total, self_send, token)
    self_arrived = to_y(self_send)
    messages = to_z(sends)
    *self_grads_second, token = call(
        self_back_second,
        "self_back_second",
        [meta_in, (g2_low, "tiles")]
        + small(rank, limit)
        + now(ws2, ws3)
        + head_inputs(second_heads[0:4], second_heads[4]),
        [pair_out] * 3,
        [limits] + back_scratch,
        back_flops,
        token,
    )
    *messages, self_arrived, token = hold(*messages, self_arrived, token)
    ffn_half, cross_total, self_keep, *sends = simple(
        slot_4,
        "slot_4",
        meta,
        [ffn_total, *messages, cross_keep, self_keep, self_arrived],
        rows_out(512, 64, 64, 128, 128, 128),
    )
    cross_total, ffn_half, token = hold(cross_total, ffn_half, token)
    messages = to_z(sends)
    ffn_arrived = to_y(ffn_half)
    placed_q, placed_c, gq, gc, gln_self, token = call(
        self_back_finish,
        "self_back_finish",
        [meta_in, (g2, "tiles"), (query_stream, "tiles_row"), (content_stream, "tiles_row")]
        + small(norms)
        + now(ws0, ws1, ws2, ws3)
        + [(x, "tiles") for x in self_grads + self_grads_second],
        [stream_out(f32, True), stream_out(f32, True), stream_out(bf16), stream_out(bf16), grads_ln],
        [],
        2 * SEQ * D * 1536,
        token,
    )
    gln = jnp.concatenate([gln_self[0:4], gln_cross[0:2], gln_ffn[0:2]], axis=0)
    *messages, ffn_arrived, gln = hold(*messages, ffn_arrived, gln)
    last_send, cross_half = simple(
        slot_5,
        "slot_5",
        meta,
        [self_keep, cross_total, *messages, gln, to_core(gln)],
        [((GROUP, 80, D), bf16), ((256, D), bf16)],
    )
    output, grad_mem, last_send = hold(output, grad_mem, last_send)
    groups = None
    if row_count > GROUP:
        groups = [list(range(r, r + GROUP)) for r in range(0, row_count, GROUP)]
    last_parts = lax.all_to_all(last_send, "rows", 0, 0, axis_index_groups=groups)
    cross_arrived = to_y(cross_half)

    def over_groups(totals):
        if row_count == GROUP:
            return totals
        groups = [list(range(r, row_count, GROUP)) for r in range(GROUP)]
        return lax.psum(totals, "rows", axis_index_groups=groups)

    def both_rows(placed_own, arrays, name):
        count = len(arrays)
        size = SEQ // 2
        one = pl.BlockSpec((size, D), lambda i, meta: (i, 0))
        block = pl.BlockSpec((size, D), lambda i, meta: (2 * (1 - meta[0]) + i, 0))
        return pl.pallas_call(
            place_rows,
            name=name,
            grid_spec=pltpu.PrefetchScalarGridSpec(
                num_scalar_prefetch=1,
                grid=(2,),
                in_specs=[one] * count + [pl.BlockSpec(memory_space=pl.ANY)] * count,
                out_specs=[block] * count,
            ),
            out_shape=[jax.ShapeDtypeStruct(x.shape, x.dtype) for x in placed_own],
            input_output_aliases={1 + count + n: n for n in range(count)},
        )(meta, *[to_core(x) for x in arrays], *placed_own)

    out_both, grad_mem_both = both_rows([placed_output, placed_mem], [output, grad_mem], "place_early")
    gq_both, gc_both = both_rows([placed_q, placed_c], [gq, gc], "place_late")

    cross_arrived, out_both, gq_both = hold(cross_arrived, out_both, gq_both)
    attention_outs = [((512, 128), f32)] * 3 + [((128, 512), f32)]
    grad_ffn_in, grad_ffn_out, *grad_cross_parts = simple(
        unpack_early,
        "unpack_early",
        meta,
        [ffn_half, ffn_arrived, cross_half, cross_arrived],
        [((D, D), f32)] * 2 + attention_outs,
        [pltpu.VMEM((D, D), bf16), pltpu.VMEM((2 * D, D), bf16)],
    )
    *grad_self_parts, gln = simple(
        unpack_late,
        "unpack_late",
        meta,
        [last_parts],
        attention_outs + [((8, D), f32)],
        [pltpu.VMEM((D, D), bf16)],
    )
    grad_ffn_in, grad_ffn_out, grad_cross_parts, grad_self_parts, gln = over_groups(
        (grad_ffn_in, grad_ffn_out, grad_cross_parts, grad_self_parts, gln)
    )
    return (
        out_both,
        gq_both,
        gc_both,
        grad_mem_both,
        gln[0],
        gln[1],
        gln[2],
        gln[3],
        *grad_self_parts,
        gln[4],
        gln[5],
        *grad_cross_parts,
        gln[6],
        gln[7],
        grad_ffn_in,
        grad_ffn_out,
    )


def solution(mesh):
    assert mesh.shape["heads"] == 4
    row_spec = P("rows", None)
    flat = P("rows")
    by_column = P(None, "heads")
    by_row = P("heads", None)
    attention = (by_column, by_column, by_column, by_row)
    in_specs = (
        (row_spec,) * 3
        + (flat,) * 5
        + (P(),) * 4
        + attention
        + (P(),) * 2
        + attention
        + (P(),) * 2
        + (by_column, by_row, row_spec)
    )
    out_specs = (
        (row_spec,) * 4
        + (P(),) * 4
        + attention
        + (P(),) * 2
        + attention
        + (P(),) * 2
        + (by_column, by_row)
    )
    return jax.shard_map(shards, mesh=mesh, in_specs=in_specs, out_specs=out_specs, check_vma=False)
```

```python
import functools

import jax
import jax.numpy as jnp
from jax import lax
from jax.experimental import pallas as pl
from jax.experimental.pallas import tpu as pltpu
from jax.sharding import PartitionSpec as P

HEAD_DIM = 64
SEQ = 1024
DOCS = 8
D = 512
TILE = 256
TILES = SEQ // TILE
FAST_Q = 256
FAST_K = 208
LONG_Q = 128
LONG_K = 640

norm_eps = 1e-05
masked_score = -1e30
hidden_rank = 1e6
gelu_root = 0.7978845608028654
gelu_cube = 0.044715

f32 = jnp.float32
bf16 = jnp.bfloat16


def dot(a, b):
    return lax.dot_general(a, b, (((1,), (0,)), ((), ())), preferred_element_type=f32)


def dot_nt(a, b):
    return lax.dot_general(a, b, (((1,), (1,)), ((), ())), preferred_element_type=f32)


def dot_tn(a, b):
    return lax.dot_general(a, b, (((0,), (0,)), ((), ())), preferred_element_type=f32)


def lanes(parts):
    return jnp.concatenate(parts, axis=1)


def layer_norm(values, gain, shift):
    centre = values - jnp.mean(values, axis=-1, keepdims=True)
    spread = jnp.mean(centre * centre, axis=-1, keepdims=True)
    return centre * lax.rsqrt(spread + norm_eps) * gain + shift


def norm_backward(values, gain, grad):
    centre = values - jnp.mean(values, axis=-1, keepdims=True)
    spread = jnp.mean(centre * centre, axis=-1, keepdims=True)
    scale = lax.rsqrt(spread + norm_eps)
    xhat = centre * scale
    eg = grad * gain
    mean_eg = jnp.mean(eg, axis=-1, keepdims=True)
    mean_egx = jnp.mean(eg * xhat, axis=-1, keepdims=True)
    grad_gain = jnp.sum(grad * xhat, axis=0, keepdims=True)
    grad_shift = jnp.sum(grad, axis=0, keepdims=True)
    return scale * (eg - mean_eg - xhat * mean_egx), grad_gain, grad_shift


def rows_of(i, size=TILE):
    return pl.ds(pl.multiple_of(i * size, size), size)


def w_query(ref):
    return ref[:, 0:128]


def w_key(ref):
    return ref[:, 128:256]


def w_value(ref):
    return ref[:, 256:384]


def w_out(ref):
    return lanes([ref[128 * j : 128 * j + 128, 384:512] for j in range(4)])


def half_masks():
    place = lax.broadcasted_iota(jnp.int32, (1, 128), 1)
    low = jnp.where(place < HEAD_DIM, 1.0, 0.0).astype(f32)
    return (low.astype(bf16), (1.0 - low).astype(bf16))


def doc_bounds(meta, d, source):
    base = 17 if source else 1
    return meta[base + d], meta[base + 8 + d]


def window_of(first, limit):
    return pl.multiple_of(jnp.minimum((first // 16) * 16, limit), 16)


def key_bias(ks, ke, k0, width):
    place = k0 + lax.broadcasted_iota(jnp.int32, (width, 128), 0)
    return jnp.where((place >= ks) & (place < ke), 0.0, masked_score)


def make_bias(rank_ref, limit_ref, ks, ke, q0, k0, span, width):
    if rank_ref is None:
        return lanes([key_bias(ks, ke, k0, width)] * (span // 128))
    place = k0 + lax.broadcasted_iota(jnp.int32, (width, 128), 0)
    ranks = rank_ref[pl.ds(k0, width), :]
    ranks = jnp.where((place < ks + 2) & (ranks < hidden_rank), -1.0, ranks)
    ranks = jnp.where((place >= ks) & (place < ke), ranks, hidden_rank)
    limits = jnp.broadcast_to(limit_ref[...], (8, SEQ))
    limits = pltpu.roll(limits, lax.rem(SEQ - q0, SEQ), 1)[0:1, 0:span]
    row = k0 + lax.broadcasted_iota(jnp.int32, (width, span), 0)
    column = q0 + lax.broadcasted_iota(jnp.int32, (width, span), 1)
    seen = (lanes([ranks] * (span // 128)) < limits) & (row != column)
    return jnp.where(seen, 0.0, masked_score)


TOGETHER = 4
STEPS = DOCS // TOGETHER


def interleave(items):
    items = [list(phases) for phases in items]
    depth = max(len(phases) for phases in items)
    results = [None] * len(items)
    for tick in range(len(items) + depth - 1):
        for phase in range(depth):
            n = tick - phase
            if 0 <= n < len(items) and phase < len(items[n]):
                run = items[n][phase]
                results[n] = run() if phase == 0 else run(results[n])
    return results


def is_fast(meta, cross):
    return meta[34 if cross else 33] == 1


def probabilities(scores, bias):
    part = scores + bias
    part = jnp.exp(part - jnp.max(part, axis=0, keepdims=True))
    return (part * (1.0 / jnp.sum(part, axis=0, keepdims=True))).astype(bf16)


def by_halves(pairs, phases):
    shared = [{} for _ in range(pairs)]
    return [phases(n, a, shared[n]) for n in range(pairs) for a in range(2)]


def for_docs(meta, cross, run, before, after):
    @pl.when(is_fast(meta, cross))
    def _():
        def step(i, carry):
            slot = lax.rem(i, 2)
            before(i, slot)
            items = []
            for place in range(TOGETHER):
                d = TOGETHER * i + place
                ts, te = doc_bounds(meta, d, False)
                ks, ke = doc_bounds(meta, d, cross)
                q0 = window_of(ts, SEQ - FAST_Q)
                k0 = window_of(ks, SEQ - FAST_K)
                items += run(d, slot, place, q0, k0, FAST_Q, FAST_K, ts, te, ks, ke, True)
            interleave(items)
            after(i, slot)
            return carry

        lax.fori_loop(0, STEPS, step, 0)

    @pl.when(jnp.logical_not(is_fast(meta, cross)))
    def _():
        def doc(d, carry):
            ts, te = doc_bounds(meta, d, False)
            ks, ke = doc_bounds(meta, d, cross)
            base = (ts // 16) * 16
            k0 = window_of(ks, SEQ - LONG_K)

            def chunk(i, carry):
                lower = base + i * LONG_Q
                q0 = pl.multiple_of(jnp.minimum(lower, SEQ - LONG_Q), 16)
                low = jnp.maximum(ts, lower)
                high = jnp.minimum(te, lower + LONG_Q)
                interleave(run(d, None, None, q0, k0, LONG_Q, LONG_K, low, high, ks, ke, False))
                return carry

            return lax.fori_loop(0, (te - base + LONG_Q - 1) // LONG_Q, chunk, carry)

        lax.fori_loop(0, DOCS, doc, 0)


def attend_docs(meta, cross, rank_ref, limit_ref, halves, p_ref, p_buf, p_sem):
    pairs = 2 * len(halves)
    masks = half_masks()

    def save(i, slot):
        return pltpu.make_async_copy(p_buf.at[slot], p_ref.at[pl.ds(TOGETHER * i, TOGETHER)], p_sem.at[slot])

    def before(i, slot):
        @pl.when(i >= 2)
        def _():
            save(i - 2, slot).wait()

    def after(i, slot):
        save(i, slot).start()

    def run(d, slot, place, q0, k0, span, width, low, high, ks, ke, fast):
        bias = make_bias(rank_ref, limit_ref, ks, ke, q0, k0, span, width)
        row = q0 + lax.broadcasted_iota(jnp.int32, (span, 128), 0)
        inside = (row >= low) & (row < high)

        def phases(n, a, pair):
            q_ref, k_ref, v_ref, mixed_ref = halves[n // 2]
            cols = slice(128 * (n % 2), 128 * (n % 2) + 128)

            def score():
                keys = k_ref[pl.ds(k0, width), cols] * masks[a]
                return dot_nt(keys, q_ref[pl.ds(q0, span), cols])

            def weigh(scores):
                part = probabilities(scores, bias)
                if fast:
                    p_buf[slot, place, 2 * n + a] = part
                return part

            def mix(part):
                if a == 0:
                    pair["values"] = jnp.transpose(v_ref[pl.ds(k0, width), cols])
                half = dot(pair["values"][64 * a : 64 * a + 64], part)
                if a == 0:
                    pair["mixed"] = half
                    return
                mixed = jnp.transpose(jnp.concatenate([pair["mixed"], half], axis=0))
                old = mixed_ref[pl.ds(q0, span), cols].astype(f32)
                mixed_ref[pl.ds(q0, span), cols] = jnp.where(inside, mixed, old).astype(bf16)

            return score, weigh, mix

        return by_halves(pairs, phases)

    for_docs(meta, cross, run, before, after)

    @pl.when(is_fast(meta, cross))
    def _():
        for i in range(STEPS - 2, STEPS):
            save(i, i % 2).wait()


def load_step(load, i, slot):
    p_ref, p_buf, p_sem = load
    return pltpu.make_async_copy(p_ref.at[pl.ds(TOGETHER * i, TOGETHER)], p_buf.at[slot], p_sem.at[slot])


def start_load(meta, cross, load):
    @pl.when(is_fast(meta, cross))
    def _():
        load_step(load, 0, 0).start()


def attend_docs_back(
    meta, cross, rank_ref, limit_ref, q_ref, k_ref, v_ref, mixed_ref, dm_ref,
    dq_ref, dk_ref, dv_ref, load,
):
    pairs = q_ref.shape[1] // 128
    masks = half_masks()
    p_buf = load[1]

    def before(i, slot):
        @pl.when(i + 1 < STEPS)
        def _():
            load_step(load, i + 1, 1 - slot).start()

        load_step(load, i, slot).wait()

    def after(i, slot):
        pass

    def run(d, slot, place, q0, k0, span, width, low, high, ks, ke, fast):
        row = q0 + lax.broadcasted_iota(jnp.int32, (span, 128), 0)
        inside = jnp.where((row >= low) & (row < high), 1.0, 0.0).astype(bf16)
        ones = jnp.ones((width, 128), bf16)
        if not fast:
            bias = make_bias(rank_ref, limit_ref, ks, ke, q0, k0, span, width)

        def phases(n, a, pair):
            cols = slice(128 * n, 128 * n + 128)
            mask = masks[a]

            def differ():
                if a == 0:
                    mixed = mixed_ref[pl.ds(q0, span), cols]
                    pair["grad"] = dm_ref[pl.ds(q0, span), cols] * inside
                    pair["left"] = lanes([pair["grad"], -(pair["grad"] * mixed)])
                right = lanes([v_ref[pl.ds(k0, width), cols] * mask, ones * mask])
                return dot_nt(right, pair["left"])

            def slope(delta):
                if fast:
                    part = p_buf[slot, place, 2 * n + a]
                else:
                    keys = k_ref[pl.ds(k0, width), cols] * mask
                    part = probabilities(dot_nt(keys, q_ref[pl.ds(q0, span), cols]), bias)
                return part, part * delta.astype(bf16)

            def spread(state):
                part, change = state
                dk = dot(change, q_ref[pl.ds(q0, span), cols] * mask)
                dv = dot(part, pair["grad"] * mask)
                if a == 0:
                    pair["keys"] = jnp.transpose(k_ref[pl.ds(k0, width), cols])
                half = dot(pair["keys"][64 * a : 64 * a + 64], change)
                if a == 0:
                    pair["sums"] = dk, dv, half
                    return
                first_dk, first_dv, first_half = pair["sums"]
                dq = jnp.transpose(jnp.concatenate([first_half, half], axis=0))
                dq_ref[pl.ds(q0, span), cols] += dq * (HEAD_DIM**-0.5)
                dk_ref[pl.ds(k0, width), cols] += first_dk + dk
                dv_ref[pl.ds(k0, width), cols] += first_dv + dv

            return differ, slope, spread

        return by_halves(pairs, phases)

    for_docs(meta, cross, run, before, after)


def spread_ranks(rank_row_ref, rank_ref):
    rank_ref[...] = jnp.transpose(jnp.broadcast_to(rank_row_ref[...], (128, SEQ)))


def prepare(
    core, seg_ref, src_ref, rank_ref, limit_ref, pad_ref,
    n0, n1, n2, n3, n4, n5, n6, n7, sq, sk, sv, so, cq, ck, cv, co,
    meta_ref, ranks_ref, limits_ref, norms_ref, ws_ref, wc_ref,
):
    meta_ref[0] = core[0]
    meta_ref[35] = core[1]
    for base, ref in ((1, seg_ref), (17, src_ref)):
        ids = ref[0]
        meta_ref[base] = 0
        meta_ref[base + 15] = SEQ
        for d in range(1, DOCS):
            cut = jnp.sum(jnp.where(ids < d, 1.0, 0.0)).astype(jnp.int32)
            meta_ref[base + d] = cut
            meta_ref[base + 7 + d] = cut
    for place, base in ((33, 1), (34, 17)):
        fast = jnp.int32(1)
        for d in range(DOCS):
            q0 = window_of(meta_ref[1 + d], SEQ - FAST_Q)
            k0 = window_of(meta_ref[base + d], SEQ - FAST_K)
            fits = (meta_ref[9 + d] - q0 <= FAST_Q) & (meta_ref[base + 8 + d] - k0 <= FAST_K)
            fast = fast & fits.astype(jnp.int32)
        meta_ref[place] = fast
    ranks = jnp.where(pad_ref[0] != 0, hidden_rank, rank_ref[0].astype(f32))
    limits = limit_ref[0].astype(f32)
    for i in range(8):
        ranks_ref[0:1, 128 * i : 128 * i + 128] = ranks[i : i + 1]
        limits_ref[0:1, 128 * i : 128 * i + 128] = limits[i : i + 1]
    for i, ref in enumerate((n0, n1, n2, n3, n4, n5, n6, n7)):
        norms_ref[i : i + 1, :] = ref[...]
    for to, parts, out in ((ws_ref, (sq, sk, sv), so), (wc_ref, (cq, ck, cv), co)):
        for i, part in enumerate(parts):
            to[:, 128 * i : 128 * i + 128] = part[...]
        for j in range(4):
            to[128 * j : 128 * j + 128, 384:512] = out[:, 128 * j : 128 * j + 128]


def self_first(
    meta, io, xq_ref, xc_ref, rank_row_ref, limit_ref, norms_ref, w0_ref, w1_ref,
    nq_ref, nc_ref, q_ref, k_ref, v_ref, mixed_ref, p_ref, rank_ref, p_buf, p_sem,
):

    spread_ranks(rank_row_ref, rank_ref)
    wq = lanes([w_query(w0_ref), w_query(w1_ref)])
    wkv = lanes([w_key(w0_ref), w_key(w1_ref), w_value(w0_ref), w_value(w1_ref)])

    def tile(i, carry):
        rows = rows_of(i)
        io.wait_rows(i)
        nq = layer_norm(xq_ref[rows, :].astype(f32), norms_ref[0:1], norms_ref[1:2]).astype(bf16)
        nc = layer_norm(xc_ref[rows, :].astype(f32), norms_ref[2:3], norms_ref[3:4]).astype(bf16)
        nq_ref[rows, :] = nq
        nc_ref[rows, :] = nc
        q_ref[rows, :] = (dot(nq, wq) * (HEAD_DIM**-0.5)).astype(bf16)
        kv = dot(nc, wkv).astype(bf16)
        k_ref[rows, :] = kv[:, :256]
        v_ref[rows, :] = kv[:, 256:]
        return carry

    lax.fori_loop(0, TILES, tile, 0)

    for ref in (nq_ref, nc_ref, q_ref, k_ref, v_ref):
        io.send(ref)
    attend_docs(meta, False, rank_ref, limit_ref, [(q_ref, k_ref, v_ref, mixed_ref)], p_ref, p_buf, p_sem)


def self_second(
    meta, io, xq_ref, nq_ref, nc_ref, rank_row_ref, limit_ref, norms_ref, w0_ref, w1_ref, w2_ref, w3_ref,
    mixed_first_ref,
    q_ref, k_ref, v_ref, mixed_ref, p_ref, second_ref, ncross_ref, rank_ref, p_buf, p_sem,
):

    spread_ranks(rank_row_ref, rank_ref)
    wq = lanes([w_query(w2_ref), w_query(w3_ref)])
    wkv = lanes([w_key(w2_ref), w_key(w3_ref), w_value(w2_ref), w_value(w3_ref)])

    def tile(i, carry):
        rows = rows_of(i)
        io.wait_rows(i)
        q_ref[rows, :] = (dot(nq_ref[rows, :], wq) * (HEAD_DIM**-0.5)).astype(bf16)
        kv = dot(nc_ref[rows, :], wkv).astype(bf16)
        k_ref[rows, :] = kv[:, :256]
        v_ref[rows, :] = kv[:, 256:]
        return carry

    lax.fori_loop(0, TILES, tile, 0)

    for ref in (q_ref, k_ref, v_ref):
        io.send(ref)
    attend_docs(meta, False, rank_ref, limit_ref, [(q_ref, k_ref, v_ref, mixed_ref)], p_ref, p_buf, p_sem)

    io.send(mixed_ref)
    io.wait("late")
    out_first = jnp.concatenate([w_out(w0_ref), w_out(w1_ref)], axis=0)
    out_second = jnp.concatenate([w_out(w2_ref), w_out(w3_ref)], axis=0)

    def tile(i, carry):
        rows = rows_of(i)
        branch = dot(mixed_first_ref[rows, :], out_first) + dot(mixed_ref[rows, :], out_second)
        second = xq_ref[rows, :].astype(f32) + branch
        second_ref[rows, :] = second
        io.send(second_ref, rows)
        ncross_ref[rows, :] = layer_norm(second, norms_ref[4:5], norms_ref[5:6]).astype(bf16)
        io.send(ncross_ref, rows)
        return carry

    lax.fori_loop(0, TILES, tile, 0)


def project_cross(io, ncross_ref, memory_ref, weights, q_ref, k_ref, v_ref):
    wq = lanes([w_query(w) for w in weights])
    wkv = lanes([w_key(w) for w in weights] + [w_value(w) for w in weights])

    def tile(i, carry):
        rows = rows_of(i)
        io.wait_rows(i)
        q_ref[rows, :] = (dot(ncross_ref[rows, :], wq) * (HEAD_DIM**-0.5)).astype(bf16)
        kv = dot(memory_ref[rows, :], wkv).astype(bf16)
        k_ref[rows, :] = kv[:, :256]
        v_ref[rows, :] = kv[:, 256:]
        return carry

    lax.fori_loop(0, TILES, tile, 0)
    for ref in (q_ref, k_ref, v_ref):
        io.send(ref)


def cross_first(
    meta, io, ncross_ref, memory_ref, w0_ref, w1_ref,
    q_ref, k_ref, v_ref, mixed_ref, p_ref, p_buf, p_sem,
):
    project_cross(io, ncross_ref, memory_ref, (w0_ref, w1_ref), q_ref, k_ref, v_ref)
    attend_docs(meta, True, None, None, [(q_ref, k_ref, v_ref, mixed_ref)], p_ref, p_buf, p_sem)


def cross_second(
    meta, io, second_ref, ncross_ref, memory_ref, norms_ref, w0_ref, w1_ref, w2_ref, w3_ref,
    mixed_first_ref,
    q_ref, k_ref, v_ref, mixed_ref, p_ref, third_ref, nffn_ref, p_buf, p_sem,
):
    project_cross(io, ncross_ref, memory_ref, (w2_ref, w3_ref), q_ref, k_ref, v_ref)
    attend_docs(meta, True, None, None, [(q_ref, k_ref, v_ref, mixed_ref)], p_ref, p_buf, p_sem)
    io.send(mixed_ref)
    io.wait("late")
    out_first = jnp.concatenate([w_out(w0_ref), w_out(w1_ref)], axis=0)
    out_second = jnp.concatenate([w_out(w2_ref), w_out(w3_ref)], axis=0)

    def tile(i, carry):
        rows = rows_of(i)
        branch = dot(mixed_first_ref[rows, :], out_first) + dot(mixed_ref[rows, :], out_second)
        third = second_ref[rows, :] + branch
        third_ref[rows, :] = third
        io.send(third_ref, rows)
        nffn_ref[rows, :] = layer_norm(third, norms_ref[6:7], norms_ref[7:8]).astype(bf16)
        io.send(nffn_ref, rows)
        return carry

    lax.fori_loop(0, TILES, tile, 0)


def ffn_both(
    meta, io, third_ref, nffn_ref, cot_ref, norms_ref, u0_ref, u1_ref, u2_ref, u3_ref,
    w0_ref, w1_ref, w2_ref, w3_ref,
    placed_ref, out_ref, g3_ref, g3_low_ref, gln_ref, own_ref, other_ref, hidden_ref, before_ref,
):
    gln_ref[...] = jnp.zeros_like(gln_ref)
    in_refs = (u0_ref, u1_ref, u2_ref, u3_ref)
    w_refs = (w0_ref, w1_ref, w2_ref, w3_ref)

    def tile(i, carry):
        rows = rows_of(i)
        io.wait_rows(i)
        nffn = nffn_ref[rows, :]
        cot = cot_ref[rows, :]
        outs = []
        grads = []

        def phases(g, c, group):
            w_in = in_refs[g]
            w_out_rows = w_refs[g]
            cols = slice(256 * c, 256 * c + 256)

            def enter():
                return dot(nffn, w_in[:, cols]), dot_nt(cot, w_out_rows[cols, :])

            def bend(state):
                x, grad_hidden = state
                square = x * x
                half = 0.5 + 0.5 * jnp.tanh(x * (gelu_root + (gelu_root * gelu_cube) * square))
                value = x * half
                rise = 2.0 * gelu_root + (6.0 * gelu_root * gelu_cube) * square
                slope = half + value * (1.0 - half) * rise
                hidden = value.astype(bf16)
                grad_before = (grad_hidden * slope).astype(bf16)
                if g < 2:
                    place = slice(512 * g + 256 * c, 512 * g + 256 * c + 256)
                    hidden_ref[rows, place] = hidden
                    before_ref[rows, place] = grad_before
                group[c] = hidden, grad_before

            def leave(_):
                if c == 1:
                    outs.append(dot(lanes([group[0][0], group[1][0]]), w_out_rows[...]))

            def leave_back(_):
                if c == 1:
                    grads.append(dot_nt(lanes([group[0][1], group[1][1]]), w_in[...]))

            return enter, bend, leave, leave_back

        interleave(by_halves(4, phases))
        third = third_ref[rows, :]
        result = (third + ((outs[0] + outs[1]) + (outs[2] + outs[3]))).astype(bf16)
        out_ref[rows, :] = result
        placed_ref[rows, :] = result
        grad_normed = (grads[0] + grads[1]) + (grads[2] + grads[3])
        grad_norm, grad_gain, grad_shift = norm_backward(third, norms_ref[6:7], grad_normed)
        g3 = cot.astype(f32) + grad_norm
        g3_ref[rows, :] = g3
        g3_low_ref[rows, :] = g3.astype(bf16)
        gln_ref[0:1, :] += grad_gain
        gln_ref[1:2, :] += grad_shift
        for ref in (out_ref, placed_ref, g3_ref, g3_low_ref):
            io.send(ref, rows)
        return carry

    lax.fori_loop(0, TILES, tile, 0)
    part = dot_tn(nffn_ref[...], before_ref[...])
    own_ref[0:512, :] = part[:, 0:512].astype(bf16)
    other_ref[0:512, :] = part[:, 512:1024].astype(bf16)
    io.send(own_ref, pl.ds(0, 512))
    io.send(other_ref, pl.ds(0, 512))
    part = dot_tn(hidden_ref[...], cot_ref[...])
    own_ref[512:1024, :] = part[0:512].astype(bf16)
    other_ref[512:1024, :] = part[512:1024].astype(bf16)
    io.send(own_ref, pl.ds(512, 512))
    io.send(other_ref, pl.ds(512, 512))


def back_start(io, g_ref, mixed_ref, w_refs, dm_ref, dq_ref, dk_ref, dv_ref):
    out_rows = jnp.concatenate([w_out(w) for w in w_refs], axis=0)

    def tile(i, carry):
        rows = rows_of(i)
        io.wait_rows(i)
        dm_ref[rows, :] = dot_nt(g_ref[rows, :], out_rows).astype(bf16)
        zeros = jnp.zeros((TILE, 256), f32)
        dq_ref[rows, :] = zeros
        dk_ref[rows, :] = zeros
        dv_ref[rows, :] = zeros
        return carry

    lax.fori_loop(0, TILES, tile, 0)


def attention_back_first(
    cross, meta, io, g_ref, nq_ref, nkv_ref, rank_row_ref, limit_ref, w0_ref, w1_ref,
    q_ref, k_ref, v_ref, mixed_ref, p_ref,
    dq_ref, dk_ref, dv_ref, own_ref, other_ref,
    rank_ref, dm_ref, dqs_ref, dks_ref, dvs_ref, p_buf, p_sem,
):
    load = (p_ref, p_buf, p_sem)
    start_load(meta, cross, load)
    if not cross:
        spread_ranks(rank_row_ref, rank_ref)
    back_start(io, g_ref, mixed_ref, (w0_ref, w1_ref), dm_ref, dqs_ref, dks_ref, dvs_ref)

    io.wait("soon")
    attend_docs_back(
        meta, cross, None if cross else rank_ref, limit_ref, q_ref, k_ref, v_ref, mixed_ref,
        dm_ref, dqs_ref, dks_ref, dvs_ref, load,
    )

    dq_ref[...] = dqs_ref[...].astype(bf16)
    dk_ref[...] = dks_ref[...].astype(bf16)
    dv_ref[...] = dvs_ref[...].astype(bf16)
    for ref in (dq_ref, dk_ref, dv_ref):
        io.send(ref)
    io.wait("late")
    nq = nq_ref[...]
    nkv = nkv_ref[...]
    for n, part in enumerate(
        (dot_tn(nq, dq_ref[...]), dot_tn(nkv, dk_ref[...]), dot_tn(nkv, dv_ref[...]))
    ):
        own_ref[:, 128 * n : 128 * n + 128] = part[:, :128].astype(bf16)
        other_ref[:, 128 * n : 128 * n + 128] = part[:, 128:].astype(bf16)
    part = dot_tn(mixed_ref[...], g_ref[...])
    for j in range(4):
        rows = slice(128 * j, 128 * j + 128)
        own_ref[rows, 384:512] = part[:128, rows].astype(bf16)
        other_ref[rows, 384:512] = part[128:, rows].astype(bf16)


def back_second_docs(
    cross, meta, io, g_ref, rank_row_ref, limit_ref, w_refs, q_ref, k_ref, v_ref, mixed_ref, p_ref,
    rank_ref, dm_ref, dqs_ref, dks_ref, dvs_ref, p_buf, p_sem,
):
    load = (p_ref, p_buf, p_sem)
    start_load(meta, cross, load)
    if not cross:
        spread_ranks(rank_row_ref, rank_ref)
    back_start(io, g_ref, mixed_ref, w_refs, dm_ref, dqs_ref, dks_ref, dvs_ref)

    io.wait("soon")
    attend_docs_back(
        meta, cross, None if cross else rank_ref, limit_ref, q_ref, k_ref, v_ref, mixed_ref,
        dm_ref, dqs_ref, dks_ref, dvs_ref, load,
    )


def stream_grads(rows, first, second, firsts, seconds):
    dq, dk, dv = first
    dq2, dk2, dv2 = (ref[rows, :].astype(bf16) for ref in second)
    w0, w1 = firsts
    w2, w3 = seconds
    grad_q = dot_nt(dq[rows, :], lanes([w_query(w0), w_query(w1)])) + dot_nt(
        dq2, lanes([w_query(w2), w_query(w3)])
    )
    kv = lanes([dk[rows, :], dv[rows, :]])
    kv2 = lanes([dk2, dv2])
    grad_kv = dot_nt(kv, lanes([w_key(w0), w_key(w1), w_value(w0), w_value(w1)])) + dot_nt(
        kv2, lanes([w_key(w2), w_key(w3), w_value(w2), w_value(w3)])
    )
    return grad_q, grad_kv


def cross_back_second(
    meta, io, g_low_ref, g_ref, second_ref, norms_ref, w0_ref, w1_ref, w2_ref, w3_ref,
    dq_ref, dk_ref, dv_ref, q_ref, k_ref, v_ref, mixed_ref, p_ref,
    g2_ref, g2_low_ref, placed_ref, gmem_ref, gln_ref,
    dm_ref, dqs_ref, dks_ref, dvs_ref, p_buf, p_sem,
):
    back_second_docs(
        True, meta, io, g_low_ref, None, None, (w2_ref, w3_ref), q_ref, k_ref, v_ref, mixed_ref, p_ref,
        None, dm_ref, dqs_ref, dks_ref, dvs_ref, p_buf, p_sem,
    )

    io.wait("late")
    gln_ref[...] = jnp.zeros_like(gln_ref)

    def tile(i, carry):
        rows = rows_of(i)
        grad_q, grad_kv = stream_grads(
            rows,
            (dq_ref, dk_ref, dv_ref),
            (dqs_ref, dks_ref, dvs_ref),
            (w0_ref, w1_ref),
            (w2_ref, w3_ref),
        )
        low_kv = grad_kv.astype(bf16)
        gmem_ref[rows, :] = low_kv
        placed_ref[rows, :] = low_kv.astype(f32)
        io.send(gmem_ref, rows)
        io.send(placed_ref, rows)
        grad_norm, grad_gain, grad_shift = norm_backward(
            second_ref[rows, :], norms_ref[4:5], grad_q
        )
        g2 = g_ref[rows, :] + grad_norm
        g2_ref[rows, :] = g2
        g2_low_ref[rows, :] = g2.astype(bf16)
        io.send(g2_ref, rows)
        io.send(g2_low_ref, rows)
        gln_ref[0:1, :] += grad_gain
        gln_ref[1:2, :] += grad_shift
        return carry

    lax.fori_loop(0, TILES, tile, 0)


def self_back_second(
    meta, io, g_low_ref, rank_row_ref, limit_ref, w2_ref, w3_ref,
    q_ref, k_ref, v_ref, mixed_ref, p_ref,
    dq_ref, dk_ref, dv_ref,
    rank_ref, dm_ref, dqs_ref, dks_ref, dvs_ref, p_buf, p_sem,
):
    back_second_docs(
        False, meta, io, g_low_ref, rank_row_ref, limit_ref, (w2_ref, w3_ref), q_ref, k_ref, v_ref,
        mixed_ref, p_ref, rank_ref, dm_ref, dqs_ref, dks_ref, dvs_ref, p_buf, p_sem,
    )
    dq_ref[...] = dqs_ref[...].astype(bf16)
    dk_ref[...] = dks_ref[...].astype(bf16)
    dv_ref[...] = dvs_ref[...].astype(bf16)


def self_back_finish(
    meta, io, g_ref, xq_ref, xc_ref, norms_ref, w0_ref, w1_ref, w2_ref, w3_ref,
    dq_ref, dk_ref, dv_ref, dq2_ref, dk2_ref, dv2_ref,
    placed_q_ref, placed_c_ref, gq_ref, gc_ref, gln_ref,
):
    gln_ref[...] = jnp.zeros_like(gln_ref)

    def tile(i, carry):
        rows = rows_of(i)
        io.wait_rows(i)
        grad_q, grad_kv = stream_grads(
            rows,
            (dq_ref, dk_ref, dv_ref),
            (dq2_ref, dk2_ref, dv2_ref),
            (w0_ref, w1_ref),
            (w2_ref, w3_ref),
        )
        grad_norm, grad_gain, grad_shift = norm_backward(
            xq_ref[rows, :].astype(f32), norms_ref[0:1], grad_q
        )
        low_q = (g_ref[rows, :] + grad_norm).astype(bf16)
        gq_ref[rows, :] = low_q
        placed_q_ref[rows, :] = low_q.astype(f32)
        io.send(gq_ref, rows)
        io.send(placed_q_ref, rows)
        gln_ref[0:1, :] += grad_gain
        gln_ref[1:2, :] += grad_shift
        grad_norm, grad_gain, grad_shift = norm_backward(
            xc_ref[rows, :].astype(f32), norms_ref[2:3], grad_kv
        )
        low_c = grad_norm.astype(bf16)
        gc_ref[rows, :] = low_c
        placed_c_ref[rows, :] = low_c.astype(f32)
        io.send(gc_ref, rows)
        io.send(placed_c_ref, rows)
        gln_ref[2:3, :] += grad_gain
        gln_ref[3:4, :] += grad_shift
        return carry

    lax.fori_loop(0, TILES, tile, 0)


def place_rows(meta, *refs):
    count = len(refs) // 3
    for n in range(count):
        refs[2 * count + n][...] = refs[n][...].astype(refs[2 * count + n].dtype)


GROUP = 8


def position(meta):
    r = meta[35]
    return lax.rem(r, 2), r // 2


def join(own, other, rows):
    return (own[rows, :].astype(f32) + other[rows, :].astype(f32)).astype(bf16)


def join_halves(meta, own, other, keep, send):
    y, _ = position(meta)
    size = keep.shape[0]
    keep[...] = join(own, other, rows_of(y, size))
    send[...] = join(own, other, rows_of(1 - y, size))


def join_chunks(meta, kept, arrived, keep, sends):
    _, z = position(meta)
    size = keep.shape[0]
    keep[...] = join(kept, arrived, rows_of(z, size))
    for s, (send, first) in enumerate(sends, 1):
        send[first : first + size, :] = join(kept, arrived, rows_of(z ^ s, size))


def add_up(kept, parts, first):
    size = kept.shape[0]
    total = kept[...].astype(f32)
    for part in parts:
        total = total + part[first : first + size, :].astype(f32)
    return total.astype(bf16)


def half_of(meta, total, parts, first, half):
    _, z = position(meta)
    size = total.shape[0]
    half[rows_of(z, size), :] = total[...]
    for s, part in enumerate(parts, 1):
        half[rows_of(z ^ s, size), :] = part[first : first + size, :]


def slot_1(meta, ffn_own, ffn_other, keep, send):
    join_halves(meta, ffn_own, ffn_other, keep, send)


def slot_2(
    meta, ffn_kept, ffn_arrived, cross_own, cross_other, ffn_keep, f1, f2, f3, keep, send
):
    join_chunks(meta, ffn_kept, ffn_arrived, ffn_keep, [(f1, 0), (f2, 0), (f3, 0)])
    join_halves(meta, cross_own, cross_other, keep, send)


def slot_3(
    meta, ffn_kept, f1, f2, f3, cross_kept, cross_arrived, self_own, self_other,
    ffn_total, cross_keep, m1, m2, m3, self_keep, self_send,
):
    join_halves(meta, self_own, self_other, self_keep, self_send)
    total = add_up(ffn_kept, (f1, f2, f3), 0)
    ffn_total[...] = total
    size = total.shape[0]
    join_chunks(meta, cross_kept, cross_arrived, cross_keep, [(m, size) for m in (m1, m2, m3)])
    for m in (m1, m2, m3):
        m[0:size, :] = total


def slot_4(
    meta, ffn_total, m1, m2, m3, cross_kept, self_kept, self_arrived,
    ffn_half, cross_total, self_keep, *sends,
):
    join_chunks(meta, self_kept, self_arrived, self_keep, [(send, 0) for send in sends])
    total = add_up(cross_kept, (m1, m2, m3), ffn_total.shape[0])
    cross_total[...] = total
    size = total.shape[0]
    for send in sends:
        send[size:, :] = total
    half_of(meta, ffn_total, (m1, m2, m3), 0, ffn_half)


def slot_5(meta, self_kept, cross_total, m1, m2, m3, gln_own, gln_other, send, cross_half):
    size = self_kept.shape[0]
    total = add_up(self_kept, (m1, m2, m3), 0)
    gln = gln_own[...] + gln_other[...]
    gln = jnp.concatenate([gln, jnp.zeros((8, D), f32)], axis=0).astype(bf16)
    for r in range(GROUP):
        send[r, 0:size, :] = total
        send[r, size : size + 16, :] = gln
    half_of(meta, cross_total, (m1, m2, m3), size, cross_half)


def unpack_attention(whole_ref, outs):
    for i in range(3):
        outs[i][...] = whole_ref[:, 128 * i : 128 * i + 128].astype(f32)
    for j in range(4):
        rows = slice(128 * j, 128 * j + 128)
        outs[3][:, rows] = whole_ref[rows, 384:512].astype(f32)


def unpack_early(meta, ffn_half, ffn_arrived, cross_half, cross_arrived, *refs):
    *outs, cross_whole, ffn_whole = refs
    y, _ = position(meta)
    cross_whole[rows_of(y, 256), :] = cross_half[...]
    cross_whole[rows_of(1 - y, 256), :] = cross_arrived[...]
    unpack_attention(cross_whole, outs[2:])
    ffn_whole[rows_of(y, 512), :] = ffn_half[...]
    ffn_whole[rows_of(1 - y, 512), :] = ffn_arrived[...]
    outs[0][...] = ffn_whole[0:512, :].astype(f32)
    outs[1][...] = ffn_whole[512:1024, :].astype(f32)


def unpack_late(meta, parts, *refs):
    *outs, gln, whole_ref = refs
    size = parts.shape[1] - 16
    total = parts[0, size : size + 16, :].astype(f32)
    for r in range(1, GROUP):
        total = total + parts[r, size : size + 16, :].astype(f32)
    gln[...] = total[0:8]
    for r in range(GROUP):
        first = size * (4 * (r % 2) + r // 2)
        whole_ref[first : first + size, :] = parts[r, 0:size, :]
    unpack_attention(whole_ref, outs)


def whole(shape):
    zeros = (0,) * len(shape)
    return pl.BlockSpec(shape, lambda d, meta: zeros)


def own_row(width):
    return pl.BlockSpec((SEQ, width), lambda d, meta: (meta[0], 0))


ANY = pl.BlockSpec(memory_space=pl.ANY)


def in_hbm(x):
    return pltpu.with_memory_space_constraint(x, pltpu.HBM)


probability_out = (pltpu.HBM((DOCS, 4, FAST_K, FAST_Q), bf16), None, ANY)
probability_scratch = [
    pltpu.VMEM((2, TOGETHER, 4, FAST_K, FAST_Q), bf16),
    pltpu.SemaphoreType.DMA((2,)),
]


class Copies:
    def __init__(self, meta):
        self.first = meta[0] * SEQ
        self.loads = {}
        self.tiles = []
        self.sends = []

    def load(self, stage, source, target, sems, own_row):
        if stage == "tiles":
            first = self.first if own_row else 0
            self.tiles.append((source, target, sems, first))
            return
        if own_row:
            source = source.at[pl.ds(pl.multiple_of(self.first, SEQ), SEQ)]
        copy = pltpu.make_async_copy(source, target, sems[0].at[sems[1], 0])
        self.loads.setdefault(stage, []).append(copy)

    def tile(self, entry, i):
        source, target, (sems, b), first = entry
        rows = pl.ds(pl.multiple_of(first + i * TILE, TILE), TILE)
        return pltpu.make_async_copy(source.at[rows], target.at[rows_of(i)], sems.at[b, i])

    def start(self):
        for copy in self.loads.get("now", []):
            copy.start()
        for i in range(TILES):
            for entry in self.tiles:
                self.tile(entry, i).start()
        for stage in ("soon", "late"):
            for copy in self.loads.get(stage, []):
                copy.start()

    def wait(self, stage):
        for copy in self.loads.pop(stage, []):
            copy.wait()

    def wait_rows(self, i):
        for entry in self.tiles:
            self.tile(entry, i).wait()

    def result(self, source, target, sem, own_row):
        self.sends.append([source, target, sem, own_row, False])

    def send(self, ref, rows=None):
        for entry in self.sends:
            source, target, sem, own_row, _ = entry
            if source is ref:
                entry[4] = True
                first = self.first if own_row else 0
                if rows is None:
                    size = source.shape[0]
                else:
                    source = source.at[rows]
                    first, size = first + rows.start, rows.size
                if rows is not None or own_row:
                    target = target.at[pl.ds(pl.multiple_of(first, size), size)]
                pltpu.make_async_copy(source, target, sem).start()

    def finish(self):
        for stage in list(self.loads):
            self.wait(stage)
        for source, _, _, _, started in self.sends:
            if not started:
                self.send(source)
        for source, target, sem, own_row, _ in self.sends:
            if own_row:
                target = target.at[pl.ds(pl.multiple_of(self.first, SEQ), SEQ)]
            pltpu.make_async_copy(source, target, sem).wait()


def out(shape, dtype, own_row=False):
    return (shape, dtype, own_row)


def call(kernel, name, operands, outs, scratch, flops, token=None):
    arrays = [operands[0][0]]
    in_specs, out_specs, out_shapes = [], [], []
    buffers = []
    loads = []
    for n, (x, how) in enumerate(operands[1:]):
        if isinstance(how, str):
            stage, _, row = how.partition("_")
            shape = ((SEQ,) + x.shape[1:]) if row else x.shape
            loads.append((n, stage, len(buffers), bool(row)))
            buffers.append(pltpu.VMEM(shape, x.dtype))
            arrays.append(in_hbm(x))
            in_specs.append(ANY)
        else:
            arrays.append(x)
            in_specs.append(how)
    results = []
    for n, (shape, dtype, how) in enumerate(outs):
        if isinstance(how, bool):
            results.append((n, len(buffers), how))
            buffers.append(pltpu.VMEM(shape, dtype))
            shape = ((2 * SEQ,) + shape[1:]) if how else shape
            out_shapes.append(pltpu.HBM(shape, dtype))
            out_specs.append(ANY)
        else:
            out_shapes.append(jax.ShapeDtypeStruct(shape, dtype) if dtype else shape)
            out_specs.append(how)
    n_in, n_out = len(in_specs), len(out_specs)
    if token is not None:
        arrays.append(token)
        in_specs.append(whole((8, 128)))
        out_specs.append(whole((8, 128)))
        out_shapes.append(jax.ShapeDtypeStruct((8, 128), f32))

    def body(meta, *refs):
        ins, refs = list(refs[:n_in]), refs[len(in_specs) - n_in + n_in :]
        results_out, refs = list(refs[:n_out]), refs[n_out:]
        if token is not None:
            token_out, refs = refs[0], refs[1:]
            token_out[...] = jnp.zeros_like(token_out)
        bufs, refs = refs[: len(buffers)], refs[len(buffers) :]
        rest = refs[: len(scratch)]
        copies = Copies(meta)
        if buffers:
            sems = refs[len(scratch)]
        for n, stage, b, row in loads:
            copies.load(stage, ins[n], bufs[b], (sems, b), row)
            ins[n] = bufs[b]
        for n, b, row in results:
            copies.result(bufs[b], results_out[n], sems.at[b, 0], row)
            results_out[n] = bufs[b]
        copies.start()
        copies.wait("now")
        if buffers:
            kernel(meta, copies, *ins, *results_out, *rest)
        else:
            kernel(meta, *ins, *results_out, *rest)
        copies.finish()

    moved = sum(x.size * x.dtype.itemsize for x in arrays[1:])
    sems = [pltpu.SemaphoreType.DMA((len(buffers), TILES))] if buffers else []
    return pl.pallas_call(
        body,
        name=name,
        grid_spec=pltpu.PrefetchScalarGridSpec(
            num_scalar_prefetch=1,
            grid=(1,),
            in_specs=in_specs,
            out_specs=out_specs,
            scratch_shapes=buffers + scratch + sems,
        ),
        out_shape=out_shapes,
        compiler_params=pltpu.CompilerParams(
            dimension_semantics=("arbitrary",), vmem_limit_bytes=50 * 1024 * 1024
        ),
        cost_estimate=pl.CostEstimate(
            flops=int(flops), bytes_accessed=int(moved), transcendentals=0
        ),
    )(*arrays)


def simple(kernel, name, meta, operands, outs, scratch=()):
    return pl.pallas_call(
        kernel,
        name=name,
        grid_spec=pltpu.PrefetchScalarGridSpec(
            num_scalar_prefetch=1,
            grid=(1,),
            in_specs=[whole(x.shape) for x in operands],
            out_specs=[whole(shape) for shape, _ in outs],
            scratch_shapes=scratch,
        ),
        out_shape=[jax.ShapeDtypeStruct(shape, dtype) for shape, dtype in outs],
        compiler_params=pltpu.CompilerParams(vmem_limit_bytes=16 * 1024 * 1024),
    )(meta, *operands)


def full(x):
    return (x, whole(x.shape))


def shards(
    query_stream,
    content_stream,
    memory,
    segment_ids,
    source_segments,
    context_rank,
    context_limit,
    padding,
    ln_query_gain,
    ln_query_bias,
    ln_content_gain,
    ln_content_bias,
    self_query,
    self_key,
    self_value,
    self_out,
    ln_cross_gain,
    ln_cross_bias,
    cross_query,
    cross_key,
    cross_value,
    cross_out,
    ln_ffn_gain,
    ln_ffn_bias,
    ffn_in,
    ffn_out,
    cotangent,
):
    core = lax.axis_index("heads") % 2

    def to_core(x):
        return lax.ppermute(x, "heads", [(h, h ^ 1) for h in range(4)])

    hold = lambda *xs: lax.optimization_barrier(xs)

    def to_chip(x):
        return lax.ppermute(x, "heads", [(h, h ^ 2) for h in range(4)])

    row = pl.BlockSpec((1, 8, 128), lambda d, core: (core[0], 0, 0))

    def token_row(x):
        return (in_hbm(x.reshape(2, 8, 128)), row)

    def fixed(x):
        zeros = (0,) * x.ndim
        return (in_hbm(x), pl.BlockSpec(x.shape, lambda d, core: zeros))

    prepared = [
        ((36,), jnp.int32, pl.BlockSpec(memory_space=pltpu.SMEM)),
        ((1, SEQ), f32, whole((1, SEQ))),
        ((1, SEQ), f32, whole((1, SEQ))),
        ((8, D), f32, whole((8, D))),
        ((D, D), bf16, whole((D, D))),
        ((D, D), bf16, whole((D, D))),
    ]
    gains = (
        ln_query_gain,
        ln_query_bias,
        ln_content_gain,
        ln_content_bias,
        ln_cross_gain,
        ln_cross_bias,
        ln_ffn_gain,
        ln_ffn_bias,
    )
    weights = (self_query, self_key, self_value, self_out)
    weights += (cross_query, cross_key, cross_value, cross_out)
    tokens = (segment_ids, source_segments, context_rank, context_limit, padding)
    meta, rank, limit, norms, ws0, wc0 = call(
        prepare,
        "prepare",
        [(jnp.stack([core, lax.axis_index("rows") % GROUP]).astype(jnp.int32), None)]
        + [token_row(x) for x in tokens]
        + [fixed(x.reshape(1, D)) for x in gains]
        + [fixed(x) for x in weights],
        prepared,
        [],
        0,
    )

    ws1 = to_core(ws0)
    ws2 = to_chip(ws0)
    wc1 = to_core(wc0)
    u0, v0 = ffn_in, ffn_out
    meta_in = (meta, None)

    heads_out = [out((SEQ, 256), bf16)] * 4

    def stream_out(dtype, own_row=False):
        return out((SEQ, D), dtype, own_row)

    def now(*xs):
        return [(x, "now") for x in xs]

    def soon(*xs):
        return [(x, "soon") for x in xs]

    def late(*xs):
        return [(x, "late") for x in xs]

    def small(*xs):
        return [(x, whole(x.shape)) for x in xs]

    limits = pltpu.VMEM((SEQ, 128), f32)
    pair_flops = 2 * SEQ * D * 768 + 2 * 2 * 4 * DOCS * FAST_Q * FAST_K * 256

    nq, nc, *first, token = call(
        self_first,
        "self_first",
        [meta_in, (query_stream, "tiles_row"), (content_stream, "tiles_row")]
        + small(rank, limit, norms)
        + now(ws0, ws1),
        [stream_out(bf16), stream_out(bf16)] + heads_out + [probability_out],
        [limits] + probability_scratch,
        pair_flops,
        jnp.zeros((8, 128), f32),
    )
    ws2, wc0, token = hold(ws2, wc0, token)
    ws3 = to_core(ws2)
    wc2 = to_chip(wc0)
    *second_heads, second, ncross, token = call(
        self_second,
        "self_second",
        [meta_in, (query_stream, "late_row")]
        + [(nq, "tiles"), (nc, "tiles")]
        + small(rank, limit, norms)
        + late(ws0, ws1)
        + now(ws2, ws3)
        + late(first[3]),
        heads_out + [probability_out, stream_out(f32), stream_out(bf16)],
        [limits] + probability_scratch,
        pair_flops + 2 * SEQ * D * D,
        token,
    )
    wc2, u0, v0, token = hold(wc2, u0, v0, token)
    wc3 = to_core(wc2)
    u2 = to_chip(u0)
    u1 = to_core(u0)
    *cross_heads, token = call(
        cross_first,
        "cross_first",
        [meta_in, (ncross, "tiles"), (memory, "tiles_row")] + now(wc0, wc1),
        heads_out + [probability_out],
        probability_scratch,
        pair_flops,
        token,
    )
    wc3, u2, v0, token = hold(wc3, u2, v0, token)
    u3 = to_core(u2)
    v2 = to_chip(v0)
    v1 = to_core(v0)
    *cross_heads_second, third, nffn, token = call(
        cross_second,
        "cross_second",
        [meta_in]
        + late(second)
        + [(ncross, "tiles"), (memory, "tiles_row")]
        + small(norms)
        + late(wc0, wc1)
        + now(wc2, wc3)
        + late(cross_heads[3]),
        heads_out + [probability_out, stream_out(f32), stream_out(bf16)],
        probability_scratch,
        pair_flops + 2 * SEQ * D * D,
        token,
    )
    u3, v2, token = hold(u3, v2, token)
    v3 = to_core(v2)
    grads_ln = ((8, D), f32, whole((8, D)))
    placed_output, output, g3, g3_low, gln_ffn, ffn_own, ffn_other, token = call(
        ffn_both,
        "ffn_both",
        [meta_in]
        + [(third, "tiles"), (nffn, "tiles"), (cotangent, "tiles_row")]
        + small(norms)
        + now(u0, u1, u2, u3, v0, v1, v2, v3),
        [
            stream_out(bf16, True),
            stream_out(bf16),
            stream_out(f32),
            stream_out(bf16),
            grads_ln,
            out((1024, D), bf16),
            out((1024, D), bf16),
        ],
        [pltpu.VMEM((SEQ, 1024), bf16), pltpu.VMEM((SEQ, 1024), bf16)],
        12 * SEQ * D * 2048,
        token,
    )

    row_count = lax.axis_size("rows")
    assert row_count % GROUP == 0

    def along_rows(x, s):
        return lax.ppermute(x, "rows", [(r, r ^ s) for r in range(row_count)])

    def to_y(x):
        return along_rows(x, 1)

    def to_z(sends):
        return [along_rows(x, 2 * s) for s, x in enumerate(sends, 1)]

    def rows_out(*sizes):
        return [((n, D), bf16) for n in sizes]

    ffn_other = to_core(ffn_other)

    back_scratch = [pltpu.VMEM((SEQ, 256), bf16)] + [pltpu.VMEM((SEQ, 256), f32)] * 3
    back_scratch += probability_scratch
    pair_out = out((SEQ, 256), bf16)
    packed_outs = [out((D, D), bf16), out((D, D), bf16)]
    back_flops = 2 * SEQ * D * 256 + 4 * 2 * 4 * DOCS * FAST_Q * FAST_K * 256

    def head_inputs(natural, p):
        return soon(*natural) + [(in_hbm(p), ANY)]

    *cross_grads, cross_own, cross_other, token = call(
        functools.partial(attention_back_first, True),
        "cross_back_first",
        [meta_in]
        + [(g3_low, "tiles")]
        + late(ncross)
        + [(memory, "late_row")]
        + small(rank, limit)
        + now(wc0, wc1)
        + head_inputs(cross_heads[0:4], cross_heads[4]),
        [pair_out] * 3 + packed_outs,
        [limits] + back_scratch,
        back_flops + 2 * SEQ * D * 1024,
        token,
    )
    ffn_other, token = hold(ffn_other, token)
    ffn_keep, ffn_send = simple(slot_1, "slot_1", meta, [ffn_own, ffn_other], rows_out(512, 512))
    ffn_send, token = hold(ffn_send, token)
    ffn_arrived = to_y(ffn_send)
    cross_other = to_core(cross_other)
    g2, g2_low, placed_mem, grad_mem, gln_cross, token = call(
        cross_back_second,
        "cross_back_second",
        [meta_in]
        + [(g3_low, "tiles")]
        + late(g3, second)
        + small(norms)
        + late(wc0, wc1)
        + now(wc2, wc3)
        + late(*cross_grads)
        + head_inputs(cross_heads_second[0:4], cross_heads_second[4]),
        [stream_out(f32), stream_out(bf16), stream_out(f32, True), stream_out(bf16), grads_ln],
        back_scratch,
        back_flops + 2 * SEQ * D * 1536,
        token,
    )
    ffn_arrived, cross_other, token = hold(ffn_arrived, cross_other, token)
    ffn_keep, *sends, cross_keep, cross_send = simple(
        slot_2,
        "slot_2",
        meta,
        [ffn_keep, ffn_arrived, cross_own, cross_other],
        rows_out(128, 128, 128, 128, 256, 256),
    )
    ffn_keep, cross_send, token = hold(ffn_keep, cross_send, token)
    ffn_parts = to_z(sends)
    cross_arrived = to_y(cross_send)

    *self_grads, self_own, self_other, token = call(
        functools.partial(attention_back_first, False),
        "self_back_first",
        [meta_in]
        + [(g2_low, "tiles")]
        + late(nq, nc)
        + small(rank, limit)
        + now(ws0, ws1)
        + head_inputs(first[0:4], first[4]),
        [pair_out] * 3 + packed_outs,
        [limits] + back_scratch,
        back_flops + 2 * SEQ * D * 1024,
        token,
    )
    *ffn_parts, cross_arrived, self_other, token = hold(
        *ffn_parts, cross_arrived, self_other, token
    )
    self_other = to_core(self_other)
    ffn_total, cross_keep, *sends, self_keep, self_send = simple(
        slot_3,
        "slot_3",
        meta,
        [ffn_keep, *ffn_parts, cross_keep, cross_arrived, self_own, self_other],
        rows_out(128, 64, 192, 192, 192, 256, 256),
    )
    ffn_total, self_send, token = hold(ffn_total, self_send, token)
    self_arrived = to_y(self_send)
    messages = to_z(sends)
    *self_grads_second, token = call(
        self_back_second,
        "self_back_second",
        [meta_in, (g2_low, "tiles")]
        + small(rank, limit)
        + now(ws2, ws3)
        + head_inputs(second_heads[0:4], second_heads[4]),
        [pair_out] * 3,
        [limits] + back_scratch,
        back_flops,
        token,
    )
    *messages, self_arrived, token = hold(*messages, self_arrived, token)
    ffn_half, cross_total, self_keep, *sends = simple(
        slot_4,
        "slot_4",
        meta,
        [ffn_total, *messages, cross_keep, self_keep, self_arrived],
        rows_out(512, 64, 64, 128, 128, 128),
    )
    cross_total, ffn_half, token = hold(cross_total, ffn_half, token)
    messages = to_z(sends)
    ffn_arrived = to_y(ffn_half)
    placed_q, placed_c, gq, gc, gln_self, token = call(
        self_back_finish,
        "self_back_finish",
        [meta_in, (g2, "tiles"), (query_stream, "tiles_row"), (content_stream, "tiles_row")]
        + small(norms)
        + now(ws0, ws1, ws2, ws3)
        + [(x, "tiles") for x in self_grads + self_grads_second],
        [stream_out(f32, True), stream_out(f32, True), stream_out(bf16), stream_out(bf16), grads_ln],
        [],
        2 * SEQ * D * 1536,
        token,
    )
    gln = jnp.concatenate([gln_self[0:4], gln_cross[0:2], gln_ffn[0:2]], axis=0)
    *messages, ffn_arrived, gln = hold(*messages, ffn_arrived, gln)
    last_send, cross_half = simple(
        slot_5,
        "slot_5",
        meta,
        [self_keep, cross_total, *messages, gln, to_core(gln)],
        [((GROUP, 80, D), bf16), ((256, D), bf16)],
    )
    output, grad_mem, last_send = hold(output, grad_mem, last_send)
    groups = None
    if row_count > GROUP:
        groups = [list(range(r, r + GROUP)) for r in range(0, row_count, GROUP)]
    last_parts = lax.all_to_all(last_send, "rows", 0, 0, axis_index_groups=groups)
    cross_arrived = to_y(cross_half)

    def over_groups(totals):
        if row_count == GROUP:
            return totals
        groups = [list(range(r, row_count, GROUP)) for r in range(GROUP)]
        return lax.psum(totals, "rows", axis_index_groups=groups)

    def both_rows(placed_own, arrays, name):
        count = len(arrays)
        size = SEQ // 2
        one = pl.BlockSpec((size, D), lambda i, meta: (i, 0))
        block = pl.BlockSpec((size, D), lambda i, meta: (2 * (1 - meta[0]) + i, 0))
        return pl.pallas_call(
            place_rows,
            name=name,
            grid_spec=pltpu.PrefetchScalarGridSpec(
                num_scalar_prefetch=1,
                grid=(2,),
                in_specs=[one] * count + [pl.BlockSpec(memory_space=pl.ANY)] * count,
                out_specs=[block] * count,
            ),
            out_shape=[jax.ShapeDtypeStruct(x.shape, x.dtype) for x in placed_own],
            input_output_aliases={1 + count + n: n for n in range(count)},
        )(meta, *[to_core(x) for x in arrays], *placed_own)

    out_both, grad_mem_both = both_rows([placed_output, placed_mem], [output, grad_mem], "place_early")
    gq_both, gc_both = both_rows([placed_q, placed_c], [gq, gc], "place_late")

    cross_arrived, out_both, gq_both = hold(cross_arrived, out_both, gq_both)
    attention_outs = [((512, 128), f32)] * 3 + [((128, 512), f32)]
    grad_ffn_in, grad_ffn_out, *grad_cross_parts = simple(
        unpack_early,
        "unpack_early",
        meta,
        [ffn_half, ffn_arrived, cross_half, cross_arrived],
        [((D, D), f32)] * 2 + attention_outs,
        [pltpu.VMEM((D, D), bf16), pltpu.VMEM((2 * D, D), bf16)],
    )
    *grad_self_parts, gln = simple(
        unpack_late,
        "unpack_late",
        meta,
        [last_parts],
        attention_outs + [((8, D), f32)],
        [pltpu.VMEM((D, D), bf16)],
    )
    grad_ffn_in, grad_ffn_out, grad_cross_parts, grad_self_parts, gln = over_groups(
        (grad_ffn_in, grad_ffn_out, grad_cross_parts, grad_self_parts, gln)
    )
    return (
        out_both,
        gq_both,
        gc_both,
        grad_mem_both,
        gln[0],
        gln[1],
        gln[2],
        gln[3],
        *grad_self_parts,
        gln[4],
        gln[5],
        *grad_cross_parts,
        gln[6],
        gln[7],
        grad_ffn_in,
        grad_ffn_out,
    )


def solution(mesh):
    assert mesh.shape["heads"] == 4
    row_spec = P("rows", None)
    flat = P("rows")
    by_column = P(None, "heads")
    by_row = P("heads", None)
    attention = (by_column, by_column, by_column, by_row)
    in_specs = (
        (row_spec,) * 3
        + (flat,) * 5
        + (P(),) * 4
        + attention
        + (P(),) * 2
        + attention
        + (P(),) * 2
        + (by_column, by_row, row_spec)
    )
    out_specs = (
        (row_spec,) * 4
        + (P(),) * 4
        + attention
        + (P(),) * 2
        + attention
        + (P(),) * 2
        + (by_column, by_row)
    )
    return jax.shard_map(shards, mesh=mesh, in_specs=in_specs, out_specs=out_specs, check_vma=False)
```

```python
import functools

import jax
import jax.numpy as jnp
from jax import lax
from jax.experimental import pallas as pl
from jax.experimental.pallas import tpu as pltpu
from jax.sharding import PartitionSpec as P

HEAD_DIM = 64
SEQ = 1024
DOCS = 8
D = 512
TILE = 256
TILES = SEQ // TILE
FAST_Q = 256
FAST_K = 208
LONG_Q = 128
LONG_K = 640

norm_eps = 1e-05
masked_score = -1e30
hidden_rank = 1e6
gelu_root = 0.7978845608028654
gelu_cube = 0.044715

f32 = jnp.float32
bf16 = jnp.bfloat16


def dot(a, b):
    return lax.dot_general(a, b, (((1,), (0,)), ((), ())), preferred_element_type=f32)


def dot_nt(a, b):
    return lax.dot_general(a, b, (((1,), (1,)), ((), ())), preferred_element_type=f32)


def dot_tn(a, b):
    return lax.dot_general(a, b, (((0,), (0,)), ((), ())), preferred_element_type=f32)


def lanes(parts):
    return jnp.concatenate(parts, axis=1)


def layer_norm(values, gain, shift):
    centre = values - jnp.mean(values, axis=-1, keepdims=True)
    spread = jnp.mean(centre * centre, axis=-1, keepdims=True)
    return centre * lax.rsqrt(spread + norm_eps) * gain + shift


def norm_backward(values, gain, grad):
    centre = values - jnp.mean(values, axis=-1, keepdims=True)
    spread = jnp.mean(centre * centre, axis=-1, keepdims=True)
    scale = lax.rsqrt(spread + norm_eps)
    xhat = centre * scale
    eg = grad * gain
    mean_eg = jnp.mean(eg, axis=-1, keepdims=True)
    mean_egx = jnp.mean(eg * xhat, axis=-1, keepdims=True)
    grad_gain = jnp.sum(grad * xhat, axis=0, keepdims=True)
    grad_shift = jnp.sum(grad, axis=0, keepdims=True)
    return scale * (eg - mean_eg - xhat * mean_egx), grad_gain, grad_shift


def rows_of(i, size=TILE):
    return pl.ds(pl.multiple_of(i * size, size), size)


def w_query(ref):
    return ref[:, 0:128]


def w_key(ref):
    return ref[:, 128:256]


def w_value(ref):
    return ref[:, 256:384]


def w_out(ref):
    return lanes([ref[128 * j : 128 * j + 128, 384:512] for j in range(4)])


def half_masks():
    place = lax.broadcasted_iota(jnp.int32, (1, 128), 1)
    low = jnp.where(place < HEAD_DIM, 1.0, 0.0).astype(f32)
    return (low.astype(bf16), (1.0 - low).astype(bf16))


def doc_bounds(meta, d, source):
    base = 17 if source else 1
    return meta[base + d], meta[base + 8 + d]


def window_of(first, limit):
    return pl.multiple_of(jnp.minimum((first // 16) * 16, limit), 16)


def key_bias(ks, ke, k0, width):
    place = k0 + lax.broadcasted_iota(jnp.int32, (width, 128), 0)
    return jnp.where((place >= ks) & (place < ke), 0.0, masked_score)


def make_bias(rank_ref, limit_ref, ks, ke, q0, k0, span, width):
    if rank_ref is None:
        return lanes([key_bias(ks, ke, k0, width)] * (span // 128))
    place = k0 + lax.broadcasted_iota(jnp.int32, (width, 128), 0)
    ranks = rank_ref[pl.ds(k0, width), :]
    ranks = jnp.where((place < ks + 2) & (ranks < hidden_rank), -1.0, ranks)
    ranks = jnp.where((place >= ks) & (place < ke), ranks, hidden_rank)
    limits = jnp.broadcast_to(limit_ref[...], (8, SEQ))
    limits = pltpu.roll(limits, lax.rem(SEQ - q0, SEQ), 1)[0:1, 0:span]
    row = k0 + lax.broadcasted_iota(jnp.int32, (width, span), 0)
    column = q0 + lax.broadcasted_iota(jnp.int32, (width, span), 1)
    seen = (lanes([ranks] * (span // 128)) < limits) & (row != column)
    return jnp.where(seen, 0.0, masked_score)


TOGETHER = 4
STEPS = DOCS // TOGETHER


LAG = 2


def interleave(items):
    items = [list(phases) for phases in items]
    depth = max(len(phases) for phases in items)
    results = [None] * len(items)
    for tick in range(len(items) + LAG * (depth - 1)):
        for phase in range(depth):
            n = tick - LAG * phase
            if 0 <= n < len(items) and phase < len(items[n]):
                run = items[n][phase]
                results[n] = run() if phase == 0 else run(results[n])
    return results


def by_halves(pairs, phases):
    shared = [{} for _ in range(pairs)]
    return [phases(n, a, shared[n]) for n in range(pairs) for a in range(2)]


def is_fast(meta, cross):
    return meta[34 if cross else 33] == 1


def both_heads(x, masks):
    return jnp.concatenate([x * masks[0], x * masks[1]], axis=0)


def pair_scores(queries, keys, masks):
    return dot_nt(both_heads(keys, masks), queries)


def pair_probabilities(scores, bias):
    width = bias.shape[0]
    result = []
    for a in range(2):
        part = scores[width * a : width * a + width] + bias
        part = jnp.exp(part - jnp.max(part, axis=0, keepdims=True))
        part = part * (1.0 / jnp.sum(part, axis=0, keepdims=True))
        result.append(part.astype(bf16))
    return result


def pair_product(rows, parts, scale=1.0):
    across = jnp.transpose(rows)
    halves = [dot(across[64 * a : 64 * a + 64], part) for a, part in enumerate(parts)]
    return jnp.transpose((jnp.concatenate(halves, axis=0) * scale).astype(bf16))


def for_docs(meta, cross, run, before, after):
    @pl.when(is_fast(meta, cross))
    def _():
        def step(i, carry):
            slot = lax.rem(i, 2)
            before(i, slot)
            items = []
            for place in range(TOGETHER):
                d = TOGETHER * i + place
                ts, te = doc_bounds(meta, d, False)
                ks, ke = doc_bounds(meta, d, cross)
                q0 = window_of(ts, SEQ - FAST_Q)
                k0 = window_of(ks, SEQ - FAST_K)
                items += run(d, slot, place, q0, k0, FAST_Q, FAST_K, ts, te, ks, ke, True)
            interleave(items)
            after(i, slot)
            return carry

        lax.fori_loop(0, STEPS, step, 0)

    @pl.when(jnp.logical_not(is_fast(meta, cross)))
    def _():
        def doc(d, carry):
            ts, te = doc_bounds(meta, d, False)
            ks, ke = doc_bounds(meta, d, cross)
            base = (ts // 16) * 16
            k0 = window_of(ks, SEQ - LONG_K)

            def chunk(i, carry):
                lower = base + i * LONG_Q
                q0 = pl.multiple_of(jnp.minimum(lower, SEQ - LONG_Q), 16)
                low = jnp.maximum(ts, lower)
                high = jnp.minimum(te, lower + LONG_Q)
                interleave(run(d, None, None, q0, k0, LONG_Q, LONG_K, low, high, ks, ke, False))
                return carry

            return lax.fori_loop(0, (te - base + LONG_Q - 1) // LONG_Q, chunk, carry)

        lax.fori_loop(0, DOCS, doc, 0)


def attend_docs(meta, cross, rank_ref, limit_ref, halves, p_ref, p_buf, p_sem):
    pairs = 2 * len(halves)
    masks = half_masks()

    def save(i, slot):
        return pltpu.make_async_copy(p_buf.at[slot], p_ref.at[pl.ds(TOGETHER * i, TOGETHER)], p_sem.at[slot])

    def before(i, slot):
        @pl.when(i >= 2)
        def _():
            save(i - 2, slot).wait()

    def after(i, slot):
        save(i, slot).start()

    def run(d, slot, place, q0, k0, span, width, low, high, ks, ke, fast):
        bias = make_bias(rank_ref, limit_ref, ks, ke, q0, k0, span, width)
        row = q0 + lax.broadcasted_iota(jnp.int32, (span, 128), 0)
        inside = (row >= low) & (row < high)

        def phases(n):
            q_ref, k_ref, v_ref, mixed_ref = halves[n // 2]
            cols = slice(128 * (n % 2), 128 * (n % 2) + 128)

            def score():
                return pair_scores(q_ref[pl.ds(q0, span), cols], k_ref[pl.ds(k0, width), cols], masks)

            def weigh(scores):
                parts = pair_probabilities(scores, bias)
                if fast:
                    for a in range(2):
                        p_buf[slot, place, 2 * n + a] = parts[a]
                return parts

            def mix(parts):
                mixed = pair_product(v_ref[pl.ds(k0, width), cols], parts).astype(f32)
                old = mixed_ref[pl.ds(q0, span), cols].astype(f32)
                mixed_ref[pl.ds(q0, span), cols] = jnp.where(inside, mixed, old).astype(bf16)

            return score, weigh, mix

        return [phases(n) for n in range(pairs)]

    for_docs(meta, cross, run, before, after)

    @pl.when(is_fast(meta, cross))
    def _():
        for i in range(STEPS - 2, STEPS):
            save(i, i % 2).wait()


def load_step(load, i, slot):
    p_ref, p_buf, p_sem = load
    return pltpu.make_async_copy(p_ref.at[pl.ds(TOGETHER * i, TOGETHER)], p_buf.at[slot], p_sem.at[slot])


def start_load(meta, cross, load):
    @pl.when(is_fast(meta, cross))
    def _():
        load_step(load, 0, 0).start()


def attend_docs_back(
    meta, cross, rank_ref, limit_ref, q_ref, k_ref, v_ref, mixed_ref, dm_ref,
    dq_ref, dk_ref, dv_ref, load,
):
    pairs = q_ref.shape[1] // 128
    masks = half_masks()
    p_buf = load[1]

    def before(i, slot):
        @pl.when(i + 1 < STEPS)
        def _():
            load_step(load, i + 1, 1 - slot).start()

        load_step(load, i, slot).wait()

    def after(i, slot):
        pass

    def run(d, slot, place, q0, k0, span, width, low, high, ks, ke, fast):
        row = q0 + lax.broadcasted_iota(jnp.int32, (span, 128), 0)
        inside = jnp.where((row >= low) & (row < high), 1.0, 0.0).astype(bf16)
        ones = jnp.ones((width, 128), bf16)
        if not fast:
            bias = make_bias(rank_ref, limit_ref, ks, ke, q0, k0, span, width)

        def phases(n):
            cols = slice(128 * n, 128 * n + 128)

            def differ():
                values = v_ref[pl.ds(k0, width), cols]
                mixed = mixed_ref[pl.ds(q0, span), cols]
                grad = dm_ref[pl.ds(q0, span), cols] * inside
                left = lanes([grad, -(grad * mixed)])
                right = both_heads(lanes([values, ones]), [lanes([m, m]) for m in masks])
                return grad, dot_nt(right, left)

            def slope(state):
                grad, delta = state
                if fast:
                    parts = [p_buf[slot, place, 2 * n + a] for a in range(2)]
                else:
                    queries = q_ref[pl.ds(q0, span), cols]
                    keys = k_ref[pl.ds(k0, width), cols]
                    parts = pair_probabilities(pair_scores(queries, keys, masks), bias)
                slopes = [
                    parts[a] * delta[width * a : width * a + width].astype(bf16) for a in range(2)
                ]
                return grad, parts, slopes

            def spread(state):
                grad, parts, slopes = state
                queries = q_ref[pl.ds(q0, span), cols]
                dk = dv = None
                for a in range(2):
                    dk_a = dot(slopes[a], queries * masks[a])
                    dv_a = dot(parts[a], grad * masks[a])
                    dk = dk_a if dk is None else dk + dk_a
                    dv = dv_a if dv is None else dv + dv_a
                dq = pair_product(k_ref[pl.ds(k0, width), cols], slopes, HEAD_DIM**-0.5)
                dq_ref[pl.ds(q0, span), cols] += dq.astype(f32)
                dk_ref[pl.ds(k0, width), cols] += dk
                dv_ref[pl.ds(k0, width), cols] += dv

            return differ, slope, spread

        return [phases(n) for n in range(pairs)]

    for_docs(meta, cross, run, before, after)


def spread_ranks(rank_row_ref, rank_ref):
    rank_ref[...] = jnp.transpose(jnp.broadcast_to(rank_row_ref[...], (128, SEQ)))


def prepare(
    core, seg_ref, src_ref, rank_ref, limit_ref, pad_ref,
    n0, n1, n2, n3, n4, n5, n6, n7, sq, sk, sv, so, cq, ck, cv, co,
    meta_ref, ranks_ref, limits_ref, norms_ref, ws_ref, wc_ref,
):
    meta_ref[0] = core[0]
    meta_ref[35] = core[1]
    for base, ref in ((1, seg_ref), (17, src_ref)):
        ids = ref[0]
        meta_ref[base] = 0
        meta_ref[base + 15] = SEQ
        for d in range(1, DOCS):
            cut = jnp.sum(jnp.where(ids < d, 1.0, 0.0)).astype(jnp.int32)
            meta_ref[base + d] = cut
            meta_ref[base + 7 + d] = cut
    for place, base in ((33, 1), (34, 17)):
        fast = jnp.int32(1)
        for d in range(DOCS):
            q0 = window_of(meta_ref[1 + d], SEQ - FAST_Q)
            k0 = window_of(meta_ref[base + d], SEQ - FAST_K)
            fits = (meta_ref[9 + d] - q0 <= FAST_Q) & (meta_ref[base + 8 + d] - k0 <= FAST_K)
            fast = fast & fits.astype(jnp.int32)
        meta_ref[place] = fast
    ranks = jnp.where(pad_ref[0] != 0, hidden_rank, rank_ref[0].astype(f32))
    limits = limit_ref[0].astype(f32)
    for i in range(8):
        ranks_ref[0:1, 128 * i : 128 * i + 128] = ranks[i : i + 1]
        limits_ref[0:1, 128 * i : 128 * i + 128] = limits[i : i + 1]
    for i, ref in enumerate((n0, n1, n2, n3, n4, n5, n6, n7)):
        norms_ref[i : i + 1, :] = ref[...]
    for to, parts, out in ((ws_ref, (sq, sk, sv), so), (wc_ref, (cq, ck, cv), co)):
        for i, part in enumerate(parts):
            to[:, 128 * i : 128 * i + 128] = part[...]
        for j in range(4):
            to[128 * j : 128 * j + 128, 384:512] = out[:, 128 * j : 128 * j + 128]


def self_first(
    meta, io, xq_ref, xc_ref, rank_row_ref, limit_ref, norms_ref, w0_ref, w1_ref,
    nq_ref, nc_ref, q_ref, k_ref, v_ref, mixed_ref, p_ref, rank_ref, p_buf, p_sem,
):

    spread_ranks(rank_row_ref, rank_ref)
    wq = lanes([w_query(w0_ref), w_query(w1_ref)])
    wkv = lanes([w_key(w0_ref), w_key(w1_ref), w_value(w0_ref), w_value(w1_ref)])

    def tile(i, carry):
        rows = rows_of(i)
        io.wait_rows(i)
        nq = layer_norm(xq_ref[rows, :].astype(f32), norms_ref[0:1], norms_ref[1:2]).astype(bf16)
        nc = layer_norm(xc_ref[rows, :].astype(f32), norms_ref[2:3], norms_ref[3:4]).astype(bf16)
        nq_ref[rows, :] = nq
        nc_ref[rows, :] = nc
        q_ref[rows, :] = (dot(nq, wq) * (HEAD_DIM**-0.5)).astype(bf16)
        kv = dot(nc, wkv).astype(bf16)
        k_ref[rows, :] = kv[:, :256]
        v_ref[rows, :] = kv[:, 256:]
        return carry

    lax.fori_loop(0, TILES, tile, 0)

    for ref in (nq_ref, nc_ref, q_ref, k_ref, v_ref):
        io.send(ref)
    attend_docs(meta, False, rank_ref, limit_ref, [(q_ref, k_ref, v_ref, mixed_ref)], p_ref, p_buf, p_sem)


def self_second(
    meta, io, xq_ref, nq_ref, nc_ref, rank_row_ref, limit_ref, norms_ref, w0_ref, w1_ref, w2_ref, w3_ref,
    mixed_first_ref,
    q_ref, k_ref, v_ref, mixed_ref, p_ref, second_ref, ncross_ref, rank_ref, p_buf, p_sem,
):

    spread_ranks(rank_row_ref, rank_ref)
    wq = lanes([w_query(w2_ref), w_query(w3_ref)])
    wkv = lanes([w_key(w2_ref), w_key(w3_ref), w_value(w2_ref), w_value(w3_ref)])

    def tile(i, carry):
        rows = rows_of(i)
        io.wait_rows(i)
        q_ref[rows, :] = (dot(nq_ref[rows, :], wq) * (HEAD_DIM**-0.5)).astype(bf16)
        kv = dot(nc_ref[rows, :], wkv).astype(bf16)
        k_ref[rows, :] = kv[:, :256]
        v_ref[rows, :] = kv[:, 256:]
        return carry

    lax.fori_loop(0, TILES, tile, 0)

    for ref in (q_ref, k_ref, v_ref):
        io.send(ref)
    attend_docs(meta, False, rank_ref, limit_ref, [(q_ref, k_ref, v_ref, mixed_ref)], p_ref, p_buf, p_sem)

    io.send(mixed_ref)
    io.wait("late")
    out_first = jnp.concatenate([w_out(w0_ref), w_out(w1_ref)], axis=0)
    out_second = jnp.concatenate([w_out(w2_ref), w_out(w3_ref)], axis=0)

    def tile(i, carry):
        rows = rows_of(i)
        branch = dot(mixed_first_ref[rows, :], out_first) + dot(mixed_ref[rows, :], out_second)
        second = xq_ref[rows, :].astype(f32) + branch
        second_ref[rows, :] = second
        io.send(second_ref, rows)
        ncross_ref[rows, :] = layer_norm(second, norms_ref[4:5], norms_ref[5:6]).astype(bf16)
        io.send(ncross_ref, rows)
        return carry

    lax.fori_loop(0, TILES, tile, 0)


def project_cross(io, ncross_ref, memory_ref, weights, q_ref, k_ref, v_ref):
    wq = lanes([w_query(w) for w in weights])
    wkv = lanes([w_key(w) for w in weights] + [w_value(w) for w in weights])

    def tile(i, carry):
        rows = rows_of(i)
        io.wait_rows(i)
        q_ref[rows, :] = (dot(ncross_ref[rows, :], wq) * (HEAD_DIM**-0.5)).astype(bf16)
        kv = dot(memory_ref[rows, :], wkv).astype(bf16)
        k_ref[rows, :] = kv[:, :256]
        v_ref[rows, :] = kv[:, 256:]
        return carry

    lax.fori_loop(0, TILES, tile, 0)
    for ref in (q_ref, k_ref, v_ref):
        io.send(ref)


def cross_first(
    meta, io, ncross_ref, memory_ref, w0_ref, w1_ref,
    q_ref, k_ref, v_ref, mixed_ref, p_ref, p_buf, p_sem,
):
    project_cross(io, ncross_ref, memory_ref, (w0_ref, w1_ref), q_ref, k_ref, v_ref)
    attend_docs(meta, True, None, None, [(q_ref, k_ref, v_ref, mixed_ref)], p_ref, p_buf, p_sem)


def cross_second(
    meta, io, second_ref, ncross_ref, memory_ref, norms_ref, w0_ref, w1_ref, w2_ref, w3_ref,
    mixed_first_ref,
    q_ref, k_ref, v_ref, mixed_ref, p_ref, third_ref, nffn_ref, p_buf, p_sem,
):
    project_cross(io, ncross_ref, memory_ref, (w2_ref, w3_ref), q_ref, k_ref, v_ref)
    attend_docs(meta, True, None, None, [(q_ref, k_ref, v_ref, mixed_ref)], p_ref, p_buf, p_sem)
    io.send(mixed_ref)
    io.wait("late")
    out_first = jnp.concatenate([w_out(w0_ref), w_out(w1_ref)], axis=0)
    out_second = jnp.concatenate([w_out(w2_ref), w_out(w3_ref)], axis=0)

    def tile(i, carry):
        rows = rows_of(i)
        branch = dot(mixed_first_ref[rows, :], out_first) + dot(mixed_ref[rows, :], out_second)
        third = second_ref[rows, :] + branch
        third_ref[rows, :] = third
        io.send(third_ref, rows)
        nffn_ref[rows, :] = layer_norm(third, norms_ref[6:7], norms_ref[7:8]).astype(bf16)
        io.send(nffn_ref, rows)
        return carry

    lax.fori_loop(0, TILES, tile, 0)


def ffn_both(
    meta, io, third_ref, nffn_ref, cot_ref, norms_ref, u0_ref, u1_ref, u2_ref, u3_ref,
    w0_ref, w1_ref, w2_ref, w3_ref,
    placed_ref, out_ref, g3_ref, g3_low_ref, gln_ref, own_ref, other_ref, hidden_ref, before_ref,
):
    gln_ref[...] = jnp.zeros_like(gln_ref)
    in_refs = (u0_ref, u1_ref, u2_ref, u3_ref)
    w_refs = (w0_ref, w1_ref, w2_ref, w3_ref)

    def tile(i, carry):
        rows = rows_of(i)
        io.wait_rows(i)
        nffn = nffn_ref[rows, :]
        cot = cot_ref[rows, :]
        outs = []
        grads = []

        def phases(g, c, group):
            w_in = in_refs[g]
            w_out_rows = w_refs[g]
            cols = slice(256 * c, 256 * c + 256)

            def enter():
                return dot(nffn, w_in[:, cols]), dot_nt(cot, w_out_rows[cols, :])

            def bend(state):
                x, grad_hidden = state
                square = x * x
                half = 0.5 + 0.5 * jnp.tanh(x * (gelu_root + (gelu_root * gelu_cube) * square))
                value = x * half
                rise = 2.0 * gelu_root + (6.0 * gelu_root * gelu_cube) * square
                slope = half + value * (1.0 - half) * rise
                hidden = value.astype(bf16)
                grad_before = (grad_hidden * slope).astype(bf16)
                if g < 2:
                    place = slice(512 * g + 256 * c, 512 * g + 256 * c + 256)
                    hidden_ref[rows, place] = hidden
                    before_ref[rows, place] = grad_before
                group[c] = hidden, grad_before

            def leave(_):
                if c == 1:
                    outs.append(dot(lanes([group[0][0], group[1][0]]), w_out_rows[...]))

            def leave_back(_):
                if c == 1:
                    grads.append(dot_nt(lanes([group[0][1], group[1][1]]), w_in[...]))

            return enter, bend, leave, leave_back

        interleave(by_halves(4, phases))
        third = third_ref[rows, :]
        result = (third + ((outs[0] + outs[1]) + (outs[2] + outs[3]))).astype(bf16)
        out_ref[rows, :] = result
        placed_ref[rows, :] = result
        grad_normed = (grads[0] + grads[1]) + (grads[2] + grads[3])
        grad_norm, grad_gain, grad_shift = norm_backward(third, norms_ref[6:7], grad_normed)
        g3 = cot.astype(f32) + grad_norm
        g3_ref[rows, :] = g3
        g3_low_ref[rows, :] = g3.astype(bf16)
        gln_ref[0:1, :] += grad_gain
        gln_ref[1:2, :] += grad_shift
        for ref in (out_ref, placed_ref, g3_ref, g3_low_ref):
            io.send(ref, rows)
        return carry

    lax.fori_loop(0, TILES, tile, 0)
    part = dot_tn(nffn_ref[...], before_ref[...])
    own_ref[0:512, :] = part[:, 0:512].astype(bf16)
    other_ref[0:512, :] = part[:, 512:1024].astype(bf16)
    io.send(own_ref, pl.ds(0, 512))
    io.send(other_ref, pl.ds(0, 512))
    part = dot_tn(hidden_ref[...], cot_ref[...])
    own_ref[512:1024, :] = part[0:512].astype(bf16)
    other_ref[512:1024, :] = part[512:1024].astype(bf16)
    io.send(own_ref, pl.ds(512, 512))
    io.send(other_ref, pl.ds(512, 512))


def back_start(io, g_ref, mixed_ref, w_refs, dm_ref, dq_ref, dk_ref, dv_ref):
    out_rows = jnp.concatenate([w_out(w) for w in w_refs], axis=0)

    def tile(i, carry):
        rows = rows_of(i)
        io.wait_rows(i)
        dm_ref[rows, :] = dot_nt(g_ref[rows, :], out_rows).astype(bf16)
        zeros = jnp.zeros((TILE, 256), f32)
        dq_ref[rows, :] = zeros
        dk_ref[rows, :] = zeros
        dv_ref[rows, :] = zeros
        return carry

    lax.fori_loop(0, TILES, tile, 0)


def attention_back_first(
    cross, meta, io, g_ref, nq_ref, nkv_ref, rank_row_ref, limit_ref, w0_ref, w1_ref,
    q_ref, k_ref, v_ref, mixed_ref, p_ref,
    dq_ref, dk_ref, dv_ref, own_ref, other_ref,
    rank_ref, dm_ref, dqs_ref, dks_ref, dvs_ref, p_buf, p_sem,
):
    load = (p_ref, p_buf, p_sem)
    start_load(meta, cross, load)
    if not cross:
        spread_ranks(rank_row_ref, rank_ref)
    back_start(io, g_ref, mixed_ref, (w0_ref, w1_ref), dm_ref, dqs_ref, dks_ref, dvs_ref)

    io.wait("soon")
    attend_docs_back(
        meta, cross, None if cross else rank_ref, limit_ref, q_ref, k_ref, v_ref, mixed_ref,
        dm_ref, dqs_ref, dks_ref, dvs_ref, load,
    )

    dq_ref[...] = dqs_ref[...].astype(bf16)
    dk_ref[...] = dks_ref[...].astype(bf16)
    dv_ref[...] = dvs_ref[...].astype(bf16)
    for ref in (dq_ref, dk_ref, dv_ref):
        io.send(ref)
    io.wait("late")
    nq = nq_ref[...]
    nkv = nkv_ref[...]
    kv = dot_tn(nkv, lanes([dk_ref[...], dv_ref[...]]))
    for n, part in enumerate((dot_tn(nq, dq_ref[...]), kv[:, 0:256], kv[:, 256:512])):
        own_ref[:, 128 * n : 128 * n + 128] = part[:, :128].astype(bf16)
        other_ref[:, 128 * n : 128 * n + 128] = part[:, 128:].astype(bf16)
    part = dot_tn(mixed_ref[...], g_ref[...])
    for j in range(4):
        rows = slice(128 * j, 128 * j + 128)
        own_ref[rows, 384:512] = part[:128, rows].astype(bf16)
        other_ref[rows, 384:512] = part[128:, rows].astype(bf16)


def back_second_docs(
    cross, meta, io, g_ref, rank_row_ref, limit_ref, w_refs, q_ref, k_ref, v_ref, mixed_ref, p_ref,
    rank_ref, dm_ref, dqs_ref, dks_ref, dvs_ref, p_buf, p_sem,
):
    load = (p_ref, p_buf, p_sem)
    start_load(meta, cross, load)
    if not cross:
        spread_ranks(rank_row_ref, rank_ref)
    back_start(io, g_ref, mixed_ref, w_refs, dm_ref, dqs_ref, dks_ref, dvs_ref)

    io.wait("soon")
    attend_docs_back(
        meta, cross, None if cross else rank_ref, limit_ref, q_ref, k_ref, v_ref, mixed_ref,
        dm_ref, dqs_ref, dks_ref, dvs_ref, load,
    )


def stream_grads(rows, first, second, firsts, seconds):
    dq, dk, dv = first
    dq2, dk2, dv2 = (ref[rows, :].astype(bf16) for ref in second)
    w0, w1 = firsts
    w2, w3 = seconds
    grad_q = dot_nt(dq[rows, :], lanes([w_query(w0), w_query(w1)])) + dot_nt(
        dq2, lanes([w_query(w2), w_query(w3)])
    )
    kv = lanes([dk[rows, :], dv[rows, :]])
    kv2 = lanes([dk2, dv2])
    grad_kv = dot_nt(kv, lanes([w_key(w0), w_key(w1), w_value(w0), w_value(w1)])) + dot_nt(
        kv2, lanes([w_key(w2), w_key(w3), w_value(w2), w_value(w3)])
    )
    return grad_q, grad_kv


def cross_back_second(
    meta, io, g_low_ref, g_ref, second_ref, norms_ref, w0_ref, w1_ref, w2_ref, w3_ref,
    dq_ref, dk_ref, dv_ref, q_ref, k_ref, v_ref, mixed_ref, p_ref,
    g2_ref, g2_low_ref, placed_ref, gmem_ref, gln_ref,
    dm_ref, dqs_ref, dks_ref, dvs_ref, p_buf, p_sem,
):
    back_second_docs(
        True, meta, io, g_low_ref, None, None, (w2_ref, w3_ref), q_ref, k_ref, v_ref, mixed_ref, p_ref,
        None, dm_ref, dqs_ref, dks_ref, dvs_ref, p_buf, p_sem,
    )

    io.wait("late")
    gln_ref[...] = jnp.zeros_like(gln_ref)

    def tile(i, carry):
        rows = rows_of(i)
        grad_q, grad_kv = stream_grads(
            rows,
            (dq_ref, dk_ref, dv_ref),
            (dqs_ref, dks_ref, dvs_ref),
            (w0_ref, w1_ref),
            (w2_ref, w3_ref),
        )
        low_kv = grad_kv.astype(bf16)
        gmem_ref[rows, :] = low_kv
        placed_ref[rows, :] = low_kv.astype(f32)
        io.send(gmem_ref, rows)
        io.send(placed_ref, rows)
        grad_norm, grad_gain, grad_shift = norm_backward(
            second_ref[rows, :], norms_ref[4:5], grad_q
        )
        g2 = g_ref[rows, :] + grad_norm
        g2_ref[rows, :] = g2
        g2_low_ref[rows, :] = g2.astype(bf16)
        io.send(g2_ref, rows)
        io.send(g2_low_ref, rows)
        gln_ref[0:1, :] += grad_gain
        gln_ref[1:2, :] += grad_shift
        return carry

    lax.fori_loop(0, TILES, tile, 0)


def self_back_second(
    meta, io, g_low_ref, rank_row_ref, limit_ref, w2_ref, w3_ref,
    q_ref, k_ref, v_ref, mixed_ref, p_ref,
    dq_ref, dk_ref, dv_ref,
    rank_ref, dm_ref, dqs_ref, dks_ref, dvs_ref, p_buf, p_sem,
):
    back_second_docs(
        False, meta, io, g_low_ref, rank_row_ref, limit_ref, (w2_ref, w3_ref), q_ref, k_ref, v_ref,
        mixed_ref, p_ref, rank_ref, dm_ref, dqs_ref, dks_ref, dvs_ref, p_buf, p_sem,
    )
    dq_ref[...] = dqs_ref[...].astype(bf16)
    dk_ref[...] = dks_ref[...].astype(bf16)
    dv_ref[...] = dvs_ref[...].astype(bf16)


def self_back_finish(
    meta, io, g_ref, xq_ref, xc_ref, norms_ref, w0_ref, w1_ref, w2_ref, w3_ref,
    dq_ref, dk_ref, dv_ref, dq2_ref, dk2_ref, dv2_ref,
    placed_q_ref, placed_c_ref, gq_ref, gc_ref, gln_ref,
):
    gln_ref[...] = jnp.zeros_like(gln_ref)

    def tile(i, carry):
        rows = rows_of(i)
        io.wait_rows(i)
        grad_q, grad_kv = stream_grads(
            rows,
            (dq_ref, dk_ref, dv_ref),
            (dq2_ref, dk2_ref, dv2_ref),
            (w0_ref, w1_ref),
            (w2_ref, w3_ref),
        )
        grad_norm, grad_gain, grad_shift = norm_backward(
            xq_ref[rows, :].astype(f32), norms_ref[0:1], grad_q
        )
        low_q = (g_ref[rows, :] + grad_norm).astype(bf16)
        gq_ref[rows, :] = low_q
        placed_q_ref[rows, :] = low_q.astype(f32)
        io.send(gq_ref, rows)
        io.send(placed_q_ref, rows)
        gln_ref[0:1, :] += grad_gain
        gln_ref[1:2, :] += grad_shift
        grad_norm, grad_gain, grad_shift = norm_backward(
            xc_ref[rows, :].astype(f32), norms_ref[2:3], grad_kv
        )
        low_c = grad_norm.astype(bf16)
        gc_ref[rows, :] = low_c
        placed_c_ref[rows, :] = low_c.astype(f32)
        io.send(gc_ref, rows)
        io.send(placed_c_ref, rows)
        gln_ref[2:3, :] += grad_gain
        gln_ref[3:4, :] += grad_shift
        return carry

    lax.fori_loop(0, TILES, tile, 0)


def place_rows(meta, *refs):
    count = len(refs) // 3
    for n in range(count):
        refs[2 * count + n][...] = refs[n][...].astype(refs[2 * count + n].dtype)


GROUP = 8


def position(meta):
    r = meta[35]
    return lax.rem(r, 2), r // 2


def join(own, other, rows):
    return (own[rows, :].astype(f32) + other[rows, :].astype(f32)).astype(bf16)


def join_halves(meta, own, other, keep, send):
    y, _ = position(meta)
    size = keep.shape[0]
    keep[...] = join(own, other, rows_of(y, size))
    send[...] = join(own, other, rows_of(1 - y, size))


def join_chunks(meta, kept, arrived, keep, sends):
    _, z = position(meta)
    size = keep.shape[0]
    keep[...] = join(kept, arrived, rows_of(z, size))
    for s, (send, first) in enumerate(sends, 1):
        send[first : first + size, :] = join(kept, arrived, rows_of(z ^ s, size))


def add_up(kept, parts, first):
    size = kept.shape[0]
    total = kept[...].astype(f32)
    for part in parts:
        total = total + part[first : first + size, :].astype(f32)
    return total.astype(bf16)


def half_of(meta, total, parts, first, half):
    _, z = position(meta)
    size = total.shape[0]
    half[rows_of(z, size), :] = total[...]
    for s, part in enumerate(parts, 1):
        half[rows_of(z ^ s, size), :] = part[first : first + size, :]


def slot_1(meta, ffn_own, ffn_other, keep, send):
    join_halves(meta, ffn_own, ffn_other, keep, send)


def slot_2(
    meta, ffn_kept, ffn_arrived, cross_own, cross_other, ffn_keep, f1, f2, f3, keep, send
):
    join_chunks(meta, ffn_kept, ffn_arrived, ffn_keep, [(f1, 0), (f2, 0), (f3, 0)])
    join_halves(meta, cross_own, cross_other, keep, send)


def slot_3(
    meta, ffn_kept, f1, f2, f3, cross_kept, cross_arrived, self_own, self_other,
    ffn_total, cross_keep, m1, m2, m3, self_keep, self_send,
):
    join_halves(meta, self_own, self_other, self_keep, self_send)
    total = add_up(ffn_kept, (f1, f2, f3), 0)
    ffn_total[...] = total
    size = total.shape[0]
    join_chunks(meta, cross_kept, cross_arrived, cross_keep, [(m, size) for m in (m1, m2, m3)])
    for m in (m1, m2, m3):
        m[0:size, :] = total


def slot_4(
    meta, ffn_total, m1, m2, m3, cross_kept, self_kept, self_arrived,
    ffn_half, cross_total, self_keep, *sends,
):
    join_chunks(meta, self_kept, self_arrived, self_keep, [(send, 0) for send in sends])
    total = add_up(cross_kept, (m1, m2, m3), ffn_total.shape[0])
    cross_total[...] = total
    size = total.shape[0]
    for send in sends:
        send[size:, :] = total
    half_of(meta, ffn_total, (m1, m2, m3), 0, ffn_half)


def slot_5(meta, self_kept, cross_total, m1, m2, m3, gln_own, gln_other, send, cross_half):
    size = self_kept.shape[0]
    total = add_up(self_kept, (m1, m2, m3), 0)
    gln = gln_own[...] + gln_other[...]
    gln = jnp.concatenate([gln, jnp.zeros((8, D), f32)], axis=0).astype(bf16)
    for r in range(GROUP):
        send[r, 0:size, :] = total
        send[r, size : size + 16, :] = gln
    half_of(meta, cross_total, (m1, m2, m3), size, cross_half)


def unpack_attention(whole_ref, outs):
    for i in range(3):
        outs[i][...] = whole_ref[:, 128 * i : 128 * i + 128].astype(f32)
    for j in range(4):
        rows = slice(128 * j, 128 * j + 128)
        outs[3][:, rows] = whole_ref[rows, 384:512].astype(f32)


def unpack_early(meta, ffn_half, ffn_arrived, cross_half, cross_arrived, *refs):
    *outs, cross_whole, ffn_whole = refs
    y, _ = position(meta)
    cross_whole[rows_of(y, 256), :] = cross_half[...]
    cross_whole[rows_of(1 - y, 256), :] = cross_arrived[...]
    unpack_attention(cross_whole, outs[2:])
    ffn_whole[rows_of(y, 512), :] = ffn_half[...]
    ffn_whole[rows_of(1 - y, 512), :] = ffn_arrived[...]
    outs[0][...] = ffn_whole[0:512, :].astype(f32)
    outs[1][...] = ffn_whole[512:1024, :].astype(f32)


def unpack_late(meta, parts, *refs):
    *outs, gln, whole_ref = refs
    size = parts.shape[1] - 16
    total = parts[0, size : size + 16, :].astype(f32)
    for r in range(1, GROUP):
        total = total + parts[r, size : size + 16, :].astype(f32)
    gln[...] = total[0:8]
    for r in range(GROUP):
        first = size * (4 * (r % 2) + r // 2)
        whole_ref[first : first + size, :] = parts[r, 0:size, :]
    unpack_attention(whole_ref, outs)


def whole(shape):
    zeros = (0,) * len(shape)
    return pl.BlockSpec(shape, lambda d, meta: zeros)


def own_row(width):
    return pl.BlockSpec((SEQ, width), lambda d, meta: (meta[0], 0))


ANY = pl.BlockSpec(memory_space=pl.ANY)


def in_hbm(x):
    return pltpu.with_memory_space_constraint(x, pltpu.HBM)


probability_out = (pltpu.HBM((DOCS, 4, FAST_K, FAST_Q), bf16), None, ANY)
probability_scratch = [
    pltpu.VMEM((2, TOGETHER, 4, FAST_K, FAST_Q), bf16),
    pltpu.SemaphoreType.DMA((2,)),
]


class Copies:
    def __init__(self, meta):
        self.first = meta[0] * SEQ
        self.loads = {}
        self.tiles = []
        self.sends = []

    def load(self, stage, source, target, sems, own_row):
        if stage == "tiles":
            first = self.first if own_row else 0
            self.tiles.append((source, target, sems, first))
            return
        if own_row:
            source = source.at[pl.ds(pl.multiple_of(self.first, SEQ), SEQ)]
        copy = pltpu.make_async_copy(source, target, sems[0].at[sems[1], 0])
        self.loads.setdefault(stage, []).append(copy)

    def tile(self, entry, i):
        source, target, (sems, b), first = entry
        rows = pl.ds(pl.multiple_of(first + i * TILE, TILE), TILE)
        return pltpu.make_async_copy(source.at[rows], target.at[rows_of(i)], sems.at[b, i])

    def start(self):
        for copy in self.loads.get("now", []):
            copy.start()
        for i in range(TILES):
            for entry in self.tiles:
                self.tile(entry, i).start()
        for stage in ("soon", "late"):
            for copy in self.loads.get(stage, []):
                copy.start()

    def wait(self, stage):
        for copy in self.loads.pop(stage, []):
            copy.wait()

    def wait_rows(self, i):
        for entry in self.tiles:
            self.tile(entry, i).wait()

    def result(self, source, target, sem, own_row):
        self.sends.append([source, target, sem, own_row, False])

    def send(self, ref, rows=None):
        for entry in self.sends:
            source, target, sem, own_row, _ = entry
            if source is ref:
                entry[4] = True
                first = self.first if own_row else 0
                if rows is None:
                    size = source.shape[0]
                else:
                    source = source.at[rows]
                    first, size = first + rows.start, rows.size
                if rows is not None or own_row:
                    target = target.at[pl.ds(pl.multiple_of(first, size), size)]
                pltpu.make_async_copy(source, target, sem).start()

    def finish(self):
        for stage in list(self.loads):
            self.wait(stage)
        for source, _, _, _, started in self.sends:
            if not started:
                self.send(source)
        for source, target, sem, own_row, _ in self.sends:
            if own_row:
                target = target.at[pl.ds(pl.multiple_of(self.first, SEQ), SEQ)]
            pltpu.make_async_copy(source, target, sem).wait()


def out(shape, dtype, own_row=False):
    return (shape, dtype, own_row)


def call(kernel, name, operands, outs, scratch, flops, token=None):
    arrays = [operands[0][0]]
    in_specs, out_specs, out_shapes = [], [], []
    buffers = []
    loads = []
    for n, (x, how) in enumerate(operands[1:]):
        if isinstance(how, str):
            stage, _, row = how.partition("_")
            shape = ((SEQ,) + x.shape[1:]) if row else x.shape
            loads.append((n, stage, len(buffers), bool(row)))
            buffers.append(pltpu.VMEM(shape, x.dtype))
            arrays.append(in_hbm(x))
            in_specs.append(ANY)
        else:
            arrays.append(x)
            in_specs.append(how)
    results = []
    for n, (shape, dtype, how) in enumerate(outs):
        if isinstance(how, bool):
            results.append((n, len(buffers), how))
            buffers.append(pltpu.VMEM(shape, dtype))
            shape = ((2 * SEQ,) + shape[1:]) if how else shape
            out_shapes.append(pltpu.HBM(shape, dtype))
            out_specs.append(ANY)
        else:
            out_shapes.append(jax.ShapeDtypeStruct(shape, dtype) if dtype else shape)
            out_specs.append(how)
    n_in, n_out = len(in_specs), len(out_specs)
    if token is not None:
        arrays.append(token)
        in_specs.append(whole((8, 128)))
        out_specs.append(whole((8, 128)))
        out_shapes.append(jax.ShapeDtypeStruct((8, 128), f32))

    def body(meta, *refs):
        ins, refs = list(refs[:n_in]), refs[len(in_specs) - n_in + n_in :]
        results_out, refs = list(refs[:n_out]), refs[n_out:]
        if token is not None:
            token_out, refs = refs[0], refs[1:]
            token_out[...] = jnp.zeros_like(token_out)
        bufs, refs = refs[: len(buffers)], refs[len(buffers) :]
        rest = refs[: len(scratch)]
        copies = Copies(meta)
        if buffers:
            sems = refs[len(scratch)]
        for n, stage, b, row in loads:
            copies.load(stage, ins[n], bufs[b], (sems, b), row)
            ins[n] = bufs[b]
        for n, b, row in results:
            copies.result(bufs[b], results_out[n], sems.at[b, 0], row)
            results_out[n] = bufs[b]
        copies.start()
        copies.wait("now")
        if buffers:
            kernel(meta, copies, *ins, *results_out, *rest)
        else:
            kernel(meta, *ins, *results_out, *rest)
        copies.finish()

    moved = sum(x.size * x.dtype.itemsize for x in arrays[1:])
    sems = [pltpu.SemaphoreType.DMA((len(buffers), TILES))] if buffers else []
    return pl.pallas_call(
        body,
        name=name,
        grid_spec=pltpu.PrefetchScalarGridSpec(
            num_scalar_prefetch=1,
            grid=(1,),
            in_specs=in_specs,
            out_specs=out_specs,
            scratch_shapes=buffers + scratch + sems,
        ),
        out_shape=out_shapes,
        compiler_params=pltpu.CompilerParams(
            dimension_semantics=("arbitrary",), vmem_limit_bytes=50 * 1024 * 1024
        ),
        cost_estimate=pl.CostEstimate(
            flops=int(flops), bytes_accessed=int(moved), transcendentals=0
        ),
    )(*arrays)


def simple(kernel, name, meta, operands, outs, scratch=()):
    return pl.pallas_call(
        kernel,
        name=name,
        grid_spec=pltpu.PrefetchScalarGridSpec(
            num_scalar_prefetch=1,
            grid=(1,),
            in_specs=[whole(x.shape) for x in operands],
            out_specs=[whole(shape) for shape, _ in outs],
            scratch_shapes=scratch,
        ),
        out_shape=[jax.ShapeDtypeStruct(shape, dtype) for shape, dtype in outs],
        compiler_params=pltpu.CompilerParams(vmem_limit_bytes=16 * 1024 * 1024),
    )(meta, *operands)


def full(x):
    return (x, whole(x.shape))


def shards(
    query_stream,
    content_stream,
    memory,
    segment_ids,
    source_segments,
    context_rank,
    context_limit,
    padding,
    ln_query_gain,
    ln_query_bias,
    ln_content_gain,
    ln_content_bias,
    self_query,
    self_key,
    self_value,
    self_out,
    ln_cross_gain,
    ln_cross_bias,
    cross_query,
    cross_key,
    cross_value,
    cross_out,
    ln_ffn_gain,
    ln_ffn_bias,
    ffn_in,
    ffn_out,
    cotangent,
):
    core = lax.axis_index("heads") % 2

    def to_core(x):
        return lax.ppermute(x, "heads", [(h, h ^ 1) for h in range(4)])

    hold = lambda *xs: lax.optimization_barrier(xs)

    def to_chip(x):
        return lax.ppermute(x, "heads", [(h, h ^ 2) for h in range(4)])

    row = pl.BlockSpec((1, 8, 128), lambda d, core: (core[0], 0, 0))

    def token_row(x):
        return (in_hbm(x.reshape(2, 8, 128)), row)

    def fixed(x):
        zeros = (0,) * x.ndim
        return (in_hbm(x), pl.BlockSpec(x.shape, lambda d, core: zeros))

    prepared = [
        ((36,), jnp.int32, pl.BlockSpec(memory_space=pltpu.SMEM)),
        ((1, SEQ), f32, whole((1, SEQ))),
        ((1, SEQ), f32, whole((1, SEQ))),
        ((8, D), f32, whole((8, D))),
        ((D, D), bf16, whole((D, D))),
        ((D, D), bf16, whole((D, D))),
    ]
    gains = (
        ln_query_gain,
        ln_query_bias,
        ln_content_gain,
        ln_content_bias,
        ln_cross_gain,
        ln_cross_bias,
        ln_ffn_gain,
        ln_ffn_bias,
    )
    weights = (self_query, self_key, self_value, self_out)
    weights += (cross_query, cross_key, cross_value, cross_out)
    tokens = (segment_ids, source_segments, context_rank, context_limit, padding)
    meta, rank, limit, norms, ws0, wc0 = call(
        prepare,
        "prepare",
        [(jnp.stack([core, lax.axis_index("rows") % GROUP]).astype(jnp.int32), None)]
        + [token_row(x) for x in tokens]
        + [fixed(x.reshape(1, D)) for x in gains]
        + [fixed(x) for x in weights],
        prepared,
        [],
        0,
    )

    ws1 = to_core(ws0)
    ws2 = to_chip(ws0)
    wc1 = to_core(wc0)
    u0, v0 = ffn_in, ffn_out
    meta_in = (meta, None)

    heads_out = [out((SEQ, 256), bf16)] * 4

    def stream_out(dtype, own_row=False):
        return out((SEQ, D), dtype, own_row)

    def now(*xs):
        return [(x, "now") for x in xs]

    def soon(*xs):
        return [(x, "soon") for x in xs]

    def late(*xs):
        return [(x, "late") for x in xs]

    def small(*xs):
        return [(x, whole(x.shape)) for x in xs]

    limits = pltpu.VMEM((SEQ, 128), f32)
    pair_flops = 2 * SEQ * D * 768 + 2 * 2 * 4 * DOCS * FAST_Q * FAST_K * 256

    nq, nc, *first, token = call(
        self_first,
        "self_first",
        [meta_in, (query_stream, "tiles_row"), (content_stream, "tiles_row")]
        + small(rank, limit, norms)
        + now(ws0, ws1),
        [stream_out(bf16), stream_out(bf16)] + heads_out + [probability_out],
        [limits] + probability_scratch,
        pair_flops,
        jnp.zeros((8, 128), f32),
    )
    ws2, wc0, token = hold(ws2, wc0, token)
    ws3 = to_core(ws2)
    wc2 = to_chip(wc0)
    *second_heads, second, ncross, token = call(
        self_second,
        "self_second",
        [meta_in, (query_stream, "late_row")]
        + [(nq, "tiles"), (nc, "tiles")]
        + small(rank, limit, norms)
        + late(ws0, ws1)
        + now(ws2, ws3)
        + late(first[3]),
        heads_out + [probability_out, stream_out(f32), stream_out(bf16)],
        [limits] + probability_scratch,
        pair_flops + 2 * SEQ * D * D,
        token,
    )
    wc2, u0, v0, token = hold(wc2, u0, v0, token)
    wc3 = to_core(wc2)
    u2 = to_chip(u0)
    u1 = to_core(u0)
    *cross_heads, token = call(
        cross_first,
        "cross_first",
        [meta_in, (ncross, "tiles"), (memory, "tiles_row")] + now(wc0, wc1),
        heads_out + [probability_out],
        probability_scratch,
        pair_flops,
        token,
    )
    wc3, u2, v0, token = hold(wc3, u2, v0, token)
    u3 = to_core(u2)
    v2 = to_chip(v0)
    v1 = to_core(v0)
    *cross_heads_second, third, nffn, token = call(
        cross_second,
        "cross_second",
        [meta_in]
        + late(second)
        + [(ncross, "tiles"), (memory, "tiles_row")]
        + small(norms)
        + late(wc0, wc1)
        + now(wc2, wc3)
        + late(cross_heads[3]),
        heads_out + [probability_out, stream_out(f32), stream_out(bf16)],
        probability_scratch,
        pair_flops + 2 * SEQ * D * D,
        token,
    )
    u3, v2, token = hold(u3, v2, token)
    v3 = to_core(v2)
    grads_ln = ((8, D), f32, whole((8, D)))
    placed_output, output, g3, g3_low, gln_ffn, ffn_own, ffn_other, token = call(
        ffn_both,
        "ffn_both",
        [meta_in]
        + [(third, "tiles"), (nffn, "tiles"), (cotangent, "tiles_row")]
        + small(norms)
        + now(u0, u1, u2, u3, v0, v1, v2, v3),
        [
            stream_out(bf16, True),
            stream_out(bf16),
            stream_out(f32),
            stream_out(bf16),
            grads_ln,
            out((1024, D), bf16),
            out((1024, D), bf16),
        ],
        [pltpu.VMEM((SEQ, 1024), bf16), pltpu.VMEM((SEQ, 1024), bf16)],
        12 * SEQ * D * 2048,
        token,
    )

    row_count = lax.axis_size("rows")
    assert row_count % GROUP == 0

    def along_rows(x, s):
        return lax.ppermute(x, "rows", [(r, r ^ s) for r in range(row_count)])

    def to_y(x):
        return along_rows(x, 1)

    def to_z(sends):
        return [along_rows(x, 2 * s) for s, x in enumerate(sends, 1)]

    def rows_out(*sizes):
        return [((n, D), bf16) for n in sizes]

    ffn_other = to_core(ffn_other)

    back_scratch = [pltpu.VMEM((SEQ, 256), bf16)] + [pltpu.VMEM((SEQ, 256), f32)] * 3
    back_scratch += probability_scratch
    pair_out = out((SEQ, 256), bf16)
    packed_outs = [out((D, D), bf16), out((D, D), bf16)]
    back_flops = 2 * SEQ * D * 256 + 4 * 2 * 4 * DOCS * FAST_Q * FAST_K * 256

    def head_inputs(natural, p):
        return soon(*natural) + [(in_hbm(p), ANY)]

    *cross_grads, cross_own, cross_other, token = call(
        functools.partial(attention_back_first, True),
        "cross_back_first",
        [meta_in]
        + [(g3_low, "tiles")]
        + late(ncross)
        + [(memory, "late_row")]
        + small(rank, limit)
        + now(wc0, wc1)
        + head_inputs(cross_heads[0:4], cross_heads[4]),
        [pair_out] * 3 + packed_outs,
        [limits] + back_scratch,
        back_flops + 2 * SEQ * D * 1024,
        token,
    )
    ffn_other, token = hold(ffn_other, token)
    ffn_keep, ffn_send = simple(slot_1, "slot_1", meta, [ffn_own, ffn_other], rows_out(512, 512))
    ffn_send, token = hold(ffn_send, token)
    ffn_arrived = to_y(ffn_send)
    cross_other = to_core(cross_other)
    g2, g2_low, placed_mem, grad_mem, gln_cross, token = call(
        cross_back_second,
        "cross_back_second",
        [meta_in]
        + [(g3_low, "tiles")]
        + late(g3, second)
        + small(norms)
        + late(wc0, wc1)
        + now(wc2, wc3)
        + late(*cross_grads)
        + head_inputs(cross_heads_second[0:4], cross_heads_second[4]),
        [stream_out(f32), stream_out(bf16), stream_out(f32, True), stream_out(bf16), grads_ln],
        back_scratch,
        back_flops + 2 * SEQ * D * 1536,
        token,
    )
    ffn_arrived, cross_other, token = hold(ffn_arrived, cross_other, token)
    ffn_keep, *sends, cross_keep, cross_send = simple(
        slot_2,
        "slot_2",
        meta,
        [ffn_keep, ffn_arrived, cross_own, cross_other],
        rows_out(128, 128, 128, 128, 256, 256),
    )
    ffn_keep, cross_send, token = hold(ffn_keep, cross_send, token)
    ffn_parts = to_z(sends)
    cross_arrived = to_y(cross_send)

    *self_grads, self_own, self_other, token = call(
        functools.partial(attention_back_first, False),
        "self_back_first",
        [meta_in]
        + [(g2_low, "tiles")]
        + late(nq, nc)
        + small(rank, limit)
        + now(ws0, ws1)
        + head_inputs(first[0:4], first[4]),
        [pair_out] * 3 + packed_outs,
        [limits] + back_scratch,
        back_flops + 2 * SEQ * D * 1024,
        token,
    )
    *ffn_parts, cross_arrived, self_other, token = hold(
        *ffn_parts, cross_arrived, self_other, token
    )
    self_other = to_core(self_other)
    ffn_total, cross_keep, *sends, self_keep, self_send = simple(
        slot_3,
        "slot_3",
        meta,
        [ffn_keep, *ffn_parts, cross_keep, cross_arrived, self_own, self_other],
        rows_out(128, 64, 192, 192, 192, 256, 256),
    )
    ffn_total, self_send, token = hold(ffn_total, self_send, token)
    self_arrived = to_y(self_send)
    messages = to_z(sends)
    *self_grads_second, token = call(
        self_back_second,
        "self_back_second",
        [meta_in, (g2_low, "tiles")]
        + small(rank, limit)
        + now(ws2, ws3)
        + head_inputs(second_heads[0:4], second_heads[4]),
        [pair_out] * 3,
        [limits] + back_scratch,
        back_flops,
        token,
    )
    *messages, self_arrived, token = hold(*messages, self_arrived, token)
    ffn_half, cross_total, self_keep, *sends = simple(
        slot_4,
        "slot_4",
        meta,
        [ffn_total, *messages, cross_keep, self_keep, self_arrived],
        rows_out(512, 64, 64, 128, 128, 128),
    )
    cross_total, ffn_half, token = hold(cross_total, ffn_half, token)
    messages = to_z(sends)
    ffn_arrived = to_y(ffn_half)
    placed_q, placed_c, gq, gc, gln_self, token = call(
        self_back_finish,
        "self_back_finish",
        [meta_in, (g2, "tiles"), (query_stream, "tiles_row"), (content_stream, "tiles_row")]
        + small(norms)
        + now(ws0, ws1, ws2, ws3)
        + [(x, "tiles") for x in self_grads + self_grads_second],
        [stream_out(f32, True), stream_out(f32, True), stream_out(bf16), stream_out(bf16), grads_ln],
        [],
        2 * SEQ * D * 1536,
        token,
    )
    gln = jnp.concatenate([gln_self[0:4], gln_cross[0:2], gln_ffn[0:2]], axis=0)
    *messages, ffn_arrived, gln = hold(*messages, ffn_arrived, gln)
    last_send, cross_half = simple(
        slot_5,
        "slot_5",
        meta,
        [self_keep, cross_total, *messages, gln, to_core(gln)],
        [((GROUP, 80, D), bf16), ((256, D), bf16)],
    )
    output, grad_mem, last_send = hold(output, grad_mem, last_send)
    groups = None
    if row_count > GROUP:
        groups = [list(range(r, r + GROUP)) for r in range(0, row_count, GROUP)]
    last_parts = lax.all_to_all(last_send, "rows", 0, 0, axis_index_groups=groups)
    cross_arrived = to_y(cross_half)

    def over_groups(totals):
        if row_count == GROUP:
            return totals
        groups = [list(range(r, row_count, GROUP)) for r in range(GROUP)]
        return lax.psum(totals, "rows", axis_index_groups=groups)

    def both_rows(placed_own, arrays, name):
        count = len(arrays)
        size = SEQ // 2
        one = pl.BlockSpec((size, D), lambda i, meta: (i, 0))
        block = pl.BlockSpec((size, D), lambda i, meta: (2 * (1 - meta[0]) + i, 0))
        return pl.pallas_call(
            place_rows,
            name=name,
            grid_spec=pltpu.PrefetchScalarGridSpec(
                num_scalar_prefetch=1,
                grid=(2,),
                in_specs=[one] * count + [pl.BlockSpec(memory_space=pl.ANY)] * count,
                out_specs=[block] * count,
            ),
            out_shape=[jax.ShapeDtypeStruct(x.shape, x.dtype) for x in placed_own],
            input_output_aliases={1 + count + n: n for n in range(count)},
        )(meta, *[to_core(x) for x in arrays], *placed_own)

    out_both, grad_mem_both = both_rows([placed_output, placed_mem], [output, grad_mem], "place_early")
    gq_both, gc_both = both_rows([placed_q, placed_c], [gq, gc], "place_late")

    cross_arrived, out_both, gq_both = hold(cross_arrived, out_both, gq_both)
    attention_outs = [((512, 128), f32)] * 3 + [((128, 512), f32)]
    grad_ffn_in, grad_ffn_out, *grad_cross_parts = simple(
        unpack_early,
        "unpack_early",
        meta,
        [ffn_half, ffn_arrived, cross_half, cross_arrived],
        [((D, D), f32)] * 2 + attention_outs,
        [pltpu.VMEM((D, D), bf16), pltpu.VMEM((2 * D, D), bf16)],
    )
    *grad_self_parts, gln = simple(
        unpack_late,
        "unpack_late",
        meta,
        [last_parts],
        attention_outs + [((8, D), f32)],
        [pltpu.VMEM((D, D), bf16)],
    )
    grad_ffn_in, grad_ffn_out, grad_cross_parts, grad_self_parts, gln = over_groups(
        (grad_ffn_in, grad_ffn_out, grad_cross_parts, grad_self_parts, gln)
    )
    return (
        out_both,
        gq_both,
        gc_both,
        grad_mem_both,
        gln[0],
        gln[1],
        gln[2],
        gln[3],
        *grad_self_parts,
        gln[4],
        gln[5],
        *grad_cross_parts,
        gln[6],
        gln[7],
        grad_ffn_in,
        grad_ffn_out,
    )


def solution(mesh):
    assert mesh.shape["heads"] == 4
    row_spec = P("rows", None)
    flat = P("rows")
    by_column = P(None, "heads")
    by_row = P("heads", None)
    attention = (by_column, by_column, by_column, by_row)
    in_specs = (
        (row_spec,) * 3
        + (flat,) * 5
        + (P(),) * 4
        + attention
        + (P(),) * 2
        + attention
        + (P(),) * 2
        + (by_column, by_row, row_spec)
    )
    out_specs = (
        (row_spec,) * 4
        + (P(),) * 4
        + attention
        + (P(),) * 2
        + attention
        + (P(),) * 2
        + (by_column, by_row)
    )
    return jax.shard_map(shards, mesh=mesh, in_specs=in_specs, out_specs=out_specs, check_vma=False)
```

```python
import functools

import jax
import jax.numpy as jnp
from jax import lax
from jax.experimental import pallas as pl
from jax.experimental.pallas import tpu as pltpu
from jax.sharding import PartitionSpec as P

HEAD_DIM = 64
SEQ = 1024
DOCS = 8
D = 512
TILE = 256
TILES = SEQ // TILE
FAST_Q = 256
FAST_K = 208
LONG_Q = 128
LONG_K = 640

norm_eps = 1e-05
masked_score = -1e30
hidden_rank = 1e6
gelu_root = 0.7978845608028654
gelu_cube = 0.044715

f32 = jnp.float32
bf16 = jnp.bfloat16


def dot(a, b):
    return lax.dot_general(a, b, (((1,), (0,)), ((), ())), preferred_element_type=f32)


def dot_nt(a, b):
    return lax.dot_general(a, b, (((1,), (1,)), ((), ())), preferred_element_type=f32)


def dot_tn(a, b):
    return lax.dot_general(a, b, (((0,), (0,)), ((), ())), preferred_element_type=f32)


def lanes(parts):
    return jnp.concatenate(parts, axis=1)


NORM_ROWS = 32


def layer_norm(values, gain, shift):
    def piece(part):
        part = part.astype(f32)
        centre = part - jnp.mean(part, axis=-1, keepdims=True)
        spread = jnp.mean(centre * centre, axis=-1, keepdims=True)
        return (centre * lax.rsqrt(spread + norm_eps) * gain + shift).astype(bf16)

    return by_pieces(piece, NORM_ROWS, 0, values)


def eight_rows(values):
    return sum(values[8 * i : 8 * i + 8] for i in range(1, values.shape[0] // 8)) + values[0:8]


def norm_backward(values, gain, grad, sums_ref, first):
    sums = []

    def piece(part, grad_part):
        part = part.astype(f32)
        centre = part - jnp.mean(part, axis=-1, keepdims=True)
        spread = jnp.mean(centre * centre, axis=-1, keepdims=True)
        scale = lax.rsqrt(spread + norm_eps)
        xhat = centre * scale
        eg = grad_part * gain
        mean_eg = jnp.mean(eg, axis=-1, keepdims=True)
        mean_egx = jnp.mean(eg * xhat, axis=-1, keepdims=True)
        sums.append((eight_rows(grad_part * xhat), eight_rows(grad_part)))
        return scale * (eg - mean_eg - xhat * mean_egx)

    result = by_pieces(piece, NORM_ROWS, 0, values, grad)
    for n, parts in enumerate(zip(*sums)):
        sums_ref[first + 8 * n : first + 8 * n + 8, :] += sum(parts[1:], parts[0])
    return result


def add_sums(sums_ref, gln_ref, count):
    gln_ref[...] = jnp.zeros_like(gln_ref)
    for n in range(count):
        gln_ref[n : n + 1, :] = jnp.sum(sums_ref[8 * n : 8 * n + 8, :], axis=0, keepdims=True)


def by_pieces(work, size, axis, *arrays):
    count = arrays[0].shape[axis] // size
    pieces = []
    for i in range(count):
        cut = (slice(size * i, size * i + size),)
        cut = cut if axis == 0 else (slice(None),) + cut
        pieces.append(work(*[x[cut] for x in arrays]))
    if not isinstance(pieces[0], tuple):
        return jnp.concatenate(pieces, axis=axis)
    return tuple(jnp.concatenate(parts, axis=axis) for parts in zip(*pieces))


def rows_of(i, size=TILE):
    return pl.ds(pl.multiple_of(i * size, size), size)


def w_query(ref):
    return ref[:, 0:128]


def w_key(ref):
    return ref[:, 128:256]


def w_value(ref):
    return ref[:, 256:384]


def w_out(ref):
    return lanes([ref[128 * j : 128 * j + 128, 384:512] for j in range(4)])


def half_masks():
    place = lax.broadcasted_iota(jnp.int32, (1, 128), 1)
    low = jnp.where(place < HEAD_DIM, 1.0, 0.0).astype(f32)
    return (low.astype(bf16), (1.0 - low).astype(bf16))


def doc_bounds(meta, d, source):
    base = 17 if source else 1
    return meta[base + d], meta[base + 8 + d]


def window_of(first, limit):
    return pl.multiple_of(jnp.minimum((first // 16) * 16, limit), 16)


def key_bias(ks, ke, k0, width):
    place = k0 + lax.broadcasted_iota(jnp.int32, (width, 128), 0)
    return jnp.where((place >= ks) & (place < ke), 0.0, masked_score)


def make_bias(rank_ref, limit_ref, ks, ke, q0, k0, span, width):
    if rank_ref is None:
        return lanes([key_bias(ks, ke, k0, width)] * (span // 128))
    place = k0 + lax.broadcasted_iota(jnp.int32, (width, 128), 0)
    ranks = rank_ref[pl.ds(k0, width), :]
    ranks = jnp.where((place < ks + 2) & (ranks < hidden_rank), -1.0, ranks)
    ranks = jnp.where((place >= ks) & (place < ke), ranks, hidden_rank)
    limits = jnp.broadcast_to(limit_ref[...], (8, SEQ))
    limits = pltpu.roll(limits, lax.rem(SEQ - q0, SEQ), 1)[0:1, 0:span]
    row = k0 + lax.broadcasted_iota(jnp.int32, (width, span), 0)
    column = q0 + lax.broadcasted_iota(jnp.int32, (width, span), 1)
    seen = (lanes([ranks] * (span // 128)) < limits) & (row != column)
    return jnp.where(seen, 0.0, masked_score)


TOGETHER = 4
STEPS = DOCS // TOGETHER


LAG = 2


def interleave(items):
    items = [list(phases) for phases in items]
    depth = max(len(phases) for phases in items)
    results = [None] * len(items)
    for tick in range(len(items) + LAG * (depth - 1)):
        for phase in range(depth):
            n = tick - LAG * phase
            if 0 <= n < len(items) and phase < len(items[n]):
                run = items[n][phase]
                results[n] = run() if phase == 0 else run(results[n])
    return results


def by_halves(pairs, phases):
    shared = [{} for _ in range(pairs)]
    return [phases(n, a, shared[n]) for n in range(pairs) for a in range(2)]


def is_fast(meta, cross):
    return meta[34 if cross else 33] == 1


def both_heads(x, masks):
    return jnp.concatenate([x * masks[0], x * masks[1]], axis=0)


def pair_scores(queries, keys, masks):
    return dot_nt(both_heads(keys, masks), queries)


def pair_probabilities(scores, bias):
    width = bias.shape[0]

    def piece(part, bias_part):
        part = part + bias_part
        part = jnp.exp(part - jnp.max(part, axis=0, keepdims=True))
        return (part * (1.0 / jnp.sum(part, axis=0, keepdims=True))).astype(bf16)

    return [
        by_pieces(piece, 128, 1, scores[width * a : width * a + width], bias) for a in range(2)
    ]


def pair_product(rows, parts, scale=1.0):
    across = jnp.transpose(rows)
    halves = [dot(across[64 * a : 64 * a + 64], part) for a, part in enumerate(parts)]
    return jnp.transpose((jnp.concatenate(halves, axis=0) * scale).astype(bf16))


def for_docs(meta, cross, run, before, after):
    @pl.when(is_fast(meta, cross))
    def _():
        def step(i, carry):
            slot = lax.rem(i, 2)
            before(i, slot)
            items = []
            for place in range(TOGETHER):
                d = TOGETHER * i + place
                ts, te = doc_bounds(meta, d, False)
                ks, ke = doc_bounds(meta, d, cross)
                q0 = window_of(ts, SEQ - FAST_Q)
                k0 = window_of(ks, SEQ - FAST_K)
                items += run(d, slot, place, q0, k0, FAST_Q, FAST_K, ts, te, ks, ke, True)
            interleave(items)
            after(i, slot)
            return carry

        lax.fori_loop(0, STEPS, step, 0)

    @pl.when(jnp.logical_not(is_fast(meta, cross)))
    def _():
        def doc(d, carry):
            ts, te = doc_bounds(meta, d, False)
            ks, ke = doc_bounds(meta, d, cross)
            base = (ts // 16) * 16
            k0 = window_of(ks, SEQ - LONG_K)

            def chunk(i, carry):
                lower = base + i * LONG_Q
                q0 = pl.multiple_of(jnp.minimum(lower, SEQ - LONG_Q), 16)
                low = jnp.maximum(ts, lower)
                high = jnp.minimum(te, lower + LONG_Q)
                interleave(run(d, None, None, q0, k0, LONG_Q, LONG_K, low, high, ks, ke, False))
                return carry

            return lax.fori_loop(0, (te - base + LONG_Q - 1) // LONG_Q, chunk, carry)

        lax.fori_loop(0, DOCS, doc, 0)


def attend_docs(meta, cross, rank_ref, limit_ref, halves, p_ref, p_buf, p_sem):
    pairs = 2 * len(halves)
    masks = half_masks()

    def save(i, slot):
        return pltpu.make_async_copy(p_buf.at[slot], p_ref.at[pl.ds(TOGETHER * i, TOGETHER)], p_sem.at[slot])

    def before(i, slot):
        @pl.when(i >= 2)
        def _():
            save(i - 2, slot).wait()

    def after(i, slot):
        save(i, slot).start()

    def run(d, slot, place, q0, k0, span, width, low, high, ks, ke, fast):
        bias = make_bias(rank_ref, limit_ref, ks, ke, q0, k0, span, width)
        row = q0 + lax.broadcasted_iota(jnp.int32, (span, 128), 0)
        inside = (row >= low) & (row < high)

        def phases(n):
            q_ref, k_ref, v_ref, mixed_ref = halves[n // 2]
            cols = slice(128 * (n % 2), 128 * (n % 2) + 128)

            def score():
                return pair_scores(q_ref[pl.ds(q0, span), cols], k_ref[pl.ds(k0, width), cols], masks)

            def weigh(scores):
                parts = pair_probabilities(scores, bias)
                if fast:
                    for a in range(2):
                        p_buf[slot, place, 2 * n + a] = parts[a]
                return parts

            def mix(parts):
                mixed = pair_product(v_ref[pl.ds(k0, width), cols], parts).astype(f32)
                old = mixed_ref[pl.ds(q0, span), cols].astype(f32)
                mixed_ref[pl.ds(q0, span), cols] = jnp.where(inside, mixed, old).astype(bf16)

            return score, weigh, mix

        return [phases(n) for n in range(pairs)]

    for_docs(meta, cross, run, before, after)

    @pl.when(is_fast(meta, cross))
    def _():
        for i in range(STEPS - 2, STEPS):
            save(i, i % 2).wait()


def load_step(load, i, slot):
    p_ref, p_buf, p_sem = load
    return pltpu.make_async_copy(p_ref.at[pl.ds(TOGETHER * i, TOGETHER)], p_buf.at[slot], p_sem.at[slot])


def start_load(meta, cross, load):
    @pl.when(is_fast(meta, cross))
    def _():
        load_step(load, 0, 0).start()


def attend_docs_back(
    meta, cross, rank_ref, limit_ref, q_ref, k_ref, v_ref, mixed_ref, dm_ref,
    dq_ref, dk_ref, dv_ref, load,
):
    pairs = q_ref.shape[1] // 128
    masks = half_masks()
    p_buf = load[1]

    def before(i, slot):
        @pl.when(i + 1 < STEPS)
        def _():
            load_step(load, i + 1, 1 - slot).start()

        load_step(load, i, slot).wait()

    def after(i, slot):
        pass

    def run(d, slot, place, q0, k0, span, width, low, high, ks, ke, fast):
        row = q0 + lax.broadcasted_iota(jnp.int32, (span, 128), 0)
        inside = jnp.where((row >= low) & (row < high), 1.0, 0.0).astype(bf16)
        ones = jnp.ones((width, 128), bf16)
        if not fast:
            bias = make_bias(rank_ref, limit_ref, ks, ke, q0, k0, span, width)

        def phases(n):
            cols = slice(128 * n, 128 * n + 128)

            def differ():
                values = v_ref[pl.ds(k0, width), cols]
                mixed = mixed_ref[pl.ds(q0, span), cols]
                grad = dm_ref[pl.ds(q0, span), cols] * inside
                left = lanes([grad, -(grad * mixed)])
                right = both_heads(lanes([values, ones]), [lanes([m, m]) for m in masks])
                return grad, dot_nt(right, left)

            def slope(state):
                grad, delta = state
                if fast:
                    parts = [p_buf[slot, place, 2 * n + a] for a in range(2)]
                else:
                    queries = q_ref[pl.ds(q0, span), cols]
                    keys = k_ref[pl.ds(k0, width), cols]
                    parts = pair_probabilities(pair_scores(queries, keys, masks), bias)
                slopes = [
                    by_pieces(
                        lambda part, change: part * change.astype(bf16),
                        16,
                        0,
                        parts[a],
                        delta[width * a : width * a + width],
                    )
                    for a in range(2)
                ]
                return grad, parts, slopes

            def spread(state):
                grad, parts, slopes = state
                queries = q_ref[pl.ds(q0, span), cols]
                dk = dv = None
                for a in range(2):
                    dk_a = dot(slopes[a], queries * masks[a])
                    dv_a = dot(parts[a], grad * masks[a])
                    dk = dk_a if dk is None else dk + dk_a
                    dv = dv_a if dv is None else dv + dv_a
                dq = pair_product(k_ref[pl.ds(k0, width), cols], slopes, HEAD_DIM**-0.5)
                dq_ref[pl.ds(q0, span), cols] += dq.astype(f32)
                dk_ref[pl.ds(k0, width), cols] += dk
                dv_ref[pl.ds(k0, width), cols] += dv

            return differ, slope, spread

        return [phases(n) for n in range(pairs)]

    for_docs(meta, cross, run, before, after)


def spread_ranks(rank_row_ref, rank_ref):
    rank_ref[...] = jnp.transpose(jnp.broadcast_to(rank_row_ref[...], (128, SEQ)))


def prepare(
    core, seg_ref, src_ref, rank_ref, limit_ref, pad_ref,
    n0, n1, n2, n3, n4, n5, n6, n7, sq, sk, sv, so, cq, ck, cv, co,
    meta_ref, ranks_ref, limits_ref, norms_ref, ws_ref, wc_ref,
):
    meta_ref[0] = core[0]
    meta_ref[35] = core[1]
    for base, ref in ((1, seg_ref), (17, src_ref)):
        ids = ref[0]
        meta_ref[base] = 0
        meta_ref[base + 15] = SEQ
        for d in range(1, DOCS):
            cut = jnp.sum(jnp.where(ids < d, 1.0, 0.0)).astype(jnp.int32)
            meta_ref[base + d] = cut
            meta_ref[base + 7 + d] = cut
    for place, base in ((33, 1), (34, 17)):
        fast = jnp.int32(1)
        for d in range(DOCS):
            q0 = window_of(meta_ref[1 + d], SEQ - FAST_Q)
            k0 = window_of(meta_ref[base + d], SEQ - FAST_K)
            fits = (meta_ref[9 + d] - q0 <= FAST_Q) & (meta_ref[base + 8 + d] - k0 <= FAST_K)
            fast = fast & fits.astype(jnp.int32)
        meta_ref[place] = fast
    ranks = jnp.where(pad_ref[0] != 0, hidden_rank, rank_ref[0].astype(f32))
    limits = limit_ref[0].astype(f32)
    for i in range(8):
        ranks_ref[0:1, 128 * i : 128 * i + 128] = ranks[i : i + 1]
        limits_ref[0:1, 128 * i : 128 * i + 128] = limits[i : i + 1]
    for i, ref in enumerate((n0, n1, n2, n3, n4, n5, n6, n7)):
        norms_ref[i : i + 1, :] = ref[...]
    for to, parts, out in ((ws_ref, (sq, sk, sv), so), (wc_ref, (cq, ck, cv), co)):
        for i, part in enumerate(parts):
            to[:, 128 * i : 128 * i + 128] = part[...]
        for j in range(4):
            to[128 * j : 128 * j + 128, 384:512] = out[:, 128 * j : 128 * j + 128]


def self_first(
    meta, io, xq_ref, xc_ref, rank_row_ref, limit_ref, norms_ref, w0_ref, w1_ref,
    nq_ref, nc_ref, q_ref, k_ref, v_ref, mixed_ref, p_ref, rank_ref, p_buf, p_sem,
):

    spread_ranks(rank_row_ref, rank_ref)
    wq = lanes([w_query(w0_ref), w_query(w1_ref)])
    wkv = lanes([w_key(w0_ref), w_key(w1_ref), w_value(w0_ref), w_value(w1_ref)])

    def tile(i, carry):
        rows = rows_of(i)
        io.wait_rows(i)
        nq = layer_norm(xq_ref[rows, :], norms_ref[0:1], norms_ref[1:2])
        nc = layer_norm(xc_ref[rows, :], norms_ref[2:3], norms_ref[3:4])
        nq_ref[rows, :] = nq
        nc_ref[rows, :] = nc
        q_ref[rows, :] = (dot(nq, wq) * (HEAD_DIM**-0.5)).astype(bf16)
        kv = dot(nc, wkv).astype(bf16)
        k_ref[rows, :] = kv[:, :256]
        v_ref[rows, :] = kv[:, 256:]
        return carry

    lax.fori_loop(0, TILES, tile, 0)

    for ref in (nq_ref, nc_ref, q_ref, k_ref, v_ref):
        io.send(ref)
    attend_docs(meta, False, rank_ref, limit_ref, [(q_ref, k_ref, v_ref, mixed_ref)], p_ref, p_buf, p_sem)


def self_second(
    meta, io, xq_ref, nq_ref, nc_ref, rank_row_ref, limit_ref, norms_ref, w0_ref, w1_ref, w2_ref, w3_ref,
    mixed_first_ref,
    q_ref, k_ref, v_ref, mixed_ref, p_ref, second_ref, ncross_ref, rank_ref, p_buf, p_sem,
):

    spread_ranks(rank_row_ref, rank_ref)
    wq = lanes([w_query(w2_ref), w_query(w3_ref)])
    wkv = lanes([w_key(w2_ref), w_key(w3_ref), w_value(w2_ref), w_value(w3_ref)])

    def tile(i, carry):
        rows = rows_of(i)
        io.wait_rows(i)
        q_ref[rows, :] = (dot(nq_ref[rows, :], wq) * (HEAD_DIM**-0.5)).astype(bf16)
        kv = dot(nc_ref[rows, :], wkv).astype(bf16)
        k_ref[rows, :] = kv[:, :256]
        v_ref[rows, :] = kv[:, 256:]
        return carry

    lax.fori_loop(0, TILES, tile, 0)

    for ref in (q_ref, k_ref, v_ref):
        io.send(ref)
    attend_docs(meta, False, rank_ref, limit_ref, [(q_ref, k_ref, v_ref, mixed_ref)], p_ref, p_buf, p_sem)

    io.send(mixed_ref)
    io.wait("late")
    out_first = jnp.concatenate([w_out(w0_ref), w_out(w1_ref)], axis=0)
    out_second = jnp.concatenate([w_out(w2_ref), w_out(w3_ref)], axis=0)

    def tile(i, carry):
        rows = rows_of(i)
        branch = dot(mixed_first_ref[rows, :], out_first) + dot(mixed_ref[rows, :], out_second)
        second = xq_ref[rows, :].astype(f32) + branch
        second_ref[rows, :] = second
        io.send(second_ref, rows)
        ncross_ref[rows, :] = layer_norm(second, norms_ref[4:5], norms_ref[5:6])
        io.send(ncross_ref, rows)
        return carry

    lax.fori_loop(0, TILES, tile, 0)


def project_cross(io, ncross_ref, memory_ref, weights, q_ref, k_ref, v_ref):
    wq = lanes([w_query(w) for w in weights])
    wkv = lanes([w_key(w) for w in weights] + [w_value(w) for w in weights])

    def tile(i, carry):
        rows = rows_of(i)
        io.wait_rows(i)
        q_ref[rows, :] = (dot(ncross_ref[rows, :], wq) * (HEAD_DIM**-0.5)).astype(bf16)
        kv = dot(memory_ref[rows, :], wkv).astype(bf16)
        k_ref[rows, :] = kv[:, :256]
        v_ref[rows, :] = kv[:, 256:]
        return carry

    lax.fori_loop(0, TILES, tile, 0)
    for ref in (q_ref, k_ref, v_ref):
        io.send(ref)


def cross_first(
    meta, io, ncross_ref, memory_ref, w0_ref, w1_ref,
    q_ref, k_ref, v_ref, mixed_ref, p_ref, p_buf, p_sem,
):
    project_cross(io, ncross_ref, memory_ref, (w0_ref, w1_ref), q_ref, k_ref, v_ref)
    attend_docs(meta, True, None, None, [(q_ref, k_ref, v_ref, mixed_ref)], p_ref, p_buf, p_sem)


def cross_second(
    meta, io, second_ref, ncross_ref, memory_ref, norms_ref, w0_ref, w1_ref, w2_ref, w3_ref,
    mixed_first_ref,
    q_ref, k_ref, v_ref, mixed_ref, p_ref, third_ref, nffn_ref, p_buf, p_sem,
):
    project_cross(io, ncross_ref, memory_ref, (w2_ref, w3_ref), q_ref, k_ref, v_ref)
    attend_docs(meta, True, None, None, [(q_ref, k_ref, v_ref, mixed_ref)], p_ref, p_buf, p_sem)
    io.send(mixed_ref)
    io.wait("late")
    out_first = jnp.concatenate([w_out(w0_ref), w_out(w1_ref)], axis=0)
    out_second = jnp.concatenate([w_out(w2_ref), w_out(w3_ref)], axis=0)

    def tile(i, carry):
        rows = rows_of(i)
        branch = dot(mixed_first_ref[rows, :], out_first) + dot(mixed_ref[rows, :], out_second)
        third = second_ref[rows, :] + branch
        third_ref[rows, :] = third
        io.send(third_ref, rows)
        nffn_ref[rows, :] = layer_norm(third, norms_ref[6:7], norms_ref[7:8])
        io.send(nffn_ref, rows)
        return carry

    lax.fori_loop(0, TILES, tile, 0)


def ffn_both(
    meta, io, third_ref, nffn_ref, cot_ref, norms_ref, u0_ref, u1_ref, u2_ref, u3_ref,
    w0_ref, w1_ref, w2_ref, w3_ref,
    placed_ref, out_ref, g3_ref, g3_low_ref, gln_ref, own_ref, other_ref, hidden_ref, before_ref, sums_ref,
):
    sums_ref[...] = jnp.zeros_like(sums_ref)
    in_refs = (u0_ref, u1_ref, u2_ref, u3_ref)
    w_refs = (w0_ref, w1_ref, w2_ref, w3_ref)

    def tile(i, carry):
        rows = rows_of(i)
        io.wait_rows(i)
        nffn = nffn_ref[rows, :]
        cot = cot_ref[rows, :]
        outs = []
        grads = []

        def phases(g, c, group):
            w_in = in_refs[g]
            w_out_rows = w_refs[g]
            cols = slice(256 * c, 256 * c + 256)

            def enter():
                return dot(nffn, w_in[:, cols]), dot_nt(cot, w_out_rows[cols, :])

            def bend(state):
                def piece(x, grad_hidden):
                    square = x * x
                    half = 0.5 + 0.5 * jnp.tanh(x * (gelu_root + (gelu_root * gelu_cube) * square))
                    value = x * half
                    rise = 2.0 * gelu_root + (6.0 * gelu_root * gelu_cube) * square
                    slope = half + value * (1.0 - half) * rise
                    return value.astype(bf16), (grad_hidden * slope).astype(bf16)

                hidden, grad_before = by_pieces(piece, 32, 0, *state)
                if g < 2:
                    place = slice(512 * g + 256 * c, 512 * g + 256 * c + 256)
                    hidden_ref[rows, place] = hidden
                    before_ref[rows, place] = grad_before
                group[c] = hidden, grad_before

            def leave(_):
                if c == 1:
                    outs.append(dot(lanes([group[0][0], group[1][0]]), w_out_rows[...]))

            def leave_back(_):
                if c == 1:
                    grads.append(dot_nt(lanes([group[0][1], group[1][1]]), w_in[...]))

            return enter, bend, leave, leave_back

        interleave(by_halves(4, phases))
        third = third_ref[rows, :]
        result = (third + ((outs[0] + outs[1]) + (outs[2] + outs[3]))).astype(bf16)
        out_ref[rows, :] = result
        placed_ref[rows, :] = result
        grad_normed = (grads[0] + grads[1]) + (grads[2] + grads[3])
        grad_norm = norm_backward(third, norms_ref[6:7], grad_normed, sums_ref, 0)
        g3 = cot.astype(f32) + grad_norm
        g3_ref[rows, :] = g3
        g3_low_ref[rows, :] = g3.astype(bf16)
        for ref in (out_ref, placed_ref, g3_ref, g3_low_ref):
            io.send(ref, rows)
        return carry

    lax.fori_loop(0, TILES, tile, 0)
    add_sums(sums_ref, gln_ref, 2)
    part = dot_tn(nffn_ref[...], before_ref[...])
    own_ref[0:512, :] = part[:, 0:512].astype(bf16)
    other_ref[0:512, :] = part[:, 512:1024].astype(bf16)
    io.send(own_ref, pl.ds(0, 512))
    io.send(other_ref, pl.ds(0, 512))
    part = dot_tn(hidden_ref[...], cot_ref[...])
    own_ref[512:1024, :] = part[0:512].astype(bf16)
    other_ref[512:1024, :] = part[512:1024].astype(bf16)
    io.send(own_ref, pl.ds(512, 512))
    io.send(other_ref, pl.ds(512, 512))


def back_start(io, g_ref, mixed_ref, w_refs, dm_ref, dq_ref, dk_ref, dv_ref):
    out_rows = jnp.concatenate([w_out(w) for w in w_refs], axis=0)

    def tile(i, carry):
        rows = rows_of(i)
        io.wait_rows(i)
        dm_ref[rows, :] = dot_nt(g_ref[rows, :], out_rows).astype(bf16)
        zeros = jnp.zeros((TILE, 256), f32)
        dq_ref[rows, :] = zeros
        dk_ref[rows, :] = zeros
        dv_ref[rows, :] = zeros
        return carry

    lax.fori_loop(0, TILES, tile, 0)


def attention_back_first(
    cross, meta, io, g_ref, nq_ref, nkv_ref, rank_row_ref, limit_ref, w0_ref, w1_ref,
    q_ref, k_ref, v_ref, mixed_ref, p_ref,
    dq_ref, dk_ref, dv_ref, own_ref, other_ref,
    rank_ref, dm_ref, dqs_ref, dks_ref, dvs_ref, p_buf, p_sem,
):
    load = (p_ref, p_buf, p_sem)
    start_load(meta, cross, load)
    if not cross:
        spread_ranks(rank_row_ref, rank_ref)
    back_start(io, g_ref, mixed_ref, (w0_ref, w1_ref), dm_ref, dqs_ref, dks_ref, dvs_ref)

    io.wait("soon")
    attend_docs_back(
        meta, cross, None if cross else rank_ref, limit_ref, q_ref, k_ref, v_ref, mixed_ref,
        dm_ref, dqs_ref, dks_ref, dvs_ref, load,
    )

    dq_ref[...] = dqs_ref[...].astype(bf16)
    dk_ref[...] = dks_ref[...].astype(bf16)
    dv_ref[...] = dvs_ref[...].astype(bf16)
    for ref in (dq_ref, dk_ref, dv_ref):
        io.send(ref)
    io.wait("late")
    nq = nq_ref[...]
    nkv = nkv_ref[...]
    kv = dot_tn(nkv, lanes([dk_ref[...], dv_ref[...]]))
    for n, part in enumerate((dot_tn(nq, dq_ref[...]), kv[:, 0:256], kv[:, 256:512])):
        own_ref[:, 128 * n : 128 * n + 128] = part[:, :128].astype(bf16)
        other_ref[:, 128 * n : 128 * n + 128] = part[:, 128:].astype(bf16)
    part = dot_tn(mixed_ref[...], g_ref[...])
    for j in range(4):
        rows = slice(128 * j, 128 * j + 128)
        own_ref[rows, 384:512] = part[:128, rows].astype(bf16)
        other_ref[rows, 384:512] = part[128:, rows].astype(bf16)


def back_second_docs(
    cross, meta, io, g_ref, rank_row_ref, limit_ref, w_refs, q_ref, k_ref, v_ref, mixed_ref, p_ref,
    rank_ref, dm_ref, dqs_ref, dks_ref, dvs_ref, p_buf, p_sem,
):
    load = (p_ref, p_buf, p_sem)
    start_load(meta, cross, load)
    if not cross:
        spread_ranks(rank_row_ref, rank_ref)
    back_start(io, g_ref, mixed_ref, w_refs, dm_ref, dqs_ref, dks_ref, dvs_ref)

    io.wait("soon")
    attend_docs_back(
        meta, cross, None if cross else rank_ref, limit_ref, q_ref, k_ref, v_ref, mixed_ref,
        dm_ref, dqs_ref, dks_ref, dvs_ref, load,
    )


def stream_grads(rows, first, second, firsts, seconds):
    dq, dk, dv = first
    dq2, dk2, dv2 = (ref[rows, :].astype(bf16) for ref in second)
    w0, w1 = firsts
    w2, w3 = seconds
    grad_q = dot_nt(dq[rows, :], lanes([w_query(w0), w_query(w1)])) + dot_nt(
        dq2, lanes([w_query(w2), w_query(w3)])
    )
    kv = lanes([dk[rows, :], dv[rows, :]])
    kv2 = lanes([dk2, dv2])
    grad_kv = dot_nt(kv, lanes([w_key(w0), w_key(w1), w_value(w0), w_value(w1)])) + dot_nt(
        kv2, lanes([w_key(w2), w_key(w3), w_value(w2), w_value(w3)])
    )
    return grad_q, grad_kv


def cross_back_second(
    meta, io, g_low_ref, g_ref, second_ref, norms_ref, w0_ref, w1_ref, w2_ref, w3_ref,
    dq_ref, dk_ref, dv_ref, q_ref, k_ref, v_ref, mixed_ref, p_ref,
    g2_ref, g2_low_ref, placed_ref, gmem_ref, gln_ref,
    dm_ref, dqs_ref, dks_ref, dvs_ref, p_buf, p_sem, sums_ref,
):
    back_second_docs(
        True, meta, io, g_low_ref, None, None, (w2_ref, w3_ref), q_ref, k_ref, v_ref, mixed_ref, p_ref,
        None, dm_ref, dqs_ref, dks_ref, dvs_ref, p_buf, p_sem,
    )

    io.wait("late")
    sums_ref[...] = jnp.zeros_like(sums_ref)

    def tile(i, carry):
        rows = rows_of(i)
        grad_q, grad_kv = stream_grads(
            rows,
            (dq_ref, dk_ref, dv_ref),
            (dqs_ref, dks_ref, dvs_ref),
            (w0_ref, w1_ref),
            (w2_ref, w3_ref),
        )
        low_kv = grad_kv.astype(bf16)
        gmem_ref[rows, :] = low_kv
        placed_ref[rows, :] = low_kv.astype(f32)
        io.send(gmem_ref, rows)
        io.send(placed_ref, rows)
        grad_norm = norm_backward(second_ref[rows, :], norms_ref[4:5], grad_q, sums_ref, 0)
        g2 = g_ref[rows, :] + grad_norm
        g2_ref[rows, :] = g2
        g2_low_ref[rows, :] = g2.astype(bf16)
        io.send(g2_ref, rows)
        io.send(g2_low_ref, rows)
        return carry

    lax.fori_loop(0, TILES, tile, 0)
    add_sums(sums_ref, gln_ref, 2)


def self_back_second(
    meta, io, g_low_ref, rank_row_ref, limit_ref, w2_ref, w3_ref,
    q_ref, k_ref, v_ref, mixed_ref, p_ref,
    dq_ref, dk_ref, dv_ref,
    rank_ref, dm_ref, dqs_ref, dks_ref, dvs_ref, p_buf, p_sem,
):
    back_second_docs(
        False, meta, io, g_low_ref, rank_row_ref, limit_ref, (w2_ref, w3_ref), q_ref, k_ref, v_ref,
        mixed_ref, p_ref, rank_ref, dm_ref, dqs_ref, dks_ref, dvs_ref, p_buf, p_sem,
    )
    dq_ref[...] = dqs_ref[...].astype(bf16)
    dk_ref[...] = dks_ref[...].astype(bf16)
    dv_ref[...] = dvs_ref[...].astype(bf16)


def self_back_finish(
    meta, io, g_ref, xq_ref, xc_ref, norms_ref, w0_ref, w1_ref, w2_ref, w3_ref,
    dq_ref, dk_ref, dv_ref, dq2_ref, dk2_ref, dv2_ref,
    placed_q_ref, placed_c_ref, gq_ref, gc_ref, gln_ref, sums_ref,
):
    sums_ref[...] = jnp.zeros_like(sums_ref)

    def tile(i, carry):
        rows = rows_of(i)
        io.wait_rows(i)
        grad_q, grad_kv = stream_grads(
            rows,
            (dq_ref, dk_ref, dv_ref),
            (dq2_ref, dk2_ref, dv2_ref),
            (w0_ref, w1_ref),
            (w2_ref, w3_ref),
        )
        grad_norm = norm_backward(xq_ref[rows, :], norms_ref[0:1], grad_q, sums_ref, 0)
        low_q = (g_ref[rows, :] + grad_norm).astype(bf16)
        gq_ref[rows, :] = low_q
        placed_q_ref[rows, :] = low_q.astype(f32)
        io.send(gq_ref, rows)
        io.send(placed_q_ref, rows)
        grad_norm = norm_backward(xc_ref[rows, :], norms_ref[2:3], grad_kv, sums_ref, 16)
        low_c = grad_norm.astype(bf16)
        gc_ref[rows, :] = low_c
        placed_c_ref[rows, :] = low_c.astype(f32)
        io.send(gc_ref, rows)
        io.send(placed_c_ref, rows)
        return carry

    lax.fori_loop(0, TILES, tile, 0)
    add_sums(sums_ref, gln_ref, 4)


def place_rows(meta, *refs):
    count = len(refs) // 3
    for n in range(count):
        refs[2 * count + n][...] = refs[n][...].astype(refs[2 * count + n].dtype)


GROUP = 8


def position(meta):
    r = meta[35]
    return lax.rem(r, 2), r // 2


def join(own, other, rows):
    return (own[rows, :].astype(f32) + other[rows, :].astype(f32)).astype(bf16)


def join_halves(meta, own, other, keep, send):
    y, _ = position(meta)
    size = keep.shape[0]
    keep[...] = join(own, other, rows_of(y, size))
    send[...] = join(own, other, rows_of(1 - y, size))


def join_chunks(meta, kept, arrived, keep, sends):
    _, z = position(meta)
    size = keep.shape[0]
    keep[...] = join(kept, arrived, rows_of(z, size))
    for s, (send, first) in enumerate(sends, 1):
        send[first : first + size, :] = join(kept, arrived, rows_of(z ^ s, size))


def add_up(kept, parts, first):
    size = kept.shape[0]
    total = kept[...].astype(f32)
    for part in parts:
        total = total + part[first : first + size, :].astype(f32)
    return total.astype(bf16)


def half_of(meta, total, parts, first, half):
    _, z = position(meta)
    size = total.shape[0]
    half[rows_of(z, size), :] = total[...]
    for s, part in enumerate(parts, 1):
        half[rows_of(z ^ s, size), :] = part[first : first + size, :]


def slot_1(meta, ffn_own, ffn_other, keep, send):
    join_halves(meta, ffn_own, ffn_other, keep, send)


def slot_2(
    meta, ffn_kept, ffn_arrived, cross_own, cross_other, ffn_keep, f1, f2, f3, keep, send
):
    join_chunks(meta, ffn_kept, ffn_arrived, ffn_keep, [(f1, 0), (f2, 0), (f3, 0)])
    join_halves(meta, cross_own, cross_other, keep, send)


def slot_3(
    meta, ffn_kept, f1, f2, f3, cross_kept, cross_arrived, self_own, self_other,
    ffn_total, cross_keep, m1, m2, m3, self_keep, self_send,
):
    join_halves(meta, self_own, self_other, self_keep, self_send)
    total = add_up(ffn_kept, (f1, f2, f3), 0)
    ffn_total[...] = total
    size = total.shape[0]
    join_chunks(meta, cross_kept, cross_arrived, cross_keep, [(m, size) for m in (m1, m2, m3)])
    for m in (m1, m2, m3):
        m[0:size, :] = total


def slot_4(
    meta, ffn_total, m1, m2, m3, cross_kept, self_kept, self_arrived,
    ffn_half, cross_total, self_keep, *sends,
):
    join_chunks(meta, self_kept, self_arrived, self_keep, [(send, 0) for send in sends])
    total = add_up(cross_kept, (m1, m2, m3), ffn_total.shape[0])
    cross_total[...] = total
    size = total.shape[0]
    for send in sends:
        send[size:, :] = total
    half_of(meta, ffn_total, (m1, m2, m3), 0, ffn_half)


def slot_5(meta, self_kept, cross_total, m1, m2, m3, gln_own, gln_other, send, cross_half):
    size = self_kept.shape[0]
    total = add_up(self_kept, (m1, m2, m3), 0)
    gln = gln_own[...] + gln_other[...]
    gln = jnp.concatenate([gln, jnp.zeros((8, D), f32)], axis=0).astype(bf16)
    for r in range(GROUP):
        send[r, 0:size, :] = total
        send[r, size : size + 16, :] = gln
    half_of(meta, cross_total, (m1, m2, m3), size, cross_half)


def unpack_attention(whole_ref, outs):
    for i in range(3):
        outs[i][...] = whole_ref[:, 128 * i : 128 * i + 128].astype(f32)
    for j in range(4):
        rows = slice(128 * j, 128 * j + 128)
        outs[3][:, rows] = whole_ref[rows, 384:512].astype(f32)


def unpack_early(meta, ffn_half, ffn_arrived, cross_half, cross_arrived, *refs):
    *outs, cross_whole, ffn_whole = refs
    y, _ = position(meta)
    cross_whole[rows_of(y, 256), :] = cross_half[...]
    cross_whole[rows_of(1 - y, 256), :] = cross_arrived[...]
    unpack_attention(cross_whole, outs[2:])
    ffn_whole[rows_of(y, 512), :] = ffn_half[...]
    ffn_whole[rows_of(1 - y, 512), :] = ffn_arrived[...]
    outs[0][...] = ffn_whole[0:512, :].astype(f32)
    outs[1][...] = ffn_whole[512:1024, :].astype(f32)


def unpack_late(meta, parts, *refs):
    *outs, gln, whole_ref = refs
    size = parts.shape[1] - 16
    total = parts[0, size : size + 16, :].astype(f32)
    for r in range(1, GROUP):
        total = total + parts[r, size : size + 16, :].astype(f32)
    gln[...] = total[0:8]
    for r in range(GROUP):
        first = size * (4 * (r % 2) + r // 2)
        whole_ref[first : first + size, :] = parts[r, 0:size, :]
    unpack_attention(whole_ref, outs)


def whole(shape):
    zeros = (0,) * len(shape)
    return pl.BlockSpec(shape, lambda d, meta: zeros)


def own_row(width):
    return pl.BlockSpec((SEQ, width), lambda d, meta: (meta[0], 0))


ANY = pl.BlockSpec(memory_space=pl.ANY)


def in_hbm(x):
    return pltpu.with_memory_space_constraint(x, pltpu.HBM)


probability_out = (pltpu.HBM((DOCS, 4, FAST_K, FAST_Q), bf16), None, ANY)
probability_scratch = [
    pltpu.VMEM((2, TOGETHER, 4, FAST_K, FAST_Q), bf16),
    pltpu.SemaphoreType.DMA((2,)),
]


class Copies:
    def __init__(self, meta):
        self.first = meta[0] * SEQ
        self.loads = {}
        self.tiles = []
        self.sends = []

    def load(self, stage, source, target, sems, own_row):
        if stage == "tiles":
            first = self.first if own_row else 0
            self.tiles.append((source, target, sems, first))
            return
        if own_row:
            source = source.at[pl.ds(pl.multiple_of(self.first, SEQ), SEQ)]
        copy = pltpu.make_async_copy(source, target, sems[0].at[sems[1], 0])
        self.loads.setdefault(stage, []).append(copy)

    def tile(self, entry, i):
        source, target, (sems, b), first = entry
        rows = pl.ds(pl.multiple_of(first + i * TILE, TILE), TILE)
        return pltpu.make_async_copy(source.at[rows], target.at[rows_of(i)], sems.at[b, i])

    def start(self):
        for copy in self.loads.get("now", []):
            copy.start()
        for i in range(TILES):
            for entry in self.tiles:
                self.tile(entry, i).start()
        for stage in ("soon", "late"):
            for copy in self.loads.get(stage, []):
                copy.start()

    def wait(self, stage):
        for copy in self.loads.pop(stage, []):
            copy.wait()

    def wait_rows(self, i):
        for entry in self.tiles:
            self.tile(entry, i).wait()

    def result(self, source, target, sem, own_row):
        self.sends.append([source, target, sem, own_row, False])

    def send(self, ref, rows=None):
        for entry in self.sends:
            source, target, sem, own_row, _ = entry
            if source is ref:
                entry[4] = True
                first = self.first if own_row else 0
                if rows is None:
                    size = source.shape[0]
                else:
                    source = source.at[rows]
                    first, size = first + rows.start, rows.size
                if rows is not None or own_row:
                    target = target.at[pl.ds(pl.multiple_of(first, size), size)]
                pltpu.make_async_copy(source, target, sem).start()

    def finish(self):
        for stage in list(self.loads):
            self.wait(stage)
        for source, _, _, _, started in self.sends:
            if not started:
                self.send(source)
        for source, target, sem, own_row, _ in self.sends:
            if own_row:
                target = target.at[pl.ds(pl.multiple_of(self.first, SEQ), SEQ)]
            pltpu.make_async_copy(source, target, sem).wait()


def out(shape, dtype, own_row=False):
    return (shape, dtype, own_row)


def call(kernel, name, operands, outs, scratch, flops, token=None):
    arrays = [operands[0][0]]
    in_specs, out_specs, out_shapes = [], [], []
    buffers = []
    loads = []
    for n, (x, how) in enumerate(operands[1:]):
        if isinstance(how, str):
            stage, _, row = how.partition("_")
            shape = ((SEQ,) + x.shape[1:]) if row else x.shape
            loads.append((n, stage, len(buffers), bool(row)))
            buffers.append(pltpu.VMEM(shape, x.dtype))
            arrays.append(in_hbm(x))
            in_specs.append(ANY)
        else:
            arrays.append(x)
            in_specs.append(how)
    results = []
    for n, (shape, dtype, how) in enumerate(outs):
        if isinstance(how, bool):
            results.append((n, len(buffers), how))
            buffers.append(pltpu.VMEM(shape, dtype))
            shape = ((2 * SEQ,) + shape[1:]) if how else shape
            out_shapes.append(pltpu.HBM(shape, dtype))
            out_specs.append(ANY)
        else:
            out_shapes.append(jax.ShapeDtypeStruct(shape, dtype) if dtype else shape)
            out_specs.append(how)
    n_in, n_out = len(in_specs), len(out_specs)
    if token is not None:
        arrays.append(token)
        in_specs.append(whole((8, 128)))
        out_specs.append(whole((8, 128)))
        out_shapes.append(jax.ShapeDtypeStruct((8, 128), f32))

    def body(meta, *refs):
        ins, refs = list(refs[:n_in]), refs[len(in_specs) - n_in + n_in :]
        results_out, refs = list(refs[:n_out]), refs[n_out:]
        if token is not None:
            token_out, refs = refs[0], refs[1:]
            token_out[...] = jnp.zeros_like(token_out)
        bufs, refs = refs[: len(buffers)], refs[len(buffers) :]
        rest = refs[: len(scratch)]
        copies = Copies(meta)
        if buffers:
            sems = refs[len(scratch)]
        for n, stage, b, row in loads:
            copies.load(stage, ins[n], bufs[b], (sems, b), row)
            ins[n] = bufs[b]
        for n, b, row in results:
            copies.result(bufs[b], results_out[n], sems.at[b, 0], row)
            results_out[n] = bufs[b]
        copies.start()
        copies.wait("now")
        if buffers:
            kernel(meta, copies, *ins, *results_out, *rest)
        else:
            kernel(meta, *ins, *results_out, *rest)
        copies.finish()

    moved = sum(x.size * x.dtype.itemsize for x in arrays[1:])
    sems = [pltpu.SemaphoreType.DMA((len(buffers), TILES))] if buffers else []
    return pl.pallas_call(
        body,
        name=name,
        grid_spec=pltpu.PrefetchScalarGridSpec(
            num_scalar_prefetch=1,
            grid=(1,),
            in_specs=in_specs,
            out_specs=out_specs,
            scratch_shapes=buffers + scratch + sems,
        ),
        out_shape=out_shapes,
        compiler_params=pltpu.CompilerParams(
            dimension_semantics=("arbitrary",), vmem_limit_bytes=50 * 1024 * 1024
        ),
        cost_estimate=pl.CostEstimate(
            flops=int(flops), bytes_accessed=int(moved), transcendentals=0
        ),
    )(*arrays)


def simple(kernel, name, meta, operands, outs, scratch=()):
    return pl.pallas_call(
        kernel,
        name=name,
        grid_spec=pltpu.PrefetchScalarGridSpec(
            num_scalar_prefetch=1,
            grid=(1,),
            in_specs=[whole(x.shape) for x in operands],
            out_specs=[whole(shape) for shape, _ in outs],
            scratch_shapes=scratch,
        ),
        out_shape=[jax.ShapeDtypeStruct(shape, dtype) for shape, dtype in outs],
        compiler_params=pltpu.CompilerParams(vmem_limit_bytes=16 * 1024 * 1024),
    )(meta, *operands)


def full(x):
    return (x, whole(x.shape))


def shards(
    query_stream,
    content_stream,
    memory,
    segment_ids,
    source_segments,
    context_rank,
    context_limit,
    padding,
    ln_query_gain,
    ln_query_bias,
    ln_content_gain,
    ln_content_bias,
    self_query,
    self_key,
    self_value,
    self_out,
    ln_cross_gain,
    ln_cross_bias,
    cross_query,
    cross_key,
    cross_value,
    cross_out,
    ln_ffn_gain,
    ln_ffn_bias,
    ffn_in,
    ffn_out,
    cotangent,
):
    core = lax.axis_index("heads") % 2

    def to_core(x):
        return lax.ppermute(x, "heads", [(h, h ^ 1) for h in range(4)])

    hold = lambda *xs: lax.optimization_barrier(xs)

    def to_chip(x):
        return lax.ppermute(x, "heads", [(h, h ^ 2) for h in range(4)])

    row = pl.BlockSpec((1, 8, 128), lambda d, core: (core[0], 0, 0))

    def token_row(x):
        return (in_hbm(x.reshape(2, 8, 128)), row)

    def fixed(x):
        zeros = (0,) * x.ndim
        return (in_hbm(x), pl.BlockSpec(x.shape, lambda d, core: zeros))

    prepared = [
        ((36,), jnp.int32, pl.BlockSpec(memory_space=pltpu.SMEM)),
        ((1, SEQ), f32, whole((1, SEQ))),
        ((1, SEQ), f32, whole((1, SEQ))),
        ((8, D), f32, whole((8, D))),
        ((D, D), bf16, whole((D, D))),
        ((D, D), bf16, whole((D, D))),
    ]
    gains = (
        ln_query_gain,
        ln_query_bias,
        ln_content_gain,
        ln_content_bias,
        ln_cross_gain,
        ln_cross_bias,
        ln_ffn_gain,
        ln_ffn_bias,
    )
    weights = (self_query, self_key, self_value, self_out)
    weights += (cross_query, cross_key, cross_value, cross_out)
    tokens = (segment_ids, source_segments, context_rank, context_limit, padding)
    meta, rank, limit, norms, ws0, wc0 = call(
        prepare,
        "prepare",
        [(jnp.stack([core, lax.axis_index("rows") % GROUP]).astype(jnp.int32), None)]
        + [token_row(x) for x in tokens]
        + [fixed(x.reshape(1, D)) for x in gains]
        + [fixed(x) for x in weights],
        prepared,
        [],
        0,
    )

    ws1 = to_core(ws0)
    ws2 = to_chip(ws0)
    wc1 = to_core(wc0)
    u0, v0 = ffn_in, ffn_out
    meta_in = (meta, None)

    heads_out = [out((SEQ, 256), bf16)] * 4

    def stream_out(dtype, own_row=False):
        return out((SEQ, D), dtype, own_row)

    def now(*xs):
        return [(x, "now") for x in xs]

    def soon(*xs):
        return [(x, "soon") for x in xs]

    def late(*xs):
        return [(x, "late") for x in xs]

    def small(*xs):
        return [(x, whole(x.shape)) for x in xs]

    limits = pltpu.VMEM((SEQ, 128), f32)
    pair_flops = 2 * SEQ * D * 768 + 2 * 2 * 4 * DOCS * FAST_Q * FAST_K * 256

    nq, nc, *first, token = call(
        self_first,
        "self_first",
        [meta_in, (query_stream, "tiles_row"), (content_stream, "tiles_row")]
        + small(rank, limit, norms)
        + now(ws0, ws1),
        [stream_out(bf16), stream_out(bf16)] + heads_out + [probability_out],
        [limits] + probability_scratch,
        pair_flops,
        jnp.zeros((8, 128), f32),
    )
    ws2, wc0, token = hold(ws2, wc0, token)
    ws3 = to_core(ws2)
    wc2 = to_chip(wc0)
    *second_heads, second, ncross, token = call(
        self_second,
        "self_second",
        [meta_in, (query_stream, "late_row")]
        + [(nq, "tiles"), (nc, "tiles")]
        + small(rank, limit, norms)
        + late(ws0, ws1)
        + now(ws2, ws3)
        + late(first[3]),
        heads_out + [probability_out, stream_out(f32), stream_out(bf16)],
        [limits] + probability_scratch,
        pair_flops + 2 * SEQ * D * D,
        token,
    )
    wc2, u0, v0, token = hold(wc2, u0, v0, token)
    wc3 = to_core(wc2)
    u2 = to_chip(u0)
    u1 = to_core(u0)
    *cross_heads, token = call(
        cross_first,
        "cross_first",
        [meta_in, (ncross, "tiles"), (memory, "tiles_row")] + now(wc0, wc1),
        heads_out + [probability_out],
        probability_scratch,
        pair_flops,
        token,
    )
    wc3, u2, v0, token = hold(wc3, u2, v0, token)
    u3 = to_core(u2)
    v2 = to_chip(v0)
    v1 = to_core(v0)
    *cross_heads_second, third, nffn, token = call(
        cross_second,
        "cross_second",
        [meta_in]
        + late(second)
        + [(ncross, "tiles"), (memory, "tiles_row")]
        + small(norms)
        + late(wc0, wc1)
        + now(wc2, wc3)
        + late(cross_heads[3]),
        heads_out + [probability_out, stream_out(f32), stream_out(bf16)],
        probability_scratch,
        pair_flops + 2 * SEQ * D * D,
        token,
    )
    u3, v2, token = hold(u3, v2, token)
    v3 = to_core(v2)
    grads_ln = ((8, D), f32, whole((8, D)))
    placed_output, output, g3, g3_low, gln_ffn, ffn_own, ffn_other, token = call(
        ffn_both,
        "ffn_both",
        [meta_in]
        + [(third, "tiles"), (nffn, "tiles"), (cotangent, "tiles_row")]
        + small(norms)
        + now(u0, u1, u2, u3, v0, v1, v2, v3),
        [
            stream_out(bf16, True),
            stream_out(bf16),
            stream_out(f32),
            stream_out(bf16),
            grads_ln,
            out((1024, D), bf16),
            out((1024, D), bf16),
        ],
        [pltpu.VMEM((SEQ, 1024), bf16), pltpu.VMEM((SEQ, 1024), bf16), pltpu.VMEM((16, D), f32)],
        12 * SEQ * D * 2048,
        token,
    )

    row_count = lax.axis_size("rows")
    assert row_count % GROUP == 0

    def along_rows(x, s):
        return lax.ppermute(x, "rows", [(r, r ^ s) for r in range(row_count)])

    def to_y(x):
        return along_rows(x, 1)

    def to_z(sends):
        return [along_rows(x, 2 * s) for s, x in enumerate(sends, 1)]

    def rows_out(*sizes):
        return [((n, D), bf16) for n in sizes]

    ffn_other = to_core(ffn_other)

    back_scratch = [pltpu.VMEM((SEQ, 256), bf16)] + [pltpu.VMEM((SEQ, 256), f32)] * 3
    back_scratch += probability_scratch
    pair_out = out((SEQ, 256), bf16)
    packed_outs = [out((D, D), bf16), out((D, D), bf16)]
    back_flops = 2 * SEQ * D * 256 + 4 * 2 * 4 * DOCS * FAST_Q * FAST_K * 256

    def head_inputs(natural, p):
        return soon(*natural) + [(in_hbm(p), ANY)]

    *cross_grads, cross_own, cross_other, token = call(
        functools.partial(attention_back_first, True),
        "cross_back_first",
        [meta_in]
        + [(g3_low, "tiles")]
        + late(ncross)
        + [(memory, "late_row")]
        + small(rank, limit)
        + now(wc0, wc1)
        + head_inputs(cross_heads[0:4], cross_heads[4]),
        [pair_out] * 3 + packed_outs,
        [limits] + back_scratch,
        back_flops + 2 * SEQ * D * 1024,
        token,
    )
    ffn_other, token = hold(ffn_other, token)
    ffn_keep, ffn_send = simple(slot_1, "slot_1", meta, [ffn_own, ffn_other], rows_out(512, 512))
    ffn_send, token = hold(ffn_send, token)
    ffn_arrived = to_y(ffn_send)
    cross_other = to_core(cross_other)
    g2, g2_low, placed_mem, grad_mem, gln_cross, token = call(
        cross_back_second,
        "cross_back_second",
        [meta_in]
        + [(g3_low, "tiles")]
        + late(g3, second)
        + small(norms)
        + late(wc0, wc1)
        + now(wc2, wc3)
        + late(*cross_grads)
        + head_inputs(cross_heads_second[0:4], cross_heads_second[4]),
        [stream_out(f32), stream_out(bf16), stream_out(f32, True), stream_out(bf16), grads_ln],
        back_scratch + [pltpu.VMEM((16, D), f32)],
        back_flops + 2 * SEQ * D * 1536,
        token,
    )
    ffn_arrived, cross_other, token = hold(ffn_arrived, cross_other, token)
    ffn_keep, *sends, cross_keep, cross_send = simple(
        slot_2,
        "slot_2",
        meta,
        [ffn_keep, ffn_arrived, cross_own, cross_other],
        rows_out(128, 128, 128, 128, 256, 256),
    )
    ffn_keep, cross_send, token = hold(ffn_keep, cross_send, token)
    ffn_parts = to_z(sends)
    cross_arrived = to_y(cross_send)

    *self_grads, self_own, self_other, token = call(
        functools.partial(attention_back_first, False),
        "self_back_first",
        [meta_in]
        + [(g2_low, "tiles")]
        + late(nq, nc)
        + small(rank, limit)
        + now(ws0, ws1)
        + head_inputs(first[0:4], first[4]),
        [pair_out] * 3 + packed_outs,
        [limits] + back_scratch,
        back_flops + 2 * SEQ * D * 1024,
        token,
    )
    *ffn_parts, cross_arrived, self_other, token = hold(
        *ffn_parts, cross_arrived, self_other, token
    )
    self_other = to_core(self_other)
    ffn_total, cross_keep, *sends, self_keep, self_send = simple(
        slot_3,
        "slot_3",
        meta,
        [ffn_keep, *ffn_parts, cross_keep, cross_arrived, self_own, self_other],
        rows_out(128, 64, 192, 192, 192, 256, 256),
    )
    ffn_total, self_send, token = hold(ffn_total, self_send, token)
    self_arrived = to_y(self_send)
    messages = to_z(sends)
    *self_grads_second, token = call(
        self_back_second,
        "self_back_second",
        [meta_in, (g2_low, "tiles")]
        + small(rank, limit)
        + now(ws2, ws3)
        + head_inputs(second_heads[0:4], second_heads[4]),
        [pair_out] * 3,
        [limits] + back_scratch,
        back_flops,
        token,
    )
    *messages, self_arrived, token = hold(*messages, self_arrived, token)
    ffn_half, cross_total, self_keep, *sends = simple(
        slot_4,
        "slot_4",
        meta,
        [ffn_total, *messages, cross_keep, self_keep, self_arrived],
        rows_out(512, 64, 64, 128, 128, 128),
    )
    cross_total, ffn_half, token = hold(cross_total, ffn_half, token)
    messages = to_z(sends)
    ffn_arrived = to_y(ffn_half)
    placed_q, placed_c, gq, gc, gln_self, token = call(
        self_back_finish,
        "self_back_finish",
        [meta_in, (g2, "tiles"), (query_stream, "tiles_row"), (content_stream, "tiles_row")]
        + small(norms)
        + now(ws0, ws1, ws2, ws3)
        + [(x, "tiles") for x in self_grads + self_grads_second],
        [stream_out(f32, True), stream_out(f32, True), stream_out(bf16), stream_out(bf16), grads_ln],
        [pltpu.VMEM((32, D), f32)],
        2 * SEQ * D * 1536,
        token,
    )
    gln = jnp.concatenate([gln_self[0:4], gln_cross[0:2], gln_ffn[0:2]], axis=0)
    *messages, ffn_arrived, gln = hold(*messages, ffn_arrived, gln)
    last_send, cross_half = simple(
        slot_5,
        "slot_5",
        meta,
        [self_keep, cross_total, *messages, gln, to_core(gln)],
        [((GROUP, 80, D), bf16), ((256, D), bf16)],
    )
    output, grad_mem, last_send = hold(output, grad_mem, last_send)
    groups = None
    if row_count > GROUP:
        groups = [list(range(r, r + GROUP)) for r in range(0, row_count, GROUP)]
    last_parts = lax.all_to_all(last_send, "rows", 0, 0, axis_index_groups=groups)
    cross_arrived = to_y(cross_half)

    def over_groups(totals):
        if row_count == GROUP:
            return totals
        groups = [list(range(r, row_count, GROUP)) for r in range(GROUP)]
        return lax.psum(totals, "rows", axis_index_groups=groups)

    def both_rows(placed_own, arrays, name):
        count = len(arrays)
        size = SEQ // 2
        one = pl.BlockSpec((size, D), lambda i, meta: (i, 0))
        block = pl.BlockSpec((size, D), lambda i, meta: (2 * (1 - meta[0]) + i, 0))
        return pl.pallas_call(
            place_rows,
            name=name,
            grid_spec=pltpu.PrefetchScalarGridSpec(
                num_scalar_prefetch=1,
                grid=(2,),
                in_specs=[one] * count + [pl.BlockSpec(memory_space=pl.ANY)] * count,
                out_specs=[block] * count,
            ),
            out_shape=[jax.ShapeDtypeStruct(x.shape, x.dtype) for x in placed_own],
            input_output_aliases={1 + count + n: n for n in range(count)},
        )(meta, *[to_core(x) for x in arrays], *placed_own)

    out_both, grad_mem_both = both_rows([placed_output, placed_mem], [output, grad_mem], "place_early")
    gq_both, gc_both = both_rows([placed_q, placed_c], [gq, gc], "place_late")

    cross_arrived, out_both, gq_both = hold(cross_arrived, out_both, gq_both)
    attention_outs = [((512, 128), f32)] * 3 + [((128, 512), f32)]
    grad_ffn_in, grad_ffn_out, *grad_cross_parts = simple(
        unpack_early,
        "unpack_early",
        meta,
        [ffn_half, ffn_arrived, cross_half, cross_arrived],
        [((D, D), f32)] * 2 + attention_outs,
        [pltpu.VMEM((D, D), bf16), pltpu.VMEM((2 * D, D), bf16)],
    )
    *grad_self_parts, gln = simple(
        unpack_late,
        "unpack_late",
        meta,
        [last_parts],
        attention_outs + [((8, D), f32)],
        [pltpu.VMEM((D, D), bf16)],
    )
    grad_ffn_in, grad_ffn_out, grad_cross_parts, grad_self_parts, gln = over_groups(
        (grad_ffn_in, grad_ffn_out, grad_cross_parts, grad_self_parts, gln)
    )
    return (
        out_both,
        gq_both,
        gc_both,
        grad_mem_both,
        gln[0],
        gln[1],
        gln[2],
        gln[3],
        *grad_self_parts,
        gln[4],
        gln[5],
        *grad_cross_parts,
        gln[6],
        gln[7],
        grad_ffn_in,
        grad_ffn_out,
    )


def solution(mesh):
    assert mesh.shape["heads"] == 4
    row_spec = P("rows", None)
    flat = P("rows")
    by_column = P(None, "heads")
    by_row = P("heads", None)
    attention = (by_column, by_column, by_column, by_row)
    in_specs = (
        (row_spec,) * 3
        + (flat,) * 5
        + (P(),) * 4
        + attention
        + (P(),) * 2
        + attention
        + (P(),) * 2
        + (by_column, by_row, row_spec)
    )
    out_specs = (
        (row_spec,) * 4
        + (P(),) * 4
        + attention
        + (P(),) * 2
        + attention
        + (P(),) * 2
        + (by_column, by_row)
    )
    return jax.shard_map(shards, mesh=mesh, in_specs=in_specs, out_specs=out_specs, check_vma=False)
```

```python
import functools

import jax
import jax.numpy as jnp
from jax import lax
from jax.experimental import pallas as pl
from jax.experimental.pallas import tpu as pltpu
from jax.sharding import PartitionSpec as P

HEAD_DIM = 64
SEQ = 1024
DOCS = 8
D = 512
TILE = 256
TILES = SEQ // TILE
FAST_Q = 256
FAST_K = 208
LONG_Q = 128
LONG_K = 640

norm_eps = 1e-05
masked_score = -1e30
hidden_rank = 1e6
gelu_root = 0.7978845608028654
gelu_cube = 0.044715

f32 = jnp.float32
bf16 = jnp.bfloat16


def dot(a, b):
    return lax.dot_general(a, b, (((1,), (0,)), ((), ())), preferred_element_type=f32)


def dot_nt(a, b):
    return lax.dot_general(a, b, (((1,), (1,)), ((), ())), preferred_element_type=f32)


def dot_tn(a, b):
    return lax.dot_general(a, b, (((0,), (0,)), ((), ())), preferred_element_type=f32)


def lanes(parts):
    return jnp.concatenate(parts, axis=1)


NORM_ROWS = 32


def layer_norm(values, gain, shift):
    def piece(part):
        part = part.astype(f32)
        centre = part - jnp.mean(part, axis=-1, keepdims=True)
        spread = jnp.mean(centre * centre, axis=-1, keepdims=True)
        return (centre * lax.rsqrt(spread + norm_eps) * gain + shift).astype(bf16)

    return by_pieces(piece, NORM_ROWS, 0, values)


def eight_rows(values):
    return sum(values[8 * i : 8 * i + 8] for i in range(1, values.shape[0] // 8)) + values[0:8]


def norm_backward(values, gain, grad, sums_ref, first):
    sums = []

    def piece(part, grad_part):
        part = part.astype(f32)
        centre = part - jnp.mean(part, axis=-1, keepdims=True)
        spread = jnp.mean(centre * centre, axis=-1, keepdims=True)
        scale = lax.rsqrt(spread + norm_eps)
        xhat = centre * scale
        eg = grad_part * gain
        mean_eg = jnp.mean(eg, axis=-1, keepdims=True)
        mean_egx = jnp.mean(eg * xhat, axis=-1, keepdims=True)
        sums.append((eight_rows(grad_part * xhat), eight_rows(grad_part)))
        return scale * (eg - mean_eg - xhat * mean_egx)

    result = by_pieces(piece, NORM_ROWS, 0, values, grad)
    for n, parts in enumerate(zip(*sums)):
        sums_ref[first + 8 * n : first + 8 * n + 8, :] += sum(parts[1:], parts[0])
    return result


def add_sums(sums_ref, gln_ref, count):
    gln_ref[...] = jnp.zeros_like(gln_ref)
    for n in range(count):
        gln_ref[n : n + 1, :] = jnp.sum(sums_ref[8 * n : 8 * n + 8, :], axis=0, keepdims=True)


def by_pieces(work, size, axis, *arrays):
    count = arrays[0].shape[axis] // size
    pieces = []
    for i in range(count):
        cut = (slice(size * i, size * i + size),)
        cut = cut if axis == 0 else (slice(None),) + cut
        pieces.append(work(*[x[cut] for x in arrays]))
    if not isinstance(pieces[0], tuple):
        return jnp.concatenate(pieces, axis=axis)
    return tuple(jnp.concatenate(parts, axis=axis) for parts in zip(*pieces))


def rows_of(i, size=TILE):
    return pl.ds(pl.multiple_of(i * size, size), size)


def w_query(ref):
    return ref[:, 0:128]


def w_key(ref):
    return ref[:, 128:256]


def w_value(ref):
    return ref[:, 256:384]


def w_out(ref):
    return lanes([ref[128 * j : 128 * j + 128, 384:512] for j in range(4)])


def half_masks():
    place = lax.broadcasted_iota(jnp.int32, (1, 128), 1)
    low = jnp.where(place < HEAD_DIM, 1.0, 0.0).astype(f32)
    return (low.astype(bf16), (1.0 - low).astype(bf16))


def doc_bounds(meta, d, source):
    base = 17 if source else 1
    return meta[base + d], meta[base + 8 + d]


def window_of(first, limit):
    return pl.multiple_of(jnp.minimum((first // 16) * 16, limit), 16)


def key_bias(ks, ke, k0, width):
    place = k0 + lax.broadcasted_iota(jnp.int32, (width, 128), 0)
    return jnp.where((place >= ks) & (place < ke), 0.0, masked_score)


def make_bias(rank_ref, limit_ref, ks, ke, q0, k0, span, width):
    if rank_ref is None:
        return lanes([key_bias(ks, ke, k0, width)] * (span // 128))
    place = k0 + lax.broadcasted_iota(jnp.int32, (width, 128), 0)
    ranks = rank_ref[pl.ds(k0, width), :]
    ranks = jnp.where((place < ks + 2) & (ranks < hidden_rank), -1.0, ranks)
    ranks = jnp.where((place >= ks) & (place < ke), ranks, hidden_rank)
    limits = jnp.broadcast_to(limit_ref[...], (8, SEQ))
    limits = pltpu.roll(limits, lax.rem(SEQ - q0, SEQ), 1)[0:1, 0:span]
    row = k0 + lax.broadcasted_iota(jnp.int32, (width, span), 0)
    column = q0 + lax.broadcasted_iota(jnp.int32, (width, span), 1)
    seen = (lanes([ranks] * (span // 128)) < limits) & (row != column)
    return jnp.where(seen, 0.0, masked_score)


TOGETHER = 4
STEPS = DOCS // TOGETHER


LAG = 2


def interleave(items):
    items = [list(phases) for phases in items]
    depth = max(len(phases) for phases in items)
    results = [None] * len(items)
    for tick in range(len(items) + LAG * (depth - 1)):
        for phase in range(depth):
            n = tick - LAG * phase
            if 0 <= n < len(items) and phase < len(items[n]):
                run = items[n][phase]
                results[n] = run() if phase == 0 else run(results[n])
    return results


def by_halves(pairs, phases):
    shared = [{} for _ in range(pairs)]
    return [phases(n, a, shared[n]) for n in range(pairs) for a in range(2)]


def is_fast(meta, cross):
    return meta[34 if cross else 33] == 1


def both_heads(x, masks):
    return jnp.concatenate([x * masks[0], x * masks[1]], axis=0)


def pair_scores(queries, keys, masks):
    return dot_nt(both_heads(keys, masks), queries)


def raised(scores, bias):
    def piece(part, bias_part):
        part = part + bias_part
        return jnp.exp((part - jnp.max(part, axis=0, keepdims=True)).astype(bf16))

    return by_pieces(piece, 128, 1, scores, bias)


def weighted_values(values, parts):
    width = values.shape[1]
    mixed = []
    shares = []
    for a, part in enumerate(parts):
        rows = jnp.concatenate([values[64 * a : 64 * a + 64], jnp.ones((16, width), bf16)], axis=0)
        sums = dot(rows, part)
        share = 1.0 / sums[64:65]
        mixed.append(sums[:64] * share)
        shares.append(part * share.astype(bf16))
    return jnp.concatenate(mixed, axis=0).astype(bf16), shares


def pair_gradient(rows, parts):
    across = jnp.transpose(rows)
    halves = [dot(across[64 * a : 64 * a + 64], part) for a, part in enumerate(parts)]
    return jnp.transpose((jnp.concatenate(halves, axis=0) * HEAD_DIM**-0.5).astype(bf16))


def for_docs(meta, cross, run, before, after):
    @pl.when(is_fast(meta, cross))
    def _():
        def step(i, carry):
            slot = lax.rem(i, 2)
            before(i, slot)
            items = []
            for place in range(TOGETHER):
                d = TOGETHER * i + place
                ts, te = doc_bounds(meta, d, False)
                ks, ke = doc_bounds(meta, d, cross)
                q0 = window_of(ts, SEQ - FAST_Q)
                k0 = window_of(ks, SEQ - FAST_K)
                items += run(d, slot, place, q0, k0, FAST_Q, FAST_K, ts, te, ks, ke, True)
            interleave(items)
            after(i, slot)
            return carry

        lax.fori_loop(0, STEPS, step, 0)

    @pl.when(jnp.logical_not(is_fast(meta, cross)))
    def _():
        def doc(d, carry):
            ts, te = doc_bounds(meta, d, False)
            ks, ke = doc_bounds(meta, d, cross)
            base = (ts // 16) * 16
            k0 = window_of(ks, SEQ - LONG_K)

            def chunk(i, carry):
                lower = base + i * LONG_Q
                q0 = pl.multiple_of(jnp.minimum(lower, SEQ - LONG_Q), 16)
                low = jnp.maximum(ts, lower)
                high = jnp.minimum(te, lower + LONG_Q)
                interleave(run(d, None, None, q0, k0, LONG_Q, LONG_K, low, high, ks, ke, False))
                return carry

            return lax.fori_loop(0, (te - base + LONG_Q - 1) // LONG_Q, chunk, carry)

        lax.fori_loop(0, DOCS, doc, 0)


def attend_docs(meta, cross, rank_ref, limit_ref, halves, p_ref, p_buf, p_sem):
    pairs = 2 * len(halves)
    masks = half_masks()

    def save(i, slot):
        return pltpu.make_async_copy(p_buf.at[slot], p_ref.at[pl.ds(TOGETHER * i, TOGETHER)], p_sem.at[slot])

    def before(i, slot):
        @pl.when(i >= 2)
        def _():
            save(i - 2, slot).wait()

    def after(i, slot):
        save(i, slot).start()

    def run(d, slot, place, q0, k0, span, width, low, high, ks, ke, fast):
        bias = make_bias(rank_ref, limit_ref, ks, ke, q0, k0, span, width)
        row = q0 + lax.broadcasted_iota(jnp.int32, (span, 128), 0)
        inside = (row >= low) & (row < high)

        def phases(n):
            q_ref, k_ref, v_ref, mixed_ref = halves[n // 2]
            cols = slice(128 * (n % 2), 128 * (n % 2) + 128)

            def score():
                return pair_scores(q_ref[pl.ds(q0, span), cols], k_ref[pl.ds(k0, width), cols], masks)

            def weigh(scores):
                return [raised(scores[width * a : width * a + width], bias) for a in range(2)]

            def mix(parts):
                values = jnp.transpose(v_ref[pl.ds(k0, width), cols])
                mixed, parts = weighted_values(values, parts)
                if fast:
                    for a in range(2):
                        p_buf[slot, place, 2 * n + a] = parts[a]
                mixed = jnp.transpose(mixed).astype(f32)
                old = mixed_ref[pl.ds(q0, span), cols].astype(f32)
                mixed_ref[pl.ds(q0, span), cols] = jnp.where(inside, mixed, old).astype(bf16)

            return score, weigh, mix

        return [phases(n) for n in range(pairs)]

    for_docs(meta, cross, run, before, after)

    @pl.when(is_fast(meta, cross))
    def _():
        for i in range(STEPS - 2, STEPS):
            save(i, i % 2).wait()


def load_step(load, i, slot):
    p_ref, p_buf, p_sem = load
    return pltpu.make_async_copy(p_ref.at[pl.ds(TOGETHER * i, TOGETHER)], p_buf.at[slot], p_sem.at[slot])


def start_load(meta, cross, load):
    @pl.when(is_fast(meta, cross))
    def _():
        load_step(load, 0, 0).start()


def attend_docs_back(
    meta, cross, rank_ref, limit_ref, q_ref, k_ref, v_ref, mixed_ref, dm_ref,
    dq_ref, dk_ref, dv_ref, load,
):
    pairs = q_ref.shape[1] // 128
    masks = half_masks()
    p_buf = load[1]

    def before(i, slot):
        @pl.when(i + 1 < STEPS)
        def _():
            load_step(load, i + 1, 1 - slot).start()

        load_step(load, i, slot).wait()

    def after(i, slot):
        pass

    def run(d, slot, place, q0, k0, span, width, low, high, ks, ke, fast):
        row = q0 + lax.broadcasted_iota(jnp.int32, (span, 128), 0)
        inside = jnp.where((row >= low) & (row < high), 1.0, 0.0).astype(bf16)
        ones = jnp.ones((width, 128), bf16)
        if not fast:
            bias = make_bias(rank_ref, limit_ref, ks, ke, q0, k0, span, width)

        def phases(n):
            cols = slice(128 * n, 128 * n + 128)

            def differ():
                values = v_ref[pl.ds(k0, width), cols]
                mixed = mixed_ref[pl.ds(q0, span), cols]
                grad = dm_ref[pl.ds(q0, span), cols] * inside
                left = lanes([grad, -(grad * mixed)])
                right = both_heads(lanes([values, ones]), [lanes([m, m]) for m in masks])
                return grad, dot_nt(right, left)

            def slope(state):
                grad, delta = state
                if fast:
                    parts = [p_buf[slot, place, 2 * n + a] for a in range(2)]
                else:
                    queries = q_ref[pl.ds(q0, span), cols]
                    keys = k_ref[pl.ds(k0, width), cols]
                    scores = pair_scores(queries, keys, masks)
                    parts = [raised(scores[width * a : width * a + width], bias) for a in range(2)]
                    parts = weighted_values(jnp.transpose(v_ref[pl.ds(k0, width), cols]), parts)[1]
                slopes = [
                    by_pieces(
                        lambda part, change: part * change.astype(bf16),
                        16,
                        0,
                        parts[a],
                        delta[width * a : width * a + width],
                    )
                    for a in range(2)
                ]
                return grad, parts, slopes

            def spread(state):
                grad, parts, slopes = state
                queries = q_ref[pl.ds(q0, span), cols]
                dk = dv = None
                for a in range(2):
                    dk_a = dot(slopes[a], queries * masks[a])
                    dv_a = dot(parts[a], grad * masks[a])
                    dk = dk_a if dk is None else dk + dk_a
                    dv = dv_a if dv is None else dv + dv_a
                dq = pair_gradient(k_ref[pl.ds(k0, width), cols], slopes)
                dq_ref[pl.ds(q0, span), cols] += dq.astype(f32)
                dk_ref[pl.ds(k0, width), cols] += dk
                dv_ref[pl.ds(k0, width), cols] += dv

            return differ, slope, spread

        return [phases(n) for n in range(pairs)]

    for_docs(meta, cross, run, before, after)


def spread_ranks(rank_row_ref, rank_ref):
    rank_ref[...] = jnp.transpose(jnp.broadcast_to(rank_row_ref[...], (128, SEQ)))


def prepare(
    core, seg_ref, src_ref, rank_ref, limit_ref, pad_ref,
    n0, n1, n2, n3, n4, n5, n6, n7, sq, sk, sv, so, cq, ck, cv, co,
    meta_ref, ranks_ref, limits_ref, norms_ref, ws_ref, wc_ref,
):
    meta_ref[0] = core[0]
    meta_ref[35] = core[1]
    for base, ref in ((1, seg_ref), (17, src_ref)):
        ids = ref[0]
        meta_ref[base] = 0
        meta_ref[base + 15] = SEQ
        for d in range(1, DOCS):
            cut = jnp.sum(jnp.where(ids < d, 1.0, 0.0)).astype(jnp.int32)
            meta_ref[base + d] = cut
            meta_ref[base + 7 + d] = cut
    for place, base in ((33, 1), (34, 17)):
        fast = jnp.int32(1)
        for d in range(DOCS):
            q0 = window_of(meta_ref[1 + d], SEQ - FAST_Q)
            k0 = window_of(meta_ref[base + d], SEQ - FAST_K)
            fits = (meta_ref[9 + d] - q0 <= FAST_Q) & (meta_ref[base + 8 + d] - k0 <= FAST_K)
            fast = fast & fits.astype(jnp.int32)
        meta_ref[place] = fast
    ranks = jnp.where(pad_ref[0] != 0, hidden_rank, rank_ref[0].astype(f32))
    limits = limit_ref[0].astype(f32)
    for i in range(8):
        ranks_ref[0:1, 128 * i : 128 * i + 128] = ranks[i : i + 1]
        limits_ref[0:1, 128 * i : 128 * i + 128] = limits[i : i + 1]
    for i, ref in enumerate((n0, n1, n2, n3, n4, n5, n6, n7)):
        norms_ref[i : i + 1, :] = ref[...]
    for to, parts, out in ((ws_ref, (sq, sk, sv), so), (wc_ref, (cq, ck, cv), co)):
        for i, part in enumerate(parts):
            to[:, 128 * i : 128 * i + 128] = part[...]
        for j in range(4):
            to[128 * j : 128 * j + 128, 384:512] = out[:, 128 * j : 128 * j + 128]


def self_first(
    meta, io, xq_ref, xc_ref, rank_row_ref, limit_ref, norms_ref, w0_ref, w1_ref,
    nq_ref, nc_ref, q_ref, k_ref, v_ref, mixed_ref, p_ref, rank_ref, p_buf, p_sem,
):

    spread_ranks(rank_row_ref, rank_ref)
    wq = lanes([w_query(w0_ref), w_query(w1_ref)])
    wkv = lanes([w_key(w0_ref), w_key(w1_ref), w_value(w0_ref), w_value(w1_ref)])

    def tile(i, carry):
        rows = rows_of(i)
        io.wait_rows(i)
        nq = layer_norm(xq_ref[rows, :], norms_ref[0:1], norms_ref[1:2])
        nc = layer_norm(xc_ref[rows, :], norms_ref[2:3], norms_ref[3:4])
        nq_ref[rows, :] = nq
        nc_ref[rows, :] = nc
        q_ref[rows, :] = (dot(nq, wq) * (HEAD_DIM**-0.5)).astype(bf16)
        kv = dot(nc, wkv).astype(bf16)
        k_ref[rows, :] = kv[:, :256]
        v_ref[rows, :] = kv[:, 256:]
        return carry

    lax.fori_loop(0, TILES, tile, 0)

    for ref in (nq_ref, nc_ref, q_ref, k_ref, v_ref):
        io.send(ref)
    attend_docs(meta, False, rank_ref, limit_ref, [(q_ref, k_ref, v_ref, mixed_ref)], p_ref, p_buf, p_sem)


def self_second(
    meta, io, xq_ref, nq_ref, nc_ref, rank_row_ref, limit_ref, norms_ref, w0_ref, w1_ref, w2_ref, w3_ref,
    mixed_first_ref,
    q_ref, k_ref, v_ref, mixed_ref, p_ref, second_ref, ncross_ref, rank_ref, p_buf, p_sem,
):

    spread_ranks(rank_row_ref, rank_ref)
    wq = lanes([w_query(w2_ref), w_query(w3_ref)])
    wkv = lanes([w_key(w2_ref), w_key(w3_ref), w_value(w2_ref), w_value(w3_ref)])

    def tile(i, carry):
        rows = rows_of(i)
        io.wait_rows(i)
        q_ref[rows, :] = (dot(nq_ref[rows, :], wq) * (HEAD_DIM**-0.5)).astype(bf16)
        kv = dot(nc_ref[rows, :], wkv).astype(bf16)
        k_ref[rows, :] = kv[:, :256]
        v_ref[rows, :] = kv[:, 256:]
        return carry

    lax.fori_loop(0, TILES, tile, 0)

    for ref in (q_ref, k_ref, v_ref):
        io.send(ref)
    attend_docs(meta, False, rank_ref, limit_ref, [(q_ref, k_ref, v_ref, mixed_ref)], p_ref, p_buf, p_sem)

    io.send(mixed_ref)
    io.wait("late")
    out_first = jnp.concatenate([w_out(w0_ref), w_out(w1_ref)], axis=0)
    out_second = jnp.concatenate([w_out(w2_ref), w_out(w3_ref)], axis=0)

    def tile(i, carry):
        rows = rows_of(i)
        branch = dot(mixed_first_ref[rows, :], out_first) + dot(mixed_ref[rows, :], out_second)
        second = xq_ref[rows, :].astype(f32) + branch
        second_ref[rows, :] = second
        io.send(second_ref, rows)
        ncross_ref[rows, :] = layer_norm(second, norms_ref[4:5], norms_ref[5:6])
        io.send(ncross_ref, rows)
        return carry

    lax.fori_loop(0, TILES, tile, 0)


def project_cross(io, ncross_ref, memory_ref, weights, q_ref, k_ref, v_ref):
    wq = lanes([w_query(w) for w in weights])
    wkv = lanes([w_key(w) for w in weights] + [w_value(w) for w in weights])

    def tile(i, carry):
        rows = rows_of(i)
        io.wait_rows(i)
        q_ref[rows, :] = (dot(ncross_ref[rows, :], wq) * (HEAD_DIM**-0.5)).astype(bf16)
        kv = dot(memory_ref[rows, :], wkv).astype(bf16)
        k_ref[rows, :] = kv[:, :256]
        v_ref[rows, :] = kv[:, 256:]
        return carry

    lax.fori_loop(0, TILES, tile, 0)
    for ref in (q_ref, k_ref, v_ref):
        io.send(ref)


def cross_first(
    meta, io, ncross_ref, memory_ref, w0_ref, w1_ref,
    q_ref, k_ref, v_ref, mixed_ref, p_ref, p_buf, p_sem,
):
    project_cross(io, ncross_ref, memory_ref, (w0_ref, w1_ref), q_ref, k_ref, v_ref)
    attend_docs(meta, True, None, None, [(q_ref, k_ref, v_ref, mixed_ref)], p_ref, p_buf, p_sem)


def cross_second(
    meta, io, second_ref, ncross_ref, memory_ref, norms_ref, w0_ref, w1_ref, w2_ref, w3_ref,
    mixed_first_ref,
    q_ref, k_ref, v_ref, mixed_ref, p_ref, third_ref, nffn_ref, p_buf, p_sem,
):
    project_cross(io, ncross_ref, memory_ref, (w2_ref, w3_ref), q_ref, k_ref, v_ref)
    attend_docs(meta, True, None, None, [(q_ref, k_ref, v_ref, mixed_ref)], p_ref, p_buf, p_sem)
    io.send(mixed_ref)
    io.wait("late")
    out_first = jnp.concatenate([w_out(w0_ref), w_out(w1_ref)], axis=0)
    out_second = jnp.concatenate([w_out(w2_ref), w_out(w3_ref)], axis=0)

    def tile(i, carry):
        rows = rows_of(i)
        branch = dot(mixed_first_ref[rows, :], out_first) + dot(mixed_ref[rows, :], out_second)
        third = second_ref[rows, :] + branch
        third_ref[rows, :] = third
        io.send(third_ref, rows)
        nffn_ref[rows, :] = layer_norm(third, norms_ref[6:7], norms_ref[7:8])
        io.send(nffn_ref, rows)
        return carry

    lax.fori_loop(0, TILES, tile, 0)


def ffn_both(
    meta, io, third_ref, nffn_ref, cot_ref, norms_ref, u0_ref, u1_ref, u2_ref, u3_ref,
    w0_ref, w1_ref, w2_ref, w3_ref,
    placed_ref, out_ref, g3_ref, g3_low_ref, gln_ref, own_ref, other_ref, hidden_ref, before_ref, sums_ref,
):
    sums_ref[...] = jnp.zeros_like(sums_ref)
    in_refs = (u0_ref, u1_ref, u2_ref, u3_ref)
    w_refs = (w0_ref, w1_ref, w2_ref, w3_ref)

    def tile(i, carry):
        rows = rows_of(i)
        io.wait_rows(i)
        nffn = nffn_ref[rows, :]
        cot = cot_ref[rows, :]
        outs = []
        grads = []

        def phases(g, c, group):
            w_in = in_refs[g]
            w_out_rows = w_refs[g]
            cols = slice(256 * c, 256 * c + 256)

            def enter():
                return dot(nffn, w_in[:, cols]), dot_nt(cot, w_out_rows[cols, :])

            def bend(state):
                def piece(x, grad_hidden):
                    square = x * x
                    argument = x * (gelu_root + (gelu_root * gelu_cube) * square)
                    half = 0.5 + 0.5 * jnp.tanh(argument.astype(bf16))
                    x = x.astype(bf16)
                    square = square.astype(bf16)
                    value = x * half
                    rise = 2.0 * gelu_root + (6.0 * gelu_root * gelu_cube) * square
                    slope = half + value * (1.0 - half) * rise
                    return value, grad_hidden.astype(bf16) * slope

                hidden, grad_before = by_pieces(piece, 32, 0, *state)
                if g < 2:
                    place = slice(512 * g + 256 * c, 512 * g + 256 * c + 256)
                    hidden_ref[rows, place] = hidden
                    before_ref[rows, place] = grad_before
                group[c] = hidden, grad_before

            def leave(_):
                if c == 1:
                    outs.append(dot(lanes([group[0][0], group[1][0]]), w_out_rows[...]))

            def leave_back(_):
                if c == 1:
                    grads.append(dot_nt(lanes([group[0][1], group[1][1]]), w_in[...]))

            return enter, bend, leave, leave_back

        interleave(by_halves(4, phases))
        third = third_ref[rows, :]
        result = (third + ((outs[0] + outs[1]) + (outs[2] + outs[3]))).astype(bf16)
        out_ref[rows, :] = result
        placed_ref[rows, :] = result
        grad_normed = (grads[0] + grads[1]) + (grads[2] + grads[3])
        grad_norm = norm_backward(third, norms_ref[6:7], grad_normed, sums_ref, 0)
        g3 = cot.astype(f32) + grad_norm
        g3_ref[rows, :] = g3
        g3_low_ref[rows, :] = g3.astype(bf16)
        for ref in (out_ref, placed_ref, g3_ref, g3_low_ref):
            io.send(ref, rows)
        return carry

    lax.fori_loop(0, TILES, tile, 0)
    add_sums(sums_ref, gln_ref, 2)
    part = dot_tn(nffn_ref[...], before_ref[...])
    own_ref[0:512, :] = part[:, 0:512].astype(bf16)
    other_ref[0:512, :] = part[:, 512:1024].astype(bf16)
    io.send(own_ref, pl.ds(0, 512))
    io.send(other_ref, pl.ds(0, 512))
    part = dot_tn(hidden_ref[...], cot_ref[...])
    own_ref[512:1024, :] = part[0:512].astype(bf16)
    other_ref[512:1024, :] = part[512:1024].astype(bf16)
    io.send(own_ref, pl.ds(512, 512))
    io.send(other_ref, pl.ds(512, 512))


def back_start(io, g_ref, mixed_ref, w_refs, dm_ref, dq_ref, dk_ref, dv_ref):
    out_rows = jnp.concatenate([w_out(w) for w in w_refs], axis=0)

    def tile(i, carry):
        rows = rows_of(i)
        io.wait_rows(i)
        dm_ref[rows, :] = dot_nt(g_ref[rows, :], out_rows).astype(bf16)
        zeros = jnp.zeros((TILE, 256), f32)
        dq_ref[rows, :] = zeros
        dk_ref[rows, :] = zeros
        dv_ref[rows, :] = zeros
        return carry

    lax.fori_loop(0, TILES, tile, 0)


def attention_back_first(
    cross, meta, io, g_ref, nq_ref, nkv_ref, rank_row_ref, limit_ref, w0_ref, w1_ref,
    q_ref, k_ref, v_ref, mixed_ref, p_ref,
    dq_ref, dk_ref, dv_ref, own_ref, other_ref,
    rank_ref, dm_ref, dqs_ref, dks_ref, dvs_ref, p_buf, p_sem,
):
    load = (p_ref, p_buf, p_sem)
    start_load(meta, cross, load)
    if not cross:
        spread_ranks(rank_row_ref, rank_ref)
    back_start(io, g_ref, mixed_ref, (w0_ref, w1_ref), dm_ref, dqs_ref, dks_ref, dvs_ref)

    io.wait("soon")
    attend_docs_back(
        meta, cross, None if cross else rank_ref, limit_ref, q_ref, k_ref, v_ref, mixed_ref,
        dm_ref, dqs_ref, dks_ref, dvs_ref, load,
    )

    dq_ref[...] = dqs_ref[...].astype(bf16)
    dk_ref[...] = dks_ref[...].astype(bf16)
    dv_ref[...] = dvs_ref[...].astype(bf16)
    for ref in (dq_ref, dk_ref, dv_ref):
        io.send(ref)
    io.wait("late")
    nq = nq_ref[...]
    nkv = nkv_ref[...]
    kv = dot_tn(nkv, lanes([dk_ref[...], dv_ref[...]]))
    for n, part in enumerate((dot_tn(nq, dq_ref[...]), kv[:, 0:256], kv[:, 256:512])):
        own_ref[:, 128 * n : 128 * n + 128] = part[:, :128].astype(bf16)
        other_ref[:, 128 * n : 128 * n + 128] = part[:, 128:].astype(bf16)
    part = dot_tn(mixed_ref[...], g_ref[...])
    for j in range(4):
        rows = slice(128 * j, 128 * j + 128)
        own_ref[rows, 384:512] = part[:128, rows].astype(bf16)
        other_ref[rows, 384:512] = part[128:, rows].astype(bf16)


def back_second_docs(
    cross, meta, io, g_ref, rank_row_ref, limit_ref, w_refs, q_ref, k_ref, v_ref, mixed_ref, p_ref,
    rank_ref, dm_ref, dqs_ref, dks_ref, dvs_ref, p_buf, p_sem,
):
    load = (p_ref, p_buf, p_sem)
    start_load(meta, cross, load)
    if not cross:
        spread_ranks(rank_row_ref, rank_ref)
    back_start(io, g_ref, mixed_ref, w_refs, dm_ref, dqs_ref, dks_ref, dvs_ref)

    io.wait("soon")
    attend_docs_back(
        meta, cross, None if cross else rank_ref, limit_ref, q_ref, k_ref, v_ref, mixed_ref,
        dm_ref, dqs_ref, dks_ref, dvs_ref, load,
    )


def stream_grads(rows, first, second, firsts, seconds):
    dq, dk, dv = first
    dq2, dk2, dv2 = (ref[rows, :].astype(bf16) for ref in second)
    w0, w1 = firsts
    w2, w3 = seconds
    grad_q = dot_nt(dq[rows, :], lanes([w_query(w0), w_query(w1)])) + dot_nt(
        dq2, lanes([w_query(w2), w_query(w3)])
    )
    kv = lanes([dk[rows, :], dv[rows, :]])
    kv2 = lanes([dk2, dv2])
    grad_kv = dot_nt(kv, lanes([w_key(w0), w_key(w1), w_value(w0), w_value(w1)])) + dot_nt(
        kv2, lanes([w_key(w2), w_key(w3), w_value(w2), w_value(w3)])
    )
    return grad_q, grad_kv


def cross_back_second(
    meta, io, g_low_ref, g_ref, second_ref, norms_ref, w0_ref, w1_ref, w2_ref, w3_ref,
    dq_ref, dk_ref, dv_ref, q_ref, k_ref, v_ref, mixed_ref, p_ref,
    g2_ref, g2_low_ref, placed_ref, gmem_ref, gln_ref,
    dm_ref, dqs_ref, dks_ref, dvs_ref, p_buf, p_sem, sums_ref,
):
    back_second_docs(
        True, meta, io, g_low_ref, None, None, (w2_ref, w3_ref), q_ref, k_ref, v_ref, mixed_ref, p_ref,
        None, dm_ref, dqs_ref, dks_ref, dvs_ref, p_buf, p_sem,
    )

    io.wait("late")
    sums_ref[...] = jnp.zeros_like(sums_ref)

    def tile(i, carry):
        rows = rows_of(i)
        grad_q, grad_kv = stream_grads(
            rows,
            (dq_ref, dk_ref, dv_ref),
            (dqs_ref, dks_ref, dvs_ref),
            (w0_ref, w1_ref),
            (w2_ref, w3_ref),
        )
        low_kv = grad_kv.astype(bf16)
        gmem_ref[rows, :] = low_kv
        placed_ref[rows, :] = low_kv.astype(f32)
        io.send(gmem_ref, rows)
        io.send(placed_ref, rows)
        grad_norm = norm_backward(second_ref[rows, :], norms_ref[4:5], grad_q, sums_ref, 0)
        g2 = g_ref[rows, :] + grad_norm
        g2_ref[rows, :] = g2
        g2_low_ref[rows, :] = g2.astype(bf16)
        io.send(g2_ref, rows)
        io.send(g2_low_ref, rows)
        return carry

    lax.fori_loop(0, TILES, tile, 0)
    add_sums(sums_ref, gln_ref, 2)


def self_back_second(
    meta, io, g_low_ref, rank_row_ref, limit_ref, w2_ref, w3_ref,
    q_ref, k_ref, v_ref, mixed_ref, p_ref,
    dq_ref, dk_ref, dv_ref,
    rank_ref, dm_ref, dqs_ref, dks_ref, dvs_ref, p_buf, p_sem,
):
    back_second_docs(
        False, meta, io, g_low_ref, rank_row_ref, limit_ref, (w2_ref, w3_ref), q_ref, k_ref, v_ref,
        mixed_ref, p_ref, rank_ref, dm_ref, dqs_ref, dks_ref, dvs_ref, p_buf, p_sem,
    )
    dq_ref[...] = dqs_ref[...].astype(bf16)
    dk_ref[...] = dks_ref[...].astype(bf16)
    dv_ref[...] = dvs_ref[...].astype(bf16)


def self_back_finish(
    meta, io, g_ref, xq_ref, xc_ref, norms_ref, w0_ref, w1_ref, w2_ref, w3_ref,
    dq_ref, dk_ref, dv_ref, dq2_ref, dk2_ref, dv2_ref,
    placed_q_ref, placed_c_ref, gq_ref, gc_ref, gln_ref, sums_ref,
):
    sums_ref[...] = jnp.zeros_like(sums_ref)

    def tile(i, carry):
        rows = rows_of(i)
        io.wait_rows(i)
        grad_q, grad_kv = stream_grads(
            rows,
            (dq_ref, dk_ref, dv_ref),
            (dq2_ref, dk2_ref, dv2_ref),
            (w0_ref, w1_ref),
            (w2_ref, w3_ref),
        )
        grad_norm = norm_backward(xq_ref[rows, :], norms_ref[0:1], grad_q, sums_ref, 0)
        low_q = (g_ref[rows, :] + grad_norm).astype(bf16)
        gq_ref[rows, :] = low_q
        placed_q_ref[rows, :] = low_q.astype(f32)
        io.send(gq_ref, rows)
        io.send(placed_q_ref, rows)
        grad_norm = norm_backward(xc_ref[rows, :], norms_ref[2:3], grad_kv, sums_ref, 16)
        low_c = grad_norm.astype(bf16)
        gc_ref[rows, :] = low_c
        placed_c_ref[rows, :] = low_c.astype(f32)
        io.send(gc_ref, rows)
        io.send(placed_c_ref, rows)
        return carry

    lax.fori_loop(0, TILES, tile, 0)
    add_sums(sums_ref, gln_ref, 4)


def place_rows(meta, *refs):
    count = len(refs) // 3
    for n in range(count):
        refs[2 * count + n][...] = refs[n][...].astype(refs[2 * count + n].dtype)


GROUP = 8


def position(meta):
    r = meta[35]
    return lax.rem(r, 2), r // 2


def join(own, other, rows):
    return (own[rows, :].astype(f32) + other[rows, :].astype(f32)).astype(bf16)


def join_halves(meta, own, other, keep, send):
    y, _ = position(meta)
    size = keep.shape[0]
    keep[...] = join(own, other, rows_of(y, size))
    send[...] = join(own, other, rows_of(1 - y, size))


def join_chunks(meta, kept, arrived, keep, sends):
    _, z = position(meta)
    size = keep.shape[0]
    keep[...] = join(kept, arrived, rows_of(z, size))
    for s, (send, first) in enumerate(sends, 1):
        send[first : first + size, :] = join(kept, arrived, rows_of(z ^ s, size))


def add_up(kept, parts, first):
    size = kept.shape[0]
    total = kept[...].astype(f32)
    for part in parts:
        total = total + part[first : first + size, :].astype(f32)
    return total.astype(bf16)


def half_of(meta, total, parts, first, half):
    _, z = position(meta)
    size = total.shape[0]
    half[rows_of(z, size), :] = total[...]
    for s, part in enumerate(parts, 1):
        half[rows_of(z ^ s, size), :] = part[first : first + size, :]


def slot_1(meta, ffn_own, ffn_other, keep, send):
    join_halves(meta, ffn_own, ffn_other, keep, send)


def slot_2(
    meta, ffn_kept, ffn_arrived, cross_own, cross_other, ffn_keep, f1, f2, f3, keep, send
):
    join_chunks(meta, ffn_kept, ffn_arrived, ffn_keep, [(f1, 0), (f2, 0), (f3, 0)])
    join_halves(meta, cross_own, cross_other, keep, send)


def slot_3(
    meta, ffn_kept, f1, f2, f3, cross_kept, cross_arrived, self_own, self_other,
    ffn_total, cross_keep, m1, m2, m3, self_keep, self_send,
):
    join_halves(meta, self_own, self_other, self_keep, self_send)
    total = add_up(ffn_kept, (f1, f2, f3), 0)
    ffn_total[...] = total
    size = total.shape[0]
    join_chunks(meta, cross_kept, cross_arrived, cross_keep, [(m, size) for m in (m1, m2, m3)])
    for m in (m1, m2, m3):
        m[0:size, :] = total


def slot_4(
    meta, ffn_total, m1, m2, m3, cross_kept, self_kept, self_arrived,
    ffn_half, cross_total, self_keep, *sends,
):
    join_chunks(meta, self_kept, self_arrived, self_keep, [(send, 0) for send in sends])
    total = add_up(cross_kept, (m1, m2, m3), ffn_total.shape[0])
    cross_total[...] = total
    size = total.shape[0]
    for send in sends:
        send[size:, :] = total
    half_of(meta, ffn_total, (m1, m2, m3), 0, ffn_half)


def slot_5(meta, self_kept, cross_total, m1, m2, m3, gln_own, gln_other, send, cross_half):
    size = self_kept.shape[0]
    total = add_up(self_kept, (m1, m2, m3), 0)
    gln = gln_own[...] + gln_other[...]
    gln = jnp.concatenate([gln, jnp.zeros((8, D), f32)], axis=0).astype(bf16)
    for r in range(GROUP):
        send[r, 0:size, :] = total
        send[r, size : size + 16, :] = gln
    half_of(meta, cross_total, (m1, m2, m3), size, cross_half)


def unpack_attention(whole_ref, outs):
    for i in range(3):
        outs[i][...] = whole_ref[:, 128 * i : 128 * i + 128].astype(f32)
    for j in range(4):
        rows = slice(128 * j, 128 * j + 128)
        outs[3][:, rows] = whole_ref[rows, 384:512].astype(f32)


def unpack_early(meta, ffn_half, ffn_arrived, cross_half, cross_arrived, *refs):
    *outs, cross_whole, ffn_whole = refs
    y, _ = position(meta)
    cross_whole[rows_of(y, 256), :] = cross_half[...]
    cross_whole[rows_of(1 - y, 256), :] = cross_arrived[...]
    unpack_attention(cross_whole, outs[2:])
    ffn_whole[rows_of(y, 512), :] = ffn_half[...]
    ffn_whole[rows_of(1 - y, 512), :] = ffn_arrived[...]
    outs[0][...] = ffn_whole[0:512, :].astype(f32)
    outs[1][...] = ffn_whole[512:1024, :].astype(f32)


def unpack_late(meta, parts, *refs):
    *outs, gln, whole_ref = refs
    size = parts.shape[1] - 16
    total = parts[0, size : size + 16, :].astype(f32)
    for r in range(1, GROUP):
        total = total + parts[r, size : size + 16, :].astype(f32)
    gln[...] = total[0:8]
    for r in range(GROUP):
        first = size * (4 * (r % 2) + r // 2)
        whole_ref[first : first + size, :] = parts[r, 0:size, :]
    unpack_attention(whole_ref, outs)


def whole(shape):
    zeros = (0,) * len(shape)
    return pl.BlockSpec(shape, lambda d, meta: zeros)


def own_row(width):
    return pl.BlockSpec((SEQ, width), lambda d, meta: (meta[0], 0))


ANY = pl.BlockSpec(memory_space=pl.ANY)


def in_hbm(x):
    return pltpu.with_memory_space_constraint(x, pltpu.HBM)


probability_out = (pltpu.HBM((DOCS, 4, FAST_K, FAST_Q), bf16), None, ANY)
probability_scratch = [
    pltpu.VMEM((2, TOGETHER, 4, FAST_K, FAST_Q), bf16),
    pltpu.SemaphoreType.DMA((2,)),
]


class Copies:
    def __init__(self, meta):
        self.first = meta[0] * SEQ
        self.loads = {}
        self.tiles = []
        self.sends = []

    def load(self, stage, source, target, sems, own_row):
        if stage == "tiles":
            first = self.first if own_row else 0
            self.tiles.append((source, target, sems, first))
            return
        if own_row:
            source = source.at[pl.ds(pl.multiple_of(self.first, SEQ), SEQ)]
        copy = pltpu.make_async_copy(source, target, sems[0].at[sems[1], 0])
        self.loads.setdefault(stage, []).append(copy)

    def tile(self, entry, i):
        source, target, (sems, b), first = entry
        rows = pl.ds(pl.multiple_of(first + i * TILE, TILE), TILE)
        return pltpu.make_async_copy(source.at[rows], target.at[rows_of(i)], sems.at[b, i])

    def start(self):
        for copy in self.loads.get("now", []):
            copy.start()
        for i in range(TILES):
            for entry in self.tiles:
                self.tile(entry, i).start()
        for stage in ("soon", "late"):
            for copy in self.loads.get(stage, []):
                copy.start()

    def wait(self, stage):
        for copy in self.loads.pop(stage, []):
            copy.wait()

    def wait_rows(self, i):
        for entry in self.tiles:
            self.tile(entry, i).wait()

    def result(self, source, target, sem, own_row):
        self.sends.append([source, target, sem, own_row, False])

    def send(self, ref, rows=None):
        for entry in self.sends:
            source, target, sem, own_row, _ = entry
            if source is ref:
                entry[4] = True
                first = self.first if own_row else 0
                if rows is None:
                    size = source.shape[0]
                else:
                    source = source.at[rows]
                    first, size = first + rows.start, rows.size
                if rows is not None or own_row:
                    target = target.at[pl.ds(pl.multiple_of(first, size), size)]
                pltpu.make_async_copy(source, target, sem).start()

    def finish(self):
        for stage in list(self.loads):
            self.wait(stage)
        for source, _, _, _, started in self.sends:
            if not started:
                self.send(source)
        for source, target, sem, own_row, _ in self.sends:
            if own_row:
                target = target.at[pl.ds(pl.multiple_of(self.first, SEQ), SEQ)]
            pltpu.make_async_copy(source, target, sem).wait()


def out(shape, dtype, own_row=False):
    return (shape, dtype, own_row)


def call(kernel, name, operands, outs, scratch, flops, token=None):
    arrays = [operands[0][0]]
    in_specs, out_specs, out_shapes = [], [], []
    buffers = []
    loads = []
    for n, (x, how) in enumerate(operands[1:]):
        if isinstance(how, str):
            stage, _, row = how.partition("_")
            shape = ((SEQ,) + x.shape[1:]) if row else x.shape
            loads.append((n, stage, len(buffers), bool(row)))
            buffers.append(pltpu.VMEM(shape, x.dtype))
            arrays.append(in_hbm(x))
            in_specs.append(ANY)
        else:
            arrays.append(x)
            in_specs.append(how)
    results = []
    for n, (shape, dtype, how) in enumerate(outs):
        if isinstance(how, bool):
            results.append((n, len(buffers), how))
            buffers.append(pltpu.VMEM(shape, dtype))
            shape = ((2 * SEQ,) + shape[1:]) if how else shape
            out_shapes.append(pltpu.HBM(shape, dtype))
            out_specs.append(ANY)
        else:
            out_shapes.append(jax.ShapeDtypeStruct(shape, dtype) if dtype else shape)
            out_specs.append(how)
    n_in, n_out = len(in_specs), len(out_specs)
    if token is not None:
        arrays.append(token)
        in_specs.append(whole((8, 128)))
        out_specs.append(whole((8, 128)))
        out_shapes.append(jax.ShapeDtypeStruct((8, 128), f32))

    def body(meta, *refs):
        ins, refs = list(refs[:n_in]), refs[len(in_specs) - n_in + n_in :]
        results_out, refs = list(refs[:n_out]), refs[n_out:]
        if token is not None:
            token_out, refs = refs[0], refs[1:]
            token_out[...] = jnp.zeros_like(token_out)
        bufs, refs = refs[: len(buffers)], refs[len(buffers) :]
        rest = refs[: len(scratch)]
        copies = Copies(meta)
        if buffers:
            sems = refs[len(scratch)]
        for n, stage, b, row in loads:
            copies.load(stage, ins[n], bufs[b], (sems, b), row)
            ins[n] = bufs[b]
        for n, b, row in results:
            copies.result(bufs[b], results_out[n], sems.at[b, 0], row)
            results_out[n] = bufs[b]
        copies.start()
        copies.wait("now")
        if buffers:
            kernel(meta, copies, *ins, *results_out, *rest)
        else:
            kernel(meta, *ins, *results_out, *rest)
        copies.finish()

    moved = sum(x.size * x.dtype.itemsize for x in arrays[1:])
    sems = [pltpu.SemaphoreType.DMA((len(buffers), TILES))] if buffers else []
    return pl.pallas_call(
        body,
        name=name,
        grid_spec=pltpu.PrefetchScalarGridSpec(
            num_scalar_prefetch=1,
            grid=(1,),
            in_specs=in_specs,
            out_specs=out_specs,
            scratch_shapes=buffers + scratch + sems,
        ),
        out_shape=out_shapes,
        compiler_params=pltpu.CompilerParams(
            dimension_semantics=("arbitrary",), vmem_limit_bytes=50 * 1024 * 1024
        ),
        cost_estimate=pl.CostEstimate(
            flops=int(flops), bytes_accessed=int(moved), transcendentals=0
        ),
    )(*arrays)


def simple(kernel, name, meta, operands, outs, scratch=()):
    return pl.pallas_call(
        kernel,
        name=name,
        grid_spec=pltpu.PrefetchScalarGridSpec(
            num_scalar_prefetch=1,
            grid=(1,),
            in_specs=[whole(x.shape) for x in operands],
            out_specs=[whole(shape) for shape, _ in outs],
            scratch_shapes=scratch,
        ),
        out_shape=[jax.ShapeDtypeStruct(shape, dtype) for shape, dtype in outs],
        compiler_params=pltpu.CompilerParams(vmem_limit_bytes=16 * 1024 * 1024),
    )(meta, *operands)


def full(x):
    return (x, whole(x.shape))


def shards(
    query_stream,
    content_stream,
    memory,
    segment_ids,
    source_segments,
    context_rank,
    context_limit,
    padding,
    ln_query_gain,
    ln_query_bias,
    ln_content_gain,
    ln_content_bias,
    self_query,
    self_key,
    self_value,
    self_out,
    ln_cross_gain,
    ln_cross_bias,
    cross_query,
    cross_key,
    cross_value,
    cross_out,
    ln_ffn_gain,
    ln_ffn_bias,
    ffn_in,
    ffn_out,
    cotangent,
):
    core = lax.axis_index("heads") % 2

    def to_core(x):
        return lax.ppermute(x, "heads", [(h, h ^ 1) for h in range(4)])

    hold = lambda *xs: lax.optimization_barrier(xs)

    def to_chip(x):
        return lax.ppermute(x, "heads", [(h, h ^ 2) for h in range(4)])

    row = pl.BlockSpec((1, 8, 128), lambda d, core: (core[0], 0, 0))

    def token_row(x):
        return (in_hbm(x.reshape(2, 8, 128)), row)

    def fixed(x):
        zeros = (0,) * x.ndim
        return (in_hbm(x), pl.BlockSpec(x.shape, lambda d, core: zeros))

    prepared = [
        ((36,), jnp.int32, pl.BlockSpec(memory_space=pltpu.SMEM)),
        ((1, SEQ), f32, whole((1, SEQ))),
        ((1, SEQ), f32, whole((1, SEQ))),
        ((8, D), f32, whole((8, D))),
        ((D, D), bf16, whole((D, D))),
        ((D, D), bf16, whole((D, D))),
    ]
    gains = (
        ln_query_gain,
        ln_query_bias,
        ln_content_gain,
        ln_content_bias,
        ln_cross_gain,
        ln_cross_bias,
        ln_ffn_gain,
        ln_ffn_bias,
    )
    weights = (self_query, self_key, self_value, self_out)
    weights += (cross_query, cross_key, cross_value, cross_out)
    tokens = (segment_ids, source_segments, context_rank, context_limit, padding)
    meta, rank, limit, norms, ws0, wc0 = call(
        prepare,
        "prepare",
        [(jnp.stack([core, lax.axis_index("rows") % GROUP]).astype(jnp.int32), None)]
        + [token_row(x) for x in tokens]
        + [fixed(x.reshape(1, D)) for x in gains]
        + [fixed(x) for x in weights],
        prepared,
        [],
        0,
    )

    ws1 = to_core(ws0)
    ws2 = to_chip(ws0)
    wc1 = to_core(wc0)
    u0, v0 = ffn_in, ffn_out
    meta_in = (meta, None)

    heads_out = [out((SEQ, 256), bf16)] * 4

    def stream_out(dtype, own_row=False):
        return out((SEQ, D), dtype, own_row)

    def now(*xs):
        return [(x, "now") for x in xs]

    def soon(*xs):
        return [(x, "soon") for x in xs]

    def late(*xs):
        return [(x, "late") for x in xs]

    def small(*xs):
        return [(x, whole(x.shape)) for x in xs]

    limits = pltpu.VMEM((SEQ, 128), f32)
    pair_flops = 2 * SEQ * D * 768 + 2 * 2 * 4 * DOCS * FAST_Q * FAST_K * 256

    nq, nc, *first, token = call(
        self_first,
        "self_first",
        [meta_in, (query_stream, "tiles_row"), (content_stream, "tiles_row")]
        + small(rank, limit, norms)
        + now(ws0, ws1),
        [stream_out(bf16), stream_out(bf16)] + heads_out + [probability_out],
        [limits] + probability_scratch,
        pair_flops,
        jnp.zeros((8, 128), f32),
    )
    ws2, wc0, token = hold(ws2, wc0, token)
    ws3 = to_core(ws2)
    wc2 = to_chip(wc0)
    *second_heads, second, ncross, token = call(
        self_second,
        "self_second",
        [meta_in, (query_stream, "late_row")]
        + [(nq, "tiles"), (nc, "tiles")]
        + small(rank, limit, norms)
        + late(ws0, ws1)
        + now(ws2, ws3)
        + late(first[3]),
        heads_out + [probability_out, stream_out(f32), stream_out(bf16)],
        [limits] + probability_scratch,
        pair_flops + 2 * SEQ * D * D,
        token,
    )
    wc2, u0, v0, token = hold(wc2, u0, v0, token)
    wc3 = to_core(wc2)
    u2 = to_chip(u0)
    u1 = to_core(u0)
    *cross_heads, token = call(
        cross_first,
        "cross_first",
        [meta_in, (ncross, "tiles"), (memory, "tiles_row")] + now(wc0, wc1),
        heads_out + [probability_out],
        probability_scratch,
        pair_flops,
        token,
    )
    wc3, u2, v0, token = hold(wc3, u2, v0, token)
    u3 = to_core(u2)
    v2 = to_chip(v0)
    v1 = to_core(v0)
    *cross_heads_second, third, nffn, token = call(
        cross_second,
        "cross_second",
        [meta_in]
        + late(second)
        + [(ncross, "tiles"), (memory, "tiles_row")]
        + small(norms)
        + late(wc0, wc1)
        + now(wc2, wc3)
        + late(cross_heads[3]),
        heads_out + [probability_out, stream_out(f32), stream_out(bf16)],
        probability_scratch,
        pair_flops + 2 * SEQ * D * D,
        token,
    )
    u3, v2, token = hold(u3, v2, token)
    v3 = to_core(v2)
    grads_ln = ((8, D), f32, whole((8, D)))
    placed_output, output, g3, g3_low, gln_ffn, ffn_own, ffn_other, token = call(
        ffn_both,
        "ffn_both",
        [meta_in]
        + [(third, "tiles"), (nffn, "tiles"), (cotangent, "tiles_row")]
        + small(norms)
        + now(u0, u1, u2, u3, v0, v1, v2, v3),
        [
            stream_out(bf16, True),
            stream_out(bf16),
            stream_out(f32),
            stream_out(bf16),
            grads_ln,
            out((1024, D), bf16),
            out((1024, D), bf16),
        ],
        [pltpu.VMEM((SEQ, 1024), bf16), pltpu.VMEM((SEQ, 1024), bf16), pltpu.VMEM((16, D), f32)],
        12 * SEQ * D * 2048,
        token,
    )

    def both_rows(placed_own, others, name):
        count = len(others)
        size = 128
        one = pl.BlockSpec((size, D), lambda i, meta: (i, 0))
        block = pl.BlockSpec((size, D), lambda i, meta: (SEQ // 128 * (1 - meta[0]) + i, 0))
        return pl.pallas_call(
            place_rows,
            name=name,
            grid_spec=pltpu.PrefetchScalarGridSpec(
                num_scalar_prefetch=1,
                grid=(SEQ // 128,),
                in_specs=[one] * count + [pl.BlockSpec(memory_space=pl.ANY)] * count,
                out_specs=[block] * count,
            ),
            out_shape=[jax.ShapeDtypeStruct(x.shape, x.dtype) for x in placed_own],
            input_output_aliases={1 + count + n: n for n in range(count)},
        )(meta, *others, *placed_own)

    row_count = lax.axis_size("rows")
    assert row_count % GROUP == 0

    def along_rows(x, s):
        return lax.ppermute(x, "rows", [(r, r ^ s) for r in range(row_count)])

    def to_y(x):
        return along_rows(x, 1)

    def to_z(sends):
        return [along_rows(x, 2 * s) for s, x in enumerate(sends, 1)]

    def rows_out(*sizes):
        return [((n, D), bf16) for n in sizes]

    ffn_other = to_core(ffn_other)
    output_other = to_core(output)

    back_scratch = [pltpu.VMEM((SEQ, 256), bf16)] + [pltpu.VMEM((SEQ, 256), f32)] * 3
    back_scratch += probability_scratch
    pair_out = out((SEQ, 256), bf16)
    packed_outs = [out((D, D), bf16), out((D, D), bf16)]
    back_flops = 2 * SEQ * D * 256 + 4 * 2 * 4 * DOCS * FAST_Q * FAST_K * 256

    def head_inputs(natural, p):
        return soon(*natural) + [(in_hbm(p), ANY)]

    *cross_grads, cross_own, cross_other, token = call(
        functools.partial(attention_back_first, True),
        "cross_back_first",
        [meta_in]
        + [(g3_low, "tiles")]
        + late(ncross)
        + [(memory, "late_row")]
        + small(rank, limit)
        + now(wc0, wc1)
        + head_inputs(cross_heads[0:4], cross_heads[4]),
        [pair_out] * 3 + packed_outs,
        [limits] + back_scratch,
        back_flops + 2 * SEQ * D * 1024,
        token,
    )
    ffn_other, output_other, token = hold(ffn_other, output_other, token)
    ffn_keep, ffn_send = simple(slot_1, "slot_1", meta, [in_hbm(ffn_own), ffn_other], rows_out(512, 512))
    ffn_send, token = hold(ffn_send, token)
    ffn_arrived = to_y(ffn_send)
    cross_other = to_core(cross_other)
    g2, g2_low, placed_mem, grad_mem, gln_cross, token = call(
        cross_back_second,
        "cross_back_second",
        [meta_in]
        + [(g3_low, "tiles")]
        + late(g3, second)
        + small(norms)
        + late(wc0, wc1)
        + now(wc2, wc3)
        + late(*cross_grads)
        + head_inputs(cross_heads_second[0:4], cross_heads_second[4]),
        [stream_out(f32), stream_out(bf16), stream_out(f32, True), stream_out(bf16), grads_ln],
        back_scratch + [pltpu.VMEM((16, D), f32)],
        back_flops + 2 * SEQ * D * 1536,
        token,
    )
    ffn_arrived, cross_other, token = hold(ffn_arrived, cross_other, token)
    ffn_keep, *sends, cross_keep, cross_send = simple(
        slot_2,
        "slot_2",
        meta,
        [ffn_keep, ffn_arrived, in_hbm(cross_own), cross_other],
        rows_out(128, 128, 128, 128, 256, 256),
    )
    ffn_keep, cross_send, token = hold(ffn_keep, cross_send, token)
    ffn_parts = to_z(sends)
    cross_arrived = to_y(cross_send)

    *self_grads, self_own, self_other, token = call(
        functools.partial(attention_back_first, False),
        "self_back_first",
        [meta_in]
        + [(g2_low, "tiles")]
        + late(nq, nc)
        + small(rank, limit)
        + now(ws0, ws1)
        + head_inputs(first[0:4], first[4]),
        [pair_out] * 3 + packed_outs,
        [limits] + back_scratch,
        back_flops + 2 * SEQ * D * 1024,
        token,
    )
    *ffn_parts, cross_arrived, self_other, token = hold(
        *ffn_parts, cross_arrived, self_other, token
    )
    self_other = to_core(self_other)
    ffn_total, cross_keep, *sends, self_keep, self_send = simple(
        slot_3,
        "slot_3",
        meta,
        [ffn_keep, *ffn_parts, cross_keep, cross_arrived, in_hbm(self_own), self_other],
        rows_out(128, 64, 192, 192, 192, 256, 256),
    )
    ffn_total, self_send, grad_mem, token = hold(ffn_total, self_send, grad_mem, token)
    mem_other = to_core(grad_mem)
    self_arrived = to_y(self_send)
    messages = to_z(sends)
    *self_grads_second, token = call(
        self_back_second,
        "self_back_second",
        [meta_in, (g2_low, "tiles")]
        + small(rank, limit)
        + now(ws2, ws3)
        + head_inputs(second_heads[0:4], second_heads[4]),
        [pair_out] * 3,
        [limits] + back_scratch,
        back_flops,
        token,
    )
    output_other, mem_other, token = hold(output_other, mem_other, token)
    out_both, grad_mem_both = both_rows(
        [placed_output, placed_mem], [output_other, mem_other], "place_early"
    )
    *messages, self_arrived, out_both, token = hold(*messages, self_arrived, out_both, token)
    ffn_half, cross_total, self_keep, *sends = simple(
        slot_4,
        "slot_4",
        meta,
        [ffn_total, *messages, cross_keep, self_keep, self_arrived],
        rows_out(512, 64, 64, 128, 128, 128),
    )
    cross_total, ffn_half, token = hold(cross_total, ffn_half, token)
    messages = to_z(sends)
    ffn_arrived = to_y(ffn_half)
    placed_q, placed_c, gq, gc, gln_self, token = call(
        self_back_finish,
        "self_back_finish",
        [meta_in, (g2, "tiles"), (query_stream, "tiles_row"), (content_stream, "tiles_row")]
        + small(norms)
        + now(ws0, ws1, ws2, ws3)
        + [(x, "tiles") for x in self_grads + self_grads_second],
        [stream_out(f32, True), stream_out(f32, True), stream_out(bf16), stream_out(bf16), grads_ln],
        [pltpu.VMEM((32, D), f32)],
        2 * SEQ * D * 1536,
        token,
    )
    gln = jnp.concatenate([gln_self[0:4], gln_cross[0:2], gln_ffn[0:2]], axis=0)
    *messages, ffn_arrived, gln = hold(*messages, ffn_arrived, gln)
    last_send, cross_half = simple(
        slot_5,
        "slot_5",
        meta,
        [self_keep, cross_total, *messages, gln, to_core(gln)],
        [((GROUP, 80, D), bf16), ((256, D), bf16)],
    )
    groups = None
    if row_count > GROUP:
        groups = [list(range(r, r + GROUP)) for r in range(0, row_count, GROUP)]
    last_parts = lax.all_to_all(last_send, "rows", 0, 0, axis_index_groups=groups)
    cross_arrived = to_y(cross_half)

    def over_groups(totals):
        if row_count == GROUP:
            return totals
        groups = [list(range(r, row_count, GROUP)) for r in range(GROUP)]
        return lax.psum(totals, "rows", axis_index_groups=groups)

    gq, gc, last_send = hold(gq, gc, last_send)
    gq_both, gc_both = both_rows([placed_q, placed_c], [to_core(gq), to_core(gc)], "place_late")

    cross_arrived, gq_both = hold(cross_arrived, gq_both)
    attention_outs = [((512, 128), f32)] * 3 + [((128, 512), f32)]
    grad_ffn_in, grad_ffn_out, *grad_cross_parts = simple(
        unpack_early,
        "unpack_early",
        meta,
        [ffn_half, ffn_arrived, cross_half, cross_arrived],
        [((D, D), f32)] * 2 + attention_outs,
        [pltpu.VMEM((D, D), bf16), pltpu.VMEM((2 * D, D), bf16)],
    )
    *grad_self_parts, gln = simple(
        unpack_late,
        "unpack_late",
        meta,
        [last_parts],
        attention_outs + [((8, D), f32)],
        [pltpu.VMEM((D, D), bf16)],
    )
    grad_ffn_in, grad_ffn_out, grad_cross_parts, grad_self_parts, gln = over_groups(
        (grad_ffn_in, grad_ffn_out, grad_cross_parts, grad_self_parts, gln)
    )
    return (
        out_both,
        gq_both,
        gc_both,
        grad_mem_both,
        gln[0],
        gln[1],
        gln[2],
        gln[3],
        *grad_self_parts,
        gln[4],
        gln[5],
        *grad_cross_parts,
        gln[6],
        gln[7],
        grad_ffn_in,
        grad_ffn_out,
    )


def solution(mesh):
    assert mesh.shape["heads"] == 4
    row_spec = P("rows", None)
    flat = P("rows")
    by_column = P(None, "heads")
    by_row = P("heads", None)
    attention = (by_column, by_column, by_column, by_row)
    in_specs = (
        (row_spec,) * 3
        + (flat,) * 5
        + (P(),) * 4
        + attention
        + (P(),) * 2
        + attention
        + (P(),) * 2
        + (by_column, by_row, row_spec)
    )
    out_specs = (
        (row_spec,) * 4
        + (P(),) * 4
        + attention
        + (P(),) * 2
        + attention
        + (P(),) * 2
        + (by_column, by_row)
    )
    return jax.shard_map(shards, mesh=mesh, in_specs=in_specs, out_specs=out_specs, check_vma=False)
```

```python
import functools

import jax
import jax.numpy as jnp
from jax import lax
from jax.experimental import pallas as pl
from jax.experimental.pallas import tpu as pltpu
from jax.sharding import PartitionSpec as P

HEAD_DIM = 64
SEQ = 1024
DOCS = 8
D = 512
TILE = 256
TILES = SEQ // TILE
FAST_Q = 256
FAST_K = 208
LONG_Q = 128
LONG_K = 640

norm_eps = 1e-05
masked_score = -1e30
hidden_rank = 1e6
gelu_root = 0.7978845608028654
gelu_cube = 0.044715

f32 = jnp.float32
bf16 = jnp.bfloat16


def dot(a, b):
    return lax.dot_general(a, b, (((1,), (0,)), ((), ())), preferred_element_type=f32)


def dot_nt(a, b):
    return lax.dot_general(a, b, (((1,), (1,)), ((), ())), preferred_element_type=f32)


def dot_tn(a, b):
    return lax.dot_general(a, b, (((0,), (0,)), ((), ())), preferred_element_type=f32)


def lanes(parts):
    return jnp.concatenate(parts, axis=1)


NORM_ROWS = 32


def layer_norm(values, gain, shift):
    def piece(part):
        part = part.astype(f32)
        centre = part - jnp.mean(part, axis=-1, keepdims=True)
        spread = jnp.mean(centre * centre, axis=-1, keepdims=True)
        return (centre * lax.rsqrt(spread + norm_eps) * gain + shift).astype(bf16)

    return by_pieces(piece, NORM_ROWS, 0, values)


def eight_rows(values):
    return sum(values[8 * i : 8 * i + 8] for i in range(1, values.shape[0] // 8)) + values[0:8]


def norm_backward(values, gain, grad, sums_ref, first):
    sums = []

    def piece(part, grad_part):
        part = part.astype(f32)
        centre = part - jnp.mean(part, axis=-1, keepdims=True)
        spread = jnp.mean(centre * centre, axis=-1, keepdims=True)
        scale = lax.rsqrt(spread + norm_eps)
        xhat = centre * scale
        eg = grad_part * gain
        mean_eg = jnp.mean(eg, axis=-1, keepdims=True)
        mean_egx = jnp.mean(eg * xhat, axis=-1, keepdims=True)
        sums.append((eight_rows(grad_part * xhat), eight_rows(grad_part)))
        return scale * (eg - mean_eg - xhat * mean_egx)

    result = by_pieces(piece, NORM_ROWS, 0, values, grad)
    for n, parts in enumerate(zip(*sums)):
        sums_ref[first + 8 * n : first + 8 * n + 8, :] += sum(parts[1:], parts[0])
    return result


def add_sums(sums_ref, gln_ref, count):
    gln_ref[...] = jnp.zeros_like(gln_ref)
    for n in range(count):
        gln_ref[n : n + 1, :] = jnp.sum(sums_ref[8 * n : 8 * n + 8, :], axis=0, keepdims=True)


def by_pieces(work, size, axis, *arrays):
    count = arrays[0].shape[axis] // size
    pieces = []
    for i in range(count):
        cut = (slice(size * i, size * i + size),)
        cut = cut if axis == 0 else (slice(None),) + cut
        pieces.append(work(*[x[cut] for x in arrays]))
    if not isinstance(pieces[0], tuple):
        return jnp.concatenate(pieces, axis=axis)
    return tuple(jnp.concatenate(parts, axis=axis) for parts in zip(*pieces))


def rows_of(i, size=TILE):
    return pl.ds(pl.multiple_of(i * size, size), size)


def w_query(ref):
    return ref[:, 0:128]


def w_key(ref):
    return ref[:, 128:256]


def w_value(ref):
    return ref[:, 256:384]


def w_out(ref):
    return lanes([ref[128 * j : 128 * j + 128, 384:512] for j in range(4)])


def half_masks():
    place = lax.broadcasted_iota(jnp.int32, (1, 128), 1)
    low = jnp.where(place < HEAD_DIM, 1.0, 0.0).astype(f32)
    return (low.astype(bf16), (1.0 - low).astype(bf16))


def doc_bounds(meta, d, source):
    base = 17 if source else 1
    return meta[base + d], meta[base + 8 + d]


def window_of(first, limit):
    return pl.multiple_of(jnp.minimum((first // 16) * 16, limit), 16)


def key_bias(ks, ke, k0, width):
    place = k0 + lax.broadcasted_iota(jnp.int32, (width, 128), 0)
    return jnp.where((place >= ks) & (place < ke), 0.0, masked_score)


def make_bias(rank_ref, limit_ref, ks, ke, q0, k0, span, width):
    if rank_ref is None:
        return lanes([key_bias(ks, ke, k0, width)] * (span // 128))
    place = k0 + lax.broadcasted_iota(jnp.int32, (width, 128), 0)
    ranks = rank_ref[pl.ds(k0, width), :]
    ranks = jnp.where((place < ks + 2) & (ranks < hidden_rank), -1.0, ranks)
    ranks = jnp.where((place >= ks) & (place < ke), ranks, hidden_rank)
    limits = jnp.broadcast_to(limit_ref[...], (8, SEQ))
    limits = pltpu.roll(limits, lax.rem(SEQ - q0, SEQ), 1)[0:1, 0:span]
    row = k0 + lax.broadcasted_iota(jnp.int32, (width, span), 0)
    column = q0 + lax.broadcasted_iota(jnp.int32, (width, span), 1)
    seen = (lanes([ranks] * (span // 128)) < limits) & (row != column)
    return jnp.where(seen, 0.0, masked_score)


TOGETHER = 4
STEPS = DOCS // TOGETHER


LAG = 2


def interleave(items):
    items = [list(phases) for phases in items]
    depth = max(len(phases) for phases in items)
    results = [None] * len(items)
    for tick in range(len(items) + LAG * (depth - 1)):
        for phase in range(depth):
            n = tick - LAG * phase
            if 0 <= n < len(items) and phase < len(items[n]):
                run = items[n][phase]
                results[n] = run() if phase == 0 else run(results[n])
    return results


def by_halves(pairs, phases):
    shared = [{} for _ in range(pairs)]
    return [phases(n, a, shared[n]) for n in range(pairs) for a in range(2)]


def is_fast(meta, cross):
    return meta[34 if cross else 33] == 1


def both_heads(x, masks):
    return jnp.concatenate([x * masks[0], x * masks[1]], axis=0)


def pair_scores(queries, keys, masks):
    return dot_nt(both_heads(keys, masks), queries)


def raised(scores, bias):
    def piece(part, bias_part):
        part = part + bias_part
        return jnp.exp((part - jnp.max(part, axis=0, keepdims=True)).astype(bf16))

    return by_pieces(piece, 128, 1, scores, bias)


def weighted_values(values, parts):
    width = values.shape[1]
    mixed = []
    shares = []
    for a, part in enumerate(parts):
        rows = jnp.concatenate([values[64 * a : 64 * a + 64], jnp.ones((16, width), bf16)], axis=0)
        sums = dot(rows, part)
        share = 1.0 / sums[64:65]
        mixed.append(sums[:64] * share)
        shares.append(part * share.astype(bf16))
    return jnp.concatenate(mixed, axis=0).astype(bf16), shares


def pair_gradient(rows, parts):
    across = jnp.transpose(rows)
    halves = [dot(across[64 * a : 64 * a + 64], part) for a, part in enumerate(parts)]
    return jnp.transpose((jnp.concatenate(halves, axis=0) * HEAD_DIM**-0.5).astype(bf16))


def for_docs(meta, cross, run, before, after):
    @pl.when(is_fast(meta, cross))
    def _():
        def step(i, carry):
            slot = lax.rem(i, 2)
            before(i, slot)
            items = []
            for place in range(TOGETHER):
                d = TOGETHER * i + place
                ts, te = doc_bounds(meta, d, False)
                ks, ke = doc_bounds(meta, d, cross)
                q0 = window_of(ts, SEQ - FAST_Q)
                k0 = window_of(ks, SEQ - FAST_K)
                items += run(d, slot, place, q0, k0, FAST_Q, FAST_K, ts, te, ks, ke, True)
            interleave(items)
            after(i, slot)
            return carry

        lax.fori_loop(0, STEPS, step, 0)

    @pl.when(jnp.logical_not(is_fast(meta, cross)))
    def _():
        def doc(d, carry):
            ts, te = doc_bounds(meta, d, False)
            ks, ke = doc_bounds(meta, d, cross)
            base = (ts // 16) * 16
            k0 = window_of(ks, SEQ - LONG_K)

            def chunk(i, carry):
                lower = base + i * LONG_Q
                q0 = pl.multiple_of(jnp.minimum(lower, SEQ - LONG_Q), 16)
                low = jnp.maximum(ts, lower)
                high = jnp.minimum(te, lower + LONG_Q)
                interleave(run(d, None, None, q0, k0, LONG_Q, LONG_K, low, high, ks, ke, False))
                return carry

            return lax.fori_loop(0, (te - base + LONG_Q - 1) // LONG_Q, chunk, carry)

        lax.fori_loop(0, DOCS, doc, 0)


def attend_docs(meta, cross, rank_ref, limit_ref, halves, p_ref, p_buf, p_sem):
    pairs = 2 * len(halves)
    masks = half_masks()

    def save(i, slot):
        return pltpu.make_async_copy(p_buf.at[slot], p_ref.at[pl.ds(TOGETHER * i, TOGETHER)], p_sem.at[slot])

    def before(i, slot):
        @pl.when(i >= 2)
        def _():
            save(i - 2, slot).wait()

    def after(i, slot):
        save(i, slot).start()

    def run(d, slot, place, q0, k0, span, width, low, high, ks, ke, fast):
        bias = make_bias(rank_ref, limit_ref, ks, ke, q0, k0, span, width)
        row = q0 + lax.broadcasted_iota(jnp.int32, (span, 128), 0)
        inside = (row >= low) & (row < high)

        def phases(n):
            q_ref, k_ref, v_ref, mixed_ref = halves[n // 2]
            cols = slice(128 * (n % 2), 128 * (n % 2) + 128)

            def score():
                return pair_scores(q_ref[pl.ds(q0, span), cols], k_ref[pl.ds(k0, width), cols], masks)

            def weigh(scores):
                return [raised(scores[width * a : width * a + width], bias) for a in range(2)]

            def mix(parts):
                values = jnp.transpose(v_ref[pl.ds(k0, width), cols])
                mixed, parts = weighted_values(values, parts)
                if fast:
                    for a in range(2):
                        p_buf[slot, place, 2 * n + a] = parts[a]
                mixed = jnp.transpose(mixed).astype(f32)
                old = mixed_ref[pl.ds(q0, span), cols].astype(f32)
                mixed_ref[pl.ds(q0, span), cols] = jnp.where(inside, mixed, old).astype(bf16)

            return score, weigh, mix

        return [phases(n) for n in range(pairs)]

    for_docs(meta, cross, run, before, after)

    @pl.when(is_fast(meta, cross))
    def _():
        for i in range(STEPS - 2, STEPS):
            save(i, i % 2).wait()


def load_step(load, i, slot):
    p_ref, p_buf, p_sem = load
    return pltpu.make_async_copy(p_ref.at[pl.ds(TOGETHER * i, TOGETHER)], p_buf.at[slot], p_sem.at[slot])


def start_load(meta, cross, load):
    @pl.when(is_fast(meta, cross))
    def _():
        load_step(load, 0, 0).start()


def attend_docs_back(
    meta, cross, rank_ref, limit_ref, q_ref, k_ref, v_ref, mixed_ref, dm_ref,
    dq_ref, dk_ref, dv_ref, load,
):
    pairs = q_ref.shape[1] // 128
    masks = half_masks()
    p_buf = load[1]

    def before(i, slot):
        @pl.when(i + 1 < STEPS)
        def _():
            load_step(load, i + 1, 1 - slot).start()

        load_step(load, i, slot).wait()

    def after(i, slot):
        pass

    def run(d, slot, place, q0, k0, span, width, low, high, ks, ke, fast):
        row = q0 + lax.broadcasted_iota(jnp.int32, (span, 128), 0)
        inside = jnp.where((row >= low) & (row < high), 1.0, 0.0).astype(bf16)
        ones = jnp.ones((width, 128), bf16)
        if not fast:
            bias = make_bias(rank_ref, limit_ref, ks, ke, q0, k0, span, width)

        def phases(n):
            cols = slice(128 * n, 128 * n + 128)

            def differ():
                values = v_ref[pl.ds(k0, width), cols]
                mixed = mixed_ref[pl.ds(q0, span), cols]
                grad = dm_ref[pl.ds(q0, span), cols] * inside
                left = lanes([grad, -(grad * mixed)])
                right = both_heads(lanes([values, ones]), [lanes([m, m]) for m in masks])
                return grad, dot_nt(right, left)

            def slope(state):
                grad, delta = state
                if fast:
                    parts = [p_buf[slot, place, 2 * n + a] for a in range(2)]
                else:
                    queries = q_ref[pl.ds(q0, span), cols]
                    keys = k_ref[pl.ds(k0, width), cols]
                    scores = pair_scores(queries, keys, masks)
                    parts = [raised(scores[width * a : width * a + width], bias) for a in range(2)]
                    parts = weighted_values(jnp.transpose(v_ref[pl.ds(k0, width), cols]), parts)[1]
                slopes = [
                    by_pieces(
                        lambda part, change: part * change.astype(bf16),
                        16,
                        0,
                        parts[a],
                        delta[width * a : width * a + width],
                    )
                    for a in range(2)
                ]
                return grad, parts, slopes

            def spread(state):
                grad, parts, slopes = state
                queries = q_ref[pl.ds(q0, span), cols]
                dk = dv = None
                for a in range(2):
                    dk_a = dot(slopes[a], queries * masks[a])
                    dv_a = dot(parts[a], grad * masks[a])
                    dk = dk_a if dk is None else dk + dk_a
                    dv = dv_a if dv is None else dv + dv_a
                dq = pair_gradient(k_ref[pl.ds(k0, width), cols], slopes)
                dq_ref[pl.ds(q0, span), cols] += dq.astype(f32)
                dk_ref[pl.ds(k0, width), cols] += dk
                dv_ref[pl.ds(k0, width), cols] += dv

            return differ, slope, spread

        return [phases(n) for n in range(pairs)]

    for_docs(meta, cross, run, before, after)


def spread_ranks(rank_row_ref, rank_ref):
    rank_ref[...] = jnp.transpose(jnp.broadcast_to(rank_row_ref[...], (128, SEQ)))


def prepare(
    core, seg_ref, src_ref, rank_ref, limit_ref, pad_ref,
    n0, n1, n2, n3, n4, n5, n6, n7, sq, sk, sv, so, cq, ck, cv, co,
    meta_ref, ranks_ref, limits_ref, norms_ref, ws_ref, wc_ref,
):
    meta_ref[0] = core[0]
    meta_ref[35] = core[1]
    for base, ref in ((1, seg_ref), (17, src_ref)):
        ids = ref[0]
        meta_ref[base] = 0
        meta_ref[base + 15] = SEQ
        for d in range(1, DOCS):
            cut = jnp.sum(jnp.where(ids < d, 1.0, 0.0)).astype(jnp.int32)
            meta_ref[base + d] = cut
            meta_ref[base + 7 + d] = cut
    for place, base in ((33, 1), (34, 17)):
        fast = jnp.int32(1)
        for d in range(DOCS):
            q0 = window_of(meta_ref[1 + d], SEQ - FAST_Q)
            k0 = window_of(meta_ref[base + d], SEQ - FAST_K)
            fits = (meta_ref[9 + d] - q0 <= FAST_Q) & (meta_ref[base + 8 + d] - k0 <= FAST_K)
            fast = fast & fits.astype(jnp.int32)
        meta_ref[place] = fast
    ranks = jnp.where(pad_ref[0] != 0, hidden_rank, rank_ref[0].astype(f32))
    limits = limit_ref[0].astype(f32)
    for i in range(8):
        ranks_ref[0:1, 128 * i : 128 * i + 128] = ranks[i : i + 1]
        limits_ref[0:1, 128 * i : 128 * i + 128] = limits[i : i + 1]
    for i, ref in enumerate((n0, n1, n2, n3, n4, n5, n6, n7)):
        norms_ref[i : i + 1, :] = ref[...]
    for to, parts, out in ((ws_ref, (sq, sk, sv), so), (wc_ref, (cq, ck, cv), co)):
        for i, part in enumerate(parts):
            to[:, 128 * i : 128 * i + 128] = part[...]
        for j in range(4):
            to[128 * j : 128 * j + 128, 384:512] = out[:, 128 * j : 128 * j + 128]


def self_first(
    meta, io, xq_ref, xc_ref, rank_row_ref, limit_ref, norms_ref, w0_ref, w1_ref,
    nq_ref, nc_ref, q_ref, k_ref, v_ref, mixed_ref, p_ref, rank_ref, p_buf, p_sem,
):

    spread_ranks(rank_row_ref, rank_ref)
    wq = lanes([w_query(w0_ref), w_query(w1_ref)])
    wkv = lanes([w_key(w0_ref), w_key(w1_ref), w_value(w0_ref), w_value(w1_ref)])

    def tile(i, carry):
        rows = rows_of(i)
        io.wait_rows(i)
        nq = layer_norm(xq_ref[rows, :], norms_ref[0:1], norms_ref[1:2])
        nc = layer_norm(xc_ref[rows, :], norms_ref[2:3], norms_ref[3:4])
        nq_ref[rows, :] = nq
        nc_ref[rows, :] = nc
        q_ref[rows, :] = (dot(nq, wq) * (HEAD_DIM**-0.5)).astype(bf16)
        kv = dot(nc, wkv).astype(bf16)
        k_ref[rows, :] = kv[:, :256]
        v_ref[rows, :] = kv[:, 256:]
        return carry

    lax.fori_loop(0, TILES, tile, 0)

    for ref in (nq_ref, nc_ref, q_ref, k_ref, v_ref):
        io.send(ref)
    attend_docs(meta, False, rank_ref, limit_ref, [(q_ref, k_ref, v_ref, mixed_ref)], p_ref, p_buf, p_sem)


def self_second(
    meta, io, xq_ref, nq_ref, nc_ref, rank_row_ref, limit_ref, norms_ref, w0_ref, w1_ref, w2_ref, w3_ref,
    mixed_first_ref,
    q_ref, k_ref, v_ref, mixed_ref, p_ref, second_ref, ncross_ref, rank_ref, p_buf, p_sem,
):

    spread_ranks(rank_row_ref, rank_ref)
    wq = lanes([w_query(w2_ref), w_query(w3_ref)])
    wkv = lanes([w_key(w2_ref), w_key(w3_ref), w_value(w2_ref), w_value(w3_ref)])

    def tile(i, carry):
        rows = rows_of(i)
        io.wait_rows(i)
        q_ref[rows, :] = (dot(nq_ref[rows, :], wq) * (HEAD_DIM**-0.5)).astype(bf16)
        kv = dot(nc_ref[rows, :], wkv).astype(bf16)
        k_ref[rows, :] = kv[:, :256]
        v_ref[rows, :] = kv[:, 256:]
        return carry

    lax.fori_loop(0, TILES, tile, 0)

    for ref in (q_ref, k_ref, v_ref):
        io.send(ref)
    attend_docs(meta, False, rank_ref, limit_ref, [(q_ref, k_ref, v_ref, mixed_ref)], p_ref, p_buf, p_sem)

    io.send(mixed_ref)
    io.wait("late")
    out_first = jnp.concatenate([w_out(w0_ref), w_out(w1_ref)], axis=0)
    out_second = jnp.concatenate([w_out(w2_ref), w_out(w3_ref)], axis=0)

    def tile(i, carry):
        rows = rows_of(i)
        branch = dot(mixed_first_ref[rows, :], out_first) + dot(mixed_ref[rows, :], out_second)
        second = xq_ref[rows, :].astype(f32) + branch
        second_ref[rows, :] = second
        io.send(second_ref, rows)
        ncross_ref[rows, :] = layer_norm(second, norms_ref[4:5], norms_ref[5:6])
        io.send(ncross_ref, rows)
        return carry

    lax.fori_loop(0, TILES, tile, 0)


def project_cross(io, ncross_ref, memory_ref, weights, q_ref, k_ref, v_ref):
    wq = lanes([w_query(w) for w in weights])
    wkv = lanes([w_key(w) for w in weights] + [w_value(w) for w in weights])

    def tile(i, carry):
        rows = rows_of(i)
        io.wait_rows(i)
        q_ref[rows, :] = (dot(ncross_ref[rows, :], wq) * (HEAD_DIM**-0.5)).astype(bf16)
        kv = dot(memory_ref[rows, :], wkv).astype(bf16)
        k_ref[rows, :] = kv[:, :256]
        v_ref[rows, :] = kv[:, 256:]
        return carry

    lax.fori_loop(0, TILES, tile, 0)
    for ref in (q_ref, k_ref, v_ref):
        io.send(ref)


def cross_first(
    meta, io, ncross_ref, memory_ref, w0_ref, w1_ref,
    q_ref, k_ref, v_ref, mixed_ref, p_ref, p_buf, p_sem,
):
    project_cross(io, ncross_ref, memory_ref, (w0_ref, w1_ref), q_ref, k_ref, v_ref)
    attend_docs(meta, True, None, None, [(q_ref, k_ref, v_ref, mixed_ref)], p_ref, p_buf, p_sem)


def cross_second(
    meta, io, second_ref, ncross_ref, memory_ref, norms_ref, w0_ref, w1_ref, w2_ref, w3_ref,
    mixed_first_ref,
    q_ref, k_ref, v_ref, mixed_ref, p_ref, third_ref, nffn_ref, p_buf, p_sem,
):
    project_cross(io, ncross_ref, memory_ref, (w2_ref, w3_ref), q_ref, k_ref, v_ref)
    attend_docs(meta, True, None, None, [(q_ref, k_ref, v_ref, mixed_ref)], p_ref, p_buf, p_sem)
    io.send(mixed_ref)
    io.wait("late")
    out_first = jnp.concatenate([w_out(w0_ref), w_out(w1_ref)], axis=0)
    out_second = jnp.concatenate([w_out(w2_ref), w_out(w3_ref)], axis=0)

    def tile(i, carry):
        rows = rows_of(i)
        branch = dot(mixed_first_ref[rows, :], out_first) + dot(mixed_ref[rows, :], out_second)
        third = second_ref[rows, :] + branch
        third_ref[rows, :] = third
        io.send(third_ref, rows)
        nffn_ref[rows, :] = layer_norm(third, norms_ref[6:7], norms_ref[7:8])
        io.send(nffn_ref, rows)
        return carry

    lax.fori_loop(0, TILES, tile, 0)


def ffn_both(
    meta, io, third_ref, nffn_ref, cot_ref, norms_ref, u0_ref, u1_ref, u2_ref, u3_ref,
    w0_ref, w1_ref, w2_ref, w3_ref,
    placed_ref, out_ref, g3_ref, g3_low_ref, gln_ref, own_ref, other_ref, hidden_ref, before_ref, sums_ref,
):
    sums_ref[...] = jnp.zeros_like(sums_ref)
    in_refs = (u0_ref, u1_ref, u2_ref, u3_ref)
    w_refs = (w0_ref, w1_ref, w2_ref, w3_ref)

    def tile(i, carry):
        rows = rows_of(i)
        io.wait_rows(i)
        nffn = nffn_ref[rows, :]
        cot = cot_ref[rows, :]
        outs = []
        grads = []

        def phases(g, c, group):
            w_in = in_refs[g]
            w_out_rows = w_refs[g]
            cols = slice(256 * c, 256 * c + 256)

            def enter():
                return dot(nffn, w_in[:, cols]), dot_nt(cot, w_out_rows[cols, :])

            def bend(state):
                def piece(x, grad_hidden):
                    square = x * x
                    argument = x * (gelu_root + (gelu_root * gelu_cube) * square)
                    half = 0.5 + 0.5 * jnp.tanh(argument.astype(bf16))
                    x = x.astype(bf16)
                    square = square.astype(bf16)
                    value = x * half
                    rise = 2.0 * gelu_root + (6.0 * gelu_root * gelu_cube) * square
                    slope = half + value * (1.0 - half) * rise
                    return value, grad_hidden.astype(bf16) * slope

                hidden, grad_before = by_pieces(piece, 32, 0, *state)
                if g < 2:
                    place = slice(512 * g + 256 * c, 512 * g + 256 * c + 256)
                    hidden_ref[rows, place] = hidden
                    before_ref[rows, place] = grad_before
                group[c] = hidden, grad_before

            def leave(_):
                if c == 1:
                    outs.append(dot(lanes([group[0][0], group[1][0]]), w_out_rows[...]))

            def leave_back(_):
                if c == 1:
                    grads.append(dot_nt(lanes([group[0][1], group[1][1]]), w_in[...]))

            return enter, bend, leave, leave_back

        interleave(by_halves(4, phases))
        third = third_ref[rows, :]
        result = (third + ((outs[0] + outs[1]) + (outs[2] + outs[3]))).astype(bf16)
        out_ref[rows, :] = result
        placed_ref[rows, :] = result
        grad_normed = (grads[0] + grads[1]) + (grads[2] + grads[3])
        grad_norm = norm_backward(third, norms_ref[6:7], grad_normed, sums_ref, 0)
        g3 = cot.astype(f32) + grad_norm
        g3_ref[rows, :] = g3
        g3_low_ref[rows, :] = g3.astype(bf16)
        for ref in (out_ref, placed_ref, g3_ref, g3_low_ref):
            io.send(ref, rows)
        return carry

    lax.fori_loop(0, TILES, tile, 0)
    add_sums(sums_ref, gln_ref, 2)
    part = dot_tn(nffn_ref[...], before_ref[...])
    own_ref[0:512, :] = part[:, 0:512].astype(bf16)
    other_ref[0:512, :] = part[:, 512:1024].astype(bf16)
    io.send(own_ref, pl.ds(0, 512))
    io.send(other_ref, pl.ds(0, 512))
    part = dot_tn(hidden_ref[...], cot_ref[...])
    own_ref[512:1024, :] = part[0:512].astype(bf16)
    other_ref[512:1024, :] = part[512:1024].astype(bf16)
    io.send(own_ref, pl.ds(512, 512))
    io.send(other_ref, pl.ds(512, 512))


def back_start(io, g_ref, mixed_ref, w_refs, dm_ref, dq_ref, dk_ref, dv_ref):
    out_rows = jnp.concatenate([w_out(w) for w in w_refs], axis=0)

    def tile(i, carry):
        rows = rows_of(i)
        io.wait_rows(i)
        dm_ref[rows, :] = dot_nt(g_ref[rows, :], out_rows).astype(bf16)
        zeros = jnp.zeros((TILE, 256), f32)
        dq_ref[rows, :] = zeros
        dk_ref[rows, :] = zeros
        dv_ref[rows, :] = zeros
        return carry

    lax.fori_loop(0, TILES, tile, 0)


def attention_back_first(
    cross, meta, io, g_ref, nq_ref, nkv_ref, rank_row_ref, limit_ref, w0_ref, w1_ref,
    q_ref, k_ref, v_ref, mixed_ref, p_ref,
    dq_ref, dk_ref, dv_ref, own_ref, other_ref,
    rank_ref, dm_ref, dqs_ref, dks_ref, dvs_ref, p_buf, p_sem,
):
    load = (p_ref, p_buf, p_sem)
    start_load(meta, cross, load)
    if not cross:
        spread_ranks(rank_row_ref, rank_ref)
    back_start(io, g_ref, mixed_ref, (w0_ref, w1_ref), dm_ref, dqs_ref, dks_ref, dvs_ref)

    io.wait("soon")
    attend_docs_back(
        meta, cross, None if cross else rank_ref, limit_ref, q_ref, k_ref, v_ref, mixed_ref,
        dm_ref, dqs_ref, dks_ref, dvs_ref, load,
    )

    dq_ref[...] = dqs_ref[...].astype(bf16)
    dk_ref[...] = dks_ref[...].astype(bf16)
    dv_ref[...] = dvs_ref[...].astype(bf16)
    for ref in (dq_ref, dk_ref, dv_ref):
        io.send(ref)
    io.wait("late")
    nq = nq_ref[...]
    nkv = nkv_ref[...]
    kv = dot_tn(nkv, lanes([dk_ref[...], dv_ref[...]]))
    for n, part in enumerate((dot_tn(nq, dq_ref[...]), kv[:, 0:256], kv[:, 256:512])):
        own_ref[:, 128 * n : 128 * n + 128] = part[:, :128].astype(bf16)
        other_ref[:, 128 * n : 128 * n + 128] = part[:, 128:].astype(bf16)
    part = dot_tn(mixed_ref[...], g_ref[...])
    for j in range(4):
        rows = slice(128 * j, 128 * j + 128)
        own_ref[rows, 384:512] = part[:128, rows].astype(bf16)
        other_ref[rows, 384:512] = part[128:, rows].astype(bf16)


def back_second_docs(
    cross, meta, io, g_ref, rank_row_ref, limit_ref, w_refs, q_ref, k_ref, v_ref, mixed_ref, p_ref,
    rank_ref, dm_ref, dqs_ref, dks_ref, dvs_ref, p_buf, p_sem,
):
    load = (p_ref, p_buf, p_sem)
    start_load(meta, cross, load)
    if not cross:
        spread_ranks(rank_row_ref, rank_ref)
    back_start(io, g_ref, mixed_ref, w_refs, dm_ref, dqs_ref, dks_ref, dvs_ref)

    io.wait("soon")
    attend_docs_back(
        meta, cross, None if cross else rank_ref, limit_ref, q_ref, k_ref, v_ref, mixed_ref,
        dm_ref, dqs_ref, dks_ref, dvs_ref, load,
    )


def stream_grads(rows, first, second, firsts, seconds):
    dq, dk, dv = first
    dq2, dk2, dv2 = (ref[rows, :].astype(bf16) for ref in second)
    w0, w1 = firsts
    w2, w3 = seconds
    grad_q = dot_nt(dq[rows, :], lanes([w_query(w0), w_query(w1)])) + dot_nt(
        dq2, lanes([w_query(w2), w_query(w3)])
    )
    kv = lanes([dk[rows, :], dv[rows, :]])
    kv2 = lanes([dk2, dv2])
    grad_kv = dot_nt(kv, lanes([w_key(w0), w_key(w1), w_value(w0), w_value(w1)])) + dot_nt(
        kv2, lanes([w_key(w2), w_key(w3), w_value(w2), w_value(w3)])
    )
    return grad_q, grad_kv


def cross_back_second(
    meta, io, g_low_ref, g_ref, second_ref, norms_ref, w0_ref, w1_ref, w2_ref, w3_ref,
    dq_ref, dk_ref, dv_ref, q_ref, k_ref, v_ref, mixed_ref, p_ref,
    g2_ref, g2_low_ref, placed_ref, gmem_ref, gln_ref,
    dm_ref, dqs_ref, dks_ref, dvs_ref, p_buf, p_sem, sums_ref,
):
    back_second_docs(
        True, meta, io, g_low_ref, None, None, (w2_ref, w3_ref), q_ref, k_ref, v_ref, mixed_ref, p_ref,
        None, dm_ref, dqs_ref, dks_ref, dvs_ref, p_buf, p_sem,
    )

    io.wait("late")
    sums_ref[...] = jnp.zeros_like(sums_ref)

    def tile(i, carry):
        rows = rows_of(i)
        grad_q, grad_kv = stream_grads(
            rows,
            (dq_ref, dk_ref, dv_ref),
            (dqs_ref, dks_ref, dvs_ref),
            (w0_ref, w1_ref),
            (w2_ref, w3_ref),
        )
        low_kv = grad_kv.astype(bf16)
        gmem_ref[rows, :] = low_kv
        placed_ref[rows, :] = low_kv.astype(f32)
        io.send(gmem_ref, rows)
        io.send(placed_ref, rows)
        grad_norm = norm_backward(second_ref[rows, :], norms_ref[4:5], grad_q, sums_ref, 0)
        g2 = g_ref[rows, :] + grad_norm
        g2_ref[rows, :] = g2
        g2_low_ref[rows, :] = g2.astype(bf16)
        io.send(g2_ref, rows)
        io.send(g2_low_ref, rows)
        return carry

    lax.fori_loop(0, TILES, tile, 0)
    add_sums(sums_ref, gln_ref, 2)


def self_back_second(
    meta, io, g_low_ref, rank_row_ref, limit_ref, w2_ref, w3_ref,
    q_ref, k_ref, v_ref, mixed_ref, p_ref,
    dq_ref, dk_ref, dv_ref,
    rank_ref, dm_ref, dqs_ref, dks_ref, dvs_ref, p_buf, p_sem,
):
    back_second_docs(
        False, meta, io, g_low_ref, rank_row_ref, limit_ref, (w2_ref, w3_ref), q_ref, k_ref, v_ref,
        mixed_ref, p_ref, rank_ref, dm_ref, dqs_ref, dks_ref, dvs_ref, p_buf, p_sem,
    )
    dq_ref[...] = dqs_ref[...].astype(bf16)
    dk_ref[...] = dks_ref[...].astype(bf16)
    dv_ref[...] = dvs_ref[...].astype(bf16)


def self_back_finish(
    meta, io, g_ref, xq_ref, xc_ref, norms_ref, w0_ref, w1_ref, w2_ref, w3_ref,
    dq_ref, dk_ref, dv_ref, dq2_ref, dk2_ref, dv2_ref,
    placed_q_ref, placed_c_ref, gq_ref, gc_ref, gln_ref, sums_ref,
):
    sums_ref[...] = jnp.zeros_like(sums_ref)

    def tile(i, carry):
        rows = rows_of(i)
        io.wait_rows(i)
        grad_q, grad_kv = stream_grads(
            rows,
            (dq_ref, dk_ref, dv_ref),
            (dq2_ref, dk2_ref, dv2_ref),
            (w0_ref, w1_ref),
            (w2_ref, w3_ref),
        )
        grad_norm = norm_backward(xq_ref[rows, :], norms_ref[0:1], grad_q, sums_ref, 0)
        low_q = (g_ref[rows, :] + grad_norm).astype(bf16)
        gq_ref[rows, :] = low_q
        placed_q_ref[rows, :] = low_q.astype(f32)
        io.send(gq_ref, rows)
        io.send(placed_q_ref, rows)
        grad_norm = norm_backward(xc_ref[rows, :], norms_ref[2:3], grad_kv, sums_ref, 16)
        low_c = grad_norm.astype(bf16)
        gc_ref[rows, :] = low_c
        placed_c_ref[rows, :] = low_c.astype(f32)
        io.send(gc_ref, rows)
        io.send(placed_c_ref, rows)
        return carry

    lax.fori_loop(0, TILES, tile, 0)
    add_sums(sums_ref, gln_ref, 4)


def place_rows(meta, *refs):
    count = len(refs) // 3
    for n in range(count):
        refs[2 * count + n][...] = refs[n][...].astype(refs[2 * count + n].dtype)


GROUP = 8


def position(meta):
    r = meta[35]
    return lax.rem(r, 2), r // 2


def join(own, other, rows):
    return (own[rows, :].astype(f32) + other[rows, :].astype(f32)).astype(bf16)


def join_halves(meta, own, other, keep, send, first, size):
    y, _ = position(meta)
    keep[first : first + size, :] = join(own, other, rows_of(y, size))
    send[first : first + size, :] = join(own, other, rows_of(1 - y, size))


def join_chunks(meta, kept, arrived, keep, sends, offset, first, size):
    _, z = position(meta)
    for s, target in enumerate((keep, *sends)):
        rows = pl.ds(pl.multiple_of(offset + (z ^ s) * size, size), size)
        target[first : first + size, :] = join(kept, arrived, rows)


def add_up(kept, parts):
    total = kept[...].astype(f32)
    for part in parts:
        total = total + part[...].astype(f32)
    return total.astype(bf16)


def slot_1(meta, ffn_own, ffn_other, cross_own, cross_other, keep, send):
    join_halves(meta, ffn_own, ffn_other, keep, send, 0, 512)
    join_halves(meta, cross_own, cross_other, keep, send, 512, 256)


def slot_2(meta, kept, arrived, keep, *sends):
    join_chunks(meta, kept, arrived, keep, sends, 0, 0, 128)
    join_chunks(meta, kept, arrived, keep, sends, 512, 128, 64)


def slot_3(meta, kept, p1, p2, p3, self_own, self_other, total, keep, send):
    total[...] = add_up(kept, (p1, p2, p3))
    join_halves(meta, self_own, self_other, keep, send, 0, 256)


def slot_4(meta, total, p1, p2, p3, self_kept, self_arrived, half, keep, *sends):
    _, z = position(meta)
    join_chunks(meta, self_kept, self_arrived, keep, sends, 0, 0, 64)
    for s, part in enumerate((total, p1, p2, p3)):
        half[rows_of(z ^ s, 128), :] = part[0:128, :]
        half[pl.ds(pl.multiple_of(512 + (z ^ s) * 64, 64), 64), :] = part[128:192, :]


def slot_5(meta, kept, p1, p2, p3, gln_own, gln_other, send):
    total = add_up(kept, (p1, p2, p3))
    size = total.shape[0]
    gln = gln_own[...] + gln_other[...]
    gln = jnp.concatenate([gln, jnp.zeros((8, D), f32)], axis=0).astype(bf16)
    for r in range(GROUP):
        send[r, 0:size, :] = total
        send[r, size : size + 16, :] = gln


def unpack_attention(whole_ref, outs):
    for i in range(3):
        outs[i][...] = whole_ref[:, 128 * i : 128 * i + 128].astype(f32)
    for j in range(4):
        rows = slice(128 * j, 128 * j + 128)
        outs[3][:, rows] = whole_ref[rows, 384:512].astype(f32)


def unpack_early(meta, half, arrived, *refs):
    *outs, cross_whole, ffn_whole = refs
    y, _ = position(meta)
    for place, part in ((y, half), (1 - y, arrived)):
        ffn_whole[rows_of(place, 512), :] = part[0:512, :]
        cross_whole[rows_of(place, 256), :] = part[512:768, :]
    unpack_attention(cross_whole, outs[2:])
    outs[0][...] = ffn_whole[0:512, :].astype(f32)
    outs[1][...] = ffn_whole[512:1024, :].astype(f32)


def unpack_late(meta, parts, *refs):
    *outs, gln, whole_ref = refs
    size = parts.shape[1] - 16
    total = parts[0, size : size + 16, :].astype(f32)
    for r in range(1, GROUP):
        total = total + parts[r, size : size + 16, :].astype(f32)
    gln[...] = total[0:8]
    for r in range(GROUP):
        first = size * (4 * (r % 2) + r // 2)
        whole_ref[first : first + size, :] = parts[r, 0:size, :]
    unpack_attention(whole_ref, outs)


def whole(shape):
    zeros = (0,) * len(shape)
    return pl.BlockSpec(shape, lambda d, meta: zeros)


def own_row(width):
    return pl.BlockSpec((SEQ, width), lambda d, meta: (meta[0], 0))


ANY = pl.BlockSpec(memory_space=pl.ANY)


def in_hbm(x):
    return pltpu.with_memory_space_constraint(x, pltpu.HBM)


probability_out = (pltpu.HBM((DOCS, 4, FAST_K, FAST_Q), bf16), None, ANY)
probability_scratch = [
    pltpu.VMEM((2, TOGETHER, 4, FAST_K, FAST_Q), bf16),
    pltpu.SemaphoreType.DMA((2,)),
]


class Copies:
    def __init__(self, meta):
        self.first = meta[0] * SEQ
        self.loads = {}
        self.tiles = []
        self.sends = []

    def load(self, stage, source, target, sems, own_row):
        if stage == "tiles":
            first = self.first if own_row else 0
            self.tiles.append((source, target, sems, first))
            return
        if own_row:
            source = source.at[pl.ds(pl.multiple_of(self.first, SEQ), SEQ)]
        copy = pltpu.make_async_copy(source, target, sems[0].at[sems[1], 0])
        self.loads.setdefault(stage, []).append(copy)

    def tile(self, entry, i):
        source, target, (sems, b), first = entry
        rows = pl.ds(pl.multiple_of(first + i * TILE, TILE), TILE)
        return pltpu.make_async_copy(source.at[rows], target.at[rows_of(i)], sems.at[b, i])

    def start(self):
        for copy in self.loads.get("now", []):
            copy.start()
        for i in range(TILES):
            for entry in self.tiles:
                self.tile(entry, i).start()
        for stage in ("soon", "late"):
            for copy in self.loads.get(stage, []):
                copy.start()

    def wait(self, stage):
        for copy in self.loads.pop(stage, []):
            copy.wait()

    def wait_rows(self, i):
        for entry in self.tiles:
            self.tile(entry, i).wait()

    def result(self, source, target, sem, own_row):
        self.sends.append([source, target, sem, own_row, False])

    def send(self, ref, rows=None):
        for entry in self.sends:
            source, target, sem, own_row, _ = entry
            if source is ref:
                entry[4] = True
                first = self.first if own_row else 0
                if rows is None:
                    size = source.shape[0]
                else:
                    source = source.at[rows]
                    first, size = first + rows.start, rows.size
                if rows is not None or own_row:
                    target = target.at[pl.ds(pl.multiple_of(first, size), size)]
                pltpu.make_async_copy(source, target, sem).start()

    def finish(self):
        for stage in list(self.loads):
            self.wait(stage)
        for source, _, _, _, started in self.sends:
            if not started:
                self.send(source)
        for source, target, sem, own_row, _ in self.sends:
            if own_row:
                target = target.at[pl.ds(pl.multiple_of(self.first, SEQ), SEQ)]
            pltpu.make_async_copy(source, target, sem).wait()


def out(shape, dtype, own_row=False):
    return (shape, dtype, own_row)


def call(kernel, name, operands, outs, scratch, flops, token=None):
    arrays = [operands[0][0]]
    in_specs, out_specs, out_shapes = [], [], []
    buffers = []
    loads = []
    for n, (x, how) in enumerate(operands[1:]):
        if isinstance(how, str):
            stage, _, row = how.partition("_")
            shape = ((SEQ,) + x.shape[1:]) if row else x.shape
            loads.append((n, stage, len(buffers), bool(row)))
            buffers.append(pltpu.VMEM(shape, x.dtype))
            arrays.append(in_hbm(x))
            in_specs.append(ANY)
        else:
            arrays.append(x)
            in_specs.append(how)
    results = []
    for n, (shape, dtype, how) in enumerate(outs):
        if isinstance(how, bool):
            results.append((n, len(buffers), how))
            buffers.append(pltpu.VMEM(shape, dtype))
            shape = ((2 * SEQ,) + shape[1:]) if how else shape
            out_shapes.append(pltpu.HBM(shape, dtype))
            out_specs.append(ANY)
        else:
            out_shapes.append(jax.ShapeDtypeStruct(shape, dtype) if dtype else shape)
            out_specs.append(how)
    n_in, n_out = len(in_specs), len(out_specs)
    if token is not None:
        arrays.append(token)
        in_specs.append(whole((8, 128)))
        out_specs.append(whole((8, 128)))
        out_shapes.append(jax.ShapeDtypeStruct((8, 128), f32))

    def body(meta, *refs):
        ins, refs = list(refs[:n_in]), refs[len(in_specs) - n_in + n_in :]
        results_out, refs = list(refs[:n_out]), refs[n_out:]
        if token is not None:
            token_out, refs = refs[0], refs[1:]
            token_out[...] = jnp.zeros_like(token_out)
        bufs, refs = refs[: len(buffers)], refs[len(buffers) :]
        rest = refs[: len(scratch)]
        copies = Copies(meta)
        if buffers:
            sems = refs[len(scratch)]
        for n, stage, b, row in loads:
            copies.load(stage, ins[n], bufs[b], (sems, b), row)
            ins[n] = bufs[b]
        for n, b, row in results:
            copies.result(bufs[b], results_out[n], sems.at[b, 0], row)
            results_out[n] = bufs[b]
        copies.start()
        copies.wait("now")
        if buffers:
            kernel(meta, copies, *ins, *results_out, *rest)
        else:
            kernel(meta, *ins, *results_out, *rest)
        copies.finish()

    moved = sum(x.size * x.dtype.itemsize for x in arrays[1:])
    sems = [pltpu.SemaphoreType.DMA((len(buffers), TILES))] if buffers else []
    return pl.pallas_call(
        body,
        name=name,
        grid_spec=pltpu.PrefetchScalarGridSpec(
            num_scalar_prefetch=1,
            grid=(1,),
            in_specs=in_specs,
            out_specs=out_specs,
            scratch_shapes=buffers + scratch + sems,
        ),
        out_shape=out_shapes,
        compiler_params=pltpu.CompilerParams(
            dimension_semantics=("arbitrary",), vmem_limit_bytes=50 * 1024 * 1024
        ),
        cost_estimate=pl.CostEstimate(
            flops=int(flops), bytes_accessed=int(moved), transcendentals=0
        ),
    )(*arrays)


def simple(kernel, name, meta, operands, outs, scratch=()):
    return pl.pallas_call(
        kernel,
        name=name,
        grid_spec=pltpu.PrefetchScalarGridSpec(
            num_scalar_prefetch=1,
            grid=(1,),
            in_specs=[whole(x.shape) for x in operands],
            out_specs=[whole(shape) for shape, _ in outs],
            scratch_shapes=scratch,
        ),
        out_shape=[jax.ShapeDtypeStruct(shape, dtype) for shape, dtype in outs],
        compiler_params=pltpu.CompilerParams(vmem_limit_bytes=16 * 1024 * 1024),
    )(meta, *operands)


def full(x):
    return (x, whole(x.shape))


def shards(
    query_stream,
    content_stream,
    memory,
    segment_ids,
    source_segments,
    context_rank,
    context_limit,
    padding,
    ln_query_gain,
    ln_query_bias,
    ln_content_gain,
    ln_content_bias,
    self_query,
    self_key,
    self_value,
    self_out,
    ln_cross_gain,
    ln_cross_bias,
    cross_query,
    cross_key,
    cross_value,
    cross_out,
    ln_ffn_gain,
    ln_ffn_bias,
    ffn_in,
    ffn_out,
    cotangent,
):
    core = lax.axis_index("heads") % 2

    def to_core(x):
        return lax.ppermute(x, "heads", [(h, h ^ 1) for h in range(4)])

    hold = lambda *xs: lax.optimization_barrier(xs)

    def to_chip(x):
        return lax.ppermute(x, "heads", [(h, h ^ 2) for h in range(4)])

    row = pl.BlockSpec((1, 8, 128), lambda d, core: (core[0], 0, 0))

    def token_row(x):
        return (in_hbm(x.reshape(2, 8, 128)), row)

    def fixed(x):
        zeros = (0,) * x.ndim
        return (in_hbm(x), pl.BlockSpec(x.shape, lambda d, core: zeros))

    prepared = [
        ((36,), jnp.int32, pl.BlockSpec(memory_space=pltpu.SMEM)),
        ((1, SEQ), f32, whole((1, SEQ))),
        ((1, SEQ), f32, whole((1, SEQ))),
        ((8, D), f32, whole((8, D))),
        ((D, D), bf16, whole((D, D))),
        ((D, D), bf16, whole((D, D))),
    ]
    gains = (
        ln_query_gain,
        ln_query_bias,
        ln_content_gain,
        ln_content_bias,
        ln_cross_gain,
        ln_cross_bias,
        ln_ffn_gain,
        ln_ffn_bias,
    )
    weights = (self_query, self_key, self_value, self_out)
    weights += (cross_query, cross_key, cross_value, cross_out)
    tokens = (segment_ids, source_segments, context_rank, context_limit, padding)
    meta, rank, limit, norms, ws0, wc0 = call(
        prepare,
        "prepare",
        [(jnp.stack([core, lax.axis_index("rows") % GROUP]).astype(jnp.int32), None)]
        + [token_row(x) for x in tokens]
        + [fixed(x.reshape(1, D)) for x in gains]
        + [fixed(x) for x in weights],
        prepared,
        [],
        0,
    )

    ws1 = to_core(ws0)
    ws2 = to_chip(ws0)
    wc1 = to_core(wc0)
    u0, v0 = ffn_in, ffn_out
    meta_in = (meta, None)

    heads_out = [out((SEQ, 256), bf16)] * 4

    def stream_out(dtype, own_row=False):
        return out((SEQ, D), dtype, own_row)

    def now(*xs):
        return [(x, "now") for x in xs]

    def soon(*xs):
        return [(x, "soon") for x in xs]

    def late(*xs):
        return [(x, "late") for x in xs]

    def small(*xs):
        return [(x, whole(x.shape)) for x in xs]

    limits = pltpu.VMEM((SEQ, 128), f32)
    pair_flops = 2 * SEQ * D * 768 + 2 * 2 * 4 * DOCS * FAST_Q * FAST_K * 256

    nq, nc, *first, token = call(
        self_first,
        "self_first",
        [meta_in, (query_stream, "tiles_row"), (content_stream, "tiles_row")]
        + small(rank, limit, norms)
        + now(ws0, ws1),
        [stream_out(bf16), stream_out(bf16)] + heads_out + [probability_out],
        [limits] + probability_scratch,
        pair_flops,
        jnp.zeros((8, 128), f32),
    )
    ws2, wc0, token = hold(ws2, wc0, token)
    ws3 = to_core(ws2)
    wc2 = to_chip(wc0)
    *second_heads, second, ncross, token = call(
        self_second,
        "self_second",
        [meta_in, (query_stream, "late_row")]
        + [(nq, "tiles"), (nc, "tiles")]
        + small(rank, limit, norms)
        + late(ws0, ws1)
        + now(ws2, ws3)
        + late(first[3]),
        heads_out + [probability_out, stream_out(f32), stream_out(bf16)],
        [limits] + probability_scratch,
        pair_flops + 2 * SEQ * D * D,
        token,
    )
    wc2, u0, v0, token = hold(wc2, u0, v0, token)
    wc3 = to_core(wc2)
    u2 = to_chip(u0)
    u1 = to_core(u0)
    *cross_heads, token = call(
        cross_first,
        "cross_first",
        [meta_in, (ncross, "tiles"), (memory, "tiles_row")] + now(wc0, wc1),
        heads_out + [probability_out],
        probability_scratch,
        pair_flops,
        token,
    )
    wc3, u2, v0, token = hold(wc3, u2, v0, token)
    u3 = to_core(u2)
    v2 = to_chip(v0)
    v1 = to_core(v0)
    *cross_heads_second, third, nffn, token = call(
        cross_second,
        "cross_second",
        [meta_in]
        + late(second)
        + [(ncross, "tiles"), (memory, "tiles_row")]
        + small(norms)
        + late(wc0, wc1)
        + now(wc2, wc3)
        + late(cross_heads[3]),
        heads_out + [probability_out, stream_out(f32), stream_out(bf16)],
        probability_scratch,
        pair_flops + 2 * SEQ * D * D,
        token,
    )
    u3, v2, token = hold(u3, v2, token)
    v3 = to_core(v2)
    grads_ln = ((8, D), f32, whole((8, D)))
    placed_output, output, g3, g3_low, gln_ffn, ffn_own, ffn_other, token = call(
        ffn_both,
        "ffn_both",
        [meta_in]
        + [(third, "tiles"), (nffn, "tiles"), (cotangent, "tiles_row")]
        + small(norms)
        + now(u0, u1, u2, u3, v0, v1, v2, v3),
        [
            stream_out(bf16, True),
            stream_out(bf16),
            stream_out(f32),
            stream_out(bf16),
            grads_ln,
            out((1024, D), bf16),
            out((1024, D), bf16),
        ],
        [pltpu.VMEM((SEQ, 1024), bf16), pltpu.VMEM((SEQ, 1024), bf16), pltpu.VMEM((16, D), f32)],
        12 * SEQ * D * 2048,
        token,
    )

    def both_rows(placed_own, others, name):
        count = len(others)
        size = SEQ // 2
        one = pl.BlockSpec((size, D), lambda i, meta: (i, 0))
        block = pl.BlockSpec((size, D), lambda i, meta: (2 * (1 - meta[0]) + i, 0))
        return pl.pallas_call(
            place_rows,
            name=name,
            grid_spec=pltpu.PrefetchScalarGridSpec(
                num_scalar_prefetch=1,
                grid=(2,),
                in_specs=[one] * count + [pl.BlockSpec(memory_space=pl.ANY)] * count,
                out_specs=[block] * count,
            ),
            out_shape=[jax.ShapeDtypeStruct(x.shape, x.dtype) for x in placed_own],
            input_output_aliases={1 + count + n: n for n in range(count)},
        )(meta, *others, *placed_own)

    row_count = lax.axis_size("rows")
    assert row_count % GROUP == 0

    def along_rows(x, s):
        return lax.ppermute(x, "rows", [(r, r ^ s) for r in range(row_count)])

    def to_y(x):
        return along_rows(x, 1)

    def to_z(sends):
        return [along_rows(x, 2 * s) for s, x in enumerate(sends, 1)]

    def rows_out(*sizes):
        return [((n, D), bf16) for n in sizes]

    ffn_other = to_core(ffn_other)
    output_other = to_core(output)

    back_scratch = [pltpu.VMEM((SEQ, 256), bf16)] + [pltpu.VMEM((SEQ, 256), f32)] * 3
    back_scratch += probability_scratch
    pair_out = out((SEQ, 256), bf16)
    packed_outs = [out((D, D), bf16), out((D, D), bf16)]
    back_flops = 2 * SEQ * D * 256 + 4 * 2 * 4 * DOCS * FAST_Q * FAST_K * 256

    def head_inputs(natural, p):
        return soon(*natural) + [(in_hbm(p), ANY)]

    *cross_grads, cross_own, cross_other, token = call(
        functools.partial(attention_back_first, True),
        "cross_back_first",
        [meta_in]
        + [(g3_low, "tiles")]
        + late(ncross)
        + [(memory, "late_row")]
        + small(rank, limit)
        + now(wc0, wc1)
        + head_inputs(cross_heads[0:4], cross_heads[4]),
        [pair_out] * 3 + packed_outs,
        [limits] + back_scratch,
        back_flops + 2 * SEQ * D * 1024,
        token,
    )
    ffn_other, output_other, cross_other, token = hold(
        ffn_other, output_other, cross_other, token
    )
    kept, send = simple(
        slot_1,
        "slot_1",
        meta,
        [ffn_own, ffn_other, cross_own, to_core(cross_other)],
        rows_out(768, 768),
    )
    send, token = hold(send, token)
    arrived = to_y(send)
    g2, g2_low, placed_mem, grad_mem, gln_cross, token = call(
        cross_back_second,
        "cross_back_second",
        [meta_in]
        + [(g3_low, "tiles")]
        + late(g3, second)
        + small(norms)
        + late(wc0, wc1)
        + now(wc2, wc3)
        + late(*cross_grads)
        + head_inputs(cross_heads_second[0:4], cross_heads_second[4]),
        [stream_out(f32), stream_out(bf16), stream_out(f32, True), stream_out(bf16), grads_ln],
        back_scratch + [pltpu.VMEM((16, D), f32)],
        back_flops + 2 * SEQ * D * 1536,
        token,
    )
    arrived, token = hold(arrived, token)
    kept, *sends = simple(
        slot_2, "slot_2", meta, [kept, arrived], rows_out(192, 192, 192, 192)
    )
    kept, token = hold(kept, token)
    parts = to_z(sends)

    *self_grads, self_own, self_other, token = call(
        functools.partial(attention_back_first, False),
        "self_back_first",
        [meta_in]
        + [(g2_low, "tiles")]
        + late(nq, nc)
        + small(rank, limit)
        + now(ws0, ws1)
        + head_inputs(first[0:4], first[4]),
        [pair_out] * 3 + packed_outs,
        [limits] + back_scratch,
        back_flops + 2 * SEQ * D * 1024,
        token,
    )
    *parts, self_other, token = hold(*parts, self_other, token)
    total, self_kept, self_send = simple(
        slot_3,
        "slot_3",
        meta,
        [kept, *parts, self_own, to_core(self_other)],
        rows_out(192, 256, 256),
    )
    total, self_send, grad_mem, token = hold(total, self_send, grad_mem, token)
    self_arrived = to_y(self_send)
    parts = to_z([total] * 3)
    mem_other = to_core(grad_mem)
    *self_grads_second, token = call(
        self_back_second,
        "self_back_second",
        [meta_in, (g2_low, "tiles")]
        + small(rank, limit)
        + now(ws2, ws3)
        + head_inputs(second_heads[0:4], second_heads[4]),
        [pair_out] * 3,
        [limits] + back_scratch,
        back_flops,
        token,
    )
    output_other, mem_other, token = hold(output_other, mem_other, token)
    out_both, grad_mem_both = both_rows(
        [placed_output, placed_mem], [output_other, mem_other], "place_early"
    )
    *parts, self_arrived, out_both, token = hold(*parts, self_arrived, out_both, token)
    half, self_kept, *sends = simple(
        slot_4,
        "slot_4",
        meta,
        [total, *parts, self_kept, self_arrived],
        rows_out(768, 64, 64, 64, 64),
    )
    half, token = hold(half, token)
    self_parts = to_z(sends)
    arrived = to_y(half)
    placed_q, placed_c, gq, gc, gln_self, token = call(
        self_back_finish,
        "self_back_finish",
        [meta_in, (g2, "tiles"), (query_stream, "tiles_row"), (content_stream, "tiles_row")]
        + small(norms)
        + now(ws0, ws1, ws2, ws3)
        + [(x, "tiles") for x in self_grads + self_grads_second],
        [stream_out(f32, True), stream_out(f32, True), stream_out(bf16), stream_out(bf16), grads_ln],
        [pltpu.VMEM((32, D), f32)],
        2 * SEQ * D * 1536,
        token,
    )
    gln = jnp.concatenate([gln_self[0:4], gln_cross[0:2], gln_ffn[0:2]], axis=0)
    gq_other, gc_other = to_core(gq), to_core(gc)
    *self_parts, gln = hold(*self_parts, gln)
    (last_send,) = simple(
        slot_5,
        "slot_5",
        meta,
        [self_kept, *self_parts, gln, to_core(gln)],
        [((GROUP, 80, D), bf16)],
    )
    last_send, arrived = hold(last_send, arrived)
    groups = None
    if row_count > GROUP:
        groups = [list(range(r, r + GROUP)) for r in range(0, row_count, GROUP)]
    last_parts = lax.all_to_all(last_send, "rows", 0, 0, axis_index_groups=groups)
    def over_groups(totals):
        if row_count == GROUP:
            return totals
        groups = [list(range(r, row_count, GROUP)) for r in range(GROUP)]
        return lax.psum(totals, "rows", axis_index_groups=groups)

    gq_both, gc_both = both_rows([placed_q, placed_c], [gq_other, gc_other], "place_late")

    attention_outs = [((512, 128), f32)] * 3 + [((128, 512), f32)]
    grad_ffn_in, grad_ffn_out, *grad_cross_parts = simple(
        unpack_early,
        "unpack_early",
        meta,
        [half, arrived],
        [((D, D), f32)] * 2 + attention_outs,
        [pltpu.VMEM((D, D), bf16), pltpu.VMEM((2 * D, D), bf16)],
    )
    *grad_self_parts, gln = simple(
        unpack_late,
        "unpack_late",
        meta,
        [last_parts],
        attention_outs + [((8, D), f32)],
        [pltpu.VMEM((D, D), bf16)],
    )
    grad_ffn_in, grad_ffn_out, grad_cross_parts, grad_self_parts, gln = over_groups(
        (grad_ffn_in, grad_ffn_out, grad_cross_parts, grad_self_parts, gln)
    )
    return (
        out_both,
        gq_both,
        gc_both,
        grad_mem_both,
        gln[0],
        gln[1],
        gln[2],
        gln[3],
        *grad_self_parts,
        gln[4],
        gln[5],
        *grad_cross_parts,
        gln[6],
        gln[7],
        grad_ffn_in,
        grad_ffn_out,
    )


def solution(mesh):
    assert mesh.shape["heads"] == 4
    row_spec = P("rows", None)
    flat = P("rows")
    by_column = P(None, "heads")
    by_row = P("heads", None)
    attention = (by_column, by_column, by_column, by_row)
    in_specs = (
        (row_spec,) * 3
        + (flat,) * 5
        + (P(),) * 4
        + attention
        + (P(),) * 2
        + attention
        + (P(),) * 2
        + (by_column, by_row, row_spec)
    )
    out_specs = (
        (row_spec,) * 4
        + (P(),) * 4
        + attention
        + (P(),) * 2
        + attention
        + (P(),) * 2
        + (by_column, by_row)
    )
    return jax.shard_map(shards, mesh=mesh, in_specs=in_specs, out_specs=out_specs, check_vma=False)
```

```python
import functools

import jax
import jax.numpy as jnp
from jax import lax
from jax.experimental import pallas as pl
from jax.experimental.pallas import tpu as pltpu
from jax.sharding import PartitionSpec as P

HEAD_DIM = 64
SEQ = 1024
DOCS = 8
D = 512
TILE = 256
TILES = SEQ // TILE
FAST_Q = 256
FAST_K = 208
LONG_Q = 128
LONG_K = 640

norm_eps = 1e-05
masked_score = -1e30
hidden_rank = 1e6
gelu_root = 0.7978845608028654
gelu_cube = 0.044715

f32 = jnp.float32
bf16 = jnp.bfloat16


def dot(a, b):
    return lax.dot_general(a, b, (((1,), (0,)), ((), ())), preferred_element_type=f32)


def dot_nt(a, b):
    return lax.dot_general(a, b, (((1,), (1,)), ((), ())), preferred_element_type=f32)


def dot_tn(a, b):
    return lax.dot_general(a, b, (((0,), (0,)), ((), ())), preferred_element_type=f32)


def lanes(parts):
    return jnp.concatenate(parts, axis=1)


NORM_ROWS = 32


def layer_norm(values, gain, shift):
    def piece(part):
        part = part.astype(f32)
        centre = part - jnp.mean(part, axis=-1, keepdims=True)
        spread = jnp.mean(centre * centre, axis=-1, keepdims=True)
        return (centre * lax.rsqrt(spread + norm_eps) * gain + shift).astype(bf16)

    return by_pieces(piece, NORM_ROWS, 0, values)


def eight_rows(values):
    return sum(values[8 * i : 8 * i + 8] for i in range(1, values.shape[0] // 8)) + values[0:8]


def norm_backward(values, gain, grad, sums_ref, first):
    sums = []

    def piece(part, grad_part):
        part = part.astype(f32)
        centre = part - jnp.mean(part, axis=-1, keepdims=True)
        spread = jnp.mean(centre * centre, axis=-1, keepdims=True)
        scale = lax.rsqrt(spread + norm_eps)
        xhat = centre * scale
        eg = grad_part * gain
        mean_eg = jnp.mean(eg, axis=-1, keepdims=True)
        mean_egx = jnp.mean(eg * xhat, axis=-1, keepdims=True)
        sums.append((eight_rows(grad_part * xhat), eight_rows(grad_part)))
        return scale * (eg - mean_eg - xhat * mean_egx)

    result = by_pieces(piece, NORM_ROWS, 0, values, grad)
    for n, parts in enumerate(zip(*sums)):
        sums_ref[first + 8 * n : first + 8 * n + 8, :] += sum(parts[1:], parts[0])
    return result


def add_sums(sums_ref, gln_ref, count):
    gln_ref[...] = jnp.zeros_like(gln_ref)
    for n in range(count):
        gln_ref[n : n + 1, :] = jnp.sum(sums_ref[8 * n : 8 * n + 8, :], axis=0, keepdims=True)


def by_pieces(work, size, axis, *arrays):
    count = arrays[0].shape[axis] // size
    pieces = []
    for i in range(count):
        cut = (slice(size * i, size * i + size),)
        cut = cut if axis == 0 else (slice(None),) + cut
        pieces.append(work(*[x[cut] for x in arrays]))
    if not isinstance(pieces[0], tuple):
        return jnp.concatenate(pieces, axis=axis)
    return tuple(jnp.concatenate(parts, axis=axis) for parts in zip(*pieces))


def rows_of(i, size=TILE):
    return pl.ds(pl.multiple_of(i * size, size), size)


def w_query(ref):
    return ref[:, 0:128]


def w_key(ref):
    return ref[:, 128:256]


def w_value(ref):
    return ref[:, 256:384]


def w_out(ref):
    return lanes([ref[128 * j : 128 * j + 128, 384:512] for j in range(4)])


def half_masks():
    place = lax.broadcasted_iota(jnp.int32, (1, 128), 1)
    low = jnp.where(place < HEAD_DIM, 1.0, 0.0).astype(f32)
    return (low.astype(bf16), (1.0 - low).astype(bf16))


def doc_bounds(meta, d, source):
    base = 17 if source else 1
    return meta[base + d], meta[base + 8 + d]


def window_of(first, limit):
    return pl.multiple_of(jnp.minimum((first // 16) * 16, limit), 16)


def key_bias(ks, ke, k0, width):
    place = k0 + lax.broadcasted_iota(jnp.int32, (width, 128), 0)
    return jnp.where((place >= ks) & (place < ke), 0.0, masked_score)


def make_bias(rank_ref, limit_ref, ks, ke, q0, k0, span, width):
    if rank_ref is None:
        return lanes([key_bias(ks, ke, k0, width)] * (span // 128))
    place = k0 + lax.broadcasted_iota(jnp.int32, (width, 128), 0)
    ranks = rank_ref[pl.ds(k0, width), :]
    ranks = jnp.where((place < ks + 2) & (ranks < hidden_rank), -1.0, ranks)
    ranks = jnp.where((place >= ks) & (place < ke), ranks, hidden_rank)
    limits = jnp.broadcast_to(limit_ref[...], (8, SEQ))
    limits = pltpu.roll(limits, lax.rem(SEQ - q0, SEQ), 1)[0:1, 0:span]
    row = k0 + lax.broadcasted_iota(jnp.int32, (width, span), 0)
    column = q0 + lax.broadcasted_iota(jnp.int32, (width, span), 1)
    seen = (lanes([ranks] * (span // 128)) < limits) & (row != column)
    return jnp.where(seen, 0.0, masked_score)


TOGETHER = 4
STEPS = DOCS // TOGETHER


LAG = 2


def interleave(items):
    items = [list(phases) for phases in items]
    depth = max(len(phases) for phases in items)
    results = [None] * len(items)
    for tick in range(len(items) + LAG * (depth - 1)):
        for phase in range(depth):
            n = tick - LAG * phase
            if 0 <= n < len(items) and phase < len(items[n]):
                run = items[n][phase]
                results[n] = run() if phase == 0 else run(results[n])
    return results


def by_halves(pairs, phases):
    shared = [{} for _ in range(pairs)]
    return [phases(n, a, shared[n]) for n in range(pairs) for a in range(2)]


def is_fast(meta, cross):
    return meta[34 if cross else 33] == 1


def both_heads(x, masks):
    return jnp.concatenate([x * masks[0], x * masks[1]], axis=0)


def pair_scores(queries, keys, masks):
    return dot_nt(both_heads(keys, masks), queries)


def raised(scores, bias):
    def piece(part, bias_part):
        part = part + bias_part
        return jnp.exp((part - jnp.max(part, axis=0, keepdims=True)).astype(bf16))

    return by_pieces(piece, 128, 1, scores, bias)


def weighted_values(values, parts):
    width = values.shape[1]
    mixed = []
    shares = []
    for a, part in enumerate(parts):
        rows = jnp.concatenate([values[64 * a : 64 * a + 64], jnp.ones((16, width), bf16)], axis=0)
        sums = dot(rows, part)
        share = 1.0 / sums[64:65]
        mixed.append(sums[:64] * share)
        shares.append(part * share.astype(bf16))
    return jnp.concatenate(mixed, axis=0).astype(bf16), shares


def pair_gradient(rows, parts):
    across = jnp.transpose(rows)
    halves = [dot(across[64 * a : 64 * a + 64], part) for a, part in enumerate(parts)]
    return jnp.transpose((jnp.concatenate(halves, axis=0) * HEAD_DIM**-0.5).astype(bf16))


def for_docs(meta, cross, run, before, after):
    @pl.when(is_fast(meta, cross))
    def _():
        def step(i, carry):
            slot = lax.rem(i, 2)
            before(i, slot)
            items = []
            for place in range(TOGETHER):
                d = TOGETHER * i + place
                ts, te = doc_bounds(meta, d, False)
                ks, ke = doc_bounds(meta, d, cross)
                q0 = window_of(ts, SEQ - FAST_Q)
                k0 = window_of(ks, SEQ - FAST_K)
                items += run(d, slot, place, q0, k0, FAST_Q, FAST_K, ts, te, ks, ke, True)
            interleave(items)
            after(i, slot)
            return carry

        lax.fori_loop(0, STEPS, step, 0)

    @pl.when(jnp.logical_not(is_fast(meta, cross)))
    def _():
        def doc(d, carry):
            ts, te = doc_bounds(meta, d, False)
            ks, ke = doc_bounds(meta, d, cross)
            base = (ts // 16) * 16
            k0 = window_of(ks, SEQ - LONG_K)

            def chunk(i, carry):
                lower = base + i * LONG_Q
                q0 = pl.multiple_of(jnp.minimum(lower, SEQ - LONG_Q), 16)
                low = jnp.maximum(ts, lower)
                high = jnp.minimum(te, lower + LONG_Q)
                interleave(run(d, None, None, q0, k0, LONG_Q, LONG_K, low, high, ks, ke, False))
                return carry

            return lax.fori_loop(0, (te - base + LONG_Q - 1) // LONG_Q, chunk, carry)

        lax.fori_loop(0, DOCS, doc, 0)


def attend_docs(meta, cross, rank_ref, limit_ref, halves, p_ref, p_buf, p_sem):
    pairs = 2 * len(halves)
    masks = half_masks()

    def save(i, slot):
        return pltpu.make_async_copy(p_buf.at[slot], p_ref.at[pl.ds(TOGETHER * i, TOGETHER)], p_sem.at[slot])

    def before(i, slot):
        @pl.when(i >= 2)
        def _():
            save(i - 2, slot).wait()

    def after(i, slot):
        save(i, slot).start()

    def run(d, slot, place, q0, k0, span, width, low, high, ks, ke, fast):
        bias = make_bias(rank_ref, limit_ref, ks, ke, q0, k0, span, width)
        row = q0 + lax.broadcasted_iota(jnp.int32, (span, 128), 0)
        inside = (row >= low) & (row < high)

        def phases(n):
            q_ref, k_ref, v_ref, mixed_ref = halves[n // 2]
            cols = slice(128 * (n % 2), 128 * (n % 2) + 128)

            def score():
                return pair_scores(q_ref[pl.ds(q0, span), cols], k_ref[pl.ds(k0, width), cols], masks)

            def weigh(scores):
                return [raised(scores[width * a : width * a + width], bias) for a in range(2)]

            def mix(parts):
                values = jnp.transpose(v_ref[pl.ds(k0, width), cols])
                mixed, parts = weighted_values(values, parts)
                if fast:
                    for a in range(2):
                        p_buf[slot, place, 2 * n + a] = parts[a]
                mixed = jnp.transpose(mixed).astype(f32)
                old = mixed_ref[pl.ds(q0, span), cols].astype(f32)
                mixed_ref[pl.ds(q0, span), cols] = jnp.where(inside, mixed, old).astype(bf16)

            return score, weigh, mix

        return [phases(n) for n in range(pairs)]

    for_docs(meta, cross, run, before, after)

    @pl.when(is_fast(meta, cross))
    def _():
        for i in range(STEPS - 2, STEPS):
            save(i, i % 2).wait()


def load_step(load, i, slot):
    p_ref, p_buf, p_sem = load
    return pltpu.make_async_copy(p_ref.at[pl.ds(TOGETHER * i, TOGETHER)], p_buf.at[slot], p_sem.at[slot])


def start_load(meta, cross, load):
    @pl.when(is_fast(meta, cross))
    def _():
        load_step(load, 0, 0).start()


def attend_docs_back(
    meta, cross, rank_ref, limit_ref, q_ref, k_ref, v_ref, mixed_ref, dm_ref,
    dq_ref, dk_ref, dv_ref, load,
):
    pairs = q_ref.shape[1] // 128
    masks = half_masks()
    p_buf = load[1]

    def before(i, slot):
        @pl.when(i + 1 < STEPS)
        def _():
            load_step(load, i + 1, 1 - slot).start()

        load_step(load, i, slot).wait()

    def after(i, slot):
        pass

    def run(d, slot, place, q0, k0, span, width, low, high, ks, ke, fast):
        row = q0 + lax.broadcasted_iota(jnp.int32, (span, 128), 0)
        inside = jnp.where((row >= low) & (row < high), 1.0, 0.0).astype(bf16)
        ones = jnp.ones((width, 128), bf16)
        if not fast:
            bias = make_bias(rank_ref, limit_ref, ks, ke, q0, k0, span, width)

        def phases(n):
            cols = slice(128 * n, 128 * n + 128)

            def differ():
                values = v_ref[pl.ds(k0, width), cols]
                mixed = mixed_ref[pl.ds(q0, span), cols]
                grad = dm_ref[pl.ds(q0, span), cols] * inside
                left = lanes([grad, -(grad * mixed)])
                right = both_heads(lanes([values, ones]), [lanes([m, m]) for m in masks])
                return grad, dot_nt(right, left)

            def slope(state):
                grad, delta = state
                if fast:
                    parts = [p_buf[slot, place, 2 * n + a] for a in range(2)]
                else:
                    queries = q_ref[pl.ds(q0, span), cols]
                    keys = k_ref[pl.ds(k0, width), cols]
                    scores = pair_scores(queries, keys, masks)
                    parts = [raised(scores[width * a : width * a + width], bias) for a in range(2)]
                    parts = weighted_values(jnp.transpose(v_ref[pl.ds(k0, width), cols]), parts)[1]
                slopes = [
                    by_pieces(
                        lambda part, change: part * change.astype(bf16),
                        16,
                        0,
                        parts[a],
                        delta[width * a : width * a + width],
                    )
                    for a in range(2)
                ]
                return grad, parts, slopes

            def spread(state):
                grad, parts, slopes = state
                queries = q_ref[pl.ds(q0, span), cols]
                dk = dv = None
                for a in range(2):
                    dk_a = dot(slopes[a], queries * masks[a])
                    dv_a = dot(parts[a], grad * masks[a])
                    dk = dk_a if dk is None else dk + dk_a
                    dv = dv_a if dv is None else dv + dv_a
                dq = pair_gradient(k_ref[pl.ds(k0, width), cols], slopes)
                dq_ref[pl.ds(q0, span), cols] += dq.astype(f32)
                dk_ref[pl.ds(k0, width), cols] += dk
                dv_ref[pl.ds(k0, width), cols] += dv

            return differ, slope, spread

        return [phases(n) for n in range(pairs)]

    for_docs(meta, cross, run, before, after)


def spread_ranks(rank_row_ref, rank_ref):
    rank_ref[...] = jnp.transpose(jnp.broadcast_to(rank_row_ref[...], (128, SEQ)))


def prepare(
    core, seg_ref, src_ref, rank_ref, limit_ref, pad_ref,
    n0, n1, n2, n3, n4, n5, n6, n7, sq, sk, sv, so, cq, ck, cv, co,
    meta_ref, ranks_ref, limits_ref, norms_ref, ws_ref, wc_ref,
):
    meta_ref[0] = core[0]
    meta_ref[35] = core[1]
    for base, ref in ((1, seg_ref), (17, src_ref)):
        ids = ref[0]
        meta_ref[base] = 0
        meta_ref[base + 15] = SEQ
        for d in range(1, DOCS):
            cut = jnp.sum(jnp.where(ids < d, 1.0, 0.0)).astype(jnp.int32)
            meta_ref[base + d] = cut
            meta_ref[base + 7 + d] = cut
    for place, base in ((33, 1), (34, 17)):
        fast = jnp.int32(1)
        for d in range(DOCS):
            q0 = window_of(meta_ref[1 + d], SEQ - FAST_Q)
            k0 = window_of(meta_ref[base + d], SEQ - FAST_K)
            fits = (meta_ref[9 + d] - q0 <= FAST_Q) & (meta_ref[base + 8 + d] - k0 <= FAST_K)
            fast = fast & fits.astype(jnp.int32)
        meta_ref[place] = fast
    ranks = jnp.where(pad_ref[0] != 0, hidden_rank, rank_ref[0].astype(f32))
    limits = limit_ref[0].astype(f32)
    for i in range(8):
        ranks_ref[0:1, 128 * i : 128 * i + 128] = ranks[i : i + 1]
        limits_ref[0:1, 128 * i : 128 * i + 128] = limits[i : i + 1]
    for i, ref in enumerate((n0, n1, n2, n3, n4, n5, n6, n7)):
        norms_ref[i : i + 1, :] = ref[...]
    for to, parts, out in ((ws_ref, (sq, sk, sv), so), (wc_ref, (cq, ck, cv), co)):
        for i, part in enumerate(parts):
            to[:, 128 * i : 128 * i + 128] = part[...]
        for j in range(4):
            to[128 * j : 128 * j + 128, 384:512] = out[:, 128 * j : 128 * j + 128]


def self_first(
    meta, io, xq_ref, xc_ref, rank_row_ref, limit_ref, norms_ref, w0_ref, w1_ref,
    nq_ref, nc_ref, q_ref, k_ref, v_ref, mixed_ref, p_ref, rank_ref, p_buf, p_sem,
):

    spread_ranks(rank_row_ref, rank_ref)
    wq = lanes([w_query(w0_ref), w_query(w1_ref)])
    wkv = lanes([w_key(w0_ref), w_key(w1_ref), w_value(w0_ref), w_value(w1_ref)])

    def tile(i, carry):
        rows = rows_of(i)
        io.wait_rows(i)
        nq = layer_norm(xq_ref[rows, :], norms_ref[0:1], norms_ref[1:2])
        nc = layer_norm(xc_ref[rows, :], norms_ref[2:3], norms_ref[3:4])
        nq_ref[rows, :] = nq
        nc_ref[rows, :] = nc
        q_ref[rows, :] = (dot(nq, wq) * (HEAD_DIM**-0.5)).astype(bf16)
        kv = dot(nc, wkv).astype(bf16)
        k_ref[rows, :] = kv[:, :256]
        v_ref[rows, :] = kv[:, 256:]
        return carry

    lax.fori_loop(0, TILES, tile, 0)

    for ref in (nq_ref, nc_ref, q_ref, k_ref, v_ref):
        io.send(ref)
    attend_docs(meta, False, rank_ref, limit_ref, [(q_ref, k_ref, v_ref, mixed_ref)], p_ref, p_buf, p_sem)


def self_second(
    meta, io, xq_ref, nq_ref, nc_ref, rank_row_ref, limit_ref, norms_ref, w0_ref, w1_ref, w2_ref, w3_ref,
    mixed_first_ref,
    q_ref, k_ref, v_ref, mixed_ref, p_ref, second_ref, ncross_ref, rank_ref, p_buf, p_sem,
):

    spread_ranks(rank_row_ref, rank_ref)
    wq = lanes([w_query(w2_ref), w_query(w3_ref)])
    wkv = lanes([w_key(w2_ref), w_key(w3_ref), w_value(w2_ref), w_value(w3_ref)])

    def tile(i, carry):
        rows = rows_of(i)
        io.wait_rows(i)
        q_ref[rows, :] = (dot(nq_ref[rows, :], wq) * (HEAD_DIM**-0.5)).astype(bf16)
        kv = dot(nc_ref[rows, :], wkv).astype(bf16)
        k_ref[rows, :] = kv[:, :256]
        v_ref[rows, :] = kv[:, 256:]
        return carry

    lax.fori_loop(0, TILES, tile, 0)

    for ref in (q_ref, k_ref, v_ref):
        io.send(ref)
    attend_docs(meta, False, rank_ref, limit_ref, [(q_ref, k_ref, v_ref, mixed_ref)], p_ref, p_buf, p_sem)

    io.send(mixed_ref)
    io.wait("late")
    out_first = jnp.concatenate([w_out(w0_ref), w_out(w1_ref)], axis=0)
    out_second = jnp.concatenate([w_out(w2_ref), w_out(w3_ref)], axis=0)

    def tile(i, carry):
        rows = rows_of(i)
        branch = dot(mixed_first_ref[rows, :], out_first) + dot(mixed_ref[rows, :], out_second)
        second = xq_ref[rows, :].astype(f32) + branch
        second_ref[rows, :] = second
        io.send(second_ref, rows)
        ncross_ref[rows, :] = layer_norm(second, norms_ref[4:5], norms_ref[5:6])
        io.send(ncross_ref, rows)
        return carry

    lax.fori_loop(0, TILES, tile, 0)


def project_cross(io, ncross_ref, memory_ref, weights, q_ref, k_ref, v_ref):
    wq = lanes([w_query(w) for w in weights])
    wkv = lanes([w_key(w) for w in weights] + [w_value(w) for w in weights])

    def tile(i, carry):
        rows = rows_of(i)
        io.wait_rows(i)
        q_ref[rows, :] = (dot(ncross_ref[rows, :], wq) * (HEAD_DIM**-0.5)).astype(bf16)
        kv = dot(memory_ref[rows, :], wkv).astype(bf16)
        k_ref[rows, :] = kv[:, :256]
        v_ref[rows, :] = kv[:, 256:]
        return carry

    lax.fori_loop(0, TILES, tile, 0)
    for ref in (q_ref, k_ref, v_ref):
        io.send(ref)


def cross_first(
    meta, io, ncross_ref, memory_ref, w0_ref, w1_ref,
    q_ref, k_ref, v_ref, mixed_ref, p_ref, p_buf, p_sem,
):
    project_cross(io, ncross_ref, memory_ref, (w0_ref, w1_ref), q_ref, k_ref, v_ref)
    attend_docs(meta, True, None, None, [(q_ref, k_ref, v_ref, mixed_ref)], p_ref, p_buf, p_sem)


def cross_second(
    meta, io, second_ref, ncross_ref, memory_ref, norms_ref, w0_ref, w1_ref, w2_ref, w3_ref,
    mixed_first_ref,
    q_ref, k_ref, v_ref, mixed_ref, p_ref, third_ref, nffn_ref, p_buf, p_sem,
):
    project_cross(io, ncross_ref, memory_ref, (w2_ref, w3_ref), q_ref, k_ref, v_ref)
    attend_docs(meta, True, None, None, [(q_ref, k_ref, v_ref, mixed_ref)], p_ref, p_buf, p_sem)
    io.send(mixed_ref)
    io.wait("late")
    out_first = jnp.concatenate([w_out(w0_ref), w_out(w1_ref)], axis=0)
    out_second = jnp.concatenate([w_out(w2_ref), w_out(w3_ref)], axis=0)

    def tile(i, carry):
        rows = rows_of(i)
        branch = dot(mixed_first_ref[rows, :], out_first) + dot(mixed_ref[rows, :], out_second)
        third = second_ref[rows, :] + branch
        third_ref[rows, :] = third
        io.send(third_ref, rows)
        nffn_ref[rows, :] = layer_norm(third, norms_ref[6:7], norms_ref[7:8])
        io.send(nffn_ref, rows)
        return carry

    lax.fori_loop(0, TILES, tile, 0)


def ffn_both(
    meta, io, third_ref, nffn_ref, cot_ref, norms_ref, u0_ref, u1_ref, u2_ref, u3_ref,
    w0_ref, w1_ref, w2_ref, w3_ref,
    placed_ref, out_ref, g3_ref, g3_low_ref, gln_ref, own_ref, other_ref, hidden_ref, before_ref, sums_ref,
):
    sums_ref[...] = jnp.zeros_like(sums_ref)
    in_refs = (u0_ref, u1_ref, u2_ref, u3_ref)
    w_refs = (w0_ref, w1_ref, w2_ref, w3_ref)

    def tile(i, carry):
        rows = rows_of(i)
        io.wait_rows(i)
        nffn = nffn_ref[rows, :]
        cot = cot_ref[rows, :]
        outs = []
        grads = []

        def phases(g, c, group):
            w_in = in_refs[g]
            w_out_rows = w_refs[g]
            cols = slice(256 * c, 256 * c + 256)

            def enter():
                return dot(nffn, w_in[:, cols]), dot_nt(cot, w_out_rows[cols, :])

            def bend(state):
                def piece(x, grad_hidden):
                    square = x * x
                    argument = x * (gelu_root + (gelu_root * gelu_cube) * square)
                    half = 0.5 + 0.5 * jnp.tanh(argument.astype(bf16))
                    x = x.astype(bf16)
                    square = square.astype(bf16)
                    value = x * half
                    rise = 2.0 * gelu_root + (6.0 * gelu_root * gelu_cube) * square
                    slope = half + value * (1.0 - half) * rise
                    return value, grad_hidden.astype(bf16) * slope

                hidden, grad_before = by_pieces(piece, 32, 0, *state)
                if g < 2:
                    place = slice(512 * g + 256 * c, 512 * g + 256 * c + 256)
                    hidden_ref[rows, place] = hidden
                    before_ref[rows, place] = grad_before
                group[c] = hidden, grad_before

            def leave(_):
                if c == 1:
                    outs.append(dot(lanes([group[0][0], group[1][0]]), w_out_rows[...]))

            def leave_back(_):
                if c == 1:
                    grads.append(dot_nt(lanes([group[0][1], group[1][1]]), w_in[...]))

            return enter, bend, leave, leave_back

        interleave(by_halves(4, phases))
        third = third_ref[rows, :]
        result = (third + ((outs[0] + outs[1]) + (outs[2] + outs[3]))).astype(bf16)
        out_ref[rows, :] = result
        placed_ref[rows, :] = result
        grad_normed = (grads[0] + grads[1]) + (grads[2] + grads[3])
        grad_norm = norm_backward(third, norms_ref[6:7], grad_normed, sums_ref, 0)
        g3 = cot.astype(f32) + grad_norm
        g3_ref[rows, :] = g3
        g3_low_ref[rows, :] = g3.astype(bf16)
        for ref in (out_ref, placed_ref, g3_ref, g3_low_ref):
            io.send(ref, rows)
        return carry

    lax.fori_loop(0, TILES, tile, 0)
    add_sums(sums_ref, gln_ref, 2)
    part = dot_tn(nffn_ref[...], before_ref[...])
    own_ref[0:512, :] = part[:, 0:512].astype(bf16)
    other_ref[0:512, :] = part[:, 512:1024].astype(bf16)
    io.send(own_ref, pl.ds(0, 512))
    io.send(other_ref, pl.ds(0, 512))
    part = dot_tn(hidden_ref[...], cot_ref[...])
    own_ref[512:1024, :] = part[0:512].astype(bf16)
    other_ref[512:1024, :] = part[512:1024].astype(bf16)
    io.send(own_ref, pl.ds(512, 512))
    io.send(other_ref, pl.ds(512, 512))


def back_start(io, g_ref, mixed_ref, w_refs, dm_ref, dq_ref, dk_ref, dv_ref):
    out_rows = jnp.concatenate([w_out(w) for w in w_refs], axis=0)

    def tile(i, carry):
        rows = rows_of(i)
        io.wait_rows(i)
        dm_ref[rows, :] = dot_nt(g_ref[rows, :], out_rows).astype(bf16)
        zeros = jnp.zeros((TILE, 256), f32)
        dq_ref[rows, :] = zeros
        dk_ref[rows, :] = zeros
        dv_ref[rows, :] = zeros
        return carry

    lax.fori_loop(0, TILES, tile, 0)


def attention_back_first(
    cross, meta, io, g_ref, nq_ref, nkv_ref, rank_row_ref, limit_ref, w0_ref, w1_ref,
    q_ref, k_ref, v_ref, mixed_ref, p_ref,
    dq_ref, dk_ref, dv_ref, own_ref, other_ref,
    rank_ref, dm_ref, dqs_ref, dks_ref, dvs_ref, p_buf, p_sem,
):
    load = (p_ref, p_buf, p_sem)
    start_load(meta, cross, load)
    if not cross:
        spread_ranks(rank_row_ref, rank_ref)
    back_start(io, g_ref, mixed_ref, (w0_ref, w1_ref), dm_ref, dqs_ref, dks_ref, dvs_ref)

    io.wait("soon")
    attend_docs_back(
        meta, cross, None if cross else rank_ref, limit_ref, q_ref, k_ref, v_ref, mixed_ref,
        dm_ref, dqs_ref, dks_ref, dvs_ref, load,
    )

    dq_ref[...] = dqs_ref[...].astype(bf16)
    dk_ref[...] = dks_ref[...].astype(bf16)
    dv_ref[...] = dvs_ref[...].astype(bf16)
    for ref in (dq_ref, dk_ref, dv_ref):
        io.send(ref)
    io.wait("late")
    nq = nq_ref[...]
    nkv = nkv_ref[...]
    kv = dot_tn(nkv, lanes([dk_ref[...], dv_ref[...]]))
    for n, part in enumerate((dot_tn(nq, dq_ref[...]), kv[:, 0:256], kv[:, 256:512])):
        own_ref[:, 128 * n : 128 * n + 128] = part[:, :128].astype(bf16)
        other_ref[:, 128 * n : 128 * n + 128] = part[:, 128:].astype(bf16)
    part = dot_tn(mixed_ref[...], g_ref[...])
    for j in range(4):
        rows = slice(128 * j, 128 * j + 128)
        own_ref[rows, 384:512] = part[:128, rows].astype(bf16)
        other_ref[rows, 384:512] = part[128:, rows].astype(bf16)


def back_second_docs(
    cross, meta, io, g_ref, rank_row_ref, limit_ref, w_refs, q_ref, k_ref, v_ref, mixed_ref, p_ref,
    rank_ref, dm_ref, dqs_ref, dks_ref, dvs_ref, p_buf, p_sem,
):
    load = (p_ref, p_buf, p_sem)
    start_load(meta, cross, load)
    if not cross:
        spread_ranks(rank_row_ref, rank_ref)
    back_start(io, g_ref, mixed_ref, w_refs, dm_ref, dqs_ref, dks_ref, dvs_ref)

    io.wait("soon")
    attend_docs_back(
        meta, cross, None if cross else rank_ref, limit_ref, q_ref, k_ref, v_ref, mixed_ref,
        dm_ref, dqs_ref, dks_ref, dvs_ref, load,
    )


def stream_grads(rows, first, second, firsts, seconds):
    dq, dk, dv = first
    dq2, dk2, dv2 = (ref[rows, :].astype(bf16) for ref in second)
    w0, w1 = firsts
    w2, w3 = seconds
    grad_q = dot_nt(dq[rows, :], lanes([w_query(w0), w_query(w1)])) + dot_nt(
        dq2, lanes([w_query(w2), w_query(w3)])
    )
    kv = lanes([dk[rows, :], dv[rows, :]])
    kv2 = lanes([dk2, dv2])
    grad_kv = dot_nt(kv, lanes([w_key(w0), w_key(w1), w_value(w0), w_value(w1)])) + dot_nt(
        kv2, lanes([w_key(w2), w_key(w3), w_value(w2), w_value(w3)])
    )
    return grad_q, grad_kv


def cross_back_second(
    meta, io, g_low_ref, g_ref, second_ref, norms_ref, w0_ref, w1_ref, w2_ref, w3_ref,
    dq_ref, dk_ref, dv_ref, q_ref, k_ref, v_ref, mixed_ref, p_ref,
    g2_ref, g2_low_ref, placed_ref, gmem_ref, gln_ref,
    dm_ref, dqs_ref, dks_ref, dvs_ref, p_buf, p_sem, sums_ref,
):
    back_second_docs(
        True, meta, io, g_low_ref, None, None, (w2_ref, w3_ref), q_ref, k_ref, v_ref, mixed_ref, p_ref,
        None, dm_ref, dqs_ref, dks_ref, dvs_ref, p_buf, p_sem,
    )

    io.wait("late")
    sums_ref[...] = jnp.zeros_like(sums_ref)

    def tile(i, carry):
        rows = rows_of(i)
        grad_q, grad_kv = stream_grads(
            rows,
            (dq_ref, dk_ref, dv_ref),
            (dqs_ref, dks_ref, dvs_ref),
            (w0_ref, w1_ref),
            (w2_ref, w3_ref),
        )
        low_kv = grad_kv.astype(bf16)
        gmem_ref[rows, :] = low_kv
        placed_ref[rows, :] = low_kv.astype(f32)
        io.send(gmem_ref, rows)
        io.send(placed_ref, rows)
        grad_norm = norm_backward(second_ref[rows, :], norms_ref[4:5], grad_q, sums_ref, 0)
        g2 = g_ref[rows, :] + grad_norm
        g2_ref[rows, :] = g2
        g2_low_ref[rows, :] = g2.astype(bf16)
        io.send(g2_ref, rows)
        io.send(g2_low_ref, rows)
        return carry

    lax.fori_loop(0, TILES, tile, 0)
    add_sums(sums_ref, gln_ref, 2)


def self_back_second(
    meta, io, g_low_ref, rank_row_ref, limit_ref, w2_ref, w3_ref,
    q_ref, k_ref, v_ref, mixed_ref, p_ref,
    dq_ref, dk_ref, dv_ref,
    rank_ref, dm_ref, dqs_ref, dks_ref, dvs_ref, p_buf, p_sem,
):
    back_second_docs(
        False, meta, io, g_low_ref, rank_row_ref, limit_ref, (w2_ref, w3_ref), q_ref, k_ref, v_ref,
        mixed_ref, p_ref, rank_ref, dm_ref, dqs_ref, dks_ref, dvs_ref, p_buf, p_sem,
    )
    dq_ref[...] = dqs_ref[...].astype(bf16)
    dk_ref[...] = dks_ref[...].astype(bf16)
    dv_ref[...] = dvs_ref[...].astype(bf16)


def self_back_finish(
    meta, io, g_ref, xq_ref, xc_ref, norms_ref, w0_ref, w1_ref, w2_ref, w3_ref,
    dq_ref, dk_ref, dv_ref, dq2_ref, dk2_ref, dv2_ref,
    placed_q_ref, placed_c_ref, gq_ref, gc_ref, gln_ref, sums_ref,
):
    sums_ref[...] = jnp.zeros_like(sums_ref)

    def tile(i, carry):
        rows = rows_of(i)
        io.wait_rows(i)
        grad_q, grad_kv = stream_grads(
            rows,
            (dq_ref, dk_ref, dv_ref),
            (dq2_ref, dk2_ref, dv2_ref),
            (w0_ref, w1_ref),
            (w2_ref, w3_ref),
        )
        grad_norm = norm_backward(xq_ref[rows, :], norms_ref[0:1], grad_q, sums_ref, 0)
        low_q = (g_ref[rows, :] + grad_norm).astype(bf16)
        gq_ref[rows, :] = low_q
        placed_q_ref[rows, :] = low_q.astype(f32)
        io.send(gq_ref, rows)
        io.send(placed_q_ref, rows)
        grad_norm = norm_backward(xc_ref[rows, :], norms_ref[2:3], grad_kv, sums_ref, 16)
        low_c = grad_norm.astype(bf16)
        gc_ref[rows, :] = low_c
        placed_c_ref[rows, :] = low_c.astype(f32)
        io.send(gc_ref, rows)
        io.send(placed_c_ref, rows)
        return carry

    lax.fori_loop(0, TILES, tile, 0)
    add_sums(sums_ref, gln_ref, 4)


def place_rows(meta, *refs):
    count = len(refs) // 3
    for n in range(count):
        refs[2 * count + n][...] = refs[n][...].astype(refs[2 * count + n].dtype)


GROUP = 8


def position(meta):
    r = meta[35]
    return lax.rem(r, 2), r // 2


def join(own, other, rows):
    return (own[rows, :].astype(f32) + other[rows, :].astype(f32)).astype(bf16)


def join_halves(meta, own, other, keep, send):
    y, _ = position(meta)
    size = keep.shape[0]
    keep[...] = join(own, other, rows_of(y, size))
    send[...] = join(own, other, rows_of(1 - y, size))


def join_chunks(meta, kept, arrived, keep, sends):
    _, z = position(meta)
    size = keep.shape[0]
    keep[...] = join(kept, arrived, rows_of(z, size))
    for s, (send, first) in enumerate(sends, 1):
        send[first : first + size, :] = join(kept, arrived, rows_of(z ^ s, size))


def add_up(kept, parts, first):
    size = kept.shape[0]
    total = kept[...].astype(f32)
    for part in parts:
        total = total + part[first : first + size, :].astype(f32)
    return total.astype(bf16)


def half_of(meta, total, parts, first, half):
    _, z = position(meta)
    size = total.shape[0]
    half[rows_of(z, size), :] = total[...]
    for s, part in enumerate(parts, 1):
        half[rows_of(z ^ s, size), :] = part[first : first + size, :]


def slot_1(meta, ffn_own, ffn_other, keep, send):
    join_halves(meta, ffn_own, ffn_other, keep, send)


def slot_2(
    meta, ffn_kept, ffn_arrived, cross_own, cross_other, ffn_keep, f1, f2, f3, keep, send
):
    join_chunks(meta, ffn_kept, ffn_arrived, ffn_keep, [(f1, 0), (f2, 0), (f3, 0)])
    join_halves(meta, cross_own, cross_other, keep, send)


def slot_3(
    meta, ffn_kept, f1, f2, f3, cross_kept, cross_arrived, self_own, self_other,
    ffn_total, cross_keep, m1, m2, m3, self_keep, self_send,
):
    join_halves(meta, self_own, self_other, self_keep, self_send)
    total = add_up(ffn_kept, (f1, f2, f3), 0)
    ffn_total[...] = total
    size = total.shape[0]
    join_chunks(meta, cross_kept, cross_arrived, cross_keep, [(m, size) for m in (m1, m2, m3)])
    for m in (m1, m2, m3):
        m[0:size, :] = total


def slot_4(
    meta, ffn_total, m1, m2, m3, cross_kept, self_kept, self_arrived,
    ffn_half, cross_total, self_keep, *sends,
):
    join_chunks(meta, self_kept, self_arrived, self_keep, [(send, 0) for send in sends])
    total = add_up(cross_kept, (m1, m2, m3), ffn_total.shape[0])
    cross_total[...] = total
    size = total.shape[0]
    for send in sends:
        send[size:, :] = total
    half_of(meta, ffn_total, (m1, m2, m3), 0, ffn_half)


def slot_5(meta, self_kept, cross_total, m1, m2, m3, send, cross_half):
    size = self_kept.shape[0]
    total = add_up(self_kept, (m1, m2, m3), 0)
    for r in range(GROUP):
        send[r] = total
    half_of(meta, cross_total, (m1, m2, m3), size, cross_half)


def join_norms(meta, own, other, send):
    for r in range(GROUP):
        send[r] = own[...] + other[...]


def unpack_attention(whole_ref, outs):
    for i in range(3):
        outs[i][...] = whole_ref[:, 128 * i : 128 * i + 128].astype(f32)
    for j in range(4):
        rows = slice(128 * j, 128 * j + 128)
        outs[3][:, rows] = whole_ref[rows, 384:512].astype(f32)


def unpack_ffn(meta, half, arrived, out_in, out_out, ffn_whole):
    y, _ = position(meta)
    ffn_whole[rows_of(y, 512), :] = half[...]
    ffn_whole[rows_of(1 - y, 512), :] = arrived[...]
    out_in[...] = ffn_whole[0:512, :].astype(f32)
    out_out[...] = ffn_whole[512:1024, :].astype(f32)


def unpack_rest(meta, cross_half, cross_arrived, parts, norm_parts, *refs):
    *outs, gln, whole_ref = refs
    y, _ = position(meta)
    whole_ref[rows_of(y, 256), :] = cross_half[...]
    whole_ref[rows_of(1 - y, 256), :] = cross_arrived[...]
    unpack_attention(whole_ref, outs[0:4])
    size = parts.shape[1]
    for r in range(GROUP):
        first = size * (4 * (r % 2) + r // 2)
        whole_ref[first : first + size, :] = parts[r]
    unpack_attention(whole_ref, outs[4:8])
    total = norm_parts[0]
    for r in range(1, GROUP):
        total = total + norm_parts[r]
    gln[...] = total


def whole(shape):
    zeros = (0,) * len(shape)
    return pl.BlockSpec(shape, lambda d, meta: zeros)


def own_row(width):
    return pl.BlockSpec((SEQ, width), lambda d, meta: (meta[0], 0))


ANY = pl.BlockSpec(memory_space=pl.ANY)


def in_hbm(x):
    return pltpu.with_memory_space_constraint(x, pltpu.HBM)


probability_out = (pltpu.HBM((DOCS, 4, FAST_K, FAST_Q), bf16), None, ANY)
probability_scratch = [
    pltpu.VMEM((2, TOGETHER, 4, FAST_K, FAST_Q), bf16),
    pltpu.SemaphoreType.DMA((2,)),
]


class Copies:
    def __init__(self, meta):
        self.first = meta[0] * SEQ
        self.loads = {}
        self.tiles = []
        self.sends = []

    def load(self, stage, source, target, sems, own_row):
        if stage == "tiles":
            first = self.first if own_row else 0
            self.tiles.append((source, target, sems, first))
            return
        if own_row:
            source = source.at[pl.ds(pl.multiple_of(self.first, SEQ), SEQ)]
        copy = pltpu.make_async_copy(source, target, sems[0].at[sems[1], 0])
        self.loads.setdefault(stage, []).append(copy)

    def tile(self, entry, i):
        source, target, (sems, b), first = entry
        rows = pl.ds(pl.multiple_of(first + i * TILE, TILE), TILE)
        return pltpu.make_async_copy(source.at[rows], target.at[rows_of(i)], sems.at[b, i])

    def start(self):
        for copy in self.loads.get("now", []):
            copy.start()
        for i in range(TILES):
            for entry in self.tiles:
                self.tile(entry, i).start()
        for stage in ("soon", "late"):
            for copy in self.loads.get(stage, []):
                copy.start()

    def wait(self, stage):
        for copy in self.loads.pop(stage, []):
            copy.wait()

    def wait_rows(self, i):
        for entry in self.tiles:
            self.tile(entry, i).wait()

    def result(self, source, target, sem, own_row):
        self.sends.append([source, target, sem, own_row, False])

    def send(self, ref, rows=None):
        for entry in self.sends:
            source, target, sem, own_row, _ = entry
            if source is ref:
                entry[4] = True
                first = self.first if own_row else 0
                if rows is None:
                    size = source.shape[0]
                else:
                    source = source.at[rows]
                    first, size = first + rows.start, rows.size
                if rows is not None or own_row:
                    target = target.at[pl.ds(pl.multiple_of(first, size), size)]
                pltpu.make_async_copy(source, target, sem).start()

    def finish(self):
        for stage in list(self.loads):
            self.wait(stage)
        for source, _, _, _, started in self.sends:
            if not started:
                self.send(source)
        for source, target, sem, own_row, _ in self.sends:
            if own_row:
                target = target.at[pl.ds(pl.multiple_of(self.first, SEQ), SEQ)]
            pltpu.make_async_copy(source, target, sem).wait()


def out(shape, dtype, own_row=False):
    return (shape, dtype, own_row)


def call(kernel, name, operands, outs, scratch, flops, token=None):
    arrays = [operands[0][0]]
    in_specs, out_specs, out_shapes = [], [], []
    buffers = []
    loads = []
    for n, (x, how) in enumerate(operands[1:]):
        if isinstance(how, str):
            stage, _, row = how.partition("_")
            shape = ((SEQ,) + x.shape[1:]) if row else x.shape
            loads.append((n, stage, len(buffers), bool(row)))
            buffers.append(pltpu.VMEM(shape, x.dtype))
            arrays.append(in_hbm(x))
            in_specs.append(ANY)
        else:
            arrays.append(x)
            in_specs.append(how)
    results = []
    for n, (shape, dtype, how) in enumerate(outs):
        if isinstance(how, bool):
            results.append((n, len(buffers), how))
            buffers.append(pltpu.VMEM(shape, dtype))
            shape = ((2 * SEQ,) + shape[1:]) if how else shape
            out_shapes.append(pltpu.HBM(shape, dtype))
            out_specs.append(ANY)
        else:
            out_shapes.append(jax.ShapeDtypeStruct(shape, dtype) if dtype else shape)
            out_specs.append(how)
    n_in, n_out = len(in_specs), len(out_specs)
    if token is not None:
        arrays.append(token)
        in_specs.append(whole((8, 128)))
        out_specs.append(whole((8, 128)))
        out_shapes.append(jax.ShapeDtypeStruct((8, 128), f32))

    def body(meta, *refs):
        ins, refs = list(refs[:n_in]), refs[len(in_specs) - n_in + n_in :]
        results_out, refs = list(refs[:n_out]), refs[n_out:]
        if token is not None:
            token_out, refs = refs[0], refs[1:]
            token_out[...] = jnp.zeros_like(token_out)
        bufs, refs = refs[: len(buffers)], refs[len(buffers) :]
        rest = refs[: len(scratch)]
        copies = Copies(meta)
        if buffers:
            sems = refs[len(scratch)]
        for n, stage, b, row in loads:
            copies.load(stage, ins[n], bufs[b], (sems, b), row)
            ins[n] = bufs[b]
        for n, b, row in results:
            copies.result(bufs[b], results_out[n], sems.at[b, 0], row)
            results_out[n] = bufs[b]
        copies.start()
        copies.wait("now")
        if buffers:
            kernel(meta, copies, *ins, *results_out, *rest)
        else:
            kernel(meta, *ins, *results_out, *rest)
        copies.finish()

    moved = sum(x.size * x.dtype.itemsize for x in arrays[1:])
    sems = [pltpu.SemaphoreType.DMA((len(buffers), TILES))] if buffers else []
    return pl.pallas_call(
        body,
        name=name,
        grid_spec=pltpu.PrefetchScalarGridSpec(
            num_scalar_prefetch=1,
            grid=(1,),
            in_specs=in_specs,
            out_specs=out_specs,
            scratch_shapes=buffers + scratch + sems,
        ),
        out_shape=out_shapes,
        compiler_params=pltpu.CompilerParams(
            dimension_semantics=("arbitrary",), vmem_limit_bytes=50 * 1024 * 1024
        ),
        cost_estimate=pl.CostEstimate(
            flops=int(flops), bytes_accessed=int(moved), transcendentals=0
        ),
    )(*arrays)


def simple(kernel, name, meta, operands, outs, scratch=()):
    return pl.pallas_call(
        kernel,
        name=name,
        grid_spec=pltpu.PrefetchScalarGridSpec(
            num_scalar_prefetch=1,
            grid=(1,),
            in_specs=[whole(x.shape) for x in operands],
            out_specs=[whole(shape) for shape, _ in outs],
            scratch_shapes=scratch,
        ),
        out_shape=[jax.ShapeDtypeStruct(shape, dtype) for shape, dtype in outs],
        compiler_params=pltpu.CompilerParams(vmem_limit_bytes=16 * 1024 * 1024),
    )(meta, *operands)


def full(x):
    return (x, whole(x.shape))


def shards(
    query_stream,
    content_stream,
    memory,
    segment_ids,
    source_segments,
    context_rank,
    context_limit,
    padding,
    ln_query_gain,
    ln_query_bias,
    ln_content_gain,
    ln_content_bias,
    self_query,
    self_key,
    self_value,
    self_out,
    ln_cross_gain,
    ln_cross_bias,
    cross_query,
    cross_key,
    cross_value,
    cross_out,
    ln_ffn_gain,
    ln_ffn_bias,
    ffn_in,
    ffn_out,
    cotangent,
):
    core = lax.axis_index("heads") % 2

    def to_core(x):
        return lax.ppermute(x, "heads", [(h, h ^ 1) for h in range(4)])

    hold = lambda *xs: lax.optimization_barrier(xs)

    def to_chip(x):
        return lax.ppermute(x, "heads", [(h, h ^ 2) for h in range(4)])

    row = pl.BlockSpec((1, 8, 128), lambda d, core: (core[0], 0, 0))

    def token_row(x):
        return (in_hbm(x.reshape(2, 8, 128)), row)

    def fixed(x):
        zeros = (0,) * x.ndim
        return (in_hbm(x), pl.BlockSpec(x.shape, lambda d, core: zeros))

    prepared = [
        ((36,), jnp.int32, pl.BlockSpec(memory_space=pltpu.SMEM)),
        ((1, SEQ), f32, whole((1, SEQ))),
        ((1, SEQ), f32, whole((1, SEQ))),
        ((8, D), f32, whole((8, D))),
        ((D, D), bf16, whole((D, D))),
        ((D, D), bf16, whole((D, D))),
    ]
    gains = (
        ln_query_gain,
        ln_query_bias,
        ln_content_gain,
        ln_content_bias,
        ln_cross_gain,
        ln_cross_bias,
        ln_ffn_gain,
        ln_ffn_bias,
    )
    weights = (self_query, self_key, self_value, self_out)
    weights += (cross_query, cross_key, cross_value, cross_out)
    tokens = (segment_ids, source_segments, context_rank, context_limit, padding)
    meta, rank, limit, norms, ws0, wc0 = call(
        prepare,
        "prepare",
        [(jnp.stack([core, lax.axis_index("rows") % GROUP]).astype(jnp.int32), None)]
        + [token_row(x) for x in tokens]
        + [fixed(x.reshape(1, D)) for x in gains]
        + [fixed(x) for x in weights],
        prepared,
        [],
        0,
    )

    ws1 = to_core(ws0)
    ws2 = to_chip(ws0)
    wc1 = to_core(wc0)
    u0, v0 = ffn_in, ffn_out
    meta_in = (meta, None)

    heads_out = [out((SEQ, 256), bf16)] * 4

    def stream_out(dtype, own_row=False):
        return out((SEQ, D), dtype, own_row)

    def now(*xs):
        return [(x, "now") for x in xs]

    def soon(*xs):
        return [(x, "soon") for x in xs]

    def late(*xs):
        return [(x, "late") for x in xs]

    def small(*xs):
        return [(x, whole(x.shape)) for x in xs]

    limits = pltpu.VMEM((SEQ, 128), f32)
    pair_flops = 2 * SEQ * D * 768 + 2 * 2 * 4 * DOCS * FAST_Q * FAST_K * 256

    nq, nc, *first, token = call(
        self_first,
        "self_first",
        [meta_in, (query_stream, "tiles_row"), (content_stream, "tiles_row")]
        + small(rank, limit, norms)
        + now(ws0, ws1),
        [stream_out(bf16), stream_out(bf16)] + heads_out + [probability_out],
        [limits] + probability_scratch,
        pair_flops,
        jnp.zeros((8, 128), f32),
    )
    ws2, wc0, token = hold(ws2, wc0, token)
    ws3 = to_core(ws2)
    wc2 = to_chip(wc0)
    *second_heads, second, ncross, token = call(
        self_second,
        "self_second",
        [meta_in, (query_stream, "late_row")]
        + [(nq, "tiles"), (nc, "tiles")]
        + small(rank, limit, norms)
        + late(ws0, ws1)
        + now(ws2, ws3)
        + late(first[3]),
        heads_out + [probability_out, stream_out(f32), stream_out(bf16)],
        [limits] + probability_scratch,
        pair_flops + 2 * SEQ * D * D,
        token,
    )
    wc2, u0, v0, token = hold(wc2, u0, v0, token)
    wc3 = to_core(wc2)
    u2 = to_chip(u0)
    u1 = to_core(u0)
    *cross_heads, token = call(
        cross_first,
        "cross_first",
        [meta_in, (ncross, "tiles"), (memory, "tiles_row")] + now(wc0, wc1),
        heads_out + [probability_out],
        probability_scratch,
        pair_flops,
        token,
    )
    wc3, u2, v0, token = hold(wc3, u2, v0, token)
    u3 = to_core(u2)
    v2 = to_chip(v0)
    v1 = to_core(v0)
    *cross_heads_second, third, nffn, token = call(
        cross_second,
        "cross_second",
        [meta_in]
        + late(second)
        + [(ncross, "tiles"), (memory, "tiles_row")]
        + small(norms)
        + late(wc0, wc1)
        + now(wc2, wc3)
        + late(cross_heads[3]),
        heads_out + [probability_out, stream_out(f32), stream_out(bf16)],
        probability_scratch,
        pair_flops + 2 * SEQ * D * D,
        token,
    )
    u3, v2, token = hold(u3, v2, token)
    v3 = to_core(v2)
    grads_ln = ((8, D), f32, whole((8, D)))
    placed_output, output, g3, g3_low, gln_ffn, ffn_own, ffn_other, token = call(
        ffn_both,
        "ffn_both",
        [meta_in]
        + [(third, "tiles"), (nffn, "tiles"), (cotangent, "tiles_row")]
        + small(norms)
        + now(u0, u1, u2, u3, v0, v1, v2, v3),
        [
            stream_out(bf16, True),
            stream_out(bf16),
            stream_out(f32),
            stream_out(bf16),
            grads_ln,
            out((1024, D), bf16),
            out((1024, D), bf16),
        ],
        [pltpu.VMEM((SEQ, 1024), bf16), pltpu.VMEM((SEQ, 1024), bf16), pltpu.VMEM((16, D), f32)],
        12 * SEQ * D * 2048,
        token,
    )

    def both_rows(placed_own, others, name):
        count = len(others)
        size = SEQ // 2
        one = pl.BlockSpec((size, D), lambda i, meta: (i, 0))
        block = pl.BlockSpec((size, D), lambda i, meta: (2 * (1 - meta[0]) + i, 0))
        return pl.pallas_call(
            place_rows,
            name=name,
            grid_spec=pltpu.PrefetchScalarGridSpec(
                num_scalar_prefetch=1,
                grid=(2,),
                in_specs=[one] * count + [pl.BlockSpec(memory_space=pl.ANY)] * count,
                out_specs=[block] * count,
            ),
            out_shape=[jax.ShapeDtypeStruct(x.shape, x.dtype) for x in placed_own],
            input_output_aliases={1 + count + n: n for n in range(count)},
        )(meta, *others, *placed_own)

    row_count = lax.axis_size("rows")
    assert row_count % GROUP == 0

    def along_rows(x, s):
        return lax.ppermute(x, "rows", [(r, r ^ s) for r in range(row_count)])

    def to_y(x):
        return along_rows(x, 1)

    def to_z(sends):
        return [along_rows(x, 2 * s) for s, x in enumerate(sends, 1)]

    def rows_out(*sizes):
        return [((n, D), bf16) for n in sizes]

    ffn_other = to_core(ffn_other)
    output_other = to_core(output)

    back_scratch = [pltpu.VMEM((SEQ, 256), bf16)] + [pltpu.VMEM((SEQ, 256), f32)] * 3
    back_scratch += probability_scratch
    pair_out = out((SEQ, 256), bf16)
    packed_outs = [out((D, D), bf16), out((D, D), bf16)]
    back_flops = 2 * SEQ * D * 256 + 4 * 2 * 4 * DOCS * FAST_Q * FAST_K * 256

    def head_inputs(natural, p):
        return soon(*natural) + [(in_hbm(p), ANY)]

    *cross_grads, cross_own, cross_other, token = call(
        functools.partial(attention_back_first, True),
        "cross_back_first",
        [meta_in]
        + [(g3_low, "tiles")]
        + late(ncross)
        + [(memory, "late_row")]
        + small(rank, limit)
        + now(wc0, wc1)
        + head_inputs(cross_heads[0:4], cross_heads[4]),
        [pair_out] * 3 + packed_outs,
        [limits] + back_scratch,
        back_flops + 2 * SEQ * D * 1024,
        token,
    )
    ffn_other, output_other, token = hold(ffn_other, output_other, token)
    ffn_keep, ffn_send = simple(slot_1, "slot_1", meta, [ffn_own, ffn_other], rows_out(512, 512))
    ffn_send, token = hold(ffn_send, token)
    ffn_arrived = to_y(ffn_send)
    cross_other = to_core(cross_other)
    g2, g2_low, placed_mem, grad_mem, gln_cross, token = call(
        cross_back_second,
        "cross_back_second",
        [meta_in]
        + [(g3_low, "tiles")]
        + late(g3, second)
        + small(norms)
        + late(wc0, wc1)
        + now(wc2, wc3)
        + late(*cross_grads)
        + head_inputs(cross_heads_second[0:4], cross_heads_second[4]),
        [stream_out(f32), stream_out(bf16), stream_out(f32, True), stream_out(bf16), grads_ln],
        back_scratch + [pltpu.VMEM((16, D), f32)],
        back_flops + 2 * SEQ * D * 1536,
        token,
    )
    ffn_arrived, cross_other, token = hold(ffn_arrived, cross_other, token)
    ffn_keep, *sends, cross_keep, cross_send = simple(
        slot_2,
        "slot_2",
        meta,
        [ffn_keep, ffn_arrived, cross_own, cross_other],
        rows_out(128, 128, 128, 128, 256, 256),
    )
    ffn_keep, cross_send, token = hold(ffn_keep, cross_send, token)
    ffn_parts = to_z(sends)
    cross_arrived = to_y(cross_send)

    *self_grads, self_own, self_other, token = call(
        functools.partial(attention_back_first, False),
        "self_back_first",
        [meta_in]
        + [(g2_low, "tiles")]
        + late(nq, nc)
        + small(rank, limit)
        + now(ws0, ws1)
        + head_inputs(first[0:4], first[4]),
        [pair_out] * 3 + packed_outs,
        [limits] + back_scratch,
        back_flops + 2 * SEQ * D * 1024,
        token,
    )
    *ffn_parts, cross_arrived, self_other, token = hold(
        *ffn_parts, cross_arrived, self_other, token
    )
    self_other = to_core(self_other)
    ffn_total, cross_keep, *sends, self_keep, self_send = simple(
        slot_3,
        "slot_3",
        meta,
        [ffn_keep, *ffn_parts, cross_keep, cross_arrived, self_own, self_other],
        rows_out(128, 64, 192, 192, 192, 256, 256),
    )
    ffn_total, self_send, grad_mem, token = hold(ffn_total, self_send, grad_mem, token)
    mem_other = to_core(grad_mem)
    self_arrived = to_y(self_send)
    messages = to_z(sends)
    *self_grads_second, token = call(
        self_back_second,
        "self_back_second",
        [meta_in, (g2_low, "tiles")]
        + small(rank, limit)
        + now(ws2, ws3)
        + head_inputs(second_heads[0:4], second_heads[4]),
        [pair_out] * 3,
        [limits] + back_scratch,
        back_flops,
        token,
    )
    output_other, mem_other, token = hold(output_other, mem_other, token)
    out_both, grad_mem_both = both_rows(
        [placed_output, placed_mem], [output_other, mem_other], "place_early"
    )
    *messages, self_arrived, out_both, token = hold(*messages, self_arrived, out_both, token)
    ffn_half, cross_total, self_keep, *sends = simple(
        slot_4,
        "slot_4",
        meta,
        [ffn_total, *messages, cross_keep, self_keep, self_arrived],
        rows_out(512, 64, 64, 128, 128, 128),
    )
    cross_total, ffn_half, token = hold(cross_total, ffn_half, token)
    messages = to_z(sends)
    ffn_arrived = to_y(ffn_half)
    placed_q, placed_c, gq, gc, gln_self, token = call(
        self_back_finish,
        "self_back_finish",
        [meta_in, (g2, "tiles"), (query_stream, "tiles_row"), (content_stream, "tiles_row")]
        + small(norms)
        + now(ws0, ws1, ws2, ws3)
        + [(x, "tiles") for x in self_grads + self_grads_second],
        [stream_out(f32, True), stream_out(f32, True), stream_out(bf16), stream_out(bf16), grads_ln],
        [pltpu.VMEM((32, D), f32)],
        2 * SEQ * D * 1536,
        token,
    )
    gln = jnp.concatenate([gln_self[0:4], gln_cross[0:2], gln_ffn[0:2]], axis=0)
    *messages, ffn_arrived, gln_ffn = hold(*messages, ffn_arrived, gln_ffn)
    last_send, cross_half = simple(
        slot_5,
        "slot_5",
        meta,
        [self_keep, cross_total, *messages],
        [((GROUP, 64, D), bf16), ((256, D), bf16)],
    )
    groups = None
    if row_count > GROUP:
        groups = [list(range(r, r + GROUP)) for r in range(0, row_count, GROUP)]
    def gather(x):
        return lax.all_to_all(x, "rows", 0, 0, axis_index_groups=groups)

    last_parts = gather(last_send)
    cross_arrived = to_y(cross_half)
    gln, cross_half = hold(gln, cross_half)
    (norm_send,) = simple(
        join_norms, "join_norms", meta, [gln, to_core(gln)], [((GROUP, 8, D), f32)]
    )
    norm_parts = gather(norm_send)

    def over_groups(totals):
        if row_count == GROUP:
            return totals
        groups = [list(range(r, row_count, GROUP)) for r in range(GROUP)]
        return lax.psum(totals, "rows", axis_index_groups=groups)

    gq_both, gc_both = both_rows([placed_q, placed_c], [to_core(gq), to_core(gc)], "place_late")

    grad_ffn_in, grad_ffn_out = simple(
        unpack_ffn,
        "unpack_ffn",
        meta,
        [ffn_half, ffn_arrived],
        [((D, D), f32)] * 2,
        [pltpu.VMEM((2 * D, D), bf16)],
    )
    attention_outs = [((512, 128), f32)] * 3 + [((128, 512), f32)]
    cross_arrived, gq_both, grad_ffn_in = hold(cross_arrived, gq_both, grad_ffn_in)
    *parts, gln = simple(
        unpack_rest,
        "unpack_rest",
        meta,
        [cross_half, cross_arrived, last_parts, norm_parts],
        attention_outs * 2 + [((8, D), f32)],
        [pltpu.VMEM((D, D), bf16)],
    )
    grad_cross_parts, grad_self_parts = parts[:4], parts[4:]
    grad_ffn_in, grad_ffn_out, grad_cross_parts, grad_self_parts, gln = over_groups(
        (grad_ffn_in, grad_ffn_out, grad_cross_parts, grad_self_parts, gln)
    )
    return (
        out_both,
        gq_both,
        gc_both,
        grad_mem_both,
        gln[0],
        gln[1],
        gln[2],
        gln[3],
        *grad_self_parts,
        gln[4],
        gln[5],
        *grad_cross_parts,
        gln[6],
        gln[7],
        grad_ffn_in,
        grad_ffn_out,
    )


def solution(mesh):
    assert mesh.shape["heads"] == 4
    row_spec = P("rows", None)
    flat = P("rows")
    by_column = P(None, "heads")
    by_row = P("heads", None)
    attention = (by_column, by_column, by_column, by_row)
    in_specs = (
        (row_spec,) * 3
        + (flat,) * 5
        + (P(),) * 4
        + attention
        + (P(),) * 2
        + attention
        + (P(),) * 2
        + (by_column, by_row, row_spec)
    )
    out_specs = (
        (row_spec,) * 4
        + (P(),) * 4
        + attention
        + (P(),) * 2
        + attention
        + (P(),) * 2
        + (by_column, by_row)
    )
    return jax.shard_map(shards, mesh=mesh, in_specs=in_specs, out_specs=out_specs, check_vma=False)
```

```python
import functools

import jax
import jax.numpy as jnp
from jax import lax
from jax.experimental import pallas as pl
from jax.experimental.pallas import tpu as pltpu
from jax.sharding import PartitionSpec as P

HEAD_DIM = 64
SEQ = 1024
DOCS = 8
D = 512
TILE = 256
TILES = SEQ // TILE
FAST_Q = 256
FAST_K = 208
LONG_Q = 128
LONG_K = 640

norm_eps = 1e-05
masked_score = -1e30
hidden_rank = 1e6
gelu_root = 0.7978845608028654
gelu_cube = 0.044715

f32 = jnp.float32
bf16 = jnp.bfloat16


def dot(a, b):
    return lax.dot_general(a, b, (((1,), (0,)), ((), ())), preferred_element_type=f32)


def dot_nt(a, b):
    return lax.dot_general(a, b, (((1,), (1,)), ((), ())), preferred_element_type=f32)


def dot_tn(a, b):
    return lax.dot_general(a, b, (((0,), (0,)), ((), ())), preferred_element_type=f32)


def lanes(parts):
    return jnp.concatenate(parts, axis=1)


NORM_ROWS = 32


def layer_norm(values, gain, shift):
    def piece(part):
        part = part.astype(f32)
        centre = part - jnp.mean(part, axis=-1, keepdims=True)
        spread = jnp.mean(centre * centre, axis=-1, keepdims=True)
        return (centre * lax.rsqrt(spread + norm_eps) * gain + shift).astype(bf16)

    return by_pieces(piece, NORM_ROWS, 0, values)


def eight_rows(values):
    return sum(values[8 * i : 8 * i + 8] for i in range(1, values.shape[0] // 8)) + values[0:8]


def norm_backward(values, gain, grad, sums_ref, first):
    sums = []

    def piece(part, grad_part):
        part = part.astype(f32)
        centre = part - jnp.mean(part, axis=-1, keepdims=True)
        spread = jnp.mean(centre * centre, axis=-1, keepdims=True)
        scale = lax.rsqrt(spread + norm_eps)
        xhat = centre * scale
        eg = grad_part * gain
        mean_eg = jnp.mean(eg, axis=-1, keepdims=True)
        mean_egx = jnp.mean(eg * xhat, axis=-1, keepdims=True)
        sums.append((eight_rows(grad_part * xhat), eight_rows(grad_part)))
        return scale * (eg - mean_eg - xhat * mean_egx)

    result = by_pieces(piece, NORM_ROWS, 0, values, grad)
    for n, parts in enumerate(zip(*sums)):
        sums_ref[first + 8 * n : first + 8 * n + 8, :] += sum(parts[1:], parts[0])
    return result


def add_sums(sums_ref, gln_ref, count):
    gln_ref[...] = jnp.zeros_like(gln_ref)
    for n in range(count):
        gln_ref[n : n + 1, :] = jnp.sum(sums_ref[8 * n : 8 * n + 8, :], axis=0, keepdims=True)


def by_pieces(work, size, axis, *arrays):
    count = arrays[0].shape[axis] // size
    pieces = []
    for i in range(count):
        cut = (slice(size * i, size * i + size),)
        cut = cut if axis == 0 else (slice(None),) + cut
        pieces.append(work(*[x[cut] for x in arrays]))
    if not isinstance(pieces[0], tuple):
        return jnp.concatenate(pieces, axis=axis)
    return tuple(jnp.concatenate(parts, axis=axis) for parts in zip(*pieces))


def rows_of(i, size=TILE):
    return pl.ds(pl.multiple_of(i * size, size), size)


def w_query(ref):
    return ref[:, 0:128]


def w_key(ref):
    return ref[:, 128:256]


def w_value(ref):
    return ref[:, 256:384]


def w_out(ref):
    return lanes([ref[128 * j : 128 * j + 128, 384:512] for j in range(4)])


def half_masks():
    place = lax.broadcasted_iota(jnp.int32, (1, 128), 1)
    low = jnp.where(place < HEAD_DIM, 1.0, 0.0).astype(f32)
    return (low.astype(bf16), (1.0 - low).astype(bf16))


def doc_bounds(meta, d, source):
    base = 17 if source else 1
    return meta[base + d], meta[base + 8 + d]


def window_of(first, limit):
    return pl.multiple_of(jnp.minimum((first // 16) * 16, limit), 16)


def key_bias(ks, ke, k0, width):
    place = k0 + lax.broadcasted_iota(jnp.int32, (width, 128), 0)
    return jnp.where((place >= ks) & (place < ke), 0.0, masked_score)


def make_bias(rank_ref, limit_ref, ks, ke, q0, k0, span, width):
    if rank_ref is None:
        return lanes([key_bias(ks, ke, k0, width)] * (span // 128))
    place = k0 + lax.broadcasted_iota(jnp.int32, (width, 128), 0)
    ranks = rank_ref[pl.ds(k0, width), :]
    ranks = jnp.where((place < ks + 2) & (ranks < hidden_rank), -1.0, ranks)
    ranks = jnp.where((place >= ks) & (place < ke), ranks, hidden_rank)
    limits = jnp.broadcast_to(limit_ref[...], (8, SEQ))
    limits = pltpu.roll(limits, lax.rem(SEQ - q0, SEQ), 1)[0:1, 0:span]
    row = k0 + lax.broadcasted_iota(jnp.int32, (width, span), 0)
    column = q0 + lax.broadcasted_iota(jnp.int32, (width, span), 1)
    seen = (lanes([ranks] * (span // 128)) < limits) & (row != column)
    return jnp.where(seen, 0.0, masked_score)


TOGETHER = 4
STEPS = DOCS // TOGETHER


LAG = 2


def interleave(items):
    items = [list(phases) for phases in items]
    depth = max(len(phases) for phases in items)
    results = [None] * len(items)
    for tick in range(len(items) + LAG * (depth - 1)):
        for phase in range(depth):
            n = tick - LAG * phase
            if 0 <= n < len(items) and phase < len(items[n]):
                run = items[n][phase]
                results[n] = run() if phase == 0 else run(results[n])
    return results


def by_halves(pairs, phases):
    shared = [{} for _ in range(pairs)]
    return [phases(n, a, shared[n]) for n in range(pairs) for a in range(2)]


def is_fast(meta, cross):
    return meta[34 if cross else 33] == 1


def both_heads(x, masks):
    return jnp.concatenate([x * masks[0], x * masks[1]], axis=0)


def pair_scores(queries, keys, masks):
    return dot_nt(both_heads(keys, masks), queries)


def raised(scores, bias):
    def piece(part, bias_part):
        part = part + bias_part
        return jnp.exp((part - jnp.max(part, axis=0, keepdims=True)).astype(bf16))

    return by_pieces(piece, 128, 1, scores, bias)


def weighted_values(values, parts):
    width = values.shape[1]
    mixed = []
    shares = []
    for a, part in enumerate(parts):
        rows = jnp.concatenate([values[64 * a : 64 * a + 64], jnp.ones((16, width), bf16)], axis=0)
        sums = dot(rows, part)
        share = 1.0 / sums[64:65]
        mixed.append(sums[:64] * share)
        shares.append(part * share.astype(bf16))
    return jnp.concatenate(mixed, axis=0).astype(bf16), shares


def pair_gradient(rows, parts):
    across = jnp.transpose(rows)
    halves = [dot(across[64 * a : 64 * a + 64], part) for a, part in enumerate(parts)]
    return jnp.transpose((jnp.concatenate(halves, axis=0) * HEAD_DIM**-0.5).astype(bf16))


def for_docs(meta, cross, run, before, after):
    @pl.when(is_fast(meta, cross))
    def _():
        def step(i, carry):
            slot = lax.rem(i, 2)
            before(i, slot)
            items = []
            for place in range(TOGETHER):
                d = TOGETHER * i + place
                ts, te = doc_bounds(meta, d, False)
                ks, ke = doc_bounds(meta, d, cross)
                q0 = window_of(ts, SEQ - FAST_Q)
                k0 = window_of(ks, SEQ - FAST_K)
                items += run(d, slot, place, q0, k0, FAST_Q, FAST_K, ts, te, ks, ke, True)
            interleave(items)
            after(i, slot)
            return carry

        lax.fori_loop(0, STEPS, step, 0)

    @pl.when(jnp.logical_not(is_fast(meta, cross)))
    def _():
        def doc(d, carry):
            ts, te = doc_bounds(meta, d, False)
            ks, ke = doc_bounds(meta, d, cross)
            base = (ts // 16) * 16
            k0 = window_of(ks, SEQ - LONG_K)

            def chunk(i, carry):
                lower = base + i * LONG_Q
                q0 = pl.multiple_of(jnp.minimum(lower, SEQ - LONG_Q), 16)
                low = jnp.maximum(ts, lower)
                high = jnp.minimum(te, lower + LONG_Q)
                interleave(run(d, None, None, q0, k0, LONG_Q, LONG_K, low, high, ks, ke, False))
                return carry

            return lax.fori_loop(0, (te - base + LONG_Q - 1) // LONG_Q, chunk, carry)

        lax.fori_loop(0, DOCS, doc, 0)


def attend_docs(meta, cross, rank_ref, limit_ref, halves, p_ref, p_buf, p_sem):
    pairs = 2 * len(halves)
    masks = half_masks()

    def save(i, slot):
        return pltpu.make_async_copy(p_buf.at[slot], p_ref.at[pl.ds(TOGETHER * i, TOGETHER)], p_sem.at[slot])

    def before(i, slot):
        @pl.when(i >= 2)
        def _():
            save(i - 2, slot).wait()

    def after(i, slot):
        save(i, slot).start()

    def run(d, slot, place, q0, k0, span, width, low, high, ks, ke, fast):
        bias = make_bias(rank_ref, limit_ref, ks, ke, q0, k0, span, width)
        row = q0 + lax.broadcasted_iota(jnp.int32, (span, 128), 0)
        inside = (row >= low) & (row < high)

        def phases(n):
            q_ref, k_ref, v_ref, mixed_ref = halves[n // 2]
            cols = slice(128 * (n % 2), 128 * (n % 2) + 128)

            def score():
                return pair_scores(q_ref[pl.ds(q0, span), cols], k_ref[pl.ds(k0, width), cols], masks)

            def weigh(scores):
                return [raised(scores[width * a : width * a + width], bias) for a in range(2)]

            def mix(parts):
                values = jnp.transpose(v_ref[pl.ds(k0, width), cols])
                mixed, parts = weighted_values(values, parts)
                if fast:
                    for a in range(2):
                        p_buf[slot, place, 2 * n + a] = parts[a]
                mixed = jnp.transpose(mixed).astype(f32)
                old = mixed_ref[pl.ds(q0, span), cols].astype(f32)
                mixed_ref[pl.ds(q0, span), cols] = jnp.where(inside, mixed, old).astype(bf16)

            return score, weigh, mix

        return [phases(n) for n in range(pairs)]

    for_docs(meta, cross, run, before, after)

    @pl.when(is_fast(meta, cross))
    def _():
        for i in range(STEPS - 2, STEPS):
            save(i, i % 2).wait()


def load_step(load, i, slot):
    p_ref, p_buf, p_sem = load
    return pltpu.make_async_copy(p_ref.at[pl.ds(TOGETHER * i, TOGETHER)], p_buf.at[slot], p_sem.at[slot])


def start_load(meta, cross, load):
    @pl.when(is_fast(meta, cross))
    def _():
        load_step(load, 0, 0).start()


def attend_docs_back(
    meta, cross, rank_ref, limit_ref, q_ref, k_ref, v_ref, mixed_ref, dm_ref,
    dq_ref, dk_ref, dv_ref, load,
):
    pairs = q_ref.shape[1] // 128
    masks = half_masks()
    p_buf = load[1]

    def before(i, slot):
        @pl.when(i + 1 < STEPS)
        def _():
            load_step(load, i + 1, 1 - slot).start()

        load_step(load, i, slot).wait()

    def after(i, slot):
        pass

    def run(d, slot, place, q0, k0, span, width, low, high, ks, ke, fast):
        row = q0 + lax.broadcasted_iota(jnp.int32, (span, 128), 0)
        inside = jnp.where((row >= low) & (row < high), 1.0, 0.0).astype(bf16)
        ones = jnp.ones((width, 128), bf16)
        if not fast:
            bias = make_bias(rank_ref, limit_ref, ks, ke, q0, k0, span, width)

        def phases(n):
            cols = slice(128 * n, 128 * n + 128)

            def differ():
                values = v_ref[pl.ds(k0, width), cols]
                mixed = mixed_ref[pl.ds(q0, span), cols]
                grad = dm_ref[pl.ds(q0, span), cols] * inside
                left = lanes([grad, -(grad * mixed)])
                right = both_heads(lanes([values, ones]), [lanes([m, m]) for m in masks])
                return grad, dot_nt(right, left)

            def slope(state):
                grad, delta = state
                if fast:
                    parts = [p_buf[slot, place, 2 * n + a] for a in range(2)]
                else:
                    queries = q_ref[pl.ds(q0, span), cols]
                    keys = k_ref[pl.ds(k0, width), cols]
                    scores = pair_scores(queries, keys, masks)
                    parts = [raised(scores[width * a : width * a + width], bias) for a in range(2)]
                    parts = weighted_values(jnp.transpose(v_ref[pl.ds(k0, width), cols]), parts)[1]
                slopes = [
                    by_pieces(
                        lambda part, change: part * change.astype(bf16),
                        16,
                        0,
                        parts[a],
                        delta[width * a : width * a + width],
                    )
                    for a in range(2)
                ]
                return grad, parts, slopes

            def spread(state):
                grad, parts, slopes = state
                queries = q_ref[pl.ds(q0, span), cols]
                dk = dv = None
                for a in range(2):
                    dk_a = dot(slopes[a], queries * masks[a])
                    dv_a = dot(parts[a], grad * masks[a])
                    dk = dk_a if dk is None else dk + dk_a
                    dv = dv_a if dv is None else dv + dv_a
                dq = pair_gradient(k_ref[pl.ds(k0, width), cols], slopes)
                dq_ref[pl.ds(q0, span), cols] += dq.astype(f32)
                dk_ref[pl.ds(k0, width), cols] += dk
                dv_ref[pl.ds(k0, width), cols] += dv

            return differ, slope, spread

        return [phases(n) for n in range(pairs)]

    for_docs(meta, cross, run, before, after)


def spread_ranks(rank_row_ref, rank_ref):
    rank_ref[...] = jnp.transpose(jnp.broadcast_to(rank_row_ref[...], (128, SEQ)))


def prepare(
    core, seg_ref, src_ref, rank_ref, limit_ref, pad_ref,
    n0, n1, n2, n3, n4, n5, n6, n7, sq, sk, sv, so, cq, ck, cv, co,
    meta_ref, ranks_ref, limits_ref, norms_ref, ws_ref, wc_ref,
):
    meta_ref[0] = core[0]
    meta_ref[35] = core[1]
    for base, ref in ((1, seg_ref), (17, src_ref)):
        ids = ref[0]
        meta_ref[base] = 0
        meta_ref[base + 15] = SEQ
        for d in range(1, DOCS):
            cut = jnp.sum(jnp.where(ids < d, 1.0, 0.0)).astype(jnp.int32)
            meta_ref[base + d] = cut
            meta_ref[base + 7 + d] = cut
    for place, base in ((33, 1), (34, 17)):
        fast = jnp.int32(1)
        for d in range(DOCS):
            q0 = window_of(meta_ref[1 + d], SEQ - FAST_Q)
            k0 = window_of(meta_ref[base + d], SEQ - FAST_K)
            fits = (meta_ref[9 + d] - q0 <= FAST_Q) & (meta_ref[base + 8 + d] - k0 <= FAST_K)
            fast = fast & fits.astype(jnp.int32)
        meta_ref[place] = fast
    ranks = jnp.where(pad_ref[0] != 0, hidden_rank, rank_ref[0].astype(f32))
    limits = limit_ref[0].astype(f32)
    for i in range(8):
        ranks_ref[0:1, 128 * i : 128 * i + 128] = ranks[i : i + 1]
        limits_ref[0:1, 128 * i : 128 * i + 128] = limits[i : i + 1]
    for i, ref in enumerate((n0, n1, n2, n3, n4, n5, n6, n7)):
        norms_ref[i : i + 1, :] = ref[...]
    for to, parts, out in ((ws_ref, (sq, sk, sv), so), (wc_ref, (cq, ck, cv), co)):
        for i, part in enumerate(parts):
            to[:, 128 * i : 128 * i + 128] = part[...]
        for j in range(4):
            to[128 * j : 128 * j + 128, 384:512] = out[:, 128 * j : 128 * j + 128]


def self_first(
    meta, io, xq_ref, xc_ref, rank_row_ref, limit_ref, norms_ref, w0_ref, w1_ref,
    nq_ref, nc_ref, q_ref, k_ref, v_ref, mixed_ref, p_ref, rank_ref, p_buf, p_sem,
):

    spread_ranks(rank_row_ref, rank_ref)
    wq = lanes([w_query(w0_ref), w_query(w1_ref)])
    wkv = lanes([w_key(w0_ref), w_key(w1_ref), w_value(w0_ref), w_value(w1_ref)])

    def tile(i, carry):
        rows = rows_of(i)
        io.wait_rows(i)
        nq = layer_norm(xq_ref[rows, :], norms_ref[0:1], norms_ref[1:2])
        nc = layer_norm(xc_ref[rows, :], norms_ref[2:3], norms_ref[3:4])
        nq_ref[rows, :] = nq
        nc_ref[rows, :] = nc
        q_ref[rows, :] = (dot(nq, wq) * (HEAD_DIM**-0.5)).astype(bf16)
        kv = dot(nc, wkv).astype(bf16)
        k_ref[rows, :] = kv[:, :256]
        v_ref[rows, :] = kv[:, 256:]
        return carry

    lax.fori_loop(0, TILES, tile, 0)

    for ref in (nq_ref, nc_ref, q_ref, k_ref, v_ref):
        io.send(ref)
    attend_docs(meta, False, rank_ref, limit_ref, [(q_ref, k_ref, v_ref, mixed_ref)], p_ref, p_buf, p_sem)


def self_second(
    meta, io, xq_ref, nq_ref, nc_ref, rank_row_ref, limit_ref, norms_ref, w0_ref, w1_ref, w2_ref, w3_ref,
    mixed_first_ref,
    q_ref, k_ref, v_ref, mixed_ref, p_ref, second_ref, ncross_ref, rank_ref, p_buf, p_sem,
):

    spread_ranks(rank_row_ref, rank_ref)
    wq = lanes([w_query(w2_ref), w_query(w3_ref)])
    wkv = lanes([w_key(w2_ref), w_key(w3_ref), w_value(w2_ref), w_value(w3_ref)])

    def tile(i, carry):
        rows = rows_of(i)
        io.wait_rows(i)
        q_ref[rows, :] = (dot(nq_ref[rows, :], wq) * (HEAD_DIM**-0.5)).astype(bf16)
        kv = dot(nc_ref[rows, :], wkv).astype(bf16)
        k_ref[rows, :] = kv[:, :256]
        v_ref[rows, :] = kv[:, 256:]
        return carry

    lax.fori_loop(0, TILES, tile, 0)

    for ref in (q_ref, k_ref, v_ref):
        io.send(ref)
    attend_docs(meta, False, rank_ref, limit_ref, [(q_ref, k_ref, v_ref, mixed_ref)], p_ref, p_buf, p_sem)

    io.send(mixed_ref)
    io.wait("late")
    out_first = jnp.concatenate([w_out(w0_ref), w_out(w1_ref)], axis=0)
    out_second = jnp.concatenate([w_out(w2_ref), w_out(w3_ref)], axis=0)

    def tile(i, carry):
        rows = rows_of(i)
        branch = dot(mixed_first_ref[rows, :], out_first) + dot(mixed_ref[rows, :], out_second)
        second = xq_ref[rows, :].astype(f32) + branch
        second_ref[rows, :] = second
        io.send(second_ref, rows)
        ncross_ref[rows, :] = layer_norm(second, norms_ref[4:5], norms_ref[5:6])
        io.send(ncross_ref, rows)
        return carry

    lax.fori_loop(0, TILES, tile, 0)


def project_cross(io, ncross_ref, memory_ref, weights, q_ref, k_ref, v_ref):
    wq = lanes([w_query(w) for w in weights])
    wkv = lanes([w_key(w) for w in weights] + [w_value(w) for w in weights])

    def tile(i, carry):
        rows = rows_of(i)
        io.wait_rows(i)
        q_ref[rows, :] = (dot(ncross_ref[rows, :], wq) * (HEAD_DIM**-0.5)).astype(bf16)
        kv = dot(memory_ref[rows, :], wkv).astype(bf16)
        k_ref[rows, :] = kv[:, :256]
        v_ref[rows, :] = kv[:, 256:]
        return carry

    lax.fori_loop(0, TILES, tile, 0)
    for ref in (q_ref, k_ref, v_ref):
        io.send(ref)


def cross_first(
    meta, io, ncross_ref, memory_ref, w0_ref, w1_ref,
    q_ref, k_ref, v_ref, mixed_ref, p_ref, p_buf, p_sem,
):
    project_cross(io, ncross_ref, memory_ref, (w0_ref, w1_ref), q_ref, k_ref, v_ref)
    attend_docs(meta, True, None, None, [(q_ref, k_ref, v_ref, mixed_ref)], p_ref, p_buf, p_sem)


def cross_second(
    meta, io, second_ref, ncross_ref, memory_ref, norms_ref, w0_ref, w1_ref, w2_ref, w3_ref,
    mixed_first_ref,
    q_ref, k_ref, v_ref, mixed_ref, p_ref, third_ref, nffn_ref, p_buf, p_sem,
):
    project_cross(io, ncross_ref, memory_ref, (w2_ref, w3_ref), q_ref, k_ref, v_ref)
    attend_docs(meta, True, None, None, [(q_ref, k_ref, v_ref, mixed_ref)], p_ref, p_buf, p_sem)
    io.send(mixed_ref)
    io.wait("late")
    out_first = jnp.concatenate([w_out(w0_ref), w_out(w1_ref)], axis=0)
    out_second = jnp.concatenate([w_out(w2_ref), w_out(w3_ref)], axis=0)

    def tile(i, carry):
        rows = rows_of(i)
        branch = dot(mixed_first_ref[rows, :], out_first) + dot(mixed_ref[rows, :], out_second)
        third = second_ref[rows, :] + branch
        third_ref[rows, :] = third
        io.send(third_ref, rows)
        nffn_ref[rows, :] = layer_norm(third, norms_ref[6:7], norms_ref[7:8])
        io.send(nffn_ref, rows)
        return carry

    lax.fori_loop(0, TILES, tile, 0)


def ffn_both(
    meta, io, third_ref, nffn_ref, cot_ref, norms_ref, u0_ref, u1_ref, u2_ref, u3_ref,
    w0_ref, w1_ref, w2_ref, w3_ref,
    placed_ref, out_ref, g3_ref, g3_low_ref, gln_ref, own_ref, other_ref, hidden_ref, before_ref, sums_ref,
):
    sums_ref[...] = jnp.zeros_like(sums_ref)
    in_refs = (u0_ref, u1_ref, u2_ref, u3_ref)
    w_refs = (w0_ref, w1_ref, w2_ref, w3_ref)

    def tile(i, carry):
        rows = rows_of(i)
        io.wait_rows(i)
        nffn = nffn_ref[rows, :]
        cot = cot_ref[rows, :]
        outs = []
        grads = []

        def phases(g, c, group):
            w_in = in_refs[g]
            w_out_rows = w_refs[g]
            cols = slice(256 * c, 256 * c + 256)

            def enter():
                return dot(nffn, w_in[:, cols]), dot_nt(cot, w_out_rows[cols, :])

            def bend(state):
                def piece(x, grad_hidden):
                    square = x * x
                    argument = x * (gelu_root + (gelu_root * gelu_cube) * square)
                    half = 0.5 + 0.5 * jnp.tanh(argument.astype(bf16))
                    x = x.astype(bf16)
                    square = square.astype(bf16)
                    value = x * half
                    rise = 2.0 * gelu_root + (6.0 * gelu_root * gelu_cube) * square
                    slope = half + value * (1.0 - half) * rise
                    return value, grad_hidden.astype(bf16) * slope

                hidden, grad_before = by_pieces(piece, 32, 0, *state)
                if g < 2:
                    place = slice(512 * g + 256 * c, 512 * g + 256 * c + 256)
                    hidden_ref[rows, place] = hidden
                    before_ref[rows, place] = grad_before
                group[c] = hidden, grad_before

            def leave(_):
                if c == 1:
                    outs.append(dot(lanes([group[0][0], group[1][0]]), w_out_rows[...]))

            def leave_back(_):
                if c == 1:
                    grads.append(dot_nt(lanes([group[0][1], group[1][1]]), w_in[...]))

            return enter, bend, leave, leave_back

        interleave(by_halves(4, phases))
        third = third_ref[rows, :]
        result = (third + ((outs[0] + outs[1]) + (outs[2] + outs[3]))).astype(bf16)
        out_ref[rows, :] = result
        placed_ref[rows, :] = result
        grad_normed = (grads[0] + grads[1]) + (grads[2] + grads[3])
        grad_norm = norm_backward(third, norms_ref[6:7], grad_normed, sums_ref, 0)
        g3 = cot.astype(f32) + grad_norm
        g3_ref[rows, :] = g3
        g3_low_ref[rows, :] = g3.astype(bf16)
        for ref in (out_ref, placed_ref, g3_ref, g3_low_ref):
            io.send(ref, rows)
        return carry

    lax.fori_loop(0, TILES, tile, 0)
    add_sums(sums_ref, gln_ref, 2)
    part = dot_tn(nffn_ref[...], before_ref[...])
    own_ref[0:512, :] = part[:, 0:512].astype(bf16)
    other_ref[0:512, :] = part[:, 512:1024].astype(bf16)
    io.send(own_ref, pl.ds(0, 512))
    io.send(other_ref, pl.ds(0, 512))
    part = dot_tn(hidden_ref[...], cot_ref[...])
    own_ref[512:1024, :] = part[0:512].astype(bf16)
    other_ref[512:1024, :] = part[512:1024].astype(bf16)
    io.send(own_ref, pl.ds(512, 512))
    io.send(other_ref, pl.ds(512, 512))


def back_start(io, g_ref, mixed_ref, w_refs, dm_ref, dq_ref, dk_ref, dv_ref):
    out_rows = jnp.concatenate([w_out(w) for w in w_refs], axis=0)

    def tile(i, carry):
        rows = rows_of(i)
        io.wait_rows(i)
        dm_ref[rows, :] = dot_nt(g_ref[rows, :], out_rows).astype(bf16)
        zeros = jnp.zeros((TILE, 256), f32)
        dq_ref[rows, :] = zeros
        dk_ref[rows, :] = zeros
        dv_ref[rows, :] = zeros
        return carry

    lax.fori_loop(0, TILES, tile, 0)


def attention_back_first(
    cross, meta, io, g_ref, nq_ref, nkv_ref, rank_row_ref, limit_ref, w0_ref, w1_ref,
    q_ref, k_ref, v_ref, mixed_ref, p_ref,
    dq_ref, dk_ref, dv_ref, own_ref, other_ref,
    rank_ref, dm_ref, dqs_ref, dks_ref, dvs_ref, p_buf, p_sem,
):
    load = (p_ref, p_buf, p_sem)
    start_load(meta, cross, load)
    if not cross:
        spread_ranks(rank_row_ref, rank_ref)
    back_start(io, g_ref, mixed_ref, (w0_ref, w1_ref), dm_ref, dqs_ref, dks_ref, dvs_ref)

    io.wait("soon")
    attend_docs_back(
        meta, cross, None if cross else rank_ref, limit_ref, q_ref, k_ref, v_ref, mixed_ref,
        dm_ref, dqs_ref, dks_ref, dvs_ref, load,
    )

    dq_ref[...] = dqs_ref[...].astype(bf16)
    dk_ref[...] = dks_ref[...].astype(bf16)
    dv_ref[...] = dvs_ref[...].astype(bf16)
    for ref in (dq_ref, dk_ref, dv_ref):
        io.send(ref)
    io.wait("late")
    nq = nq_ref[...]
    nkv = nkv_ref[...]
    kv = dot_tn(nkv, lanes([dk_ref[...], dv_ref[...]]))
    for n, part in enumerate((dot_tn(nq, dq_ref[...]), kv[:, 0:256], kv[:, 256:512])):
        own_ref[:, 128 * n : 128 * n + 128] = part[:, :128].astype(bf16)
        other_ref[:, 128 * n : 128 * n + 128] = part[:, 128:].astype(bf16)
    part = dot_tn(mixed_ref[...], g_ref[...])
    for j in range(4):
        rows = slice(128 * j, 128 * j + 128)
        own_ref[rows, 384:512] = part[:128, rows].astype(bf16)
        other_ref[rows, 384:512] = part[128:, rows].astype(bf16)


def back_second_docs(
    cross, meta, io, g_ref, rank_row_ref, limit_ref, w_refs, q_ref, k_ref, v_ref, mixed_ref, p_ref,
    rank_ref, dm_ref, dqs_ref, dks_ref, dvs_ref, p_buf, p_sem,
):
    load = (p_ref, p_buf, p_sem)
    start_load(meta, cross, load)
    if not cross:
        spread_ranks(rank_row_ref, rank_ref)
    back_start(io, g_ref, mixed_ref, w_refs, dm_ref, dqs_ref, dks_ref, dvs_ref)

    io.wait("soon")
    attend_docs_back(
        meta, cross, None if cross else rank_ref, limit_ref, q_ref, k_ref, v_ref, mixed_ref,
        dm_ref, dqs_ref, dks_ref, dvs_ref, load,
    )


def stream_grads(rows, first, second, firsts, seconds):
    dq, dk, dv = first
    dq2, dk2, dv2 = (ref[rows, :].astype(bf16) for ref in second)
    w0, w1 = firsts
    w2, w3 = seconds
    grad_q = dot_nt(dq[rows, :], lanes([w_query(w0), w_query(w1)])) + dot_nt(
        dq2, lanes([w_query(w2), w_query(w3)])
    )
    kv = lanes([dk[rows, :], dv[rows, :]])
    kv2 = lanes([dk2, dv2])
    grad_kv = dot_nt(kv, lanes([w_key(w0), w_key(w1), w_value(w0), w_value(w1)])) + dot_nt(
        kv2, lanes([w_key(w2), w_key(w3), w_value(w2), w_value(w3)])
    )
    return grad_q, grad_kv


def cross_back_second(
    meta, io, g_low_ref, g_ref, second_ref, norms_ref, w0_ref, w1_ref, w2_ref, w3_ref,
    dq_ref, dk_ref, dv_ref, q_ref, k_ref, v_ref, mixed_ref, p_ref,
    g2_ref, g2_low_ref, placed_ref, gmem_ref, gln_ref,
    dm_ref, dqs_ref, dks_ref, dvs_ref, p_buf, p_sem, sums_ref,
):
    back_second_docs(
        True, meta, io, g_low_ref, None, None, (w2_ref, w3_ref), q_ref, k_ref, v_ref, mixed_ref, p_ref,
        None, dm_ref, dqs_ref, dks_ref, dvs_ref, p_buf, p_sem,
    )

    io.wait("late")
    sums_ref[...] = jnp.zeros_like(sums_ref)

    def tile(i, carry):
        rows = rows_of(i)
        grad_q, grad_kv = stream_grads(
            rows,
            (dq_ref, dk_ref, dv_ref),
            (dqs_ref, dks_ref, dvs_ref),
            (w0_ref, w1_ref),
            (w2_ref, w3_ref),
        )
        low_kv = grad_kv.astype(bf16)
        gmem_ref[rows, :] = low_kv
        placed_ref[rows, :] = low_kv.astype(f32)
        io.send(gmem_ref, rows)
        io.send(placed_ref, rows)
        grad_norm = norm_backward(second_ref[rows, :], norms_ref[4:5], grad_q, sums_ref, 0)
        g2 = g_ref[rows, :] + grad_norm
        g2_ref[rows, :] = g2
        g2_low_ref[rows, :] = g2.astype(bf16)
        io.send(g2_ref, rows)
        io.send(g2_low_ref, rows)
        return carry

    lax.fori_loop(0, TILES, tile, 0)
    add_sums(sums_ref, gln_ref, 2)


def self_back_second(
    meta, io, g_low_ref, rank_row_ref, limit_ref, w2_ref, w3_ref,
    q_ref, k_ref, v_ref, mixed_ref, p_ref,
    dq_ref, dk_ref, dv_ref,
    rank_ref, dm_ref, dqs_ref, dks_ref, dvs_ref, p_buf, p_sem,
):
    back_second_docs(
        False, meta, io, g_low_ref, rank_row_ref, limit_ref, (w2_ref, w3_ref), q_ref, k_ref, v_ref,
        mixed_ref, p_ref, rank_ref, dm_ref, dqs_ref, dks_ref, dvs_ref, p_buf, p_sem,
    )
    dq_ref[...] = dqs_ref[...].astype(bf16)
    dk_ref[...] = dks_ref[...].astype(bf16)
    dv_ref[...] = dvs_ref[...].astype(bf16)


def self_back_finish(
    meta, io, g_ref, xq_ref, xc_ref, norms_ref, w0_ref, w1_ref, w2_ref, w3_ref,
    dq_ref, dk_ref, dv_ref, dq2_ref, dk2_ref, dv2_ref,
    placed_q_ref, placed_c_ref, gq_ref, gc_ref, gln_ref, sums_ref,
):
    sums_ref[...] = jnp.zeros_like(sums_ref)

    def tile(i, carry):
        rows = rows_of(i)
        io.wait_rows(i)
        grad_q, grad_kv = stream_grads(
            rows,
            (dq_ref, dk_ref, dv_ref),
            (dq2_ref, dk2_ref, dv2_ref),
            (w0_ref, w1_ref),
            (w2_ref, w3_ref),
        )
        grad_norm = norm_backward(xq_ref[rows, :], norms_ref[0:1], grad_q, sums_ref, 0)
        low_q = (g_ref[rows, :] + grad_norm).astype(bf16)
        gq_ref[rows, :] = low_q
        placed_q_ref[rows, :] = low_q.astype(f32)
        io.send(gq_ref, rows)
        io.send(placed_q_ref, rows)
        grad_norm = norm_backward(xc_ref[rows, :], norms_ref[2:3], grad_kv, sums_ref, 16)
        low_c = grad_norm.astype(bf16)
        gc_ref[rows, :] = low_c
        placed_c_ref[rows, :] = low_c.astype(f32)
        io.send(gc_ref, rows)
        io.send(placed_c_ref, rows)
        return carry

    lax.fori_loop(0, TILES, tile, 0)
    add_sums(sums_ref, gln_ref, 4)


def place_rows(meta, *refs):
    count = len(refs) // 3
    for n in range(count):
        refs[2 * count + n][...] = refs[n][...].astype(refs[2 * count + n].dtype)


GROUP = 8


def position(meta):
    r = meta[35]
    return lax.rem(r, 2), r // 2


def join(own, other, rows):
    return (own[rows, :].astype(f32) + other[rows, :].astype(f32)).astype(bf16)


def join_halves(meta, own, other, keep, send):
    y, _ = position(meta)
    size = keep.shape[0]
    keep[...] = join(own, other, rows_of(y, size))
    send[...] = join(own, other, rows_of(1 - y, size))


def join_chunks(meta, kept, arrived, keep, sends):
    _, z = position(meta)
    size = keep.shape[0]
    keep[...] = join(kept, arrived, rows_of(z, size))
    for s, (send, first) in enumerate(sends, 1):
        send[first : first + size, :] = join(kept, arrived, rows_of(z ^ s, size))


def add_up(kept, parts, first):
    size = kept.shape[0]
    total = kept[...].astype(f32)
    for part in parts:
        total = total + part[first : first + size, :].astype(f32)
    return total.astype(bf16)


def half_of(meta, total, parts, first, half):
    _, z = position(meta)
    size = total.shape[0]
    half[rows_of(z, size), :] = total[...]
    for s, part in enumerate(parts, 1):
        half[rows_of(z ^ s, size), :] = part[first : first + size, :]


def slot_1(meta, ffn_own, ffn_other, keep, send):
    join_halves(meta, ffn_own, ffn_other, keep, send)


def slot_2(
    meta, ffn_kept, ffn_arrived, cross_own, cross_other, ffn_keep, f1, f2, f3, keep, send
):
    join_chunks(meta, ffn_kept, ffn_arrived, ffn_keep, [(f1, 0), (f2, 0), (f3, 0)])
    join_halves(meta, cross_own, cross_other, keep, send)


def slot_3(
    meta, ffn_kept, f1, f2, f3, cross_kept, cross_arrived, self_own, self_other,
    ffn_total, cross_keep, m1, m2, m3, self_keep, self_send,
):
    join_halves(meta, self_own, self_other, self_keep, self_send)
    total = add_up(ffn_kept, (f1, f2, f3), 0)
    ffn_total[...] = total
    size = total.shape[0]
    join_chunks(meta, cross_kept, cross_arrived, cross_keep, [(m, size) for m in (m1, m2, m3)])
    for m in (m1, m2, m3):
        m[0:size, :] = total


def slot_4(
    meta, ffn_total, m1, m2, m3, cross_kept, self_kept, self_arrived,
    ffn_half, cross_total, self_keep, *sends,
):
    join_chunks(meta, self_kept, self_arrived, self_keep, [(send, 0) for send in sends])
    total = add_up(cross_kept, (m1, m2, m3), ffn_total.shape[0])
    cross_total[...] = total
    size = total.shape[0]
    for send in sends:
        send[size:, :] = total
    half_of(meta, ffn_total, (m1, m2, m3), 0, ffn_half)


def slot_5(meta, self_kept, cross_total, m1, m2, m3, send, cross_half):
    size = self_kept.shape[0]
    total = add_up(self_kept, (m1, m2, m3), 0)
    for r in range(GROUP):
        send[r] = total
    half_of(meta, cross_total, (m1, m2, m3), size, cross_half)


def unpack_attention(whole_ref, outs):
    for i in range(3):
        outs[i][...] = whole_ref[:, 128 * i : 128 * i + 128].astype(f32)
    for j in range(4):
        rows = slice(128 * j, 128 * j + 128)
        outs[3][:, rows] = whole_ref[rows, 384:512].astype(f32)


def unpack_ffn(meta, half, arrived, out_in, out_out, ffn_whole):
    y, _ = position(meta)
    ffn_whole[rows_of(y, 512), :] = half[...]
    ffn_whole[rows_of(1 - y, 512), :] = arrived[...]
    out_in[...] = ffn_whole[0:512, :].astype(f32)
    out_out[...] = ffn_whole[512:1024, :].astype(f32)


def unpack_rest(meta, cross_half, cross_arrived, parts, *refs):
    *outs, whole_ref = refs
    y, _ = position(meta)
    whole_ref[rows_of(y, 256), :] = cross_half[...]
    whole_ref[rows_of(1 - y, 256), :] = cross_arrived[...]
    unpack_attention(whole_ref, outs[0:4])
    size = parts.shape[1]
    for r in range(GROUP):
        first = size * (4 * (r % 2) + r // 2)
        whole_ref[first : first + size, :] = parts[r]
    unpack_attention(whole_ref, outs[4:8])


def whole(shape):
    zeros = (0,) * len(shape)
    return pl.BlockSpec(shape, lambda d, meta: zeros)


def own_row(width):
    return pl.BlockSpec((SEQ, width), lambda d, meta: (meta[0], 0))


ANY = pl.BlockSpec(memory_space=pl.ANY)


def in_hbm(x):
    return pltpu.with_memory_space_constraint(x, pltpu.HBM)


probability_out = (pltpu.HBM((DOCS, 4, FAST_K, FAST_Q), bf16), None, ANY)
probability_scratch = [
    pltpu.VMEM((2, TOGETHER, 4, FAST_K, FAST_Q), bf16),
    pltpu.SemaphoreType.DMA((2,)),
]


class Copies:
    def __init__(self, meta):
        self.first = meta[0] * SEQ
        self.loads = {}
        self.tiles = []
        self.sends = []

    def load(self, stage, source, target, sems, own_row):
        if stage == "tiles":
            first = self.first if own_row else 0
            self.tiles.append((source, target, sems, first))
            return
        if own_row:
            source = source.at[pl.ds(pl.multiple_of(self.first, SEQ), SEQ)]
        copy = pltpu.make_async_copy(source, target, sems[0].at[sems[1], 0])
        self.loads.setdefault(stage, []).append(copy)

    def tile(self, entry, i):
        source, target, (sems, b), first = entry
        rows = pl.ds(pl.multiple_of(first + i * TILE, TILE), TILE)
        return pltpu.make_async_copy(source.at[rows], target.at[rows_of(i)], sems.at[b, i])

    def start(self):
        for copy in self.loads.get("now", []):
            copy.start()
        for i in range(TILES):
            for entry in self.tiles:
                self.tile(entry, i).start()
        for stage in ("soon", "late"):
            for copy in self.loads.get(stage, []):
                copy.start()

    def wait(self, stage):
        for copy in self.loads.pop(stage, []):
            copy.wait()

    def wait_rows(self, i):
        for entry in self.tiles:
            self.tile(entry, i).wait()

    def result(self, source, target, sem, own_row):
        self.sends.append([source, target, sem, own_row, False])

    def send(self, ref, rows=None):
        for entry in self.sends:
            source, target, sem, own_row, _ = entry
            if source is ref:
                entry[4] = True
                first = self.first if own_row else 0
                if rows is None:
                    size = source.shape[0]
                else:
                    source = source.at[rows]
                    first, size = first + rows.start, rows.size
                if rows is not None or own_row:
                    target = target.at[pl.ds(pl.multiple_of(first, size), size)]
                pltpu.make_async_copy(source, target, sem).start()

    def finish(self):
        for stage in list(self.loads):
            self.wait(stage)
        for source, _, _, _, started in self.sends:
            if not started:
                self.send(source)
        for source, target, sem, own_row, _ in self.sends:
            if own_row:
                target = target.at[pl.ds(pl.multiple_of(self.first, SEQ), SEQ)]
            pltpu.make_async_copy(source, target, sem).wait()


def out(shape, dtype, own_row=False):
    return (shape, dtype, own_row)


def call(kernel, name, operands, outs, scratch, flops, token=None):
    arrays = [operands[0][0]]
    in_specs, out_specs, out_shapes = [], [], []
    buffers = []
    loads = []
    for n, (x, how) in enumerate(operands[1:]):
        if isinstance(how, str):
            stage, _, row = how.partition("_")
            shape = ((SEQ,) + x.shape[1:]) if row else x.shape
            loads.append((n, stage, len(buffers), bool(row)))
            buffers.append(pltpu.VMEM(shape, x.dtype))
            arrays.append(in_hbm(x))
            in_specs.append(ANY)
        else:
            arrays.append(x)
            in_specs.append(how)
    results = []
    for n, (shape, dtype, how) in enumerate(outs):
        if isinstance(how, bool):
            results.append((n, len(buffers), how))
            buffers.append(pltpu.VMEM(shape, dtype))
            shape = ((2 * SEQ,) + shape[1:]) if how else shape
            out_shapes.append(pltpu.HBM(shape, dtype))
            out_specs.append(ANY)
        else:
            out_shapes.append(jax.ShapeDtypeStruct(shape, dtype) if dtype else shape)
            out_specs.append(how)
    n_in, n_out = len(in_specs), len(out_specs)
    if token is not None:
        arrays.append(token)
        in_specs.append(whole((8, 128)))
        out_specs.append(whole((8, 128)))
        out_shapes.append(jax.ShapeDtypeStruct((8, 128), f32))

    def body(meta, *refs):
        ins, refs = list(refs[:n_in]), refs[len(in_specs) - n_in + n_in :]
        results_out, refs = list(refs[:n_out]), refs[n_out:]
        if token is not None:
            token_out, refs = refs[0], refs[1:]
            token_out[...] = jnp.zeros_like(token_out)
        bufs, refs = refs[: len(buffers)], refs[len(buffers) :]
        rest = refs[: len(scratch)]
        copies = Copies(meta)
        if buffers:
            sems = refs[len(scratch)]
        for n, stage, b, row in loads:
            copies.load(stage, ins[n], bufs[b], (sems, b), row)
            ins[n] = bufs[b]
        for n, b, row in results:
            copies.result(bufs[b], results_out[n], sems.at[b, 0], row)
            results_out[n] = bufs[b]
        copies.start()
        copies.wait("now")
        if buffers:
            kernel(meta, copies, *ins, *results_out, *rest)
        else:
            kernel(meta, *ins, *results_out, *rest)
        copies.finish()

    moved = sum(x.size * x.dtype.itemsize for x in arrays[1:])
    sems = [pltpu.SemaphoreType.DMA((len(buffers), TILES))] if buffers else []
    return pl.pallas_call(
        body,
        name=name,
        grid_spec=pltpu.PrefetchScalarGridSpec(
            num_scalar_prefetch=1,
            grid=(1,),
            in_specs=in_specs,
            out_specs=out_specs,
            scratch_shapes=buffers + scratch + sems,
        ),
        out_shape=out_shapes,
        compiler_params=pltpu.CompilerParams(
            dimension_semantics=("arbitrary",), vmem_limit_bytes=50 * 1024 * 1024
        ),
        cost_estimate=pl.CostEstimate(
            flops=int(flops), bytes_accessed=int(moved), transcendentals=0
        ),
    )(*arrays)


def simple(kernel, name, meta, operands, outs, scratch=()):
    return pl.pallas_call(
        kernel,
        name=name,
        grid_spec=pltpu.PrefetchScalarGridSpec(
            num_scalar_prefetch=1,
            grid=(1,),
            in_specs=[whole(x.shape) for x in operands],
            out_specs=[whole(shape) for shape, _ in outs],
            scratch_shapes=scratch,
        ),
        out_shape=[jax.ShapeDtypeStruct(shape, dtype) for shape, dtype in outs],
        compiler_params=pltpu.CompilerParams(vmem_limit_bytes=16 * 1024 * 1024),
    )(meta, *operands)


def full(x):
    return (x, whole(x.shape))


def shards(
    query_stream,
    content_stream,
    memory,
    segment_ids,
    source_segments,
    context_rank,
    context_limit,
    padding,
    ln_query_gain,
    ln_query_bias,
    ln_content_gain,
    ln_content_bias,
    self_query,
    self_key,
    self_value,
    self_out,
    ln_cross_gain,
    ln_cross_bias,
    cross_query,
    cross_key,
    cross_value,
    cross_out,
    ln_ffn_gain,
    ln_ffn_bias,
    ffn_in,
    ffn_out,
    cotangent,
):
    core = lax.axis_index("heads") % 2

    def to_core(x):
        return lax.ppermute(x, "heads", [(h, h ^ 1) for h in range(4)])

    hold = lambda *xs: lax.optimization_barrier(xs)

    def to_chip(x):
        return lax.ppermute(x, "heads", [(h, h ^ 2) for h in range(4)])

    row = pl.BlockSpec((1, 8, 128), lambda d, core: (core[0], 0, 0))

    def token_row(x):
        return (in_hbm(x.reshape(2, 8, 128)), row)

    def fixed(x):
        zeros = (0,) * x.ndim
        return (in_hbm(x), pl.BlockSpec(x.shape, lambda d, core: zeros))

    prepared = [
        ((36,), jnp.int32, pl.BlockSpec(memory_space=pltpu.SMEM)),
        ((1, SEQ), f32, whole((1, SEQ))),
        ((1, SEQ), f32, whole((1, SEQ))),
        ((8, D), f32, whole((8, D))),
        ((D, D), bf16, whole((D, D))),
        ((D, D), bf16, whole((D, D))),
    ]
    gains = (
        ln_query_gain,
        ln_query_bias,
        ln_content_gain,
        ln_content_bias,
        ln_cross_gain,
        ln_cross_bias,
        ln_ffn_gain,
        ln_ffn_bias,
    )
    weights = (self_query, self_key, self_value, self_out)
    weights += (cross_query, cross_key, cross_value, cross_out)
    tokens = (segment_ids, source_segments, context_rank, context_limit, padding)
    meta, rank, limit, norms, ws0, wc0 = call(
        prepare,
        "prepare",
        [(jnp.stack([core, lax.axis_index("rows") % GROUP]).astype(jnp.int32), None)]
        + [token_row(x) for x in tokens]
        + [fixed(x.reshape(1, D)) for x in gains]
        + [fixed(x) for x in weights],
        prepared,
        [],
        0,
    )

    ws1 = to_core(ws0)
    ws2 = to_chip(ws0)
    wc1 = to_core(wc0)
    u0, v0 = ffn_in, ffn_out
    meta_in = (meta, None)

    heads_out = [out((SEQ, 256), bf16)] * 4

    def stream_out(dtype, own_row=False):
        return out((SEQ, D), dtype, own_row)

    def now(*xs):
        return [(x, "now") for x in xs]

    def soon(*xs):
        return [(x, "soon") for x in xs]

    def late(*xs):
        return [(x, "late") for x in xs]

    def small(*xs):
        return [(x, whole(x.shape)) for x in xs]

    limits = pltpu.VMEM((SEQ, 128), f32)
    pair_flops = 2 * SEQ * D * 768 + 2 * 2 * 4 * DOCS * FAST_Q * FAST_K * 256

    nq, nc, *first, token = call(
        self_first,
        "self_first",
        [meta_in, (query_stream, "tiles_row"), (content_stream, "tiles_row")]
        + small(rank, limit, norms)
        + now(ws0, ws1),
        [stream_out(bf16), stream_out(bf16)] + heads_out + [probability_out],
        [limits] + probability_scratch,
        pair_flops,
        jnp.zeros((8, 128), f32),
    )
    ws2, wc0, token = hold(ws2, wc0, token)
    ws3 = to_core(ws2)
    wc2 = to_chip(wc0)
    *second_heads, second, ncross, token = call(
        self_second,
        "self_second",
        [meta_in, (query_stream, "late_row")]
        + [(nq, "tiles"), (nc, "tiles")]
        + small(rank, limit, norms)
        + late(ws0, ws1)
        + now(ws2, ws3)
        + late(first[3]),
        heads_out + [probability_out, stream_out(f32), stream_out(bf16)],
        [limits] + probability_scratch,
        pair_flops + 2 * SEQ * D * D,
        token,
    )
    wc2, u0, v0, token = hold(wc2, u0, v0, token)
    wc3 = to_core(wc2)
    u2 = to_chip(u0)
    u1 = to_core(u0)
    *cross_heads, token = call(
        cross_first,
        "cross_first",
        [meta_in, (ncross, "tiles"), (memory, "tiles_row")] + now(wc0, wc1),
        heads_out + [probability_out],
        probability_scratch,
        pair_flops,
        token,
    )
    wc3, u2, v0, token = hold(wc3, u2, v0, token)
    u3 = to_core(u2)
    v2 = to_chip(v0)
    v1 = to_core(v0)
    *cross_heads_second, third, nffn, token = call(
        cross_second,
        "cross_second",
        [meta_in]
        + late(second)
        + [(ncross, "tiles"), (memory, "tiles_row")]
        + small(norms)
        + late(wc0, wc1)
        + now(wc2, wc3)
        + late(cross_heads[3]),
        heads_out + [probability_out, stream_out(f32), stream_out(bf16)],
        probability_scratch,
        pair_flops + 2 * SEQ * D * D,
        token,
    )
    u3, v2, token = hold(u3, v2, token)
    v3 = to_core(v2)
    grads_ln = ((8, D), f32, whole((8, D)))
    placed_output, output, g3, g3_low, gln_ffn, ffn_own, ffn_other, token = call(
        ffn_both,
        "ffn_both",
        [meta_in]
        + [(third, "tiles"), (nffn, "tiles"), (cotangent, "tiles_row")]
        + small(norms)
        + now(u0, u1, u2, u3, v0, v1, v2, v3),
        [
            stream_out(bf16, True),
            stream_out(bf16),
            stream_out(f32),
            stream_out(bf16),
            grads_ln,
            out((1024, D), bf16),
            out((1024, D), bf16),
        ],
        [pltpu.VMEM((SEQ, 1024), bf16), pltpu.VMEM((SEQ, 1024), bf16), pltpu.VMEM((16, D), f32)],
        12 * SEQ * D * 2048,
        token,
    )

    def both_rows(placed_own, others, name):
        count = len(others)
        size = SEQ // 2
        one = pl.BlockSpec((size, D), lambda i, meta: (i, 0))
        block = pl.BlockSpec((size, D), lambda i, meta: (2 * (1 - meta[0]) + i, 0))
        return pl.pallas_call(
            place_rows,
            name=name,
            grid_spec=pltpu.PrefetchScalarGridSpec(
                num_scalar_prefetch=1,
                grid=(2,),
                in_specs=[one] * count + [pl.BlockSpec(memory_space=pl.ANY)] * count,
                out_specs=[block] * count,
            ),
            out_shape=[jax.ShapeDtypeStruct(x.shape, x.dtype) for x in placed_own],
            input_output_aliases={1 + count + n: n for n in range(count)},
        )(meta, *others, *placed_own)

    row_count = lax.axis_size("rows")
    assert row_count % GROUP == 0

    def along_rows(x, s):
        return lax.ppermute(x, "rows", [(r, r ^ s) for r in range(row_count)])

    def to_y(x):
        return along_rows(x, 1)

    def to_z(sends):
        return [along_rows(x, 2 * s) for s, x in enumerate(sends, 1)]

    def rows_out(*sizes):
        return [((n, D), bf16) for n in sizes]

    ffn_other = to_core(ffn_other)
    output_other = to_core(output)

    back_scratch = [pltpu.VMEM((SEQ, 256), bf16)] + [pltpu.VMEM((SEQ, 256), f32)] * 3
    back_scratch += probability_scratch
    pair_out = out((SEQ, 256), bf16)
    packed_outs = [((D, D), bf16, whole((D, D)))] * 2
    back_flops = 2 * SEQ * D * 256 + 4 * 2 * 4 * DOCS * FAST_Q * FAST_K * 256

    def head_inputs(natural, p):
        return soon(*natural) + [(in_hbm(p), ANY)]

    *cross_grads, cross_own, cross_other, token = call(
        functools.partial(attention_back_first, True),
        "cross_back_first",
        [meta_in]
        + [(g3_low, "tiles")]
        + late(ncross)
        + [(memory, "late_row")]
        + small(rank, limit)
        + now(wc0, wc1)
        + head_inputs(cross_heads[0:4], cross_heads[4]),
        [pair_out] * 3 + packed_outs,
        [limits] + back_scratch,
        back_flops + 2 * SEQ * D * 1024,
        token,
    )
    ffn_other, output_other, token = hold(ffn_other, output_other, token)
    ffn_keep, ffn_send = simple(slot_1, "slot_1", meta, [ffn_own, ffn_other], rows_out(512, 512))
    ffn_send, token = hold(ffn_send, token)
    ffn_arrived = to_y(ffn_send)
    cross_other = to_core(cross_other)
    g2, g2_low, placed_mem, grad_mem, gln_cross, token = call(
        cross_back_second,
        "cross_back_second",
        [meta_in]
        + [(g3_low, "tiles")]
        + late(g3, second)
        + small(norms)
        + late(wc0, wc1)
        + now(wc2, wc3)
        + late(*cross_grads)
        + head_inputs(cross_heads_second[0:4], cross_heads_second[4]),
        [stream_out(f32), stream_out(bf16), stream_out(f32, True), stream_out(bf16), grads_ln],
        back_scratch + [pltpu.VMEM((16, D), f32)],
        back_flops + 2 * SEQ * D * 1536,
        token,
    )
    ffn_arrived, cross_other, token = hold(ffn_arrived, cross_other, token)
    ffn_keep, *sends, cross_keep, cross_send = simple(
        slot_2,
        "slot_2",
        meta,
        [ffn_keep, ffn_arrived, cross_own, cross_other],
        rows_out(128, 128, 128, 128, 256, 256),
    )
    ffn_keep, cross_send, token = hold(ffn_keep, cross_send, token)
    ffn_parts = to_z(sends)
    cross_arrived = to_y(cross_send)

    *self_grads, self_own, self_other, token = call(
        functools.partial(attention_back_first, False),
        "self_back_first",
        [meta_in]
        + [(g2_low, "tiles")]
        + late(nq, nc)
        + small(rank, limit)
        + now(ws0, ws1)
        + head_inputs(first[0:4], first[4]),
        [pair_out] * 3 + packed_outs,
        [limits] + back_scratch,
        back_flops + 2 * SEQ * D * 1024,
        token,
    )
    *ffn_parts, cross_arrived, self_other, token = hold(
        *ffn_parts, cross_arrived, self_other, token
    )
    self_other = to_core(self_other)
    ffn_total, cross_keep, *sends, self_keep, self_send = simple(
        slot_3,
        "slot_3",
        meta,
        [ffn_keep, *ffn_parts, cross_keep, cross_arrived, self_own, self_other],
        rows_out(128, 64, 192, 192, 192, 256, 256),
    )
    ffn_total, self_send, grad_mem, token = hold(ffn_total, self_send, grad_mem, token)
    mem_other = to_core(grad_mem)
    self_arrived = to_y(self_send)
    messages = to_z(sends)
    *self_grads_second, token = call(
        self_back_second,
        "self_back_second",
        [meta_in, (g2_low, "tiles")]
        + small(rank, limit)
        + now(ws2, ws3)
        + head_inputs(second_heads[0:4], second_heads[4]),
        [pair_out] * 3,
        [limits] + back_scratch,
        back_flops,
        token,
    )
    output_other, mem_other, token = hold(output_other, mem_other, token)
    out_both, grad_mem_both = both_rows(
        [placed_output, placed_mem], [output_other, mem_other], "place_early"
    )
    *messages, self_arrived, out_both, token = hold(*messages, self_arrived, out_both, token)
    ffn_half, cross_total, self_keep, *sends = simple(
        slot_4,
        "slot_4",
        meta,
        [ffn_total, *messages, cross_keep, self_keep, self_arrived],
        rows_out(512, 64, 64, 128, 128, 128),
    )
    cross_total, ffn_half, token = hold(cross_total, ffn_half, token)
    messages = to_z(sends)
    ffn_arrived = to_y(ffn_half)
    placed_q, placed_c, gq, gc, gln_self, token = call(
        self_back_finish,
        "self_back_finish",
        [meta_in, (g2, "tiles"), (query_stream, "tiles_row"), (content_stream, "tiles_row")]
        + small(norms)
        + now(ws0, ws1, ws2, ws3)
        + [(x, "tiles") for x in self_grads + self_grads_second],
        [stream_out(f32, True), stream_out(f32, True), stream_out(bf16), stream_out(bf16), grads_ln],
        [pltpu.VMEM((32, D), f32)],
        2 * SEQ * D * 1536,
        token,
    )
    gln = jnp.concatenate([gln_self[0:4], gln_cross[0:2], gln_ffn[0:2]], axis=0)
    *messages, ffn_arrived, gln_ffn = hold(*messages, ffn_arrived, gln_ffn)
    last_send, cross_half = simple(
        slot_5,
        "slot_5",
        meta,
        [self_keep, cross_total, *messages],
        [((GROUP, 64, D), bf16), ((256, D), bf16)],
    )
    groups = None
    if row_count > GROUP:
        groups = [list(range(r, r + GROUP)) for r in range(0, row_count, GROUP)]
    def gather(x):
        return lax.all_to_all(x, "rows", 0, 0, axis_index_groups=groups)

    last_parts = gather(last_send)
    cross_arrived = to_y(cross_half)
    gln, cross_half = hold(gln, cross_half)
    gln = gln + to_core(gln)
    for step in (1, 2, 4):
        gln = gln + along_rows(gln, step)

    def over_groups(totals):
        if row_count == GROUP:
            return totals
        groups = [list(range(r, row_count, GROUP)) for r in range(GROUP)]
        return lax.psum(totals, "rows", axis_index_groups=groups)

    gq_both, gc_both = both_rows([placed_q, placed_c], [to_core(gq), to_core(gc)], "place_late")

    grad_ffn_in, grad_ffn_out = simple(
        unpack_ffn,
        "unpack_ffn",
        meta,
        [ffn_half, ffn_arrived],
        [((D, D), f32)] * 2,
        [pltpu.VMEM((2 * D, D), bf16)],
    )
    attention_outs = [((512, 128), f32)] * 3 + [((128, 512), f32)]
    cross_arrived, gq_both, grad_ffn_in = hold(cross_arrived, gq_both, grad_ffn_in)
    parts = simple(
        unpack_rest,
        "unpack_rest",
        meta,
        [cross_half, cross_arrived, last_parts],
        attention_outs * 2,
        [pltpu.VMEM((D, D), bf16)],
    )
    grad_cross_parts, grad_self_parts = parts[:4], parts[4:]
    grad_ffn_in, grad_ffn_out, grad_cross_parts, grad_self_parts, gln = over_groups(
        (grad_ffn_in, grad_ffn_out, grad_cross_parts, grad_self_parts, gln)
    )
    return (
        out_both,
        gq_both,
        gc_both,
        grad_mem_both,
        gln[0],
        gln[1],
        gln[2],
        gln[3],
        *grad_self_parts,
        gln[4],
        gln[5],
        *grad_cross_parts,
        gln[6],
        gln[7],
        grad_ffn_in,
        grad_ffn_out,
    )


def solution(mesh):
    assert mesh.shape["heads"] == 4
    row_spec = P("rows", None)
    flat = P("rows")
    by_column = P(None, "heads")
    by_row = P("heads", None)
    attention = (by_column, by_column, by_column, by_row)
    in_specs = (
        (row_spec,) * 3
        + (flat,) * 5
        + (P(),) * 4
        + attention
        + (P(),) * 2
        + attention
        + (P(),) * 2
        + (by_column, by_row, row_spec)
    )
    out_specs = (
        (row_spec,) * 4
        + (P(),) * 4
        + attention
        + (P(),) * 2
        + attention
        + (P(),) * 2
        + (by_column, by_row)
    )
    return jax.shard_map(shards, mesh=mesh, in_specs=in_specs, out_specs=out_specs, check_vma=False)
```

```python
import functools

import jax
import jax.numpy as jnp
from jax import lax
from jax.experimental import pallas as pl
from jax.experimental.pallas import tpu as pltpu
from jax.sharding import PartitionSpec as P

HEAD_DIM = 64
SEQ = 1024
DOCS = 8
D = 512
TILE = 256
TILES = SEQ // TILE
FAST_Q = 256
FAST_K = 208
LONG_Q = 128
LONG_K = 640

norm_eps = 1e-05
masked_score = -1e30
hidden_rank = 1e6
gelu_root = 0.7978845608028654
gelu_cube = 0.044715

f32 = jnp.float32
bf16 = jnp.bfloat16


def dot(a, b):
    return lax.dot_general(a, b, (((1,), (0,)), ((), ())), preferred_element_type=f32)


def dot_nt(a, b):
    return lax.dot_general(a, b, (((1,), (1,)), ((), ())), preferred_element_type=f32)


def dot_tn(a, b):
    return lax.dot_general(a, b, (((0,), (0,)), ((), ())), preferred_element_type=f32)


def lanes(parts):
    return jnp.concatenate(parts, axis=1)


NORM_ROWS = 32


def layer_norm(values, gain, shift):
    def piece(part):
        part = part.astype(f32)
        centre = part - jnp.mean(part, axis=-1, keepdims=True)
        spread = jnp.mean(centre * centre, axis=-1, keepdims=True)
        return (centre * lax.rsqrt(spread + norm_eps) * gain + shift).astype(bf16)

    return by_pieces(piece, NORM_ROWS, 0, values)


def eight_rows(values):
    return sum(values[8 * i : 8 * i + 8] for i in range(1, values.shape[0] // 8)) + values[0:8]


def norm_backward(values, gain, grad, sums_ref, first):
    sums = []

    def piece(part, grad_part):
        part = part.astype(f32)
        centre = part - jnp.mean(part, axis=-1, keepdims=True)
        spread = jnp.mean(centre * centre, axis=-1, keepdims=True)
        scale = lax.rsqrt(spread + norm_eps)
        xhat = centre * scale
        eg = grad_part * gain
        mean_eg = jnp.mean(eg, axis=-1, keepdims=True)
        mean_egx = jnp.mean(eg * xhat, axis=-1, keepdims=True)
        sums.append((eight_rows(grad_part * xhat), eight_rows(grad_part)))
        return scale * (eg - mean_eg - xhat * mean_egx)

    result = by_pieces(piece, NORM_ROWS, 0, values, grad)
    for n, parts in enumerate(zip(*sums)):
        sums_ref[first + 8 * n : first + 8 * n + 8, :] += sum(parts[1:], parts[0])
    return result


def add_sums(sums_ref, gln_ref, count):
    gln_ref[...] = jnp.zeros_like(gln_ref)
    for n in range(count):
        gln_ref[n : n + 1, :] = jnp.sum(sums_ref[8 * n : 8 * n + 8, :], axis=0, keepdims=True)


def by_pieces(work, size, axis, *arrays):
    count = arrays[0].shape[axis] // size
    pieces = []
    for i in range(count):
        cut = (slice(size * i, size * i + size),)
        cut = cut if axis == 0 else (slice(None),) + cut
        pieces.append(work(*[x[cut] for x in arrays]))
    if not isinstance(pieces[0], tuple):
        return jnp.concatenate(pieces, axis=axis)
    return tuple(jnp.concatenate(parts, axis=axis) for parts in zip(*pieces))


def rows_of(i, size=TILE):
    return pl.ds(pl.multiple_of(i * size, size), size)


def w_query(ref):
    return ref[:, 0:128]


def w_key(ref):
    return ref[:, 128:256]


def w_value(ref):
    return ref[:, 256:384]


def w_out(ref):
    return lanes([ref[128 * j : 128 * j + 128, 384:512] for j in range(4)])


def half_masks():
    place = lax.broadcasted_iota(jnp.int32, (1, 128), 1)
    low = jnp.where(place < HEAD_DIM, 1.0, 0.0).astype(f32)
    return (low.astype(bf16), (1.0 - low).astype(bf16))


def doc_bounds(meta, d, source):
    base = 17 if source else 1
    return meta[base + d], meta[base + 8 + d]


def window_of(first, limit):
    return pl.multiple_of(jnp.minimum((first // 16) * 16, limit), 16)


def key_bias(ks, ke, k0, width):
    place = k0 + lax.broadcasted_iota(jnp.int32, (width, 128), 0)
    return jnp.where((place >= ks) & (place < ke), 0.0, masked_score)


def make_bias(rank_ref, limit_ref, ks, ke, q0, k0, span, width):
    if rank_ref is None:
        return lanes([key_bias(ks, ke, k0, width)] * (span // 128))
    place = k0 + lax.broadcasted_iota(jnp.int32, (width, 128), 0)
    ranks = rank_ref[pl.ds(k0, width), :]
    ranks = jnp.where((place < ks + 2) & (ranks < hidden_rank), -1.0, ranks)
    ranks = jnp.where((place >= ks) & (place < ke), ranks, hidden_rank)
    limits = jnp.broadcast_to(limit_ref[...], (8, SEQ))
    limits = pltpu.roll(limits, lax.rem(SEQ - q0, SEQ), 1)[0:1, 0:span]
    row = k0 + lax.broadcasted_iota(jnp.int32, (width, span), 0)
    column = q0 + lax.broadcasted_iota(jnp.int32, (width, span), 1)
    seen = (lanes([ranks] * (span // 128)) < limits) & (row != column)
    return jnp.where(seen, 0.0, masked_score)


TOGETHER = 4
STEPS = DOCS // TOGETHER


LAG = 2


def interleave(items):
    items = [list(phases) for phases in items]
    depth = max(len(phases) for phases in items)
    results = [None] * len(items)
    for tick in range(len(items) + LAG * (depth - 1)):
        for phase in range(depth):
            n = tick - LAG * phase
            if 0 <= n < len(items) and phase < len(items[n]):
                run = items[n][phase]
                results[n] = run() if phase == 0 else run(results[n])
    return results


def by_halves(pairs, phases):
    shared = [{} for _ in range(pairs)]
    return [phases(n, a, shared[n]) for n in range(pairs) for a in range(2)]


def is_fast(meta, cross):
    return meta[34 if cross else 33] == 1


def both_heads(x, masks):
    return jnp.concatenate([x * masks[0], x * masks[1]], axis=0)


def pair_scores(queries, keys, masks):
    return dot_nt(both_heads(keys, masks), queries)


def raised(scores, bias):
    def piece(part, bias_part):
        part = part + bias_part
        return jnp.exp((part - jnp.max(part, axis=0, keepdims=True)).astype(bf16))

    return by_pieces(piece, 128, 1, scores, bias)


def weighted_values(values, parts):
    width = values.shape[1]
    mixed = []
    shares = []
    for a, part in enumerate(parts):
        rows = jnp.concatenate([values[64 * a : 64 * a + 64], jnp.ones((16, width), bf16)], axis=0)
        sums = dot(rows, part)
        share = 1.0 / sums[64:65]
        mixed.append(sums[:64] * share)
        shares.append(part * share.astype(bf16))
    return jnp.concatenate(mixed, axis=0).astype(bf16), shares


def pair_gradient(rows, parts):
    across = jnp.transpose(rows)
    halves = [dot(across[64 * a : 64 * a + 64], part) for a, part in enumerate(parts)]
    return jnp.transpose((jnp.concatenate(halves, axis=0) * HEAD_DIM**-0.5).astype(bf16))


def for_docs(meta, cross, run, before, after):
    @pl.when(is_fast(meta, cross))
    def _():
        def step(i, carry):
            slot = lax.rem(i, 2)
            before(i, slot)
            items = []
            for place in range(TOGETHER):
                d = TOGETHER * i + place
                ts, te = doc_bounds(meta, d, False)
                ks, ke = doc_bounds(meta, d, cross)
                q0 = window_of(ts, SEQ - FAST_Q)
                k0 = window_of(ks, SEQ - FAST_K)
                items += run(d, slot, place, q0, k0, FAST_Q, FAST_K, ts, te, ks, ke, True)
            interleave(items)
            after(i, slot)
            return carry

        lax.fori_loop(0, STEPS, step, 0)

    @pl.when(jnp.logical_not(is_fast(meta, cross)))
    def _():
        def doc(d, carry):
            ts, te = doc_bounds(meta, d, False)
            ks, ke = doc_bounds(meta, d, cross)
            base = (ts // 16) * 16
            k0 = window_of(ks, SEQ - LONG_K)

            def chunk(i, carry):
                lower = base + i * LONG_Q
                q0 = pl.multiple_of(jnp.minimum(lower, SEQ - LONG_Q), 16)
                low = jnp.maximum(ts, lower)
                high = jnp.minimum(te, lower + LONG_Q)
                interleave(run(d, None, None, q0, k0, LONG_Q, LONG_K, low, high, ks, ke, False))
                return carry

            return lax.fori_loop(0, (te - base + LONG_Q - 1) // LONG_Q, chunk, carry)

        lax.fori_loop(0, DOCS, doc, 0)


def attend_docs(meta, cross, rank_ref, limit_ref, halves, p_ref, p_buf, p_sem):
    pairs = 2 * len(halves)
    masks = half_masks()

    def save(i, slot):
        return pltpu.make_async_copy(p_buf.at[slot], p_ref.at[pl.ds(TOGETHER * i, TOGETHER)], p_sem.at[slot])

    def before(i, slot):
        @pl.when(i >= 2)
        def _():
            save(i - 2, slot).wait()

    def after(i, slot):
        save(i, slot).start()

    def run(d, slot, place, q0, k0, span, width, low, high, ks, ke, fast):
        bias = make_bias(rank_ref, limit_ref, ks, ke, q0, k0, span, width)
        row = q0 + lax.broadcasted_iota(jnp.int32, (span, 128), 0)
        inside = (row >= low) & (row < high)

        def phases(n):
            q_ref, k_ref, v_ref, mixed_ref = halves[n // 2]
            cols = slice(128 * (n % 2), 128 * (n % 2) + 128)

            def score():
                return pair_scores(q_ref[pl.ds(q0, span), cols], k_ref[pl.ds(k0, width), cols], masks)

            def weigh(scores):
                return [raised(scores[width * a : width * a + width], bias) for a in range(2)]

            def mix(parts):
                values = jnp.transpose(v_ref[pl.ds(k0, width), cols])
                mixed, parts = weighted_values(values, parts)
                if fast:
                    for a in range(2):
                        p_buf[slot, place, 2 * n + a] = parts[a]
                mixed = jnp.transpose(mixed).astype(f32)
                old = mixed_ref[pl.ds(q0, span), cols].astype(f32)
                mixed_ref[pl.ds(q0, span), cols] = jnp.where(inside, mixed, old).astype(bf16)

            return score, weigh, mix

        return [phases(n) for n in range(pairs)]

    for_docs(meta, cross, run, before, after)

    @pl.when(is_fast(meta, cross))
    def _():
        for i in range(STEPS - 2, STEPS):
            save(i, i % 2).wait()


def load_step(load, i, slot):
    p_ref, p_buf, p_sem = load
    return pltpu.make_async_copy(p_ref.at[pl.ds(TOGETHER * i, TOGETHER)], p_buf.at[slot], p_sem.at[slot])


def start_load(meta, cross, load):
    @pl.when(is_fast(meta, cross))
    def _():
        load_step(load, 0, 0).start()


def attend_docs_back(
    meta, cross, rank_ref, limit_ref, q_ref, k_ref, v_ref, mixed_ref, dm_ref,
    dq_ref, dk_ref, dv_ref, load,
):
    pairs = q_ref.shape[1] // 128
    masks = half_masks()
    p_buf = load[1]

    def before(i, slot):
        @pl.when(i + 1 < STEPS)
        def _():
            load_step(load, i + 1, 1 - slot).start()

        load_step(load, i, slot).wait()

    def after(i, slot):
        pass

    def run(d, slot, place, q0, k0, span, width, low, high, ks, ke, fast):
        row = q0 + lax.broadcasted_iota(jnp.int32, (span, 128), 0)
        inside = jnp.where((row >= low) & (row < high), 1.0, 0.0).astype(bf16)
        ones = jnp.ones((width, 128), bf16)
        if not fast:
            bias = make_bias(rank_ref, limit_ref, ks, ke, q0, k0, span, width)

        def phases(n):
            cols = slice(128 * n, 128 * n + 128)

            def differ():
                values = v_ref[pl.ds(k0, width), cols]
                mixed = mixed_ref[pl.ds(q0, span), cols]
                grad = dm_ref[pl.ds(q0, span), cols] * inside
                left = lanes([grad, -(grad * mixed)])
                right = both_heads(lanes([values, ones]), [lanes([m, m]) for m in masks])
                return grad, dot_nt(right, left)

            def slope(state):
                grad, delta = state
                if fast:
                    parts = [p_buf[slot, place, 2 * n + a] for a in range(2)]
                else:
                    queries = q_ref[pl.ds(q0, span), cols]
                    keys = k_ref[pl.ds(k0, width), cols]
                    scores = pair_scores(queries, keys, masks)
                    parts = [raised(scores[width * a : width * a + width], bias) for a in range(2)]
                    parts = weighted_values(jnp.transpose(v_ref[pl.ds(k0, width), cols]), parts)[1]
                slopes = [
                    by_pieces(
                        lambda part, change: part * change.astype(bf16),
                        16,
                        0,
                        parts[a],
                        delta[width * a : width * a + width],
                    )
                    for a in range(2)
                ]
                return grad, parts, slopes

            def spread(state):
                grad, parts, slopes = state
                queries = q_ref[pl.ds(q0, span), cols]
                dk = dv = None
                for a in range(2):
                    dk_a = dot(slopes[a], queries * masks[a])
                    dv_a = dot(parts[a], grad * masks[a])
                    dk = dk_a if dk is None else dk + dk_a
                    dv = dv_a if dv is None else dv + dv_a
                dq = pair_gradient(k_ref[pl.ds(k0, width), cols], slopes)
                dq_ref[pl.ds(q0, span), cols] += dq.astype(f32)
                dk_ref[pl.ds(k0, width), cols] += dk
                dv_ref[pl.ds(k0, width), cols] += dv

            return differ, slope, spread

        return [phases(n) for n in range(pairs)]

    for_docs(meta, cross, run, before, after)


def spread_ranks(rank_row_ref, rank_ref):
    rank_ref[...] = jnp.transpose(jnp.broadcast_to(rank_row_ref[...], (128, SEQ)))


def prepare(
    core, seg_ref, src_ref, rank_ref, limit_ref, pad_ref,
    n0, n1, n2, n3, n4, n5, n6, n7, sq, sk, sv, so, cq, ck, cv, co,
    meta_ref, ranks_ref, limits_ref, norms_ref, ws_ref, wc_ref,
):
    meta_ref[0] = core[0]
    meta_ref[35] = core[1]
    for base, ref in ((1, seg_ref), (17, src_ref)):
        ids = ref[0]
        meta_ref[base] = 0
        meta_ref[base + 15] = SEQ
        for d in range(1, DOCS):
            cut = jnp.sum(jnp.where(ids < d, 1.0, 0.0)).astype(jnp.int32)
            meta_ref[base + d] = cut
            meta_ref[base + 7 + d] = cut
    for place, base in ((33, 1), (34, 17)):
        fast = jnp.int32(1)
        for d in range(DOCS):
            q0 = window_of(meta_ref[1 + d], SEQ - FAST_Q)
            k0 = window_of(meta_ref[base + d], SEQ - FAST_K)
            fits = (meta_ref[9 + d] - q0 <= FAST_Q) & (meta_ref[base + 8 + d] - k0 <= FAST_K)
            fast = fast & fits.astype(jnp.int32)
        meta_ref[place] = fast
    ranks = jnp.where(pad_ref[0] != 0, hidden_rank, rank_ref[0].astype(f32))
    limits = limit_ref[0].astype(f32)
    for i in range(8):
        ranks_ref[0:1, 128 * i : 128 * i + 128] = ranks[i : i + 1]
        limits_ref[0:1, 128 * i : 128 * i + 128] = limits[i : i + 1]
    for i, ref in enumerate((n0, n1, n2, n3, n4, n5, n6, n7)):
        norms_ref[i : i + 1, :] = ref[...]
    for to, parts, out in ((ws_ref, (sq, sk, sv), so), (wc_ref, (cq, ck, cv), co)):
        for i, part in enumerate(parts):
            to[:, 128 * i : 128 * i + 128] = part[...]
        for j in range(4):
            to[128 * j : 128 * j + 128, 384:512] = out[:, 128 * j : 128 * j + 128]


def self_first(
    meta, io, xq_ref, xc_ref, rank_row_ref, limit_ref, norms_ref, w0_ref, w1_ref,
    nq_ref, nc_ref, q_ref, k_ref, v_ref, mixed_ref, p_ref, rank_ref, p_buf, p_sem,
):

    spread_ranks(rank_row_ref, rank_ref)
    wq = lanes([w_query(w0_ref), w_query(w1_ref)])
    wkv = lanes([w_key(w0_ref), w_key(w1_ref), w_value(w0_ref), w_value(w1_ref)])

    def tile(i, carry):
        rows = rows_of(i)
        io.wait_rows(i)
        nq = layer_norm(xq_ref[rows, :], norms_ref[0:1], norms_ref[1:2])
        nc = layer_norm(xc_ref[rows, :], norms_ref[2:3], norms_ref[3:4])
        nq_ref[rows, :] = nq
        nc_ref[rows, :] = nc
        q_ref[rows, :] = (dot(nq, wq) * (HEAD_DIM**-0.5)).astype(bf16)
        kv = dot(nc, wkv).astype(bf16)
        k_ref[rows, :] = kv[:, :256]
        v_ref[rows, :] = kv[:, 256:]
        return carry

    lax.fori_loop(0, TILES, tile, 0)

    for ref in (nq_ref, nc_ref, q_ref, k_ref, v_ref):
        io.send(ref)
    attend_docs(meta, False, rank_ref, limit_ref, [(q_ref, k_ref, v_ref, mixed_ref)], p_ref, p_buf, p_sem)


def self_second(
    meta, io, xq_ref, nq_ref, nc_ref, rank_row_ref, limit_ref, norms_ref, w0_ref, w1_ref, w2_ref, w3_ref,
    mixed_first_ref,
    q_ref, k_ref, v_ref, mixed_ref, p_ref, second_ref, ncross_ref, rank_ref, p_buf, p_sem,
):

    spread_ranks(rank_row_ref, rank_ref)
    wq = lanes([w_query(w2_ref), w_query(w3_ref)])
    wkv = lanes([w_key(w2_ref), w_key(w3_ref), w_value(w2_ref), w_value(w3_ref)])

    def tile(i, carry):
        rows = rows_of(i)
        io.wait_rows(i)
        q_ref[rows, :] = (dot(nq_ref[rows, :], wq) * (HEAD_DIM**-0.5)).astype(bf16)
        kv = dot(nc_ref[rows, :], wkv).astype(bf16)
        k_ref[rows, :] = kv[:, :256]
        v_ref[rows, :] = kv[:, 256:]
        return carry

    lax.fori_loop(0, TILES, tile, 0)

    for ref in (q_ref, k_ref, v_ref):
        io.send(ref)
    attend_docs(meta, False, rank_ref, limit_ref, [(q_ref, k_ref, v_ref, mixed_ref)], p_ref, p_buf, p_sem)

    io.send(mixed_ref)
    io.wait("late")
    out_first = jnp.concatenate([w_out(w0_ref), w_out(w1_ref)], axis=0)
    out_second = jnp.concatenate([w_out(w2_ref), w_out(w3_ref)], axis=0)

    def tile(i, carry):
        rows = rows_of(i)
        branch = dot(mixed_first_ref[rows, :], out_first) + dot(mixed_ref[rows, :], out_second)
        second = xq_ref[rows, :].astype(f32) + branch
        second_ref[rows, :] = second
        io.send(second_ref, rows)
        ncross_ref[rows, :] = layer_norm(second, norms_ref[4:5], norms_ref[5:6])
        io.send(ncross_ref, rows)
        return carry

    lax.fori_loop(0, TILES, tile, 0)


def project_cross(io, ncross_ref, memory_ref, weights, q_ref, k_ref, v_ref):
    wq = lanes([w_query(w) for w in weights])
    wkv = lanes([w_key(w) for w in weights] + [w_value(w) for w in weights])

    def tile(i, carry):
        rows = rows_of(i)
        io.wait_rows(i)
        q_ref[rows, :] = (dot(ncross_ref[rows, :], wq) * (HEAD_DIM**-0.5)).astype(bf16)
        kv = dot(memory_ref[rows, :], wkv).astype(bf16)
        k_ref[rows, :] = kv[:, :256]
        v_ref[rows, :] = kv[:, 256:]
        return carry

    lax.fori_loop(0, TILES, tile, 0)
    for ref in (q_ref, k_ref, v_ref):
        io.send(ref)


def cross_first(
    meta, io, ncross_ref, memory_ref, w0_ref, w1_ref,
    q_ref, k_ref, v_ref, mixed_ref, p_ref, p_buf, p_sem,
):
    project_cross(io, ncross_ref, memory_ref, (w0_ref, w1_ref), q_ref, k_ref, v_ref)
    attend_docs(meta, True, None, None, [(q_ref, k_ref, v_ref, mixed_ref)], p_ref, p_buf, p_sem)


def cross_second(
    meta, io, second_ref, ncross_ref, memory_ref, norms_ref, w0_ref, w1_ref, w2_ref, w3_ref,
    mixed_first_ref,
    q_ref, k_ref, v_ref, mixed_ref, p_ref, third_ref, nffn_ref, p_buf, p_sem,
):
    project_cross(io, ncross_ref, memory_ref, (w2_ref, w3_ref), q_ref, k_ref, v_ref)
    attend_docs(meta, True, None, None, [(q_ref, k_ref, v_ref, mixed_ref)], p_ref, p_buf, p_sem)
    io.send(mixed_ref)
    io.wait("late")
    out_first = jnp.concatenate([w_out(w0_ref), w_out(w1_ref)], axis=0)
    out_second = jnp.concatenate([w_out(w2_ref), w_out(w3_ref)], axis=0)

    def tile(i, carry):
        rows = rows_of(i)
        branch = dot(mixed_first_ref[rows, :], out_first) + dot(mixed_ref[rows, :], out_second)
        third = second_ref[rows, :] + branch
        third_ref[rows, :] = third
        nffn_ref[rows, :] = layer_norm(third, norms_ref[6:7], norms_ref[7:8])
        return carry

    lax.fori_loop(0, TILES, tile, 0)


def ffn_both(
    meta, io, third_ref, nffn_ref, cot_ref, norms_ref, u0_ref, u1_ref, u2_ref, u3_ref,
    w0_ref, w1_ref, w2_ref, w3_ref,
    placed_ref, out_ref, g3_ref, g3_low_ref, gln_ref, own_ref, other_ref, hidden_ref, before_ref, sums_ref,
):
    sums_ref[...] = jnp.zeros_like(sums_ref)
    in_refs = (u0_ref, u1_ref, u2_ref, u3_ref)
    w_refs = (w0_ref, w1_ref, w2_ref, w3_ref)

    def tile(i, carry):
        rows = rows_of(i)
        io.wait_rows(i)
        nffn = nffn_ref[rows, :]
        cot = cot_ref[rows, :]
        outs = []
        grads = []

        def phases(g, c, group):
            w_in = in_refs[g]
            w_out_rows = w_refs[g]
            cols = slice(256 * c, 256 * c + 256)

            def enter():
                return dot(nffn, w_in[:, cols]), dot_nt(cot, w_out_rows[cols, :])

            def bend(state):
                def piece(x, grad_hidden):
                    square = x * x
                    argument = x * (gelu_root + (gelu_root * gelu_cube) * square)
                    half = 0.5 + 0.5 * jnp.tanh(argument.astype(bf16))
                    x = x.astype(bf16)
                    square = square.astype(bf16)
                    value = x * half
                    rise = 2.0 * gelu_root + (6.0 * gelu_root * gelu_cube) * square
                    slope = half + value * (1.0 - half) * rise
                    return value, grad_hidden.astype(bf16) * slope

                hidden, grad_before = by_pieces(piece, 32, 0, *state)
                if g < 2:
                    place = slice(512 * g + 256 * c, 512 * g + 256 * c + 256)
                    hidden_ref[rows, place] = hidden
                    before_ref[rows, place] = grad_before
                group[c] = hidden, grad_before

            def leave(_):
                if c == 1:
                    outs.append(dot(lanes([group[0][0], group[1][0]]), w_out_rows[...]))

            def leave_back(_):
                if c == 1:
                    grads.append(dot_nt(lanes([group[0][1], group[1][1]]), w_in[...]))

            return enter, bend, leave, leave_back

        interleave(by_halves(4, phases))
        third = third_ref[rows, :]
        result = (third + ((outs[0] + outs[1]) + (outs[2] + outs[3]))).astype(bf16)
        out_ref[rows, :] = result
        placed_ref[rows, :] = result
        grad_normed = (grads[0] + grads[1]) + (grads[2] + grads[3])
        grad_norm = norm_backward(third, norms_ref[6:7], grad_normed, sums_ref, 0)
        g3 = cot.astype(f32) + grad_norm
        g3_ref[rows, :] = g3
        g3_low_ref[rows, :] = g3.astype(bf16)
        for ref in (out_ref, placed_ref, g3_ref, g3_low_ref):
            io.send(ref, rows)
        return carry

    lax.fori_loop(0, TILES, tile, 0)
    add_sums(sums_ref, gln_ref, 2)
    part = dot_tn(nffn_ref[...], before_ref[...])
    own_ref[0:512, :] = part[:, 0:512].astype(bf16)
    other_ref[0:512, :] = part[:, 512:1024].astype(bf16)
    io.send(own_ref, pl.ds(0, 512))
    io.send(other_ref, pl.ds(0, 512))
    part = dot_tn(hidden_ref[...], cot_ref[...])
    own_ref[512:1024, :] = part[0:512].astype(bf16)
    other_ref[512:1024, :] = part[512:1024].astype(bf16)
    io.send(own_ref, pl.ds(512, 512))
    io.send(other_ref, pl.ds(512, 512))


def back_start(io, g_ref, mixed_ref, w_refs, dm_ref, dq_ref, dk_ref, dv_ref):
    out_rows = jnp.concatenate([w_out(w) for w in w_refs], axis=0)

    def tile(i, carry):
        rows = rows_of(i)
        io.wait_rows(i)
        dm_ref[rows, :] = dot_nt(g_ref[rows, :], out_rows).astype(bf16)
        zeros = jnp.zeros((TILE, 256), f32)
        dq_ref[rows, :] = zeros
        dk_ref[rows, :] = zeros
        dv_ref[rows, :] = zeros
        return carry

    lax.fori_loop(0, TILES, tile, 0)


def attention_back_first(
    cross, meta, io, g_ref, nq_ref, nkv_ref, rank_row_ref, limit_ref, w0_ref, w1_ref,
    q_ref, k_ref, v_ref, mixed_ref, p_ref,
    dq_ref, dk_ref, dv_ref, own_ref, other_ref,
    rank_ref, dm_ref, dqs_ref, dks_ref, dvs_ref, p_buf, p_sem,
):
    load = (p_ref, p_buf, p_sem)
    start_load(meta, cross, load)
    if not cross:
        spread_ranks(rank_row_ref, rank_ref)
    back_start(io, g_ref, mixed_ref, (w0_ref, w1_ref), dm_ref, dqs_ref, dks_ref, dvs_ref)

    io.wait("soon")
    attend_docs_back(
        meta, cross, None if cross else rank_ref, limit_ref, q_ref, k_ref, v_ref, mixed_ref,
        dm_ref, dqs_ref, dks_ref, dvs_ref, load,
    )

    dq_ref[...] = dqs_ref[...].astype(bf16)
    dk_ref[...] = dks_ref[...].astype(bf16)
    dv_ref[...] = dvs_ref[...].astype(bf16)
    for ref in (dq_ref, dk_ref, dv_ref):
        io.send(ref)
    io.wait("late")
    nq = nq_ref[...]
    nkv = nkv_ref[...]
    kv = dot_tn(nkv, lanes([dk_ref[...], dv_ref[...]]))
    for n, part in enumerate((dot_tn(nq, dq_ref[...]), kv[:, 0:256], kv[:, 256:512])):
        own_ref[:, 128 * n : 128 * n + 128] = part[:, :128].astype(bf16)
        other_ref[:, 128 * n : 128 * n + 128] = part[:, 128:].astype(bf16)
    part = dot_tn(mixed_ref[...], g_ref[...])
    for j in range(4):
        rows = slice(128 * j, 128 * j + 128)
        own_ref[rows, 384:512] = part[:128, rows].astype(bf16)
        other_ref[rows, 384:512] = part[128:, rows].astype(bf16)


def back_second_docs(
    cross, meta, io, g_ref, rank_row_ref, limit_ref, w_refs, q_ref, k_ref, v_ref, mixed_ref, p_ref,
    rank_ref, dm_ref, dqs_ref, dks_ref, dvs_ref, p_buf, p_sem,
):
    load = (p_ref, p_buf, p_sem)
    start_load(meta, cross, load)
    if not cross:
        spread_ranks(rank_row_ref, rank_ref)
    back_start(io, g_ref, mixed_ref, w_refs, dm_ref, dqs_ref, dks_ref, dvs_ref)

    io.wait("soon")
    attend_docs_back(
        meta, cross, None if cross else rank_ref, limit_ref, q_ref, k_ref, v_ref, mixed_ref,
        dm_ref, dqs_ref, dks_ref, dvs_ref, load,
    )


def stream_grads(rows, first, second, firsts, seconds):
    dq, dk, dv = first
    dq2, dk2, dv2 = (ref[rows, :].astype(bf16) for ref in second)
    w0, w1 = firsts
    w2, w3 = seconds
    grad_q = dot_nt(dq[rows, :], lanes([w_query(w0), w_query(w1)])) + dot_nt(
        dq2, lanes([w_query(w2), w_query(w3)])
    )
    kv = lanes([dk[rows, :], dv[rows, :]])
    kv2 = lanes([dk2, dv2])
    grad_kv = dot_nt(kv, lanes([w_key(w0), w_key(w1), w_value(w0), w_value(w1)])) + dot_nt(
        kv2, lanes([w_key(w2), w_key(w3), w_value(w2), w_value(w3)])
    )
    return grad_q, grad_kv


def cross_back_second(
    meta, io, g_low_ref, g_ref, second_ref, norms_ref, w0_ref, w1_ref, w2_ref, w3_ref,
    dq_ref, dk_ref, dv_ref, q_ref, k_ref, v_ref, mixed_ref, p_ref,
    g2_ref, g2_low_ref, placed_ref, gmem_ref, gln_ref,
    dm_ref, dqs_ref, dks_ref, dvs_ref, p_buf, p_sem, sums_ref,
):
    back_second_docs(
        True, meta, io, g_low_ref, None, None, (w2_ref, w3_ref), q_ref, k_ref, v_ref, mixed_ref, p_ref,
        None, dm_ref, dqs_ref, dks_ref, dvs_ref, p_buf, p_sem,
    )

    io.wait("late")
    sums_ref[...] = jnp.zeros_like(sums_ref)

    def tile(i, carry):
        rows = rows_of(i)
        grad_q, grad_kv = stream_grads(
            rows,
            (dq_ref, dk_ref, dv_ref),
            (dqs_ref, dks_ref, dvs_ref),
            (w0_ref, w1_ref),
            (w2_ref, w3_ref),
        )
        low_kv = grad_kv.astype(bf16)
        gmem_ref[rows, :] = low_kv
        placed_ref[rows, :] = low_kv.astype(f32)
        io.send(gmem_ref, rows)
        io.send(placed_ref, rows)
        grad_norm = norm_backward(second_ref[rows, :], norms_ref[4:5], grad_q, sums_ref, 0)
        g2 = g_ref[rows, :] + grad_norm
        g2_ref[rows, :] = g2
        g2_low_ref[rows, :] = g2.astype(bf16)
        io.send(g2_ref, rows)
        io.send(g2_low_ref, rows)
        return carry

    lax.fori_loop(0, TILES, tile, 0)
    add_sums(sums_ref, gln_ref, 2)


def self_back_second(
    meta, io, g_low_ref, rank_row_ref, limit_ref, w2_ref, w3_ref,
    q_ref, k_ref, v_ref, mixed_ref, p_ref,
    dq_ref, dk_ref, dv_ref,
    rank_ref, dm_ref, dqs_ref, dks_ref, dvs_ref, p_buf, p_sem,
):
    back_second_docs(
        False, meta, io, g_low_ref, rank_row_ref, limit_ref, (w2_ref, w3_ref), q_ref, k_ref, v_ref,
        mixed_ref, p_ref, rank_ref, dm_ref, dqs_ref, dks_ref, dvs_ref, p_buf, p_sem,
    )
    dq_ref[...] = dqs_ref[...].astype(bf16)
    dk_ref[...] = dks_ref[...].astype(bf16)
    dv_ref[...] = dvs_ref[...].astype(bf16)


def self_back_finish(
    meta, io, g_ref, xq_ref, xc_ref, norms_ref, w0_ref, w1_ref, w2_ref, w3_ref,
    dq_ref, dk_ref, dv_ref, dq2_ref, dk2_ref, dv2_ref,
    placed_q_ref, placed_c_ref, gq_ref, gc_ref, gln_ref, sums_ref,
):
    sums_ref[...] = jnp.zeros_like(sums_ref)

    def tile(i, carry):
        rows = rows_of(i)
        io.wait_rows(i)
        grad_q, grad_kv = stream_grads(
            rows,
            (dq_ref, dk_ref, dv_ref),
            (dq2_ref, dk2_ref, dv2_ref),
            (w0_ref, w1_ref),
            (w2_ref, w3_ref),
        )
        grad_norm = norm_backward(xq_ref[rows, :], norms_ref[0:1], grad_q, sums_ref, 0)
        low_q = (g_ref[rows, :] + grad_norm).astype(bf16)
        gq_ref[rows, :] = low_q
        placed_q_ref[rows, :] = low_q.astype(f32)
        io.send(gq_ref, rows)
        io.send(placed_q_ref, rows)
        grad_norm = norm_backward(xc_ref[rows, :], norms_ref[2:3], grad_kv, sums_ref, 16)
        low_c = grad_norm.astype(bf16)
        gc_ref[rows, :] = low_c
        placed_c_ref[rows, :] = low_c.astype(f32)
        io.send(gc_ref, rows)
        io.send(placed_c_ref, rows)
        return carry

    lax.fori_loop(0, TILES, tile, 0)
    add_sums(sums_ref, gln_ref, 4)


def place_rows(meta, *refs):
    count = len(refs) // 3
    for n in range(count):
        refs[2 * count + n][...] = refs[n][...].astype(refs[2 * count + n].dtype)


GROUP = 8


def position(meta):
    r = meta[35]
    return lax.rem(r, 2), r // 2


def join(own, other, rows):
    return (own[rows, :].astype(f32) + other[rows, :].astype(f32)).astype(bf16)


def join_halves(meta, own, other, keep, send):
    y, _ = position(meta)
    size = keep.shape[0]
    keep[...] = join(own, other, rows_of(y, size))
    send[...] = join(own, other, rows_of(1 - y, size))


def join_chunks(meta, kept, arrived, keep, sends):
    _, z = position(meta)
    size = keep.shape[0]
    keep[...] = join(kept, arrived, rows_of(z, size))
    for s, (send, first) in enumerate(sends, 1):
        send[first : first + size, :] = join(kept, arrived, rows_of(z ^ s, size))


def add_up(kept, parts, first):
    size = kept.shape[0]
    total = kept[...].astype(f32)
    for part in parts:
        total = total + part[first : first + size, :].astype(f32)
    return total.astype(bf16)


def half_of(meta, total, parts, first, half):
    _, z = position(meta)
    size = total.shape[0]
    half[rows_of(z, size), :] = total[...]
    for s, part in enumerate(parts, 1):
        half[rows_of(z ^ s, size), :] = part[first : first + size, :]


def slot_1(meta, ffn_own, ffn_other, keep, send):
    join_halves(meta, ffn_own, ffn_other, keep, send)


def slot_2(
    meta, ffn_kept, ffn_arrived, cross_own, cross_other, ffn_keep, f1, f2, f3, keep, send
):
    join_chunks(meta, ffn_kept, ffn_arrived, ffn_keep, [(f1, 0), (f2, 0), (f3, 0)])
    join_halves(meta, cross_own, cross_other, keep, send)


def slot_3(
    meta, ffn_kept, f1, f2, f3, cross_kept, cross_arrived, self_own, self_other,
    ffn_total, cross_keep, m1, m2, m3, self_keep, self_send,
):
    join_halves(meta, self_own, self_other, self_keep, self_send)
    total = add_up(ffn_kept, (f1, f2, f3), 0)
    ffn_total[...] = total
    size = total.shape[0]
    join_chunks(meta, cross_kept, cross_arrived, cross_keep, [(m, size) for m in (m1, m2, m3)])
    for m in (m1, m2, m3):
        m[0:size, :] = total


def slot_4(
    meta, ffn_total, m1, m2, m3, cross_kept, self_kept, self_arrived,
    ffn_half, cross_total, self_keep, *sends,
):
    join_chunks(meta, self_kept, self_arrived, self_keep, [(send, 0) for send in sends])
    total = add_up(cross_kept, (m1, m2, m3), ffn_total.shape[0])
    cross_total[...] = total
    size = total.shape[0]
    for send in sends:
        send[size:, :] = total
    half_of(meta, ffn_total, (m1, m2, m3), 0, ffn_half)


def slot_5(meta, self_kept, cross_total, m1, m2, m3, gln_own, gln_other, send, cross_half):
    size = self_kept.shape[0]
    total = add_up(self_kept, (m1, m2, m3), 0)
    gln = gln_own[...] + gln_other[...]
    gln = jnp.concatenate([gln, jnp.zeros((8, D), f32)], axis=0).astype(bf16)
    for r in range(GROUP):
        send[r, 0:size, :] = total
        send[r, size : size + 16, :] = gln
    half_of(meta, cross_total, (m1, m2, m3), size, cross_half)


def unpack_attention(whole_ref, outs):
    for i in range(3):
        outs[i][...] = whole_ref[:, 128 * i : 128 * i + 128].astype(f32)
    for j in range(4):
        rows = slice(128 * j, 128 * j + 128)
        outs[3][:, rows] = whole_ref[rows, 384:512].astype(f32)


def unpack_ffn(meta, half, arrived, out_in, out_out, ffn_whole):
    y, _ = position(meta)
    ffn_whole[rows_of(y, 512), :] = half[...]
    ffn_whole[rows_of(1 - y, 512), :] = arrived[...]
    out_in[...] = ffn_whole[0:512, :].astype(f32)
    out_out[...] = ffn_whole[512:1024, :].astype(f32)


def unpack_rest(meta, cross_half, cross_arrived, parts, *refs):
    *outs, gln, whole_ref = refs
    y, _ = position(meta)
    whole_ref[rows_of(y, 256), :] = cross_half[...]
    whole_ref[rows_of(1 - y, 256), :] = cross_arrived[...]
    unpack_attention(whole_ref, outs[0:4])
    size = parts.shape[1] - 16
    total = parts[0, size : size + 16, :].astype(f32)
    for r in range(1, GROUP):
        total = total + parts[r, size : size + 16, :].astype(f32)
    gln[...] = total[0:8]
    for r in range(GROUP):
        first = size * (4 * (r % 2) + r // 2)
        whole_ref[first : first + size, :] = parts[r, 0:size, :]
    unpack_attention(whole_ref, outs[4:8])


def whole(shape):
    zeros = (0,) * len(shape)
    return pl.BlockSpec(shape, lambda d, meta: zeros)


def own_row(width):
    return pl.BlockSpec((SEQ, width), lambda d, meta: (meta[0], 0))


ANY = pl.BlockSpec(memory_space=pl.ANY)


def in_hbm(x):
    return pltpu.with_memory_space_constraint(x, pltpu.HBM)


probability_out = (pltpu.HBM((DOCS, 4, FAST_K, FAST_Q), bf16), None, ANY)
probability_scratch = [
    pltpu.VMEM((2, TOGETHER, 4, FAST_K, FAST_Q), bf16),
    pltpu.SemaphoreType.DMA((2,)),
]


class Copies:
    def __init__(self, meta):
        self.first = meta[0] * SEQ
        self.loads = {}
        self.tiles = []
        self.sends = []

    def load(self, stage, source, target, sems, own_row):
        if stage == "tiles":
            first = self.first if own_row else 0
            self.tiles.append((source, target, sems, first))
            return
        if own_row:
            source = source.at[pl.ds(pl.multiple_of(self.first, SEQ), SEQ)]
        copy = pltpu.make_async_copy(source, target, sems[0].at[sems[1], 0])
        self.loads.setdefault(stage, []).append(copy)

    def tile(self, entry, i):
        source, target, (sems, b), first = entry
        rows = pl.ds(pl.multiple_of(first + i * TILE, TILE), TILE)
        return pltpu.make_async_copy(source.at[rows], target.at[rows_of(i)], sems.at[b, i])

    def start(self):
        for copy in self.loads.get("now", []):
            copy.start()
        for i in range(TILES):
            for entry in self.tiles:
                self.tile(entry, i).start()
        for stage in ("soon", "late"):
            for copy in self.loads.get(stage, []):
                copy.start()

    def wait(self, stage):
        for copy in self.loads.pop(stage, []):
            copy.wait()

    def wait_rows(self, i):
        for entry in self.tiles:
            self.tile(entry, i).wait()

    def result(self, source, target, sem, own_row):
        self.sends.append([source, target, sem, own_row, False])

    def send(self, ref, rows=None):
        for entry in self.sends:
            source, target, sem, own_row, _ = entry
            if source is ref:
                entry[4] = True
                first = self.first if own_row else 0
                if rows is None:
                    size = source.shape[0]
                else:
                    source = source.at[rows]
                    first, size = first + rows.start, rows.size
                if rows is not None or own_row:
                    target = target.at[pl.ds(pl.multiple_of(first, size), size)]
                pltpu.make_async_copy(source, target, sem).start()

    def finish(self):
        for stage in list(self.loads):
            self.wait(stage)
        for source, _, _, _, started in self.sends:
            if not started:
                self.send(source)
        for source, target, sem, own_row, _ in self.sends:
            if own_row:
                target = target.at[pl.ds(pl.multiple_of(self.first, SEQ), SEQ)]
            pltpu.make_async_copy(source, target, sem).wait()


def out(shape, dtype, own_row=False):
    return (shape, dtype, own_row)


def call(kernel, name, operands, outs, scratch, flops, token=None):
    arrays = [operands[0][0]]
    in_specs, out_specs, out_shapes = [], [], []
    buffers = []
    loads = []
    for n, (x, how) in enumerate(operands[1:]):
        if isinstance(how, str):
            stage, _, row = how.partition("_")
            shape = ((SEQ,) + x.shape[1:]) if row else x.shape
            loads.append((n, stage, len(buffers), bool(row)))
            buffers.append(pltpu.VMEM(shape, x.dtype))
            arrays.append(in_hbm(x))
            in_specs.append(ANY)
        else:
            arrays.append(x)
            in_specs.append(how)
    results = []
    for n, (shape, dtype, how) in enumerate(outs):
        if isinstance(how, bool):
            results.append((n, len(buffers), how))
            buffers.append(pltpu.VMEM(shape, dtype))
            shape = ((2 * SEQ,) + shape[1:]) if how else shape
            out_shapes.append(pltpu.HBM(shape, dtype))
            out_specs.append(ANY)
        else:
            out_shapes.append(jax.ShapeDtypeStruct(shape, dtype) if dtype else shape)
            out_specs.append(how)
    n_in, n_out = len(in_specs), len(out_specs)
    if token is not None:
        arrays.append(token)
        in_specs.append(whole((8, 128)))
        out_specs.append(whole((8, 128)))
        out_shapes.append(jax.ShapeDtypeStruct((8, 128), f32))

    def body(meta, *refs):
        ins, refs = list(refs[:n_in]), refs[len(in_specs) - n_in + n_in :]
        results_out, refs = list(refs[:n_out]), refs[n_out:]
        if token is not None:
            token_out, refs = refs[0], refs[1:]
            token_out[...] = jnp.zeros_like(token_out)
        bufs, refs = refs[: len(buffers)], refs[len(buffers) :]
        rest = refs[: len(scratch)]
        copies = Copies(meta)
        if buffers:
            sems = refs[len(scratch)]
        for n, stage, b, row in loads:
            copies.load(stage, ins[n], bufs[b], (sems, b), row)
            ins[n] = bufs[b]
        for n, b, row in results:
            copies.result(bufs[b], results_out[n], sems.at[b, 0], row)
            results_out[n] = bufs[b]
        copies.start()
        copies.wait("now")
        if buffers:
            kernel(meta, copies, *ins, *results_out, *rest)
        else:
            kernel(meta, *ins, *results_out, *rest)
        copies.finish()

    moved = sum(x.size * x.dtype.itemsize for x in arrays[1:])
    sems = [pltpu.SemaphoreType.DMA((len(buffers), TILES))] if buffers else []
    return pl.pallas_call(
        body,
        name=name,
        grid_spec=pltpu.PrefetchScalarGridSpec(
            num_scalar_prefetch=1,
            grid=(1,),
            in_specs=in_specs,
            out_specs=out_specs,
            scratch_shapes=buffers + scratch + sems,
        ),
        out_shape=out_shapes,
        compiler_params=pltpu.CompilerParams(
            dimension_semantics=("arbitrary",), vmem_limit_bytes=40 * 1024 * 1024
        ),
        cost_estimate=pl.CostEstimate(
            flops=int(flops), bytes_accessed=int(moved), transcendentals=0
        ),
    )(*arrays)


def simple(kernel, name, meta, operands, outs, scratch=()):
    return pl.pallas_call(
        kernel,
        name=name,
        grid_spec=pltpu.PrefetchScalarGridSpec(
            num_scalar_prefetch=1,
            grid=(1,),
            in_specs=[whole(x.shape) for x in operands],
            out_specs=[whole(shape) for shape, _ in outs],
            scratch_shapes=scratch,
        ),
        out_shape=[jax.ShapeDtypeStruct(shape, dtype) for shape, dtype in outs],
        compiler_params=pltpu.CompilerParams(vmem_limit_bytes=16 * 1024 * 1024),
    )(meta, *operands)


def full(x):
    return (x, whole(x.shape))


def shards(
    query_stream,
    content_stream,
    memory,
    segment_ids,
    source_segments,
    context_rank,
    context_limit,
    padding,
    ln_query_gain,
    ln_query_bias,
    ln_content_gain,
    ln_content_bias,
    self_query,
    self_key,
    self_value,
    self_out,
    ln_cross_gain,
    ln_cross_bias,
    cross_query,
    cross_key,
    cross_value,
    cross_out,
    ln_ffn_gain,
    ln_ffn_bias,
    ffn_in,
    ffn_out,
    cotangent,
):
    core = lax.axis_index("heads") % 2

    def to_core(x):
        return lax.ppermute(x, "heads", [(h, h ^ 1) for h in range(4)])

    hold = lambda *xs: lax.optimization_barrier(xs)

    def to_chip(x):
        return lax.ppermute(x, "heads", [(h, h ^ 2) for h in range(4)])

    row = pl.BlockSpec((1, 8, 128), lambda d, core: (core[0], 0, 0))

    def token_row(x):
        return (in_hbm(x.reshape(2, 8, 128)), row)

    def fixed(x):
        zeros = (0,) * x.ndim
        return (in_hbm(x), pl.BlockSpec(x.shape, lambda d, core: zeros))

    prepared = [
        ((36,), jnp.int32, pl.BlockSpec(memory_space=pltpu.SMEM)),
        ((1, SEQ), f32, whole((1, SEQ))),
        ((1, SEQ), f32, whole((1, SEQ))),
        ((8, D), f32, whole((8, D))),
        ((D, D), bf16, whole((D, D))),
        ((D, D), bf16, whole((D, D))),
    ]
    gains = (
        ln_query_gain,
        ln_query_bias,
        ln_content_gain,
        ln_content_bias,
        ln_cross_gain,
        ln_cross_bias,
        ln_ffn_gain,
        ln_ffn_bias,
    )
    weights = (self_query, self_key, self_value, self_out)
    weights += (cross_query, cross_key, cross_value, cross_out)
    tokens = (segment_ids, source_segments, context_rank, context_limit, padding)
    meta, rank, limit, norms, ws0, wc0 = call(
        prepare,
        "prepare",
        [(jnp.stack([core, lax.axis_index("rows") % GROUP]).astype(jnp.int32), None)]
        + [token_row(x) for x in tokens]
        + [fixed(x.reshape(1, D)) for x in gains]
        + [fixed(x) for x in weights],
        prepared,
        [],
        0,
    )

    ws1 = to_core(ws0)
    ws2 = to_chip(ws0)
    wc1 = to_core(wc0)
    u0, v0 = ffn_in, ffn_out
    meta_in = (meta, None)

    heads_out = [out((SEQ, 256), bf16)] * 4

    def stream_out(dtype, own_row=False):
        return out((SEQ, D), dtype, own_row)

    def now(*xs):
        return [(x, "now") for x in xs]

    def soon(*xs):
        return [(x, "soon") for x in xs]

    def late(*xs):
        return [(x, "late") for x in xs]

    def small(*xs):
        return [(x, whole(x.shape)) for x in xs]

    limits = pltpu.VMEM((SEQ, 128), f32)
    pair_flops = 2 * SEQ * D * 768 + 2 * 2 * 4 * DOCS * FAST_Q * FAST_K * 256

    nq, nc, *first, token = call(
        self_first,
        "self_first",
        [meta_in, (query_stream, "tiles_row"), (content_stream, "tiles_row")]
        + small(rank, limit, norms)
        + now(ws0, ws1),
        [stream_out(bf16), stream_out(bf16)] + heads_out + [probability_out],
        [limits] + probability_scratch,
        pair_flops,
        jnp.zeros((8, 128), f32),
    )
    ws2, wc0, token = hold(ws2, wc0, token)
    ws3 = to_core(ws2)
    wc2 = to_chip(wc0)
    *second_heads, second, ncross, token = call(
        self_second,
        "self_second",
        [meta_in, (query_stream, "late_row")]
        + [(nq, "tiles"), (nc, "tiles")]
        + small(rank, limit, norms)
        + late(ws0, ws1)
        + now(ws2, ws3)
        + late(first[3]),
        heads_out + [probability_out, stream_out(f32), stream_out(bf16)],
        [limits] + probability_scratch,
        pair_flops + 2 * SEQ * D * D,
        token,
    )
    wc2, u0, v0, token = hold(wc2, u0, v0, token)
    wc3 = to_core(wc2)
    u2 = to_chip(u0)
    u1 = to_core(u0)
    *cross_heads, token = call(
        cross_first,
        "cross_first",
        [meta_in, (ncross, "tiles"), (memory, "tiles_row")] + now(wc0, wc1),
        heads_out + [probability_out],
        probability_scratch,
        pair_flops,
        token,
    )
    wc3, u2, v0, token = hold(wc3, u2, v0, token)
    u3 = to_core(u2)
    v2 = to_chip(v0)
    v1 = to_core(v0)
    *cross_heads_second, third, nffn, token = call(
        cross_second,
        "cross_second",
        [meta_in]
        + late(second)
        + [(ncross, "tiles"), (memory, "tiles_row")]
        + small(norms)
        + late(wc0, wc1)
        + now(wc2, wc3)
        + late(cross_heads[3]),
        heads_out
        + [probability_out, ((SEQ, D), f32, whole((SEQ, D))), ((SEQ, D), bf16, whole((SEQ, D)))],
        probability_scratch,
        pair_flops + 2 * SEQ * D * D,
        token,
    )
    u3, v2, token = hold(u3, v2, token)
    v3 = to_core(v2)
    grads_ln = ((8, D), f32, whole((8, D)))
    placed_output, output, g3, g3_low, gln_ffn, ffn_own, ffn_other, token = call(
        ffn_both,
        "ffn_both",
        [meta_in]
        + small(third, nffn)
        + [(cotangent, "tiles_row")]
        + small(norms)
        + now(u0, u1, u2, u3, v0, v1, v2, v3),
        [
            stream_out(bf16, True),
            stream_out(bf16),
            stream_out(f32),
            stream_out(bf16),
            grads_ln,
            out((1024, D), bf16),
            out((1024, D), bf16),
        ],
        [pltpu.VMEM((SEQ, 1024), bf16), pltpu.VMEM((SEQ, 1024), bf16), pltpu.VMEM((16, D), f32)],
        12 * SEQ * D * 2048,
        token,
    )

    def both_rows(placed_own, others, name):
        count = len(others)
        size = SEQ // 2
        one = pl.BlockSpec((size, D), lambda i, meta: (i, 0))
        block = pl.BlockSpec((size, D), lambda i, meta: (2 * (1 - meta[0]) + i, 0))
        return pl.pallas_call(
            place_rows,
            name=name,
            grid_spec=pltpu.PrefetchScalarGridSpec(
                num_scalar_prefetch=1,
                grid=(2,),
                in_specs=[one] * count + [pl.BlockSpec(memory_space=pl.ANY)] * count,
                out_specs=[block] * count,
            ),
            out_shape=[jax.ShapeDtypeStruct(x.shape, x.dtype) for x in placed_own],
            input_output_aliases={1 + count + n: n for n in range(count)},
        )(meta, *others, *placed_own)

    row_count = lax.axis_size("rows")
    assert row_count % GROUP == 0

    def along_rows(x, s):
        return lax.ppermute(x, "rows", [(r, r ^ s) for r in range(row_count)])

    def to_y(x):
        return along_rows(x, 1)

    def to_z(sends):
        return [along_rows(x, 2 * s) for s, x in enumerate(sends, 1)]

    def rows_out(*sizes):
        return [((n, D), bf16) for n in sizes]

    ffn_other = to_core(ffn_other)
    output_other = to_core(output)

    back_scratch = [pltpu.VMEM((SEQ, 256), bf16)] + [pltpu.VMEM((SEQ, 256), f32)] * 3
    back_scratch += probability_scratch
    pair_out = out((SEQ, 256), bf16)
    packed_outs = [((D, D), bf16, whole((D, D)))] * 2
    back_flops = 2 * SEQ * D * 256 + 4 * 2 * 4 * DOCS * FAST_Q * FAST_K * 256

    def head_inputs(natural, p):
        return soon(*natural) + [(in_hbm(p), ANY)]

    *cross_grads, cross_own, cross_other, token = call(
        functools.partial(attention_back_first, True),
        "cross_back_first",
        [meta_in]
        + [(g3_low, "tiles")]
        + late(ncross)
        + [(memory, "late_row")]
        + small(rank, limit)
        + now(wc0, wc1)
        + head_inputs(cross_heads[0:4], cross_heads[4]),
        [pair_out] * 3 + packed_outs,
        [limits] + back_scratch,
        back_flops + 2 * SEQ * D * 1024,
        token,
    )
    ffn_other, output_other, token = hold(ffn_other, output_other, token)
    ffn_keep, ffn_send = simple(slot_1, "slot_1", meta, [ffn_own, ffn_other], rows_out(512, 512))
    ffn_send, token = hold(ffn_send, token)
    ffn_arrived = to_y(ffn_send)
    cross_other = to_core(cross_other)
    g2, g2_low, placed_mem, grad_mem, gln_cross, token = call(
        cross_back_second,
        "cross_back_second",
        [meta_in]
        + [(g3_low, "tiles")]
        + late(g3, second)
        + small(norms)
        + late(wc0, wc1)
        + now(wc2, wc3)
        + late(*cross_grads)
        + head_inputs(cross_heads_second[0:4], cross_heads_second[4]),
        [stream_out(f32), stream_out(bf16), stream_out(f32, True), stream_out(bf16), grads_ln],
        back_scratch + [pltpu.VMEM((16, D), f32)],
        back_flops + 2 * SEQ * D * 1536,
        token,
    )
    ffn_arrived, cross_other, token = hold(ffn_arrived, cross_other, token)
    ffn_keep, *sends, cross_keep, cross_send = simple(
        slot_2,
        "slot_2",
        meta,
        [ffn_keep, ffn_arrived, cross_own, cross_other],
        rows_out(128, 128, 128, 128, 256, 256),
    )
    ffn_keep, cross_send, token = hold(ffn_keep, cross_send, token)
    ffn_parts = to_z(sends)
    cross_arrived = to_y(cross_send)

    *self_grads, self_own, self_other, token = call(
        functools.partial(attention_back_first, False),
        "self_back_first",
        [meta_in]
        + [(g2_low, "tiles")]
        + late(nq, nc)
        + small(rank, limit)
        + now(ws0, ws1)
        + head_inputs(first[0:4], first[4]),
        [pair_out] * 3 + packed_outs,
        [limits] + back_scratch,
        back_flops + 2 * SEQ * D * 1024,
        token,
    )
    *ffn_parts, cross_arrived, self_other, token = hold(
        *ffn_parts, cross_arrived, self_other, token
    )
    self_other = to_core(self_other)
    ffn_total, cross_keep, *sends, self_keep, self_send = simple(
        slot_3,
        "slot_3",
        meta,
        [ffn_keep, *ffn_parts, cross_keep, cross_arrived, self_own, self_other],
        rows_out(128, 64, 192, 192, 192, 256, 256),
    )
    ffn_total, self_send, grad_mem, token = hold(ffn_total, self_send, grad_mem, token)
    mem_other = to_core(grad_mem)
    self_arrived = to_y(self_send)
    messages = to_z(sends)
    *self_grads_second, token = call(
        self_back_second,
        "self_back_second",
        [meta_in, (g2_low, "tiles")]
        + small(rank, limit)
        + now(ws2, ws3)
        + head_inputs(second_heads[0:4], second_heads[4]),
        [pair_out] * 3,
        [limits] + back_scratch,
        back_flops,
        token,
    )
    output_other, mem_other, token = hold(output_other, mem_other, token)
    out_both, grad_mem_both = both_rows(
        [placed_output, placed_mem], [output_other, mem_other], "place_early"
    )
    *messages, self_arrived, out_both, token = hold(*messages, self_arrived, out_both, token)
    ffn_half, cross_total, self_keep, *sends = simple(
        slot_4,
        "slot_4",
        meta,
        [ffn_total, *messages, cross_keep, self_keep, self_arrived],
        rows_out(512, 64, 64, 128, 128, 128),
    )
    cross_total, ffn_half, token = hold(cross_total, ffn_half, token)
    messages = to_z(sends)
    ffn_arrived = to_y(ffn_half)
    placed_q, placed_c, gq, gc, gln_self, token = call(
        self_back_finish,
        "self_back_finish",
        [meta_in, (g2, "tiles"), (query_stream, "tiles_row"), (content_stream, "tiles_row")]
        + small(norms)
        + now(ws0, ws1, ws2, ws3)
        + [(x, "tiles") for x in self_grads + self_grads_second],
        [stream_out(f32, True), stream_out(f32, True), stream_out(bf16), stream_out(bf16), grads_ln],
        [pltpu.VMEM((32, D), f32)],
        2 * SEQ * D * 1536,
        token,
    )
    gln = jnp.concatenate([gln_self[0:4], gln_cross[0:2], gln_ffn[0:2]], axis=0)
    gln_other = to_core(gln)
    *messages, ffn_arrived, gln_ffn = hold(*messages, ffn_arrived, gln_ffn)
    last_send, cross_half = simple(
        slot_5,
        "slot_5",
        meta,
        [self_keep, cross_total, *messages, gln, gln_other],
        [((GROUP, 80, D), bf16), ((256, D), bf16)],
    )
    groups = None
    if row_count > GROUP:
        groups = [list(range(r, r + GROUP)) for r in range(0, row_count, GROUP)]
    def gather(x):
        return lax.all_to_all(x, "rows", 0, 0, axis_index_groups=groups)

    last_parts = gather(last_send)
    cross_arrived = to_y(cross_half)
    def over_groups(totals):
        if row_count == GROUP:
            return totals
        groups = [list(range(r, row_count, GROUP)) for r in range(GROUP)]
        return lax.psum(totals, "rows", axis_index_groups=groups)

    gq_both, gc_both = both_rows([placed_q, placed_c], [to_core(gq), to_core(gc)], "place_late")

    grad_ffn_in, grad_ffn_out = simple(
        unpack_ffn,
        "unpack_ffn",
        meta,
        [ffn_half, ffn_arrived],
        [((D, D), f32)] * 2,
        [pltpu.VMEM((2 * D, D), bf16)],
    )
    attention_outs = [((512, 128), f32)] * 3 + [((128, 512), f32)]
    cross_arrived, gq_both, grad_ffn_in = hold(cross_arrived, gq_both, grad_ffn_in)
    *parts, gln = simple(
        unpack_rest,
        "unpack_rest",
        meta,
        [cross_half, cross_arrived, last_parts],
        attention_outs * 2 + [((8, D), f32)],
        [pltpu.VMEM((D, D), bf16)],
    )
    grad_cross_parts, grad_self_parts = parts[:4], parts[4:]
    grad_ffn_in, grad_ffn_out, grad_cross_parts, grad_self_parts, gln = over_groups(
        (grad_ffn_in, grad_ffn_out, grad_cross_parts, grad_self_parts, gln)
    )
    return (
        out_both,
        gq_both,
        gc_both,
        grad_mem_both,
        gln[0],
        gln[1],
        gln[2],
        gln[3],
        *grad_self_parts,
        gln[4],
        gln[5],
        *grad_cross_parts,
        gln[6],
        gln[7],
        grad_ffn_in,
        grad_ffn_out,
    )


def solution(mesh):
    assert mesh.shape["heads"] == 4
    row_spec = P("rows", None)
    flat = P("rows")
    by_column = P(None, "heads")
    by_row = P("heads", None)
    attention = (by_column, by_column, by_column, by_row)
    in_specs = (
        (row_spec,) * 3
        + (flat,) * 5
        + (P(),) * 4
        + attention
        + (P(),) * 2
        + attention
        + (P(),) * 2
        + (by_column, by_row, row_spec)
    )
    out_specs = (
        (row_spec,) * 4
        + (P(),) * 4
        + attention
        + (P(),) * 2
        + attention
        + (P(),) * 2
        + (by_column, by_row)
    )
    return jax.shard_map(shards, mesh=mesh, in_specs=in_specs, out_specs=out_specs, check_vma=False)
```

```python
import functools

import jax
import jax.numpy as jnp
from jax import lax
from jax.experimental import pallas as pl
from jax.experimental.pallas import tpu as pltpu
from jax.sharding import PartitionSpec as P

HEAD_DIM = 64
SEQ = 1024
DOCS = 8
D = 512
TILE = 256
TILES = SEQ // TILE
FAST_Q = 256
FAST_K = 208
LONG_Q = 128
LONG_K = 640

norm_eps = 1e-05
masked_score = -1e30
hidden_rank = 1e6
gelu_root = 0.7978845608028654
gelu_cube = 0.044715

f32 = jnp.float32
bf16 = jnp.bfloat16


def dot(a, b):
    return lax.dot_general(a, b, (((1,), (0,)), ((), ())), preferred_element_type=f32)


def dot_nt(a, b):
    return lax.dot_general(a, b, (((1,), (1,)), ((), ())), preferred_element_type=f32)


def dot_tn(a, b):
    return lax.dot_general(a, b, (((0,), (0,)), ((), ())), preferred_element_type=f32)


def lanes(parts):
    return jnp.concatenate(parts, axis=1)


NORM_ROWS = 32


def layer_norm(values, gain, shift):
    def piece(part):
        part = part.astype(f32)
        centre = part - jnp.mean(part, axis=-1, keepdims=True)
        spread = jnp.mean(centre * centre, axis=-1, keepdims=True)
        return (centre * lax.rsqrt(spread + norm_eps) * gain + shift).astype(bf16)

    return by_pieces(piece, NORM_ROWS, 0, values)


def eight_rows(values):
    return sum(values[8 * i : 8 * i + 8] for i in range(1, values.shape[0] // 8)) + values[0:8]


def norm_backward(values, gain, grad, sums_ref, first):
    sums = []

    def piece(part, grad_part):
        part = part.astype(f32)
        centre = part - jnp.mean(part, axis=-1, keepdims=True)
        spread = jnp.mean(centre * centre, axis=-1, keepdims=True)
        scale = lax.rsqrt(spread + norm_eps)
        xhat = centre * scale
        eg = grad_part * gain
        mean_eg = jnp.mean(eg, axis=-1, keepdims=True)
        mean_egx = jnp.mean(eg * xhat, axis=-1, keepdims=True)
        sums.append((eight_rows(grad_part * xhat), eight_rows(grad_part)))
        return scale * (eg - mean_eg - xhat * mean_egx)

    result = by_pieces(piece, NORM_ROWS, 0, values, grad)
    for n, parts in enumerate(zip(*sums)):
        sums_ref[first + 8 * n : first + 8 * n + 8, :] += sum(parts[1:], parts[0])
    return result


def add_sums(sums_ref, gln_ref, count):
    gln_ref[...] = jnp.zeros_like(gln_ref)
    for n in range(count):
        gln_ref[n : n + 1, :] = jnp.sum(sums_ref[8 * n : 8 * n + 8, :], axis=0, keepdims=True)


def by_pieces(work, size, axis, *arrays):
    count = arrays[0].shape[axis] // size
    pieces = []
    for i in range(count):
        cut = (slice(size * i, size * i + size),)
        cut = cut if axis == 0 else (slice(None),) + cut
        pieces.append(work(*[x[cut] for x in arrays]))
    if not isinstance(pieces[0], tuple):
        return jnp.concatenate(pieces, axis=axis)
    return tuple(jnp.concatenate(parts, axis=axis) for parts in zip(*pieces))


def rows_of(i, size=TILE):
    return pl.ds(pl.multiple_of(i * size, size), size)


def w_query(ref):
    return ref[:, 0:128]


def w_key(ref):
    return ref[:, 128:256]


def w_value(ref):
    return ref[:, 256:384]


def w_out(ref):
    return lanes([ref[128 * j : 128 * j + 128, 384:512] for j in range(4)])


def half_masks():
    place = lax.broadcasted_iota(jnp.int32, (1, 128), 1)
    low = jnp.where(place < HEAD_DIM, 1.0, 0.0).astype(f32)
    return (low.astype(bf16), (1.0 - low).astype(bf16))


def doc_bounds(meta, d, source):
    base = 17 if source else 1
    return meta[base + d], meta[base + 8 + d]


def window_of(first, limit):
    return pl.multiple_of(jnp.minimum((first // 16) * 16, limit), 16)


def key_bias(ks, ke, k0, width):
    place = k0 + lax.broadcasted_iota(jnp.int32, (width, 128), 0)
    return jnp.where((place >= ks) & (place < ke), 0.0, masked_score)


def make_bias(rank_ref, limit_ref, ks, ke, q0, k0, span, width):
    if rank_ref is None:
        return lanes([key_bias(ks, ke, k0, width)] * (span // 128))
    place = k0 + lax.broadcasted_iota(jnp.int32, (width, 128), 0)
    ranks = rank_ref[pl.ds(k0, width), :]
    ranks = jnp.where((place < ks + 2) & (ranks < hidden_rank), -1.0, ranks)
    ranks = jnp.where((place >= ks) & (place < ke), ranks, hidden_rank)
    limits = jnp.broadcast_to(limit_ref[...], (8, SEQ))
    limits = pltpu.roll(limits, lax.rem(SEQ - q0, SEQ), 1)[0:1, 0:span]
    row = k0 + lax.broadcasted_iota(jnp.int32, (width, span), 0)
    column = q0 + lax.broadcasted_iota(jnp.int32, (width, span), 1)
    seen = (lanes([ranks] * (span // 128)) < limits) & (row != column)
    return jnp.where(seen, 0.0, masked_score)


TOGETHER = 4
STEPS = DOCS // TOGETHER


LAG = 2


def interleave(items):
    items = [list(phases) for phases in items]
    depth = max(len(phases) for phases in items)
    results = [None] * len(items)
    for tick in range(len(items) + LAG * (depth - 1)):
        for phase in range(depth):
            n = tick - LAG * phase
            if 0 <= n < len(items) and phase < len(items[n]):
                run = items[n][phase]
                results[n] = run() if phase == 0 else run(results[n])
    return results


def by_halves(pairs, phases):
    shared = [{} for _ in range(pairs)]
    return [phases(n, a, shared[n]) for n in range(pairs) for a in range(2)]


def is_fast(meta, cross):
    return meta[34 if cross else 33] == 1


def both_heads(x, masks):
    return jnp.concatenate([x * masks[0], x * masks[1]], axis=0)


def pair_scores(queries, keys, masks):
    return dot_nt(both_heads(keys, masks), queries)


def raised(scores, bias):
    def piece(part, bias_part):
        part = part + bias_part
        return jnp.exp((part - jnp.max(part, axis=0, keepdims=True)).astype(bf16))

    return by_pieces(piece, 128, 1, scores, bias)


def weighted_values(values, parts):
    width = values.shape[1]
    mixed = []
    shares = []
    for a, part in enumerate(parts):
        rows = jnp.concatenate([values[64 * a : 64 * a + 64], jnp.ones((16, width), bf16)], axis=0)
        sums = dot(rows, part)
        share = 1.0 / sums[64:65]
        mixed.append(sums[:64] * share)
        shares.append(part * share.astype(bf16))
    return jnp.concatenate(mixed, axis=0).astype(bf16), shares


def pair_gradient(rows, parts):
    across = jnp.transpose(rows)
    halves = [dot(across[64 * a : 64 * a + 64], part) for a, part in enumerate(parts)]
    return jnp.transpose((jnp.concatenate(halves, axis=0) * HEAD_DIM**-0.5).astype(bf16))


def for_docs(meta, cross, run, before, after):
    @pl.when(is_fast(meta, cross))
    def _():
        def step(i, carry):
            slot = lax.rem(i, 2)
            before(i, slot)
            items = []
            for place in range(TOGETHER):
                d = TOGETHER * i + place
                ts, te = doc_bounds(meta, d, False)
                ks, ke = doc_bounds(meta, d, cross)
                q0 = window_of(ts, SEQ - FAST_Q)
                k0 = window_of(ks, SEQ - FAST_K)
                items += run(d, slot, place, q0, k0, FAST_Q, FAST_K, ts, te, ks, ke, True)
            interleave(items)
            after(i, slot)
            return carry

        lax.fori_loop(0, STEPS, step, 0)

    @pl.when(jnp.logical_not(is_fast(meta, cross)))
    def _():
        def doc(d, carry):
            ts, te = doc_bounds(meta, d, False)
            ks, ke = doc_bounds(meta, d, cross)
            base = (ts // 16) * 16
            k0 = window_of(ks, SEQ - LONG_K)

            def chunk(i, carry):
                lower = base + i * LONG_Q
                q0 = pl.multiple_of(jnp.minimum(lower, SEQ - LONG_Q), 16)
                low = jnp.maximum(ts, lower)
                high = jnp.minimum(te, lower + LONG_Q)
                interleave(run(d, None, None, q0, k0, LONG_Q, LONG_K, low, high, ks, ke, False))
                return carry

            return lax.fori_loop(0, (te - base + LONG_Q - 1) // LONG_Q, chunk, carry)

        lax.fori_loop(0, DOCS, doc, 0)


def attend_docs(meta, cross, rank_ref, limit_ref, halves, p_ref, p_buf, p_sem):
    pairs = 2 * len(halves)
    masks = half_masks()

    def save(i, slot):
        return pltpu.make_async_copy(p_buf.at[slot], p_ref.at[pl.ds(TOGETHER * i, TOGETHER)], p_sem.at[slot])

    def before(i, slot):
        @pl.when(i >= 2)
        def _():
            save(i - 2, slot).wait()

    def after(i, slot):
        save(i, slot).start()

    def run(d, slot, place, q0, k0, span, width, low, high, ks, ke, fast):
        bias = make_bias(rank_ref, limit_ref, ks, ke, q0, k0, span, width)
        row = q0 + lax.broadcasted_iota(jnp.int32, (span, 128), 0)
        inside = (row >= low) & (row < high)

        def phases(n):
            q_ref, k_ref, v_ref, mixed_ref = halves[n // 2]
            cols = slice(128 * (n % 2), 128 * (n % 2) + 128)

            def score():
                return pair_scores(q_ref[pl.ds(q0, span), cols], k_ref[pl.ds(k0, width), cols], masks)

            def weigh(scores):
                return [raised(scores[width * a : width * a + width], bias) for a in range(2)]

            def mix(parts):
                values = jnp.transpose(v_ref[pl.ds(k0, width), cols])
                mixed, parts = weighted_values(values, parts)
                if fast:
                    for a in range(2):
                        p_buf[slot, place, 2 * n + a] = parts[a]
                mixed = jnp.transpose(mixed).astype(f32)
                old = mixed_ref[pl.ds(q0, span), cols].astype(f32)
                mixed_ref[pl.ds(q0, span), cols] = jnp.where(inside, mixed, old).astype(bf16)

            return score, weigh, mix

        return [phases(n) for n in range(pairs)]

    for_docs(meta, cross, run, before, after)

    @pl.when(is_fast(meta, cross))
    def _():
        for i in range(STEPS - 2, STEPS):
            save(i, i % 2).wait()


def load_step(load, i, slot):
    p_ref, p_buf, p_sem = load
    return pltpu.make_async_copy(p_ref.at[pl.ds(TOGETHER * i, TOGETHER)], p_buf.at[slot], p_sem.at[slot])


def start_load(meta, cross, load):
    @pl.when(is_fast(meta, cross))
    def _():
        load_step(load, 0, 0).start()


def attend_docs_back(
    meta, cross, rank_ref, limit_ref, q_ref, k_ref, v_ref, mixed_ref, dm_ref,
    dq_ref, dk_ref, dv_ref, load,
):
    pairs = q_ref.shape[1] // 128
    masks = half_masks()
    p_buf = load[1]

    def before(i, slot):
        @pl.when(i + 1 < STEPS)
        def _():
            load_step(load, i + 1, 1 - slot).start()

        load_step(load, i, slot).wait()

    def after(i, slot):
        pass

    def run(d, slot, place, q0, k0, span, width, low, high, ks, ke, fast):
        row = q0 + lax.broadcasted_iota(jnp.int32, (span, 128), 0)
        inside = jnp.where((row >= low) & (row < high), 1.0, 0.0).astype(bf16)
        ones = jnp.ones((width, 128), bf16)
        if not fast:
            bias = make_bias(rank_ref, limit_ref, ks, ke, q0, k0, span, width)

        def phases(n):
            cols = slice(128 * n, 128 * n + 128)

            def differ():
                values = v_ref[pl.ds(k0, width), cols]
                mixed = mixed_ref[pl.ds(q0, span), cols]
                grad = dm_ref[pl.ds(q0, span), cols] * inside
                left = lanes([grad, -(grad * mixed)])
                right = both_heads(lanes([values, ones]), [lanes([m, m]) for m in masks])
                return grad, dot_nt(right, left)

            def slope(state):
                grad, delta = state
                if fast:
                    parts = [p_buf[slot, place, 2 * n + a] for a in range(2)]
                else:
                    queries = q_ref[pl.ds(q0, span), cols]
                    keys = k_ref[pl.ds(k0, width), cols]
                    scores = pair_scores(queries, keys, masks)
                    parts = [raised(scores[width * a : width * a + width], bias) for a in range(2)]
                    parts = weighted_values(jnp.transpose(v_ref[pl.ds(k0, width), cols]), parts)[1]
                slopes = [
                    by_pieces(
                        lambda part, change: part * change.astype(bf16),
                        16,
                        0,
                        parts[a],
                        delta[width * a : width * a + width],
                    )
                    for a in range(2)
                ]
                return grad, parts, slopes

            def spread(state):
                grad, parts, slopes = state
                queries = q_ref[pl.ds(q0, span), cols]
                dk = dv = None
                for a in range(2):
                    dk_a = dot(slopes[a], queries * masks[a])
                    dv_a = dot(parts[a], grad * masks[a])
                    dk = dk_a if dk is None else dk + dk_a
                    dv = dv_a if dv is None else dv + dv_a
                dq = pair_gradient(k_ref[pl.ds(k0, width), cols], slopes)
                dq_ref[pl.ds(q0, span), cols] += dq.astype(f32)
                dk_ref[pl.ds(k0, width), cols] += dk
                dv_ref[pl.ds(k0, width), cols] += dv

            return differ, slope, spread

        return [phases(n) for n in range(pairs)]

    for_docs(meta, cross, run, before, after)


def spread_ranks(rank_row_ref, rank_ref):
    rank_ref[...] = jnp.transpose(jnp.broadcast_to(rank_row_ref[...], (128, SEQ)))


def prepare(
    core, seg_ref, src_ref, rank_ref, limit_ref, pad_ref,
    n0, n1, n2, n3, n4, n5, n6, n7, sq, sk, sv, so, cq, ck, cv, co,
    meta_ref, ranks_ref, limits_ref, norms_ref, ws_ref, wc_ref,
):
    meta_ref[0] = core[0]
    meta_ref[35] = core[1]
    for base, ref in ((1, seg_ref), (17, src_ref)):
        ids = ref[0]
        meta_ref[base] = 0
        meta_ref[base + 15] = SEQ
        for d in range(1, DOCS):
            cut = jnp.sum(jnp.where(ids < d, 1.0, 0.0)).astype(jnp.int32)
            meta_ref[base + d] = cut
            meta_ref[base + 7 + d] = cut
    for place, base in ((33, 1), (34, 17)):
        fast = jnp.int32(1)
        for d in range(DOCS):
            q0 = window_of(meta_ref[1 + d], SEQ - FAST_Q)
            k0 = window_of(meta_ref[base + d], SEQ - FAST_K)
            fits = (meta_ref[9 + d] - q0 <= FAST_Q) & (meta_ref[base + 8 + d] - k0 <= FAST_K)
            fast = fast & fits.astype(jnp.int32)
        meta_ref[place] = fast
    ranks = jnp.where(pad_ref[0] != 0, hidden_rank, rank_ref[0].astype(f32))
    limits = limit_ref[0].astype(f32)
    for i in range(8):
        ranks_ref[0:1, 128 * i : 128 * i + 128] = ranks[i : i + 1]
        limits_ref[0:1, 128 * i : 128 * i + 128] = limits[i : i + 1]
    for i, ref in enumerate((n0, n1, n2, n3, n4, n5, n6, n7)):
        norms_ref[i : i + 1, :] = ref[...]
    for to, parts, out in ((ws_ref, (sq, sk, sv), so), (wc_ref, (cq, ck, cv), co)):
        for i, part in enumerate(parts):
            to[:, 128 * i : 128 * i + 128] = part[...]
        for j in range(4):
            to[128 * j : 128 * j + 128, 384:512] = out[:, 128 * j : 128 * j + 128]


def self_first(
    meta, io, xq_ref, xc_ref, rank_row_ref, limit_ref, norms_ref, w0_ref, w1_ref,
    nq_ref, nc_ref, q_ref, k_ref, v_ref, mixed_ref, p_ref, rank_ref, p_buf, p_sem,
):

    spread_ranks(rank_row_ref, rank_ref)
    wq = lanes([w_query(w0_ref), w_query(w1_ref)])
    wkv = lanes([w_key(w0_ref), w_key(w1_ref), w_value(w0_ref), w_value(w1_ref)])

    def tile(i, carry):
        rows = rows_of(i)
        io.wait_rows(i)
        nq = layer_norm(xq_ref[rows, :], norms_ref[0:1], norms_ref[1:2])
        nc = layer_norm(xc_ref[rows, :], norms_ref[2:3], norms_ref[3:4])
        nq_ref[rows, :] = nq
        nc_ref[rows, :] = nc
        q_ref[rows, :] = (dot(nq, wq) * (HEAD_DIM**-0.5)).astype(bf16)
        kv = dot(nc, wkv).astype(bf16)
        k_ref[rows, :] = kv[:, :256]
        v_ref[rows, :] = kv[:, 256:]
        return carry

    lax.fori_loop(0, TILES, tile, 0)

    for ref in (nq_ref, nc_ref, q_ref, k_ref, v_ref):
        io.send(ref)
    attend_docs(meta, False, rank_ref, limit_ref, [(q_ref, k_ref, v_ref, mixed_ref)], p_ref, p_buf, p_sem)


def self_second(
    meta, io, xq_ref, nq_ref, nc_ref, rank_row_ref, limit_ref, norms_ref, w0_ref, w1_ref, w2_ref, w3_ref,
    mixed_first_ref,
    q_ref, k_ref, v_ref, mixed_ref, p_ref, second_ref, ncross_ref, rank_ref, p_buf, p_sem,
):

    spread_ranks(rank_row_ref, rank_ref)
    wq = lanes([w_query(w2_ref), w_query(w3_ref)])
    wkv = lanes([w_key(w2_ref), w_key(w3_ref), w_value(w2_ref), w_value(w3_ref)])

    def tile(i, carry):
        rows = rows_of(i)
        io.wait_rows(i)
        q_ref[rows, :] = (dot(nq_ref[rows, :], wq) * (HEAD_DIM**-0.5)).astype(bf16)
        kv = dot(nc_ref[rows, :], wkv).astype(bf16)
        k_ref[rows, :] = kv[:, :256]
        v_ref[rows, :] = kv[:, 256:]
        return carry

    lax.fori_loop(0, TILES, tile, 0)

    for ref in (q_ref, k_ref, v_ref):
        io.send(ref)
    attend_docs(meta, False, rank_ref, limit_ref, [(q_ref, k_ref, v_ref, mixed_ref)], p_ref, p_buf, p_sem)

    io.send(mixed_ref)
    io.wait("late")
    out_first = jnp.concatenate([w_out(w0_ref), w_out(w1_ref)], axis=0)
    out_second = jnp.concatenate([w_out(w2_ref), w_out(w3_ref)], axis=0)

    def tile(i, carry):
        rows = rows_of(i)
        branch = dot(mixed_first_ref[rows, :], out_first) + dot(mixed_ref[rows, :], out_second)
        second = xq_ref[rows, :].astype(f32) + branch
        second_ref[rows, :] = second.astype(bf16)
        io.send(second_ref, rows)
        ncross_ref[rows, :] = layer_norm(second, norms_ref[4:5], norms_ref[5:6])
        io.send(ncross_ref, rows)
        return carry

    lax.fori_loop(0, TILES, tile, 0)


def project_cross(io, ncross_ref, memory_ref, weights, q_ref, k_ref, v_ref):
    wq = lanes([w_query(w) for w in weights])
    wkv = lanes([w_key(w) for w in weights] + [w_value(w) for w in weights])

    def tile(i, carry):
        rows = rows_of(i)
        io.wait_rows(i)
        q_ref[rows, :] = (dot(ncross_ref[rows, :], wq) * (HEAD_DIM**-0.5)).astype(bf16)
        kv = dot(memory_ref[rows, :], wkv).astype(bf16)
        k_ref[rows, :] = kv[:, :256]
        v_ref[rows, :] = kv[:, 256:]
        return carry

    lax.fori_loop(0, TILES, tile, 0)
    for ref in (q_ref, k_ref, v_ref):
        io.send(ref)


def cross_first(
    meta, io, ncross_ref, memory_ref, w0_ref, w1_ref,
    q_ref, k_ref, v_ref, mixed_ref, p_ref, p_buf, p_sem,
):
    project_cross(io, ncross_ref, memory_ref, (w0_ref, w1_ref), q_ref, k_ref, v_ref)
    attend_docs(meta, True, None, None, [(q_ref, k_ref, v_ref, mixed_ref)], p_ref, p_buf, p_sem)


def cross_second(
    meta, io, second_ref, ncross_ref, memory_ref, norms_ref, w0_ref, w1_ref, w2_ref, w3_ref,
    mixed_first_ref,
    q_ref, k_ref, v_ref, mixed_ref, p_ref, third_ref, nffn_ref, p_buf, p_sem,
):
    project_cross(io, ncross_ref, memory_ref, (w2_ref, w3_ref), q_ref, k_ref, v_ref)
    attend_docs(meta, True, None, None, [(q_ref, k_ref, v_ref, mixed_ref)], p_ref, p_buf, p_sem)
    io.send(mixed_ref)
    io.wait("late")
    out_first = jnp.concatenate([w_out(w0_ref), w_out(w1_ref)], axis=0)
    out_second = jnp.concatenate([w_out(w2_ref), w_out(w3_ref)], axis=0)

    def tile(i, carry):
        rows = rows_of(i)
        branch = dot(mixed_first_ref[rows, :], out_first) + dot(mixed_ref[rows, :], out_second)
        third = second_ref[rows, :].astype(f32) + branch
        third_ref[rows, :] = third
        nffn_ref[rows, :] = layer_norm(third, norms_ref[6:7], norms_ref[7:8])
        return carry

    lax.fori_loop(0, TILES, tile, 0)


def ffn_both(
    meta, io, third_ref, nffn_ref, cot_ref, norms_ref, u0_ref, u1_ref, u2_ref, u3_ref,
    w0_ref, w1_ref, w2_ref, w3_ref,
    placed_ref, out_ref, g3_low_ref, gln_ref, own_ref, other_ref, hidden_ref, before_ref, sums_ref,
):
    sums_ref[...] = jnp.zeros_like(sums_ref)
    in_refs = (u0_ref, u1_ref, u2_ref, u3_ref)
    w_refs = (w0_ref, w1_ref, w2_ref, w3_ref)

    def tile(i, carry):
        rows = rows_of(i)
        io.wait_rows(i)
        nffn = nffn_ref[rows, :]
        cot = cot_ref[rows, :]
        outs = []
        grads = []

        def phases(g, c, group):
            w_in = in_refs[g]
            w_out_rows = w_refs[g]
            cols = slice(256 * c, 256 * c + 256)

            def enter():
                return dot(nffn, w_in[:, cols]), dot_nt(cot, w_out_rows[cols, :])

            def bend(state):
                def piece(x, grad_hidden):
                    square = x * x
                    argument = x * (gelu_root + (gelu_root * gelu_cube) * square)
                    half = 0.5 + 0.5 * jnp.tanh(argument.astype(bf16))
                    x = x.astype(bf16)
                    square = square.astype(bf16)
                    value = x * half
                    rise = 2.0 * gelu_root + (6.0 * gelu_root * gelu_cube) * square
                    slope = half + value * (1.0 - half) * rise
                    return value, grad_hidden.astype(bf16) * slope

                hidden, grad_before = by_pieces(piece, 32, 0, *state)
                if g < 2:
                    place = slice(512 * g + 256 * c, 512 * g + 256 * c + 256)
                    hidden_ref[rows, place] = hidden
                    before_ref[rows, place] = grad_before
                group[c] = hidden, grad_before

            def leave(_):
                if c == 1:
                    outs.append(dot(lanes([group[0][0], group[1][0]]), w_out_rows[...]))

            def leave_back(_):
                if c == 1:
                    grads.append(dot_nt(lanes([group[0][1], group[1][1]]), w_in[...]))

            return enter, bend, leave, leave_back

        interleave(by_halves(4, phases))
        third = third_ref[rows, :]
        result = (third + ((outs[0] + outs[1]) + (outs[2] + outs[3]))).astype(bf16)
        out_ref[rows, :] = result
        placed_ref[rows, :] = result
        grad_normed = (grads[0] + grads[1]) + (grads[2] + grads[3])
        grad_norm = norm_backward(third, norms_ref[6:7], grad_normed, sums_ref, 0)
        g3_low_ref[rows, :] = (cot.astype(f32) + grad_norm).astype(bf16)
        for ref in (out_ref, placed_ref, g3_low_ref):
            io.send(ref, rows)
        return carry

    lax.fori_loop(0, TILES, tile, 0)
    add_sums(sums_ref, gln_ref, 2)
    part = dot_tn(nffn_ref[...], before_ref[...])
    own_ref[0:512, :] = part[:, 0:512].astype(bf16)
    other_ref[0:512, :] = part[:, 512:1024].astype(bf16)
    io.send(own_ref, pl.ds(0, 512))
    io.send(other_ref, pl.ds(0, 512))
    part = dot_tn(hidden_ref[...], cot_ref[...])
    own_ref[512:1024, :] = part[0:512].astype(bf16)
    other_ref[512:1024, :] = part[512:1024].astype(bf16)
    io.send(own_ref, pl.ds(512, 512))
    io.send(other_ref, pl.ds(512, 512))


def back_start(io, g_ref, mixed_ref, w_refs, dm_ref, dq_ref, dk_ref, dv_ref):
    out_rows = jnp.concatenate([w_out(w) for w in w_refs], axis=0)

    def tile(i, carry):
        rows = rows_of(i)
        io.wait_rows(i)
        dm_ref[rows, :] = dot_nt(g_ref[rows, :], out_rows).astype(bf16)
        zeros = jnp.zeros((TILE, 256), f32)
        dq_ref[rows, :] = zeros
        dk_ref[rows, :] = zeros
        dv_ref[rows, :] = zeros
        return carry

    lax.fori_loop(0, TILES, tile, 0)


def attention_back_first(
    cross, meta, io, g_ref, nq_ref, nkv_ref, rank_row_ref, limit_ref, w0_ref, w1_ref,
    q_ref, k_ref, v_ref, mixed_ref, p_ref,
    dq_ref, dk_ref, dv_ref, own_ref, other_ref,
    rank_ref, dm_ref, dqs_ref, dks_ref, dvs_ref, p_buf, p_sem,
):
    load = (p_ref, p_buf, p_sem)
    start_load(meta, cross, load)
    if not cross:
        spread_ranks(rank_row_ref, rank_ref)
    back_start(io, g_ref, mixed_ref, (w0_ref, w1_ref), dm_ref, dqs_ref, dks_ref, dvs_ref)

    io.wait("soon")
    attend_docs_back(
        meta, cross, None if cross else rank_ref, limit_ref, q_ref, k_ref, v_ref, mixed_ref,
        dm_ref, dqs_ref, dks_ref, dvs_ref, load,
    )

    dq_ref[...] = dqs_ref[...].astype(bf16)
    dk_ref[...] = dks_ref[...].astype(bf16)
    dv_ref[...] = dvs_ref[...].astype(bf16)
    for ref in (dq_ref, dk_ref, dv_ref):
        io.send(ref)
    io.wait("late")
    nq = nq_ref[...]
    nkv = nkv_ref[...]
    kv = dot_tn(nkv, lanes([dk_ref[...], dv_ref[...]]))
    for n, part in enumerate((dot_tn(nq, dq_ref[...]), kv[:, 0:256], kv[:, 256:512])):
        own_ref[:, 128 * n : 128 * n + 128] = part[:, :128].astype(bf16)
        other_ref[:, 128 * n : 128 * n + 128] = part[:, 128:].astype(bf16)
    part = dot_tn(mixed_ref[...], g_ref[...])
    for j in range(4):
        rows = slice(128 * j, 128 * j + 128)
        own_ref[rows, 384:512] = part[:128, rows].astype(bf16)
        other_ref[rows, 384:512] = part[128:, rows].astype(bf16)


def back_second_docs(
    cross, meta, io, g_ref, rank_row_ref, limit_ref, w_refs, q_ref, k_ref, v_ref, mixed_ref, p_ref,
    rank_ref, dm_ref, dqs_ref, dks_ref, dvs_ref, p_buf, p_sem,
):
    load = (p_ref, p_buf, p_sem)
    start_load(meta, cross, load)
    if not cross:
        spread_ranks(rank_row_ref, rank_ref)
    back_start(io, g_ref, mixed_ref, w_refs, dm_ref, dqs_ref, dks_ref, dvs_ref)

    io.wait("soon")
    attend_docs_back(
        meta, cross, None if cross else rank_ref, limit_ref, q_ref, k_ref, v_ref, mixed_ref,
        dm_ref, dqs_ref, dks_ref, dvs_ref, load,
    )


def stream_grads(rows, first, second, firsts, seconds):
    dq, dk, dv = first
    dq2, dk2, dv2 = (ref[rows, :].astype(bf16) for ref in second)
    w0, w1 = firsts
    w2, w3 = seconds
    grad_q = dot_nt(dq[rows, :], lanes([w_query(w0), w_query(w1)])) + dot_nt(
        dq2, lanes([w_query(w2), w_query(w3)])
    )
    kv = lanes([dk[rows, :], dv[rows, :]])
    kv2 = lanes([dk2, dv2])
    grad_kv = dot_nt(kv, lanes([w_key(w0), w_key(w1), w_value(w0), w_value(w1)])) + dot_nt(
        kv2, lanes([w_key(w2), w_key(w3), w_value(w2), w_value(w3)])
    )
    return grad_q, grad_kv


def cross_back_second(
    meta, io, g_low_ref, second_ref, norms_ref, w0_ref, w1_ref, w2_ref, w3_ref,
    dq_ref, dk_ref, dv_ref, q_ref, k_ref, v_ref, mixed_ref, p_ref,
    g2_low_ref, placed_ref, gmem_ref, gln_ref,
    dm_ref, dqs_ref, dks_ref, dvs_ref, p_buf, p_sem, sums_ref,
):
    back_second_docs(
        True, meta, io, g_low_ref, None, None, (w2_ref, w3_ref), q_ref, k_ref, v_ref, mixed_ref, p_ref,
        None, dm_ref, dqs_ref, dks_ref, dvs_ref, p_buf, p_sem,
    )

    io.wait("late")
    sums_ref[...] = jnp.zeros_like(sums_ref)

    def tile(i, carry):
        rows = rows_of(i)
        grad_q, grad_kv = stream_grads(
            rows,
            (dq_ref, dk_ref, dv_ref),
            (dqs_ref, dks_ref, dvs_ref),
            (w0_ref, w1_ref),
            (w2_ref, w3_ref),
        )
        low_kv = grad_kv.astype(bf16)
        gmem_ref[rows, :] = low_kv
        placed_ref[rows, :] = low_kv.astype(f32)
        io.send(gmem_ref, rows)
        io.send(placed_ref, rows)
        grad_norm = norm_backward(second_ref[rows, :], norms_ref[4:5], grad_q, sums_ref, 0)
        g2_low_ref[rows, :] = (g_low_ref[rows, :].astype(f32) + grad_norm).astype(bf16)
        io.send(g2_low_ref, rows)
        return carry

    lax.fori_loop(0, TILES, tile, 0)
    add_sums(sums_ref, gln_ref, 2)


def self_back_second(
    meta, io, g_low_ref, rank_row_ref, limit_ref, w2_ref, w3_ref,
    q_ref, k_ref, v_ref, mixed_ref, p_ref,
    dq_ref, dk_ref, dv_ref,
    rank_ref, dm_ref, dqs_ref, dks_ref, dvs_ref, p_buf, p_sem,
):
    back_second_docs(
        False, meta, io, g_low_ref, rank_row_ref, limit_ref, (w2_ref, w3_ref), q_ref, k_ref, v_ref,
        mixed_ref, p_ref, rank_ref, dm_ref, dqs_ref, dks_ref, dvs_ref, p_buf, p_sem,
    )
    dq_ref[...] = dqs_ref[...].astype(bf16)
    dk_ref[...] = dks_ref[...].astype(bf16)
    dv_ref[...] = dvs_ref[...].astype(bf16)


def self_back_finish(
    meta, io, g_ref, xq_ref, xc_ref, norms_ref, w0_ref, w1_ref, w2_ref, w3_ref,
    dq_ref, dk_ref, dv_ref, dq2_ref, dk2_ref, dv2_ref,
    placed_q_ref, placed_c_ref, gq_ref, gc_ref, gln_ref, sums_ref,
):
    sums_ref[...] = jnp.zeros_like(sums_ref)

    def tile(i, carry):
        rows = rows_of(i)
        io.wait_rows(i)
        grad_q, grad_kv = stream_grads(
            rows,
            (dq_ref, dk_ref, dv_ref),
            (dq2_ref, dk2_ref, dv2_ref),
            (w0_ref, w1_ref),
            (w2_ref, w3_ref),
        )
        grad_norm = norm_backward(xq_ref[rows, :], norms_ref[0:1], grad_q, sums_ref, 0)
        low_q = (g_ref[rows, :].astype(f32) + grad_norm).astype(bf16)
        gq_ref[rows, :] = low_q
        placed_q_ref[rows, :] = low_q.astype(f32)
        io.send(gq_ref, rows)
        io.send(placed_q_ref, rows)
        grad_norm = norm_backward(xc_ref[rows, :], norms_ref[2:3], grad_kv, sums_ref, 16)
        low_c = grad_norm.astype(bf16)
        gc_ref[rows, :] = low_c
        placed_c_ref[rows, :] = low_c.astype(f32)
        io.send(gc_ref, rows)
        io.send(placed_c_ref, rows)
        return carry

    lax.fori_loop(0, TILES, tile, 0)
    add_sums(sums_ref, gln_ref, 4)


def place_rows(meta, *refs):
    count = len(refs) // 3
    for n in range(count):
        refs[2 * count + n][...] = refs[n][...].astype(refs[2 * count + n].dtype)


GROUP = 8


def position(meta):
    r = meta[35]
    return lax.rem(r, 2), r // 2


def join(own, other, rows):
    return (own[rows, :].astype(f32) + other[rows, :].astype(f32)).astype(bf16)


def join_halves(meta, own, other, keep, send):
    y, _ = position(meta)
    size = keep.shape[0]
    keep[...] = join(own, other, rows_of(y, size))
    send[...] = join(own, other, rows_of(1 - y, size))


def join_chunks(meta, kept, arrived, keep, sends):
    _, z = position(meta)
    size = keep.shape[0]
    keep[...] = join(kept, arrived, rows_of(z, size))
    for s, (send, first) in enumerate(sends, 1):
        send[first : first + size, :] = join(kept, arrived, rows_of(z ^ s, size))


def add_up(kept, parts, first):
    size = kept.shape[0]
    total = kept[...].astype(f32)
    for part in parts:
        total = total + part[first : first + size, :].astype(f32)
    return total.astype(bf16)


def half_of(meta, total, parts, first, half):
    _, z = position(meta)
    size = total.shape[0]
    half[rows_of(z, size), :] = total[...]
    for s, part in enumerate(parts, 1):
        half[rows_of(z ^ s, size), :] = part[first : first + size, :]


def slot_1(meta, ffn_own, ffn_other, keep, send):
    join_halves(meta, ffn_own, ffn_other, keep, send)


def slot_2(
    meta, ffn_kept, ffn_arrived, cross_own, cross_other, ffn_keep, f1, f2, f3, keep, send
):
    join_chunks(meta, ffn_kept, ffn_arrived, ffn_keep, [(f1, 0), (f2, 0), (f3, 0)])
    join_halves(meta, cross_own, cross_other, keep, send)


def slot_3(
    meta, ffn_kept, f1, f2, f3, cross_kept, cross_arrived, self_own, self_other,
    ffn_total, cross_keep, m1, m2, m3, self_keep, self_send,
):
    join_halves(meta, self_own, self_other, self_keep, self_send)
    total = add_up(ffn_kept, (f1, f2, f3), 0)
    ffn_total[...] = total
    size = total.shape[0]
    join_chunks(meta, cross_kept, cross_arrived, cross_keep, [(m, size) for m in (m1, m2, m3)])
    for m in (m1, m2, m3):
        m[0:size, :] = total


def slot_4(
    meta, ffn_total, m1, m2, m3, cross_kept, self_kept, self_arrived,
    ffn_half, cross_total, self_keep, *sends,
):
    join_chunks(meta, self_kept, self_arrived, self_keep, [(send, 0) for send in sends])
    total = add_up(cross_kept, (m1, m2, m3), ffn_total.shape[0])
    cross_total[...] = total
    size = total.shape[0]
    for send in sends:
        send[size:, :] = total
    half_of(meta, ffn_total, (m1, m2, m3), 0, ffn_half)


def slot_5(meta, self_kept, cross_total, m1, m2, m3, gln_own, gln_other, send, cross_half):
    size = self_kept.shape[0]
    total = add_up(self_kept, (m1, m2, m3), 0)
    gln = gln_own[...] + gln_other[...]
    gln = jnp.concatenate([gln, jnp.zeros((8, D), f32)], axis=0).astype(bf16)
    for r in range(GROUP):
        send[r, 0:size, :] = total
        send[r, size : size + 16, :] = gln
    half_of(meta, cross_total, (m1, m2, m3), size, cross_half)


def unpack_attention(whole_ref, outs):
    for i in range(3):
        outs[i][...] = whole_ref[:, 128 * i : 128 * i + 128].astype(f32)
    for j in range(4):
        rows = slice(128 * j, 128 * j + 128)
        outs[3][:, rows] = whole_ref[rows, 384:512].astype(f32)


def unpack_ffn(meta, half, arrived, out_in, out_out, ffn_whole):
    y, _ = position(meta)
    ffn_whole[rows_of(y, 512), :] = half[...]
    ffn_whole[rows_of(1 - y, 512), :] = arrived[...]
    out_in[...] = ffn_whole[0:512, :].astype(f32)
    out_out[...] = ffn_whole[512:1024, :].astype(f32)


def unpack_rest(meta, cross_half, cross_arrived, parts, *refs):
    *outs, gln, whole_ref = refs
    y, _ = position(meta)
    whole_ref[rows_of(y, 256), :] = cross_half[...]
    whole_ref[rows_of(1 - y, 256), :] = cross_arrived[...]
    unpack_attention(whole_ref, outs[0:4])
    size = parts.shape[1] - 16
    total = parts[0, size : size + 16, :].astype(f32)
    for r in range(1, GROUP):
        total = total + parts[r, size : size + 16, :].astype(f32)
    gln[...] = total[0:8]
    for r in range(GROUP):
        first = size * (4 * (r % 2) + r // 2)
        whole_ref[first : first + size, :] = parts[r, 0:size, :]
    unpack_attention(whole_ref, outs[4:8])


def whole(shape):
    zeros = (0,) * len(shape)
    return pl.BlockSpec(shape, lambda d, meta: zeros)


def own_row(width):
    return pl.BlockSpec((SEQ, width), lambda d, meta: (meta[0], 0))


ANY = pl.BlockSpec(memory_space=pl.ANY)


def in_hbm(x):
    return pltpu.with_memory_space_constraint(x, pltpu.HBM)


probability_out = (pltpu.HBM((DOCS, 4, FAST_K, FAST_Q), bf16), None, ANY)
probability_scratch = [
    pltpu.VMEM((2, TOGETHER, 4, FAST_K, FAST_Q), bf16),
    pltpu.SemaphoreType.DMA((2,)),
]


class Copies:
    def __init__(self, meta):
        self.first = meta[0] * SEQ
        self.loads = {}
        self.tiles = []
        self.sends = []

    def load(self, stage, source, target, sems, own_row):
        if stage == "fresh":
            stage = "now"
        if stage == "tiles":
            first = self.first if own_row else 0
            self.tiles.append((source, target, sems, first))
            return
        if own_row:
            source = source.at[pl.ds(pl.multiple_of(self.first, SEQ), SEQ)]
        copy = pltpu.make_async_copy(source, target, sems[0].at[sems[1], 0])
        self.loads.setdefault(stage, []).append(copy)

    def tile(self, entry, i):
        source, target, (sems, b), first = entry
        rows = pl.ds(pl.multiple_of(first + i * TILE, TILE), TILE)
        return pltpu.make_async_copy(source.at[rows], target.at[rows_of(i)], sems.at[b, i])

    def start(self):
        for copy in self.loads.get("now", []):
            copy.start()
        for i in range(TILES):
            for entry in self.tiles:
                self.tile(entry, i).start()
        for stage in ("soon", "late"):
            for copy in self.loads.get(stage, []):
                copy.start()

    def wait(self, stage):
        for copy in self.loads.pop(stage, []):
            copy.wait()

    def wait_rows(self, i):
        for entry in self.tiles:
            self.tile(entry, i).wait()

    def result(self, source, target, sem, own_row):
        self.sends.append([source, target, sem, own_row, False])

    def send(self, ref, rows=None):
        for entry in self.sends:
            source, target, sem, own_row, _ = entry
            if source is ref:
                entry[4] = True
                first = self.first if own_row else 0
                if rows is None:
                    size = source.shape[0]
                else:
                    source = source.at[rows]
                    first, size = first + rows.start, rows.size
                if rows is not None or own_row:
                    target = target.at[pl.ds(pl.multiple_of(first, size), size)]
                pltpu.make_async_copy(source, target, sem).start()

    def finish(self):
        for stage in list(self.loads):
            self.wait(stage)
        for source, _, _, _, started in self.sends:
            if not started:
                self.send(source)
        for source, target, sem, own_row, _ in self.sends:
            if own_row:
                target = target.at[pl.ds(pl.multiple_of(self.first, SEQ), SEQ)]
            pltpu.make_async_copy(source, target, sem).wait()


def out(shape, dtype, own_row=False):
    return (shape, dtype, own_row)


def call(kernel, name, operands, outs, scratch, flops, token=None):
    arrays = [operands[0][0]]
    in_specs, out_specs, out_shapes = [], [], []
    buffers = []
    loads = []
    for n, (x, how) in enumerate(operands[1:]):
        if isinstance(how, str):
            stage, _, row = how.partition("_")
            shape = ((SEQ,) + x.shape[1:]) if row else x.shape
            loads.append((n, stage, len(buffers), bool(row)))
            buffers.append(pltpu.VMEM(shape, x.dtype))
            arrays.append(x if stage == "fresh" else in_hbm(x))
            in_specs.append(ANY)
        else:
            arrays.append(x)
            in_specs.append(how)
    results = []
    for n, (shape, dtype, how) in enumerate(outs):
        if isinstance(how, bool):
            results.append((n, len(buffers), how))
            buffers.append(pltpu.VMEM(shape, dtype))
            shape = ((2 * SEQ,) + shape[1:]) if how else shape
            out_shapes.append(pltpu.HBM(shape, dtype))
            out_specs.append(ANY)
        else:
            out_shapes.append(jax.ShapeDtypeStruct(shape, dtype) if dtype else shape)
            out_specs.append(how)
    n_in, n_out = len(in_specs), len(out_specs)
    if token is not None:
        arrays.append(token)
        in_specs.append(whole((8, 128)))
        out_specs.append(whole((8, 128)))
        out_shapes.append(jax.ShapeDtypeStruct((8, 128), f32))

    def body(meta, *refs):
        ins, refs = list(refs[:n_in]), refs[len(in_specs) - n_in + n_in :]
        results_out, refs = list(refs[:n_out]), refs[n_out:]
        if token is not None:
            token_out, refs = refs[0], refs[1:]
            token_out[...] = jnp.zeros_like(token_out)
        bufs, refs = refs[: len(buffers)], refs[len(buffers) :]
        rest = refs[: len(scratch)]
        copies = Copies(meta)
        if buffers:
            sems = refs[len(scratch)]
        for n, stage, b, row in loads:
            copies.load(stage, ins[n], bufs[b], (sems, b), row)
            ins[n] = bufs[b]
        for n, b, row in results:
            copies.result(bufs[b], results_out[n], sems.at[b, 0], row)
            results_out[n] = bufs[b]
        copies.start()
        copies.wait("now")
        if buffers:
            kernel(meta, copies, *ins, *results_out, *rest)
        else:
            kernel(meta, *ins, *results_out, *rest)
        copies.finish()

    moved = sum(x.size * x.dtype.itemsize for x in arrays[1:])
    sems = [pltpu.SemaphoreType.DMA((len(buffers), TILES))] if buffers else []
    return pl.pallas_call(
        body,
        name=name,
        grid_spec=pltpu.PrefetchScalarGridSpec(
            num_scalar_prefetch=1,
            grid=(1,),
            in_specs=in_specs,
            out_specs=out_specs,
            scratch_shapes=buffers + scratch + sems,
        ),
        out_shape=out_shapes,
        compiler_params=pltpu.CompilerParams(
            dimension_semantics=("arbitrary",), vmem_limit_bytes=40 * 1024 * 1024
        ),
        cost_estimate=pl.CostEstimate(
            flops=int(flops), bytes_accessed=int(moved), transcendentals=0
        ),
    )(*arrays)


def simple(kernel, name, meta, operands, outs, scratch=()):
    return pl.pallas_call(
        kernel,
        name=name,
        grid_spec=pltpu.PrefetchScalarGridSpec(
            num_scalar_prefetch=1,
            grid=(1,),
            in_specs=[whole(x.shape) for x in operands],
            out_specs=[whole(shape) for shape, _ in outs],
            scratch_shapes=scratch,
        ),
        out_shape=[jax.ShapeDtypeStruct(shape, dtype) for shape, dtype in outs],
        compiler_params=pltpu.CompilerParams(vmem_limit_bytes=16 * 1024 * 1024),
    )(meta, *operands)


def full(x):
    return (x, whole(x.shape))


def shards(
    query_stream,
    content_stream,
    memory,
    segment_ids,
    source_segments,
    context_rank,
    context_limit,
    padding,
    ln_query_gain,
    ln_query_bias,
    ln_content_gain,
    ln_content_bias,
    self_query,
    self_key,
    self_value,
    self_out,
    ln_cross_gain,
    ln_cross_bias,
    cross_query,
    cross_key,
    cross_value,
    cross_out,
    ln_ffn_gain,
    ln_ffn_bias,
    ffn_in,
    ffn_out,
    cotangent,
):
    core = lax.axis_index("heads") % 2

    def to_core(x):
        return lax.ppermute(x, "heads", [(h, h ^ 1) for h in range(4)])

    hold = lambda *xs: lax.optimization_barrier(xs)

    def to_chip(x):
        return lax.ppermute(x, "heads", [(h, h ^ 2) for h in range(4)])

    row = pl.BlockSpec((1, 8, 128), lambda d, core: (core[0], 0, 0))

    def token_row(x):
        return (in_hbm(x.reshape(2, 8, 128)), row)

    def fixed(x):
        zeros = (0,) * x.ndim
        return (in_hbm(x), pl.BlockSpec(x.shape, lambda d, core: zeros))

    prepared = [
        ((36,), jnp.int32, pl.BlockSpec(memory_space=pltpu.SMEM)),
        ((1, SEQ), f32, whole((1, SEQ))),
        ((1, SEQ), f32, whole((1, SEQ))),
        ((8, D), f32, whole((8, D))),
        ((D, D), bf16, whole((D, D))),
        ((D, D), bf16, whole((D, D))),
    ]
    gains = (
        ln_query_gain,
        ln_query_bias,
        ln_content_gain,
        ln_content_bias,
        ln_cross_gain,
        ln_cross_bias,
        ln_ffn_gain,
        ln_ffn_bias,
    )
    weights = (self_query, self_key, self_value, self_out)
    weights += (cross_query, cross_key, cross_value, cross_out)
    tokens = (segment_ids, source_segments, context_rank, context_limit, padding)
    meta, rank, limit, norms, ws0, wc0 = call(
        prepare,
        "prepare",
        [(jnp.stack([core, lax.axis_index("rows") % GROUP]).astype(jnp.int32), None)]
        + [token_row(x) for x in tokens]
        + [fixed(x.reshape(1, D)) for x in gains]
        + [fixed(x) for x in weights],
        prepared,
        [],
        0,
    )

    ws1 = to_core(ws0)
    ws2 = to_chip(ws0)
    wc1 = to_core(wc0)
    u0, v0 = ffn_in, ffn_out
    meta_in = (meta, None)

    heads_out = [out((SEQ, 256), bf16)] * 4

    def stream_out(dtype, own_row=False):
        return out((SEQ, D), dtype, own_row)

    def now(*xs):
        return [(x, "now") for x in xs]

    def fresh(*xs):
        return [(x, "fresh") for x in xs]

    def soon(*xs):
        return [(x, "soon") for x in xs]

    def late(*xs):
        return [(x, "late") for x in xs]

    def small(*xs):
        return [(x, whole(x.shape)) for x in xs]

    limits = pltpu.VMEM((SEQ, 128), f32)
    pair_flops = 2 * SEQ * D * 768 + 2 * 2 * 4 * DOCS * FAST_Q * FAST_K * 256

    nq, nc, *first, token = call(
        self_first,
        "self_first",
        [meta_in, (query_stream, "tiles_row"), (content_stream, "tiles_row")]
        + small(rank, limit, norms)
        + fresh(ws0, ws1),
        [stream_out(bf16), stream_out(bf16)] + heads_out + [probability_out],
        [limits] + probability_scratch,
        pair_flops,
        jnp.zeros((8, 128), f32),
    )
    ws2, wc0, token = hold(ws2, wc0, token)
    ws3 = to_core(ws2)
    wc2 = to_chip(wc0)
    *second_heads, second, ncross, token = call(
        self_second,
        "self_second",
        [meta_in, (query_stream, "late_row")]
        + [(nq, "tiles"), (nc, "tiles")]
        + small(rank, limit, norms)
        + late(ws0, ws1)
        + fresh(ws2, ws3)
        + late(first[3]),
        heads_out + [probability_out, stream_out(bf16), stream_out(bf16)],
        [limits] + probability_scratch,
        pair_flops + 2 * SEQ * D * D,
        token,
    )
    wc2, u0, v0, token = hold(wc2, u0, v0, token)
    wc3 = to_core(wc2)
    u2 = to_chip(u0)
    u1 = to_core(u0)
    *cross_heads, token = call(
        cross_first,
        "cross_first",
        [meta_in, (ncross, "tiles"), (memory, "tiles_row")] + fresh(wc0, wc1),
        heads_out + [probability_out],
        probability_scratch,
        pair_flops,
        token,
    )
    wc3, u2, v0, token = hold(wc3, u2, v0, token)
    u3 = to_core(u2)
    v2 = to_chip(v0)
    v1 = to_core(v0)
    *cross_heads_second, third, nffn, token = call(
        cross_second,
        "cross_second",
        [meta_in]
        + late(second)
        + [(ncross, "tiles"), (memory, "tiles_row")]
        + small(norms)
        + late(wc0, wc1)
        + fresh(wc2, wc3)
        + late(cross_heads[3]),
        heads_out
        + [probability_out, ((SEQ, D), f32, whole((SEQ, D))), ((SEQ, D), bf16, whole((SEQ, D)))],
        probability_scratch,
        pair_flops + 2 * SEQ * D * D,
        token,
    )
    u3, v2, token = hold(u3, v2, token)
    v3 = to_core(v2)
    grads_ln = ((8, D), f32, whole((8, D)))
    placed_output, output, g3_low, gln_ffn, ffn_own, ffn_other, token = call(
        ffn_both,
        "ffn_both",
        [meta_in]
        + small(third, nffn)
        + [(cotangent, "tiles_row")]
        + small(norms)
        + now(u0) + fresh(u1, u2, u3) + now(v0) + fresh(v1, v2, v3),
        [
            stream_out(bf16, True),
            stream_out(bf16),
            stream_out(bf16),
            grads_ln,
            out((1024, D), bf16),
            out((1024, D), bf16),
        ],
        [pltpu.VMEM((SEQ, 1024), bf16), pltpu.VMEM((SEQ, 1024), bf16), pltpu.VMEM((16, D), f32)],
        12 * SEQ * D * 2048,
        token,
    )

    def both_rows(placed_own, others, name):
        count = len(others)
        size = SEQ // 2
        one = pl.BlockSpec((size, D), lambda i, meta: (i, 0))
        block = pl.BlockSpec((size, D), lambda i, meta: (2 * (1 - meta[0]) + i, 0))
        return pl.pallas_call(
            place_rows,
            name=name,
            grid_spec=pltpu.PrefetchScalarGridSpec(
                num_scalar_prefetch=1,
                grid=(2,),
                in_specs=[one] * count + [pl.BlockSpec(memory_space=pl.ANY)] * count,
                out_specs=[block] * count,
            ),
            out_shape=[jax.ShapeDtypeStruct(x.shape, x.dtype) for x in placed_own],
            input_output_aliases={1 + count + n: n for n in range(count)},
        )(meta, *others, *placed_own)

    row_count = lax.axis_size("rows")
    assert row_count % GROUP == 0

    def along_rows(x, s):
        return lax.ppermute(x, "rows", [(r, r ^ s) for r in range(row_count)])

    def to_y(x):
        return along_rows(x, 1)

    def to_z(sends):
        return [along_rows(x, 2 * s) for s, x in enumerate(sends, 1)]

    def rows_out(*sizes):
        return [((n, D), bf16) for n in sizes]

    ffn_other = to_core(ffn_other)
    output_other = to_core(output)

    back_scratch = [pltpu.VMEM((SEQ, 256), bf16)] + [pltpu.VMEM((SEQ, 256), f32)] * 3
    back_scratch += probability_scratch
    pair_out = out((SEQ, 256), bf16)
    packed_outs = [((D, D), bf16, whole((D, D)))] * 2
    back_flops = 2 * SEQ * D * 256 + 4 * 2 * 4 * DOCS * FAST_Q * FAST_K * 256

    def head_inputs(natural, p):
        return soon(*natural) + [(in_hbm(p), ANY)]

    *cross_grads, cross_own, cross_other, token = call(
        functools.partial(attention_back_first, True),
        "cross_back_first",
        [meta_in]
        + [(g3_low, "tiles")]
        + late(ncross)
        + [(memory, "late_row")]
        + small(rank, limit)
        + now(wc0, wc1)
        + head_inputs(cross_heads[0:4], cross_heads[4]),
        [pair_out] * 3 + packed_outs,
        [limits] + back_scratch,
        back_flops + 2 * SEQ * D * 1024,
        token,
    )
    ffn_other, output_other, token = hold(ffn_other, output_other, token)
    ffn_keep, ffn_send = simple(slot_1, "slot_1", meta, [ffn_own, ffn_other], rows_out(512, 512))
    ffn_send, token = hold(ffn_send, token)
    ffn_arrived = to_y(ffn_send)
    cross_other = to_core(cross_other)
    g2_low, placed_mem, grad_mem, gln_cross, token = call(
        cross_back_second,
        "cross_back_second",
        [meta_in]
        + [(g3_low, "tiles")]
        + late(second)
        + small(norms)
        + late(wc0, wc1)
        + now(wc2, wc3)
        + late(*cross_grads)
        + head_inputs(cross_heads_second[0:4], cross_heads_second[4]),
        [stream_out(bf16), stream_out(f32, True), stream_out(bf16), grads_ln],
        back_scratch + [pltpu.VMEM((16, D), f32)],
        back_flops + 2 * SEQ * D * 1536,
        token,
    )
    ffn_arrived, cross_other, token = hold(ffn_arrived, cross_other, token)
    ffn_keep, *sends, cross_keep, cross_send = simple(
        slot_2,
        "slot_2",
        meta,
        [ffn_keep, ffn_arrived, cross_own, cross_other],
        rows_out(128, 128, 128, 128, 256, 256),
    )
    ffn_keep, cross_send, token = hold(ffn_keep, cross_send, token)
    ffn_parts = to_z(sends)
    cross_arrived = to_y(cross_send)

    *self_grads, self_own, self_other, token = call(
        functools.partial(attention_back_first, False),
        "self_back_first",
        [meta_in]
        + [(g2_low, "tiles")]
        + late(nq, nc)
        + small(rank, limit)
        + now(ws0, ws1)
        + head_inputs(first[0:4], first[4]),
        [pair_out] * 3 + packed_outs,
        [limits] + back_scratch,
        back_flops + 2 * SEQ * D * 1024,
        token,
    )
    *ffn_parts, cross_arrived, self_other, token = hold(
        *ffn_parts, cross_arrived, self_other, token
    )
    self_other = to_core(self_other)
    ffn_total, cross_keep, *sends, self_keep, self_send = simple(
        slot_3,
        "slot_3",
        meta,
        [ffn_keep, *ffn_parts, cross_keep, cross_arrived, self_own, self_other],
        rows_out(128, 64, 192, 192, 192, 256, 256),
    )
    ffn_total, self_send, grad_mem, token = hold(ffn_total, self_send, grad_mem, token)
    mem_other = to_core(grad_mem)
    self_arrived = to_y(self_send)
    messages = to_z(sends)
    *self_grads_second, token = call(
        self_back_second,
        "self_back_second",
        [meta_in, (g2_low, "tiles")]
        + small(rank, limit)
        + now(ws2, ws3)
        + head_inputs(second_heads[0:4], second_heads[4]),
        [pair_out] * 3,
        [limits] + back_scratch,
        back_flops,
        token,
    )
    *messages, self_arrived, mem_other, token = hold(*messages, self_arrived, mem_other, token)
    ffn_half, cross_total, self_keep, *sends = simple(
        slot_4,
        "slot_4",
        meta,
        [ffn_total, *messages, cross_keep, self_keep, self_arrived],
        rows_out(512, 64, 64, 128, 128, 128),
    )
    cross_total, ffn_half, token = hold(cross_total, ffn_half, token)
    messages = to_z(sends)
    ffn_arrived = to_y(ffn_half)
    placed_q, placed_c, gq, gc, gln_self, token = call(
        self_back_finish,
        "self_back_finish",
        [meta_in, (g2_low, "tiles"), (query_stream, "tiles_row"), (content_stream, "tiles_row")]
        + small(norms)
        + now(ws0, ws1, ws2, ws3)
        + [(x, "tiles") for x in self_grads + self_grads_second],
        [stream_out(f32, True), stream_out(f32, True), stream_out(bf16), stream_out(bf16), grads_ln],
        [pltpu.VMEM((32, D), f32)],
        2 * SEQ * D * 1536,
        token,
    )
    gln = jnp.concatenate([gln_self[0:4], gln_cross[0:2], gln_ffn[0:2]], axis=0)
    gln_other = to_core(gln)
    *messages, ffn_arrived, gln_ffn = hold(*messages, ffn_arrived, gln_ffn)
    last_send, cross_half = simple(
        slot_5,
        "slot_5",
        meta,
        [self_keep, cross_total, *messages, gln, gln_other],
        [((GROUP, 80, D), bf16), ((256, D), bf16)],
    )
    groups = None
    if row_count > GROUP:
        groups = [list(range(r, r + GROUP)) for r in range(0, row_count, GROUP)]
    def gather(x):
        return lax.all_to_all(x, "rows", 0, 0, axis_index_groups=groups)

    last_parts = gather(last_send)
    cross_arrived = to_y(cross_half)
    def over_groups(totals):
        if row_count == GROUP:
            return totals
        groups = [list(range(r, row_count, GROUP)) for r in range(GROUP)]
        return lax.psum(totals, "rows", axis_index_groups=groups)

    gq_both, gc_both = both_rows([placed_q, placed_c], [to_core(gq), to_core(gc)], "place_late")

    grad_ffn_in, grad_ffn_out = simple(
        unpack_ffn,
        "unpack_ffn",
        meta,
        [ffn_half, ffn_arrived],
        [((D, D), f32)] * 2,
        [pltpu.VMEM((2 * D, D), bf16)],
    )
    attention_outs = [((512, 128), f32)] * 3 + [((128, 512), f32)]
    out_both, grad_mem_both = both_rows(
        [placed_output, placed_mem], [output_other, mem_other], "place_early"
    )
    cross_arrived, gq_both, out_both, grad_ffn_in = hold(
        cross_arrived, gq_both, out_both, grad_ffn_in
    )
    *parts, gln = simple(
        unpack_rest,
        "unpack_rest",
        meta,
        [cross_half, cross_arrived, last_parts],
        attention_outs * 2 + [((8, D), f32)],
        [pltpu.VMEM((D, D), bf16)],
    )
    grad_cross_parts, grad_self_parts = parts[:4], parts[4:]
    grad_ffn_in, grad_ffn_out, grad_cross_parts, grad_self_parts, gln = over_groups(
        (grad_ffn_in, grad_ffn_out, grad_cross_parts, grad_self_parts, gln)
    )
    return (
        out_both,
        gq_both,
        gc_both,
        grad_mem_both,
        gln[0],
        gln[1],
        gln[2],
        gln[3],
        *grad_self_parts,
        gln[4],
        gln[5],
        *grad_cross_parts,
        gln[6],
        gln[7],
        grad_ffn_in,
        grad_ffn_out,
    )


def solution(mesh):
    assert mesh.shape["heads"] == 4
    row_spec = P("rows", None)
    flat = P("rows")
    by_column = P(None, "heads")
    by_row = P("heads", None)
    attention = (by_column, by_column, by_column, by_row)
    in_specs = (
        (row_spec,) * 3
        + (flat,) * 5
        + (P(),) * 4
        + attention
        + (P(),) * 2
        + attention
        + (P(),) * 2
        + (by_column, by_row, row_spec)
    )
    out_specs = (
        (row_spec,) * 4
        + (P(),) * 4
        + attention
        + (P(),) * 2
        + attention
        + (P(),) * 2
        + (by_column, by_row)
    )
    return jax.shard_map(shards, mesh=mesh, in_specs=in_specs, out_specs=out_specs, check_vma=False)
```

```python
import functools

import jax
import jax.numpy as jnp
from jax import lax
from jax.experimental import pallas as pl
from jax.experimental.pallas import tpu as pltpu
from jax.sharding import PartitionSpec as P

HEAD_DIM = 64
SEQ = 1024
DOCS = 8
D = 512
TILE = 256
TILES = SEQ // TILE
FAST_Q = 256
FAST_K = 208
LONG_Q = 128
LONG_K = 640

norm_eps = 1e-05
masked_score = -1e30
hidden_rank = 1e6
gelu_root = 0.7978845608028654
gelu_cube = 0.044715

f32 = jnp.float32
bf16 = jnp.bfloat16


def dot(a, b):
    return lax.dot_general(a, b, (((1,), (0,)), ((), ())), preferred_element_type=f32)


def dot_nt(a, b):
    return lax.dot_general(a, b, (((1,), (1,)), ((), ())), preferred_element_type=f32)


def dot_tn(a, b):
    return lax.dot_general(a, b, (((0,), (0,)), ((), ())), preferred_element_type=f32)


def lanes(parts):
    return jnp.concatenate(parts, axis=1)


NORM_ROWS = 32


def layer_norm(values, gain, shift):
    def piece(part):
        part = part.astype(f32)
        centre = part - jnp.mean(part, axis=-1, keepdims=True)
        spread = jnp.mean(centre * centre, axis=-1, keepdims=True)
        return (centre * lax.rsqrt(spread + norm_eps) * gain + shift).astype(bf16)

    return by_pieces(piece, NORM_ROWS, 0, values)


def eight_rows(values):
    return sum(values[8 * i : 8 * i + 8] for i in range(1, values.shape[0] // 8)) + values[0:8]


def norm_backward(values, gain, grad, sums_ref, first):
    sums = []

    def piece(part, grad_part):
        part = part.astype(f32)
        centre = part - jnp.mean(part, axis=-1, keepdims=True)
        spread = jnp.mean(centre * centre, axis=-1, keepdims=True)
        scale = lax.rsqrt(spread + norm_eps)
        xhat = centre * scale
        eg = grad_part * gain
        mean_eg = jnp.mean(eg, axis=-1, keepdims=True)
        mean_egx = jnp.mean(eg * xhat, axis=-1, keepdims=True)
        sums.append((eight_rows(grad_part * xhat), eight_rows(grad_part)))
        return scale * (eg - mean_eg - xhat * mean_egx)

    result = by_pieces(piece, NORM_ROWS, 0, values, grad)
    for n, parts in enumerate(zip(*sums)):
        sums_ref[first + 8 * n : first + 8 * n + 8, :] += sum(parts[1:], parts[0])
    return result


def add_sums(sums_ref, gln_ref, count):
    gln_ref[...] = jnp.zeros_like(gln_ref)
    for n in range(count):
        gln_ref[n : n + 1, :] = jnp.sum(sums_ref[8 * n : 8 * n + 8, :], axis=0, keepdims=True)


def by_pieces(work, size, axis, *arrays):
    count = arrays[0].shape[axis] // size
    pieces = []
    for i in range(count):
        cut = (slice(size * i, size * i + size),)
        cut = cut if axis == 0 else (slice(None),) + cut
        pieces.append(work(*[x[cut] for x in arrays]))
    if not isinstance(pieces[0], tuple):
        return jnp.concatenate(pieces, axis=axis)
    return tuple(jnp.concatenate(parts, axis=axis) for parts in zip(*pieces))


def rows_of(i, size=TILE):
    return pl.ds(pl.multiple_of(i * size, size), size)


def w_query(ref):
    return ref[:, 0:128]


def w_key(ref):
    return ref[:, 128:256]


def w_value(ref):
    return ref[:, 256:384]


def w_out(ref):
    return lanes([ref[128 * j : 128 * j + 128, 384:512] for j in range(4)])


def half_masks():
    place = lax.broadcasted_iota(jnp.int32, (1, 128), 1)
    low = jnp.where(place < HEAD_DIM, 1.0, 0.0).astype(f32)
    return (low.astype(bf16), (1.0 - low).astype(bf16))


def doc_bounds(meta, d, source):
    base = 17 if source else 1
    return meta[base + d], meta[base + 8 + d]


def window_of(first, limit):
    return pl.multiple_of(jnp.minimum((first // 16) * 16, limit), 16)


def key_bias(ks, ke, k0, width):
    place = k0 + lax.broadcasted_iota(jnp.int32, (width, 128), 0)
    return jnp.where((place >= ks) & (place < ke), 0.0, masked_score)


def make_bias(rank_ref, limit_ref, ks, ke, q0, k0, span, width):
    if rank_ref is None:
        return lanes([key_bias(ks, ke, k0, width)] * (span // 128))
    place = k0 + lax.broadcasted_iota(jnp.int32, (width, 128), 0)
    ranks = rank_ref[pl.ds(k0, width), :]
    ranks = jnp.where((place < ks + 2) & (ranks < hidden_rank), -1.0, ranks)
    ranks = jnp.where((place >= ks) & (place < ke), ranks, hidden_rank)
    limits = jnp.broadcast_to(limit_ref[...], (8, SEQ))
    limits = pltpu.roll(limits, lax.rem(SEQ - q0, SEQ), 1)[0:1, 0:span]
    row = k0 + lax.broadcasted_iota(jnp.int32, (width, span), 0)
    column = q0 + lax.broadcasted_iota(jnp.int32, (width, span), 1)
    seen = (lanes([ranks] * (span // 128)) < limits) & (row != column)
    return jnp.where(seen, 0.0, masked_score)


TOGETHER = 4
STEPS = DOCS // TOGETHER


LAG = 2


def interleave(items):
    items = [list(phases) for phases in items]
    depth = max(len(phases) for phases in items)
    results = [None] * len(items)
    for tick in range(len(items) + LAG * (depth - 1)):
        for phase in range(depth):
            n = tick - LAG * phase
            if 0 <= n < len(items) and phase < len(items[n]):
                run = items[n][phase]
                results[n] = run() if phase == 0 else run(results[n])
    return results


def by_halves(pairs, phases):
    shared = [{} for _ in range(pairs)]
    return [phases(n, a, shared[n]) for n in range(pairs) for a in range(2)]


def is_fast(meta, cross):
    return meta[34 if cross else 33] == 1


def both_heads(x, masks):
    return jnp.concatenate([x * masks[0], x * masks[1]], axis=0)


def pair_scores(queries, keys, masks):
    return dot_nt(both_heads(keys, masks), queries)


def raised(scores, bias):
    def piece(part, bias_part):
        part = part + bias_part
        return jnp.exp((part - jnp.max(part, axis=0, keepdims=True)).astype(bf16))

    return by_pieces(piece, 128, 1, scores, bias)


def weighted_values(values, parts):
    width = values.shape[1]
    mixed = []
    shares = []
    for a, part in enumerate(parts):
        rows = jnp.concatenate([values[64 * a : 64 * a + 64], jnp.ones((16, width), bf16)], axis=0)
        sums = dot(rows, part)
        share = 1.0 / sums[64:65]
        mixed.append(sums[:64] * share)
        shares.append(part * share.astype(bf16))
    return jnp.concatenate(mixed, axis=0).astype(bf16), shares


def pair_gradient(rows, parts):
    across = jnp.transpose(rows)
    halves = [dot(across[64 * a : 64 * a + 64], part) for a, part in enumerate(parts)]
    return jnp.transpose((jnp.concatenate(halves, axis=0) * HEAD_DIM**-0.5).astype(bf16))


def for_docs(meta, cross, run, before, after):
    @pl.when(is_fast(meta, cross))
    def _():
        def step(i, carry):
            slot = lax.rem(i, 2)
            before(i, slot)
            items = []
            for place in range(TOGETHER):
                d = TOGETHER * i + place
                ts, te = doc_bounds(meta, d, False)
                ks, ke = doc_bounds(meta, d, cross)
                q0 = window_of(ts, SEQ - FAST_Q)
                k0 = window_of(ks, SEQ - FAST_K)
                items += run(d, slot, place, q0, k0, FAST_Q, FAST_K, ts, te, ks, ke, True)
            interleave(items)
            after(i, slot)
            return carry

        lax.fori_loop(0, STEPS, step, 0)

    @pl.when(jnp.logical_not(is_fast(meta, cross)))
    def _():
        def doc(d, carry):
            ts, te = doc_bounds(meta, d, False)
            ks, ke = doc_bounds(meta, d, cross)
            base = (ts // 16) * 16
            k0 = window_of(ks, SEQ - LONG_K)

            def chunk(i, carry):
                lower = base + i * LONG_Q
                q0 = pl.multiple_of(jnp.minimum(lower, SEQ - LONG_Q), 16)
                low = jnp.maximum(ts, lower)
                high = jnp.minimum(te, lower + LONG_Q)
                interleave(run(d, None, None, q0, k0, LONG_Q, LONG_K, low, high, ks, ke, False))
                return carry

            return lax.fori_loop(0, (te - base + LONG_Q - 1) // LONG_Q, chunk, carry)

        lax.fori_loop(0, DOCS, doc, 0)


def attend_docs(meta, cross, rank_ref, limit_ref, halves, p_ref, p_buf, p_sem):
    pairs = 2 * len(halves)
    masks = half_masks()

    def save(i, slot):
        return pltpu.make_async_copy(p_buf.at[slot], p_ref.at[pl.ds(TOGETHER * i, TOGETHER)], p_sem.at[slot])

    def before(i, slot):
        @pl.when(i >= 2)
        def _():
            save(i - 2, slot).wait()

    def after(i, slot):
        save(i, slot).start()

    def run(d, slot, place, q0, k0, span, width, low, high, ks, ke, fast):
        bias = make_bias(rank_ref, limit_ref, ks, ke, q0, k0, span, width)
        row = q0 + lax.broadcasted_iota(jnp.int32, (span, 128), 0)
        inside = (row >= low) & (row < high)

        def phases(n):
            q_ref, k_ref, v_ref, mixed_ref = halves[n // 2]
            cols = slice(128 * (n % 2), 128 * (n % 2) + 128)

            def score():
                return pair_scores(q_ref[pl.ds(q0, span), cols], k_ref[pl.ds(k0, width), cols], masks)

            def weigh(scores):
                return [raised(scores[width * a : width * a + width], bias) for a in range(2)]

            def mix(parts):
                values = jnp.transpose(v_ref[pl.ds(k0, width), cols])
                mixed, parts = weighted_values(values, parts)
                if fast:
                    for a in range(2):
                        p_buf[slot, place, 2 * n + a] = parts[a]
                mixed = jnp.transpose(mixed).astype(f32)
                old = mixed_ref[pl.ds(q0, span), cols].astype(f32)
                mixed_ref[pl.ds(q0, span), cols] = jnp.where(inside, mixed, old).astype(bf16)

            return score, weigh, mix

        return [phases(n) for n in range(pairs)]

    for_docs(meta, cross, run, before, after)

    @pl.when(is_fast(meta, cross))
    def _():
        for i in range(STEPS - 2, STEPS):
            save(i, i % 2).wait()


def load_step(load, i, slot):
    p_ref, p_buf, p_sem = load
    return pltpu.make_async_copy(p_ref.at[pl.ds(TOGETHER * i, TOGETHER)], p_buf.at[slot], p_sem.at[slot])


def start_load(meta, cross, load):
    @pl.when(is_fast(meta, cross))
    def _():
        load_step(load, 0, 0).start()


def attend_docs_back(
    meta, cross, rank_ref, limit_ref, q_ref, k_ref, v_ref, mixed_ref, dm_ref,
    dq_ref, dk_ref, dv_ref, load,
):
    pairs = q_ref.shape[1] // 128
    masks = half_masks()
    p_buf = load[1]

    def before(i, slot):
        @pl.when(i + 1 < STEPS)
        def _():
            load_step(load, i + 1, 1 - slot).start()

        load_step(load, i, slot).wait()

    def after(i, slot):
        pass

    def run(d, slot, place, q0, k0, span, width, low, high, ks, ke, fast):
        row = q0 + lax.broadcasted_iota(jnp.int32, (span, 128), 0)
        inside = jnp.where((row >= low) & (row < high), 1.0, 0.0).astype(bf16)
        ones = jnp.ones((width, 128), bf16)
        if not fast:
            bias = make_bias(rank_ref, limit_ref, ks, ke, q0, k0, span, width)

        def phases(n):
            cols = slice(128 * n, 128 * n + 128)

            def differ():
                values = v_ref[pl.ds(k0, width), cols]
                mixed = mixed_ref[pl.ds(q0, span), cols]
                grad = dm_ref[pl.ds(q0, span), cols] * inside
                left = lanes([grad, -(grad * mixed)])
                right = both_heads(lanes([values, ones]), [lanes([m, m]) for m in masks])
                return grad, dot_nt(right, left)

            def slope(state):
                grad, delta = state
                if fast:
                    parts = [p_buf[slot, place, 2 * n + a] for a in range(2)]
                else:
                    queries = q_ref[pl.ds(q0, span), cols]
                    keys = k_ref[pl.ds(k0, width), cols]
                    scores = pair_scores(queries, keys, masks)
                    parts = [raised(scores[width * a : width * a + width], bias) for a in range(2)]
                    parts = weighted_values(jnp.transpose(v_ref[pl.ds(k0, width), cols]), parts)[1]
                slopes = [
                    by_pieces(
                        lambda part, change: part * change.astype(bf16),
                        16,
                        0,
                        parts[a],
                        delta[width * a : width * a + width],
                    )
                    for a in range(2)
                ]
                return grad, parts, slopes

            def spread(state):
                grad, parts, slopes = state
                queries = q_ref[pl.ds(q0, span), cols]
                dk = dv = None
                for a in range(2):
                    dk_a = dot(slopes[a], queries * masks[a])
                    dv_a = dot(parts[a], grad * masks[a])
                    dk = dk_a if dk is None else dk + dk_a
                    dv = dv_a if dv is None else dv + dv_a
                dq = pair_gradient(k_ref[pl.ds(k0, width), cols], slopes)
                dq_ref[pl.ds(q0, span), cols] += dq.astype(f32)
                dk_ref[pl.ds(k0, width), cols] += dk
                dv_ref[pl.ds(k0, width), cols] += dv

            return differ, slope, spread

        return [phases(n) for n in range(pairs)]

    for_docs(meta, cross, run, before, after)


def spread_ranks(rank_row_ref, rank_ref):
    rank_ref[...] = jnp.transpose(jnp.broadcast_to(rank_row_ref[...], (128, SEQ)))


def prepare(
    core, seg_ref, src_ref, rank_ref, limit_ref, pad_ref,
    n0, n1, n2, n3, n4, n5, n6, n7, sq, sk, sv, so, cq, ck, cv, co,
    meta_ref, ranks_ref, limits_ref, norms_ref, ws_ref, wc_ref,
):
    meta_ref[0] = core[0]
    meta_ref[35] = core[1]
    for base, ref in ((1, seg_ref), (17, src_ref)):
        ids = ref[0]
        meta_ref[base] = 0
        meta_ref[base + 15] = SEQ
        for d in range(1, DOCS):
            cut = jnp.sum(jnp.where(ids < d, 1.0, 0.0)).astype(jnp.int32)
            meta_ref[base + d] = cut
            meta_ref[base + 7 + d] = cut
    for place, base in ((33, 1), (34, 17)):
        fast = jnp.int32(1)
        for d in range(DOCS):
            q0 = window_of(meta_ref[1 + d], SEQ - FAST_Q)
            k0 = window_of(meta_ref[base + d], SEQ - FAST_K)
            fits = (meta_ref[9 + d] - q0 <= FAST_Q) & (meta_ref[base + 8 + d] - k0 <= FAST_K)
            fast = fast & fits.astype(jnp.int32)
        meta_ref[place] = fast
    ranks = jnp.where(pad_ref[0] != 0, hidden_rank, rank_ref[0].astype(f32))
    limits = limit_ref[0].astype(f32)
    for i in range(8):
        ranks_ref[0:1, 128 * i : 128 * i + 128] = ranks[i : i + 1]
        limits_ref[0:1, 128 * i : 128 * i + 128] = limits[i : i + 1]
    for i, ref in enumerate((n0, n1, n2, n3, n4, n5, n6, n7)):
        norms_ref[i : i + 1, :] = ref[...]
    for to, parts, out in ((ws_ref, (sq, sk, sv), so), (wc_ref, (cq, ck, cv), co)):
        for i, part in enumerate(parts):
            to[:, 128 * i : 128 * i + 128] = part[...]
        for j in range(4):
            to[128 * j : 128 * j + 128, 384:512] = out[:, 128 * j : 128 * j + 128]


def self_first(
    meta, io, xq_ref, xc_ref, rank_row_ref, limit_ref, norms_ref, w0_ref, w1_ref,
    nq_ref, nc_ref, q_ref, k_ref, v_ref, mixed_ref, p_ref, rank_ref, p_buf, p_sem,
):

    spread_ranks(rank_row_ref, rank_ref)
    wq = lanes([w_query(w0_ref), w_query(w1_ref)])
    wkv = lanes([w_key(w0_ref), w_key(w1_ref), w_value(w0_ref), w_value(w1_ref)])

    def tile(i, carry):
        rows = rows_of(i)
        io.wait_rows(i)
        nq = layer_norm(xq_ref[rows, :], norms_ref[0:1], norms_ref[1:2])
        nc = layer_norm(xc_ref[rows, :], norms_ref[2:3], norms_ref[3:4])
        nq_ref[rows, :] = nq
        nc_ref[rows, :] = nc
        q_ref[rows, :] = (dot(nq, wq) * (HEAD_DIM**-0.5)).astype(bf16)
        kv = dot(nc, wkv).astype(bf16)
        k_ref[rows, :] = kv[:, :256]
        v_ref[rows, :] = kv[:, 256:]
        return carry

    lax.fori_loop(0, TILES, tile, 0)

    for ref in (nq_ref, nc_ref, q_ref, k_ref, v_ref):
        io.send(ref)
    attend_docs(meta, False, rank_ref, limit_ref, [(q_ref, k_ref, v_ref, mixed_ref)], p_ref, p_buf, p_sem)


def self_second(
    meta, io, xq_ref, nq_ref, nc_ref, rank_row_ref, limit_ref, norms_ref, w0_ref, w1_ref, w2_ref, w3_ref,
    mixed_first_ref,
    q_ref, k_ref, v_ref, mixed_ref, p_ref, second_ref, ncross_ref, rank_ref, p_buf, p_sem,
):

    spread_ranks(rank_row_ref, rank_ref)
    wq = lanes([w_query(w2_ref), w_query(w3_ref)])
    wkv = lanes([w_key(w2_ref), w_key(w3_ref), w_value(w2_ref), w_value(w3_ref)])

    def tile(i, carry):
        rows = rows_of(i)
        io.wait_rows(i)
        q_ref[rows, :] = (dot(nq_ref[rows, :], wq) * (HEAD_DIM**-0.5)).astype(bf16)
        kv = dot(nc_ref[rows, :], wkv).astype(bf16)
        k_ref[rows, :] = kv[:, :256]
        v_ref[rows, :] = kv[:, 256:]
        return carry

    lax.fori_loop(0, TILES, tile, 0)

    for ref in (q_ref, k_ref, v_ref):
        io.send(ref)
    attend_docs(meta, False, rank_ref, limit_ref, [(q_ref, k_ref, v_ref, mixed_ref)], p_ref, p_buf, p_sem)

    io.send(mixed_ref)
    io.wait("late")
    out_first = jnp.concatenate([w_out(w0_ref), w_out(w1_ref)], axis=0)
    out_second = jnp.concatenate([w_out(w2_ref), w_out(w3_ref)], axis=0)

    def tile(i, carry):
        rows = rows_of(i)
        branch = dot(mixed_first_ref[rows, :], out_first) + dot(mixed_ref[rows, :], out_second)
        second = xq_ref[rows, :].astype(f32) + branch
        second_ref[rows, :] = second.astype(bf16)
        io.send(second_ref, rows)
        ncross_ref[rows, :] = layer_norm(second, norms_ref[4:5], norms_ref[5:6])
        io.send(ncross_ref, rows)
        return carry

    lax.fori_loop(0, TILES, tile, 0)


def project_cross(io, ncross_ref, memory_ref, weights, q_ref, k_ref, v_ref):
    wq = lanes([w_query(w) for w in weights])
    wkv = lanes([w_key(w) for w in weights] + [w_value(w) for w in weights])

    def tile(i, carry):
        rows = rows_of(i)
        io.wait_rows(i)
        q_ref[rows, :] = (dot(ncross_ref[rows, :], wq) * (HEAD_DIM**-0.5)).astype(bf16)
        kv = dot(memory_ref[rows, :], wkv).astype(bf16)
        k_ref[rows, :] = kv[:, :256]
        v_ref[rows, :] = kv[:, 256:]
        return carry

    lax.fori_loop(0, TILES, tile, 0)
    for ref in (q_ref, k_ref, v_ref):
        io.send(ref)


def cross_first(
    meta, io, ncross_ref, memory_ref, w0_ref, w1_ref,
    q_ref, k_ref, v_ref, mixed_ref, p_ref, p_buf, p_sem,
):
    project_cross(io, ncross_ref, memory_ref, (w0_ref, w1_ref), q_ref, k_ref, v_ref)
    attend_docs(meta, True, None, None, [(q_ref, k_ref, v_ref, mixed_ref)], p_ref, p_buf, p_sem)


def cross_second(
    meta, io, second_ref, ncross_ref, memory_ref, norms_ref, w0_ref, w1_ref, w2_ref, w3_ref,
    mixed_first_ref,
    q_ref, k_ref, v_ref, mixed_ref, p_ref, third_ref, nffn_ref, p_buf, p_sem,
):
    project_cross(io, ncross_ref, memory_ref, (w2_ref, w3_ref), q_ref, k_ref, v_ref)
    attend_docs(meta, True, None, None, [(q_ref, k_ref, v_ref, mixed_ref)], p_ref, p_buf, p_sem)
    io.send(mixed_ref)
    io.wait("late")
    out_first = jnp.concatenate([w_out(w0_ref), w_out(w1_ref)], axis=0)
    out_second = jnp.concatenate([w_out(w2_ref), w_out(w3_ref)], axis=0)

    def tile(i, carry):
        rows = rows_of(i)
        branch = dot(mixed_first_ref[rows, :], out_first) + dot(mixed_ref[rows, :], out_second)
        third = second_ref[rows, :].astype(f32) + branch
        third_ref[rows, :] = third
        nffn_ref[rows, :] = layer_norm(third, norms_ref[6:7], norms_ref[7:8])
        return carry

    lax.fori_loop(0, TILES, tile, 0)


def ffn_both(
    meta, io, third_ref, nffn_ref, cot_ref, norms_ref, u0_ref, u1_ref, u2_ref, u3_ref,
    w0_ref, w1_ref, w2_ref, w3_ref,
    placed_ref, out_ref, g3_low_ref, gln_ref, own_ref, other_ref, hidden_ref, before_ref, sums_ref,
):
    sums_ref[...] = jnp.zeros_like(sums_ref)
    in_refs = (u0_ref, u1_ref, u2_ref, u3_ref)
    w_refs = (w0_ref, w1_ref, w2_ref, w3_ref)

    def tile(i, carry):
        rows = rows_of(i)
        io.wait_rows(i)
        nffn = nffn_ref[rows, :]
        cot = cot_ref[rows, :]
        outs = []
        grads = []

        def phases(g, c, group):
            w_in = in_refs[g]
            w_out_rows = w_refs[g]
            cols = slice(256 * c, 256 * c + 256)

            def enter():
                return dot(nffn, w_in[:, cols]), dot_nt(cot, w_out_rows[cols, :])

            def bend(state):
                def piece(x, grad_hidden):
                    square = x * x
                    argument = x * (gelu_root + (gelu_root * gelu_cube) * square)
                    half = 0.5 + 0.5 * jnp.tanh(argument.astype(bf16))
                    x = x.astype(bf16)
                    square = square.astype(bf16)
                    value = x * half
                    rise = 2.0 * gelu_root + (6.0 * gelu_root * gelu_cube) * square
                    slope = half + value * (1.0 - half) * rise
                    return value, grad_hidden.astype(bf16) * slope

                hidden, grad_before = by_pieces(piece, 32, 0, *state)
                if g < 2:
                    place = slice(512 * g + 256 * c, 512 * g + 256 * c + 256)
                    hidden_ref[rows, place] = hidden
                    before_ref[rows, place] = grad_before
                group[c] = hidden, grad_before

            def leave(_):
                if c == 1:
                    outs.append(dot(lanes([group[0][0], group[1][0]]), w_out_rows[...]))

            def leave_back(_):
                if c == 1:
                    grads.append(dot_nt(lanes([group[0][1], group[1][1]]), w_in[...]))

            return enter, bend, leave, leave_back

        interleave(by_halves(4, phases))
        third = third_ref[rows, :]
        result = (third + ((outs[0] + outs[1]) + (outs[2] + outs[3]))).astype(bf16)
        out_ref[rows, :] = result
        placed_ref[rows, :] = result
        grad_normed = (grads[0] + grads[1]) + (grads[2] + grads[3])
        grad_norm = norm_backward(third, norms_ref[6:7], grad_normed, sums_ref, 0)
        g3_low_ref[rows, :] = (cot.astype(f32) + grad_norm).astype(bf16)
        for ref in (out_ref, placed_ref, g3_low_ref):
            io.send(ref, rows)
        return carry

    lax.fori_loop(0, TILES, tile, 0)
    add_sums(sums_ref, gln_ref, 2)
    part = dot_tn(nffn_ref[...], before_ref[...])
    own_ref[0:512, :] = part[:, 0:512].astype(bf16)
    other_ref[0:512, :] = part[:, 512:1024].astype(bf16)
    io.send(own_ref, pl.ds(0, 512))
    io.send(other_ref, pl.ds(0, 512))
    part = dot_tn(hidden_ref[...], cot_ref[...])
    own_ref[512:1024, :] = part[0:512].astype(bf16)
    other_ref[512:1024, :] = part[512:1024].astype(bf16)
    io.send(own_ref, pl.ds(512, 512))
    io.send(other_ref, pl.ds(512, 512))


def back_start(io, g_ref, mixed_ref, w_refs, dm_ref, dq_ref, dk_ref, dv_ref):
    out_rows = jnp.concatenate([w_out(w) for w in w_refs], axis=0)

    def tile(i, carry):
        rows = rows_of(i)
        io.wait_rows(i)
        dm_ref[rows, :] = dot_nt(g_ref[rows, :], out_rows).astype(bf16)
        zeros = jnp.zeros((TILE, 256), f32)
        dq_ref[rows, :] = zeros
        dk_ref[rows, :] = zeros
        dv_ref[rows, :] = zeros
        return carry

    lax.fori_loop(0, TILES, tile, 0)


def attention_back_first(
    cross, meta, io, g_ref, nq_ref, nkv_ref, rank_row_ref, limit_ref, w0_ref, w1_ref,
    q_ref, k_ref, v_ref, mixed_ref, p_ref,
    dq_ref, dk_ref, dv_ref, own_ref, other_ref,
    rank_ref, dm_ref, dqs_ref, dks_ref, dvs_ref, p_buf, p_sem,
):
    load = (p_ref, p_buf, p_sem)
    start_load(meta, cross, load)
    if not cross:
        spread_ranks(rank_row_ref, rank_ref)
    back_start(io, g_ref, mixed_ref, (w0_ref, w1_ref), dm_ref, dqs_ref, dks_ref, dvs_ref)

    io.wait("soon")
    attend_docs_back(
        meta, cross, None if cross else rank_ref, limit_ref, q_ref, k_ref, v_ref, mixed_ref,
        dm_ref, dqs_ref, dks_ref, dvs_ref, load,
    )

    dq_ref[...] = dqs_ref[...].astype(bf16)
    dk_ref[...] = dks_ref[...].astype(bf16)
    dv_ref[...] = dvs_ref[...].astype(bf16)
    for ref in (dq_ref, dk_ref, dv_ref):
        io.send(ref)
    io.wait("late")
    nq = nq_ref[...]
    nkv = nkv_ref[...]
    kv = dot_tn(nkv, lanes([dk_ref[...], dv_ref[...]]))
    for n, part in enumerate((dot_tn(nq, dq_ref[...]), kv[:, 0:256], kv[:, 256:512])):
        own_ref[:, 128 * n : 128 * n + 128] = part[:, :128].astype(bf16)
        other_ref[:, 128 * n : 128 * n + 128] = part[:, 128:].astype(bf16)
    part = dot_tn(mixed_ref[...], g_ref[...])
    for j in range(4):
        rows = slice(128 * j, 128 * j + 128)
        own_ref[rows, 384:512] = part[:128, rows].astype(bf16)
        other_ref[rows, 384:512] = part[128:, rows].astype(bf16)


def back_second_docs(
    cross, meta, io, g_ref, rank_row_ref, limit_ref, w_refs, q_ref, k_ref, v_ref, mixed_ref, p_ref,
    rank_ref, dm_ref, dqs_ref, dks_ref, dvs_ref, p_buf, p_sem,
):
    load = (p_ref, p_buf, p_sem)
    start_load(meta, cross, load)
    if not cross:
        spread_ranks(rank_row_ref, rank_ref)
    back_start(io, g_ref, mixed_ref, w_refs, dm_ref, dqs_ref, dks_ref, dvs_ref)

    io.wait("soon")
    attend_docs_back(
        meta, cross, None if cross else rank_ref, limit_ref, q_ref, k_ref, v_ref, mixed_ref,
        dm_ref, dqs_ref, dks_ref, dvs_ref, load,
    )


def stream_grads(rows, first, second, firsts, seconds):
    dq, dk, dv = first
    dq2, dk2, dv2 = (ref[rows, :].astype(bf16) for ref in second)
    w0, w1 = firsts
    w2, w3 = seconds
    grad_q = dot_nt(dq[rows, :], lanes([w_query(w0), w_query(w1)])) + dot_nt(
        dq2, lanes([w_query(w2), w_query(w3)])
    )
    kv = lanes([dk[rows, :], dv[rows, :]])
    kv2 = lanes([dk2, dv2])
    grad_kv = dot_nt(kv, lanes([w_key(w0), w_key(w1), w_value(w0), w_value(w1)])) + dot_nt(
        kv2, lanes([w_key(w2), w_key(w3), w_value(w2), w_value(w3)])
    )
    return grad_q, grad_kv


def cross_back_second(
    meta, io, g_low_ref, second_ref, norms_ref, w0_ref, w1_ref, w2_ref, w3_ref,
    dq_ref, dk_ref, dv_ref, q_ref, k_ref, v_ref, mixed_ref, p_ref,
    g2_low_ref, placed_ref, gmem_ref, gln_ref,
    dm_ref, dqs_ref, dks_ref, dvs_ref, p_buf, p_sem, sums_ref,
):
    back_second_docs(
        True, meta, io, g_low_ref, None, None, (w2_ref, w3_ref), q_ref, k_ref, v_ref, mixed_ref, p_ref,
        None, dm_ref, dqs_ref, dks_ref, dvs_ref, p_buf, p_sem,
    )

    io.wait("late")
    sums_ref[...] = jnp.zeros_like(sums_ref)

    def tile(i, carry):
        rows = rows_of(i)
        grad_q, grad_kv = stream_grads(
            rows,
            (dq_ref, dk_ref, dv_ref),
            (dqs_ref, dks_ref, dvs_ref),
            (w0_ref, w1_ref),
            (w2_ref, w3_ref),
        )
        low_kv = grad_kv.astype(bf16)
        gmem_ref[rows, :] = low_kv
        placed_ref[rows, :] = low_kv.astype(f32)
        io.send(gmem_ref, rows)
        io.send(placed_ref, rows)
        grad_norm = norm_backward(second_ref[rows, :], norms_ref[4:5], grad_q, sums_ref, 0)
        g2_low_ref[rows, :] = (g_low_ref[rows, :].astype(f32) + grad_norm).astype(bf16)
        io.send(g2_low_ref, rows)
        return carry

    lax.fori_loop(0, TILES, tile, 0)
    add_sums(sums_ref, gln_ref, 2)


def self_back_second(
    meta, io, g_low_ref, rank_row_ref, limit_ref, w2_ref, w3_ref,
    q_ref, k_ref, v_ref, mixed_ref, p_ref,
    dq_ref, dk_ref, dv_ref,
    rank_ref, dm_ref, dqs_ref, dks_ref, dvs_ref, p_buf, p_sem,
):
    back_second_docs(
        False, meta, io, g_low_ref, rank_row_ref, limit_ref, (w2_ref, w3_ref), q_ref, k_ref, v_ref,
        mixed_ref, p_ref, rank_ref, dm_ref, dqs_ref, dks_ref, dvs_ref, p_buf, p_sem,
    )
    dq_ref[...] = dqs_ref[...].astype(bf16)
    dk_ref[...] = dks_ref[...].astype(bf16)
    dv_ref[...] = dvs_ref[...].astype(bf16)


def self_back_finish(
    meta, io, g_ref, xq_ref, xc_ref, norms_ref, w0_ref, w1_ref, w2_ref, w3_ref,
    dq_ref, dk_ref, dv_ref, dq2_ref, dk2_ref, dv2_ref,
    placed_q_ref, placed_c_ref, gq_ref, gc_ref, gln_ref, sums_ref,
):
    sums_ref[...] = jnp.zeros_like(sums_ref)

    def tile(i, carry):
        rows = rows_of(i)
        io.wait_rows(i)
        grad_q, grad_kv = stream_grads(
            rows,
            (dq_ref, dk_ref, dv_ref),
            (dq2_ref, dk2_ref, dv2_ref),
            (w0_ref, w1_ref),
            (w2_ref, w3_ref),
        )
        grad_norm = norm_backward(xq_ref[rows, :], norms_ref[0:1], grad_q, sums_ref, 0)
        low_q = (g_ref[rows, :].astype(f32) + grad_norm).astype(bf16)
        gq_ref[rows, :] = low_q
        placed_q_ref[rows, :] = low_q.astype(f32)
        io.send(gq_ref, rows)
        io.send(placed_q_ref, rows)
        grad_norm = norm_backward(xc_ref[rows, :], norms_ref[2:3], grad_kv, sums_ref, 16)
        low_c = grad_norm.astype(bf16)
        gc_ref[rows, :] = low_c
        placed_c_ref[rows, :] = low_c.astype(f32)
        io.send(gc_ref, rows)
        io.send(placed_c_ref, rows)
        return carry

    lax.fori_loop(0, TILES, tile, 0)
    add_sums(sums_ref, gln_ref, 4)


def place_rows(meta, *refs):
    count = len(refs) // 3
    for n in range(count):
        refs[2 * count + n][...] = refs[n][...].astype(refs[2 * count + n].dtype)


GROUP = 8


def position(meta):
    r = meta[35]
    return lax.rem(r, 2), r // 2


def join(own, other, rows):
    return (own[rows, :].astype(f32) + other[rows, :].astype(f32)).astype(bf16)


def join_halves(meta, own, other, keep, send):
    y, _ = position(meta)
    size = keep.shape[0]
    keep[...] = join(own, other, rows_of(y, size))
    send[...] = join(own, other, rows_of(1 - y, size))


def join_chunks(meta, kept, arrived, keep, sends):
    _, z = position(meta)
    size = keep.shape[0]
    keep[...] = join(kept, arrived, rows_of(z, size))
    for s, (send, first) in enumerate(sends, 1):
        send[first : first + size, :] = join(kept, arrived, rows_of(z ^ s, size))


def add_up(kept, parts, first):
    size = kept.shape[0]
    total = kept[...].astype(f32)
    for part in parts:
        total = total + part[first : first + size, :].astype(f32)
    return total.astype(bf16)


def half_of(meta, total, parts, first, half):
    _, z = position(meta)
    size = total.shape[0]
    half[rows_of(z, size), :] = total[...]
    for s, part in enumerate(parts, 1):
        half[rows_of(z ^ s, size), :] = part[first : first + size, :]


def slot_1(meta, ffn_own, ffn_other, keep, send):
    join_halves(meta, ffn_own, ffn_other, keep, send)


def slot_2(
    meta, ffn_kept, ffn_arrived, cross_own, cross_other, ffn_keep, f1, f2, f3, keep, send
):
    join_chunks(meta, ffn_kept, ffn_arrived, ffn_keep, [(f1, 0), (f2, 0), (f3, 0)])
    join_halves(meta, cross_own, cross_other, keep, send)


def slot_3(
    meta, ffn_kept, f1, f2, f3, cross_kept, cross_arrived, self_own, self_other,
    ffn_total, cross_keep, m1, m2, m3, self_keep, self_send,
):
    join_halves(meta, self_own, self_other, self_keep, self_send)
    total = add_up(ffn_kept, (f1, f2, f3), 0)
    ffn_total[...] = total
    size = total.shape[0]
    join_chunks(meta, cross_kept, cross_arrived, cross_keep, [(m, size) for m in (m1, m2, m3)])
    for m in (m1, m2, m3):
        m[0:size, :] = total


def slot_4(
    meta, ffn_total, m1, m2, m3, cross_kept, self_kept, self_arrived,
    ffn_half, cross_total, self_keep, *sends,
):
    join_chunks(meta, self_kept, self_arrived, self_keep, [(send, 0) for send in sends])
    total = add_up(cross_kept, (m1, m2, m3), ffn_total.shape[0])
    cross_total[...] = total
    size = total.shape[0]
    for send in sends:
        send[size:, :] = total
    half_of(meta, ffn_total, (m1, m2, m3), 0, ffn_half)


def slot_5(meta, self_kept, cross_total, m1, m2, m3, gln_own, gln_other, send, cross_half):
    size = self_kept.shape[0]
    total = add_up(self_kept, (m1, m2, m3), 0)
    gln = gln_own[...] + gln_other[...]
    gln = jnp.concatenate([gln, jnp.zeros((8, D), f32)], axis=0).astype(bf16)
    for r in range(GROUP):
        send[r, 0:size, :] = total
        send[r, size : size + 16, :] = gln
    half_of(meta, cross_total, (m1, m2, m3), size, cross_half)


def unpack_attention(whole_ref, outs):
    for i in range(3):
        outs[i][...] = whole_ref[:, 128 * i : 128 * i + 128].astype(f32)
    for j in range(4):
        rows = slice(128 * j, 128 * j + 128)
        outs[3][:, rows] = whole_ref[rows, 384:512].astype(f32)


def unpack_ffn(meta, half, arrived, out_in, out_out, ffn_whole):
    y, _ = position(meta)
    ffn_whole[rows_of(y, 512), :] = half[...]
    ffn_whole[rows_of(1 - y, 512), :] = arrived[...]
    out_in[...] = ffn_whole[0:512, :].astype(f32)
    out_out[...] = ffn_whole[512:1024, :].astype(f32)


def unpack_rest(meta, cross_half, cross_arrived, parts, *refs):
    *outs, gln, whole_ref = refs
    y, _ = position(meta)
    whole_ref[rows_of(y, 256), :] = cross_half[...]
    whole_ref[rows_of(1 - y, 256), :] = cross_arrived[...]
    unpack_attention(whole_ref, outs[0:4])
    size = parts.shape[1] - 16
    total = parts[0, size : size + 16, :].astype(f32)
    for r in range(1, GROUP):
        total = total + parts[r, size : size + 16, :].astype(f32)
    gln[...] = total[0:8]
    for r in range(GROUP):
        first = size * (4 * (r % 2) + r // 2)
        whole_ref[first : first + size, :] = parts[r, 0:size, :]
    unpack_attention(whole_ref, outs[4:8])


def whole(shape):
    zeros = (0,) * len(shape)
    return pl.BlockSpec(shape, lambda d, meta: zeros)


def own_row(width):
    return pl.BlockSpec((SEQ, width), lambda d, meta: (meta[0], 0))


ANY = pl.BlockSpec(memory_space=pl.ANY)


def in_hbm(x):
    return pltpu.with_memory_space_constraint(x, pltpu.HBM)


probability_out = (pltpu.HBM((DOCS, 4, FAST_K, FAST_Q), bf16), None, ANY)
probability_scratch = [
    pltpu.VMEM((2, TOGETHER, 4, FAST_K, FAST_Q), bf16),
    pltpu.SemaphoreType.DMA((2,)),
]


class Copies:
    def __init__(self, meta):
        self.first = meta[0] * SEQ
        self.loads = {}
        self.tiles = []
        self.sends = []

    def load(self, stage, source, target, sems, own_row):
        if stage == "fresh":
            stage = "now"
        if stage == "tiles":
            first = self.first if own_row else 0
            self.tiles.append((source, target, sems, first))
            return
        if own_row:
            source = source.at[pl.ds(pl.multiple_of(self.first, SEQ), SEQ)]
        copy = pltpu.make_async_copy(source, target, sems[0].at[sems[1], 0])
        self.loads.setdefault(stage, []).append(copy)

    def tile(self, entry, i):
        source, target, (sems, b), first = entry
        rows = pl.ds(pl.multiple_of(first + i * TILE, TILE), TILE)
        return pltpu.make_async_copy(source.at[rows], target.at[rows_of(i)], sems.at[b, i])

    def start(self):
        for copy in self.loads.get("now", []):
            copy.start()
        for i in range(TILES):
            for entry in self.tiles:
                self.tile(entry, i).start()
        for stage in ("soon", "late"):
            for copy in self.loads.get(stage, []):
                copy.start()

    def wait(self, stage):
        for copy in self.loads.pop(stage, []):
            copy.wait()

    def wait_rows(self, i):
        for entry in self.tiles:
            self.tile(entry, i).wait()

    def result(self, source, target, sem, own_row):
        self.sends.append([source, target, sem, own_row, False])

    def send(self, ref, rows=None):
        for entry in self.sends:
            source, target, sem, own_row, _ = entry
            if source is ref:
                entry[4] = True
                first = self.first if own_row else 0
                if rows is None:
                    size = source.shape[0]
                else:
                    source = source.at[rows]
                    first, size = first + rows.start, rows.size
                if rows is not None or own_row:
                    target = target.at[pl.ds(pl.multiple_of(first, size), size)]
                pltpu.make_async_copy(source, target, sem).start()

    def finish(self):
        for stage in list(self.loads):
            self.wait(stage)
        for source, _, _, _, started in self.sends:
            if not started:
                self.send(source)
        for source, target, sem, own_row, _ in self.sends:
            if own_row:
                target = target.at[pl.ds(pl.multiple_of(self.first, SEQ), SEQ)]
            pltpu.make_async_copy(source, target, sem).wait()


def out(shape, dtype, own_row=False):
    return (shape, dtype, own_row)


def call(kernel, name, operands, outs, scratch, flops, token=None):
    arrays = [operands[0][0]]
    in_specs, out_specs, out_shapes = [], [], []
    buffers = []
    loads = []
    for n, (x, how) in enumerate(operands[1:]):
        if isinstance(how, str):
            stage, _, row = how.partition("_")
            shape = ((SEQ,) + x.shape[1:]) if row else x.shape
            loads.append((n, stage, len(buffers), bool(row)))
            buffers.append(pltpu.VMEM(shape, x.dtype))
            arrays.append(x if stage == "fresh" else in_hbm(x))
            in_specs.append(ANY)
        else:
            arrays.append(x)
            in_specs.append(how)
    results = []
    for n, (shape, dtype, how) in enumerate(outs):
        if isinstance(how, bool):
            results.append((n, len(buffers), how))
            buffers.append(pltpu.VMEM(shape, dtype))
            shape = ((2 * SEQ,) + shape[1:]) if how else shape
            out_shapes.append(pltpu.HBM(shape, dtype))
            out_specs.append(ANY)
        else:
            out_shapes.append(jax.ShapeDtypeStruct(shape, dtype) if dtype else shape)
            out_specs.append(how)
    n_in, n_out = len(in_specs), len(out_specs)
    if token is not None:
        arrays.append(token)
        in_specs.append(whole((8, 128)))
        out_specs.append(whole((8, 128)))
        out_shapes.append(jax.ShapeDtypeStruct((8, 128), f32))

    def body(meta, *refs):
        ins, refs = list(refs[:n_in]), refs[len(in_specs) - n_in + n_in :]
        results_out, refs = list(refs[:n_out]), refs[n_out:]
        if token is not None:
            token_out, refs = refs[0], refs[1:]
            token_out[...] = jnp.zeros_like(token_out)
        bufs, refs = refs[: len(buffers)], refs[len(buffers) :]
        rest = refs[: len(scratch)]
        copies = Copies(meta)
        if buffers:
            sems = refs[len(scratch)]
        for n, stage, b, row in loads:
            copies.load(stage, ins[n], bufs[b], (sems, b), row)
            ins[n] = bufs[b]
        for n, b, row in results:
            copies.result(bufs[b], results_out[n], sems.at[b, 0], row)
            results_out[n] = bufs[b]
        copies.start()
        copies.wait("now")
        if buffers:
            kernel(meta, copies, *ins, *results_out, *rest)
        else:
            kernel(meta, *ins, *results_out, *rest)
        copies.finish()

    moved = sum(x.size * x.dtype.itemsize for x in arrays[1:])
    sems = [pltpu.SemaphoreType.DMA((len(buffers), TILES))] if buffers else []
    return pl.pallas_call(
        body,
        name=name,
        grid_spec=pltpu.PrefetchScalarGridSpec(
            num_scalar_prefetch=1,
            grid=(1,),
            in_specs=in_specs,
            out_specs=out_specs,
            scratch_shapes=buffers + scratch + sems,
        ),
        out_shape=out_shapes,
        compiler_params=pltpu.CompilerParams(
            dimension_semantics=("arbitrary",), vmem_limit_bytes=40 * 1024 * 1024
        ),
        cost_estimate=pl.CostEstimate(
            flops=int(flops), bytes_accessed=int(moved), transcendentals=0
        ),
    )(*arrays)


def simple(kernel, name, meta, operands, outs, scratch=()):
    return pl.pallas_call(
        kernel,
        name=name,
        grid_spec=pltpu.PrefetchScalarGridSpec(
            num_scalar_prefetch=1,
            grid=(1,),
            in_specs=[whole(x.shape) for x in operands],
            out_specs=[whole(shape) for shape, _ in outs],
            scratch_shapes=scratch,
        ),
        out_shape=[jax.ShapeDtypeStruct(shape, dtype) for shape, dtype in outs],
        compiler_params=pltpu.CompilerParams(vmem_limit_bytes=16 * 1024 * 1024),
    )(meta, *operands)


def full(x):
    return (x, whole(x.shape))


def shards(
    query_stream,
    content_stream,
    memory,
    segment_ids,
    source_segments,
    context_rank,
    context_limit,
    padding,
    ln_query_gain,
    ln_query_bias,
    ln_content_gain,
    ln_content_bias,
    self_query,
    self_key,
    self_value,
    self_out,
    ln_cross_gain,
    ln_cross_bias,
    cross_query,
    cross_key,
    cross_value,
    cross_out,
    ln_ffn_gain,
    ln_ffn_bias,
    ffn_in,
    ffn_out,
    cotangent,
):
    core = lax.axis_index("heads") % 2

    def to_core(x):
        return lax.ppermute(x, "heads", [(h, h ^ 1) for h in range(4)])

    hold = lambda *xs: lax.optimization_barrier(xs)

    def to_chip(x):
        return lax.ppermute(x, "heads", [(h, h ^ 2) for h in range(4)])

    row = pl.BlockSpec((1, 8, 128), lambda d, core: (core[0], 0, 0))

    def token_row(x):
        return (in_hbm(x.reshape(2, 8, 128)), row)

    def fixed(x):
        zeros = (0,) * x.ndim
        return (in_hbm(x), pl.BlockSpec(x.shape, lambda d, core: zeros))

    prepared = [
        ((36,), jnp.int32, pl.BlockSpec(memory_space=pltpu.SMEM)),
        ((1, SEQ), f32, whole((1, SEQ))),
        ((1, SEQ), f32, whole((1, SEQ))),
        ((8, D), f32, whole((8, D))),
        ((D, D), bf16, whole((D, D))),
        ((D, D), bf16, whole((D, D))),
    ]
    gains = (
        ln_query_gain,
        ln_query_bias,
        ln_content_gain,
        ln_content_bias,
        ln_cross_gain,
        ln_cross_bias,
        ln_ffn_gain,
        ln_ffn_bias,
    )
    weights = (self_query, self_key, self_value, self_out)
    weights += (cross_query, cross_key, cross_value, cross_out)
    tokens = (segment_ids, source_segments, context_rank, context_limit, padding)
    meta, rank, limit, norms, ws0, wc0 = call(
        prepare,
        "prepare",
        [(jnp.stack([core, lax.axis_index("rows") % GROUP]).astype(jnp.int32), None)]
        + [token_row(x) for x in tokens]
        + [fixed(x.reshape(1, D)) for x in gains]
        + [fixed(x) for x in weights],
        prepared,
        [],
        0,
    )

    ws1 = to_core(ws0)
    ws2 = to_chip(ws0)
    wc1 = to_core(wc0)
    u0, v0 = ffn_in, ffn_out
    meta_in = (meta, None)

    heads_out = [out((SEQ, 256), bf16)] * 4

    def stream_out(dtype, own_row=False):
        return out((SEQ, D), dtype, own_row)

    def now(*xs):
        return [(x, "now") for x in xs]

    def fresh(*xs):
        return [(x, "fresh") for x in xs]

    def soon(*xs):
        return [(x, "soon") for x in xs]

    def late(*xs):
        return [(x, "late") for x in xs]

    def small(*xs):
        return [(x, whole(x.shape)) for x in xs]

    limits = pltpu.VMEM((SEQ, 128), f32)
    pair_flops = 2 * SEQ * D * 768 + 2 * 2 * 4 * DOCS * FAST_Q * FAST_K * 256

    nq, nc, *first, token = call(
        self_first,
        "self_first",
        [meta_in, (query_stream, "tiles_row"), (content_stream, "tiles_row")]
        + small(rank, limit, norms)
        + fresh(ws0, ws1),
        [stream_out(bf16), stream_out(bf16)] + heads_out + [probability_out],
        [limits] + probability_scratch,
        pair_flops,
        jnp.zeros((8, 128), f32),
    )
    ws2, wc0, u0, token = hold(ws2, wc0, u0, token)
    ws3 = to_core(ws2)
    wc2 = to_chip(wc0)
    u2 = to_chip(u0)
    *second_heads, second, ncross, token = call(
        self_second,
        "self_second",
        [meta_in, (query_stream, "late_row")]
        + [(nq, "tiles"), (nc, "tiles")]
        + small(rank, limit, norms)
        + late(ws0, ws1)
        + fresh(ws2, ws3)
        + late(first[3]),
        heads_out + [probability_out, stream_out(bf16), stream_out(bf16)],
        [limits] + probability_scratch,
        pair_flops + 2 * SEQ * D * D,
        token,
    )
    u0, token = hold(u0, token)
    u1 = to_core(u0)
    *cross_heads, token = call(
        cross_first,
        "cross_first",
        [meta_in, (ncross, "tiles"), (memory, "tiles_row")] + fresh(wc0, wc1),
        heads_out + [probability_out],
        probability_scratch,
        pair_flops,
        token,
    )
    wc2, u2, v0, token = hold(wc2, u2, v0, token)
    wc3 = to_core(wc2)
    u3 = to_core(u2)
    v2 = to_chip(v0)
    v1 = to_core(v0)
    *cross_heads_second, third, nffn, token = call(
        cross_second,
        "cross_second",
        [meta_in]
        + late(second)
        + [(ncross, "tiles"), (memory, "tiles_row")]
        + small(norms)
        + late(wc0, wc1)
        + fresh(wc2, wc3)
        + late(cross_heads[3]),
        heads_out
        + [probability_out, ((SEQ, D), f32, whole((SEQ, D))), ((SEQ, D), bf16, whole((SEQ, D)))],
        probability_scratch,
        pair_flops + 2 * SEQ * D * D,
        token,
    )
    u3, v2, token = hold(u3, v2, token)
    v3 = to_core(v2)
    grads_ln = ((8, D), f32, whole((8, D)))
    placed_output, output, g3_low, gln_ffn, ffn_own, ffn_other, token = call(
        ffn_both,
        "ffn_both",
        [meta_in]
        + small(third, nffn)
        + [(cotangent, "tiles_row")]
        + small(norms)
        + now(u0) + fresh(u1, u2, u3) + now(v0) + fresh(v1, v2, v3),
        [
            stream_out(bf16, True),
            stream_out(bf16),
            stream_out(bf16),
            grads_ln,
            out((1024, D), bf16),
            out((1024, D), bf16),
        ],
        [pltpu.VMEM((SEQ, 1024), bf16), pltpu.VMEM((SEQ, 1024), bf16), pltpu.VMEM((16, D), f32)],
        12 * SEQ * D * 2048,
        token,
    )

    def both_rows(placed_own, others, name):
        count = len(others)
        size = SEQ // 2
        one = pl.BlockSpec((size, D), lambda i, meta: (i, 0))
        block = pl.BlockSpec((size, D), lambda i, meta: (2 * (1 - meta[0]) + i, 0))
        return pl.pallas_call(
            place_rows,
            name=name,
            grid_spec=pltpu.PrefetchScalarGridSpec(
                num_scalar_prefetch=1,
                grid=(2,),
                in_specs=[one] * count + [pl.BlockSpec(memory_space=pl.ANY)] * count,
                out_specs=[block] * count,
            ),
            out_shape=[jax.ShapeDtypeStruct(x.shape, x.dtype) for x in placed_own],
            input_output_aliases={1 + count + n: n for n in range(count)},
        )(meta, *others, *placed_own)

    row_count = lax.axis_size("rows")
    assert row_count % GROUP == 0

    def along_rows(x, s):
        return lax.ppermute(x, "rows", [(r, r ^ s) for r in range(row_count)])

    def to_y(x):
        return along_rows(x, 1)

    def to_z(sends):
        return [along_rows(x, 2 * s) for s, x in enumerate(sends, 1)]

    def rows_out(*sizes):
        return [((n, D), bf16) for n in sizes]

    ffn_other = to_core(ffn_other)
    output_other = to_core(output)

    back_scratch = [pltpu.VMEM((SEQ, 256), bf16)] + [pltpu.VMEM((SEQ, 256), f32)] * 3
    back_scratch += probability_scratch
    pair_out = out((SEQ, 256), bf16)
    packed_outs = [((D, D), bf16, whole((D, D)))] * 2
    back_flops = 2 * SEQ * D * 256 + 4 * 2 * 4 * DOCS * FAST_Q * FAST_K * 256

    def head_inputs(natural, p):
        return soon(*natural) + [(in_hbm(p), ANY)]

    *cross_grads, cross_own, cross_other, token = call(
        functools.partial(attention_back_first, True),
        "cross_back_first",
        [meta_in]
        + [(g3_low, "tiles")]
        + late(ncross)
        + [(memory, "late_row")]
        + small(rank, limit)
        + now(wc0, wc1)
        + head_inputs(cross_heads[0:4], cross_heads[4]),
        [pair_out] * 3 + packed_outs,
        [limits] + back_scratch,
        back_flops + 2 * SEQ * D * 1024,
        token,
    )
    ffn_other, output_other, token = hold(ffn_other, output_other, token)
    ffn_keep, ffn_send = simple(slot_1, "slot_1", meta, [ffn_own, ffn_other], rows_out(512, 512))
    ffn_send, token = hold(ffn_send, token)
    ffn_arrived = to_y(ffn_send)
    cross_other = to_core(cross_other)
    g2_low, placed_mem, grad_mem, gln_cross, token = call(
        cross_back_second,
        "cross_back_second",
        [meta_in]
        + [(g3_low, "tiles")]
        + late(second)
        + small(norms)
        + late(wc0, wc1)
        + now(wc2, wc3)
        + late(*cross_grads)
        + head_inputs(cross_heads_second[0:4], cross_heads_second[4]),
        [stream_out(bf16), stream_out(f32, True), stream_out(bf16), grads_ln],
        back_scratch + [pltpu.VMEM((16, D), f32)],
        back_flops + 2 * SEQ * D * 1536,
        token,
    )
    ffn_arrived, cross_other, token = hold(ffn_arrived, cross_other, token)
    ffn_keep, *sends, cross_keep, cross_send = simple(
        slot_2,
        "slot_2",
        meta,
        [ffn_keep, ffn_arrived, cross_own, cross_other],
        rows_out(128, 128, 128, 128, 256, 256),
    )
    ffn_keep, cross_send, token = hold(ffn_keep, cross_send, token)
    ffn_parts = to_z(sends)
    cross_arrived = to_y(cross_send)

    *self_grads, self_own, self_other, token = call(
        functools.partial(attention_back_first, False),
        "self_back_first",
        [meta_in]
        + [(g2_low, "tiles")]
        + late(nq, nc)
        + small(rank, limit)
        + now(ws0, ws1)
        + head_inputs(first[0:4], first[4]),
        [pair_out] * 3 + packed_outs,
        [limits] + back_scratch,
        back_flops + 2 * SEQ * D * 1024,
        token,
    )
    *ffn_parts, cross_arrived, self_other, token = hold(
        *ffn_parts, cross_arrived, self_other, token
    )
    self_other = to_core(self_other)
    ffn_total, cross_keep, *sends, self_keep, self_send = simple(
        slot_3,
        "slot_3",
        meta,
        [ffn_keep, *ffn_parts, cross_keep, cross_arrived, self_own, self_other],
        rows_out(128, 64, 192, 192, 192, 256, 256),
    )
    ffn_total, self_send, grad_mem, token = hold(ffn_total, self_send, grad_mem, token)
    mem_other = to_core(grad_mem)
    self_arrived = to_y(self_send)
    messages = to_z(sends)
    *self_grads_second, token = call(
        self_back_second,
        "self_back_second",
        [meta_in, (g2_low, "tiles")]
        + small(rank, limit)
        + now(ws2, ws3)
        + head_inputs(second_heads[0:4], second_heads[4]),
        [pair_out] * 3,
        [limits] + back_scratch,
        back_flops,
        token,
    )
    *messages, self_arrived, mem_other, token = hold(*messages, self_arrived, mem_other, token)
    ffn_half, cross_total, self_keep, *sends = simple(
        slot_4,
        "slot_4",
        meta,
        [ffn_total, *messages, cross_keep, self_keep, self_arrived],
        rows_out(512, 64, 64, 128, 128, 128),
    )
    cross_total, ffn_half, token = hold(cross_total, ffn_half, token)
    messages = to_z(sends)
    ffn_arrived = to_y(ffn_half)
    placed_q, placed_c, gq, gc, gln_self, token = call(
        self_back_finish,
        "self_back_finish",
        [meta_in, (g2_low, "tiles"), (query_stream, "tiles_row"), (content_stream, "tiles_row")]
        + small(norms)
        + now(ws0, ws1, ws2, ws3)
        + [(x, "tiles") for x in self_grads + self_grads_second],
        [stream_out(f32, True), stream_out(f32, True), stream_out(bf16), stream_out(bf16), grads_ln],
        [pltpu.VMEM((32, D), f32)],
        2 * SEQ * D * 1536,
        token,
    )
    gln = jnp.concatenate([gln_self[0:4], gln_cross[0:2], gln_ffn[0:2]], axis=0)
    gln_other = to_core(gln)
    *messages, ffn_arrived, gln_ffn = hold(*messages, ffn_arrived, gln_ffn)
    last_send, cross_half = simple(
        slot_5,
        "slot_5",
        meta,
        [self_keep, cross_total, *messages, gln, gln_other],
        [((GROUP, 80, D), bf16), ((256, D), bf16)],
    )
    groups = None
    if row_count > GROUP:
        groups = [list(range(r, r + GROUP)) for r in range(0, row_count, GROUP)]
    def gather(x):
        return lax.all_to_all(x, "rows", 0, 0, axis_index_groups=groups)

    last_parts = gather(last_send)
    cross_arrived = to_y(cross_half)
    def over_groups(totals):
        if row_count == GROUP:
            return totals
        groups = [list(range(r, row_count, GROUP)) for r in range(GROUP)]
        return lax.psum(totals, "rows", axis_index_groups=groups)

    gq_both, gc_both = both_rows([placed_q, placed_c], [to_core(gq), to_core(gc)], "place_late")

    grad_ffn_in, grad_ffn_out = simple(
        unpack_ffn,
        "unpack_ffn",
        meta,
        [ffn_half, ffn_arrived],
        [((D, D), f32)] * 2,
        [pltpu.VMEM((2 * D, D), bf16)],
    )
    attention_outs = [((512, 128), f32)] * 3 + [((128, 512), f32)]
    out_both, grad_mem_both = both_rows(
        [placed_output, placed_mem], [output_other, mem_other], "place_early"
    )
    cross_arrived, gq_both, out_both, grad_ffn_in = hold(
        cross_arrived, gq_both, out_both, grad_ffn_in
    )
    *parts, gln = simple(
        unpack_rest,
        "unpack_rest",
        meta,
        [cross_half, cross_arrived, last_parts],
        attention_outs * 2 + [((8, D), f32)],
        [pltpu.VMEM((D, D), bf16)],
    )
    grad_cross_parts, grad_self_parts = parts[:4], parts[4:]
    grad_ffn_in, grad_ffn_out, grad_cross_parts, grad_self_parts, gln = over_groups(
        (grad_ffn_in, grad_ffn_out, grad_cross_parts, grad_self_parts, gln)
    )
    return (
        out_both,
        gq_both,
        gc_both,
        grad_mem_both,
        gln[0],
        gln[1],
        gln[2],
        gln[3],
        *grad_self_parts,
        gln[4],
        gln[5],
        *grad_cross_parts,
        gln[6],
        gln[7],
        grad_ffn_in,
        grad_ffn_out,
    )


def solution(mesh):
    assert mesh.shape["heads"] == 4
    row_spec = P("rows", None)
    flat = P("rows")
    by_column = P(None, "heads")
    by_row = P("heads", None)
    attention = (by_column, by_column, by_column, by_row)
    in_specs = (
        (row_spec,) * 3
        + (flat,) * 5
        + (P(),) * 4
        + attention
        + (P(),) * 2
        + attention
        + (P(),) * 2
        + (by_column, by_row, row_spec)
    )
    out_specs = (
        (row_spec,) * 4
        + (P(),) * 4
        + attention
        + (P(),) * 2
        + attention
        + (P(),) * 2
        + (by_column, by_row)
    )
    return jax.shard_map(shards, mesh=mesh, in_specs=in_specs, out_specs=out_specs, check_vma=False)
```

```python
import functools

import jax
import jax.numpy as jnp
from jax import lax
from jax.experimental import pallas as pl
from jax.experimental.pallas import tpu as pltpu
from jax.sharding import PartitionSpec as P

HEAD_DIM = 64
SEQ = 1024
DOCS = 8
D = 512
TILE = 256
TILES = SEQ // TILE
FAST_Q = 256
FAST_K = 208
LONG_Q = 128
LONG_K = 640

norm_eps = 1e-05
masked_score = -1e30
hidden_rank = 1e6
gelu_root = 0.7978845608028654
gelu_cube = 0.044715

f32 = jnp.float32
bf16 = jnp.bfloat16


def dot(a, b):
    return lax.dot_general(a, b, (((1,), (0,)), ((), ())), preferred_element_type=f32)


def dot_nt(a, b):
    return lax.dot_general(a, b, (((1,), (1,)), ((), ())), preferred_element_type=f32)


def dot_tn(a, b):
    return lax.dot_general(a, b, (((0,), (0,)), ((), ())), preferred_element_type=f32)


def lanes(parts):
    return jnp.concatenate(parts, axis=1)


NORM_ROWS = 32


def layer_norm(values, gain, shift):
    def piece(part):
        part = part.astype(f32)
        centre = part - jnp.mean(part, axis=-1, keepdims=True)
        spread = jnp.mean(centre * centre, axis=-1, keepdims=True)
        return (centre * lax.rsqrt(spread + norm_eps) * gain + shift).astype(bf16)

    return by_pieces(piece, NORM_ROWS, 0, values)


def eight_rows(values):
    return sum(values[8 * i : 8 * i + 8] for i in range(1, values.shape[0] // 8)) + values[0:8]


def norm_backward(values, gain, grad, sums_ref, first):
    sums = []

    def piece(part, grad_part):
        part = part.astype(f32)
        centre = part - jnp.mean(part, axis=-1, keepdims=True)
        spread = jnp.mean(centre * centre, axis=-1, keepdims=True)
        scale = lax.rsqrt(spread + norm_eps)
        xhat = centre * scale
        eg = grad_part * gain
        mean_eg = jnp.mean(eg, axis=-1, keepdims=True)
        mean_egx = jnp.mean(eg * xhat, axis=-1, keepdims=True)
        sums.append((eight_rows(grad_part * xhat), eight_rows(grad_part)))
        return scale * (eg - mean_eg - xhat * mean_egx)

    result = by_pieces(piece, NORM_ROWS, 0, values, grad)
    for n, parts in enumerate(zip(*sums)):
        sums_ref[first + 8 * n : first + 8 * n + 8, :] += sum(parts[1:], parts[0])
    return result


def add_sums(sums_ref, gln_ref, count):
    gln_ref[...] = jnp.zeros_like(gln_ref)
    for n in range(count):
        gln_ref[n : n + 1, :] = jnp.sum(sums_ref[8 * n : 8 * n + 8, :], axis=0, keepdims=True)


def by_pieces(work, size, axis, *arrays):
    count = arrays[0].shape[axis] // size
    pieces = []
    for i in range(count):
        cut = (slice(size * i, size * i + size),)
        cut = cut if axis == 0 else (slice(None),) + cut
        pieces.append(work(*[x[cut] for x in arrays]))
    if not isinstance(pieces[0], tuple):
        return jnp.concatenate(pieces, axis=axis)
    return tuple(jnp.concatenate(parts, axis=axis) for parts in zip(*pieces))


def rows_of(i, size=TILE):
    return pl.ds(pl.multiple_of(i * size, size), size)


def w_query(ref):
    return ref[:, 0:128]


def w_key(ref):
    return ref[:, 128:256]


def w_value(ref):
    return ref[:, 256:384]


def w_out(ref):
    return lanes([ref[128 * j : 128 * j + 128, 384:512] for j in range(4)])


def half_masks():
    place = lax.broadcasted_iota(jnp.int32, (1, 128), 1)
    low = jnp.where(place < HEAD_DIM, 1.0, 0.0).astype(f32)
    return (low.astype(bf16), (1.0 - low).astype(bf16))


def doc_bounds(meta, d, source):
    base = 17 if source else 1
    return meta[base + d], meta[base + 8 + d]


def window_of(first, limit):
    return pl.multiple_of(jnp.minimum((first // 16) * 16, limit), 16)


def key_bias(ks, ke, k0, width):
    place = k0 + lax.broadcasted_iota(jnp.int32, (width, 128), 0)
    return jnp.where((place >= ks) & (place < ke), 0.0, masked_score)


def make_bias(rank_ref, limit_ref, ks, ke, q0, k0, span, width):
    if rank_ref is None:
        return lanes([key_bias(ks, ke, k0, width)] * (span // 128))
    place = k0 + lax.broadcasted_iota(jnp.int32, (width, 128), 0)
    ranks = rank_ref[pl.ds(k0, width), :]
    ranks = jnp.where((place < ks + 2) & (ranks < hidden_rank), -1.0, ranks)
    ranks = jnp.where((place >= ks) & (place < ke), ranks, hidden_rank)
    limits = jnp.broadcast_to(limit_ref[...], (8, SEQ))
    limits = pltpu.roll(limits, lax.rem(SEQ - q0, SEQ), 1)[0:1, 0:span]
    row = k0 + lax.broadcasted_iota(jnp.int32, (width, span), 0)
    column = q0 + lax.broadcasted_iota(jnp.int32, (width, span), 1)
    seen = (lanes([ranks] * (span // 128)) < limits) & (row != column)
    return jnp.where(seen, 0.0, masked_score)


TOGETHER = 4
STEPS = DOCS // TOGETHER


LAG = 2


def interleave(items):
    items = [list(phases) for phases in items]
    depth = max(len(phases) for phases in items)
    results = [None] * len(items)
    for tick in range(len(items) + LAG * (depth - 1)):
        for phase in range(depth):
            n = tick - LAG * phase
            if 0 <= n < len(items) and phase < len(items[n]):
                run = items[n][phase]
                results[n] = run() if phase == 0 else run(results[n])
    return results


def by_halves(pairs, phases):
    shared = [{} for _ in range(pairs)]
    return [phases(n, a, shared[n]) for n in range(pairs) for a in range(2)]


def is_fast(meta, cross):
    return meta[34 if cross else 33] == 1


def both_heads(x, masks):
    return jnp.concatenate([x * masks[0], x * masks[1]], axis=0)


def pair_scores(queries, keys, masks):
    return dot_nt(both_heads(keys, masks), queries)


def raised(scores, bias):
    def piece(part, bias_part):
        part = part + bias_part
        return jnp.exp((part - jnp.max(part, axis=0, keepdims=True)).astype(bf16))

    return by_pieces(piece, 128, 1, scores, bias)


def weighted_values(values, parts):
    width = values.shape[1]
    mixed = []
    shares = []
    for a, part in enumerate(parts):
        rows = jnp.concatenate([values[64 * a : 64 * a + 64], jnp.ones((16, width), bf16)], axis=0)
        sums = dot(rows, part)
        share = 1.0 / sums[64:65]
        mixed.append(sums[:64] * share)
        shares.append(part * share.astype(bf16))
    return jnp.concatenate(mixed, axis=0).astype(bf16), shares


def pair_gradient(rows, parts):
    across = jnp.transpose(rows)
    halves = [dot(across[64 * a : 64 * a + 64], part) for a, part in enumerate(parts)]
    return jnp.transpose((jnp.concatenate(halves, axis=0) * HEAD_DIM**-0.5).astype(bf16))


def for_docs(meta, cross, run, before, after):
    @pl.when(is_fast(meta, cross))
    def _():
        def step(i, carry):
            slot = lax.rem(i, 2)
            before(i, slot)
            items = []
            for place in range(TOGETHER):
                d = TOGETHER * i + place
                ts, te = doc_bounds(meta, d, False)
                ks, ke = doc_bounds(meta, d, cross)
                q0 = window_of(ts, SEQ - FAST_Q)
                k0 = window_of(ks, SEQ - FAST_K)
                items += run(d, slot, place, q0, k0, FAST_Q, FAST_K, ts, te, ks, ke, True)
            interleave(items)
            after(i, slot)
            return carry

        lax.fori_loop(0, STEPS, step, 0)

    @pl.when(jnp.logical_not(is_fast(meta, cross)))
    def _():
        def doc(d, carry):
            ts, te = doc_bounds(meta, d, False)
            ks, ke = doc_bounds(meta, d, cross)
            base = (ts // 16) * 16
            k0 = window_of(ks, SEQ - LONG_K)

            def chunk(i, carry):
                lower = base + i * LONG_Q
                q0 = pl.multiple_of(jnp.minimum(lower, SEQ - LONG_Q), 16)
                low = jnp.maximum(ts, lower)
                high = jnp.minimum(te, lower + LONG_Q)
                interleave(run(d, None, None, q0, k0, LONG_Q, LONG_K, low, high, ks, ke, False))
                return carry

            return lax.fori_loop(0, (te - base + LONG_Q - 1) // LONG_Q, chunk, carry)

        lax.fori_loop(0, DOCS, doc, 0)


def attend_docs(meta, cross, rank_ref, limit_ref, halves, p_ref, p_buf, p_sem):
    pairs = 2 * len(halves)
    masks = half_masks()

    def save(i, slot):
        return pltpu.make_async_copy(p_buf.at[slot], p_ref.at[pl.ds(TOGETHER * i, TOGETHER)], p_sem.at[slot])

    def before(i, slot):
        @pl.when(i >= 2)
        def _():
            save(i - 2, slot).wait()

    def after(i, slot):
        save(i, slot).start()

    def run(d, slot, place, q0, k0, span, width, low, high, ks, ke, fast):
        bias = make_bias(rank_ref, limit_ref, ks, ke, q0, k0, span, width)
        row = q0 + lax.broadcasted_iota(jnp.int32, (span, 128), 0)
        inside = (row >= low) & (row < high)

        def phases(n):
            q_ref, k_ref, v_ref, mixed_ref = halves[n // 2]
            cols = slice(128 * (n % 2), 128 * (n % 2) + 128)

            def score():
                return pair_scores(q_ref[pl.ds(q0, span), cols], k_ref[pl.ds(k0, width), cols], masks)

            def weigh(scores):
                return [raised(scores[width * a : width * a + width], bias) for a in range(2)]

            def mix(parts):
                values = jnp.transpose(v_ref[pl.ds(k0, width), cols])
                mixed, parts = weighted_values(values, parts)
                if fast:
                    for a in range(2):
                        p_buf[slot, place, 2 * n + a] = parts[a]
                mixed = jnp.transpose(mixed).astype(f32)
                old = mixed_ref[pl.ds(q0, span), cols].astype(f32)
                mixed_ref[pl.ds(q0, span), cols] = jnp.where(inside, mixed, old).astype(bf16)

            return score, weigh, mix

        return [phases(n) for n in range(pairs)]

    for_docs(meta, cross, run, before, after)

    @pl.when(is_fast(meta, cross))
    def _():
        for i in range(STEPS - 2, STEPS):
            save(i, i % 2).wait()


def load_step(load, i, slot):
    p_ref, p_buf, p_sem = load
    return pltpu.make_async_copy(p_ref.at[pl.ds(TOGETHER * i, TOGETHER)], p_buf.at[slot], p_sem.at[slot])


def start_load(meta, cross, load):
    @pl.when(is_fast(meta, cross))
    def _():
        load_step(load, 0, 0).start()


def attend_docs_back(
    meta, cross, rank_ref, limit_ref, q_ref, k_ref, v_ref, mixed_ref, dm_ref,
    dq_ref, dk_ref, dv_ref, load,
):
    pairs = q_ref.shape[1] // 128
    masks = half_masks()
    p_buf = load[1]

    def before(i, slot):
        @pl.when(i + 1 < STEPS)
        def _():
            load_step(load, i + 1, 1 - slot).start()

        load_step(load, i, slot).wait()

    def after(i, slot):
        pass

    def run(d, slot, place, q0, k0, span, width, low, high, ks, ke, fast):
        row = q0 + lax.broadcasted_iota(jnp.int32, (span, 128), 0)
        inside = jnp.where((row >= low) & (row < high), 1.0, 0.0).astype(bf16)
        ones = jnp.ones((width, 128), bf16)
        if not fast:
            bias = make_bias(rank_ref, limit_ref, ks, ke, q0, k0, span, width)

        def phases(n):
            cols = slice(128 * n, 128 * n + 128)

            def differ():
                values = v_ref[pl.ds(k0, width), cols]
                mixed = mixed_ref[pl.ds(q0, span), cols]
                grad = dm_ref[pl.ds(q0, span), cols] * inside
                left = lanes([grad, -(grad * mixed)])
                right = both_heads(lanes([values, ones]), [lanes([m, m]) for m in masks])
                return grad, dot_nt(right, left)

            def slope(state):
                grad, delta = state
                if fast:
                    parts = [p_buf[slot, place, 2 * n + a] for a in range(2)]
                else:
                    queries = q_ref[pl.ds(q0, span), cols]
                    keys = k_ref[pl.ds(k0, width), cols]
                    scores = pair_scores(queries, keys, masks)
                    parts = [raised(scores[width * a : width * a + width], bias) for a in range(2)]
                    parts = weighted_values(jnp.transpose(v_ref[pl.ds(k0, width), cols]), parts)[1]
                slopes = [
                    by_pieces(
                        lambda part, change: part * change.astype(bf16),
                        16,
                        0,
                        parts[a],
                        delta[width * a : width * a + width],
                    )
                    for a in range(2)
                ]
                return grad, parts, slopes

            def spread(state):
                grad, parts, slopes = state
                queries = q_ref[pl.ds(q0, span), cols]
                dk = dv = None
                for a in range(2):
                    dk_a = dot(slopes[a], queries * masks[a])
                    dv_a = dot(parts[a], grad * masks[a])
                    dk = dk_a if dk is None else dk + dk_a
                    dv = dv_a if dv is None else dv + dv_a
                dq = pair_gradient(k_ref[pl.ds(k0, width), cols], slopes)
                dq_ref[pl.ds(q0, span), cols] += dq.astype(f32)
                dk_ref[pl.ds(k0, width), cols] += dk
                dv_ref[pl.ds(k0, width), cols] += dv

            return differ, slope, spread

        return [phases(n) for n in range(pairs)]

    for_docs(meta, cross, run, before, after)


def spread_ranks(rank_row_ref, rank_ref):
    rank_ref[...] = jnp.transpose(jnp.broadcast_to(rank_row_ref[...], (128, SEQ)))


def prepare(
    core, seg_ref, src_ref, rank_ref, limit_ref, pad_ref,
    n0, n1, n2, n3, n4, n5, n6, n7, sq, sk, sv, so, cq, ck, cv, co,
    meta_ref, ranks_ref, limits_ref, norms_ref, ws_ref, wc_ref,
):
    meta_ref[0] = core[0]
    meta_ref[35] = core[1]
    for base, ref in ((1, seg_ref), (17, src_ref)):
        ids = ref[0]
        meta_ref[base] = 0
        meta_ref[base + 15] = SEQ
        for d in range(1, DOCS):
            cut = jnp.sum(jnp.where(ids < d, 1.0, 0.0)).astype(jnp.int32)
            meta_ref[base + d] = cut
            meta_ref[base + 7 + d] = cut
    for place, base in ((33, 1), (34, 17)):
        fast = jnp.int32(1)
        for d in range(DOCS):
            q0 = window_of(meta_ref[1 + d], SEQ - FAST_Q)
            k0 = window_of(meta_ref[base + d], SEQ - FAST_K)
            fits = (meta_ref[9 + d] - q0 <= FAST_Q) & (meta_ref[base + 8 + d] - k0 <= FAST_K)
            fast = fast & fits.astype(jnp.int32)
        meta_ref[place] = fast
    ranks = jnp.where(pad_ref[0] != 0, hidden_rank, rank_ref[0].astype(f32))
    limits = limit_ref[0].astype(f32)
    for i in range(8):
        ranks_ref[0:1, 128 * i : 128 * i + 128] = ranks[i : i + 1]
        limits_ref[0:1, 128 * i : 128 * i + 128] = limits[i : i + 1]
    for i, ref in enumerate((n0, n1, n2, n3, n4, n5, n6, n7)):
        norms_ref[i : i + 1, :] = ref[...]
    for to, parts, out in ((ws_ref, (sq, sk, sv), so), (wc_ref, (cq, ck, cv), co)):
        for i, part in enumerate(parts):
            to[:, 128 * i : 128 * i + 128] = part[...]
        for j in range(4):
            to[128 * j : 128 * j + 128, 384:512] = out[:, 128 * j : 128 * j + 128]


def self_first(
    meta, io, xq_ref, xc_ref, rank_row_ref, limit_ref, norms_ref, w0_ref, w1_ref,
    nq_ref, nc_ref, q_ref, k_ref, v_ref, mixed_ref, p_ref, rank_ref, p_buf, p_sem,
):

    spread_ranks(rank_row_ref, rank_ref)
    wq = lanes([w_query(w0_ref), w_query(w1_ref)])
    wkv = lanes([w_key(w0_ref), w_key(w1_ref), w_value(w0_ref), w_value(w1_ref)])

    def tile(i, carry):
        rows = rows_of(i)
        io.wait_rows(i)
        nq = layer_norm(xq_ref[rows, :], norms_ref[0:1], norms_ref[1:2])
        nc = layer_norm(xc_ref[rows, :], norms_ref[2:3], norms_ref[3:4])
        nq_ref[rows, :] = nq
        nc_ref[rows, :] = nc
        q_ref[rows, :] = (dot(nq, wq) * (HEAD_DIM**-0.5)).astype(bf16)
        kv = dot(nc, wkv).astype(bf16)
        k_ref[rows, :] = kv[:, :256]
        v_ref[rows, :] = kv[:, 256:]
        return carry

    lax.fori_loop(0, TILES, tile, 0)

    for ref in (nq_ref, nc_ref, q_ref, k_ref, v_ref):
        io.send(ref)
    attend_docs(meta, False, rank_ref, limit_ref, [(q_ref, k_ref, v_ref, mixed_ref)], p_ref, p_buf, p_sem)


def self_second(
    meta, io, xq_ref, nq_ref, nc_ref, rank_row_ref, limit_ref, norms_ref, w0_ref, w1_ref, w2_ref, w3_ref,
    mixed_first_ref,
    q_ref, k_ref, v_ref, mixed_ref, p_ref, second_ref, ncross_ref, rank_ref, p_buf, p_sem,
):

    spread_ranks(rank_row_ref, rank_ref)
    wq = lanes([w_query(w2_ref), w_query(w3_ref)])
    wkv = lanes([w_key(w2_ref), w_key(w3_ref), w_value(w2_ref), w_value(w3_ref)])

    def tile(i, carry):
        rows = rows_of(i)
        io.wait_rows(i)
        q_ref[rows, :] = (dot(nq_ref[rows, :], wq) * (HEAD_DIM**-0.5)).astype(bf16)
        kv = dot(nc_ref[rows, :], wkv).astype(bf16)
        k_ref[rows, :] = kv[:, :256]
        v_ref[rows, :] = kv[:, 256:]
        return carry

    lax.fori_loop(0, TILES, tile, 0)

    for ref in (q_ref, k_ref, v_ref):
        io.send(ref)
    attend_docs(meta, False, rank_ref, limit_ref, [(q_ref, k_ref, v_ref, mixed_ref)], p_ref, p_buf, p_sem)

    io.send(mixed_ref)
    io.wait("late")
    out_first = jnp.concatenate([w_out(w0_ref), w_out(w1_ref)], axis=0)
    out_second = jnp.concatenate([w_out(w2_ref), w_out(w3_ref)], axis=0)

    def tile(i, carry):
        rows = rows_of(i)
        branch = dot(mixed_first_ref[rows, :], out_first) + dot(mixed_ref[rows, :], out_second)
        second = xq_ref[rows, :].astype(f32) + branch
        second_ref[rows, :] = second.astype(bf16)
        io.send(second_ref, rows)
        ncross_ref[rows, :] = layer_norm(second, norms_ref[4:5], norms_ref[5:6])
        io.send(ncross_ref, rows)
        return carry

    lax.fori_loop(0, TILES, tile, 0)


def project_cross(io, ncross_ref, memory_ref, weights, q_ref, k_ref, v_ref):
    wq = lanes([w_query(w) for w in weights])
    wkv = lanes([w_key(w) for w in weights] + [w_value(w) for w in weights])

    def tile(i, carry):
        rows = rows_of(i)
        io.wait_rows(i)
        q_ref[rows, :] = (dot(ncross_ref[rows, :], wq) * (HEAD_DIM**-0.5)).astype(bf16)
        kv = dot(memory_ref[rows, :], wkv).astype(bf16)
        k_ref[rows, :] = kv[:, :256]
        v_ref[rows, :] = kv[:, 256:]
        return carry

    lax.fori_loop(0, TILES, tile, 0)
    for ref in (q_ref, k_ref, v_ref):
        io.send(ref)


def cross_first(
    meta, io, ncross_ref, memory_ref, w0_ref, w1_ref,
    q_ref, k_ref, v_ref, mixed_ref, p_ref, p_buf, p_sem,
):
    project_cross(io, ncross_ref, memory_ref, (w0_ref, w1_ref), q_ref, k_ref, v_ref)
    attend_docs(meta, True, None, None, [(q_ref, k_ref, v_ref, mixed_ref)], p_ref, p_buf, p_sem)


def cross_second(
    meta, io, second_ref, ncross_ref, memory_ref, norms_ref, w0_ref, w1_ref, w2_ref, w3_ref,
    mixed_first_ref,
    q_ref, k_ref, v_ref, mixed_ref, p_ref, third_ref, nffn_ref, p_buf, p_sem,
):
    project_cross(io, ncross_ref, memory_ref, (w2_ref, w3_ref), q_ref, k_ref, v_ref)
    attend_docs(meta, True, None, None, [(q_ref, k_ref, v_ref, mixed_ref)], p_ref, p_buf, p_sem)
    io.send(mixed_ref)
    io.wait("late")
    out_first = jnp.concatenate([w_out(w0_ref), w_out(w1_ref)], axis=0)
    out_second = jnp.concatenate([w_out(w2_ref), w_out(w3_ref)], axis=0)

    def tile(i, carry):
        rows = rows_of(i)
        branch = dot(mixed_first_ref[rows, :], out_first) + dot(mixed_ref[rows, :], out_second)
        third = second_ref[rows, :].astype(f32) + branch
        third_ref[rows, :] = third
        nffn_ref[rows, :] = layer_norm(third, norms_ref[6:7], norms_ref[7:8])
        return carry

    lax.fori_loop(0, TILES, tile, 0)


def ffn_both(
    meta, io, third_ref, nffn_ref, cot_ref, norms_ref, u0_ref, u1_ref, u2_ref, u3_ref,
    w0_ref, w1_ref, w2_ref, w3_ref,
    placed_ref, out_ref, g3_low_ref, gln_ref, own_ref, other_ref, hidden_ref, before_ref, sums_ref,
):
    sums_ref[...] = jnp.zeros_like(sums_ref)
    in_refs = (u0_ref, u1_ref, u2_ref, u3_ref)
    w_refs = (w0_ref, w1_ref, w2_ref, w3_ref)

    def tile(i, carry):
        rows = rows_of(i)
        io.wait_rows(i)
        nffn = nffn_ref[rows, :]
        cot = cot_ref[rows, :]
        outs = []
        grads = []

        def phases(g, c, group):
            w_in = in_refs[g]
            w_out_rows = w_refs[g]
            cols = slice(256 * c, 256 * c + 256)

            def enter():
                return dot(nffn, w_in[:, cols]), dot_nt(cot, w_out_rows[cols, :])

            def bend(state):
                def piece(x, grad_hidden):
                    square = x * x
                    argument = x * (gelu_root + (gelu_root * gelu_cube) * square)
                    half = 0.5 + 0.5 * jnp.tanh(argument.astype(bf16))
                    x = x.astype(bf16)
                    square = square.astype(bf16)
                    value = x * half
                    rise = 2.0 * gelu_root + (6.0 * gelu_root * gelu_cube) * square
                    slope = half + value * (1.0 - half) * rise
                    return value, grad_hidden.astype(bf16) * slope

                hidden, grad_before = by_pieces(piece, 32, 0, *state)
                if g < 2:
                    place = slice(512 * g + 256 * c, 512 * g + 256 * c + 256)
                    hidden_ref[rows, place] = hidden
                    before_ref[rows, place] = grad_before
                group[c] = hidden, grad_before

            def leave(_):
                if c == 1:
                    outs.append(dot(lanes([group[0][0], group[1][0]]), w_out_rows[...]))

            def leave_back(_):
                if c == 1:
                    grads.append(dot_nt(lanes([group[0][1], group[1][1]]), w_in[...]))

            return enter, bend, leave, leave_back

        interleave(by_halves(4, phases))
        third = third_ref[rows, :]
        result = (third + ((outs[0] + outs[1]) + (outs[2] + outs[3]))).astype(bf16)
        out_ref[rows, :] = result
        placed_ref[rows, :] = result
        grad_normed = (grads[0] + grads[1]) + (grads[2] + grads[3])
        grad_norm = norm_backward(third, norms_ref[6:7], grad_normed, sums_ref, 0)
        g3_low_ref[rows, :] = (cot.astype(f32) + grad_norm).astype(bf16)
        for ref in (out_ref, placed_ref, g3_low_ref):
            io.send(ref, rows)
        return carry

    lax.fori_loop(0, TILES, tile, 0)
    add_sums(sums_ref, gln_ref, 2)
    part = dot_tn(nffn_ref[...], before_ref[...])
    own_ref[0:512, :] = part[:, 0:512].astype(bf16)
    other_ref[0:512, :] = part[:, 512:1024].astype(bf16)
    io.send(own_ref, pl.ds(0, 512))
    io.send(other_ref, pl.ds(0, 512))
    part = dot_tn(hidden_ref[...], cot_ref[...])
    own_ref[512:1024, :] = part[0:512].astype(bf16)
    other_ref[512:1024, :] = part[512:1024].astype(bf16)
    io.send(own_ref, pl.ds(512, 512))
    io.send(other_ref, pl.ds(512, 512))


def back_start(io, g_ref, mixed_ref, w_refs, dm_ref, dq_ref, dk_ref, dv_ref):
    out_rows = jnp.concatenate([w_out(w) for w in w_refs], axis=0)

    def tile(i, carry):
        rows = rows_of(i)
        io.wait_rows(i)
        dm_ref[rows, :] = dot_nt(g_ref[rows, :], out_rows).astype(bf16)
        zeros = jnp.zeros((TILE, 256), f32)
        dq_ref[rows, :] = zeros
        dk_ref[rows, :] = zeros
        dv_ref[rows, :] = zeros
        return carry

    lax.fori_loop(0, TILES, tile, 0)


def attention_back_first(
    cross, meta, io, g_ref, nq_ref, nkv_ref, rank_row_ref, limit_ref, w0_ref, w1_ref,
    q_ref, k_ref, v_ref, mixed_ref, p_ref,
    dq_ref, dk_ref, dv_ref, own_ref, other_ref,
    rank_ref, dm_ref, dqs_ref, dks_ref, dvs_ref, p_buf, p_sem,
):
    load = (p_ref, p_buf, p_sem)
    start_load(meta, cross, load)
    if not cross:
        spread_ranks(rank_row_ref, rank_ref)
    back_start(io, g_ref, mixed_ref, (w0_ref, w1_ref), dm_ref, dqs_ref, dks_ref, dvs_ref)

    io.wait("soon")
    attend_docs_back(
        meta, cross, None if cross else rank_ref, limit_ref, q_ref, k_ref, v_ref, mixed_ref,
        dm_ref, dqs_ref, dks_ref, dvs_ref, load,
    )

    dq_ref[...] = dqs_ref[...].astype(bf16)
    dk_ref[...] = dks_ref[...].astype(bf16)
    dv_ref[...] = dvs_ref[...].astype(bf16)
    for ref in (dq_ref, dk_ref, dv_ref):
        io.send(ref)
    io.wait("late")
    nq = nq_ref[...]
    nkv = nkv_ref[...]
    kv = dot_tn(nkv, lanes([dk_ref[...], dv_ref[...]]))
    for n, part in enumerate((dot_tn(nq, dq_ref[...]), kv[:, 0:256], kv[:, 256:512])):
        own_ref[:, 128 * n : 128 * n + 128] = part[:, :128].astype(bf16)
        other_ref[:, 128 * n : 128 * n + 128] = part[:, 128:].astype(bf16)
    part = dot_tn(mixed_ref[...], g_ref[...])
    for j in range(4):
        rows = slice(128 * j, 128 * j + 128)
        own_ref[rows, 384:512] = part[:128, rows].astype(bf16)
        other_ref[rows, 384:512] = part[128:, rows].astype(bf16)


def back_second_docs(
    cross, meta, io, g_ref, rank_row_ref, limit_ref, w_refs, q_ref, k_ref, v_ref, mixed_ref, p_ref,
    rank_ref, dm_ref, dqs_ref, dks_ref, dvs_ref, p_buf, p_sem,
):
    load = (p_ref, p_buf, p_sem)
    start_load(meta, cross, load)
    if not cross:
        spread_ranks(rank_row_ref, rank_ref)
    back_start(io, g_ref, mixed_ref, w_refs, dm_ref, dqs_ref, dks_ref, dvs_ref)

    io.wait("soon")
    attend_docs_back(
        meta, cross, None if cross else rank_ref, limit_ref, q_ref, k_ref, v_ref, mixed_ref,
        dm_ref, dqs_ref, dks_ref, dvs_ref, load,
    )


def stream_grads(rows, first, second, firsts, seconds):
    dq, dk, dv = first
    dq2, dk2, dv2 = (ref[rows, :].astype(bf16) for ref in second)
    w0, w1 = firsts
    w2, w3 = seconds
    grad_q = dot_nt(dq[rows, :], lanes([w_query(w0), w_query(w1)])) + dot_nt(
        dq2, lanes([w_query(w2), w_query(w3)])
    )
    kv = lanes([dk[rows, :], dv[rows, :]])
    kv2 = lanes([dk2, dv2])
    grad_kv = dot_nt(kv, lanes([w_key(w0), w_key(w1), w_value(w0), w_value(w1)])) + dot_nt(
        kv2, lanes([w_key(w2), w_key(w3), w_value(w2), w_value(w3)])
    )
    return grad_q, grad_kv


def cross_back_second(
    meta, io, g_low_ref, second_ref, norms_ref, w0_ref, w1_ref, w2_ref, w3_ref,
    dq_ref, dk_ref, dv_ref, q_ref, k_ref, v_ref, mixed_ref, p_ref,
    g2_low_ref, placed_ref, gmem_ref, gln_ref,
    dm_ref, dqs_ref, dks_ref, dvs_ref, p_buf, p_sem, sums_ref,
):
    back_second_docs(
        True, meta, io, g_low_ref, None, None, (w2_ref, w3_ref), q_ref, k_ref, v_ref, mixed_ref, p_ref,
        None, dm_ref, dqs_ref, dks_ref, dvs_ref, p_buf, p_sem,
    )

    io.wait("late")
    sums_ref[...] = jnp.zeros_like(sums_ref)

    def tile(i, carry):
        rows = rows_of(i)
        grad_q, grad_kv = stream_grads(
            rows,
            (dq_ref, dk_ref, dv_ref),
            (dqs_ref, dks_ref, dvs_ref),
            (w0_ref, w1_ref),
            (w2_ref, w3_ref),
        )
        low_kv = grad_kv.astype(bf16)
        gmem_ref[rows, :] = low_kv
        placed_ref[rows, :] = low_kv.astype(f32)
        io.send(gmem_ref, rows)
        io.send(placed_ref, rows)
        grad_norm = norm_backward(second_ref[rows, :], norms_ref[4:5], grad_q, sums_ref, 0)
        g2_low_ref[rows, :] = (g_low_ref[rows, :].astype(f32) + grad_norm).astype(bf16)
        io.send(g2_low_ref, rows)
        return carry

    lax.fori_loop(0, TILES, tile, 0)
    add_sums(sums_ref, gln_ref, 2)


def self_back_second(
    meta, io, g_low_ref, rank_row_ref, limit_ref, w2_ref, w3_ref,
    q_ref, k_ref, v_ref, mixed_ref, p_ref,
    dq_ref, dk_ref, dv_ref,
    rank_ref, dm_ref, dqs_ref, dks_ref, dvs_ref, p_buf, p_sem,
):
    back_second_docs(
        False, meta, io, g_low_ref, rank_row_ref, limit_ref, (w2_ref, w3_ref), q_ref, k_ref, v_ref,
        mixed_ref, p_ref, rank_ref, dm_ref, dqs_ref, dks_ref, dvs_ref, p_buf, p_sem,
    )
    dq_ref[...] = dqs_ref[...].astype(bf16)
    dk_ref[...] = dks_ref[...].astype(bf16)
    dv_ref[...] = dvs_ref[...].astype(bf16)


def self_back_finish(
    meta, io, g_ref, xq_ref, xc_ref, norms_ref, w0_ref, w1_ref, w2_ref, w3_ref,
    dq_ref, dk_ref, dv_ref, dq2_ref, dk2_ref, dv2_ref,
    gq_ref, gc_ref, gln_ref, sums_ref,
):
    sums_ref[...] = jnp.zeros_like(sums_ref)

    def tile(i, carry):
        rows = rows_of(i)
        io.wait_rows(i)
        grad_q, grad_kv = stream_grads(
            rows,
            (dq_ref, dk_ref, dv_ref),
            (dq2_ref, dk2_ref, dv2_ref),
            (w0_ref, w1_ref),
            (w2_ref, w3_ref),
        )
        grad_norm = norm_backward(xq_ref[rows, :], norms_ref[0:1], grad_q, sums_ref, 0)
        low_q = (g_ref[rows, :].astype(f32) + grad_norm).astype(bf16)
        gq_ref[rows, :] = low_q
        grad_norm = norm_backward(xc_ref[rows, :], norms_ref[2:3], grad_kv, sums_ref, 16)
        low_c = grad_norm.astype(bf16)
        gc_ref[rows, :] = low_c
        return carry

    lax.fori_loop(0, TILES, tile, 0)
    add_sums(sums_ref, gln_ref, 4)


def place_rows(meta, *refs):
    count = len(refs) // 3
    for n in range(count):
        refs[2 * count + n][...] = refs[n][...].astype(refs[2 * count + n].dtype)


GROUP = 8


def position(meta):
    r = meta[35]
    return lax.rem(r, 2), r // 2


def place_both(meta, *refs):
    count = len(refs) // 3
    mine = pl.program_id(0) == meta[0]
    for n in range(count):
        own, other, both = refs[n], refs[count + n], refs[2 * count + n]

        @pl.when(mine)
        def _(own=own, both=both):
            both[...] = own[...].astype(both.dtype)

        @pl.when(jnp.logical_not(mine))
        def _(other=other, both=both):
            both[...] = other[...].astype(both.dtype)


def join(own, other, rows):
    return (own[rows, :].astype(f32) + other[rows, :].astype(f32)).astype(bf16)


def join_halves(meta, own, other, keep, send):
    y, _ = position(meta)
    size = keep.shape[0]
    keep[...] = join(own, other, rows_of(y, size))
    send[...] = join(own, other, rows_of(1 - y, size))


def join_chunks(meta, kept, arrived, keep, sends):
    _, z = position(meta)
    size = keep.shape[0]
    keep[...] = join(kept, arrived, rows_of(z, size))
    for s, (send, first) in enumerate(sends, 1):
        send[first : first + size, :] = join(kept, arrived, rows_of(z ^ s, size))


def add_up(kept, parts, first):
    size = kept.shape[0]
    total = kept[...].astype(f32)
    for part in parts:
        total = total + part[first : first + size, :].astype(f32)
    return total.astype(bf16)


def half_of(meta, total, parts, first, half):
    _, z = position(meta)
    size = total.shape[0]
    half[rows_of(z, size), :] = total[...]
    for s, part in enumerate(parts, 1):
        half[rows_of(z ^ s, size), :] = part[first : first + size, :]


def slot_1(meta, ffn_own, ffn_other, keep, send):
    join_halves(meta, ffn_own, ffn_other, keep, send)


def slot_2(
    meta, ffn_kept, ffn_arrived, cross_own, cross_other, ffn_keep, f1, f2, f3, keep, send
):
    join_chunks(meta, ffn_kept, ffn_arrived, ffn_keep, [(f1, 0), (f2, 0), (f3, 0)])
    join_halves(meta, cross_own, cross_other, keep, send)


def slot_3(
    meta, ffn_kept, f1, f2, f3, cross_kept, cross_arrived, self_own, self_other,
    ffn_total, cross_keep, m1, m2, m3, self_keep, self_send,
):
    join_halves(meta, self_own, self_other, self_keep, self_send)
    total = add_up(ffn_kept, (f1, f2, f3), 0)
    ffn_total[...] = total
    size = total.shape[0]
    join_chunks(meta, cross_kept, cross_arrived, cross_keep, [(m, size) for m in (m1, m2, m3)])
    for m in (m1, m2, m3):
        m[0:size, :] = total


def slot_4(
    meta, ffn_total, m1, m2, m3, cross_kept, self_kept, self_arrived,
    ffn_half, cross_total, self_keep, *sends,
):
    join_chunks(meta, self_kept, self_arrived, self_keep, [(send, 0) for send in sends])
    total = add_up(cross_kept, (m1, m2, m3), ffn_total.shape[0])
    cross_total[...] = total
    size = total.shape[0]
    for send in sends:
        send[size:, :] = total
    half_of(meta, ffn_total, (m1, m2, m3), 0, ffn_half)


def slot_5(meta, self_kept, cross_total, m1, m2, m3, gln_own, gln_other, send, cross_half):
    size = self_kept.shape[0]
    total = add_up(self_kept, (m1, m2, m3), 0)
    gln = gln_own[...] + gln_other[...]
    gln = jnp.concatenate([gln, jnp.zeros((8, D), f32)], axis=0).astype(bf16)
    for r in range(GROUP):
        send[r, 0:size, :] = total
        send[r, size : size + 16, :] = gln
    half_of(meta, cross_total, (m1, m2, m3), size, cross_half)


def unpack_attention(whole_ref, outs):
    for i in range(3):
        outs[i][...] = whole_ref[:, 128 * i : 128 * i + 128].astype(f32)
    for j in range(4):
        rows = slice(128 * j, 128 * j + 128)
        outs[3][:, rows] = whole_ref[rows, 384:512].astype(f32)


def unpack_ffn(meta, half, arrived, out_in, out_out, ffn_whole):
    y, _ = position(meta)
    ffn_whole[rows_of(y, 512), :] = half[...]
    ffn_whole[rows_of(1 - y, 512), :] = arrived[...]
    out_in[...] = ffn_whole[0:512, :].astype(f32)
    out_out[...] = ffn_whole[512:1024, :].astype(f32)


def unpack_rest(meta, cross_half, cross_arrived, parts, *refs):
    *outs, whole_ref = refs
    y, _ = position(meta)
    whole_ref[rows_of(y, 256), :] = cross_half[...]
    whole_ref[rows_of(1 - y, 256), :] = cross_arrived[...]
    unpack_attention(whole_ref, outs[0:4])
    size = parts.shape[1] - 16
    total = parts[0, size : size + 16, :].astype(f32)
    for r in range(1, GROUP):
        total = total + parts[r, size : size + 16, :].astype(f32)
    for n in range(8):
        outs[8 + n][...] = total[n : n + 1]
    for r in range(GROUP):
        first = size * (4 * (r % 2) + r // 2)
        whole_ref[first : first + size, :] = parts[r, 0:size, :]
    unpack_attention(whole_ref, outs[4:8])


def whole(shape):
    zeros = (0,) * len(shape)
    return pl.BlockSpec(shape, lambda d, meta: zeros)


def own_row(width):
    return pl.BlockSpec((SEQ, width), lambda d, meta: (meta[0], 0))


ANY = pl.BlockSpec(memory_space=pl.ANY)


def in_hbm(x):
    return pltpu.with_memory_space_constraint(x, pltpu.HBM)


probability_out = (pltpu.HBM((DOCS, 4, FAST_K, FAST_Q), bf16), None, ANY)
probability_scratch = [
    pltpu.VMEM((2, TOGETHER, 4, FAST_K, FAST_Q), bf16),
    pltpu.SemaphoreType.DMA((2,)),
]


class Copies:
    def __init__(self, meta):
        self.first = meta[0] * SEQ
        self.loads = {}
        self.tiles = []
        self.sends = []

    def load(self, stage, source, target, sems, own_row):
        if stage == "fresh":
            stage = "now"
        if stage == "tiles":
            first = self.first if own_row else 0
            self.tiles.append((source, target, sems, first))
            return
        if own_row:
            source = source.at[pl.ds(pl.multiple_of(self.first, SEQ), SEQ)]
        copy = pltpu.make_async_copy(source, target, sems[0].at[sems[1], 0])
        self.loads.setdefault(stage, []).append(copy)

    def tile(self, entry, i):
        source, target, (sems, b), first = entry
        rows = pl.ds(pl.multiple_of(first + i * TILE, TILE), TILE)
        return pltpu.make_async_copy(source.at[rows], target.at[rows_of(i)], sems.at[b, i])

    def start(self):
        for copy in self.loads.get("now", []):
            copy.start()
        for i in range(TILES):
            for entry in self.tiles:
                self.tile(entry, i).start()
        for stage in ("soon", "late"):
            for copy in self.loads.get(stage, []):
                copy.start()

    def wait(self, stage):
        for copy in self.loads.pop(stage, []):
            copy.wait()

    def wait_rows(self, i):
        for entry in self.tiles:
            self.tile(entry, i).wait()

    def result(self, source, target, sem, own_row):
        self.sends.append([source, target, sem, own_row, False])

    def send(self, ref, rows=None):
        for entry in self.sends:
            source, target, sem, own_row, _ = entry
            if source is ref:
                entry[4] = True
                first = self.first if own_row else 0
                if rows is None:
                    size = source.shape[0]
                else:
                    source = source.at[rows]
                    first, size = first + rows.start, rows.size
                if rows is not None or own_row:
                    target = target.at[pl.ds(pl.multiple_of(first, size), size)]
                pltpu.make_async_copy(source, target, sem).start()

    def finish(self):
        for stage in list(self.loads):
            self.wait(stage)
        for source, _, _, _, started in self.sends:
            if not started:
                self.send(source)
        for source, target, sem, own_row, _ in self.sends:
            if own_row:
                target = target.at[pl.ds(pl.multiple_of(self.first, SEQ), SEQ)]
            pltpu.make_async_copy(source, target, sem).wait()


def out(shape, dtype, own_row=False):
    return (shape, dtype, own_row)


def call(kernel, name, operands, outs, scratch, flops, token=None):
    arrays = [operands[0][0]]
    in_specs, out_specs, out_shapes = [], [], []
    buffers = []
    loads = []
    for n, (x, how) in enumerate(operands[1:]):
        if isinstance(how, str):
            stage, _, row = how.partition("_")
            shape = ((SEQ,) + x.shape[1:]) if row else x.shape
            loads.append((n, stage, len(buffers), bool(row)))
            buffers.append(pltpu.VMEM(shape, x.dtype))
            arrays.append(x if stage == "fresh" else in_hbm(x))
            in_specs.append(ANY)
        else:
            arrays.append(x)
            in_specs.append(how)
    results = []
    for n, (shape, dtype, how) in enumerate(outs):
        if isinstance(how, bool):
            results.append((n, len(buffers), how))
            buffers.append(pltpu.VMEM(shape, dtype))
            shape = ((2 * SEQ,) + shape[1:]) if how else shape
            out_shapes.append(pltpu.HBM(shape, dtype))
            out_specs.append(ANY)
        else:
            out_shapes.append(jax.ShapeDtypeStruct(shape, dtype) if dtype else shape)
            out_specs.append(how)
    n_in, n_out = len(in_specs), len(out_specs)
    if token is not None:
        arrays.append(token)
        in_specs.append(whole((8, 128)))
        out_specs.append(whole((8, 128)))
        out_shapes.append(jax.ShapeDtypeStruct((8, 128), f32))

    def body(meta, *refs):
        ins, refs = list(refs[:n_in]), refs[len(in_specs) - n_in + n_in :]
        results_out, refs = list(refs[:n_out]), refs[n_out:]
        if token is not None:
            token_out, refs = refs[0], refs[1:]
            token_out[...] = jnp.zeros_like(token_out)
        bufs, refs = refs[: len(buffers)], refs[len(buffers) :]
        rest = refs[: len(scratch)]
        copies = Copies(meta)
        if buffers:
            sems = refs[len(scratch)]
        for n, stage, b, row in loads:
            copies.load(stage, ins[n], bufs[b], (sems, b), row)
            ins[n] = bufs[b]
        for n, b, row in results:
            copies.result(bufs[b], results_out[n], sems.at[b, 0], row)
            results_out[n] = bufs[b]
        copies.start()
        copies.wait("now")
        if buffers:
            kernel(meta, copies, *ins, *results_out, *rest)
        else:
            kernel(meta, *ins, *results_out, *rest)
        copies.finish()

    moved = sum(x.size * x.dtype.itemsize for x in arrays[1:])
    sems = [pltpu.SemaphoreType.DMA((len(buffers), TILES))] if buffers else []
    return pl.pallas_call(
        body,
        name=name,
        grid_spec=pltpu.PrefetchScalarGridSpec(
            num_scalar_prefetch=1,
            grid=(1,),
            in_specs=in_specs,
            out_specs=out_specs,
            scratch_shapes=buffers + scratch + sems,
        ),
        out_shape=out_shapes,
        compiler_params=pltpu.CompilerParams(
            dimension_semantics=("arbitrary",), vmem_limit_bytes=40 * 1024 * 1024
        ),
        cost_estimate=pl.CostEstimate(
            flops=int(flops), bytes_accessed=int(moved), transcendentals=0
        ),
    )(*arrays)


def simple(kernel, name, meta, operands, outs, scratch=()):
    return pl.pallas_call(
        kernel,
        name=name,
        grid_spec=pltpu.PrefetchScalarGridSpec(
            num_scalar_prefetch=1,
            grid=(1,),
            in_specs=[whole(x.shape) for x in operands],
            out_specs=[whole(shape) for shape, _ in outs],
            scratch_shapes=scratch,
        ),
        out_shape=[jax.ShapeDtypeStruct(shape, dtype) for shape, dtype in outs],
        compiler_params=pltpu.CompilerParams(vmem_limit_bytes=16 * 1024 * 1024),
    )(meta, *operands)


def full(x):
    return (x, whole(x.shape))


def shards(
    query_stream,
    content_stream,
    memory,
    segment_ids,
    source_segments,
    context_rank,
    context_limit,
    padding,
    ln_query_gain,
    ln_query_bias,
    ln_content_gain,
    ln_content_bias,
    self_query,
    self_key,
    self_value,
    self_out,
    ln_cross_gain,
    ln_cross_bias,
    cross_query,
    cross_key,
    cross_value,
    cross_out,
    ln_ffn_gain,
    ln_ffn_bias,
    ffn_in,
    ffn_out,
    cotangent,
):
    core = lax.axis_index("heads") % 2

    def to_core(x):
        return lax.ppermute(x, "heads", [(h, h ^ 1) for h in range(4)])

    hold = lambda *xs: lax.optimization_barrier(xs)

    def to_chip(x):
        return lax.ppermute(x, "heads", [(h, h ^ 2) for h in range(4)])

    row = pl.BlockSpec((1, 8, 128), lambda d, core: (core[0], 0, 0))

    def token_row(x):
        return (in_hbm(x.reshape(2, 8, 128)), row)

    def fixed(x):
        zeros = (0,) * x.ndim
        return (in_hbm(x), pl.BlockSpec(x.shape, lambda d, core: zeros))

    prepared = [
        ((36,), jnp.int32, pl.BlockSpec(memory_space=pltpu.SMEM)),
        ((1, SEQ), f32, whole((1, SEQ))),
        ((1, SEQ), f32, whole((1, SEQ))),
        ((8, D), f32, whole((8, D))),
        ((D, D), bf16, whole((D, D))),
        ((D, D), bf16, whole((D, D))),
    ]
    gains = (
        ln_query_gain,
        ln_query_bias,
        ln_content_gain,
        ln_content_bias,
        ln_cross_gain,
        ln_cross_bias,
        ln_ffn_gain,
        ln_ffn_bias,
    )
    weights = (self_query, self_key, self_value, self_out)
    weights += (cross_query, cross_key, cross_value, cross_out)
    tokens = (segment_ids, source_segments, context_rank, context_limit, padding)
    meta, rank, limit, norms, ws0, wc0 = call(
        prepare,
        "prepare",
        [(jnp.stack([core, lax.axis_index("rows") % GROUP]).astype(jnp.int32), None)]
        + [token_row(x) for x in tokens]
        + [fixed(x.reshape(1, D)) for x in gains]
        + [fixed(x) for x in weights],
        prepared,
        [],
        0,
    )

    ws1 = to_core(ws0)
    ws2 = to_chip(ws0)
    wc1 = to_core(wc0)
    u0, v0 = ffn_in, ffn_out
    meta_in = (meta, None)

    heads_out = [out((SEQ, 256), bf16)] * 4

    def stream_out(dtype, own_row=False):
        return out((SEQ, D), dtype, own_row)

    def now(*xs):
        return [(x, "now") for x in xs]

    def fresh(*xs):
        return [(x, "fresh") for x in xs]

    def soon(*xs):
        return [(x, "soon") for x in xs]

    def late(*xs):
        return [(x, "late") for x in xs]

    def small(*xs):
        return [(x, whole(x.shape)) for x in xs]

    limits = pltpu.VMEM((SEQ, 128), f32)
    pair_flops = 2 * SEQ * D * 768 + 2 * 2 * 4 * DOCS * FAST_Q * FAST_K * 256

    nq, nc, *first, token = call(
        self_first,
        "self_first",
        [meta_in, (query_stream, "tiles_row"), (content_stream, "tiles_row")]
        + small(rank, limit, norms)
        + fresh(ws0, ws1),
        [stream_out(bf16), stream_out(bf16)] + heads_out + [probability_out],
        [limits] + probability_scratch,
        pair_flops,
        jnp.zeros((8, 128), f32),
    )
    ws2, wc0, u0, token = hold(ws2, wc0, u0, token)
    ws3 = to_core(ws2)
    wc2 = to_chip(wc0)
    u2 = to_chip(u0)
    *second_heads, second, ncross, token = call(
        self_second,
        "self_second",
        [meta_in, (query_stream, "late_row")]
        + [(nq, "tiles"), (nc, "tiles")]
        + small(rank, limit, norms)
        + late(ws0, ws1)
        + fresh(ws2, ws3)
        + late(first[3]),
        heads_out + [probability_out, stream_out(bf16), stream_out(bf16)],
        [limits] + probability_scratch,
        pair_flops + 2 * SEQ * D * D,
        token,
    )
    u0, token = hold(u0, token)
    u1 = to_core(u0)
    *cross_heads, token = call(
        cross_first,
        "cross_first",
        [meta_in, (ncross, "tiles"), (memory, "tiles_row")] + fresh(wc0, wc1),
        heads_out + [probability_out],
        probability_scratch,
        pair_flops,
        token,
    )
    wc2, u2, v0, token = hold(wc2, u2, v0, token)
    wc3 = to_core(wc2)
    u3 = to_core(u2)
    v2 = to_chip(v0)
    v1 = to_core(v0)
    *cross_heads_second, third, nffn, token = call(
        cross_second,
        "cross_second",
        [meta_in]
        + late(second)
        + [(ncross, "tiles"), (memory, "tiles_row")]
        + small(norms)
        + late(wc0, wc1)
        + fresh(wc2, wc3)
        + late(cross_heads[3]),
        heads_out
        + [probability_out, ((SEQ, D), f32, whole((SEQ, D))), ((SEQ, D), bf16, whole((SEQ, D)))],
        probability_scratch,
        pair_flops + 2 * SEQ * D * D,
        token,
    )
    u3, v2, token = hold(u3, v2, token)
    v3 = to_core(v2)
    grads_ln = ((8, D), f32, whole((8, D)))
    placed_output, output, g3_low, gln_ffn, ffn_own, ffn_other, token = call(
        ffn_both,
        "ffn_both",
        [meta_in]
        + small(third, nffn)
        + [(cotangent, "tiles_row")]
        + small(norms)
        + now(u0) + fresh(u1, u2, u3) + now(v0) + fresh(v1, v2, v3),
        [
            stream_out(bf16, True),
            stream_out(bf16),
            stream_out(bf16),
            grads_ln,
            out((1024, D), bf16),
            out((1024, D), bf16),
        ],
        [pltpu.VMEM((SEQ, 1024), bf16), pltpu.VMEM((SEQ, 1024), bf16), pltpu.VMEM((16, D), f32)],
        12 * SEQ * D * 2048,
        token,
    )

    def both_rows(placed_own, others, name):
        count = len(others)
        size = SEQ // 2
        one = pl.BlockSpec((size, D), lambda i, meta: (i, 0))
        block = pl.BlockSpec((size, D), lambda i, meta: (2 * (1 - meta[0]) + i, 0))
        return pl.pallas_call(
            place_rows,
            name=name,
            grid_spec=pltpu.PrefetchScalarGridSpec(
                num_scalar_prefetch=1,
                grid=(2,),
                in_specs=[one] * count + [pl.BlockSpec(memory_space=pl.ANY)] * count,
                out_specs=[block] * count,
            ),
            out_shape=[jax.ShapeDtypeStruct(x.shape, x.dtype) for x in placed_own],
            input_output_aliases={1 + count + n: n for n in range(count)},
        )(meta, *others, *placed_own)

    row_count = lax.axis_size("rows")
    assert row_count % GROUP == 0

    def along_rows(x, s):
        return lax.ppermute(x, "rows", [(r, r ^ s) for r in range(row_count)])

    def to_y(x):
        return along_rows(x, 1)

    def to_z(sends):
        return [along_rows(x, 2 * s) for s, x in enumerate(sends, 1)]

    def rows_out(*sizes):
        return [((n, D), bf16) for n in sizes]

    ffn_other = to_core(ffn_other)
    output_other = to_core(output)

    back_scratch = [pltpu.VMEM((SEQ, 256), bf16)] + [pltpu.VMEM((SEQ, 256), f32)] * 3
    back_scratch += probability_scratch
    pair_out = out((SEQ, 256), bf16)
    packed_outs = [((D, D), bf16, whole((D, D)))] * 2
    back_flops = 2 * SEQ * D * 256 + 4 * 2 * 4 * DOCS * FAST_Q * FAST_K * 256

    def head_inputs(natural, p):
        return soon(*natural) + [(in_hbm(p), ANY)]

    *cross_grads, cross_own, cross_other, token = call(
        functools.partial(attention_back_first, True),
        "cross_back_first",
        [meta_in]
        + [(g3_low, "tiles")]
        + late(ncross)
        + [(memory, "late_row")]
        + small(rank, limit)
        + now(wc0, wc1)
        + head_inputs(cross_heads[0:4], cross_heads[4]),
        [pair_out] * 3 + packed_outs,
        [limits] + back_scratch,
        back_flops + 2 * SEQ * D * 1024,
        token,
    )
    ffn_other, output_other, token = hold(ffn_other, output_other, token)
    ffn_keep, ffn_send = simple(slot_1, "slot_1", meta, [ffn_own, ffn_other], rows_out(512, 512))
    ffn_send, token = hold(ffn_send, token)
    ffn_arrived = to_y(ffn_send)
    cross_other = to_core(cross_other)
    g2_low, placed_mem, grad_mem, gln_cross, token = call(
        cross_back_second,
        "cross_back_second",
        [meta_in]
        + [(g3_low, "tiles")]
        + late(second)
        + small(norms)
        + late(wc0, wc1)
        + now(wc2, wc3)
        + late(*cross_grads)
        + head_inputs(cross_heads_second[0:4], cross_heads_second[4]),
        [stream_out(bf16), stream_out(f32, True), stream_out(bf16), grads_ln],
        back_scratch + [pltpu.VMEM((16, D), f32)],
        back_flops + 2 * SEQ * D * 1536,
        token,
    )
    ffn_arrived, cross_other, token = hold(ffn_arrived, cross_other, token)
    ffn_keep, *sends, cross_keep, cross_send = simple(
        slot_2,
        "slot_2",
        meta,
        [ffn_keep, ffn_arrived, cross_own, cross_other],
        rows_out(128, 128, 128, 128, 256, 256),
    )
    ffn_keep, cross_send, token = hold(ffn_keep, cross_send, token)
    ffn_parts = to_z(sends)
    cross_arrived = to_y(cross_send)

    *self_grads, self_own, self_other, token = call(
        functools.partial(attention_back_first, False),
        "self_back_first",
        [meta_in]
        + [(g2_low, "tiles")]
        + late(nq, nc)
        + small(rank, limit)
        + now(ws0, ws1)
        + head_inputs(first[0:4], first[4]),
        [pair_out] * 3 + packed_outs,
        [limits] + back_scratch,
        back_flops + 2 * SEQ * D * 1024,
        token,
    )
    *ffn_parts, cross_arrived, self_other, token = hold(
        *ffn_parts, cross_arrived, self_other, token
    )
    self_other = to_core(self_other)
    ffn_total, cross_keep, *sends, self_keep, self_send = simple(
        slot_3,
        "slot_3",
        meta,
        [ffn_keep, *ffn_parts, cross_keep, cross_arrived, self_own, self_other],
        rows_out(128, 64, 192, 192, 192, 256, 256),
    )
    ffn_total, self_send, grad_mem, token = hold(ffn_total, self_send, grad_mem, token)
    mem_other = to_core(grad_mem)
    self_arrived = to_y(self_send)
    messages = to_z(sends)
    *self_grads_second, token = call(
        self_back_second,
        "self_back_second",
        [meta_in, (g2_low, "tiles")]
        + small(rank, limit)
        + now(ws2, ws3)
        + head_inputs(second_heads[0:4], second_heads[4]),
        [((SEQ, 256), bf16, whole((SEQ, 256)))] * 3,
        [limits] + back_scratch,
        back_flops,
        token,
    )
    output_other, mem_other, token = hold(output_other, mem_other, token)
    out_both, grad_mem_both = both_rows(
        [placed_output, placed_mem], [output_other, mem_other], "place_early"
    )
    *messages, self_arrived, out_both, token = hold(*messages, self_arrived, out_both, token)
    ffn_half, cross_total, self_keep, *sends = simple(
        slot_4,
        "slot_4",
        meta,
        [ffn_total, *messages, cross_keep, self_keep, self_arrived],
        rows_out(512, 64, 64, 128, 128, 128),
    )
    cross_total, ffn_half, token = hold(cross_total, ffn_half, token)
    messages = to_z(sends)
    ffn_arrived = to_y(ffn_half)
    gq, gc, gln_self, token = call(
        self_back_finish,
        "self_back_finish",
        [meta_in, (g2_low, "tiles"), (query_stream, "tiles_row"), (content_stream, "tiles_row")]
        + small(norms)
        + now(ws0, ws1, ws2, ws3)
        + [(x, "tiles") for x in self_grads]
        + small(*self_grads_second),
        [((SEQ, D), bf16, whole((SEQ, D)))] * 2 + [grads_ln],
        [pltpu.VMEM((32, D), f32)],
        2 * SEQ * D * 1536,
        token,
    )
    gln = jnp.concatenate([gln_self[0:4], gln_cross[0:2], gln_ffn[0:2]], axis=0)
    gln_other = to_core(gln)
    *messages, ffn_arrived, gln_ffn = hold(*messages, ffn_arrived, gln_ffn)
    last_send, cross_half = simple(
        slot_5,
        "slot_5",
        meta,
        [self_keep, cross_total, *messages, gln, gln_other],
        [((GROUP, 80, D), bf16), ((256, D), bf16)],
    )
    groups = None
    if row_count > GROUP:
        groups = [list(range(r, r + GROUP)) for r in range(0, row_count, GROUP)]
    def gather(x):
        return lax.all_to_all(x, "rows", 0, 0, axis_index_groups=groups)

    gq_other, gc_other = to_core(gq), to_core(gc)
    last_parts = gather(last_send)
    cross_arrived = to_y(cross_half)
    def over_groups(totals):
        if row_count == GROUP:
            return totals
        groups = [list(range(r, row_count, GROUP)) for r in range(GROUP)]
        return lax.psum(totals, "rows", axis_index_groups=groups)

    def when_mine(mine):
        def index(r, i, meta):
            return (jnp.where((r == meta[0]) == mine, i, 0), 0)

        return pl.BlockSpec((SEQ // 2, D), index)

    placed_block = pl.BlockSpec((SEQ // 2, D), lambda r, i, meta: (2 * r + i, 0))
    gq_both, gc_both = pl.pallas_call(
        place_both,
        name="place_late",
        grid_spec=pltpu.PrefetchScalarGridSpec(
            num_scalar_prefetch=1,
            grid=(2, 2),
            in_specs=[when_mine(True)] * 2 + [when_mine(False)] * 2,
            out_specs=[placed_block] * 2,
        ),
        out_shape=[jax.ShapeDtypeStruct((2 * SEQ, D), f32)] * 2,
    )(meta, gq, gc, gq_other, gc_other)

    grad_ffn_in, grad_ffn_out = simple(
        unpack_ffn,
        "unpack_ffn",
        meta,
        [ffn_half, ffn_arrived],
        [((D, D), f32)] * 2,
        [pltpu.VMEM((2 * D, D), bf16)],
    )
    attention_outs = [((512, 128), f32)] * 3 + [((128, 512), f32)]
    cross_arrived, gq_both, grad_ffn_in = hold(cross_arrived, gq_both, grad_ffn_in)
    parts = simple(
        unpack_rest,
        "unpack_rest",
        meta,
        [cross_half, cross_arrived, last_parts],
        attention_outs * 2 + [((1, D), f32)] * 8,
        [pltpu.VMEM((D, D), bf16)],
    )
    grad_cross_parts, grad_self_parts = parts[0:4], parts[4:8]
    gln = [x.reshape(D) for x in parts[8:16]]
    grad_ffn_in, grad_ffn_out, grad_cross_parts, grad_self_parts, gln = over_groups(
        (grad_ffn_in, grad_ffn_out, grad_cross_parts, grad_self_parts, gln)
    )
    return (
        out_both,
        gq_both,
        gc_both,
        grad_mem_both,
        gln[0],
        gln[1],
        gln[2],
        gln[3],
        *grad_self_parts,
        gln[4],
        gln[5],
        *grad_cross_parts,
        gln[6],
        gln[7],
        grad_ffn_in,
        grad_ffn_out,
    )


def solution(mesh):
    assert mesh.shape["heads"] == 4
    row_spec = P("rows", None)
    flat = P("rows")
    by_column = P(None, "heads")
    by_row = P("heads", None)
    attention = (by_column, by_column, by_column, by_row)
    in_specs = (
        (row_spec,) * 3
        + (flat,) * 5
        + (P(),) * 4
        + attention
        + (P(),) * 2
        + attention
        + (P(),) * 2
        + (by_column, by_row, row_spec)
    )
    out_specs = (
        (row_spec,) * 4
        + (P(),) * 4
        + attention
        + (P(),) * 2
        + attention
        + (P(),) * 2
        + (by_column, by_row)
    )
    return jax.shard_map(shards, mesh=mesh, in_specs=in_specs, out_specs=out_specs, check_vma=False)
```

```python
import functools

import jax
import jax.numpy as jnp
from jax import lax
from jax.experimental import pallas as pl
from jax.experimental.pallas import tpu as pltpu
from jax.sharding import PartitionSpec as P

HEAD_DIM = 64
SEQ = 1024
DOCS = 8
D = 512
TILE = 256
TILES = SEQ // TILE
FAST_Q = 256
FAST_K = 208
LONG_Q = 128
LONG_K = 640

norm_eps = 1e-05
masked_score = -1e30
hidden_rank = 1e6
gelu_root = 0.7978845608028654
gelu_cube = 0.044715

f32 = jnp.float32
bf16 = jnp.bfloat16


def dot(a, b):
    return lax.dot_general(a, b, (((1,), (0,)), ((), ())), preferred_element_type=f32)


def dot_nt(a, b):
    return lax.dot_general(a, b, (((1,), (1,)), ((), ())), preferred_element_type=f32)


def dot_tn(a, b):
    return lax.dot_general(a, b, (((0,), (0,)), ((), ())), preferred_element_type=f32)


def lanes(parts):
    return jnp.concatenate(parts, axis=1)


NORM_ROWS = 32


def layer_norm(values, gain, shift):
    def piece(part):
        part = part.astype(f32)
        centre = part - jnp.mean(part, axis=-1, keepdims=True)
        spread = jnp.mean(centre * centre, axis=-1, keepdims=True)
        return (centre * lax.rsqrt(spread + norm_eps) * gain + shift).astype(bf16)

    return by_pieces(piece, NORM_ROWS, 0, values)


def eight_rows(values):
    return sum(values[8 * i : 8 * i + 8] for i in range(1, values.shape[0] // 8)) + values[0:8]


def norm_backward(values, gain, grad, sums_ref, first):
    sums = []

    def piece(part, grad_part):
        part = part.astype(f32)
        centre = part - jnp.mean(part, axis=-1, keepdims=True)
        spread = jnp.mean(centre * centre, axis=-1, keepdims=True)
        scale = lax.rsqrt(spread + norm_eps)
        xhat = centre * scale
        eg = grad_part * gain
        mean_eg = jnp.mean(eg, axis=-1, keepdims=True)
        mean_egx = jnp.mean(eg * xhat, axis=-1, keepdims=True)
        sums.append((eight_rows(grad_part * xhat), eight_rows(grad_part)))
        return scale * (eg - mean_eg - xhat * mean_egx)

    result = by_pieces(piece, NORM_ROWS, 0, values, grad)
    for n, parts in enumerate(zip(*sums)):
        sums_ref[first + 8 * n : first + 8 * n + 8, :] += sum(parts[1:], parts[0])
    return result


def add_sums(sums_ref, gln_ref, count):
    gln_ref[...] = jnp.zeros_like(gln_ref)
    for n in range(count):
        gln_ref[n : n + 1, :] = jnp.sum(sums_ref[8 * n : 8 * n + 8, :], axis=0, keepdims=True)


def by_pieces(work, size, axis, *arrays):
    count = arrays[0].shape[axis] // size
    pieces = []
    for i in range(count):
        cut = (slice(size * i, size * i + size),)
        cut = cut if axis == 0 else (slice(None),) + cut
        pieces.append(work(*[x[cut] for x in arrays]))
    if not isinstance(pieces[0], tuple):
        return jnp.concatenate(pieces, axis=axis)
    return tuple(jnp.concatenate(parts, axis=axis) for parts in zip(*pieces))


def rows_of(i, size=TILE):
    return pl.ds(pl.multiple_of(i * size, size), size)


def w_query(ref):
    return ref[:, 0:128]


def w_key(ref):
    return ref[:, 128:256]


def w_value(ref):
    return ref[:, 256:384]


def w_out(ref):
    return lanes([ref[128 * j : 128 * j + 128, 384:512] for j in range(4)])


def half_masks():
    place = lax.broadcasted_iota(jnp.int32, (1, 128), 1)
    low = jnp.where(place < HEAD_DIM, 1.0, 0.0).astype(f32)
    return (low.astype(bf16), (1.0 - low).astype(bf16))


def doc_bounds(meta, d, source):
    base = 17 if source else 1
    return meta[base + d], meta[base + 8 + d]


def window_of(first, limit):
    return pl.multiple_of(jnp.minimum((first // 16) * 16, limit), 16)


def key_bias(ks, ke, k0, width):
    place = k0 + lax.broadcasted_iota(jnp.int32, (width, 128), 0)
    return jnp.where((place >= ks) & (place < ke), 0.0, masked_score)


def make_bias(rank_ref, limit_ref, ks, ke, q0, k0, span, width):
    if rank_ref is None:
        return lanes([key_bias(ks, ke, k0, width)] * (span // 128))
    place = k0 + lax.broadcasted_iota(jnp.int32, (width, 128), 0)
    ranks = rank_ref[pl.ds(k0, width), :]
    ranks = jnp.where((place < ks + 2) & (ranks < hidden_rank), -1.0, ranks)
    ranks = jnp.where((place >= ks) & (place < ke), ranks, hidden_rank)
    limits = jnp.broadcast_to(limit_ref[...], (8, SEQ))
    limits = pltpu.roll(limits, lax.rem(SEQ - q0, SEQ), 1)[0:1, 0:span]
    row = k0 + lax.broadcasted_iota(jnp.int32, (width, span), 0)
    column = q0 + lax.broadcasted_iota(jnp.int32, (width, span), 1)
    seen = (lanes([ranks] * (span // 128)) < limits) & (row != column)
    return jnp.where(seen, 0.0, masked_score)


TOGETHER = 4
STEPS = DOCS // TOGETHER


LAG = 2


def interleave(items):
    items = [list(phases) for phases in items]
    depth = max(len(phases) for phases in items)
    results = [None] * len(items)
    for tick in range(len(items) + LAG * (depth - 1)):
        for phase in range(depth):
            n = tick - LAG * phase
            if 0 <= n < len(items) and phase < len(items[n]):
                run = items[n][phase]
                results[n] = run() if phase == 0 else run(results[n])
    return results


def by_halves(pairs, phases):
    shared = [{} for _ in range(pairs)]
    return [phases(n, a, shared[n]) for n in range(pairs) for a in range(2)]


def is_fast(meta, cross):
    return meta[34 if cross else 33] == 1


def both_heads(x, masks):
    return jnp.concatenate([x * masks[0], x * masks[1]], axis=0)


def pair_scores(queries, keys, masks):
    return dot_nt(both_heads(keys, masks), queries)


def raised(scores, bias):
    def piece(part, bias_part):
        part = part + bias_part
        return jnp.exp((part - jnp.max(part, axis=0, keepdims=True)).astype(bf16))

    return by_pieces(piece, 128, 1, scores, bias)


def weighted_values(values, parts):
    width = values.shape[1]
    mixed = []
    shares = []
    for a, part in enumerate(parts):
        rows = jnp.concatenate([values[64 * a : 64 * a + 64], jnp.ones((16, width), bf16)], axis=0)
        sums = dot(rows, part)
        share = 1.0 / sums[64:65]
        mixed.append(sums[:64] * share)
        shares.append(part * share.astype(bf16))
    return jnp.concatenate(mixed, axis=0).astype(bf16), shares


def pair_gradient(rows, parts):
    across = jnp.transpose(rows)
    halves = [dot(across[64 * a : 64 * a + 64], part) for a, part in enumerate(parts)]
    return jnp.transpose((jnp.concatenate(halves, axis=0) * HEAD_DIM**-0.5).astype(bf16))


def for_docs(meta, cross, run, before, after):
    @pl.when(is_fast(meta, cross))
    def _():
        def step(i, carry):
            slot = lax.rem(i, 2)
            before(i, slot)
            items = []
            for place in range(TOGETHER):
                d = TOGETHER * i + place
                ts, te = doc_bounds(meta, d, False)
                ks, ke = doc_bounds(meta, d, cross)
                q0 = window_of(ts, SEQ - FAST_Q)
                k0 = window_of(ks, SEQ - FAST_K)
                items += run(d, slot, place, q0, k0, FAST_Q, FAST_K, ts, te, ks, ke, True)
            interleave(items)
            after(i, slot)
            return carry

        lax.fori_loop(0, STEPS, step, 0)

    @pl.when(jnp.logical_not(is_fast(meta, cross)))
    def _():
        def doc(d, carry):
            ts, te = doc_bounds(meta, d, False)
            ks, ke = doc_bounds(meta, d, cross)
            base = (ts // 16) * 16
            k0 = window_of(ks, SEQ - LONG_K)

            def chunk(i, carry):
                lower = base + i * LONG_Q
                q0 = pl.multiple_of(jnp.minimum(lower, SEQ - LONG_Q), 16)
                low = jnp.maximum(ts, lower)
                high = jnp.minimum(te, lower + LONG_Q)
                interleave(run(d, None, None, q0, k0, LONG_Q, LONG_K, low, high, ks, ke, False))
                return carry

            return lax.fori_loop(0, (te - base + LONG_Q - 1) // LONG_Q, chunk, carry)

        lax.fori_loop(0, DOCS, doc, 0)


def attend_docs(meta, cross, rank_ref, limit_ref, halves, p_ref, p_buf, p_sem):
    pairs = 2 * len(halves)
    masks = half_masks()

    def save(i, slot):
        return pltpu.make_async_copy(p_buf.at[slot], p_ref.at[pl.ds(TOGETHER * i, TOGETHER)], p_sem.at[slot])

    def before(i, slot):
        @pl.when(i >= 2)
        def _():
            save(i - 2, slot).wait()

    def after(i, slot):
        save(i, slot).start()

    def run(d, slot, place, q0, k0, span, width, low, high, ks, ke, fast):
        bias = make_bias(rank_ref, limit_ref, ks, ke, q0, k0, span, width)
        row = q0 + lax.broadcasted_iota(jnp.int32, (span, 128), 0)
        inside = (row >= low) & (row < high)

        def phases(n):
            q_ref, k_ref, v_ref, mixed_ref = halves[n // 2]
            cols = slice(128 * (n % 2), 128 * (n % 2) + 128)

            def score():
                return pair_scores(q_ref[pl.ds(q0, span), cols], k_ref[pl.ds(k0, width), cols], masks)

            def weigh(scores):
                return [raised(scores[width * a : width * a + width], bias) for a in range(2)]

            def mix(parts):
                values = jnp.transpose(v_ref[pl.ds(k0, width), cols])
                mixed, parts = weighted_values(values, parts)
                if fast:
                    for a in range(2):
                        p_buf[slot, place, 2 * n + a] = parts[a]
                mixed = jnp.transpose(mixed).astype(f32)
                old = mixed_ref[pl.ds(q0, span), cols].astype(f32)
                mixed_ref[pl.ds(q0, span), cols] = jnp.where(inside, mixed, old).astype(bf16)

            return score, weigh, mix

        return [phases(n) for n in range(pairs)]

    for_docs(meta, cross, run, before, after)

    @pl.when(is_fast(meta, cross))
    def _():
        for i in range(STEPS - 2, STEPS):
            save(i, i % 2).wait()


def load_step(load, i, slot):
    p_ref, p_buf, p_sem = load
    return pltpu.make_async_copy(p_ref.at[pl.ds(TOGETHER * i, TOGETHER)], p_buf.at[slot], p_sem.at[slot])


def start_load(meta, cross, load):
    @pl.when(is_fast(meta, cross))
    def _():
        load_step(load, 0, 0).start()


def attend_docs_back(
    meta, cross, rank_ref, limit_ref, q_ref, k_ref, v_ref, mixed_ref, dm_ref,
    dq_ref, dk_ref, dv_ref, load,
):
    pairs = q_ref.shape[1] // 128
    masks = half_masks()
    p_buf = load[1]

    def before(i, slot):
        @pl.when(i + 1 < STEPS)
        def _():
            load_step(load, i + 1, 1 - slot).start()

        load_step(load, i, slot).wait()

    def after(i, slot):
        pass

    def run(d, slot, place, q0, k0, span, width, low, high, ks, ke, fast):
        row = q0 + lax.broadcasted_iota(jnp.int32, (span, 128), 0)
        inside = jnp.where((row >= low) & (row < high), 1.0, 0.0).astype(bf16)
        ones = jnp.ones((width, 128), bf16)
        if not fast:
            bias = make_bias(rank_ref, limit_ref, ks, ke, q0, k0, span, width)

        def phases(n):
            cols = slice(128 * n, 128 * n + 128)

            def differ():
                values = v_ref[pl.ds(k0, width), cols]
                mixed = mixed_ref[pl.ds(q0, span), cols]
                grad = dm_ref[pl.ds(q0, span), cols] * inside
                left = lanes([grad, -(grad * mixed)])
                right = both_heads(lanes([values, ones]), [lanes([m, m]) for m in masks])
                return grad, dot_nt(right, left)

            def slope(state):
                grad, delta = state
                if fast:
                    parts = [p_buf[slot, place, 2 * n + a] for a in range(2)]
                else:
                    queries = q_ref[pl.ds(q0, span), cols]
                    keys = k_ref[pl.ds(k0, width), cols]
                    scores = pair_scores(queries, keys, masks)
                    parts = [raised(scores[width * a : width * a + width], bias) for a in range(2)]
                    parts = weighted_values(jnp.transpose(v_ref[pl.ds(k0, width), cols]), parts)[1]
                slopes = [
                    by_pieces(
                        lambda part, change: part * change.astype(bf16),
                        16,
                        0,
                        parts[a],
                        delta[width * a : width * a + width],
                    )
                    for a in range(2)
                ]
                return grad, parts, slopes

            def spread(state):
                grad, parts, slopes = state
                queries = q_ref[pl.ds(q0, span), cols]
                dk = dv = None
                for a in range(2):
                    dk_a = dot(slopes[a], queries * masks[a])
                    dv_a = dot(parts[a], grad * masks[a])
                    dk = dk_a if dk is None else dk + dk_a
                    dv = dv_a if dv is None else dv + dv_a
                dq = pair_gradient(k_ref[pl.ds(k0, width), cols], slopes)
                dq_ref[pl.ds(q0, span), cols] += dq.astype(f32)
                dk_ref[pl.ds(k0, width), cols] += dk
                dv_ref[pl.ds(k0, width), cols] += dv

            return differ, slope, spread

        return [phases(n) for n in range(pairs)]

    for_docs(meta, cross, run, before, after)


def spread_ranks(rank_row_ref, rank_ref):
    rank_ref[...] = jnp.transpose(jnp.broadcast_to(rank_row_ref[...], (128, SEQ)))


def prepare(
    core, seg_ref, src_ref, rank_ref, limit_ref, pad_ref,
    n0, n1, n2, n3, n4, n5, n6, n7, sq, sk, sv, so, cq, ck, cv, co,
    meta_ref, ranks_ref, limits_ref, norms_ref, ws_ref, wc_ref,
):
    meta_ref[0] = core[0]
    meta_ref[35] = core[1]
    for base, ref in ((1, seg_ref), (17, src_ref)):
        ids = ref[0]
        meta_ref[base] = 0
        meta_ref[base + 15] = SEQ
        for d in range(1, DOCS):
            cut = jnp.sum(jnp.where(ids < d, 1.0, 0.0)).astype(jnp.int32)
            meta_ref[base + d] = cut
            meta_ref[base + 7 + d] = cut
    for place, base in ((33, 1), (34, 17)):
        fast = jnp.int32(1)
        for d in range(DOCS):
            q0 = window_of(meta_ref[1 + d], SEQ - FAST_Q)
            k0 = window_of(meta_ref[base + d], SEQ - FAST_K)
            fits = (meta_ref[9 + d] - q0 <= FAST_Q) & (meta_ref[base + 8 + d] - k0 <= FAST_K)
            fast = fast & fits.astype(jnp.int32)
        meta_ref[place] = fast
    ranks = jnp.where(pad_ref[0] != 0, hidden_rank, rank_ref[0].astype(f32))
    limits = limit_ref[0].astype(f32)
    for i in range(8):
        ranks_ref[0:1, 128 * i : 128 * i + 128] = ranks[i : i + 1]
        limits_ref[0:1, 128 * i : 128 * i + 128] = limits[i : i + 1]
    for i, ref in enumerate((n0, n1, n2, n3, n4, n5, n6, n7)):
        norms_ref[i : i + 1, :] = ref[...]
    for to, parts, out in ((ws_ref, (sq, sk, sv), so), (wc_ref, (cq, ck, cv), co)):
        for i, part in enumerate(parts):
            to[:, 128 * i : 128 * i + 128] = part[...]
        for j in range(4):
            to[128 * j : 128 * j + 128, 384:512] = out[:, 128 * j : 128 * j + 128]


def self_first(
    meta, io, xq_ref, xc_ref, rank_row_ref, limit_ref, norms_ref, w0_ref, w1_ref,
    nq_ref, nc_ref, q_ref, k_ref, v_ref, mixed_ref, p_ref, rank_ref, p_buf, p_sem,
):

    spread_ranks(rank_row_ref, rank_ref)
    wq = lanes([w_query(w0_ref), w_query(w1_ref)])
    wkv = lanes([w_key(w0_ref), w_key(w1_ref), w_value(w0_ref), w_value(w1_ref)])

    def tile(i, carry):
        rows = rows_of(i)
        io.wait_rows(i)
        nq = layer_norm(xq_ref[rows, :], norms_ref[0:1], norms_ref[1:2])
        nc = layer_norm(xc_ref[rows, :], norms_ref[2:3], norms_ref[3:4])
        nq_ref[rows, :] = nq
        nc_ref[rows, :] = nc
        q_ref[rows, :] = (dot(nq, wq) * (HEAD_DIM**-0.5)).astype(bf16)
        kv = dot(nc, wkv).astype(bf16)
        k_ref[rows, :] = kv[:, :256]
        v_ref[rows, :] = kv[:, 256:]
        return carry

    lax.fori_loop(0, TILES, tile, 0)

    for ref in (nq_ref, nc_ref, q_ref, k_ref, v_ref):
        io.send(ref)
    attend_docs(meta, False, rank_ref, limit_ref, [(q_ref, k_ref, v_ref, mixed_ref)], p_ref, p_buf, p_sem)


def self_second(
    meta, io, xq_ref, nq_ref, nc_ref, rank_row_ref, limit_ref, norms_ref, w0_ref, w1_ref, w2_ref, w3_ref,
    mixed_first_ref,
    q_ref, k_ref, v_ref, mixed_ref, p_ref, second_ref, ncross_ref, rank_ref, p_buf, p_sem,
):

    spread_ranks(rank_row_ref, rank_ref)
    wq = lanes([w_query(w2_ref), w_query(w3_ref)])
    wkv = lanes([w_key(w2_ref), w_key(w3_ref), w_value(w2_ref), w_value(w3_ref)])

    def tile(i, carry):
        rows = rows_of(i)
        io.wait_rows(i)
        q_ref[rows, :] = (dot(nq_ref[rows, :], wq) * (HEAD_DIM**-0.5)).astype(bf16)
        kv = dot(nc_ref[rows, :], wkv).astype(bf16)
        k_ref[rows, :] = kv[:, :256]
        v_ref[rows, :] = kv[:, 256:]
        return carry

    lax.fori_loop(0, TILES, tile, 0)

    for ref in (q_ref, k_ref, v_ref):
        io.send(ref)
    attend_docs(meta, False, rank_ref, limit_ref, [(q_ref, k_ref, v_ref, mixed_ref)], p_ref, p_buf, p_sem)

    io.send(mixed_ref)
    io.wait("late")
    out_first = jnp.concatenate([w_out(w0_ref), w_out(w1_ref)], axis=0)
    out_second = jnp.concatenate([w_out(w2_ref), w_out(w3_ref)], axis=0)

    def tile(i, carry):
        rows = rows_of(i)
        branch = dot(mixed_first_ref[rows, :], out_first) + dot(mixed_ref[rows, :], out_second)
        second = xq_ref[rows, :].astype(f32) + branch
        second_ref[rows, :] = second.astype(bf16)
        io.send(second_ref, rows)
        ncross_ref[rows, :] = layer_norm(second, norms_ref[4:5], norms_ref[5:6])
        io.send(ncross_ref, rows)
        return carry

    lax.fori_loop(0, TILES, tile, 0)


def project_cross(io, ncross_ref, memory_ref, weights, q_ref, k_ref, v_ref):
    wq = lanes([w_query(w) for w in weights])
    wkv = lanes([w_key(w) for w in weights] + [w_value(w) for w in weights])

    def tile(i, carry):
        rows = rows_of(i)
        io.wait_rows(i)
        q_ref[rows, :] = (dot(ncross_ref[rows, :], wq) * (HEAD_DIM**-0.5)).astype(bf16)
        kv = dot(memory_ref[rows, :], wkv).astype(bf16)
        k_ref[rows, :] = kv[:, :256]
        v_ref[rows, :] = kv[:, 256:]
        return carry

    lax.fori_loop(0, TILES, tile, 0)
    for ref in (q_ref, k_ref, v_ref):
        io.send(ref)


def cross_first(
    meta, io, ncross_ref, memory_ref, w0_ref, w1_ref,
    q_ref, k_ref, v_ref, mixed_ref, p_ref, p_buf, p_sem,
):
    project_cross(io, ncross_ref, memory_ref, (w0_ref, w1_ref), q_ref, k_ref, v_ref)
    attend_docs(meta, True, None, None, [(q_ref, k_ref, v_ref, mixed_ref)], p_ref, p_buf, p_sem)


def cross_second(
    meta, io, second_ref, ncross_ref, memory_ref, norms_ref, w0_ref, w1_ref, w2_ref, w3_ref,
    mixed_first_ref,
    q_ref, k_ref, v_ref, mixed_ref, p_ref, third_ref, nffn_ref, p_buf, p_sem,
):
    project_cross(io, ncross_ref, memory_ref, (w2_ref, w3_ref), q_ref, k_ref, v_ref)
    attend_docs(meta, True, None, None, [(q_ref, k_ref, v_ref, mixed_ref)], p_ref, p_buf, p_sem)
    io.send(mixed_ref)
    io.wait("late")
    out_first = jnp.concatenate([w_out(w0_ref), w_out(w1_ref)], axis=0)
    out_second = jnp.concatenate([w_out(w2_ref), w_out(w3_ref)], axis=0)

    def tile(i, carry):
        rows = rows_of(i)
        branch = dot(mixed_first_ref[rows, :], out_first) + dot(mixed_ref[rows, :], out_second)
        third = second_ref[rows, :].astype(f32) + branch
        third_ref[rows, :] = third
        nffn_ref[rows, :] = layer_norm(third, norms_ref[6:7], norms_ref[7:8])
        return carry

    lax.fori_loop(0, TILES, tile, 0)


def ffn_both(
    meta, io, third_ref, nffn_ref, cot_ref, norms_ref, u0_ref, u1_ref, u2_ref, u3_ref,
    w0_ref, w1_ref, w2_ref, w3_ref,
    placed_ref, out_ref, g3_low_ref, gln_ref, own_ref, other_ref, hidden_ref, before_ref, sums_ref,
):
    sums_ref[...] = jnp.zeros_like(sums_ref)
    in_refs = (u0_ref, u1_ref, u2_ref, u3_ref)
    w_refs = (w0_ref, w1_ref, w2_ref, w3_ref)

    def tile(i, carry):
        rows = rows_of(i)
        io.wait_rows(i)
        nffn = nffn_ref[rows, :]
        cot = cot_ref[rows, :]
        outs = []
        grads = []

        def phases(g, c, group):
            w_in = in_refs[g]
            w_out_rows = w_refs[g]
            cols = slice(256 * c, 256 * c + 256)

            def enter():
                return dot(nffn, w_in[:, cols]), dot_nt(cot, w_out_rows[cols, :])

            def bend(state):
                def piece(x, grad_hidden):
                    square = x * x
                    argument = x * (gelu_root + (gelu_root * gelu_cube) * square)
                    half = 0.5 + 0.5 * jnp.tanh(argument.astype(bf16))
                    x = x.astype(bf16)
                    square = square.astype(bf16)
                    value = x * half
                    rise = 2.0 * gelu_root + (6.0 * gelu_root * gelu_cube) * square
                    slope = half + value * (1.0 - half) * rise
                    return value, grad_hidden.astype(bf16) * slope

                hidden, grad_before = by_pieces(piece, 32, 0, *state)
                if g < 2:
                    place = slice(512 * g + 256 * c, 512 * g + 256 * c + 256)
                    hidden_ref[rows, place] = hidden
                    before_ref[rows, place] = grad_before
                group[c] = hidden, grad_before

            def leave(_):
                if c == 1:
                    outs.append(dot(lanes([group[0][0], group[1][0]]), w_out_rows[...]))

            def leave_back(_):
                if c == 1:
                    grads.append(dot_nt(lanes([group[0][1], group[1][1]]), w_in[...]))

            return enter, bend, leave, leave_back

        interleave(by_halves(4, phases))
        third = third_ref[rows, :]
        result = (third + ((outs[0] + outs[1]) + (outs[2] + outs[3]))).astype(bf16)
        out_ref[rows, :] = result
        placed_ref[rows, :] = result
        grad_normed = (grads[0] + grads[1]) + (grads[2] + grads[3])
        grad_norm = norm_backward(third, norms_ref[6:7], grad_normed, sums_ref, 0)
        g3_low_ref[rows, :] = (cot.astype(f32) + grad_norm).astype(bf16)
        for ref in (out_ref, placed_ref, g3_low_ref):
            io.send(ref, rows)
        return carry

    lax.fori_loop(0, TILES, tile, 0)
    add_sums(sums_ref, gln_ref, 2)
    part = dot_tn(nffn_ref[...], before_ref[...])
    own_ref[0:512, :] = part[:, 0:512].astype(bf16)
    other_ref[0:512, :] = part[:, 512:1024].astype(bf16)
    io.send(own_ref, pl.ds(0, 512))
    io.send(other_ref, pl.ds(0, 512))
    part = dot_tn(hidden_ref[...], cot_ref[...])
    own_ref[512:1024, :] = part[0:512].astype(bf16)
    other_ref[512:1024, :] = part[512:1024].astype(bf16)
    io.send(own_ref, pl.ds(512, 512))
    io.send(other_ref, pl.ds(512, 512))


def back_start(io, g_ref, mixed_ref, w_refs, dm_ref, dq_ref, dk_ref, dv_ref):
    out_rows = jnp.concatenate([w_out(w) for w in w_refs], axis=0)

    def tile(i, carry):
        rows = rows_of(i)
        io.wait_rows(i)
        dm_ref[rows, :] = dot_nt(g_ref[rows, :], out_rows).astype(bf16)
        zeros = jnp.zeros((TILE, 256), f32)
        dq_ref[rows, :] = zeros
        dk_ref[rows, :] = zeros
        dv_ref[rows, :] = zeros
        return carry

    lax.fori_loop(0, TILES, tile, 0)


def attention_back_first(
    cross, meta, io, g_ref, nq_ref, nkv_ref, rank_row_ref, limit_ref, w0_ref, w1_ref,
    q_ref, k_ref, v_ref, mixed_ref, p_ref,
    dq_ref, dk_ref, dv_ref, own_ref, other_ref,
    rank_ref, dm_ref, dqs_ref, dks_ref, dvs_ref, p_buf, p_sem,
):
    load = (p_ref, p_buf, p_sem)
    start_load(meta, cross, load)
    if not cross:
        spread_ranks(rank_row_ref, rank_ref)
    back_start(io, g_ref, mixed_ref, (w0_ref, w1_ref), dm_ref, dqs_ref, dks_ref, dvs_ref)

    io.wait("soon")
    attend_docs_back(
        meta, cross, None if cross else rank_ref, limit_ref, q_ref, k_ref, v_ref, mixed_ref,
        dm_ref, dqs_ref, dks_ref, dvs_ref, load,
    )

    dq_ref[...] = dqs_ref[...].astype(bf16)
    dk_ref[...] = dks_ref[...].astype(bf16)
    dv_ref[...] = dvs_ref[...].astype(bf16)
    for ref in (dq_ref, dk_ref, dv_ref):
        io.send(ref)
    io.wait("late")
    nq = nq_ref[...]
    nkv = nkv_ref[...]
    kv = dot_tn(nkv, lanes([dk_ref[...], dv_ref[...]]))
    for n, part in enumerate((dot_tn(nq, dq_ref[...]), kv[:, 0:256], kv[:, 256:512])):
        own_ref[:, 128 * n : 128 * n + 128] = part[:, :128].astype(bf16)
        other_ref[:, 128 * n : 128 * n + 128] = part[:, 128:].astype(bf16)
    part = dot_tn(mixed_ref[...], g_ref[...])
    for j in range(4):
        rows = slice(128 * j, 128 * j + 128)
        own_ref[rows, 384:512] = part[:128, rows].astype(bf16)
        other_ref[rows, 384:512] = part[128:, rows].astype(bf16)


def back_second_docs(
    cross, meta, io, g_ref, rank_row_ref, limit_ref, w_refs, q_ref, k_ref, v_ref, mixed_ref, p_ref,
    rank_ref, dm_ref, dqs_ref, dks_ref, dvs_ref, p_buf, p_sem,
):
    load = (p_ref, p_buf, p_sem)
    start_load(meta, cross, load)
    if not cross:
        spread_ranks(rank_row_ref, rank_ref)
    back_start(io, g_ref, mixed_ref, w_refs, dm_ref, dqs_ref, dks_ref, dvs_ref)

    io.wait("soon")
    attend_docs_back(
        meta, cross, None if cross else rank_ref, limit_ref, q_ref, k_ref, v_ref, mixed_ref,
        dm_ref, dqs_ref, dks_ref, dvs_ref, load,
    )


def stream_grads(rows, first, second, firsts, seconds):
    dq, dk, dv = first
    dq2, dk2, dv2 = (ref[rows, :].astype(bf16) for ref in second)
    w0, w1 = firsts
    w2, w3 = seconds
    grad_q = dot_nt(dq[rows, :], lanes([w_query(w0), w_query(w1)])) + dot_nt(
        dq2, lanes([w_query(w2), w_query(w3)])
    )
    kv = lanes([dk[rows, :], dv[rows, :]])
    kv2 = lanes([dk2, dv2])
    grad_kv = dot_nt(kv, lanes([w_key(w0), w_key(w1), w_value(w0), w_value(w1)])) + dot_nt(
        kv2, lanes([w_key(w2), w_key(w3), w_value(w2), w_value(w3)])
    )
    return grad_q, grad_kv


def cross_back_second(
    meta, io, g_low_ref, second_ref, norms_ref, w0_ref, w1_ref, w2_ref, w3_ref,
    dq_ref, dk_ref, dv_ref, q_ref, k_ref, v_ref, mixed_ref, p_ref,
    g2_low_ref, placed_ref, gmem_ref, gln_ref,
    dm_ref, dqs_ref, dks_ref, dvs_ref, p_buf, p_sem, sums_ref,
):
    back_second_docs(
        True, meta, io, g_low_ref, None, None, (w2_ref, w3_ref), q_ref, k_ref, v_ref, mixed_ref, p_ref,
        None, dm_ref, dqs_ref, dks_ref, dvs_ref, p_buf, p_sem,
    )

    io.wait("late")
    sums_ref[...] = jnp.zeros_like(sums_ref)

    def tile(i, carry):
        rows = rows_of(i)
        grad_q, grad_kv = stream_grads(
            rows,
            (dq_ref, dk_ref, dv_ref),
            (dqs_ref, dks_ref, dvs_ref),
            (w0_ref, w1_ref),
            (w2_ref, w3_ref),
        )
        low_kv = grad_kv.astype(bf16)
        gmem_ref[rows, :] = low_kv
        placed_ref[rows, :] = low_kv.astype(f32)
        io.send(gmem_ref, rows)
        io.send(placed_ref, rows)
        grad_norm = norm_backward(second_ref[rows, :], norms_ref[4:5], grad_q, sums_ref, 0)
        g2_low_ref[rows, :] = (g_low_ref[rows, :].astype(f32) + grad_norm).astype(bf16)
        io.send(g2_low_ref, rows)
        return carry

    lax.fori_loop(0, TILES, tile, 0)
    add_sums(sums_ref, gln_ref, 2)


def self_back_second(
    meta, io, g_low_ref, rank_row_ref, limit_ref, w2_ref, w3_ref,
    q_ref, k_ref, v_ref, mixed_ref, p_ref,
    dq_ref, dk_ref, dv_ref,
    rank_ref, dm_ref, dqs_ref, dks_ref, dvs_ref, p_buf, p_sem,
):
    back_second_docs(
        False, meta, io, g_low_ref, rank_row_ref, limit_ref, (w2_ref, w3_ref), q_ref, k_ref, v_ref,
        mixed_ref, p_ref, rank_ref, dm_ref, dqs_ref, dks_ref, dvs_ref, p_buf, p_sem,
    )
    dq_ref[...] = dqs_ref[...].astype(bf16)
    dk_ref[...] = dks_ref[...].astype(bf16)
    dv_ref[...] = dvs_ref[...].astype(bf16)


def self_back_finish(
    meta, io, g_ref, xq_ref, xc_ref, norms_ref, w0_ref, w1_ref, w2_ref, w3_ref,
    dq_ref, dk_ref, dv_ref, dq2_ref, dk2_ref, dv2_ref,
    placed_q_ref, placed_c_ref, gq_ref, gc_ref, gln_ref, sums_ref,
):
    sums_ref[...] = jnp.zeros_like(sums_ref)

    def tile(i, carry):
        rows = rows_of(i)
        io.wait_rows(i)
        grad_q, grad_kv = stream_grads(
            rows,
            (dq_ref, dk_ref, dv_ref),
            (dq2_ref, dk2_ref, dv2_ref),
            (w0_ref, w1_ref),
            (w2_ref, w3_ref),
        )
        grad_norm = norm_backward(xq_ref[rows, :], norms_ref[0:1], grad_q, sums_ref, 0)
        low_q = (g_ref[rows, :].astype(f32) + grad_norm).astype(bf16)
        gq_ref[rows, :] = low_q
        placed_q_ref[rows, :] = low_q.astype(f32)
        io.send(placed_q_ref, rows)
        grad_norm = norm_backward(xc_ref[rows, :], norms_ref[2:3], grad_kv, sums_ref, 16)
        low_c = grad_norm.astype(bf16)
        gc_ref[rows, :] = low_c
        placed_c_ref[rows, :] = low_c.astype(f32)
        io.send(placed_c_ref, rows)
        return carry

    lax.fori_loop(0, TILES, tile, 0)
    add_sums(sums_ref, gln_ref, 4)


def place_rows(meta, *refs):
    count = len(refs) // 3
    for n in range(count):
        refs[2 * count + n][...] = refs[n][...].astype(refs[2 * count + n].dtype)


GROUP = 8


def position(meta):
    r = meta[35]
    return lax.rem(r, 2), r // 2


def join(own, other, rows):
    return (own[rows, :].astype(f32) + other[rows, :].astype(f32)).astype(bf16)


def join_halves(meta, own, other, keep, send):
    y, _ = position(meta)
    size = keep.shape[0]
    keep[...] = join(own, other, rows_of(y, size))
    send[...] = join(own, other, rows_of(1 - y, size))


def join_chunks(meta, kept, arrived, keep, sends):
    _, z = position(meta)
    size = keep.shape[0]
    keep[...] = join(kept, arrived, rows_of(z, size))
    for s, (send, first) in enumerate(sends, 1):
        send[first : first + size, :] = join(kept, arrived, rows_of(z ^ s, size))


def add_up(kept, parts, first):
    size = kept.shape[0]
    total = kept[...].astype(f32)
    for part in parts:
        total = total + part[first : first + size, :].astype(f32)
    return total.astype(bf16)


def half_of(meta, total, parts, first, half):
    _, z = position(meta)
    size = total.shape[0]
    half[rows_of(z, size), :] = total[...]
    for s, part in enumerate(parts, 1):
        half[rows_of(z ^ s, size), :] = part[first : first + size, :]


def slot_1(meta, ffn_own, ffn_other, keep, send):
    join_halves(meta, ffn_own, ffn_other, keep, send)


def slot_2(
    meta, ffn_kept, ffn_arrived, cross_own, cross_other, ffn_keep, f1, f2, f3, keep, send
):
    join_chunks(meta, ffn_kept, ffn_arrived, ffn_keep, [(f1, 0), (f2, 0), (f3, 0)])
    join_halves(meta, cross_own, cross_other, keep, send)


def slot_3(
    meta, ffn_kept, f1, f2, f3, cross_kept, cross_arrived, self_own, self_other,
    ffn_total, cross_keep, m1, m2, m3, self_keep, self_send,
):
    join_halves(meta, self_own, self_other, self_keep, self_send)
    total = add_up(ffn_kept, (f1, f2, f3), 0)
    ffn_total[...] = total
    size = total.shape[0]
    join_chunks(meta, cross_kept, cross_arrived, cross_keep, [(m, size) for m in (m1, m2, m3)])
    for m in (m1, m2, m3):
        m[0:size, :] = total


def slot_4(
    meta, ffn_total, m1, m2, m3, cross_kept, self_kept, self_arrived,
    ffn_half, cross_total, self_keep, *sends,
):
    join_chunks(meta, self_kept, self_arrived, self_keep, [(send, 0) for send in sends])
    total = add_up(cross_kept, (m1, m2, m3), ffn_total.shape[0])
    cross_total[...] = total
    size = total.shape[0]
    for send in sends:
        send[size:, :] = total
    half_of(meta, ffn_total, (m1, m2, m3), 0, ffn_half)


def slot_5(meta, self_kept, cross_total, m1, m2, m3, gln_own, gln_other, send, cross_half):
    size = self_kept.shape[0]
    total = add_up(self_kept, (m1, m2, m3), 0)
    gln = gln_own[...] + gln_other[...]
    gln = jnp.concatenate([gln, jnp.zeros((8, D), f32)], axis=0).astype(bf16)
    for r in range(GROUP):
        send[r, 0:size, :] = total
        send[r, size : size + 16, :] = gln
    half_of(meta, cross_total, (m1, m2, m3), size, cross_half)


def unpack_attention(whole_ref, outs):
    for i in range(3):
        outs[i][...] = whole_ref[:, 128 * i : 128 * i + 128].astype(f32)
    for j in range(4):
        rows = slice(128 * j, 128 * j + 128)
        outs[3][:, rows] = whole_ref[rows, 384:512].astype(f32)


def unpack_ffn(meta, half, arrived, out_in, out_out, ffn_whole):
    y, _ = position(meta)
    ffn_whole[rows_of(y, 512), :] = half[...]
    ffn_whole[rows_of(1 - y, 512), :] = arrived[...]
    out_in[...] = ffn_whole[0:512, :].astype(f32)
    out_out[...] = ffn_whole[512:1024, :].astype(f32)


def unpack_rest(meta, cross_half, cross_arrived, parts, *refs):
    *outs, whole_ref = refs
    y, _ = position(meta)
    whole_ref[rows_of(y, 256), :] = cross_half[...]
    whole_ref[rows_of(1 - y, 256), :] = cross_arrived[...]
    unpack_attention(whole_ref, outs[0:4])
    size = parts.shape[1] - 16
    total = parts[0, size : size + 16, :].astype(f32)
    for r in range(1, GROUP):
        total = total + parts[r, size : size + 16, :].astype(f32)
    for n in range(8):
        outs[8 + n][...] = total[n : n + 1]
    for r in range(GROUP):
        first = size * (4 * (r % 2) + r // 2)
        whole_ref[first : first + size, :] = parts[r, 0:size, :]
    unpack_attention(whole_ref, outs[4:8])


def whole(shape):
    zeros = (0,) * len(shape)
    return pl.BlockSpec(shape, lambda d, meta: zeros)


def own_row(width):
    return pl.BlockSpec((SEQ, width), lambda d, meta: (meta[0], 0))


ANY = pl.BlockSpec(memory_space=pl.ANY)


def in_hbm(x):
    return pltpu.with_memory_space_constraint(x, pltpu.HBM)


probability_out = (pltpu.HBM((DOCS, 4, FAST_K, FAST_Q), bf16), None, ANY)
probability_scratch = [
    pltpu.VMEM((2, TOGETHER, 4, FAST_K, FAST_Q), bf16),
    pltpu.SemaphoreType.DMA((2,)),
]


class Copies:
    def __init__(self, meta):
        self.first = meta[0] * SEQ
        self.loads = {}
        self.tiles = []
        self.sends = []

    def load(self, stage, source, target, sems, own_row):
        if stage == "fresh":
            stage = "now"
        if stage == "tiles":
            first = self.first if own_row else 0
            self.tiles.append((source, target, sems, first))
            return
        if own_row:
            source = source.at[pl.ds(pl.multiple_of(self.first, SEQ), SEQ)]
        copy = pltpu.make_async_copy(source, target, sems[0].at[sems[1], 0])
        self.loads.setdefault(stage, []).append(copy)

    def tile(self, entry, i):
        source, target, (sems, b), first = entry
        rows = pl.ds(pl.multiple_of(first + i * TILE, TILE), TILE)
        return pltpu.make_async_copy(source.at[rows], target.at[rows_of(i)], sems.at[b, i])

    def start(self):
        for copy in self.loads.get("now", []):
            copy.start()
        for i in range(TILES):
            for entry in self.tiles:
                self.tile(entry, i).start()
        for stage in ("soon", "late"):
            for copy in self.loads.get(stage, []):
                copy.start()

    def wait(self, stage):
        for copy in self.loads.pop(stage, []):
            copy.wait()

    def wait_rows(self, i):
        for entry in self.tiles:
            self.tile(entry, i).wait()

    def result(self, source, target, sem, own_row):
        self.sends.append([source, target, sem, own_row, False])

    def send(self, ref, rows=None):
        for entry in self.sends:
            source, target, sem, own_row, _ = entry
            if source is ref:
                entry[4] = True
                first = self.first if own_row else 0
                if rows is None:
                    size = source.shape[0]
                else:
                    source = source.at[rows]
                    first, size = first + rows.start, rows.size
                if rows is not None or own_row:
                    target = target.at[pl.ds(pl.multiple_of(first, size), size)]
                pltpu.make_async_copy(source, target, sem).start()

    def finish(self):
        for stage in list(self.loads):
            self.wait(stage)
        for source, _, _, _, started in self.sends:
            if not started:
                self.send(source)
        for source, target, sem, own_row, _ in self.sends:
            if own_row:
                target = target.at[pl.ds(pl.multiple_of(self.first, SEQ), SEQ)]
            pltpu.make_async_copy(source, target, sem).wait()


def out(shape, dtype, own_row=False):
    return (shape, dtype, own_row)


def call(kernel, name, operands, outs, scratch, flops, token=None):
    arrays = [operands[0][0]]
    in_specs, out_specs, out_shapes = [], [], []
    buffers = []
    loads = []
    for n, (x, how) in enumerate(operands[1:]):
        if isinstance(how, str):
            stage, _, row = how.partition("_")
            shape = ((SEQ,) + x.shape[1:]) if row else x.shape
            loads.append((n, stage, len(buffers), bool(row)))
            buffers.append(pltpu.VMEM(shape, x.dtype))
            arrays.append(x if stage == "fresh" else in_hbm(x))
            in_specs.append(ANY)
        else:
            arrays.append(x)
            in_specs.append(how)
    results = []
    for n, (shape, dtype, how) in enumerate(outs):
        if isinstance(how, bool):
            results.append((n, len(buffers), how))
            buffers.append(pltpu.VMEM(shape, dtype))
            shape = ((2 * SEQ,) + shape[1:]) if how else shape
            out_shapes.append(pltpu.HBM(shape, dtype))
            out_specs.append(ANY)
        else:
            out_shapes.append(jax.ShapeDtypeStruct(shape, dtype) if dtype else shape)
            out_specs.append(how)
    n_in, n_out = len(in_specs), len(out_specs)
    if token is not None:
        arrays.append(token)
        in_specs.append(whole((8, 128)))
        out_specs.append(whole((8, 128)))
        out_shapes.append(jax.ShapeDtypeStruct((8, 128), f32))

    def body(meta, *refs):
        ins, refs = list(refs[:n_in]), refs[len(in_specs) - n_in + n_in :]
        results_out, refs = list(refs[:n_out]), refs[n_out:]
        if token is not None:
            token_out, refs = refs[0], refs[1:]
            token_out[...] = jnp.zeros_like(token_out)
        bufs, refs = refs[: len(buffers)], refs[len(buffers) :]
        rest = refs[: len(scratch)]
        copies = Copies(meta)
        if buffers:
            sems = refs[len(scratch)]
        for n, stage, b, row in loads:
            copies.load(stage, ins[n], bufs[b], (sems, b), row)
            ins[n] = bufs[b]
        for n, b, row in results:
            copies.result(bufs[b], results_out[n], sems.at[b, 0], row)
            results_out[n] = bufs[b]
        copies.start()
        copies.wait("now")
        if buffers:
            kernel(meta, copies, *ins, *results_out, *rest)
        else:
            kernel(meta, *ins, *results_out, *rest)
        copies.finish()

    moved = sum(x.size * x.dtype.itemsize for x in arrays[1:])
    sems = [pltpu.SemaphoreType.DMA((len(buffers), TILES))] if buffers else []
    return pl.pallas_call(
        body,
        name=name,
        grid_spec=pltpu.PrefetchScalarGridSpec(
            num_scalar_prefetch=1,
            grid=(1,),
            in_specs=in_specs,
            out_specs=out_specs,
            scratch_shapes=buffers + scratch + sems,
        ),
        out_shape=out_shapes,
        compiler_params=pltpu.CompilerParams(
            dimension_semantics=("arbitrary",), vmem_limit_bytes=40 * 1024 * 1024
        ),
        cost_estimate=pl.CostEstimate(
            flops=int(flops), bytes_accessed=int(moved), transcendentals=0
        ),
    )(*arrays)


def simple(kernel, name, meta, operands, outs, scratch=()):
    return pl.pallas_call(
        kernel,
        name=name,
        grid_spec=pltpu.PrefetchScalarGridSpec(
            num_scalar_prefetch=1,
            grid=(1,),
            in_specs=[whole(x.shape) for x in operands],
            out_specs=[whole(shape) for shape, _ in outs],
            scratch_shapes=scratch,
        ),
        out_shape=[jax.ShapeDtypeStruct(shape, dtype) for shape, dtype in outs],
        compiler_params=pltpu.CompilerParams(vmem_limit_bytes=16 * 1024 * 1024),
    )(meta, *operands)


def full(x):
    return (x, whole(x.shape))


def shards(
    query_stream,
    content_stream,
    memory,
    segment_ids,
    source_segments,
    context_rank,
    context_limit,
    padding,
    ln_query_gain,
    ln_query_bias,
    ln_content_gain,
    ln_content_bias,
    self_query,
    self_key,
    self_value,
    self_out,
    ln_cross_gain,
    ln_cross_bias,
    cross_query,
    cross_key,
    cross_value,
    cross_out,
    ln_ffn_gain,
    ln_ffn_bias,
    ffn_in,
    ffn_out,
    cotangent,
):
    core = lax.axis_index("heads") % 2

    def to_core(x):
        return lax.ppermute(x, "heads", [(h, h ^ 1) for h in range(4)])

    hold = lambda *xs: lax.optimization_barrier(xs)

    def to_chip(x):
        return lax.ppermute(x, "heads", [(h, h ^ 2) for h in range(4)])

    row = pl.BlockSpec((1, 8, 128), lambda d, core: (core[0], 0, 0))

    def token_row(x):
        return (in_hbm(x.reshape(2, 8, 128)), row)

    def fixed(x):
        zeros = (0,) * x.ndim
        return (in_hbm(x), pl.BlockSpec(x.shape, lambda d, core: zeros))

    prepared = [
        ((36,), jnp.int32, pl.BlockSpec(memory_space=pltpu.SMEM)),
        ((1, SEQ), f32, whole((1, SEQ))),
        ((1, SEQ), f32, whole((1, SEQ))),
        ((8, D), f32, whole((8, D))),
        ((D, D), bf16, whole((D, D))),
        ((D, D), bf16, whole((D, D))),
    ]
    gains = (
        ln_query_gain,
        ln_query_bias,
        ln_content_gain,
        ln_content_bias,
        ln_cross_gain,
        ln_cross_bias,
        ln_ffn_gain,
        ln_ffn_bias,
    )
    weights = (self_query, self_key, self_value, self_out)
    weights += (cross_query, cross_key, cross_value, cross_out)
    tokens = (segment_ids, source_segments, context_rank, context_limit, padding)
    meta, rank, limit, norms, ws0, wc0 = call(
        prepare,
        "prepare",
        [(jnp.stack([core, lax.axis_index("rows") % GROUP]).astype(jnp.int32), None)]
        + [token_row(x) for x in tokens]
        + [fixed(x.reshape(1, D)) for x in gains]
        + [fixed(x) for x in weights],
        prepared,
        [],
        0,
    )

    ws1 = to_core(ws0)
    ws2 = to_chip(ws0)
    wc1 = to_core(wc0)
    u0, v0 = ffn_in, ffn_out
    meta_in = (meta, None)

    heads_out = [out((SEQ, 256), bf16)] * 4

    def stream_out(dtype, own_row=False):
        return out((SEQ, D), dtype, own_row)

    def now(*xs):
        return [(x, "now") for x in xs]

    def fresh(*xs):
        return [(x, "fresh") for x in xs]

    def soon(*xs):
        return [(x, "soon") for x in xs]

    def late(*xs):
        return [(x, "late") for x in xs]

    def small(*xs):
        return [(x, whole(x.shape)) for x in xs]

    limits = pltpu.VMEM((SEQ, 128), f32)
    pair_flops = 2 * SEQ * D * 768 + 2 * 2 * 4 * DOCS * FAST_Q * FAST_K * 256

    nq, nc, *first, token = call(
        self_first,
        "self_first",
        [meta_in, (query_stream, "tiles_row"), (content_stream, "tiles_row")]
        + small(rank, limit, norms)
        + fresh(ws0, ws1),
        [stream_out(bf16), stream_out(bf16)] + heads_out + [probability_out],
        [limits] + probability_scratch,
        pair_flops,
        jnp.zeros((8, 128), f32),
    )
    ws2, wc0, u0, token = hold(ws2, wc0, u0, token)
    ws3 = to_core(ws2)
    wc2 = to_chip(wc0)
    u2 = to_chip(u0)
    *second_heads, second, ncross, token = call(
        self_second,
        "self_second",
        [meta_in, (query_stream, "late_row")]
        + [(nq, "tiles"), (nc, "tiles")]
        + small(rank, limit, norms)
        + late(ws0, ws1)
        + fresh(ws2, ws3)
        + late(first[3]),
        heads_out + [probability_out, stream_out(bf16), stream_out(bf16)],
        [limits] + probability_scratch,
        pair_flops + 2 * SEQ * D * D,
        token,
    )
    u0, token = hold(u0, token)
    u1 = to_core(u0)
    *cross_heads, token = call(
        cross_first,
        "cross_first",
        [meta_in, (ncross, "tiles"), (memory, "tiles_row")] + fresh(wc0, wc1),
        heads_out + [probability_out],
        probability_scratch,
        pair_flops,
        token,
    )
    wc2, u2, v0, token = hold(wc2, u2, v0, token)
    wc3 = to_core(wc2)
    u3 = to_core(u2)
    v2 = to_chip(v0)
    v1 = to_core(v0)
    *cross_heads_second, third, nffn, token = call(
        cross_second,
        "cross_second",
        [meta_in]
        + late(second)
        + [(ncross, "tiles"), (memory, "tiles_row")]
        + small(norms)
        + late(wc0, wc1)
        + fresh(wc2, wc3)
        + late(cross_heads[3]),
        heads_out
        + [probability_out, ((SEQ, D), f32, whole((SEQ, D))), ((SEQ, D), bf16, whole((SEQ, D)))],
        probability_scratch,
        pair_flops + 2 * SEQ * D * D,
        token,
    )
    u3, v2, token = hold(u3, v2, token)
    v3 = to_core(v2)
    grads_ln = ((8, D), f32, whole((8, D)))
    placed_output, output, g3_low, gln_ffn, ffn_own, ffn_other, token = call(
        ffn_both,
        "ffn_both",
        [meta_in]
        + small(third, nffn)
        + [(cotangent, "tiles_row")]
        + small(norms)
        + now(u0) + fresh(u1, u2, u3) + now(v0) + fresh(v1, v2, v3),
        [
            stream_out(bf16, True),
            stream_out(bf16),
            stream_out(bf16),
            grads_ln,
            out((1024, D), bf16),
            out((1024, D), bf16),
        ],
        [pltpu.VMEM((SEQ, 1024), bf16), pltpu.VMEM((SEQ, 1024), bf16), pltpu.VMEM((16, D), f32)],
        12 * SEQ * D * 2048,
        token,
    )

    def both_rows(placed_own, others, name):
        count = len(others)
        size = SEQ // 2
        one = pl.BlockSpec((size, D), lambda i, meta: (i, 0))
        block = pl.BlockSpec((size, D), lambda i, meta: (2 * (1 - meta[0]) + i, 0))
        return pl.pallas_call(
            place_rows,
            name=name,
            grid_spec=pltpu.PrefetchScalarGridSpec(
                num_scalar_prefetch=1,
                grid=(2,),
                in_specs=[one] * count + [pl.BlockSpec(memory_space=pl.ANY)] * count,
                out_specs=[block] * count,
            ),
            out_shape=[jax.ShapeDtypeStruct(x.shape, x.dtype) for x in placed_own],
            input_output_aliases={1 + count + n: n for n in range(count)},
        )(meta, *others, *placed_own)

    row_count = lax.axis_size("rows")
    assert row_count % GROUP == 0

    def along_rows(x, s):
        return lax.ppermute(x, "rows", [(r, r ^ s) for r in range(row_count)])

    def to_y(x):
        return along_rows(x, 1)

    def to_z(sends):
        return [along_rows(x, 2 * s) for s, x in enumerate(sends, 1)]

    def rows_out(*sizes):
        return [((n, D), bf16) for n in sizes]

    ffn_other = to_core(ffn_other)
    output_other = to_core(output)

    back_scratch = [pltpu.VMEM((SEQ, 256), bf16)] + [pltpu.VMEM((SEQ, 256), f32)] * 3
    back_scratch += probability_scratch
    pair_out = out((SEQ, 256), bf16)
    packed_outs = [((D, D), bf16, whole((D, D)))] * 2
    back_flops = 2 * SEQ * D * 256 + 4 * 2 * 4 * DOCS * FAST_Q * FAST_K * 256

    def head_inputs(natural, p):
        return soon(*natural) + [(in_hbm(p), ANY)]

    *cross_grads, cross_own, cross_other, token = call(
        functools.partial(attention_back_first, True),
        "cross_back_first",
        [meta_in]
        + [(g3_low, "tiles")]
        + late(ncross)
        + [(memory, "late_row")]
        + small(rank, limit)
        + now(wc0, wc1)
        + head_inputs(cross_heads[0:4], cross_heads[4]),
        [pair_out] * 3 + packed_outs,
        [limits] + back_scratch,
        back_flops + 2 * SEQ * D * 1024,
        token,
    )
    ffn_other, output_other, token = hold(ffn_other, output_other, token)
    ffn_keep, ffn_send = simple(slot_1, "slot_1", meta, [ffn_own, ffn_other], rows_out(512, 512))
    ffn_send, token = hold(ffn_send, token)
    ffn_arrived = to_y(ffn_send)
    cross_other = to_core(cross_other)
    g2_low, placed_mem, grad_mem, gln_cross, token = call(
        cross_back_second,
        "cross_back_second",
        [meta_in]
        + [(g3_low, "tiles")]
        + late(second)
        + small(norms)
        + late(wc0, wc1)
        + now(wc2, wc3)
        + late(*cross_grads)
        + head_inputs(cross_heads_second[0:4], cross_heads_second[4]),
        [stream_out(bf16), stream_out(f32, True), stream_out(bf16), grads_ln],
        back_scratch + [pltpu.VMEM((16, D), f32)],
        back_flops + 2 * SEQ * D * 1536,
        token,
    )
    ffn_arrived, cross_other, token = hold(ffn_arrived, cross_other, token)
    ffn_keep, *sends, cross_keep, cross_send = simple(
        slot_2,
        "slot_2",
        meta,
        [ffn_keep, ffn_arrived, cross_own, cross_other],
        rows_out(128, 128, 128, 128, 256, 256),
    )
    ffn_keep, cross_send, token = hold(ffn_keep, cross_send, token)
    ffn_parts = to_z(sends)
    cross_arrived = to_y(cross_send)

    *self_grads, self_own, self_other, token = call(
        functools.partial(attention_back_first, False),
        "self_back_first",
        [meta_in]
        + [(g2_low, "tiles")]
        + late(nq, nc)
        + small(rank, limit)
        + now(ws0, ws1)
        + head_inputs(first[0:4], first[4]),
        [pair_out] * 3 + packed_outs,
        [limits] + back_scratch,
        back_flops + 2 * SEQ * D * 1024,
        token,
    )
    *ffn_parts, cross_arrived, self_other, token = hold(
        *ffn_parts, cross_arrived, self_other, token
    )
    self_other = to_core(self_other)
    ffn_total, cross_keep, *sends, self_keep, self_send = simple(
        slot_3,
        "slot_3",
        meta,
        [ffn_keep, *ffn_parts, cross_keep, cross_arrived, self_own, self_other],
        rows_out(128, 64, 192, 192, 192, 256, 256),
    )
    ffn_total, self_send, grad_mem, token = hold(ffn_total, self_send, grad_mem, token)
    mem_other = to_core(grad_mem)
    self_arrived = to_y(self_send)
    messages = to_z(sends)
    *self_grads_second, token = call(
        self_back_second,
        "self_back_second",
        [meta_in, (g2_low, "tiles")]
        + small(rank, limit)
        + now(ws2, ws3)
        + head_inputs(second_heads[0:4], second_heads[4]),
        [((SEQ, 256), bf16, whole((SEQ, 256)))] * 3,
        [limits] + back_scratch,
        back_flops,
        token,
    )
    *messages, self_arrived, mem_other, token = hold(*messages, self_arrived, mem_other, token)
    ffn_half, cross_total, self_keep, *sends = simple(
        slot_4,
        "slot_4",
        meta,
        [ffn_total, *messages, cross_keep, self_keep, self_arrived],
        rows_out(512, 64, 64, 128, 128, 128),
    )
    cross_total, ffn_half, token = hold(cross_total, ffn_half, token)
    messages = to_z(sends)
    ffn_arrived = to_y(ffn_half)
    placed_q, placed_c, gq, gc, gln_self, token = call(
        self_back_finish,
        "self_back_finish",
        [meta_in, (g2_low, "tiles"), (query_stream, "tiles_row"), (content_stream, "tiles_row")]
        + small(norms)
        + now(ws0, ws1, ws2, ws3)
        + [(x, "tiles") for x in self_grads]
        + small(*self_grads_second),
        [stream_out(f32, True)] * 2 + [((SEQ, D), bf16, whole((SEQ, D)))] * 2 + [grads_ln],
        [pltpu.VMEM((32, D), f32)],
        2 * SEQ * D * 1536,
        token,
    )
    gln = jnp.concatenate([gln_self[0:4], gln_cross[0:2], gln_ffn[0:2]], axis=0)
    gln_other = to_core(gln)
    *messages, ffn_arrived, gln_ffn = hold(*messages, ffn_arrived, gln_ffn)
    last_send, cross_half = simple(
        slot_5,
        "slot_5",
        meta,
        [self_keep, cross_total, *messages, gln, gln_other],
        [((GROUP, 80, D), bf16), ((256, D), bf16)],
    )
    groups = None
    if row_count > GROUP:
        groups = [list(range(r, r + GROUP)) for r in range(0, row_count, GROUP)]
    def gather(x):
        return lax.all_to_all(x, "rows", 0, 0, axis_index_groups=groups)

    last_parts = gather(last_send)
    cross_arrived = to_y(cross_half)
    def over_groups(totals):
        if row_count == GROUP:
            return totals
        groups = [list(range(r, row_count, GROUP)) for r in range(GROUP)]
        return lax.psum(totals, "rows", axis_index_groups=groups)

    gq_both, gc_both = both_rows([placed_q, placed_c], [to_core(gq), to_core(gc)], "place_late")

    grad_ffn_in, grad_ffn_out = simple(
        unpack_ffn,
        "unpack_ffn",
        meta,
        [ffn_half, ffn_arrived],
        [((D, D), f32)] * 2,
        [pltpu.VMEM((2 * D, D), bf16)],
    )
    attention_outs = [((512, 128), f32)] * 3 + [((128, 512), f32)]
    out_both, grad_mem_both = both_rows(
        [placed_output, placed_mem], [output_other, mem_other], "place_early"
    )
    cross_arrived, gq_both, out_both, grad_ffn_in = hold(
        cross_arrived, gq_both, out_both, grad_ffn_in
    )
    parts = simple(
        unpack_rest,
        "unpack_rest",
        meta,
        [cross_half, cross_arrived, last_parts],
        attention_outs * 2 + [((1, D), f32)] * 8,
        [pltpu.VMEM((D, D), bf16)],
    )
    grad_cross_parts, grad_self_parts = parts[0:4], parts[4:8]
    gln = [x.reshape(D) for x in parts[8:16]]
    grad_ffn_in, grad_ffn_out, grad_cross_parts, grad_self_parts, gln = over_groups(
        (grad_ffn_in, grad_ffn_out, grad_cross_parts, grad_self_parts, gln)
    )
    return (
        out_both,
        gq_both,
        gc_both,
        grad_mem_both,
        gln[0],
        gln[1],
        gln[2],
        gln[3],
        *grad_self_parts,
        gln[4],
        gln[5],
        *grad_cross_parts,
        gln[6],
        gln[7],
        grad_ffn_in,
        grad_ffn_out,
    )


def solution(mesh):
    assert mesh.shape["heads"] == 4
    row_spec = P("rows", None)
    flat = P("rows")
    by_column = P(None, "heads")
    by_row = P("heads", None)
    attention = (by_column, by_column, by_column, by_row)
    in_specs = (
        (row_spec,) * 3
        + (flat,) * 5
        + (P(),) * 4
        + attention
        + (P(),) * 2
        + attention
        + (P(),) * 2
        + (by_column, by_row, row_spec)
    )
    out_specs = (
        (row_spec,) * 4
        + (P(),) * 4
        + attention
        + (P(),) * 2
        + attention
        + (P(),) * 2
        + (by_column, by_row)
    )
    return jax.shard_map(shards, mesh=mesh, in_specs=in_specs, out_specs=out_specs, check_vma=False)
```

```python
import functools

import jax
import jax.numpy as jnp
from jax import lax
from jax.experimental import pallas as pl
from jax.experimental.pallas import tpu as pltpu
from jax.sharding import PartitionSpec as P

HEAD_DIM = 64
SEQ = 1024
DOCS = 8
D = 512
TILE = 256
TILES = SEQ // TILE
FAST_Q = 256
FAST_K = 208
LONG_Q = 128
LONG_K = 640

norm_eps = 1e-05
masked_score = -1e30
hidden_rank = 1e6
gelu_root = 0.7978845608028654
gelu_cube = 0.044715

f32 = jnp.float32
bf16 = jnp.bfloat16


def dot(a, b):
    return lax.dot_general(a, b, (((1,), (0,)), ((), ())), preferred_element_type=f32)


def dot_nt(a, b):
    return lax.dot_general(a, b, (((1,), (1,)), ((), ())), preferred_element_type=f32)


def dot_tn(a, b):
    return lax.dot_general(a, b, (((0,), (0,)), ((), ())), preferred_element_type=f32)


def lanes(parts):
    return jnp.concatenate(parts, axis=1)


NORM_ROWS = 32


def layer_norm(values, gain, shift):
    def piece(part):
        part = part.astype(f32)
        centre = part - jnp.mean(part, axis=-1, keepdims=True)
        spread = jnp.mean(centre * centre, axis=-1, keepdims=True)
        return (centre * lax.rsqrt(spread + norm_eps) * gain + shift).astype(bf16)

    return by_pieces(piece, NORM_ROWS, 0, values)


def eight_rows(values):
    return sum(values[8 * i : 8 * i + 8] for i in range(1, values.shape[0] // 8)) + values[0:8]


def norm_backward(values, gain, grad, sums_ref, first):
    sums = []

    def piece(part, grad_part):
        part = part.astype(f32)
        centre = part - jnp.mean(part, axis=-1, keepdims=True)
        spread = jnp.mean(centre * centre, axis=-1, keepdims=True)
        scale = lax.rsqrt(spread + norm_eps)
        xhat = centre * scale
        eg = grad_part * gain
        mean_eg = jnp.mean(eg, axis=-1, keepdims=True)
        mean_egx = jnp.mean(eg * xhat, axis=-1, keepdims=True)
        sums.append((eight_rows(grad_part * xhat), eight_rows(grad_part)))
        return scale * (eg - mean_eg - xhat * mean_egx)

    result = by_pieces(piece, NORM_ROWS, 0, values, grad)
    for n, parts in enumerate(zip(*sums)):
        sums_ref[first + 8 * n : first + 8 * n + 8, :] += sum(parts[1:], parts[0])
    return result


def add_sums(sums_ref, gln_ref, count):
    gln_ref[...] = jnp.zeros_like(gln_ref)
    for n in range(count):
        gln_ref[n : n + 1, :] = jnp.sum(sums_ref[8 * n : 8 * n + 8, :], axis=0, keepdims=True)


def by_pieces(work, size, axis, *arrays):
    count = arrays[0].shape[axis] // size
    pieces = []
    for i in range(count):
        cut = (slice(size * i, size * i + size),)
        cut = cut if axis == 0 else (slice(None),) + cut
        pieces.append(work(*[x[cut] for x in arrays]))
    if not isinstance(pieces[0], tuple):
        return jnp.concatenate(pieces, axis=axis)
    return tuple(jnp.concatenate(parts, axis=axis) for parts in zip(*pieces))


def rows_of(i, size=TILE):
    return pl.ds(pl.multiple_of(i * size, size), size)


def w_query(ref):
    return ref[:, 0:128]


def w_key(ref):
    return ref[:, 128:256]


def w_value(ref):
    return ref[:, 256:384]


def w_out(ref):
    return lanes([ref[128 * j : 128 * j + 128, 384:512] for j in range(4)])


def half_masks():
    place = lax.broadcasted_iota(jnp.int32, (1, 128), 1)
    low = jnp.where(place < HEAD_DIM, 1.0, 0.0).astype(f32)
    return (low.astype(bf16), (1.0 - low).astype(bf16))


def doc_bounds(meta, d, source):
    base = 17 if source else 1
    return meta[base + d], meta[base + 8 + d]


def window_of(first, limit):
    return pl.multiple_of(jnp.minimum((first // 16) * 16, limit), 16)


def key_bias(ks, ke, k0, width):
    place = k0 + lax.broadcasted_iota(jnp.int32, (width, 128), 0)
    return jnp.where((place >= ks) & (place < ke), 0.0, masked_score)


def make_bias(rank_ref, limit_ref, ks, ke, q0, k0, span, width):
    if rank_ref is None:
        return lanes([key_bias(ks, ke, k0, width)] * (span // 128))
    place = k0 + lax.broadcasted_iota(jnp.int32, (width, 128), 0)
    ranks = rank_ref[pl.ds(k0, width), :]
    ranks = jnp.where((place < ks + 2) & (ranks < hidden_rank), -1.0, ranks)
    ranks = jnp.where((place >= ks) & (place < ke), ranks, hidden_rank)
    limits = jnp.broadcast_to(limit_ref[...], (8, SEQ))
    limits = pltpu.roll(limits, lax.rem(SEQ - q0, SEQ), 1)[0:1, 0:span]
    row = k0 + lax.broadcasted_iota(jnp.int32, (width, span), 0)
    column = q0 + lax.broadcasted_iota(jnp.int32, (width, span), 1)
    seen = (lanes([ranks] * (span // 128)) < limits) & (row != column)
    return jnp.where(seen, 0.0, masked_score)


TOGETHER = 4
STEPS = DOCS // TOGETHER


LAG = 2


def interleave(items):
    items = [list(phases) for phases in items]
    depth = max(len(phases) for phases in items)
    results = [None] * len(items)
    for tick in range(len(items) + LAG * (depth - 1)):
        for phase in range(depth):
            n = tick - LAG * phase
            if 0 <= n < len(items) and phase < len(items[n]):
                run = items[n][phase]
                results[n] = run() if phase == 0 else run(results[n])
    return results


def by_halves(pairs, phases):
    shared = [{} for _ in range(pairs)]
    return [phases(n, a, shared[n]) for n in range(pairs) for a in range(2)]


def is_fast(meta, cross):
    return meta[34 if cross else 33] == 1


def both_heads(x, masks):
    return jnp.concatenate([x * masks[0], x * masks[1]], axis=0)


def pair_scores(queries, keys, masks):
    return dot_nt(both_heads(keys, masks), queries)


def raised(scores, bias):
    def piece(part, bias_part):
        part = part + bias_part
        return jnp.exp((part - jnp.max(part, axis=0, keepdims=True)).astype(bf16))

    return by_pieces(piece, 128, 1, scores, bias)


def weighted_values(values, parts):
    width = values.shape[1]
    mixed = []
    shares = []
    for a, part in enumerate(parts):
        rows = jnp.concatenate([values[64 * a : 64 * a + 64], jnp.ones((16, width), bf16)], axis=0)
        sums = dot(rows, part)
        share = 1.0 / sums[64:65]
        mixed.append(sums[:64] * share)
        shares.append(part * share.astype(bf16))
    return jnp.concatenate(mixed, axis=0).astype(bf16), shares


def pair_gradient(rows, parts):
    across = jnp.transpose(rows)
    halves = [dot(across[64 * a : 64 * a + 64], part) for a, part in enumerate(parts)]
    return jnp.transpose((jnp.concatenate(halves, axis=0) * HEAD_DIM**-0.5).astype(bf16))


def for_docs(meta, cross, run, before, after):
    @pl.when(is_fast(meta, cross))
    def _():
        def step(i, carry):
            slot = lax.rem(i, 2)
            before(i, slot)
            items = []
            for place in range(TOGETHER):
                d = TOGETHER * i + place
                ts, te = doc_bounds(meta, d, False)
                ks, ke = doc_bounds(meta, d, cross)
                q0 = window_of(ts, SEQ - FAST_Q)
                k0 = window_of(ks, SEQ - FAST_K)
                items += run(d, slot, place, q0, k0, FAST_Q, FAST_K, ts, te, ks, ke, True)
            interleave(items)
            after(i, slot)
            return carry

        lax.fori_loop(0, STEPS, step, 0)

    @pl.when(jnp.logical_not(is_fast(meta, cross)))
    def _():
        def doc(d, carry):
            ts, te = doc_bounds(meta, d, False)
            ks, ke = doc_bounds(meta, d, cross)
            base = (ts // 16) * 16
            k0 = window_of(ks, SEQ - LONG_K)

            def chunk(i, carry):
                lower = base + i * LONG_Q
                q0 = pl.multiple_of(jnp.minimum(lower, SEQ - LONG_Q), 16)
                low = jnp.maximum(ts, lower)
                high = jnp.minimum(te, lower + LONG_Q)
                interleave(run(d, None, None, q0, k0, LONG_Q, LONG_K, low, high, ks, ke, False))
                return carry

            return lax.fori_loop(0, (te - base + LONG_Q - 1) // LONG_Q, chunk, carry)

        lax.fori_loop(0, DOCS, doc, 0)


def attend_docs(meta, cross, rank_ref, limit_ref, halves, p_ref, p_buf, p_sem):
    pairs = 2 * len(halves)
    masks = half_masks()

    def save(i, slot):
        return pltpu.make_async_copy(p_buf.at[slot], p_ref.at[pl.ds(TOGETHER * i, TOGETHER)], p_sem.at[slot])

    def before(i, slot):
        @pl.when(i >= 2)
        def _():
            save(i - 2, slot).wait()

    def after(i, slot):
        save(i, slot).start()

    def run(d, slot, place, q0, k0, span, width, low, high, ks, ke, fast):
        bias = make_bias(rank_ref, limit_ref, ks, ke, q0, k0, span, width)
        row = q0 + lax.broadcasted_iota(jnp.int32, (span, 128), 0)
        inside = (row >= low) & (row < high)

        def phases(n):
            q_ref, k_ref, v_ref, mixed_ref = halves[n // 2]
            cols = slice(128 * (n % 2), 128 * (n % 2) + 128)

            def score():
                return pair_scores(q_ref[pl.ds(q0, span), cols], k_ref[pl.ds(k0, width), cols], masks)

            def weigh(scores):
                return [raised(scores[width * a : width * a + width], bias) for a in range(2)]

            def mix(parts):
                values = jnp.transpose(v_ref[pl.ds(k0, width), cols])
                mixed, parts = weighted_values(values, parts)
                if fast:
                    for a in range(2):
                        p_buf[slot, place, 2 * n + a] = parts[a]
                mixed = jnp.transpose(mixed).astype(f32)
                old = mixed_ref[pl.ds(q0, span), cols].astype(f32)
                mixed_ref[pl.ds(q0, span), cols] = jnp.where(inside, mixed, old).astype(bf16)

            return score, weigh, mix

        return [phases(n) for n in range(pairs)]

    for_docs(meta, cross, run, before, after)

    @pl.when(is_fast(meta, cross))
    def _():
        for i in range(STEPS - 2, STEPS):
            save(i, i % 2).wait()


def load_step(load, i, slot):
    p_ref, p_buf, p_sem = load
    return pltpu.make_async_copy(p_ref.at[pl.ds(TOGETHER * i, TOGETHER)], p_buf.at[slot], p_sem.at[slot])


def start_load(meta, cross, load):
    @pl.when(is_fast(meta, cross))
    def _():
        load_step(load, 0, 0).start()


def attend_docs_back(
    meta, cross, rank_ref, limit_ref, q_ref, k_ref, v_ref, mixed_ref, dm_ref,
    dq_ref, dk_ref, dv_ref, load,
):
    pairs = q_ref.shape[1] // 128
    masks = half_masks()
    p_buf = load[1]

    def before(i, slot):
        @pl.when(i + 1 < STEPS)
        def _():
            load_step(load, i + 1, 1 - slot).start()

        load_step(load, i, slot).wait()

    def after(i, slot):
        pass

    def run(d, slot, place, q0, k0, span, width, low, high, ks, ke, fast):
        row = q0 + lax.broadcasted_iota(jnp.int32, (span, 128), 0)
        inside = jnp.where((row >= low) & (row < high), 1.0, 0.0).astype(bf16)
        ones = jnp.ones((width, 128), bf16)
        if not fast:
            bias = make_bias(rank_ref, limit_ref, ks, ke, q0, k0, span, width)

        def phases(n):
            cols = slice(128 * n, 128 * n + 128)

            def differ():
                values = v_ref[pl.ds(k0, width), cols]
                mixed = mixed_ref[pl.ds(q0, span), cols]
                grad = dm_ref[pl.ds(q0, span), cols] * inside
                left = lanes([grad, -(grad * mixed)])
                right = both_heads(lanes([values, ones]), [lanes([m, m]) for m in masks])
                return grad, dot_nt(right, left)

            def slope(state):
                grad, delta = state
                if fast:
                    parts = [p_buf[slot, place, 2 * n + a] for a in range(2)]
                else:
                    queries = q_ref[pl.ds(q0, span), cols]
                    keys = k_ref[pl.ds(k0, width), cols]
                    scores = pair_scores(queries, keys, masks)
                    parts = [raised(scores[width * a : width * a + width], bias) for a in range(2)]
                    parts = weighted_values(jnp.transpose(v_ref[pl.ds(k0, width), cols]), parts)[1]
                slopes = [
                    by_pieces(
                        lambda part, change: part * change.astype(bf16),
                        16,
                        0,
                        parts[a],
                        delta[width * a : width * a + width],
                    )
                    for a in range(2)
                ]
                return grad, parts, slopes

            def spread(state):
                grad, parts, slopes = state
                queries = q_ref[pl.ds(q0, span), cols]
                dk = dv = None
                for a in range(2):
                    dk_a = dot(slopes[a], queries * masks[a])
                    dv_a = dot(parts[a], grad * masks[a])
                    dk = dk_a if dk is None else dk + dk_a
                    dv = dv_a if dv is None else dv + dv_a
                dq = pair_gradient(k_ref[pl.ds(k0, width), cols], slopes)
                dq_ref[pl.ds(q0, span), cols] += dq.astype(f32)
                dk_ref[pl.ds(k0, width), cols] += dk
                dv_ref[pl.ds(k0, width), cols] += dv

            return differ, slope, spread

        return [phases(n) for n in range(pairs)]

    for_docs(meta, cross, run, before, after)


def spread_ranks(rank_row_ref, rank_ref):
    rank_ref[...] = jnp.transpose(jnp.broadcast_to(rank_row_ref[...], (128, SEQ)))


def prepare(
    core, seg_ref, src_ref, rank_ref, limit_ref, pad_ref,
    n0, n1, n2, n3, n4, n5, n6, n7, sq, sk, sv, so, cq, ck, cv, co,
    meta_ref, ranks_ref, limits_ref, norms_ref, ws_ref, wc_ref,
):
    meta_ref[0] = core[0]
    meta_ref[35] = core[1]
    for base, ref in ((1, seg_ref), (17, src_ref)):
        ids = ref[0]
        meta_ref[base] = 0
        meta_ref[base + 15] = SEQ
        for d in range(1, DOCS):
            cut = jnp.sum(jnp.where(ids < d, 1.0, 0.0)).astype(jnp.int32)
            meta_ref[base + d] = cut
            meta_ref[base + 7 + d] = cut
    for place, base in ((33, 1), (34, 17)):
        fast = jnp.int32(1)
        for d in range(DOCS):
            q0 = window_of(meta_ref[1 + d], SEQ - FAST_Q)
            k0 = window_of(meta_ref[base + d], SEQ - FAST_K)
            fits = (meta_ref[9 + d] - q0 <= FAST_Q) & (meta_ref[base + 8 + d] - k0 <= FAST_K)
            fast = fast & fits.astype(jnp.int32)
        meta_ref[place] = fast
    ranks = jnp.where(pad_ref[0] != 0, hidden_rank, rank_ref[0].astype(f32))
    limits = limit_ref[0].astype(f32)
    for i in range(8):
        ranks_ref[0:1, 128 * i : 128 * i + 128] = ranks[i : i + 1]
        limits_ref[0:1, 128 * i : 128 * i + 128] = limits[i : i + 1]
    for i, ref in enumerate((n0, n1, n2, n3, n4, n5, n6, n7)):
        norms_ref[i : i + 1, :] = ref[...]
    for to, parts, out in ((ws_ref, (sq, sk, sv), so), (wc_ref, (cq, ck, cv), co)):
        for i, part in enumerate(parts):
            to[:, 128 * i : 128 * i + 128] = part[...]
        for j in range(4):
            to[128 * j : 128 * j + 128, 384:512] = out[:, 128 * j : 128 * j + 128]


def self_first(
    meta, io, xq_ref, xc_ref, rank_row_ref, limit_ref, norms_ref, w0_ref, w1_ref,
    nq_ref, nc_ref, q_ref, k_ref, v_ref, mixed_ref, p_ref, rank_ref, p_buf, p_sem,
):

    spread_ranks(rank_row_ref, rank_ref)
    wq = lanes([w_query(w0_ref), w_query(w1_ref)])
    wkv = lanes([w_key(w0_ref), w_key(w1_ref), w_value(w0_ref), w_value(w1_ref)])

    def tile(i, carry):
        rows = rows_of(i)
        io.wait_rows(i)
        nq = layer_norm(xq_ref[rows, :], norms_ref[0:1], norms_ref[1:2])
        nc = layer_norm(xc_ref[rows, :], norms_ref[2:3], norms_ref[3:4])
        nq_ref[rows, :] = nq
        nc_ref[rows, :] = nc
        q_ref[rows, :] = (dot(nq, wq) * (HEAD_DIM**-0.5)).astype(bf16)
        kv = dot(nc, wkv).astype(bf16)
        k_ref[rows, :] = kv[:, :256]
        v_ref[rows, :] = kv[:, 256:]
        return carry

    lax.fori_loop(0, TILES, tile, 0)

    for ref in (nq_ref, nc_ref, q_ref, k_ref, v_ref):
        io.send(ref)
    attend_docs(meta, False, rank_ref, limit_ref, [(q_ref, k_ref, v_ref, mixed_ref)], p_ref, p_buf, p_sem)


def self_second(
    meta, io, xq_ref, nq_ref, nc_ref, rank_row_ref, limit_ref, norms_ref, w0_ref, w1_ref, w2_ref, w3_ref,
    mixed_first_ref,
    q_ref, k_ref, v_ref, mixed_ref, p_ref, second_ref, ncross_ref, rank_ref, p_buf, p_sem,
):

    spread_ranks(rank_row_ref, rank_ref)
    wq = lanes([w_query(w2_ref), w_query(w3_ref)])
    wkv = lanes([w_key(w2_ref), w_key(w3_ref), w_value(w2_ref), w_value(w3_ref)])

    def tile(i, carry):
        rows = rows_of(i)
        io.wait_rows(i)
        q_ref[rows, :] = (dot(nq_ref[rows, :], wq) * (HEAD_DIM**-0.5)).astype(bf16)
        kv = dot(nc_ref[rows, :], wkv).astype(bf16)
        k_ref[rows, :] = kv[:, :256]
        v_ref[rows, :] = kv[:, 256:]
        return carry

    lax.fori_loop(0, TILES, tile, 0)

    for ref in (q_ref, k_ref, v_ref):
        io.send(ref)
    attend_docs(meta, False, rank_ref, limit_ref, [(q_ref, k_ref, v_ref, mixed_ref)], p_ref, p_buf, p_sem)

    io.send(mixed_ref)
    io.wait("late")
    out_first = jnp.concatenate([w_out(w0_ref), w_out(w1_ref)], axis=0)
    out_second = jnp.concatenate([w_out(w2_ref), w_out(w3_ref)], axis=0)

    def tile(i, carry):
        rows = rows_of(i)
        branch = dot(mixed_first_ref[rows, :], out_first) + dot(mixed_ref[rows, :], out_second)
        second = xq_ref[rows, :].astype(f32) + branch
        second_ref[rows, :] = second.astype(bf16)
        io.send(second_ref, rows)
        ncross_ref[rows, :] = layer_norm(second, norms_ref[4:5], norms_ref[5:6])
        io.send(ncross_ref, rows)
        return carry

    lax.fori_loop(0, TILES, tile, 0)


def project_cross(io, ncross_ref, memory_ref, weights, q_ref, k_ref, v_ref):
    wq = lanes([w_query(w) for w in weights])
    wkv = lanes([w_key(w) for w in weights] + [w_value(w) for w in weights])

    def tile(i, carry):
        rows = rows_of(i)
        io.wait_rows(i)
        q_ref[rows, :] = (dot(ncross_ref[rows, :], wq) * (HEAD_DIM**-0.5)).astype(bf16)
        kv = dot(memory_ref[rows, :], wkv).astype(bf16)
        k_ref[rows, :] = kv[:, :256]
        v_ref[rows, :] = kv[:, 256:]
        return carry

    lax.fori_loop(0, TILES, tile, 0)
    for ref in (q_ref, k_ref, v_ref):
        io.send(ref)


def cross_first(
    meta, io, ncross_ref, memory_ref, w0_ref, w1_ref,
    q_ref, k_ref, v_ref, mixed_ref, p_ref, p_buf, p_sem,
):
    project_cross(io, ncross_ref, memory_ref, (w0_ref, w1_ref), q_ref, k_ref, v_ref)
    attend_docs(meta, True, None, None, [(q_ref, k_ref, v_ref, mixed_ref)], p_ref, p_buf, p_sem)


def cross_second(
    meta, io, second_ref, ncross_ref, memory_ref, norms_ref, w0_ref, w1_ref, w2_ref, w3_ref,
    mixed_first_ref,
    q_ref, k_ref, v_ref, mixed_ref, p_ref, third_ref, nffn_ref, p_buf, p_sem,
):
    project_cross(io, ncross_ref, memory_ref, (w2_ref, w3_ref), q_ref, k_ref, v_ref)
    attend_docs(meta, True, None, None, [(q_ref, k_ref, v_ref, mixed_ref)], p_ref, p_buf, p_sem)
    io.send(mixed_ref)
    io.wait("late")
    out_first = jnp.concatenate([w_out(w0_ref), w_out(w1_ref)], axis=0)
    out_second = jnp.concatenate([w_out(w2_ref), w_out(w3_ref)], axis=0)

    def tile(i, carry):
        rows = rows_of(i)
        branch = dot(mixed_first_ref[rows, :], out_first) + dot(mixed_ref[rows, :], out_second)
        third = second_ref[rows, :].astype(f32) + branch
        third_ref[rows, :] = third
        nffn_ref[rows, :] = layer_norm(third, norms_ref[6:7], norms_ref[7:8])
        return carry

    lax.fori_loop(0, TILES, tile, 0)


def ffn_both(
    meta, io, third_ref, nffn_ref, cot_ref, norms_ref, u0_ref, u1_ref, u2_ref, u3_ref,
    w0_ref, w1_ref, w2_ref, w3_ref,
    placed_ref, out_ref, g3_low_ref, gln_ref, own_ref, other_ref, hidden_ref, before_ref, sums_ref,
):
    sums_ref[...] = jnp.zeros_like(sums_ref)
    in_refs = (u0_ref, u1_ref, u2_ref, u3_ref)
    w_refs = (w0_ref, w1_ref, w2_ref, w3_ref)

    def tile(i, carry):
        rows = rows_of(i)
        io.wait_rows(i)
        nffn = nffn_ref[rows, :]
        cot = cot_ref[rows, :]
        outs = []
        grads = []

        def phases(g, c, group):
            w_in = in_refs[g]
            w_out_rows = w_refs[g]
            cols = slice(256 * c, 256 * c + 256)

            def enter():
                return dot(nffn, w_in[:, cols]), dot_nt(cot, w_out_rows[cols, :])

            def bend(state):
                def piece(x, grad_hidden):
                    square = x * x
                    argument = x * (gelu_root + (gelu_root * gelu_cube) * square)
                    half = 0.5 + 0.5 * jnp.tanh(argument.astype(bf16))
                    x = x.astype(bf16)
                    square = square.astype(bf16)
                    value = x * half
                    rise = 2.0 * gelu_root + (6.0 * gelu_root * gelu_cube) * square
                    slope = half + value * (1.0 - half) * rise
                    return value, grad_hidden.astype(bf16) * slope

                hidden, grad_before = by_pieces(piece, 32, 0, *state)
                if g < 2:
                    place = slice(512 * g + 256 * c, 512 * g + 256 * c + 256)
                    hidden_ref[rows, place] = hidden
                    before_ref[rows, place] = grad_before
                group[c] = hidden, grad_before

            def leave(_):
                if c == 1:
                    outs.append(dot(lanes([group[0][0], group[1][0]]), w_out_rows[...]))

            def leave_back(_):
                if c == 1:
                    grads.append(dot_nt(lanes([group[0][1], group[1][1]]), w_in[...]))

            return enter, bend, leave, leave_back

        interleave(by_halves(4, phases))
        third = third_ref[rows, :]
        result = (third + ((outs[0] + outs[1]) + (outs[2] + outs[3]))).astype(bf16)
        out_ref[rows, :] = result
        placed_ref[rows, :] = result
        grad_normed = (grads[0] + grads[1]) + (grads[2] + grads[3])
        grad_norm = norm_backward(third, norms_ref[6:7], grad_normed, sums_ref, 0)
        g3_low_ref[rows, :] = (cot.astype(f32) + grad_norm).astype(bf16)
        for ref in (out_ref, placed_ref, g3_low_ref):
            io.send(ref, rows)
        return carry

    lax.fori_loop(0, TILES, tile, 0)
    add_sums(sums_ref, gln_ref, 2)
    part = dot_tn(nffn_ref[...], before_ref[...])
    own_ref[0:512, :] = part[:, 0:512].astype(bf16)
    other_ref[0:512, :] = part[:, 512:1024].astype(bf16)
    io.send(own_ref, pl.ds(0, 512))
    io.send(other_ref, pl.ds(0, 512))
    part = dot_tn(hidden_ref[...], cot_ref[...])
    own_ref[512:1024, :] = part[0:512].astype(bf16)
    other_ref[512:1024, :] = part[512:1024].astype(bf16)
    io.send(own_ref, pl.ds(512, 512))
    io.send(other_ref, pl.ds(512, 512))


def back_start(io, g_ref, mixed_ref, w_refs, dm_ref, dq_ref, dk_ref, dv_ref):
    out_rows = jnp.concatenate([w_out(w) for w in w_refs], axis=0)

    def tile(i, carry):
        rows = rows_of(i)
        io.wait_rows(i)
        dm_ref[rows, :] = dot_nt(g_ref[rows, :], out_rows).astype(bf16)
        zeros = jnp.zeros((TILE, 256), f32)
        dq_ref[rows, :] = zeros
        dk_ref[rows, :] = zeros
        dv_ref[rows, :] = zeros
        return carry

    lax.fori_loop(0, TILES, tile, 0)


def attention_back_first(
    cross, meta, io, g_ref, nq_ref, nkv_ref, rank_row_ref, limit_ref, w0_ref, w1_ref,
    q_ref, k_ref, v_ref, mixed_ref, p_ref,
    dq_ref, dk_ref, dv_ref, own_ref, other_ref,
    rank_ref, dm_ref, dqs_ref, dks_ref, dvs_ref, p_buf, p_sem,
):
    load = (p_ref, p_buf, p_sem)
    start_load(meta, cross, load)
    if not cross:
        spread_ranks(rank_row_ref, rank_ref)
    back_start(io, g_ref, mixed_ref, (w0_ref, w1_ref), dm_ref, dqs_ref, dks_ref, dvs_ref)

    io.wait("soon")
    attend_docs_back(
        meta, cross, None if cross else rank_ref, limit_ref, q_ref, k_ref, v_ref, mixed_ref,
        dm_ref, dqs_ref, dks_ref, dvs_ref, load,
    )

    dq_ref[...] = dqs_ref[...].astype(bf16)
    dk_ref[...] = dks_ref[...].astype(bf16)
    dv_ref[...] = dvs_ref[...].astype(bf16)
    for ref in (dq_ref, dk_ref, dv_ref):
        io.send(ref)
    io.wait("late")
    nq = nq_ref[...]
    nkv = nkv_ref[...]
    kv = dot_tn(nkv, lanes([dk_ref[...], dv_ref[...]]))
    for n, part in enumerate((dot_tn(nq, dq_ref[...]), kv[:, 0:256], kv[:, 256:512])):
        own_ref[:, 128 * n : 128 * n + 128] = part[:, :128].astype(bf16)
        other_ref[:, 128 * n : 128 * n + 128] = part[:, 128:].astype(bf16)
    part = dot_tn(mixed_ref[...], g_ref[...])
    for j in range(4):
        rows = slice(128 * j, 128 * j + 128)
        own_ref[rows, 384:512] = part[:128, rows].astype(bf16)
        other_ref[rows, 384:512] = part[128:, rows].astype(bf16)


def back_second_docs(
    cross, meta, io, g_ref, rank_row_ref, limit_ref, w_refs, q_ref, k_ref, v_ref, mixed_ref, p_ref,
    rank_ref, dm_ref, dqs_ref, dks_ref, dvs_ref, p_buf, p_sem,
):
    load = (p_ref, p_buf, p_sem)
    start_load(meta, cross, load)
    if not cross:
        spread_ranks(rank_row_ref, rank_ref)
    back_start(io, g_ref, mixed_ref, w_refs, dm_ref, dqs_ref, dks_ref, dvs_ref)

    io.wait("soon")
    attend_docs_back(
        meta, cross, None if cross else rank_ref, limit_ref, q_ref, k_ref, v_ref, mixed_ref,
        dm_ref, dqs_ref, dks_ref, dvs_ref, load,
    )


def stream_grads(rows, first, second, firsts, seconds):
    dq, dk, dv = first
    dq2, dk2, dv2 = (ref[rows, :].astype(bf16) for ref in second)
    w0, w1 = firsts
    w2, w3 = seconds
    grad_q = dot_nt(dq[rows, :], lanes([w_query(w0), w_query(w1)])) + dot_nt(
        dq2, lanes([w_query(w2), w_query(w3)])
    )
    kv = lanes([dk[rows, :], dv[rows, :]])
    kv2 = lanes([dk2, dv2])
    grad_kv = dot_nt(kv, lanes([w_key(w0), w_key(w1), w_value(w0), w_value(w1)])) + dot_nt(
        kv2, lanes([w_key(w2), w_key(w3), w_value(w2), w_value(w3)])
    )
    return grad_q, grad_kv


def cross_back_second(
    meta, io, g_low_ref, second_ref, norms_ref, w0_ref, w1_ref, w2_ref, w3_ref,
    dq_ref, dk_ref, dv_ref, q_ref, k_ref, v_ref, mixed_ref, p_ref,
    g2_low_ref, placed_ref, gmem_ref, gln_ref,
    dm_ref, dqs_ref, dks_ref, dvs_ref, p_buf, p_sem, sums_ref,
):
    back_second_docs(
        True, meta, io, g_low_ref, None, None, (w2_ref, w3_ref), q_ref, k_ref, v_ref, mixed_ref, p_ref,
        None, dm_ref, dqs_ref, dks_ref, dvs_ref, p_buf, p_sem,
    )

    io.wait("late")
    sums_ref[...] = jnp.zeros_like(sums_ref)

    def tile(i, carry):
        rows = rows_of(i)
        grad_q, grad_kv = stream_grads(
            rows,
            (dq_ref, dk_ref, dv_ref),
            (dqs_ref, dks_ref, dvs_ref),
            (w0_ref, w1_ref),
            (w2_ref, w3_ref),
        )
        low_kv = grad_kv.astype(bf16)
        gmem_ref[rows, :] = low_kv
        placed_ref[rows, :] = low_kv.astype(f32)
        io.send(gmem_ref, rows)
        io.send(placed_ref, rows)
        grad_norm = norm_backward(second_ref[rows, :], norms_ref[4:5], grad_q, sums_ref, 0)
        g2_low_ref[rows, :] = (g_low_ref[rows, :].astype(f32) + grad_norm).astype(bf16)
        io.send(g2_low_ref, rows)
        return carry

    lax.fori_loop(0, TILES, tile, 0)
    add_sums(sums_ref, gln_ref, 2)


def self_back_second(
    meta, io, g_low_ref, rank_row_ref, limit_ref, w2_ref, w3_ref,
    q_ref, k_ref, v_ref, mixed_ref, p_ref,
    dq_ref, dk_ref, dv_ref,
    rank_ref, dm_ref, dqs_ref, dks_ref, dvs_ref, p_buf, p_sem,
):
    back_second_docs(
        False, meta, io, g_low_ref, rank_row_ref, limit_ref, (w2_ref, w3_ref), q_ref, k_ref, v_ref,
        mixed_ref, p_ref, rank_ref, dm_ref, dqs_ref, dks_ref, dvs_ref, p_buf, p_sem,
    )
    dq_ref[...] = dqs_ref[...].astype(bf16)
    dk_ref[...] = dks_ref[...].astype(bf16)
    dv_ref[...] = dvs_ref[...].astype(bf16)


def self_back_finish(
    meta, io, g_ref, xq_ref, xc_ref, norms_ref, w0_ref, w1_ref, w2_ref, w3_ref,
    dq_ref, dk_ref, dv_ref, dq2_ref, dk2_ref, dv2_ref,
    placed_q_ref, placed_c_ref, gq_ref, gc_ref, gln_ref, sums_ref,
):
    sums_ref[...] = jnp.zeros_like(sums_ref)

    def tile(i, carry):
        rows = rows_of(i)
        io.wait_rows(i)
        grad_q, grad_kv = stream_grads(
            rows,
            (dq_ref, dk_ref, dv_ref),
            (dq2_ref, dk2_ref, dv2_ref),
            (w0_ref, w1_ref),
            (w2_ref, w3_ref),
        )
        grad_norm = norm_backward(xq_ref[rows, :], norms_ref[0:1], grad_q, sums_ref, 0)
        low_q = (g_ref[rows, :].astype(f32) + grad_norm).astype(bf16)
        gq_ref[rows, :] = low_q
        io.send(gq_ref, rows)
        placed_q_ref[rows, :] = low_q.astype(f32)
        io.send(placed_q_ref, rows)
        grad_norm = norm_backward(xc_ref[rows, :], norms_ref[2:3], grad_kv, sums_ref, 16)
        low_c = grad_norm.astype(bf16)
        gc_ref[rows, :] = low_c
        io.send(gc_ref, rows)
        placed_c_ref[rows, :] = low_c.astype(f32)
        io.send(placed_c_ref, rows)
        return carry

    lax.fori_loop(0, TILES, tile, 0)
    add_sums(sums_ref, gln_ref, 4)


def place_rows(meta, *refs):
    count = len(refs) // 3
    for n in range(count):
        refs[2 * count + n][...] = refs[n][...].astype(refs[2 * count + n].dtype)


GROUP = 8


def position(meta):
    r = meta[35]
    return lax.rem(r, 2), r // 2


def join(own, other, rows):
    return (own[rows, :].astype(f32) + other[rows, :].astype(f32)).astype(bf16)


def join_halves(meta, own, other, keep, send):
    y, _ = position(meta)
    size = keep.shape[0]
    keep[...] = join(own, other, rows_of(y, size))
    send[...] = join(own, other, rows_of(1 - y, size))


def join_chunks(meta, kept, arrived, keep, sends):
    _, z = position(meta)
    size = keep.shape[0]
    keep[...] = join(kept, arrived, rows_of(z, size))
    for s, (send, first) in enumerate(sends, 1):
        send[first : first + size, :] = join(kept, arrived, rows_of(z ^ s, size))


def add_up(kept, parts, first):
    size = kept.shape[0]
    total = kept[...].astype(f32)
    for part in parts:
        total = total + part[first : first + size, :].astype(f32)
    return total.astype(bf16)


def half_of(meta, total, parts, first, half):
    _, z = position(meta)
    size = total.shape[0]
    half[rows_of(z, size), :] = total[...]
    for s, part in enumerate(parts, 1):
        half[rows_of(z ^ s, size), :] = part[first : first + size, :]


def slot_1(meta, ffn_own, ffn_other, keep, send):
    join_halves(meta, ffn_own, ffn_other, keep, send)


def slot_2(
    meta, ffn_kept, ffn_arrived, cross_own, cross_other, ffn_keep, f1, f2, f3, keep, send
):
    join_chunks(meta, ffn_kept, ffn_arrived, ffn_keep, [(f1, 0), (f2, 0), (f3, 0)])
    join_halves(meta, cross_own, cross_other, keep, send)


def slot_3(
    meta, ffn_kept, f1, f2, f3, cross_kept, cross_arrived, self_own, self_other,
    ffn_total, cross_keep, m1, m2, m3, self_keep, self_send,
):
    join_halves(meta, self_own, self_other, self_keep, self_send)
    total = add_up(ffn_kept, (f1, f2, f3), 0)
    ffn_total[...] = total
    size = total.shape[0]
    join_chunks(meta, cross_kept, cross_arrived, cross_keep, [(m, size) for m in (m1, m2, m3)])
    for m in (m1, m2, m3):
        m[0:size, :] = total


def slot_4(
    meta, ffn_total, m1, m2, m3, cross_kept, self_kept, self_arrived,
    ffn_half, cross_total, self_keep, *sends,
):
    join_chunks(meta, self_kept, self_arrived, self_keep, [(send, 0) for send in sends])
    total = add_up(cross_kept, (m1, m2, m3), ffn_total.shape[0])
    cross_total[...] = total
    size = total.shape[0]
    for send in sends:
        send[size:, :] = total
    half_of(meta, ffn_total, (m1, m2, m3), 0, ffn_half)


def slot_5(meta, self_kept, cross_total, m1, m2, m3, gln_own, gln_other, send, cross_half):
    size = self_kept.shape[0]
    total = add_up(self_kept, (m1, m2, m3), 0)
    gln = gln_own[...] + gln_other[...]
    gln = jnp.concatenate([gln, jnp.zeros((8, D), f32)], axis=0).astype(bf16)
    for r in range(GROUP):
        send[r, 0:size, :] = total
        send[r, size : size + 16, :] = gln
    half_of(meta, cross_total, (m1, m2, m3), size, cross_half)


def unpack_attention(whole_ref, outs):
    for i in range(3):
        outs[i][...] = whole_ref[:, 128 * i : 128 * i + 128].astype(f32)
    for j in range(4):
        rows = slice(128 * j, 128 * j + 128)
        outs[3][:, rows] = whole_ref[rows, 384:512].astype(f32)


def unpack_ffn(meta, half, arrived, out_in, out_out, ffn_whole):
    y, _ = position(meta)
    ffn_whole[rows_of(y, 512), :] = half[...]
    ffn_whole[rows_of(1 - y, 512), :] = arrived[...]
    out_in[...] = ffn_whole[0:512, :].astype(f32)
    out_out[...] = ffn_whole[512:1024, :].astype(f32)


def unpack_rest(meta, cross_half, cross_arrived, parts, *refs):
    *outs, whole_ref = refs
    y, _ = position(meta)
    whole_ref[rows_of(y, 256), :] = cross_half[...]
    whole_ref[rows_of(1 - y, 256), :] = cross_arrived[...]
    unpack_attention(whole_ref, outs[0:4])
    size = parts.shape[1] - 16
    total = parts[0, size : size + 16, :].astype(f32)
    for r in range(1, GROUP):
        total = total + parts[r, size : size + 16, :].astype(f32)
    for n in range(8):
        outs[8 + n][...] = total[n : n + 1]
    for r in range(GROUP):
        first = size * (4 * (r % 2) + r // 2)
        whole_ref[first : first + size, :] = parts[r, 0:size, :]
    unpack_attention(whole_ref, outs[4:8])


def whole(shape):
    zeros = (0,) * len(shape)
    return pl.BlockSpec(shape, lambda d, meta: zeros)


def own_row(width):
    return pl.BlockSpec((SEQ, width), lambda d, meta: (meta[0], 0))


ANY = pl.BlockSpec(memory_space=pl.ANY)


def in_hbm(x):
    return pltpu.with_memory_space_constraint(x, pltpu.HBM)


probability_out = (pltpu.HBM((DOCS, 4, FAST_K, FAST_Q), bf16), None, ANY)
probability_scratch = [
    pltpu.VMEM((2, TOGETHER, 4, FAST_K, FAST_Q), bf16),
    pltpu.SemaphoreType.DMA((2,)),
]


class Copies:
    def __init__(self, meta):
        self.first = meta[0] * SEQ
        self.loads = {}
        self.tiles = []
        self.sends = []

    def load(self, stage, source, target, sems, own_row):
        if stage == "fresh":
            stage = "now"
        if stage == "tiles":
            first = self.first if own_row else 0
            self.tiles.append((source, target, sems, first))
            return
        if own_row:
            source = source.at[pl.ds(pl.multiple_of(self.first, SEQ), SEQ)]
        copy = pltpu.make_async_copy(source, target, sems[0].at[sems[1], 0])
        self.loads.setdefault(stage, []).append(copy)

    def tile(self, entry, i):
        source, target, (sems, b), first = entry
        rows = pl.ds(pl.multiple_of(first + i * TILE, TILE), TILE)
        return pltpu.make_async_copy(source.at[rows], target.at[rows_of(i)], sems.at[b, i])

    def start(self):
        for copy in self.loads.get("now", []):
            copy.start()
        for i in range(TILES):
            for entry in self.tiles:
                self.tile(entry, i).start()
        for stage in ("soon", "late"):
            for copy in self.loads.get(stage, []):
                copy.start()

    def wait(self, stage):
        for copy in self.loads.pop(stage, []):
            copy.wait()

    def wait_rows(self, i):
        for entry in self.tiles:
            self.tile(entry, i).wait()

    def result(self, source, target, sem, own_row):
        self.sends.append([source, target, sem, own_row, False])

    def send(self, ref, rows=None):
        for entry in self.sends:
            source, target, sem, own_row, _ = entry
            if source is ref:
                entry[4] = True
                first = self.first if own_row else 0
                if rows is None:
                    size = source.shape[0]
                else:
                    source = source.at[rows]
                    first, size = first + rows.start, rows.size
                if rows is not None or own_row:
                    target = target.at[pl.ds(pl.multiple_of(first, size), size)]
                pltpu.make_async_copy(source, target, sem).start()

    def finish(self):
        for stage in list(self.loads):
            self.wait(stage)
        for source, _, _, _, started in self.sends:
            if not started:
                self.send(source)
        for source, target, sem, own_row, _ in self.sends:
            if own_row:
                target = target.at[pl.ds(pl.multiple_of(self.first, SEQ), SEQ)]
            pltpu.make_async_copy(source, target, sem).wait()


def out(shape, dtype, own_row=False):
    return (shape, dtype, own_row)


def call(kernel, name, operands, outs, scratch, flops, token=None):
    arrays = [operands[0][0]]
    in_specs, out_specs, out_shapes = [], [], []
    buffers = []
    loads = []
    for n, (x, how) in enumerate(operands[1:]):
        if isinstance(how, str):
            stage, _, row = how.partition("_")
            shape = ((SEQ,) + x.shape[1:]) if row else x.shape
            loads.append((n, stage, len(buffers), bool(row)))
            buffers.append(pltpu.VMEM(shape, x.dtype))
            arrays.append(x if stage == "fresh" else in_hbm(x))
            in_specs.append(ANY)
        else:
            arrays.append(x)
            in_specs.append(how)
    results = []
    for n, (shape, dtype, how) in enumerate(outs):
        if isinstance(how, bool):
            results.append((n, len(buffers), how))
            buffers.append(pltpu.VMEM(shape, dtype))
            shape = ((2 * SEQ,) + shape[1:]) if how else shape
            out_shapes.append(pltpu.HBM(shape, dtype))
            out_specs.append(ANY)
        else:
            out_shapes.append(jax.ShapeDtypeStruct(shape, dtype) if dtype else shape)
            out_specs.append(how)
    n_in, n_out = len(in_specs), len(out_specs)
    if token is not None:
        arrays.append(token)
        in_specs.append(whole((8, 128)))
        out_specs.append(whole((8, 128)))
        out_shapes.append(jax.ShapeDtypeStruct((8, 128), f32))

    def body(meta, *refs):
        ins, refs = list(refs[:n_in]), refs[len(in_specs) - n_in + n_in :]
        results_out, refs = list(refs[:n_out]), refs[n_out:]
        if token is not None:
            token_out, refs = refs[0], refs[1:]
            token_out[...] = jnp.zeros_like(token_out)
        bufs, refs = refs[: len(buffers)], refs[len(buffers) :]
        rest = refs[: len(scratch)]
        copies = Copies(meta)
        if buffers:
            sems = refs[len(scratch)]
        for n, stage, b, row in loads:
            copies.load(stage, ins[n], bufs[b], (sems, b), row)
            ins[n] = bufs[b]
        for n, b, row in results:
            copies.result(bufs[b], results_out[n], sems.at[b, 0], row)
            results_out[n] = bufs[b]
        copies.start()
        copies.wait("now")
        if buffers:
            kernel(meta, copies, *ins, *results_out, *rest)
        else:
            kernel(meta, *ins, *results_out, *rest)
        copies.finish()

    moved = sum(x.size * x.dtype.itemsize for x in arrays[1:])
    sems = [pltpu.SemaphoreType.DMA((len(buffers), TILES))] if buffers else []
    return pl.pallas_call(
        body,
        name=name,
        grid_spec=pltpu.PrefetchScalarGridSpec(
            num_scalar_prefetch=1,
            grid=(1,),
            in_specs=in_specs,
            out_specs=out_specs,
            scratch_shapes=buffers + scratch + sems,
        ),
        out_shape=out_shapes,
        compiler_params=pltpu.CompilerParams(
            dimension_semantics=("arbitrary",), vmem_limit_bytes=40 * 1024 * 1024
        ),
        cost_estimate=pl.CostEstimate(
            flops=int(flops), bytes_accessed=int(moved), transcendentals=0
        ),
    )(*arrays)


def simple(kernel, name, meta, operands, outs, scratch=()):
    return pl.pallas_call(
        kernel,
        name=name,
        grid_spec=pltpu.PrefetchScalarGridSpec(
            num_scalar_prefetch=1,
            grid=(1,),
            in_specs=[whole(x.shape) for x in operands],
            out_specs=[whole(shape) for shape, _ in outs],
            scratch_shapes=scratch,
        ),
        out_shape=[jax.ShapeDtypeStruct(shape, dtype) for shape, dtype in outs],
        compiler_params=pltpu.CompilerParams(vmem_limit_bytes=16 * 1024 * 1024),
    )(meta, *operands)


def full(x):
    return (x, whole(x.shape))


def shards(
    query_stream,
    content_stream,
    memory,
    segment_ids,
    source_segments,
    context_rank,
    context_limit,
    padding,
    ln_query_gain,
    ln_query_bias,
    ln_content_gain,
    ln_content_bias,
    self_query,
    self_key,
    self_value,
    self_out,
    ln_cross_gain,
    ln_cross_bias,
    cross_query,
    cross_key,
    cross_value,
    cross_out,
    ln_ffn_gain,
    ln_ffn_bias,
    ffn_in,
    ffn_out,
    cotangent,
):
    core = lax.axis_index("heads") % 2

    def to_core(x):
        return lax.ppermute(x, "heads", [(h, h ^ 1) for h in range(4)])

    hold = lambda *xs: lax.optimization_barrier(xs)

    def to_chip(x):
        return lax.ppermute(x, "heads", [(h, h ^ 2) for h in range(4)])

    row = pl.BlockSpec((1, 8, 128), lambda d, core: (core[0], 0, 0))

    def token_row(x):
        return (in_hbm(x.reshape(2, 8, 128)), row)

    def fixed(x):
        zeros = (0,) * x.ndim
        return (in_hbm(x), pl.BlockSpec(x.shape, lambda d, core: zeros))

    prepared = [
        ((36,), jnp.int32, pl.BlockSpec(memory_space=pltpu.SMEM)),
        ((1, SEQ), f32, whole((1, SEQ))),
        ((1, SEQ), f32, whole((1, SEQ))),
        ((8, D), f32, whole((8, D))),
        ((D, D), bf16, whole((D, D))),
        ((D, D), bf16, whole((D, D))),
    ]
    gains = (
        ln_query_gain,
        ln_query_bias,
        ln_content_gain,
        ln_content_bias,
        ln_cross_gain,
        ln_cross_bias,
        ln_ffn_gain,
        ln_ffn_bias,
    )
    weights = (self_query, self_key, self_value, self_out)
    weights += (cross_query, cross_key, cross_value, cross_out)
    tokens = (segment_ids, source_segments, context_rank, context_limit, padding)
    meta, rank, limit, norms, ws0, wc0 = call(
        prepare,
        "prepare",
        [(jnp.stack([core, lax.axis_index("rows") % GROUP]).astype(jnp.int32), None)]
        + [token_row(x) for x in tokens]
        + [fixed(x.reshape(1, D)) for x in gains]
        + [fixed(x) for x in weights],
        prepared,
        [],
        0,
    )

    ws1 = to_core(ws0)
    ws2 = to_chip(ws0)
    wc1 = to_core(wc0)
    u0, v0 = ffn_in, ffn_out
    meta_in = (meta, None)

    heads_out = [out((SEQ, 256), bf16)] * 4

    def stream_out(dtype, own_row=False):
        return out((SEQ, D), dtype, own_row)

    def now(*xs):
        return [(x, "now") for x in xs]

    def fresh(*xs):
        return [(x, "fresh") for x in xs]

    def soon(*xs):
        return [(x, "soon") for x in xs]

    def late(*xs):
        return [(x, "late") for x in xs]

    def small(*xs):
        return [(x, whole(x.shape)) for x in xs]

    limits = pltpu.VMEM((SEQ, 128), f32)
    pair_flops = 2 * SEQ * D * 768 + 2 * 2 * 4 * DOCS * FAST_Q * FAST_K * 256

    nq, nc, *first, token = call(
        self_first,
        "self_first",
        [meta_in, (query_stream, "tiles_row"), (content_stream, "tiles_row")]
        + small(rank, limit, norms)
        + fresh(ws0, ws1),
        [stream_out(bf16), stream_out(bf16)] + heads_out + [probability_out],
        [limits] + probability_scratch,
        pair_flops,
        jnp.zeros((8, 128), f32),
    )
    ws2, wc0, token = hold(ws2, wc0, token)
    ws3 = to_core(ws2)
    wc2 = to_chip(wc0)
    *second_heads, second, ncross, token = call(
        self_second,
        "self_second",
        [meta_in, (query_stream, "late_row")]
        + [(nq, "tiles"), (nc, "tiles")]
        + small(rank, limit, norms)
        + late(ws0, ws1)
        + fresh(ws2, ws3)
        + late(first[3]),
        heads_out + [probability_out, stream_out(bf16), stream_out(bf16)],
        [limits] + probability_scratch,
        pair_flops + 2 * SEQ * D * D,
        token,
    )
    wc2, u0, v0, token = hold(wc2, u0, v0, token)
    wc3 = to_core(wc2)
    u2 = to_chip(u0)
    v2 = to_chip(v0)
    u1 = to_core(u0)
    *cross_heads, token = call(
        cross_first,
        "cross_first",
        [meta_in, (ncross, "tiles"), (memory, "tiles_row")] + fresh(wc0, wc1),
        heads_out + [probability_out],
        probability_scratch,
        pair_flops,
        token,
    )
    wc3, v0, token = hold(wc3, v0, token)
    v1 = to_core(v0)
    *cross_heads_second, third, nffn, token = call(
        cross_second,
        "cross_second",
        [meta_in]
        + late(second)
        + [(ncross, "tiles"), (memory, "tiles_row")]
        + small(norms)
        + late(wc0, wc1)
        + fresh(wc2, wc3)
        + late(cross_heads[3]),
        heads_out
        + [probability_out, ((SEQ, D), f32, whole((SEQ, D))), ((SEQ, D), bf16, whole((SEQ, D)))],
        probability_scratch,
        pair_flops + 2 * SEQ * D * D,
        token,
    )
    u2, v2, token = hold(u2, v2, token)
    u3 = to_core(u2)
    v3 = to_core(v2)
    grads_ln = ((8, D), f32, whole((8, D)))
    placed_output, output, g3_low, gln_ffn, ffn_own, ffn_other, token = call(
        ffn_both,
        "ffn_both",
        [meta_in]
        + small(third, nffn)
        + [(cotangent, "tiles_row")]
        + small(norms)
        + now(u0) + fresh(u1, u2, u3) + now(v0) + fresh(v1, v2, v3),
        [
            stream_out(bf16, True),
            stream_out(bf16),
            stream_out(bf16),
            grads_ln,
            out((1024, D), bf16),
            out((1024, D), bf16),
        ],
        [pltpu.VMEM((SEQ, 1024), bf16), pltpu.VMEM((SEQ, 1024), bf16), pltpu.VMEM((16, D), f32)],
        12 * SEQ * D * 2048,
        token,
    )

    def both_rows(placed_own, others, name):
        count = len(others)
        size = SEQ // 2
        one = pl.BlockSpec((size, D), lambda i, meta: (i, 0))
        block = pl.BlockSpec((size, D), lambda i, meta: (2 * (1 - meta[0]) + i, 0))
        return pl.pallas_call(
            place_rows,
            name=name,
            grid_spec=pltpu.PrefetchScalarGridSpec(
                num_scalar_prefetch=1,
                grid=(2,),
                in_specs=[one] * count + [pl.BlockSpec(memory_space=pl.ANY)] * count,
                out_specs=[block] * count,
            ),
            out_shape=[jax.ShapeDtypeStruct(x.shape, x.dtype) for x in placed_own],
            input_output_aliases={1 + count + n: n for n in range(count)},
        )(meta, *others, *placed_own)

    row_count = lax.axis_size("rows")
    assert row_count % GROUP == 0

    def along_rows(x, s):
        return lax.ppermute(x, "rows", [(r, r ^ s) for r in range(row_count)])

    def to_y(x):
        return along_rows(x, 1)

    def to_z(sends):
        return [along_rows(x, 2 * s) for s, x in enumerate(sends, 1)]

    def rows_out(*sizes):
        return [((n, D), bf16) for n in sizes]

    ffn_other = to_core(ffn_other)
    output_other = to_core(output)

    back_scratch = [pltpu.VMEM((SEQ, 256), bf16)] + [pltpu.VMEM((SEQ, 256), f32)] * 3
    back_scratch += probability_scratch
    pair_out = out((SEQ, 256), bf16)
    packed_outs = [((D, D), bf16, whole((D, D)))] * 2
    back_flops = 2 * SEQ * D * 256 + 4 * 2 * 4 * DOCS * FAST_Q * FAST_K * 256

    def head_inputs(natural, p):
        return soon(*natural) + [(in_hbm(p), ANY)]

    *cross_grads, cross_own, cross_other, token = call(
        functools.partial(attention_back_first, True),
        "cross_back_first",
        [meta_in]
        + [(g3_low, "tiles")]
        + late(ncross)
        + [(memory, "late_row")]
        + small(rank, limit)
        + now(wc0, wc1)
        + head_inputs(cross_heads[0:4], cross_heads[4]),
        [pair_out] * 3 + packed_outs,
        [limits] + back_scratch,
        back_flops + 2 * SEQ * D * 1024,
        token,
    )
    ffn_other, output_other, token = hold(ffn_other, output_other, token)
    ffn_keep, ffn_send = simple(slot_1, "slot_1", meta, [ffn_own, ffn_other], rows_out(512, 512))
    ffn_send, token = hold(ffn_send, token)
    ffn_arrived = to_y(ffn_send)
    cross_other = to_core(cross_other)
    g2_low, placed_mem, grad_mem, gln_cross, token = call(
        cross_back_second,
        "cross_back_second",
        [meta_in]
        + [(g3_low, "tiles")]
        + late(second)
        + small(norms)
        + late(wc0, wc1)
        + now(wc2, wc3)
        + late(*cross_grads)
        + head_inputs(cross_heads_second[0:4], cross_heads_second[4]),
        [stream_out(bf16), stream_out(f32, True), stream_out(bf16), grads_ln],
        back_scratch + [pltpu.VMEM((16, D), f32)],
        back_flops + 2 * SEQ * D * 1536,
        token,
    )
    ffn_arrived, cross_other, token = hold(ffn_arrived, cross_other, token)
    ffn_keep, *sends, cross_keep, cross_send = simple(
        slot_2,
        "slot_2",
        meta,
        [ffn_keep, ffn_arrived, cross_own, cross_other],
        rows_out(128, 128, 128, 128, 256, 256),
    )
    ffn_keep, cross_send, token = hold(ffn_keep, cross_send, token)
    ffn_parts = to_z(sends)
    cross_arrived = to_y(cross_send)

    *self_grads, self_own, self_other, token = call(
        functools.partial(attention_back_first, False),
        "self_back_first",
        [meta_in]
        + [(g2_low, "tiles")]
        + late(nq, nc)
        + small(rank, limit)
        + now(ws0, ws1)
        + head_inputs(first[0:4], first[4]),
        [pair_out] * 3 + packed_outs,
        [limits] + back_scratch,
        back_flops + 2 * SEQ * D * 1024,
        token,
    )
    *ffn_parts, cross_arrived, self_other, token = hold(
        *ffn_parts, cross_arrived, self_other, token
    )
    self_other = to_core(self_other)
    ffn_total, cross_keep, *sends, self_keep, self_send = simple(
        slot_3,
        "slot_3",
        meta,
        [ffn_keep, *ffn_parts, cross_keep, cross_arrived, self_own, self_other],
        rows_out(128, 64, 192, 192, 192, 256, 256),
    )
    ffn_total, self_send, grad_mem, token = hold(ffn_total, self_send, grad_mem, token)
    mem_other = to_core(grad_mem)
    self_arrived = to_y(self_send)
    messages = to_z(sends)
    *self_grads_second, token = call(
        self_back_second,
        "self_back_second",
        [meta_in, (g2_low, "tiles")]
        + small(rank, limit)
        + now(ws2, ws3)
        + head_inputs(second_heads[0:4], second_heads[4]),
        [((SEQ, 256), bf16, whole((SEQ, 256)))] * 3,
        [limits] + back_scratch,
        back_flops,
        token,
    )
    *messages, self_arrived, mem_other, token = hold(*messages, self_arrived, mem_other, token)
    ffn_half, cross_total, self_keep, *sends = simple(
        slot_4,
        "slot_4",
        meta,
        [ffn_total, *messages, cross_keep, self_keep, self_arrived],
        rows_out(512, 64, 64, 128, 128, 128),
    )
    cross_total, ffn_half, token = hold(cross_total, ffn_half, token)
    messages = to_z(sends)
    ffn_arrived = to_y(ffn_half)
    placed_q, placed_c, gq, gc, gln_self, token = call(
        self_back_finish,
        "self_back_finish",
        [meta_in, (g2_low, "tiles"), (query_stream, "tiles_row"), (content_stream, "tiles_row")]
        + small(norms)
        + now(ws0, ws1, ws2, ws3)
        + [(x, "tiles") for x in self_grads]
        + small(*self_grads_second),
        [stream_out(f32, True), stream_out(f32, True), stream_out(bf16), stream_out(bf16), grads_ln],
        [pltpu.VMEM((32, D), f32)],
        2 * SEQ * D * 1536,
        token,
    )
    gln = jnp.concatenate([gln_self[0:4], gln_cross[0:2], gln_ffn[0:2]], axis=0)
    gln_other = to_core(gln)
    *messages, ffn_arrived, gln_ffn = hold(*messages, ffn_arrived, gln_ffn)
    last_send, cross_half = simple(
        slot_5,
        "slot_5",
        meta,
        [self_keep, cross_total, *messages, gln, gln_other],
        [((GROUP, 80, D), bf16), ((256, D), bf16)],
    )
    groups = None
    if row_count > GROUP:
        groups = [list(range(r, r + GROUP)) for r in range(0, row_count, GROUP)]
    def gather(x):
        return lax.all_to_all(x, "rows", 0, 0, axis_index_groups=groups)

    last_parts = gather(last_send)
    cross_arrived = to_y(cross_half)
    def over_groups(totals):
        if row_count == GROUP:
            return totals
        groups = [list(range(r, row_count, GROUP)) for r in range(GROUP)]
        return lax.psum(totals, "rows", axis_index_groups=groups)

    gq_both, gc_both = both_rows([placed_q, placed_c], [to_core(gq), to_core(gc)], "place_late")

    grad_ffn_in, grad_ffn_out = simple(
        unpack_ffn,
        "unpack_ffn",
        meta,
        [ffn_half, ffn_arrived],
        [((D, D), f32)] * 2,
        [pltpu.VMEM((2 * D, D), bf16)],
    )
    attention_outs = [((512, 128), f32)] * 3 + [((128, 512), f32)]
    out_both, grad_mem_both = both_rows(
        [placed_output, placed_mem], [output_other, mem_other], "place_early"
    )
    cross_arrived, gq_both, out_both, grad_ffn_in = hold(
        cross_arrived, gq_both, out_both, grad_ffn_in
    )
    parts = simple(
        unpack_rest,
        "unpack_rest",
        meta,
        [cross_half, cross_arrived, last_parts],
        attention_outs * 2 + [((1, D), f32)] * 8,
        [pltpu.VMEM((D, D), bf16)],
    )
    grad_cross_parts, grad_self_parts = parts[0:4], parts[4:8]
    gln = [x.reshape(D) for x in parts[8:16]]
    grad_ffn_in, grad_ffn_out, grad_cross_parts, grad_self_parts, gln = over_groups(
        (grad_ffn_in, grad_ffn_out, grad_cross_parts, grad_self_parts, gln)
    )
    return (
        out_both,
        gq_both,
        gc_both,
        grad_mem_both,
        gln[0],
        gln[1],
        gln[2],
        gln[3],
        *grad_self_parts,
        gln[4],
        gln[5],
        *grad_cross_parts,
        gln[6],
        gln[7],
        grad_ffn_in,
        grad_ffn_out,
    )


def solution(mesh):
    assert mesh.shape["heads"] == 4
    row_spec = P("rows", None)
    flat = P("rows")
    by_column = P(None, "heads")
    by_row = P("heads", None)
    attention = (by_column, by_column, by_column, by_row)
    in_specs = (
        (row_spec,) * 3
        + (flat,) * 5
        + (P(),) * 4
        + attention
        + (P(),) * 2
        + attention
        + (P(),) * 2
        + (by_column, by_row, row_spec)
    )
    out_specs = (
        (row_spec,) * 4
        + (P(),) * 4
        + attention
        + (P(),) * 2
        + attention
        + (P(),) * 2
        + (by_column, by_row)
    )
    return jax.shard_map(shards, mesh=mesh, in_specs=in_specs, out_specs=out_specs, check_vma=False)
```
